32 devices in a mesh: row: 8 (over z, x), col: 4 (over y, core).
Axes of the slice: x: 2, y: 2, z: 4, core: 2. Of those that a mesh axis runs over, the one named last changes fastest.
Arguments:
- tokens: float32 [16384, 1024], P(('row', 'col')), may hold values from -6 to 6
- teacher: float32 [16384, 1024], P(('row', 'col')), may hold values from -6 to 6
- segments: int32 [16384], P('row'), may hold values from -1 to 2, as said below
- live_mask: int32 [16384], P('row'), may hold values from 0 to 1, as said below
- weight_qkv: float32 [3, 1024, 1024], P(None, 'row', 'col'), may hold values from -0.1875 to 0.1875
- weight_proj: float32 [1024, 1024], P('col', 'row'), may hold values from -0.5 to 0.5
- weight_up: float32 [1024, 4096], P('row', 'col'), may hold values from -0.1875 to 0.1875
- weight_down: float32 [4096, 1024], P('col', 'row'), may hold values from -0.09375 to 0.09375
- norm_params: float32 [4, 1024], replicated, may hold values from -1 to 2, as said below
- first_qkv: float32 [3, 1024, 1024], P(None, 'row', 'col')
- first_proj: float32 [1024, 1024], P('col', 'row')
- first_up: float32 [1024, 4096], P('row', 'col')
- first_down: float32 [4096, 1024], P('col', 'row')
- first_norms: float32 [4, 1024], replicated
- second_qkv: float32 [3, 1024, 1024], P(None, 'row', 'col'), as said below
- second_proj: float32 [1024, 1024], P('col', 'row'), as said below
- second_up: float32 [1024, 4096], P('row', 'col'), as said below
- second_down: float32 [4096, 1024], P('col', 'row'), as said below
- second_norms: float32 [4, 1024], replicated, as said below
Outputs:
- loss_value: float32 [], replicated
- token_grad: float32 [16384, 1024], P(('row', 'col'))
- updated_qkv: float32 [3, 1024, 1024], P(None, 'row', 'col')
- updated_proj: float32 [1024, 1024], P('col', 'row')
- updated_up: float32 [1024, 4096], P('row', 'col')
- updated_down: float32 [4096, 1024], P('col', 'row')
- updated_norms: float32 [4, 1024], replicated
- momentum_qkv: float32 [3, 1024, 1024], P(None, 'row', 'col')
- momentum_proj: float32 [1024, 1024], P('col', 'row')
- momentum_up: float32 [1024, 4096], P('row', 'col')
- momentum_down: float32 [4096, 1024], P('col', 'row')
- momentum_norms: float32 [4, 1024], replicated
- variance_qkv: float32 [3, 1024, 1024], P(None, 'row', 'col')
- variance_proj: float32 [1024, 1024], P('col', 'row')
- variance_up: float32 [1024, 4096], P('row', 'col')
- variance_down: float32 [4096, 1024], P('col', 'row')
- variance_norms: float32 [4, 1024], replicated
The draws below stay inside these ranges and needn't reach their ends.
Inputs may be any that keep to these rules, and one draw needn't show every extreme that they name: `segments`: within each group of 2048 slots, image i (0 to 2) is one run of 577 slots numbered i, the runs in order of i with padding slots, numbered -1, between or around them. `live_mask`: 1 on the first slot of every image, 0 on every padding slot. `norm_params`: rows 0 and 2 are positive. `second_qkv`: Positive. `second_proj`: Positive. `second_up`: Positive. `second_down`: Positive. `second_norms`: Positive.
All inputs are finite; a program needn't handle non-finite values.
Results may differ from the reference program's by a relative error of at most 0.012.
The reference program's roundings to bfloat16 on the way count: a program that leaves them out, or rounds other values in their place, can miss the bound.
Values may be sent and summed in bfloat16 or wider, within the bound.
No kernel may reach another device: no remote copies, remote signals or barrier semaphores. Data moves between devices by JAX's collectives and lax.ppermute only.
A program may use at most 192 MiB of HBM per device.

```python
import math
import jax
import jax.numpy as jnp
from jax import lax

D = 1024
HEADS = 16
HEAD_DIM = 64
FF = 4096
PATCHES = 577
STEP = 10
TOK_DEV = 512
GROUP = 2048
TOKENS = 16384
QBLOCK = 512
N_ROW = 8
N_COL = 4


def packing(key):
    group_slots = TOK_DEV * N_COL
    image_count = group_slots // PATCHES
    spare_slots = group_slots - image_count * PATCHES
    offsets = jnp.sort(jax.random.randint(key, (N_ROW, image_count), 0, spare_slots + 1), axis=1)
    image_starts = offsets + jnp.arange(image_count, dtype=jnp.int32)[None, :] * PATCHES
    positions = jnp.arange(group_slots, dtype=jnp.int32)
    covered = (positions[None, None, :] >= image_starts[:, :, None]) & (positions[None, None, :] < image_starts[:, :, None] + PATCHES)
    numbered = jnp.sum(covered.astype(jnp.int32) * jnp.arange(image_count, dtype=jnp.int32)[None, :, None], axis=1)
    segment_ids = jnp.where(jnp.any(covered, axis=1), numbered, -1)
    leading = jnp.any(positions[None, None, :] == image_starts[:, :, None], axis=1)
    return (segment_ids, leading)


def draw_segments(key, part):
    segment_ids, leading = packing(key)
    return segment_ids.reshape(TOKENS).astype(jnp.int32)


def draw_live_mask(key, part):
    segment_ids, leading = packing(key)
    key = jax.random.fold_in(key, 2)
    group_slots = TOK_DEV * N_COL
    positions = jnp.arange(group_slots, dtype=jnp.int32)
    column = positions // TOK_DEV
    row_index = jnp.arange(N_ROW, dtype=jnp.int32)[:, None]
    row_span = max(N_ROW - 1, 1)
    col_span = max(N_COL - 1, 1)
    threshold = 1000 * (row_span + 2 * row_index) * (col_span + 2 * column[None, :]) // (10 * row_span * col_span)
    dice_roll = jax.random.randint(key, (N_ROW, group_slots), 0, 1000)
    live_slots = ((dice_roll < threshold) | leading) & (segment_ids >= 0)
    return live_slots.astype(jnp.int32).reshape(TOKENS)


def draw_norm_params(key, part):
    key = jax.random.fold_in(key, 3)
    gain_key, bias_key = jax.random.split(key)
    gains = jnp.exp(jax.random.uniform(gain_key, (2, D), jnp.float32, math.log(0.5), math.log(2.0)))
    shifts = 0.3 * jnp.clip(jax.random.normal(bias_key, (2, D), jnp.float32), -3.0, 3.0)
    return jnp.stack([gains[0], shifts[0], gains[1], shifts[1]])


def grad_size(factor):
    return factor * 4.0 / math.sqrt(TOKENS)


def first_draw(key, shape, factor):
    return grad_size(factor) * jnp.clip(jax.random.normal(key, shape, jnp.float32), -4.0, 4.0)


def second_draw(key, shape, factor):
    spread = jax.random.uniform(key, shape, jnp.float32, 0.0, math.log(4.0))
    return grad_size(factor) ** 2 * jnp.exp(spread)


def steady_first(key, shape, magnitude):
    return magnitude * jnp.clip(jax.random.normal(key, shape, jnp.float32), -4.0, 4.0)


def steady_second(key, shape, magnitude):
    spread = jax.random.uniform(key, shape, jnp.float32, 0.0, math.log(4.0))
    return magnitude ** 2 * jnp.exp(spread)


def draw_first_qkv(key, part):
    key = jax.random.fold_in(key, 11)
    return first_draw(key, (3, D, D), 1.0)


def draw_first_proj(key, part):
    key = jax.random.fold_in(key, 12)
    return first_draw(key, (D, D), 0.5)


def draw_first_up(key, part):
    key = jax.random.fold_in(key, 13)
    return first_draw(key, (D, FF), 1.0)


def draw_first_down(key, part):
    key = jax.random.fold_in(key, 14)
    return first_draw(key, (FF, D), 1.0)


def draw_first_norms(key, part):
    key = jax.random.fold_in(key, 15)
    return steady_first(key, (4, D), 2.0)


def draw_second_qkv(key, part):
    key = jax.random.fold_in(key, 21)
    return second_draw(key, (3, D, D), 1.0)


def draw_second_proj(key, part):
    key = jax.random.fold_in(key, 22)
    return steady_second(key, (D, D), 0.2)


def draw_second_up(key, part):
    key = jax.random.fold_in(key, 23)
    return second_draw(key, (D, FF), 1.0)


def draw_second_down(key, part):
    key = jax.random.fold_in(key, 24)
    return second_draw(key, (FF, D), 1.0)


def draw_second_norms(key, part):
    key = jax.random.fold_in(key, 25)
    return steady_second(key, (4, D), 2.0)


def level_of(rng, shape, pieces, low, top_value):
    gain = 1.0
    for dim, blocks in pieces:
        steps = jax.random.uniform(jax.random.fold_in(jax.random.fold_in(rng, 6), dim), (blocks,), jnp.float32, low / len(pieces), top_value / len(pieces))
        gain = gain * jnp.repeat(jnp.exp(steps), shape[dim] // blocks).reshape((-1,) + (1,) * (len(shape) - 1 - dim))
    return gain


def scatter_about(stream_key, shape, scale, reach, cuts=(), kind=jnp.bfloat16):
    array = jax.random.normal(stream_key, shape, jnp.float32) * scale
    if len(cuts) > 0:
        array = level_of(stream_key, shape, cuts, -0.22, 0.18) * array
    return jnp.clip(array, min=-reach, max=reach).astype(kind)


def setup_inputs(seed: int = 0) -> dict:
    keys = jax.random.split(jax.random.key(seed), 20)
    tokens = scatter_about(keys[0], (TOKENS, D), 1.0, 6.0, ((0, 32),), jnp.float32)
    teacher = scatter_about(keys[1], (TOKENS, D), 1.0, 6.0, ((0, 32),), jnp.float32)
    segments = draw_segments(jax.random.fold_in(keys[19], 71), 0)
    live_mask = draw_live_mask(jax.random.fold_in(keys[19], 71), 0)
    weight_qkv = scatter_about(keys[4], (3, D, D), D ** -0.5, 0.1875, ((1, 8), (2, 4)), jnp.float32)
    weight_proj = scatter_about(keys[5], (D, D), (D // 8) ** -0.5, 0.5, ((0, 4), (1, 8)), jnp.float32)
    weight_up = scatter_about(keys[6], (D, FF), D ** -0.5, 0.1875, ((0, 8), (1, 4)), jnp.float32)
    weight_down = scatter_about(keys[7], (FF, D), FF ** -0.5, 0.09375, ((0, 4), (1, 8)), jnp.float32)
    norm_params = draw_norm_params(jax.random.fold_in(keys[19], 71), 0)
    first_qkv = draw_first_qkv(jax.random.fold_in(keys[19], 71), 0)
    first_proj = draw_first_proj(jax.random.fold_in(keys[19], 71), 0)
    first_up = draw_first_up(jax.random.fold_in(keys[19], 71), 0)
    first_down = draw_first_down(jax.random.fold_in(keys[19], 71), 0)
    first_norms = draw_first_norms(jax.random.fold_in(keys[19], 71), 0)
    second_qkv = draw_second_qkv(jax.random.fold_in(keys[19], 71), 0)
    second_proj = draw_second_proj(jax.random.fold_in(keys[19], 71), 0)
    second_up = draw_second_up(jax.random.fold_in(keys[19], 71), 0)
    second_down = draw_second_down(jax.random.fold_in(keys[19], 71), 0)
    second_norms = draw_second_norms(jax.random.fold_in(keys[19], 71), 0)
    return {"tokens": tokens, "teacher": teacher, "segments": segments, "live_mask": live_mask, "weight_qkv": weight_qkv, "weight_proj": weight_proj, "weight_up": weight_up, "weight_down": weight_down, "norm_params": norm_params, "first_qkv": first_qkv, "first_proj": first_proj, "first_up": first_up, "first_down": first_down, "first_norms": first_norms, "second_qkv": second_qkv, "second_proj": second_proj, "second_up": second_up, "second_down": second_down, "second_norms": second_norms}


@jax.custom_vjp
def low(v):
    return lax.optimization_barrier(v.astype(jnp.bfloat16)).astype(jnp.float32)

@jax.custom_vjp
def low_back(v):
    return v

def low_keep(v):
    return (low(v), None)

def low_pass(kept, grad):
    return (grad,)

def back_keep(v):
    return (v, None)

def back_low(kept, grad):
    return (low(grad),)
low.defvjp(low_keep, low_pass)
low_back.defvjp(back_keep, back_low)
highest = lax.Precision.HIGHEST
layer_eps = 1e-06
adam_eps = 1e-08
learn_rate = 0.03
norm_rate = 0.25
moment_decay = 0.5
weight_decay = 0.05

def layer_norm(values, gain_row, bias_row):
    average = lax.optimization_barrier(jnp.mean(values, axis=-1, keepdims=True))
    centred = values - average
    variance = lax.optimization_barrier(jnp.mean(centred * centred, axis=-1, keepdims=True))
    return centred * lax.rsqrt(variance + layer_eps) * gain_row + bias_row

def attend(queries, key_rows, value_rows, query_segments, key_segments, key_live, row_start):
    scores = jnp.einsum('qhe,khe->hqk', queries, key_rows, precision=highest) * HEAD_DIM ** (-0.5)
    scores = low_back(scores)
    row_ids = row_start + jnp.arange(queries.shape[0], dtype=jnp.int32)
    col_ids = jnp.arange(key_rows.shape[0], dtype=jnp.int32)
    allowed = (query_segments[:, None] == key_segments[None, :]) & (key_live[None, :] == 1) | (row_ids[:, None] == col_ids[None, :])
    scores = jnp.where(allowed[None], scores, -jnp.inf)
    largest = lax.optimization_barrier(jnp.max(scores, axis=-1, keepdims=True))
    weights = jnp.exp(scores - largest)
    probabilities = low(weights / lax.optimization_barrier(jnp.sum(weights, axis=-1, keepdims=True)))
    return jnp.einsum('hqk,khe->qhe', probabilities, value_rows, precision=highest)

def group_loss(tokens, teacher, segments, live_mask, weight_qkv, weight_proj, weight_up, weight_down, norm_params):
    normed_one = low(layer_norm(tokens, norm_params[0], norm_params[1]))
    projected = low_back(low(jnp.einsum('td,kde->kte', normed_one, weight_qkv, precision=highest)))
    heads = projected.reshape(3, GROUP, HEADS, HEAD_DIM)
    block_count = GROUP // QBLOCK
    query_blocks = heads[0].reshape(block_count, QBLOCK, HEADS, HEAD_DIM)
    segment_blocks = segments.reshape(block_count, QBLOCK)
    block_starts = jnp.arange(block_count, dtype=jnp.int32) * QBLOCK

    def one_block(item):
        return attend(item[0], heads[1], heads[2], item[1], segments, live_mask, item[2])
    mixed = lax.map(jax.checkpoint(one_block), (query_blocks, segment_blocks, block_starts))
    mixed = low_back(low(mixed.reshape(GROUP, D)))
    residual = tokens + low_back(jnp.dot(mixed, weight_proj, precision=highest))
    normed_two = low(layer_norm(residual, norm_params[2], norm_params[3]))
    hidden = low_back(jnp.dot(normed_two, weight_up, precision=highest))
    active = low(jax.nn.gelu(hidden, approximate=False))
    output = residual + low_back(jnp.dot(active, weight_down, precision=highest))
    error = output - teacher
    return jnp.sum(live_mask.astype(jnp.float32)[:, None] * error * error)

def adam_step(weight, gradient, momentum, variance, decay_rate, rate):
    momentum = moment_decay * momentum + (1.0 - moment_decay) * gradient
    variance = moment_decay * variance + (1.0 - moment_decay) * gradient * gradient
    correction = 1.0 - moment_decay ** STEP
    direction = momentum / correction / (jnp.sqrt(variance / correction) + adam_eps)
    return (weight - rate * (direction + decay_rate * weight), momentum, variance)

def reference(tokens, teacher, segments, live_mask, weight_qkv, weight_proj, weight_up, weight_down, norm_params, first_qkv, first_proj, first_up, first_down, first_norms, second_qkv, second_proj, second_up, second_down, second_norms):
    live_count = jnp.sum(live_mask.astype(jnp.float32))

    def forward(token_rows, qkv_matrix, proj_matrix, up_matrix, down_matrix, norm_rows):
        low_qkv = low(qkv_matrix)
        low_proj = low(proj_matrix)
        low_up = low(up_matrix)
        low_down = low(down_matrix)
        stacked = (token_rows.reshape(N_ROW, GROUP, D), teacher.reshape(N_ROW, GROUP, D), segments.reshape(N_ROW, GROUP), live_mask.reshape(N_ROW, GROUP))

        def step_group(running, item):
            return (running + group_loss(item[0], item[1], item[2], item[3], low_qkv, low_proj, low_up, low_down, norm_rows), None)
        running, ignored = lax.scan(step_group, jnp.zeros((), jnp.float32), stacked)
        return running
    loss_sum, pullback = jax.vjp(forward, tokens, weight_qkv, weight_proj, weight_up, weight_down, norm_params)
    gradients = pullback(jnp.ones((), jnp.float32) / live_count)
    loss_value = loss_sum / live_count
    new_qkv = adam_step(weight_qkv, gradients[1], first_qkv, second_qkv, weight_decay, learn_rate)
    new_proj = adam_step(weight_proj, gradients[2], first_proj, second_proj, weight_decay, learn_rate)
    new_up = adam_step(weight_up, gradients[3], first_up, second_up, weight_decay, learn_rate)
    new_down = adam_step(weight_down, gradients[4], first_down, second_down, weight_decay, learn_rate)
    new_norms = adam_step(norm_params, gradients[5], first_norms, second_norms, 0.0, norm_rate)
    return (loss_value, gradients[0], new_qkv[0], new_proj[0], new_up[0], new_down[0], new_norms[0], new_qkv[1], new_proj[1], new_up[1], new_down[1], new_norms[1], new_qkv[2], new_proj[2], new_up[2], new_down[2], new_norms[2])
```

```python
import functools

import jax
import jax.numpy as jnp
from jax import lax
from jax.experimental import pallas as pl
from jax.experimental.pallas import tpu as pltpu
from jax.sharding import PartitionSpec as P

HEAD_DIM = 64
PATCHES = 577
STEP = 10
WINDOW = 640
QROWS = 128
N_Z = 4
N_CORE = 2

layer_eps = 1e-06
adam_eps = 1e-08
learn_rate = 0.03
norm_rate = 0.25
moment_decay = 0.5
weight_decay = 0.05

bf16 = jnp.bfloat16
f32 = jnp.float32


def norm_forward(values, gain_row, bias_row):
    average = jnp.mean(values, axis=-1, keepdims=True)
    centred = values - average
    variance = jnp.mean(centred * centred, axis=-1, keepdims=True)
    inverse = lax.rsqrt(variance + layer_eps)
    scaled = centred * inverse
    return (scaled * gain_row + bias_row, scaled, inverse)


def norm_backward(upstream, scaled, inverse, gain_row):
    weighted = upstream * gain_row
    return inverse * (
        weighted
        - jnp.mean(weighted, axis=-1, keepdims=True)
        - scaled * jnp.mean(weighted * scaled, axis=-1, keepdims=True)
    )


def gelu_slope(hidden):
    return (
        0.5 * (1.0 + lax.erf(hidden * 0.7071067811865476))
        + hidden * jnp.exp(-0.5 * hidden * hidden) * 0.3989422804014327
    )


def adam_step(weight, gradient, momentum, variance, decay_rate, rate):
    momentum = moment_decay * momentum + (1.0 - moment_decay) * gradient
    variance = moment_decay * variance + (1.0 - moment_decay) * gradient * gradient
    correction = 1.0 - moment_decay**STEP
    direction = momentum / correction / (jnp.sqrt(variance / correction) + adam_eps)
    return (weight - rate * (direction + decay_rate * weight), momentum, variance)


def dot(left, right, left_dim, right_dim):
    return lax.dot_general(
        left, right, (((left_dim,), (right_dim,)), ((), ())), preferred_element_type=f32
    )


def head_lanes(width, head):
    lanes = lax.broadcasted_iota(jnp.int32, (1, width), 1)
    return (lanes >= head * HEAD_DIM) & (lanes < (head + 1) * HEAD_DIM)


def attend_weights(q_part, k_all, bias, row_start, rows_in):
    scores = dot(q_part, k_all, 1, 1) * HEAD_DIM ** (-0.5)
    rows, window = scores.shape
    row_ids = row_start + lax.broadcasted_iota(jnp.int32, (rows, window), 0)
    col_ids = lax.broadcasted_iota(jnp.int32, (rows, window), 1)
    scores = jnp.where(row_ids == col_ids, scores, scores + bias)
    weights = jnp.exp(scores - jnp.max(scores, axis=-1, keepdims=True))
    totals = jnp.sum(weights, axis=-1, keepdims=True)
    return weights * jnp.where(rows_in, 1.0 / totals, 0.0)


def rows_inside(rows, row_start, first):
    ids = row_start + lax.broadcasted_iota(jnp.int32, (rows, 1), 0)
    return (ids >= first) & (ids < first + PATCHES)


def attend_forward_kernel(lanes, starts, firsts, bias_ref, q_ref, k_ref, v_ref, out_ref):
    image = pl.program_id(0)

    @pl.when(image == 0)
    def _():
        out_ref[...] = v_ref[...]

    start = pl.multiple_of(starts[image], 16)
    first = firsts[image]
    bias = bias_ref[0]
    for tile in range(q_ref.shape[1] // lanes):
        cols = slice(tile * lanes, (tile + 1) * lanes)
        k_all = k_ref[pl.ds(start, WINDOW), cols]
        v_all = v_ref[pl.ds(start, WINDOW), cols]
        for row in range(0, WINDOW, QROWS):
            at = pl.ds(pl.multiple_of(start + row, 16), QROWS)
            q_part = q_ref[at, cols]
            inside = rows_inside(QROWS, row, first)
            mixed = None
            for head in range(lanes // HEAD_DIM):
                mine = head_lanes(lanes, head)
                q_head = jnp.where(mine, q_part, jnp.zeros_like(q_part))
                weights = attend_weights(q_head, k_all, bias, row, inside).astype(bf16)
                part = dot(weights, v_all, 1, 0)
                mixed = part if mixed is None else jnp.where(mine, part, mixed)
            out_ref[at, cols] = jnp.where(inside, mixed.astype(bf16), out_ref[at, cols])


def attend_backward_kernel(
    lanes, starts, firsts, bias_ref, q_ref, k_ref, v_ref, go_ref, out_ref, p_ref, s_ref
):
    image = pl.program_id(0)
    width = q_ref.shape[1]

    @pl.when(image == 0)
    def _():
        out_ref[:, : 2 * width] = jnp.zeros((out_ref.shape[0], 2 * width), bf16)
        out_ref[:, 2 * width :] = go_ref[...]

    start = pl.multiple_of(starts[image], 16)
    first = firsts[image]
    bias = bias_ref[0]
    whole = pl.ds(start, WINDOW)
    inside_all = rows_inside(WINDOW, 0, first)
    for tile in range(width // lanes):
        cols = slice(tile * lanes, (tile + 1) * lanes)
        k_cols = slice(width + tile * lanes, width + (tile + 1) * lanes)
        v_cols = slice(2 * width + tile * lanes, 2 * width + (tile + 1) * lanes)
        k_all = k_ref[whole, cols]
        v_all = v_ref[whole, cols]
        q_all = q_ref[whole, cols]
        go_all = go_ref[whole, cols]
        key_grad = None
        value_grad = None
        for head in range(lanes // HEAD_DIM):
            mine = head_lanes(lanes, head)
            for row in range(0, WINDOW, QROWS):
                at = pl.ds(pl.multiple_of(start + row, 16), QROWS)
                q_part = q_ref[at, cols]
                go_part = go_ref[at, cols]
                inside = rows_inside(QROWS, row, first)
                q_head = jnp.where(mine, q_part, jnp.zeros_like(q_part))
                go_head = jnp.where(mine, go_part, jnp.zeros_like(go_part))
                weights = attend_weights(q_head, k_all, bias, row, inside)
                weight_grad = dot(go_head, v_all, 1, 1)
                product = weights * weight_grad
                score_grad = (
                    product - weights * jnp.sum(product, axis=-1, keepdims=True)
                ).astype(bf16)
                p_ref[row : row + QROWS, :] = weights.astype(bf16)
                s_ref[row : row + QROWS, :] = score_grad
                query_grad = (dot(score_grad, k_all, 1, 0) * HEAD_DIM ** (-0.5)).astype(bf16)
                out_ref[at, cols] = jnp.where(inside & mine, query_grad, out_ref[at, cols])
            q_mine = jnp.where(mine, q_all, jnp.zeros_like(q_all))
            go_mine = jnp.where(mine, go_all, jnp.zeros_like(go_all))
            key_part = dot(q_mine, s_ref[...], 0, 0)
            value_part = dot(go_mine, p_ref[...], 0, 0)
            key_grad = key_part if key_grad is None else key_grad + key_part
            value_grad = value_part if value_grad is None else value_grad + value_part
        key_rows = (key_grad.T * HEAD_DIM ** (-0.5)).astype(bf16)
        value_rows = value_grad.T.astype(bf16)
        out_ref[whole, k_cols] = jnp.where(inside_all, key_rows, out_ref[whole, k_cols])
        out_ref[whole, v_cols] = jnp.where(inside_all, value_rows, out_ref[whole, v_cols])


def qkv_operands(projected, width):
    group_rows = projected.shape[0]
    if width % 128 == 0:
        specs = [
            pl.BlockSpec((group_rows, width), functools.partial(lambda n, i, *_: (0, n), n))
            for n in range(3)
        ]
        return [projected] * 3, specs
    parts = [projected[:, n * width : (n + 1) * width] for n in range(3)]
    return parts, [pl.BlockSpec((group_rows, width), lambda i, *_: (0, 0))] * 3


def attend_call(kernel, projected, extra, out_width, scratch, geometry, matmuls, name):
    starts, firsts, bias = geometry
    group_rows = projected.shape[0]
    width = projected.shape[1] // 3
    images = starts.shape[0]
    operands, specs = qkv_operands(projected, width)
    work = images * (width // HEAD_DIM) * WINDOW * WINDOW
    return pl.pallas_call(
        functools.partial(kernel, min(128, width)),
        grid_spec=pltpu.PrefetchScalarGridSpec(
            num_scalar_prefetch=2,
            grid=(images,),
            in_specs=[pl.BlockSpec((1, 1, WINDOW), lambda i, *_: (i, 0, 0))]
            + specs
            + [pl.BlockSpec((group_rows, width), lambda i, *_: (0, 0)) for _ in extra],
            out_specs=pl.BlockSpec((group_rows, out_width), lambda i, *_: (0, 0)),
            scratch_shapes=scratch,
        ),
        out_shape=jax.ShapeDtypeStruct((group_rows, out_width), bf16),
        compiler_params=pltpu.CompilerParams(vmem_limit_bytes=48 * 1024 * 1024),
        cost_estimate=pl.CostEstimate(
            flops=8 * matmuls * work * HEAD_DIM,
            bytes_accessed=2 * group_rows * (3 * width + out_width),
            transcendentals=work,
        ),
        name=name,
    )(starts, firsts, bias, *operands, *extra)


def attend_geometry(segments, live_mask):
    group_rows = segments.shape[0]
    images = group_rows // PATCHES
    positions = jnp.arange(group_rows, dtype=jnp.int32)
    numbers = jnp.arange(images, dtype=jnp.int32)
    begin = jnp.min(
        jnp.where(segments[None, :] == numbers[:, None], positions[None, :], group_rows - PATCHES),
        axis=1,
    )
    starts = jnp.minimum(begin // 16 * 16, group_rows - WINDOW)
    firsts = begin - starts
    visible = (segments[None, :] == numbers[:, None]) & (live_mask[None, :] == 1)
    bias = jnp.where(visible, 0.0, -1e30).astype(f32)
    bias = jnp.stack(
        [lax.dynamic_slice_in_dim(bias[n], starts[n], WINDOW, 0) for n in range(images)]
    )
    return starts, firsts, bias[:, None, :]


def local(
    n_row,
    n_col,
    tokens,
    teacher,
    segments,
    live_mask,
    weight_qkv,
    weight_proj,
    weight_up,
    weight_down,
    norm_params,
    first_qkv,
    first_proj,
    first_up,
    first_down,
    first_norms,
    second_qkv,
    second_proj,
    second_up,
    second_down,
    second_norms,
):
    n_x = n_row // N_Z
    n_y = n_col // N_CORE
    row = lax.axis_index("row")
    col = lax.axis_index("col")
    z_at, x_at = row // n_x, row % n_x
    y_at, core_at = col // N_CORE, col % N_CORE
    rows = tokens.shape[0]
    group_rows = segments.shape[0]
    slab = weight_qkv.shape[1]
    width = weight_qkv.shape[2]
    model = tokens.shape[1]

    def send_row(value, dz, dx):
        perm = [
            (z * n_x + x, (z + dz) % N_Z * n_x + (x + dx) % n_x)
            for z in range(N_Z)
            for x in range(n_x)
        ]
        return lax.ppermute(value, "row", perm)

    def send_col(value, dy, dc):
        perm = [
            (y * N_CORE + c, (y + dy) % n_y * N_CORE + (c + dc) % N_CORE)
            for y in range(n_y)
            for c in range(N_CORE)
        ]
        return lax.ppermute(value, "col", perm)

    def reduce_all(value, axis, size):
        step = 1
        while step < size:
            value = value + lax.ppermute(value, axis, [(i, i ^ step) for i in range(size)])
            step *= 2
        return value

    def relative(value):
        lead = value.shape[:-1]
        value = value.reshape(lead + (N_Z, n_x, slab))
        value = jnp.roll(value, (-z_at, -x_at), axis=(-3, -2))
        return jnp.swapaxes(value, -3, -2).reshape(lead + (model,))

    def absolute(value):
        lead = value.shape[:-1]
        value = jnp.swapaxes(value.reshape(lead + (n_x, N_Z, slab)), -3, -2)
        return jnp.roll(value, (z_at, x_at), axis=(-3, -2)).reshape(lead + (model,))

    def place(dy, dc):
        return ((y_at + dy) % n_y * N_CORE + (core_at + dc) % N_CORE) * rows

    offsets = [(dc, dy) for dc in range(N_CORE) for dy in range(n_y)]

    def gather_z(shard):
        return jnp.concatenate([shard] + [send_row(shard, -k, 0) for k in range(1, N_Z)], axis=0)

    def gather_x(part):
        return jnp.concatenate([part] + [send_row(part, 0, -k) for k in range(1, n_x)], axis=0)

    def gather_y(part):
        return [part] + [send_col(part, -k, 0) for k in range(1, n_y)]

    def gather_core(parts):
        return parts + [send_col(part, 0, -1) for part in parts]

    def reduce_core(parts):
        return [
            parts[dy] + send_col(parts[n_y + dy].astype(bf16), 0, 1).astype(f32)
            for dy in range(n_y)
        ]

    def reduce_y(parts):
        total = parts[0]
        for k in range(1, n_y):
            total = total + send_col(parts[k].astype(bf16), k, 0).astype(f32)
        return total

    def reduce_x(part):
        depth = part.shape[0] // n_x
        total = part[:depth]
        for k in range(1, n_x):
            piece = part[k * depth : (k + 1) * depth].astype(bf16)
            total = total + send_row(piece, 0, k).astype(f32)
        return total

    def reduce_z(part):
        depth = part.shape[0] // N_Z
        total = part[:depth]
        for k in range(1, N_Z):
            piece = part[k * depth : (k + 1) * depth].astype(bf16)
            total = total + send_row(piece, k, 0).astype(f32)
        return total

    live_count = reduce_all(jnp.sum(live_mask.astype(f32)), "row", n_row)
    own_live = lax.dynamic_slice_in_dim(live_mask, col * rows, rows, 0).astype(f32)
    geometry = attend_geometry(segments, live_mask)

    shard_qkv = jnp.transpose(weight_qkv.astype(bf16), (1, 0, 2)).reshape(slab, 3 * width)
    shard_a = jnp.concatenate([weight_proj.T, weight_up], axis=1).astype(bf16)
    shard_b = weight_down.T.astype(bf16)

    params = relative(norm_params)
    tokens = relative(tokens)
    teacher = relative(teacher)

    normed_one, scaled_one, inverse_one = norm_forward(tokens, params[0], params[1])
    low_one = normed_one.astype(bf16)

    near_qkv = gather_z(shard_qkv)
    blocks_one = gather_core(gather_y(low_one))
    full_qkv = gather_x(near_qkv)
    shard_a, shard_b, near_qkv = lax.optimization_barrier((shard_a, shard_b, near_qkv))
    full_a = gather_core(gather_y(gather_x(gather_z(shard_a))))
    full_b = gather_core([gather_x(part) for part in gather_y(gather_z(shard_b))])
    full_proj = [part[:, :width] for part in full_a]
    full_up = [part[:, width:] for part in full_a]

    group_one = jnp.zeros((group_rows, model), bf16)
    for (dc, dy), block in zip(offsets, blocks_one):
        group_one = lax.dynamic_update_slice_in_dim(group_one, block, place(dy, dc), 0)
    projected = dot(group_one, full_qkv, 1, 0).astype(bf16)
    mixed = attend_call(
        attend_forward_kernel, projected, [], width, [], geometry, 2, "attention_forward"
    )

    blocks_mixed = []
    for dc, dy in offsets:
        piece = lax.dynamic_slice_in_dim(mixed, place(-dy, -dc), rows, 0)
        blocks_mixed.append(piece if (dc, dy) == (0, 0) else send_col(piece, -dy, -dc))
    residual = tokens
    for block, part in zip(blocks_mixed, full_proj):
        residual = residual + dot(block, part, 1, 1)

    normed_two, scaled_two, inverse_two = norm_forward(residual, params[2], params[3])
    low_two = normed_two.astype(bf16)
    hidden = [dot(low_two, part, 1, 0) for part in full_up]
    active = [jax.nn.gelu(part, approximate=False).astype(bf16) for part in hidden]
    error = residual - teacher
    for block, part in zip(active, full_b):
        error = error + dot(block, part, 1, 1)
    loss_local = jnp.sum(own_live[:, None] * error * error)
    grad_output = 2.0 * own_live[:, None] * error / live_count
    grad_branch = grad_output.astype(bf16)

    grad_down = [dot(grad_branch, block, 0, 0) for block in active]
    grad_hidden = [
        (dot(grad_branch, part, 1, 0) * gelu_slope(block)).astype(bf16)
        for part, block in zip(full_b, hidden)
    ]
    grad_up = [dot(low_two, block, 0, 0) for block in grad_hidden]
    grad_two = 0.0
    for block, part in zip(grad_hidden, full_up):
        grad_two = grad_two + dot(block, part, 1, 1)
    grad_residual = grad_output + norm_backward(grad_two, scaled_two, inverse_two, params[2])
    grad_low = grad_residual.astype(bf16)

    grad_group = jnp.zeros((group_rows, width), bf16)
    for (dc, dy), part in zip(offsets, full_proj):
        piece = dot(grad_low, part, 1, 0).astype(bf16)
        piece = piece if (dc, dy) == (0, 0) else send_col(piece, dy, dc)
        grad_group = lax.dynamic_update_slice_in_dim(grad_group, piece, place(-dy, -dc), 0)
    grad_proj = [dot(grad_low, block, 0, 0) for block in blocks_mixed]

    grad_b = reduce_core(grad_down)
    depth = model // n_x
    grad_b = [reduce_x(part) for part in grad_b]
    grad_b = reduce_z(reduce_y(grad_b))
    grad_a = [jnp.concatenate(pair, axis=1) for pair in zip(grad_proj, grad_up)]
    grad_a = reduce_z(reduce_x(reduce_y(reduce_core(grad_a))))

    grad_projected = attend_call(
        attend_backward_kernel,
        projected,
        [grad_group],
        3 * width,
        [pltpu.VMEM((WINDOW, WINDOW), bf16)] * 2,
        geometry,
        5,
        "attention_backward",
    )

    grad_qkv = reduce_z(reduce_x(dot(group_one, grad_projected, 0, 0)))
    parts = [
        dot(
            lax.dynamic_slice_in_dim(grad_projected, place(dy, dc), rows, 0),
            full_qkv,
            1,
            1,
        )
        for dc, dy in offsets
    ]
    grad_one = reduce_y(reduce_core(parts))
    token_grad = grad_residual + norm_backward(grad_one, scaled_one, inverse_one, params[0])
    token_grad = absolute(token_grad)

    norm_local = absolute(
        jnp.stack(
            [
                jnp.sum(grad_one * scaled_one, axis=0),
                jnp.sum(grad_one, axis=0),
                jnp.sum(grad_two * scaled_two, axis=0),
                jnp.sum(grad_two, axis=0),
            ]
        )
    )
    sums = jnp.concatenate([norm_local, jnp.full((1, model), loss_local)], axis=0)
    sums = reduce_all(reduce_all(sums, "col", n_col), "row", n_row)
    loss_sum = sums[4, 0]

    grad_qkv = jnp.transpose(grad_qkv.reshape(slab, 3, width), (1, 0, 2))
    new_qkv = adam_step(weight_qkv, grad_qkv, first_qkv, second_qkv, weight_decay, learn_rate)
    new_proj = adam_step(
        weight_proj, grad_a[:, :width].T, first_proj, second_proj, weight_decay, learn_rate
    )
    new_up = adam_step(weight_up, grad_a[:, width:], first_up, second_up, weight_decay, learn_rate)
    new_down = adam_step(
        weight_down, grad_b.T, first_down, second_down, weight_decay, learn_rate
    )
    new_norms = adam_step(norm_params, sums[:4], first_norms, second_norms, 0.0, norm_rate)
    return (
        loss_sum / live_count,
        token_grad,
        new_qkv[0],
        new_proj[0],
        new_up[0],
        new_down[0],
        new_norms[0],
        new_qkv[1],
        new_proj[1],
        new_up[1],
        new_down[1],
        new_norms[1],
        new_qkv[2],
        new_proj[2],
        new_up[2],
        new_down[2],
        new_norms[2],
    )


def solution(mesh):
    matrices = (P(None, "row", "col"), P("col", "row"), P("row", "col"), P("col", "row"), P())
    tokens = P(("row", "col"), None)
    return jax.shard_map(
        functools.partial(local, mesh.shape["row"], mesh.shape["col"]),
        mesh=mesh,
        in_specs=(tokens, tokens, P("row"), P("row")) + matrices * 3,
        out_specs=(P(), tokens) + matrices * 3,
        check_vma=False,
    )
```

```python
import functools

import jax
import jax.numpy as jnp
from jax import lax
from jax.experimental import pallas as pl
from jax.experimental.pallas import tpu as pltpu
from jax.sharding import PartitionSpec as P

HEAD_DIM = 64
PATCHES = 577
STEP = 10
WINDOW = 640
QROWS = 320
N_Z = 4
N_CORE = 2

layer_eps = 1e-06
adam_eps = 1e-08
learn_rate = 0.03
norm_rate = 0.25
moment_decay = 0.5
weight_decay = 0.05

bf16 = jnp.bfloat16
f32 = jnp.float32


def norm_forward(values, gain_row, bias_row):
    average = jnp.mean(values, axis=-1, keepdims=True)
    centred = values - average
    variance = jnp.mean(centred * centred, axis=-1, keepdims=True)
    inverse = lax.rsqrt(variance + layer_eps)
    scaled = centred * inverse
    return (scaled * gain_row + bias_row, scaled, inverse)


def norm_backward(upstream, scaled, inverse, gain_row):
    weighted = upstream * gain_row
    return inverse * (
        weighted
        - jnp.mean(weighted, axis=-1, keepdims=True)
        - scaled * jnp.mean(weighted * scaled, axis=-1, keepdims=True)
    )


def gelu_slope(hidden):
    return (
        0.5 * (1.0 + lax.erf(hidden * 0.7071067811865476))
        + hidden * jnp.exp(-0.5 * hidden * hidden) * 0.3989422804014327
    )


def adam_step(weight, gradient, momentum, variance, decay_rate, rate):
    momentum = moment_decay * momentum + (1.0 - moment_decay) * gradient
    variance = moment_decay * variance + (1.0 - moment_decay) * gradient * gradient
    correction = 1.0 - moment_decay**STEP
    direction = momentum / correction / (jnp.sqrt(variance / correction) + adam_eps)
    return (weight - rate * (direction + decay_rate * weight), momentum, variance)


def dot(left, right, left_dim, right_dim):
    return lax.dot_general(
        left, right, (((left_dim,), (right_dim,)), ((), ())), preferred_element_type=f32
    )


def head_lanes(width, head):
    lanes = lax.broadcasted_iota(jnp.int32, (1, width), 1)
    return (lanes >= head * HEAD_DIM) & (lanes < (head + 1) * HEAD_DIM)


def attend_weights(q_part, k_all, bias, row_start, rows_in):
    scores = dot(q_part, k_all, 1, 1) * HEAD_DIM ** (-0.5)
    rows, window = scores.shape
    row_ids = row_start + lax.broadcasted_iota(jnp.int32, (rows, window), 0)
    col_ids = lax.broadcasted_iota(jnp.int32, (rows, window), 1)
    scores = jnp.where(row_ids == col_ids, scores, scores + bias)
    weights = jnp.exp(scores - jnp.max(scores, axis=-1, keepdims=True))
    totals = jnp.sum(weights, axis=-1, keepdims=True)
    return weights * jnp.where(rows_in, 1.0 / totals, 0.0)


def rows_inside(rows, row_start, first):
    ids = row_start + lax.broadcasted_iota(jnp.int32, (rows, 1), 0)
    return (ids >= first) & (ids < first + PATCHES)


def attend_forward_kernel(lanes, starts, firsts, bias_ref, q_ref, k_ref, v_ref, out_ref):
    image = pl.program_id(0)

    @pl.when(image == 0)
    def _():
        out_ref[...] = v_ref[...]

    start = pl.multiple_of(starts[image], 16)
    first = firsts[image]
    bias = bias_ref[0]
    for tile in range(q_ref.shape[1] // lanes):
        cols = slice(tile * lanes, (tile + 1) * lanes)
        k_all = k_ref[pl.ds(start, WINDOW), cols]
        v_all = v_ref[pl.ds(start, WINDOW), cols]
        for row in range(0, WINDOW, QROWS):
            at = pl.ds(pl.multiple_of(start + row, 16), QROWS)
            q_part = q_ref[at, cols]
            inside = rows_inside(QROWS, row, first)
            mixed = None
            for head in range(lanes // HEAD_DIM):
                mine = head_lanes(lanes, head)
                q_head = jnp.where(mine, q_part, jnp.zeros_like(q_part))
                weights = attend_weights(q_head, k_all, bias, row, inside).astype(bf16)
                part = dot(weights, v_all, 1, 0)
                mixed = part if mixed is None else jnp.where(mine, part, mixed)
            out_ref[at, cols] = jnp.where(inside, mixed.astype(bf16), out_ref[at, cols])


def attend_backward_kernel(
    lanes, starts, firsts, bias_ref, q_ref, k_ref, v_ref, go_ref, out_ref, p_ref, s_ref
):
    image = pl.program_id(0)
    width = q_ref.shape[1]

    @pl.when(image == 0)
    def _():
        out_ref[:, : 2 * width] = jnp.zeros((out_ref.shape[0], 2 * width), bf16)
        out_ref[:, 2 * width :] = go_ref[...]

    start = pl.multiple_of(starts[image], 16)
    first = firsts[image]
    bias = bias_ref[0]
    whole = pl.ds(start, WINDOW)
    inside_all = rows_inside(WINDOW, 0, first)
    for tile in range(width // lanes):
        cols = slice(tile * lanes, (tile + 1) * lanes)
        k_cols = slice(width + tile * lanes, width + (tile + 1) * lanes)
        v_cols = slice(2 * width + tile * lanes, 2 * width + (tile + 1) * lanes)
        k_all = k_ref[whole, cols]
        v_all = v_ref[whole, cols]
        q_all = q_ref[whole, cols]
        go_all = go_ref[whole, cols]
        key_grad = None
        value_grad = None
        for head in range(lanes // HEAD_DIM):
            mine = head_lanes(lanes, head)
            for row in range(0, WINDOW, QROWS):
                at = pl.ds(pl.multiple_of(start + row, 16), QROWS)
                q_part = q_ref[at, cols]
                go_part = go_ref[at, cols]
                inside = rows_inside(QROWS, row, first)
                q_head = jnp.where(mine, q_part, jnp.zeros_like(q_part))
                go_head = jnp.where(mine, go_part, jnp.zeros_like(go_part))
                weights = attend_weights(q_head, k_all, bias, row, inside)
                weight_grad = dot(go_head, v_all, 1, 1)
                product = weights * weight_grad
                score_grad = (
                    product - weights * jnp.sum(product, axis=-1, keepdims=True)
                ).astype(bf16)
                p_ref[row : row + QROWS, :] = weights.astype(bf16)
                s_ref[row : row + QROWS, :] = score_grad
                query_grad = (dot(score_grad, k_all, 1, 0) * HEAD_DIM ** (-0.5)).astype(bf16)
                out_ref[at, cols] = jnp.where(inside & mine, query_grad, out_ref[at, cols])
            q_mine = jnp.where(mine, q_all, jnp.zeros_like(q_all))
            go_mine = jnp.where(mine, go_all, jnp.zeros_like(go_all))
            key_part = dot(q_mine, s_ref[...], 0, 0)
            value_part = dot(go_mine, p_ref[...], 0, 0)
            key_grad = key_part if key_grad is None else key_grad + key_part
            value_grad = value_part if value_grad is None else value_grad + value_part
        key_rows = (key_grad.T * HEAD_DIM ** (-0.5)).astype(bf16)
        value_rows = value_grad.T.astype(bf16)
        out_ref[whole, k_cols] = jnp.where(inside_all, key_rows, out_ref[whole, k_cols])
        out_ref[whole, v_cols] = jnp.where(inside_all, value_rows, out_ref[whole, v_cols])


def qkv_operands(projected, width):
    group_rows = projected.shape[0]
    if width % 128 == 0:
        specs = [
            pl.BlockSpec((group_rows, width), functools.partial(lambda n, i, *_: (0, n), n))
            for n in range(3)
        ]
        return [projected] * 3, specs
    parts = [projected[:, n * width : (n + 1) * width] for n in range(3)]
    return parts, [pl.BlockSpec((group_rows, width), lambda i, *_: (0, 0))] * 3


def attend_call(kernel, projected, extra, out_width, scratch, geometry, matmuls, name):
    starts, firsts, bias = geometry
    group_rows = projected.shape[0]
    width = projected.shape[1] // 3
    images = starts.shape[0]
    operands, specs = qkv_operands(projected, width)
    work = images * (width // HEAD_DIM) * WINDOW * WINDOW
    return pl.pallas_call(
        functools.partial(kernel, min(128, width)),
        grid_spec=pltpu.PrefetchScalarGridSpec(
            num_scalar_prefetch=2,
            grid=(images,),
            in_specs=[pl.BlockSpec((1, 1, WINDOW), lambda i, *_: (i, 0, 0))]
            + specs
            + [pl.BlockSpec((group_rows, width), lambda i, *_: (0, 0)) for _ in extra],
            out_specs=pl.BlockSpec((group_rows, out_width), lambda i, *_: (0, 0)),
            scratch_shapes=scratch,
        ),
        out_shape=jax.ShapeDtypeStruct((group_rows, out_width), bf16),
        compiler_params=pltpu.CompilerParams(vmem_limit_bytes=48 * 1024 * 1024),
        cost_estimate=pl.CostEstimate(
            flops=2 * matmuls * work * HEAD_DIM,
            bytes_accessed=2 * group_rows * (3 * width + out_width),
            transcendentals=0,
        ),
        name=name,
    )(starts, firsts, bias, *operands, *extra)


def attend_geometry(segments, live_mask):
    group_rows = segments.shape[0]
    images = group_rows // PATCHES
    positions = jnp.arange(group_rows, dtype=jnp.int32)
    numbers = jnp.arange(images, dtype=jnp.int32)
    begin = jnp.min(
        jnp.where(segments[None, :] == numbers[:, None], positions[None, :], group_rows - PATCHES),
        axis=1,
    )
    starts = jnp.minimum(begin // 16 * 16, group_rows - WINDOW)
    firsts = begin - starts
    visible = (segments[None, :] == numbers[:, None]) & (live_mask[None, :] == 1)
    bias = jnp.where(visible, 0.0, -1e30).astype(f32)
    bias = jnp.stack(
        [lax.dynamic_slice_in_dim(bias[n], starts[n], WINDOW, 0) for n in range(images)]
    )
    return starts, firsts, bias[:, None, :]


def plain_call(kernel, out_shape, *operands, grid=(), in_specs=None, out_specs=None, scratch=(), scalars=(), name=None):
    params = pltpu.CompilerParams(vmem_limit_bytes=48 * 1024 * 1024)
    if in_specs is None:
        in_specs = [pl.BlockSpec(a.shape, functools.partial(lambda n, *_: (0,) * n, a.ndim)) for a in operands]
    if out_specs is None:
        out_specs = jax.tree.map(
            lambda s: pl.BlockSpec(s.shape, functools.partial(lambda n, *_: (0,) * n, len(s.shape))), out_shape
        )
    return pl.pallas_call(
        kernel,
        grid_spec=pltpu.PrefetchScalarGridSpec(
            num_scalar_prefetch=len(scalars),
            grid=grid,
            in_specs=in_specs,
            out_specs=out_specs,
            scratch_shapes=list(scratch),
        ),
        out_shape=out_shape,
        compiler_params=params,
        name=name,
    )(*scalars, *operands)


def shaped(shape, dtype):
    return jax.ShapeDtypeStruct(tuple(shape), dtype)


def row_blocks(rows, *widths):
    return [pl.BlockSpec((rows, w), lambda i, *_: (i, 0)) for w in widths]


def fixed(shape):
    return pl.BlockSpec(tuple(shape), functools.partial(lambda n, *_: (0,) * n, len(shape)))


def stack(pieces):
    if len(pieces) == 1:
        return pieces[0]
    depth, width = pieces[0].shape

    def kernel(*refs):
        for n, ref in enumerate(refs[:-1]):
            refs[-1][n * depth : (n + 1) * depth, :] = ref[...]

    return plain_call(kernel, shaped((len(pieces) * depth, width), pieces[0].dtype), *pieces, name="stack")


def source_block(at_ref, dx, kz, n_x):
    z = lax.rem(at_ref[0] + kz, N_Z)
    x = lax.rem(at_ref[1] + dx, n_x)
    return z * n_x + x


def enter_kernel(n_x, slab, at_ref, tok_ref, tea_ref, par_ref, tok_out, tea_out, par_out, low_out):
    for dx in range(n_x):
        for kz in range(N_Z):
            here = slice((dx * N_Z + kz) * slab, (dx * N_Z + kz + 1) * slab)
            there = pl.ds(pl.multiple_of(source_block(at_ref, dx, kz, n_x) * slab, slab), slab)
            tok_out[:, here] = tok_ref[:, there]
            tea_out[:, here] = tea_ref[:, there]
            par_out[:, here] = par_ref[:, there]
    normed, _, _ = norm_forward(tok_out[...], par_out[0:1, :], par_out[1:2, :])
    low_out[...] = normed.astype(bf16)


def proj_kernel(count, *refs):
    blocks, parts = refs[:count], refs[count : 2 * count]
    tok_ref, par_ref, res_out, low_out = refs[2 * count :]
    total = tok_ref[...]
    for block, part in zip(blocks, parts):
        total = total + dot(block[...], part[...], 1, 1)
    res_out[...] = total
    normed, _, _ = norm_forward(total, par_ref[2:3, :], par_ref[3:4, :])
    low_out[...] = normed.astype(bf16)


ERF_TOP = (
    -2.72614225801306e-10,
    2.77068142495902e-08,
    -2.10102402082508e-06,
    -5.69250639462346e-05,
    -7.34990630326855e-04,
    -2.95459980854025e-03,
    -1.60960333262415e-02,
)
ERF_LOW = (
    -1.45660718464996e-05,
    -2.13374055278905e-04,
    -1.68282697438203e-03,
    -7.37332916720468e-03,
    -1.42647390514189e-02,
)


def erf(value):
    value = jnp.clip(value, -4.0, 4.0)
    square = value * value
    top = jnp.full_like(square, ERF_TOP[0])
    for number in ERF_TOP[1:]:
        top = top * square + number
    low = jnp.full_like(square, ERF_LOW[0])
    for number in ERF_LOW[1:]:
        low = low * square + number
    inverse = pl.reciprocal(low, approx=True)
    inverse = inverse * (2.0 - low * inverse)
    return value * top * inverse


def up_kernel(count, *refs):
    low_ref, parts, (act_out, slope_out) = refs[0], refs[1 : 1 + count], refs[1 + count :]
    depth = parts[0].shape[0]
    hidden = None
    for n, part in enumerate(parts):
        piece = dot(low_ref[:, n * depth : (n + 1) * depth], part[...], 1, 0)
        hidden = piece if hidden is None else hidden + piece
    share = 0.5 * (1.0 + erf(hidden * 0.7071067811865476))
    act_out[...] = (hidden * share).astype(bf16)
    slope_out[...] = share + hidden * jnp.exp(-0.5 * hidden * hidden) * 0.3989422804014327


def up_call(low, parts):
    rows, model = low.shape
    depth, width = parts[0].shape
    tile = min(256, width)
    cols = lambda n: pl.BlockSpec((n, tile), lambda i, *_: (0, i))
    return plain_call(
        functools.partial(up_kernel, len(parts)),
        (shaped((rows, width), bf16), shaped((rows, width), f32)),
        low,
        *parts,
        grid=(width // tile,),
        in_specs=[fixed(low.shape)] + [cols(depth)] * len(parts),
        out_specs=(cols(rows), cols(rows)),
        name="up",
    )


def back_kernel(count, adds, *refs):
    gm_ref, low_ref, slope_ref, acc_ref = refs[:4]
    downs = refs[4 : 4 + count]
    ups = refs[4 + count : 4 + 2 * count]
    received = refs[4 + 2 * count : 4 + 2 * count + adds]
    grads = refs[4 + 2 * count + adds : 4 + 3 * count + adds]
    total_ref = refs[-1]
    depth = downs[0].shape[0]

    @pl.when(pl.program_id(0) == 0)
    def _():
        total_ref[...] = acc_ref[...]

    upstream = None
    for n, part in enumerate(downs):
        piece = dot(gm_ref[:, n * depth : (n + 1) * depth], part[...], 1, 0)
        upstream = piece if upstream is None else upstream + piece
    grad = (upstream * slope_ref[...]).astype(bf16)
    for n in range(count):
        cols = slice(n * depth, (n + 1) * depth)
        piece = dot(low_ref[:, cols], grad, 0, 0)
        if adds:
            piece = piece + received[0][cols, :].astype(f32)
        grads[n][...] = piece.astype(bf16)
        total_ref[:, cols] += dot(grad, ups[n][...], 1, 1)


def back_call(gm, low, slope, acc, downs, ups, received):
    rows, model = low.shape
    depth, width = ups[0].shape
    count = len(ups)
    tile = min(256, width)
    cols = lambda n: pl.BlockSpec((n, tile), lambda i, *_: (0, i))
    out = plain_call(
        functools.partial(back_kernel, count, len(received)),
        tuple(shaped((depth, width), bf16) for _ in ups) + (shaped((rows, model), f32),),
        gm,
        low,
        slope,
        acc,
        *downs,
        *ups,
        *received,
        grid=(width // tile,),
        in_specs=[fixed(gm.shape), fixed(low.shape), cols(rows), fixed(acc.shape)]
        + [cols(depth)] * (2 * count)
        + [cols(model)] * len(received),
        out_specs=tuple(cols(depth) for _ in ups) + (fixed((rows, model)),),
        name="back",
    )
    return out[:-1], out[-1]


def norm_sums(grad, scaled, out_ref, first):
    sums = jnp.concatenate(
        [
            jnp.sum(grad * scaled, axis=0, keepdims=True),
            jnp.sum(grad, axis=0, keepdims=True),
            jnp.zeros((6, grad.shape[1]), f32),
        ],
        axis=0,
    )
    out_ref[...] = jnp.where(first, sums, out_ref[...] + sums)


def middle_kernel(grad_ref, res_ref, gout_ref, par_ref, full_out, low_out, sum_out):
    _, scaled, inverse = norm_forward(res_ref[...], par_ref[2:3, :], par_ref[3:4, :])
    grad = grad_ref[...]
    full = gout_ref[...] + norm_backward(grad, scaled, inverse, par_ref[2:3, :])
    full_out[...] = full
    low_out[...] = full.astype(bf16)
    norm_sums(grad, scaled, sum_out, pl.program_id(0) == 0)


def leave_kernel(n_x, slab, count, at_ref, *refs):
    own_ref, received = refs[0], refs[1 : 1 + count]
    tok_ref, res_ref, par_ref, out_ref, sum_out = refs[1 + count :]
    _, scaled, inverse = norm_forward(tok_ref[...], par_ref[0:1, :], par_ref[1:2, :])
    grad = own_ref[...]
    for ref in received:
        grad = grad + ref[...].astype(f32)
    full = res_ref[...] + norm_backward(grad, scaled, inverse, par_ref[0:1, :])
    norm_sums(grad, scaled, sum_out, pl.program_id(0) == 0)
    if slab % 128:
        out_ref[...] = full
        return
    for dx in range(n_x):
        for kz in range(N_Z):
            here = slice((dx * N_Z + kz) * slab, (dx * N_Z + kz + 1) * slab)
            there = pl.ds(pl.multiple_of(source_block(at_ref, dx, kz, n_x) * slab, slab), slab)
            out_ref[:, there] = full[:, here]


def split_kernel(count, *refs):
    total = refs[0][...].astype(f32)
    for ref in refs[1:count]:
        total = total + ref[...].astype(f32)
    outs = refs[count:]
    depth = outs[0].shape[0]
    outs[0][...] = total[:depth]
    for n, out in enumerate(outs[1:], 1):
        out[...] = total[n * depth : (n + 1) * depth].astype(bf16)


def split_call(parts):
    rows, width = parts[0].shape
    depth = rows // N_Z
    shapes = (shaped((depth, width), f32),) + (shaped((depth, width), bf16),) * (N_Z - 1)
    return plain_call(functools.partial(split_kernel, len(parts)), shapes, *parts, name="split")


def adam_kernel(layout, pieces, *refs):
    grad = refs[0][...]
    for ref in refs[1:pieces]:
        grad = grad + ref[...].astype(f32)
    count = len(layout)
    states = refs[pieces : pieces + 3 * count]
    outs = refs[pieces + 3 * count :]
    for n, (start, size, turned) in enumerate(layout):
        weight, first, second = states[3 * n : 3 * n + 3]
        part = grad[:, start : start + size]
        if turned:
            part = part.T
        if len(weight.shape) == 3:
            depth = size // weight.shape[0]
            for k in range(weight.shape[0]):
                new = adam_step(
                    weight[k], part[:, k * depth : (k + 1) * depth], first[k], second[k], weight_decay, learn_rate
                )
                for out, value in zip(outs[3 * n : 3 * n + 3], new):
                    out[k] = value
        else:
            new = adam_step(weight[...], part, first[...], second[...], weight_decay, learn_rate)
            for out, value in zip(outs[3 * n : 3 * n + 3], new):
                out[...] = value


def adam_call(layout, pieces, *states):
    shapes = tuple(shaped(s.shape, f32) for s in states)
    out = plain_call(
        functools.partial(adam_kernel, layout, len(pieces)), shapes, *pieces, *states, name="adam"
    )
    return [out[3 * n : 3 * n + 3] for n in range(len(layout))]


def tie(*values):
    return lax.optimization_barrier(values)


def local(
    n_row,
    n_col,
    tokens,
    teacher,
    segments,
    live_mask,
    weight_qkv,
    weight_proj,
    weight_up,
    weight_down,
    norm_params,
    first_qkv,
    first_proj,
    first_up,
    first_down,
    first_norms,
    second_qkv,
    second_proj,
    second_up,
    second_down,
    second_norms,
):
    n_x = n_row // N_Z
    n_y = n_col // N_CORE
    row = lax.axis_index("row")
    col = lax.axis_index("col")
    z_at, x_at = row // n_x, row % n_x
    y_at, core_at = col // N_CORE, col % N_CORE
    rows = tokens.shape[0]
    group_rows = segments.shape[0]
    slab = weight_qkv.shape[1]
    width = weight_qkv.shape[2]
    model = tokens.shape[1]
    depth = N_Z * slab
    part_rows = min(128, rows)

    def send_row(value, dz, dx):
        perm = [
            (z * n_x + x, (z + dz) % N_Z * n_x + (x + dx) % n_x)
            for z in range(N_Z)
            for x in range(n_x)
        ]
        return lax.ppermute(value, "row", perm)

    def send_col(value, dy, dc):
        perm = [
            (y * N_CORE + c, (y + dy) % n_y * N_CORE + (c + dc) % N_CORE)
            for y in range(n_y)
            for c in range(N_CORE)
        ]
        return lax.ppermute(value, "col", perm)

    def reduce_all(value, axis, size):
        step = 1
        while step < size:
            value = value + lax.ppermute(value, axis, [(i, i ^ step) for i in range(size)])
            step *= 2
        return value

    def relative(value):
        lead = value.shape[:-1]
        value = value.reshape(lead + (N_Z, n_x, slab))
        value = jnp.roll(value, (-z_at, -x_at), axis=(-3, -2))
        return jnp.swapaxes(value, -3, -2).reshape(lead + (model,))

    def absolute(value):
        lead = value.shape[:-1]
        value = jnp.swapaxes(value.reshape(lead + (n_x, N_Z, slab)), -3, -2)
        return jnp.roll(value, (z_at, x_at), axis=(-3, -2)).reshape(lead + (model,))

    def place(dy, dc):
        return ((y_at + dy) % n_y * N_CORE + (core_at + dc) % N_CORE) * rows

    offsets = [(dc, dy) for dc in range(N_CORE) for dy in range(n_y)]
    places = jnp.stack([z_at, x_at]).astype(jnp.int32)

    def fetch_z(shard):
        return [shard] + [send_row(shard, -k, 0) for k in range(1, N_Z)]

    def fetch_x(part):
        return [part] + [send_row(part, 0, -k) for k in range(1, n_x)]

    def fetch_y(part):
        return [part] + [send_col(part, -k, 0) for k in range(1, n_y)]

    def fetch_core(part):
        return send_col(part, 0, -1)

    low_qkv = weight_qkv.astype(bf16)
    shard_qkv = jnp.concatenate([low_qkv[n] for n in range(3)], axis=1)
    near_qkv = fetch_z(shard_qkv)
    shard_proj = weight_proj.astype(bf16).T
    shard_up = weight_up.astype(bf16)
    shard_down = weight_down.astype(bf16).T

    if slab % 128 == 0:
        tokens, teacher, params, low_one = plain_call(
            functools.partial(enter_kernel, n_x, slab),
            (
                shaped(tokens.shape, f32),
                shaped(tokens.shape, f32),
                shaped(norm_params.shape, f32),
                shaped(tokens.shape, bf16),
            ),
            tokens,
            teacher,
            norm_params,
            grid=(rows // part_rows,),
            in_specs=row_blocks(part_rows, model, model) + [fixed(norm_params.shape)],
            out_specs=tuple(
                row_blocks(part_rows, model, model)
                + [fixed(norm_params.shape)]
                + row_blocks(part_rows, model)
            ),
            scalars=(places,),
            name="enter",
        )
    else:
        params = relative(norm_params)
        tokens = relative(tokens)
        teacher = relative(teacher)
        low_one = norm_forward(tokens, params[0], params[1])[0].astype(bf16)

    blocks_one = fetch_y(low_one)
    near_qkv, shard_proj, shard_up = tie(near_qkv, shard_proj, shard_up)
    near_proj = fetch_z(shard_proj)
    near_up = fetch_z(shard_up)
    full_qkv = stack(fetch_x(stack(near_qkv)))
    blocks_one = blocks_one + [fetch_core(block) for block in blocks_one]
    full_proj = fetch_y(stack(fetch_x(stack(near_proj))))
    full_proj = full_proj + [fetch_core(part) for part in full_proj]

    geometry = attend_geometry(segments, live_mask)
    live_count = reduce_all(jnp.sum(live_mask.astype(f32)), "row", n_row)
    own_live = lax.dynamic_slice_in_dim(live_mask, col * rows, rows, 0).astype(f32)

    group_one = jnp.zeros((group_rows, model), bf16)
    for (dc, dy), block in zip(offsets, blocks_one):
        group_one = lax.dynamic_update_slice_in_dim(group_one, block, place(dy, dc), 0)
    group_one, full_qkv, full_proj = tie(group_one, full_qkv, full_proj)
    projected = dot(group_one, full_qkv, 1, 0).astype(bf16)

    near_up, shard_down = tie(near_up, shard_down)
    near_down = fetch_z(shard_down)
    block_up = stack(near_up)
    projected, block_up = tie(projected, block_up)
    mixed = attend_call(
        attend_forward_kernel, projected, [], width, [], geometry, 2, "attention_forward"
    )

    blocks_mixed = []
    for dc, dy in offsets:
        piece = lax.dynamic_slice_in_dim(mixed, place(-dy, -dc), rows, 0)
        blocks_mixed.append(piece if (dc, dy) == (0, 0) else send_col(piece, -dy, -dc))

    beside_up = fetch_x(block_up)
    full_up = {}
    for dx in range(n_x):
        for dy, part in enumerate(fetch_y(beside_up[dx])):
            full_up[0, dy, dx] = part
    block_down = stack(near_down)
    beside_down = fetch_y(block_down)
    full_down = {}
    for dy in range(n_y):
        for dx, part in enumerate(fetch_x(beside_down[dy])):
            full_down[0, dy, dx] = part
    blocks_mixed, block_down, beside_up = tie(blocks_mixed, block_down, beside_up)
    for dy in range(n_y):
        for dx in range(n_x):
            full_up[1, dy, dx] = fetch_core(full_up[0, dy, dx])
            full_down[1, dy, dx] = fetch_core(full_down[0, dy, dx])

    count = len(offsets)
    residual, low_two = plain_call(
        functools.partial(proj_kernel, count),
        (shaped(tokens.shape, f32), shaped(tokens.shape, bf16)),
        *blocks_mixed,
        *full_proj,
        tokens,
        params,
        grid=(rows // part_rows,),
        in_specs=row_blocks(part_rows, *([width] * count))
        + [fixed((model, width))] * count
        + row_blocks(part_rows, model)
        + [fixed(params.shape)],
        out_specs=tuple(row_blocks(part_rows, model, model)),
        name="proj",
    )
    halves = range(n_x)
    active, slope = {}, {}
    error = [residual[:, dx * depth : (dx + 1) * depth] - teacher[:, dx * depth : (dx + 1) * depth] for dx in halves]
    for dc, dy in offsets:
        active[dc, dy], slope[dc, dy] = up_call(low_two, [full_up[dc, dy, dx] for dx in halves])
    for dc, dy in offsets:
        for dx in halves:
            error[dx] = error[dx] + dot(active[dc, dy], full_down[dc, dy, dx], 1, 1)
    error = jnp.concatenate(error, axis=1)
    loss_local = jnp.sum(own_live[:, None] * error * error)
    grad_output = 2.0 * own_live[:, None] * error / live_count
    grad_branch = grad_output.astype(bf16)

    def half(value, dx):
        return value[:, dx * depth : (dx + 1) * depth]

    other = N_CORE - 1
    sent_down = [
        send_col(dot(grad_branch, active[other, dy], 0, 0).astype(bf16), 0, 1) for dy in range(n_y)
    ]
    grad_two = jnp.zeros((rows, model), f32)
    sent_up = []
    hold_down = {}
    for n, dy in enumerate(reversed(range(n_y))):
        pieces, grad_two = back_call(
            grad_branch,
            low_two,
            slope[other, dy],
            grad_two,
            [full_down[other, dy, dx] for dx in halves],
            [full_up[other, dy, dx] for dx in halves],
            [],
        )
        sent_up.append((dy, [send_col(piece, 0, 1) for piece in pieces]))
        if n == 0:
            for k in range(n_y):
                for dx in halves:
                    hold_down[k, dx] = (
                        dot(half(grad_branch, dx), active[0, k], 0, 0)
                        + sent_down[k][dx * depth : (dx + 1) * depth].astype(f32)
                    ).astype(bf16)
            grad_two, hold_down = tie(grad_two, hold_down)
    sent_up = dict(sent_up)
    hold_up = {}
    for dy in reversed(range(n_y)):
        pieces, grad_two = back_call(
            grad_branch,
            low_two,
            slope[0, dy],
            grad_two,
            [full_down[0, dy, dx] for dx in halves],
            [full_up[0, dy, dx] for dx in halves],
            [stack(sent_up[dy])],
        )
        for dx in halves:
            hold_up[dy, dx] = pieces[dx]

    grad_residual, grad_low, sums_two = plain_call(
        middle_kernel,
        (shaped(tokens.shape, f32), shaped(tokens.shape, bf16), shaped((8, model), f32)),
        grad_two,
        residual,
        grad_output,
        params,
        grid=(rows // part_rows,),
        in_specs=row_blocks(part_rows, model, model, model) + [fixed(params.shape)],
        out_specs=tuple(row_blocks(part_rows, model, model) + [fixed((8, model))]),
        name="middle",
    )

    grad_group = jnp.zeros((group_rows, width), bf16)
    for (dc, dy), part in zip(offsets, full_proj):
        piece = dot(grad_low, part, 1, 0).astype(bf16)
        piece = piece if (dc, dy) == (0, 0) else send_col(piece, dy, dc)
        grad_group = lax.dynamic_update_slice_in_dim(grad_group, piece, place(-dy, -dc), 0)
    grad_proj = {key: dot(grad_low, block, 0, 0) for key, block in zip(offsets, blocks_mixed)}
    grad_proj = [
        grad_proj[0, dy] + send_col(grad_proj[other, dy].astype(bf16), 0, 1).astype(f32)
        for dy in range(n_y)
    ]
    for k in range(1, n_y):
        grad_proj[0] = grad_proj[0] + send_col(grad_proj[k].astype(bf16), k, 0).astype(f32)
    grad_proj = grad_proj[0]

    next_down = [hold_down[0, 0]] + [hold_down[dy, 0] for dy in range(1, n_y)]
    for dy in range(1, n_y):
        total = hold_down[dy, 0].astype(f32)
        for dx in range(1, n_x):
            total = total + send_row(hold_down[dy, dx], 0, dx).astype(f32)
        next_down[dy] = total.astype(bf16)
    grad_group, next_down = tie(grad_group, next_down)
    parts_down = [next_down[0]]
    parts_down += [send_col(next_down[dy], dy, 0) for dy in range(1, n_y)]
    parts_down += [send_row(hold_down[0, dx], 0, dx) for dx in range(1, n_x)]
    next_up = [hold_up[0, 0]] + [None] * (n_x - 1)
    for dx in range(1, n_x):
        total = hold_up[0, dx].astype(f32)
        for dy in range(1, n_y):
            total = total + send_col(hold_up[dy, dx], dy, 0).astype(f32)
        next_up[dx] = total.astype(bf16)
    grad_group, next_up = tie(grad_group, next_up)
    parts_up = [next_up[0]]
    parts_up += [send_row(next_up[dx], 0, dx) for dx in range(1, n_x)]
    parts_up += [send_col(hold_up[dy, 0], dy, 0) for dy in range(1, n_y)]

    grad_projected = attend_call(
        attend_backward_kernel,
        projected,
        [grad_group],
        3 * width,
        [pltpu.VMEM((WINDOW, WINDOW), bf16)] * 2,
        geometry,
        5,
        "attention_backward",
    )
    last_down = split_call(parts_down)
    grad_projected, last_down = tie(grad_projected, last_down)
    last_down = [last_down[0]] + [send_row(last_down[k], k, 0) for k in range(1, N_Z)]

    grad_qkv = []
    for dx in reversed(halves):
        cols = slice(dx * depth, (dx + 1) * depth)
        piece = jnp.concatenate(
            [dot(group_one[:, cols], grad_projected, 0, 0).astype(bf16), grad_proj[cols].astype(bf16)],
            axis=1,
        )
        grad_qkv.append(piece if dx == 0 else send_row(piece, 0, dx))
    parts = {
        key: dot(
            lax.dynamic_slice_in_dim(grad_projected, place(key[1], key[0]), rows, 0),
            full_qkv,
            1,
            1,
        )
        for key in reversed(offsets)
    }
    parts = [
        parts[0, dy] + send_col(parts[other, dy].astype(bf16), 0, 1).astype(f32)
        for dy in range(n_y)
    ]
    received = [send_col(parts[k].astype(bf16), k, 0) for k in range(1, n_y)]
    last_up = split_call(parts_up)
    received, last_up = tie(received, last_up)
    last_up = [last_up[0]] + [send_row(last_up[k], k, 0) for k in range(1, N_Z)]
    last_qkv = split_call(list(reversed(grad_qkv)))
    last_qkv = [last_qkv[0]] + [send_row(last_qkv[k], k, 0) for k in range(1, N_Z)]

    token_grad, sums_one = plain_call(
        functools.partial(leave_kernel, n_x, slab, len(received)),
        (shaped(tokens.shape, f32), shaped((8, model), f32)),
        parts[0],
        *received,
        tokens,
        grad_residual,
        params,
        grid=(rows // part_rows,),
        in_specs=row_blocks(part_rows, *([model] * (3 + len(received)))) + [fixed(params.shape)],
        out_specs=tuple(row_blocks(part_rows, model) + [fixed((8, model))]),
        scalars=(places,),
        name="leave",
    )
    if slab % 128:
        token_grad = absolute(token_grad)

    norm_local = absolute(jnp.concatenate([sums_one[:2], sums_two[:2]], axis=0))
    sums = jnp.concatenate([norm_local, jnp.full((1, model), loss_local)], axis=0)
    sums = reduce_all(reduce_all(sums, "col", n_col), "row", n_row)
    loss_sum = sums[4, 0]

    (new_down,) = adam_call(
        [(0, weight_down.shape[0], True)], last_down, weight_down, first_down, second_down
    )
    (new_up,) = adam_call([(0, weight_up.shape[1], False)], last_up, weight_up, first_up, second_up)
    new_qkv, new_proj = adam_call(
        [(0, 3 * width, False), (3 * width, width, True)],
        last_qkv,
        weight_qkv,
        first_qkv,
        second_qkv,
        weight_proj,
        first_proj,
        second_proj,
    )
    new_norms = adam_step(norm_params, sums[:4], first_norms, second_norms, 0.0, norm_rate)
    return (
        loss_sum / live_count,
        token_grad,
        new_qkv[0],
        new_proj[0],
        new_up[0],
        new_down[0],
        new_norms[0],
        new_qkv[1],
        new_proj[1],
        new_up[1],
        new_down[1],
        new_norms[1],
        new_qkv[2],
        new_proj[2],
        new_up[2],
        new_down[2],
        new_norms[2],
    )


def solution(mesh):
    matrices = (P(None, "row", "col"), P("col", "row"), P("row", "col"), P("col", "row"), P())
    tokens = P(("row", "col"), None)
    return jax.shard_map(
        functools.partial(local, mesh.shape["row"], mesh.shape["col"]),
        mesh=mesh,
        in_specs=(tokens, tokens, P("row"), P("row")) + matrices * 3,
        out_specs=(P(), tokens) + matrices * 3,
        check_vma=False,
    )
```

```python
import functools

import jax
import jax.numpy as jnp
from jax import lax
from jax.experimental import pallas as pl
from jax.experimental.pallas import tpu as pltpu
from jax.sharding import PartitionSpec as P

HEAD_DIM = 64
PATCHES = 577
STEP = 10
WINDOW = 640
QROWS = 320
N_Z = 4
N_CORE = 2

layer_eps = 1e-06
adam_eps = 1e-08
learn_rate = 0.03
norm_rate = 0.25
moment_decay = 0.5
weight_decay = 0.05

bf16 = jnp.bfloat16
f32 = jnp.float32


def norm_forward(values, gain_row, bias_row):
    average = jnp.mean(values, axis=-1, keepdims=True)
    centred = values - average
    variance = jnp.mean(centred * centred, axis=-1, keepdims=True)
    inverse = lax.rsqrt(variance + layer_eps)
    scaled = centred * inverse
    return (scaled * gain_row + bias_row, scaled, inverse)


def norm_backward(upstream, scaled, inverse, gain_row):
    weighted = upstream * gain_row
    return inverse * (
        weighted
        - jnp.mean(weighted, axis=-1, keepdims=True)
        - scaled * jnp.mean(weighted * scaled, axis=-1, keepdims=True)
    )


def gelu_slope(hidden):
    return (
        0.5 * (1.0 + lax.erf(hidden * 0.7071067811865476))
        + hidden * jnp.exp(-0.5 * hidden * hidden) * 0.3989422804014327
    )


def adam_step(weight, gradient, momentum, variance, decay_rate, rate):
    momentum = moment_decay * momentum + (1.0 - moment_decay) * gradient
    variance = moment_decay * variance + (1.0 - moment_decay) * gradient * gradient
    correction = 1.0 - moment_decay**STEP
    direction = momentum / correction / (jnp.sqrt(variance / correction) + adam_eps)
    return (weight - rate * (direction + decay_rate * weight), momentum, variance)


def dot(left, right, left_dim, right_dim):
    return lax.dot_general(
        left, right, (((left_dim,), (right_dim,)), ((), ())), preferred_element_type=f32
    )


def head_lanes(width, head):
    lanes = lax.broadcasted_iota(jnp.int32, (1, width), 1)
    return (lanes >= head * HEAD_DIM) & (lanes < (head + 1) * HEAD_DIM)


def attend_weights(q_part, k_all, bias, row_start, rows_in):
    scores = dot(q_part, k_all, 1, 1) * HEAD_DIM ** (-0.5)
    rows, window = scores.shape
    row_ids = row_start + lax.broadcasted_iota(jnp.int32, (rows, window), 0)
    col_ids = lax.broadcasted_iota(jnp.int32, (rows, window), 1)
    scores = jnp.where(row_ids == col_ids, scores, scores + bias)
    weights = jnp.exp(scores - jnp.max(scores, axis=-1, keepdims=True))
    totals = jnp.sum(weights, axis=-1, keepdims=True)
    return weights * jnp.where(rows_in, 1.0 / totals, 0.0)


def image_window(begin, code_ref, group_rows):
    image = pl.program_id(0)
    start = jnp.minimum(begin[image] // 16 * 16, group_rows - WINDOW)
    first = begin[image] - start
    start = pl.multiple_of(start, 16)
    code = code_ref[pl.ds(start, WINDOW), :]
    bias = jnp.where(code == image, 0.0, -1e30).astype(f32).T[0:1, :]
    return image, start, first, bias


def rows_inside(rows, row_start, first):
    ids = row_start + lax.broadcasted_iota(jnp.int32, (rows, 1), 0)
    return (ids >= first) & (ids < first + PATCHES)


def attend_forward_kernel(lanes, begin, code_ref, q_ref, k_ref, v_ref, out_ref):
    image, start, first, bias = image_window(begin, code_ref, q_ref.shape[0])

    @pl.when(image == 0)
    def _():
        out_ref[...] = v_ref[...]

    for tile in range(q_ref.shape[1] // lanes):
        cols = slice(tile * lanes, (tile + 1) * lanes)
        k_all = k_ref[pl.ds(start, WINDOW), cols]
        v_all = v_ref[pl.ds(start, WINDOW), cols]
        for row in range(0, WINDOW, QROWS):
            at = pl.ds(pl.multiple_of(start + row, 16), QROWS)
            q_part = q_ref[at, cols]
            inside = rows_inside(QROWS, row, first)
            mixed = None
            for head in range(lanes // HEAD_DIM):
                mine = head_lanes(lanes, head)
                q_head = jnp.where(mine, q_part, jnp.zeros_like(q_part))
                weights = attend_weights(q_head, k_all, bias, row, inside).astype(bf16)
                part = dot(weights, v_all, 1, 0)
                mixed = part if mixed is None else jnp.where(mine, part, mixed)
            out_ref[at, cols] = jnp.where(inside, mixed.astype(bf16), out_ref[at, cols])


def attend_backward_kernel(
    lanes, begin, code_ref, q_ref, k_ref, v_ref, go_ref, out_ref, p_ref, s_ref
):
    image, start, first, bias = image_window(begin, code_ref, q_ref.shape[0])
    width = q_ref.shape[1]

    @pl.when(image == 0)
    def _():
        out_ref[:, : 2 * width] = jnp.zeros((out_ref.shape[0], 2 * width), bf16)
        out_ref[:, 2 * width :] = go_ref[...]

    whole = pl.ds(start, WINDOW)
    inside_all = rows_inside(WINDOW, 0, first)
    for tile in range(width // lanes):
        cols = slice(tile * lanes, (tile + 1) * lanes)
        k_cols = slice(width + tile * lanes, width + (tile + 1) * lanes)
        v_cols = slice(2 * width + tile * lanes, 2 * width + (tile + 1) * lanes)
        k_all = k_ref[whole, cols]
        v_all = v_ref[whole, cols]
        q_all = q_ref[whole, cols]
        go_all = go_ref[whole, cols]
        key_grad = None
        value_grad = None
        for head in range(lanes // HEAD_DIM):
            mine = head_lanes(lanes, head)
            for row in range(0, WINDOW, QROWS):
                at = pl.ds(pl.multiple_of(start + row, 16), QROWS)
                q_part = q_ref[at, cols]
                go_part = go_ref[at, cols]
                inside = rows_inside(QROWS, row, first)
                q_head = jnp.where(mine, q_part, jnp.zeros_like(q_part))
                go_head = jnp.where(mine, go_part, jnp.zeros_like(go_part))
                weights = attend_weights(q_head, k_all, bias, row, inside)
                weight_grad = dot(go_head, v_all, 1, 1)
                product = weights * weight_grad
                score_grad = (
                    product - weights * jnp.sum(product, axis=-1, keepdims=True)
                ).astype(bf16)
                p_ref[row : row + QROWS, :] = weights.astype(bf16)
                s_ref[row : row + QROWS, :] = score_grad
                query_grad = (dot(score_grad, k_all, 1, 0) * HEAD_DIM ** (-0.5)).astype(bf16)
                out_ref[at, cols] = jnp.where(inside & mine, query_grad, out_ref[at, cols])
            q_mine = jnp.where(mine, q_all, jnp.zeros_like(q_all))
            go_mine = jnp.where(mine, go_all, jnp.zeros_like(go_all))
            key_part = dot(q_mine, s_ref[...], 0, 0)
            value_part = dot(go_mine, p_ref[...], 0, 0)
            key_grad = key_part if key_grad is None else key_grad + key_part
            value_grad = value_part if value_grad is None else value_grad + value_part
        key_rows = (key_grad.T * HEAD_DIM ** (-0.5)).astype(bf16)
        value_rows = value_grad.T.astype(bf16)
        out_ref[whole, k_cols] = jnp.where(inside_all, key_rows, out_ref[whole, k_cols])
        out_ref[whole, v_cols] = jnp.where(inside_all, value_rows, out_ref[whole, v_cols])


def qkv_operands(projected, width):
    group_rows = projected.shape[0]
    if width % 128 == 0:
        specs = [
            pl.BlockSpec((group_rows, width), functools.partial(lambda n, i, *_: (0, n), n))
            for n in range(3)
        ]
        return [projected] * 3, specs
    parts = [projected[:, n * width : (n + 1) * width] for n in range(3)]
    return parts, [pl.BlockSpec((group_rows, width), lambda i, *_: (0, 0))] * 3


def attend_call(kernel, projected, extra, out_width, scratch, geometry, mebibytes, name):
    begin, code = geometry
    group_rows = projected.shape[0]
    width = projected.shape[1] // 3
    operands, specs = qkv_operands(projected, width)
    return pl.pallas_call(
        functools.partial(kernel, min(128, width)),
        grid_spec=pltpu.PrefetchScalarGridSpec(
            num_scalar_prefetch=1,
            grid=begin.shape,
            in_specs=[fixed(code.shape)] + specs + [fixed((group_rows, width)) for _ in extra],
            out_specs=fixed((group_rows, out_width)),
            scratch_shapes=scratch,
        ),
        out_shape=jax.ShapeDtypeStruct((group_rows, out_width), bf16),
        compiler_params=pltpu.CompilerParams(vmem_limit_bytes=mebibytes * 1024 * 1024),
        name=name,
    )(begin, code, *operands, *extra)


def attend_geometry(segments, live_mask):
    group_rows = segments.shape[0]
    numbers = jnp.arange(group_rows // PATCHES, dtype=jnp.int32)
    positions = jnp.arange(group_rows, dtype=jnp.int32)
    begin = jnp.min(
        jnp.where(segments[None, :] == numbers[:, None], positions[None, :], group_rows - PATCHES),
        axis=1,
    )
    code = jnp.where(live_mask == 1, segments, -1)
    return begin, jnp.broadcast_to(code[:, None], (group_rows, 128))


def plain_call(kernel, out_shape, *operands, grid=(), in_specs=None, out_specs=None, scratch=(), scalars=(), mebibytes=16, name=None):
    params = pltpu.CompilerParams(vmem_limit_bytes=mebibytes * 1024 * 1024)
    if in_specs is None:
        in_specs = [pl.BlockSpec(a.shape, functools.partial(lambda n, *_: (0,) * n, a.ndim)) for a in operands]
    if out_specs is None:
        out_specs = jax.tree.map(
            lambda s: pl.BlockSpec(s.shape, functools.partial(lambda n, *_: (0,) * n, len(s.shape))), out_shape
        )
    return pl.pallas_call(
        kernel,
        grid_spec=pltpu.PrefetchScalarGridSpec(
            num_scalar_prefetch=len(scalars),
            grid=grid,
            in_specs=in_specs,
            out_specs=out_specs,
            scratch_shapes=list(scratch),
        ),
        out_shape=out_shape,
        compiler_params=params,
        name=name,
    )(*scalars, *operands)


def shaped(shape, dtype):
    return jax.ShapeDtypeStruct(tuple(shape), dtype)


def row_blocks(rows, *widths):
    return [pl.BlockSpec((rows, w), lambda i, *_: (i, 0)) for w in widths]


def fixed(shape):
    return pl.BlockSpec(tuple(shape), functools.partial(lambda n, *_: (0,) * n, len(shape)))


def stack(pieces):
    if len(pieces) == 1:
        return pieces[0]
    depth, width = pieces[0].shape

    def kernel(*refs):
        for n, ref in enumerate(refs[:-1]):
            refs[-1][n * depth : (n + 1) * depth, :] = ref[...]

    return plain_call(kernel, shaped((len(pieces) * depth, width), pieces[0].dtype), *pieces, name="stack")


def source_block(at_ref, dx, kz, n_x):
    z = lax.rem(at_ref[0] + kz, N_Z)
    x = lax.rem(at_ref[1] + dx, n_x)
    return z * n_x + x


def first_kernel(n_x, slab, at_ref, tok_ref, par_ref, low_out):
    normed, _, _ = norm_forward(tok_ref[...], par_ref[0:1, :], par_ref[1:2, :])
    low = normed.astype(bf16)
    for z in range(N_Z):
        for x in range(n_x):
            dx = lax.rem(x - at_ref[1] + n_x, n_x)
            kz = lax.rem(z - at_ref[0] + N_Z, N_Z)
            there = pl.ds(pl.multiple_of((dx * N_Z + kz) * slab, slab), slab)
            here = slice((z * n_x + x) * slab, (z * n_x + x + 1) * slab)
            low_out[:, there] = low[:, here]


def enter_kernel(n_x, slab, at_ref, tok_ref, tea_ref, par_ref, tok_out, tea_out, par_out):
    for dx in range(n_x):
        for kz in range(N_Z):
            here = slice((dx * N_Z + kz) * slab, (dx * N_Z + kz + 1) * slab)
            there = pl.ds(pl.multiple_of(source_block(at_ref, dx, kz, n_x) * slab, slab), slab)
            tok_out[:, here] = tok_ref[:, there]
            tea_out[:, here] = tea_ref[:, there]
            par_out[:, here] = par_ref[:, there]


def proj_kernel(count, *refs):
    blocks, parts = refs[:count], refs[count : 2 * count]
    tok_ref, par_ref, res_out, low_out, turned_out = refs[2 * count :]
    total = tok_ref[...]
    for block, part in zip(blocks, parts):
        total = total + dot(block[...], part[...], 1, 1)
    res_out[...] = total
    normed, _, _ = norm_forward(total, par_ref[2:3, :], par_ref[3:4, :])
    low_out[...] = normed.astype(bf16)
    turned_out[...] = normed.T.astype(bf16)


ERF_TOP = (
    -2.72614225801306e-10,
    2.77068142495902e-08,
    -2.10102402082508e-06,
    -5.69250639462346e-05,
    -7.34990630326855e-04,
    -2.95459980854025e-03,
    -1.60960333262415e-02,
)
ERF_LOW = (
    -1.45660718464996e-05,
    -2.13374055278905e-04,
    -1.68282697438203e-03,
    -7.37332916720468e-03,
    -1.42647390514189e-02,
)


def erf(value):
    value = jnp.clip(value, -4.0, 4.0)
    square = value * value
    top = jnp.full_like(square, ERF_TOP[0])
    for number in ERF_TOP[1:]:
        top = top * square + number
    low = jnp.full_like(square, ERF_LOW[0])
    for number in ERF_LOW[1:]:
        low = low * square + number
    inverse = pl.reciprocal(low, approx=True)
    inverse = inverse * (2.0 - low * inverse)
    return value * top * inverse


def up_kernel(count, *refs):
    low_ref, parts, (act_out, slope_out) = refs[0], refs[1 : 1 + count], refs[1 + count :]
    depth = parts[0].shape[0]
    hidden = None
    for n, part in enumerate(parts):
        piece = dot(low_ref[:, n * depth : (n + 1) * depth], part[...], 1, 0)
        hidden = piece if hidden is None else hidden + piece
    share = 0.5 * (1.0 + erf(hidden * 0.7071067811865476))
    act_out[...] = (hidden * share).astype(bf16)
    slope_out[...] = share + hidden * jnp.exp(-0.5 * hidden * hidden) * 0.3989422804014327


def up_call(low, parts):
    rows, model = low.shape
    depth, width = parts[0].shape
    tile = min(256, width)
    cols = lambda n: pl.BlockSpec((n, tile), lambda i, *_: (0, i))
    return plain_call(
        functools.partial(up_kernel, len(parts)),
        (shaped((rows, width), bf16), shaped((rows, width), f32)),
        low,
        *parts,
        grid=(width // tile,),
        in_specs=[fixed(low.shape)] + [cols(depth)] * len(parts),
        out_specs=(cols(rows), cols(rows)),
        name="up",
    )


def down_kernel(acts, parts_each, last, *refs):
    base_ref = refs[0]
    active = refs[1 : 1 + acts]
    parts = refs[1 + acts : 1 + acts + acts * parts_each]
    rest = refs[1 + acts + acts * parts_each :]
    depth = parts[0].shape[0]
    columns = []
    for k in range(parts_each):
        total = base_ref[:, k * depth : (k + 1) * depth]
        for n in range(acts):
            total = total + dot(active[n][...], parts[n * parts_each + k][...], 1, 1)
        columns.append(total)
    total = jnp.concatenate(columns, axis=1)
    if not last:
        rest[0][...] = total
        return
    tea_ref, live_ref, count_ref, grad_out, low_out, turned_out, loss_out = rest
    error = total - tea_ref[...]
    live = live_ref[...]
    weighted = live * error
    grad = 2.0 * weighted / count_ref[...]
    grad_out[...] = grad
    low_out[...] = grad.astype(bf16)
    turned_out[...] = grad.T.astype(bf16)
    sums = jnp.sum(weighted * error, axis=0, keepdims=True)
    sums = jnp.concatenate([sums, jnp.zeros((7, sums.shape[1]), f32)], axis=0)
    loss_out[...] = jnp.where(pl.program_id(0) == 0, sums, loss_out[...] + sums)


def down_call(part_rows, base, active, parts, last=()):
    rows, model = base.shape
    width = active[0].shape[1]
    each = len(parts) // len(active)
    in_specs = row_blocks(part_rows, model, *([width] * len(active))) + [
        fixed(part.shape) for part in parts
    ]
    shapes = shaped(base.shape, f32)
    out_specs = row_blocks(part_rows, model)[0]
    if last:
        in_specs += row_blocks(part_rows, model, 1) + [fixed((1, 1))]
        shapes = (
            shapes,
            shaped(base.shape, bf16),
            shaped((model, rows), bf16),
            shaped((8, model), f32),
        )
        out_specs = (
            out_specs,
            out_specs,
            pl.BlockSpec((model, part_rows), lambda i, *_: (0, i)),
            fixed((8, model)),
        )
    return plain_call(
        functools.partial(down_kernel, len(active), each, bool(last)),
        shapes,
        base,
        *active,
        *parts,
        *last,
        grid=(rows // part_rows,),
        in_specs=in_specs,
        out_specs=out_specs,
        mebibytes=28,
        name="down",
    )


def back_kernel(count, adds, *refs):
    gm_ref, turned_ref, slope_ref, acc_ref = refs[:4]
    downs = refs[4 : 4 + count]
    ups = refs[4 + count : 4 + 2 * count]
    received = refs[4 + 2 * count : 4 + 2 * count + adds]
    grad_refs = refs[4 + 2 * count + adds : -1]
    total_ref = refs[-1]
    depth = downs[0].shape[0]

    @pl.when(pl.program_id(0) == 0)
    def _():
        total_ref[...] = acc_ref[...]

    upstream = None
    for n, part in enumerate(downs):
        piece = dot(gm_ref[:, n * depth : (n + 1) * depth], part[...], 1, 0)
        upstream = piece if upstream is None else upstream + piece
    grad = (upstream * slope_ref[...]).astype(bf16)
    for n in range(count):
        cols = slice(n * depth, (n + 1) * depth)
        piece = dot(turned_ref[cols, :], grad, 1, 0)
        if adds:
            piece = piece + received[0][cols, :].astype(f32)
        if len(grad_refs) == 1:
            grad_refs[0][cols, :] = piece.astype(bf16)
        else:
            grad_refs[n][...] = piece.astype(bf16)
        total_ref[:, cols] += dot(grad, ups[n][...], 1, 1)


def back_call(gm, turned, slope, acc, downs, ups, received):
    rows, model = gm.shape
    depth, width = ups[0].shape
    count = len(ups)
    tile = min(256, width)
    cols = lambda n: pl.BlockSpec((n, tile), lambda i, *_: (0, i))
    heights = [depth] * count if received else [model]
    out = plain_call(
        functools.partial(back_kernel, count, len(received)),
        tuple(shaped((n, width), bf16) for n in heights) + (shaped((rows, model), f32),),
        gm,
        turned,
        slope,
        acc,
        *downs,
        *ups,
        *received,
        grid=(width // tile,),
        in_specs=[fixed(gm.shape), fixed(turned.shape), cols(rows), fixed(acc.shape)]
        + [cols(depth)] * (2 * count)
        + [cols(model)] * len(received),
        out_specs=tuple(cols(n) for n in heights) + (fixed((rows, model)),),
        mebibytes=28,
        name="back",
    )
    return out[:-1], out[-1]


def norm_sums(grad, scaled, out_ref, first):
    sums = jnp.concatenate(
        [
            jnp.sum(grad * scaled, axis=0, keepdims=True),
            jnp.sum(grad, axis=0, keepdims=True),
            jnp.zeros((6, grad.shape[1]), f32),
        ],
        axis=0,
    )
    out_ref[...] = jnp.where(first, sums, out_ref[...] + sums)


def middle_kernel(grad_ref, res_ref, gout_ref, par_ref, full_out, low_out, sum_out):
    _, scaled, inverse = norm_forward(res_ref[...], par_ref[2:3, :], par_ref[3:4, :])
    grad = grad_ref[...]
    full = gout_ref[...] + norm_backward(grad, scaled, inverse, par_ref[2:3, :])
    full_out[...] = full
    low_out[...] = full.astype(bf16)
    norm_sums(grad, scaled, sum_out, pl.program_id(0) == 0)


def leave_kernel(n_x, slab, count, at_ref, *refs):
    own_ref, received = refs[0], refs[1 : 1 + count]
    tok_ref, res_ref, par_ref, two_ref, loss_ref, out_ref, sum_out, sum_ref = refs[1 + count :]
    _, scaled, inverse = norm_forward(tok_ref[...], par_ref[0:1, :], par_ref[1:2, :])
    grad = own_ref[...]
    for ref in received:
        grad = grad + ref[...].astype(f32)
    full = res_ref[...] + norm_backward(grad, scaled, inverse, par_ref[0:1, :])
    norm_sums(grad, scaled, sum_ref, pl.program_id(0) == 0)
    sums = jnp.concatenate(
        [sum_ref[0:2, :], two_ref[0:2, :], loss_ref[0:1, :], jnp.zeros((3, full.shape[1]), f32)], axis=0
    )
    if slab % 128:
        out_ref[...] = full
        sum_out[...] = sums
        return
    for dx in range(n_x):
        for kz in range(N_Z):
            here = slice((dx * N_Z + kz) * slab, (dx * N_Z + kz + 1) * slab)
            there = pl.ds(pl.multiple_of(source_block(at_ref, dx, kz, n_x) * slab, slab), slab)
            out_ref[:, there] = full[:, here]
            sum_out[:, there] = sums[:, here]


def split_kernel(count, *refs):
    total = refs[0][...].astype(f32)
    for ref in refs[1:count]:
        total = total + ref[...].astype(f32)
    outs = refs[count:]
    depth = outs[0].shape[0]
    outs[0][...] = total[:depth]
    for n, out in enumerate(outs[1:], 1):
        out[...] = total[n * depth : (n + 1) * depth].astype(bf16)


def split_call(parts):
    rows, width = parts[0].shape
    depth = rows // N_Z
    shapes = (shaped((depth, width), f32),) + (shaped((depth, width), bf16),) * (N_Z - 1)
    return plain_call(functools.partial(split_kernel, len(parts)), shapes, *parts, name="split")


def adam_kernel(layout, pieces, *refs):
    grad = refs[0][...]
    for ref in refs[1:pieces]:
        grad = grad + ref[...].astype(f32)
    count = len(layout)
    states = refs[pieces : pieces + 3 * count]
    outs = refs[pieces + 3 * count :]
    for n, (start, size, turned) in enumerate(layout):
        weight, first, second = states[3 * n : 3 * n + 3]
        part = grad[:, start : start + size]
        if turned:
            part = part.T
        if len(weight.shape) == 3:
            depth = size // weight.shape[0]
            for k in range(weight.shape[0]):
                new = adam_step(
                    weight[k], part[:, k * depth : (k + 1) * depth], first[k], second[k], weight_decay, learn_rate
                )
                for out, value in zip(outs[3 * n : 3 * n + 3], new):
                    out[k] = value
        else:
            new = adam_step(weight[...], part, first[...], second[...], weight_decay, learn_rate)
            for out, value in zip(outs[3 * n : 3 * n + 3], new):
                out[...] = value


def adam_call(layout, pieces, *states):
    shapes = tuple(shaped(s.shape, f32) for s in states)
    out = plain_call(
        functools.partial(adam_kernel, layout, len(pieces)), shapes, *pieces, *states, name="adam"
    )
    return [out[3 * n : 3 * n + 3] for n in range(len(layout))]


def tie(*values):
    return lax.optimization_barrier(values)


def local(
    n_row,
    n_col,
    tokens,
    teacher,
    segments,
    live_mask,
    weight_qkv,
    weight_proj,
    weight_up,
    weight_down,
    norm_params,
    first_qkv,
    first_proj,
    first_up,
    first_down,
    first_norms,
    second_qkv,
    second_proj,
    second_up,
    second_down,
    second_norms,
):
    n_x = n_row // N_Z
    n_y = n_col // N_CORE
    row = lax.axis_index("row")
    col = lax.axis_index("col")
    z_at, x_at = row // n_x, row % n_x
    y_at, core_at = col // N_CORE, col % N_CORE
    rows = tokens.shape[0]
    group_rows = segments.shape[0]
    slab = weight_qkv.shape[1]
    width = weight_qkv.shape[2]
    model = tokens.shape[1]
    depth = N_Z * slab
    part_rows = min(128, rows)

    def send_row(value, dz, dx):
        perm = [
            (z * n_x + x, (z + dz) % N_Z * n_x + (x + dx) % n_x)
            for z in range(N_Z)
            for x in range(n_x)
        ]
        return lax.ppermute(value, "row", perm)

    def send_col(value, dy, dc):
        perm = [
            (y * N_CORE + c, (y + dy) % n_y * N_CORE + (c + dc) % N_CORE)
            for y in range(n_y)
            for c in range(N_CORE)
        ]
        return lax.ppermute(value, "col", perm)

    def reduce_all(value, axis, size):
        step = 1
        while step < size:
            value = value + lax.ppermute(value, axis, [(i, i ^ step) for i in range(size)])
            step *= 2
        return value

    def relative(value):
        lead = value.shape[:-1]
        value = value.reshape(lead + (N_Z, n_x, slab))
        value = jnp.roll(value, (-z_at, -x_at), axis=(-3, -2))
        return jnp.swapaxes(value, -3, -2).reshape(lead + (model,))

    def absolute(value):
        lead = value.shape[:-1]
        value = jnp.swapaxes(value.reshape(lead + (n_x, N_Z, slab)), -3, -2)
        return jnp.roll(value, (z_at, x_at), axis=(-3, -2)).reshape(lead + (model,))

    def place(dy, dc):
        return ((y_at + dy) % n_y * N_CORE + (core_at + dc) % N_CORE) * rows

    offsets = [(dc, dy) for dc in range(N_CORE) for dy in range(n_y)]
    places = jnp.stack([z_at, x_at]).astype(jnp.int32)
    halves = range(n_x)
    other = N_CORE - 1

    def fetch_z(shard):
        return [shard] + [send_row(shard, -k, 0) for k in range(1, N_Z)]

    def fetch_x(part):
        return [part] + [send_row(part, 0, -k) for k in range(1, n_x)]

    def fetch_y(part):
        return [part] + [send_col(part, -k, 0) for k in range(1, n_y)]

    def fetch_core(part):
        return send_col(part, 0, -1)

    low_qkv = weight_qkv.astype(bf16)
    shard_qkv = jnp.concatenate([low_qkv[n] for n in range(3)], axis=1)
    shard_down = weight_down.astype(bf16).T
    shard_qkv, shard_down, tokens = tie(shard_qkv, shard_down, tokens)
    near_qkv = fetch_z(shard_qkv)
    shards_down = fetch_y(shard_down)
    if slab % 128 == 0:
        low_one = plain_call(
            functools.partial(first_kernel, n_x, slab),
            shaped(tokens.shape, bf16),
            tokens,
            norm_params,
            grid=(rows // part_rows,),
            in_specs=row_blocks(part_rows, model) + [fixed(norm_params.shape)],
            out_specs=row_blocks(part_rows, model)[0],
            scalars=(places,),
            name="first",
        )
    else:
        params = relative(norm_params)
        low_one = norm_forward(relative(tokens), params[0], params[1])[0].astype(bf16)
    blocks_one = fetch_y(low_one)
    shard_proj = weight_proj.astype(bf16).T
    shard_up = weight_up.astype(bf16)
    near_qkv, shards_down, shard_proj, shard_up, low_one, tokens, teacher = tie(
        near_qkv, shards_down, shard_proj, shard_up, low_one, tokens, teacher
    )

    part_qkv = fetch_x(stack(near_qkv))
    near_proj = fetch_z(shard_proj)
    near_up = fetch_z(shard_up)
    if slab % 128 == 0:
        tokens, teacher, params = plain_call(
            functools.partial(enter_kernel, n_x, slab),
            (shaped(tokens.shape, f32), shaped(tokens.shape, f32), shaped(norm_params.shape, f32)),
            tokens,
            teacher,
            norm_params,
            grid=(rows // part_rows,),
            in_specs=row_blocks(part_rows, model, model) + [fixed(norm_params.shape)],
            out_specs=tuple(row_blocks(part_rows, model, model) + [fixed(norm_params.shape)]),
            scalars=(places,),
            name="enter",
        )
    else:
        tokens = relative(tokens)
        teacher = relative(teacher)
    geometry = attend_geometry(segments, live_mask)
    own_live = lax.dynamic_slice_in_dim(live_mask, col * rows, rows, 0).astype(f32)[:, None]
    live_count = reduce_all(jnp.sum(live_mask.astype(f32)), "row", n_row).reshape(1, 1)
    part_proj = stack(fetch_x(stack(near_proj)))
    part_qkv, blocks_one, near_up, part_proj, geometry, live_count, own_live, shards_down, tokens = tie(
        part_qkv, blocks_one, near_up, part_proj, geometry, live_count, own_live, shards_down, tokens
    )

    block_up = stack(near_up)
    beside_up = fetch_x(block_up)
    across_up = fetch_y(block_up)
    near_down = fetch_z(shards_down[0])
    blocks_one = blocks_one + [fetch_core(block) for block in blocks_one]
    full_proj = fetch_y(part_proj)
    full_qkv = stack(part_qkv)
    group_one = jnp.zeros((group_rows, model), bf16)
    for (dc, dy), block in zip(offsets, blocks_one):
        group_one = lax.dynamic_update_slice_in_dim(group_one, block, place(dy, dc), 0)
    projected = dot(group_one, full_qkv, 1, 0).astype(bf16)
    mixed = attend_call(
        attend_forward_kernel, projected, [], width, [], geometry, 24, "attention_forward"
    )
    mixed, beside_up, across_up, near_down, full_proj, shards_down = tie(
        mixed, beside_up, across_up, near_down, full_proj, shards_down
    )

    blocks_mixed = []
    for dc, dy in offsets:
        piece = lax.dynamic_slice_in_dim(mixed, place(-dy, -dc), rows, 0)
        blocks_mixed.append(piece if (dc, dy) == (0, 0) else send_col(piece, -dy, -dc))
    full_proj = full_proj + [fetch_core(part) for part in full_proj]
    beside_down = [fetch_x(stack(near_down))]
    far_down = [fetch_z(shard) for shard in shards_down[1:]]
    full_up = {(0, 0, dx): beside_up[dx] for dx in halves}
    for dx in halves:
        full_up[1, 0, dx] = fetch_core(full_up[0, 0, dx])
    blocks_mixed, full_proj, beside_up = tie(blocks_mixed, full_proj, beside_up)

    for dy in range(1, n_y):
        full_up[0, dy, 0] = across_up[dy]
    for dx in range(1, n_x):
        for dy, part in enumerate(fetch_y(beside_up[dx])[1:], 1):
            full_up[0, dy, dx] = part
    count = len(offsets)
    residual, low_two, turned_two = plain_call(
        functools.partial(proj_kernel, count),
        (
            shaped(tokens.shape, f32),
            shaped(tokens.shape, bf16),
            shaped((model, rows), bf16),
        ),
        *blocks_mixed,
        *full_proj,
        tokens,
        params,
        grid=(rows // part_rows,),
        in_specs=row_blocks(part_rows, *([width] * count))
        + [fixed((model, width))] * count
        + row_blocks(part_rows, model)
        + [fixed(params.shape)],
        out_specs=tuple(row_blocks(part_rows, model, model))
        + (pl.BlockSpec((model, part_rows), lambda i, *_: (0, i)),),
        mebibytes=20,
        name="proj",
    )
    active, slope = {}, {}
    for dc in range(N_CORE):
        active[dc, 0], slope[dc, 0] = up_call(low_two, [full_up[dc, 0, dx] for dx in halves])
    beside_down, far_down, active, full_up = tie(beside_down, far_down, active, full_up)

    full_down = {(0, 0, dx): beside_down[0][dx] for dx in halves}
    for dy in range(1, n_y):
        for dx, part in enumerate(fetch_x(stack(far_down[dy - 1]))):
            full_down[0, dy, dx] = part
    for dy in range(n_y):
        for dx in halves:
            full_down[1, dy, dx] = fetch_core(full_down[0, dy, dx])
            if dy:
                full_up[1, dy, dx] = fetch_core(full_up[0, dy, dx])
    for dc, dy in offsets:
        if dy:
            active[dc, dy], slope[dc, dy] = up_call(low_two, [full_up[dc, dy, dx] for dx in halves])
    total = residual
    for dy in range(n_y):
        outcome = down_call(
            part_rows,
            total,
            [active[dc, dy] for dc in range(N_CORE)],
            [full_down[dc, dy, dx] for dc in range(N_CORE) for dx in halves],
            (teacher, own_live, live_count) if dy == n_y - 1 else (),
        )
        total = outcome
    grad_output, grad_branch, turned_branch, loss_rows = outcome

    sent_down = {
        dy: send_col(dot(turned_branch, active[other, dy], 1, 0).astype(bf16), 0, 1)
        for dy in reversed(range(n_y))
    }
    grad_two = jnp.zeros((rows, model), f32)
    sent_up = {}
    for dy in reversed(range(n_y)):
        (piece,), grad_two = back_call(
            grad_branch,
            turned_two,
            slope[other, dy],
            grad_two,
            [full_down[other, dy, dx] for dx in halves],
            [full_up[other, dy, dx] for dx in halves],
            [],
        )
        sent_up[dy] = send_col(piece, 0, 1)
    turned_branch, grad_two = tie(turned_branch, grad_two)
    hold_down = {}
    for dy in reversed(range(n_y)):
        for dx in halves:
            cols = slice(dx * depth, (dx + 1) * depth)
            hold_down[dy, dx] = (
                dot(turned_branch[cols], active[0, dy], 1, 0) + sent_down[dy][cols].astype(f32)
            ).astype(bf16)
    grad_two, hold_down = tie(grad_two, hold_down)

    def reduce_down_x(dy):
        return [hold_down[dy, 0]] + [send_row(hold_down[dy, dx], 0, dx) for dx in halves[1:]]

    summed_down = {dy: reduce_down_x(dy) for dy in range(1, n_y)}
    hold_up = {}
    for dy in reversed(range(n_y)):
        pieces, grad_two = back_call(
            grad_branch,
            turned_two,
            slope[0, dy],
            grad_two,
            [full_down[0, dy, dx] for dx in halves],
            [full_up[0, dy, dx] for dx in halves],
            [sent_up[dy]],
        )
        for dx in halves:
            hold_up[dy, dx] = pieces[dx]
    grad_residual, grad_low, sums_two = plain_call(
        middle_kernel,
        (shaped(tokens.shape, f32), shaped(tokens.shape, bf16), shaped((8, model), f32)),
        grad_two,
        residual,
        grad_output,
        params,
        grid=(rows // part_rows,),
        in_specs=row_blocks(part_rows, model, model, model) + [fixed(params.shape)],
        out_specs=tuple(row_blocks(part_rows, model, model) + [fixed((8, model))]),
        name="middle",
    )
    pieces_attn = {
        key: dot(grad_low, part, 1, 0).astype(bf16) for key, part in zip(offsets, full_proj)
    }
    summed_down, pieces_attn, hold_up, hold_down, grad_low = tie(
        summed_down, pieces_attn, hold_up, hold_down, grad_low
    )

    grad_group = jnp.zeros((group_rows, width), bf16)
    for dc, dy in offsets:
        piece = pieces_attn[dc, dy]
        piece = piece if (dc, dy) == (0, 0) else send_col(piece, dy, dc)
        grad_group = lax.dynamic_update_slice_in_dim(grad_group, piece, place(-dy, -dc), 0)
    grad_proj = {key: dot(grad_low, block, 0, 0).astype(bf16) for key, block in zip(offsets, blocks_mixed)}
    sent_proj = [send_col(grad_proj[other, dy], 0, 1) for dy in range(n_y)]
    summed_down[0] = reduce_down_x(0)
    spread_down = {}

    def reduce_z(parts):
        pieces = split_call(parts)
        return [pieces[0]] + [send_row(pieces[k], k, 0) for k in range(1, N_Z)]

    for dy in range(1, n_y):
        spread_down[dy] = reduce_z(summed_down[dy])
    diagonal_up = {
        (dy, dx): send_col(hold_up[dy, dx], dy, 0) for dy in range(1, n_y) for dx in halves[1:]
    }
    grad_projected = attend_call(
        attend_backward_kernel,
        projected,
        [grad_group],
        3 * width,
        [pltpu.VMEM((WINDOW, WINDOW), bf16)] * 2,
        geometry,
        28,
        "attention_backward",
    )
    grad_projected, summed_down, spread_down, diagonal_up, sent_proj, hold_up = tie(
        grad_projected, summed_down, spread_down, diagonal_up, sent_proj, hold_up
    )

    next_up = {}
    for dx in halves[1:]:
        total = hold_up[0, dx].astype(f32)
        for dy in range(1, n_y):
            total = total + diagonal_up[dy, dx].astype(f32)
        next_up[dx] = total.astype(bf16)
    parts_up = [hold_up[0, 0]]
    parts_up += [send_row(next_up[dx], 0, dx) for dx in halves[1:]]
    parts_up += [send_col(hold_up[dy, 0], dy, 0) for dy in range(1, n_y)]
    spread_down[0] = reduce_z(summed_down[0])
    hold_proj = [
        (grad_proj[0, dy].astype(f32) + sent_proj[dy].astype(f32)).astype(bf16) for dy in range(n_y)
    ]
    part_proj = [hold_proj[0]] + [send_col(hold_proj[k], k, 0) for k in range(1, n_y)]
    parts = {
        key: dot(
            lax.dynamic_slice_in_dim(grad_projected, place(key[1], key[0]), rows, 0),
            full_qkv,
            1,
            1,
        )
        for key in reversed(offsets)
    }
    sent_one = [send_col(parts[other, dy].astype(bf16), 0, 1) for dy in range(n_y)]
    grad_qkv = [dot(group_one[:, dx * depth : (dx + 1) * depth], grad_projected, 0, 0).astype(bf16) for dx in halves]
    end_down = {}
    for dy in range(1, n_y):
        total = spread_down[dy][0]
        for piece in spread_down[dy][1:]:
            total = total + piece.astype(f32)
        end_down[dy] = total.astype(bf16)
    parts_up, spread_down, part_proj, sent_one, grad_qkv, end_down, parts = tie(
        parts_up, spread_down, part_proj, sent_one, grad_qkv, end_down, parts
    )

    last_up = reduce_z(parts_up)
    total = part_proj[0].astype(f32)
    for piece in part_proj[1:]:
        total = total + piece.astype(f32)
    total = total.astype(bf16)
    grad_qkv = [
        jnp.concatenate([grad_qkv[dx], total[dx * depth : (dx + 1) * depth]], axis=1) for dx in halves
    ]
    parts_qkv = [grad_qkv[0]] + [send_row(grad_qkv[dx], 0, dx) for dx in halves[1:]]
    parts = [parts[0, dy] + sent_one[dy].astype(f32) for dy in range(n_y)]
    received = [send_col(parts[k].astype(bf16), k, 0) for k in range(1, n_y)]
    last_down = spread_down[0] + [send_col(end_down[k], k, 0) for k in range(1, n_y)]
    parts_qkv, received, last_up, last_down = tie(parts_qkv, received, last_up, last_down)

    last_qkv = reduce_z(parts_qkv)
    token_grad, sums = plain_call(
        functools.partial(leave_kernel, n_x, slab, len(received)),
        (shaped(tokens.shape, f32), shaped((8, model), f32)),
        parts[0],
        *received,
        tokens,
        grad_residual,
        params,
        sums_two,
        loss_rows,
        grid=(rows // part_rows,),
        in_specs=row_blocks(part_rows, *([model] * (3 + len(received))))
        + [fixed(params.shape), fixed((8, model)), fixed((8, model))],
        out_specs=tuple(row_blocks(part_rows, model) + [fixed((8, model))]),
        scratch=[pltpu.VMEM((8, model), f32)],
        scalars=(places,),
        name="leave",
    )
    if slab % 128:
        token_grad = absolute(token_grad)
        sums = absolute(sums)
    sums = reduce_all(reduce_all(sums, "col", n_col), "row", n_row)
    loss_sum = jnp.sum(sums[4])
    live_count = live_count[0, 0]

    (new_down,) = adam_call(
        [(0, weight_down.shape[0], True)], last_down, weight_down, first_down, second_down
    )
    (new_up,) = adam_call([(0, weight_up.shape[1], False)], last_up, weight_up, first_up, second_up)
    new_qkv, new_proj = adam_call(
        [(0, 3 * width, False), (3 * width, width, True)],
        last_qkv,
        weight_qkv,
        first_qkv,
        second_qkv,
        weight_proj,
        first_proj,
        second_proj,
    )
    new_norms = adam_step(norm_params, sums[:4], first_norms, second_norms, 0.0, norm_rate)
    return (
        loss_sum / live_count,
        token_grad,
        new_qkv[0],
        new_proj[0],
        new_up[0],
        new_down[0],
        new_norms[0],
        new_qkv[1],
        new_proj[1],
        new_up[1],
        new_down[1],
        new_norms[1],
        new_qkv[2],
        new_proj[2],
        new_up[2],
        new_down[2],
        new_norms[2],
    )


def solution(mesh):
    matrices = (P(None, "row", "col"), P("col", "row"), P("row", "col"), P("col", "row"), P())
    tokens = P(("row", "col"), None)
    return jax.shard_map(
        functools.partial(local, mesh.shape["row"], mesh.shape["col"]),
        mesh=mesh,
        in_specs=(tokens, tokens, P("row"), P("row")) + matrices * 3,
        out_specs=(P(), tokens) + matrices * 3,
        check_vma=False,
    )
```

```python
import functools

import jax
import jax.numpy as jnp
from jax import lax
from jax.experimental import pallas as pl
from jax.experimental.pallas import tpu as pltpu
from jax.sharding import PartitionSpec as P

HEAD_DIM = 64
PATCHES = 577
STEP = 10
WINDOW = 640
QROWS = 320
TILE = 256
SMALL = pl.CostEstimate(flops=1024, bytes_accessed=1024, transcendentals=0)
N_Z = 4
N_CORE = 2

layer_eps = 1e-06
adam_eps = 1e-08
learn_rate = 0.03
norm_rate = 0.25
moment_decay = 0.5
weight_decay = 0.05

bf16 = jnp.bfloat16
f32 = jnp.float32


def norm_forward(values, gain_row, bias_row):
    average = jnp.mean(values, axis=-1, keepdims=True)
    centred = values - average
    variance = jnp.mean(centred * centred, axis=-1, keepdims=True)
    inverse = lax.rsqrt(variance + layer_eps)
    scaled = centred * inverse
    return (scaled * gain_row + bias_row, scaled, inverse)


def norm_backward(upstream, scaled, inverse, gain_row):
    weighted = upstream * gain_row
    return inverse * (
        weighted
        - jnp.mean(weighted, axis=-1, keepdims=True)
        - scaled * jnp.mean(weighted * scaled, axis=-1, keepdims=True)
    )


def gelu_slope(hidden):
    return (
        0.5 * (1.0 + lax.erf(hidden * 0.7071067811865476))
        + hidden * jnp.exp(-0.5 * hidden * hidden) * 0.3989422804014327
    )


def adam_step(weight, gradient, momentum, variance, decay_rate, rate):
    momentum = moment_decay * momentum + (1.0 - moment_decay) * gradient
    variance = moment_decay * variance + (1.0 - moment_decay) * gradient * gradient
    correction = 1.0 - moment_decay**STEP
    direction = momentum / correction / (jnp.sqrt(variance / correction) + adam_eps)
    return (weight - rate * (direction + decay_rate * weight), momentum, variance)


def dot(left, right, left_dim, right_dim):
    return lax.dot_general(
        left, right, (((left_dim,), (right_dim,)), ((), ())), preferred_element_type=f32
    )


def head_lanes(width, head):
    lanes = lax.broadcasted_iota(jnp.int32, (1, width), 1)
    return (lanes >= head * HEAD_DIM) & (lanes < (head + 1) * HEAD_DIM)


def attend_weights(q_part, k_all, bias, row_start, rows_in):
    scores = dot(q_part, k_all, 1, 1) * HEAD_DIM ** (-0.5)
    rows, window = scores.shape
    row_ids = row_start + lax.broadcasted_iota(jnp.int32, (rows, window), 0)
    col_ids = lax.broadcasted_iota(jnp.int32, (rows, window), 1)
    scores = jnp.where(row_ids == col_ids, scores, scores + bias)
    weights = jnp.exp(scores - jnp.max(scores, axis=-1, keepdims=True))
    totals = jnp.sum(weights, axis=-1, keepdims=True)
    return weights * jnp.where(rows_in, 1.0 / totals, 0.0)


def image_window(begin, code_ref, group_rows):
    image = pl.program_id(0)
    start = jnp.minimum(begin[image] // 16 * 16, group_rows - WINDOW)
    first = begin[image] - start
    start = pl.multiple_of(start, 16)
    code = code_ref[pl.ds(start, WINDOW), :]
    bias = jnp.where(code == image, 0.0, -1e30).astype(f32).T[0:1, :]
    return image, start, first, bias


def rows_inside(rows, row_start, first):
    ids = row_start + lax.broadcasted_iota(jnp.int32, (rows, 1), 0)
    return (ids >= first) & (ids < first + PATCHES)


def attend_forward_kernel(lanes, begin, code_ref, q_ref, k_ref, v_ref, out_ref):
    image, start, first, bias = image_window(begin, code_ref, q_ref.shape[0])

    @pl.when(image == 0)
    def _():
        out_ref[...] = v_ref[...]

    for tile in range(q_ref.shape[1] // lanes):
        cols = slice(tile * lanes, (tile + 1) * lanes)
        k_all = k_ref[pl.ds(start, WINDOW), cols]
        v_all = v_ref[pl.ds(start, WINDOW), cols]
        for row in range(0, WINDOW, QROWS):
            at = pl.ds(pl.multiple_of(start + row, 16), QROWS)
            q_part = q_ref[at, cols]
            inside = rows_inside(QROWS, row, first)
            mixed = None
            for head in range(lanes // HEAD_DIM):
                mine = head_lanes(lanes, head)
                q_head = jnp.where(mine, q_part, jnp.zeros_like(q_part))
                weights = attend_weights(q_head, k_all, bias, row, inside).astype(bf16)
                part = dot(weights, v_all, 1, 0)
                mixed = part if mixed is None else jnp.where(mine, part, mixed)
            out_ref[at, cols] = jnp.where(inside, mixed.astype(bf16), out_ref[at, cols])


def attend_backward_kernel(
    lanes, begin, code_ref, q_ref, k_ref, v_ref, go_ref, out_ref, p_ref, s_ref
):
    image, start, first, bias = image_window(begin, code_ref, q_ref.shape[0])
    width = q_ref.shape[1]

    @pl.when(image == 0)
    def _():
        out_ref[:, : 2 * width] = jnp.zeros((out_ref.shape[0], 2 * width), bf16)
        out_ref[:, 2 * width :] = go_ref[...]

    whole = pl.ds(start, WINDOW)
    inside_all = rows_inside(WINDOW, 0, first)
    for tile in range(width // lanes):
        cols = slice(tile * lanes, (tile + 1) * lanes)
        k_cols = slice(width + tile * lanes, width + (tile + 1) * lanes)
        v_cols = slice(2 * width + tile * lanes, 2 * width + (tile + 1) * lanes)
        k_all = k_ref[whole, cols]
        v_all = v_ref[whole, cols]
        q_all = q_ref[whole, cols]
        go_all = go_ref[whole, cols]
        key_grad = None
        value_grad = None
        for head in range(lanes // HEAD_DIM):
            mine = head_lanes(lanes, head)
            for row in range(0, WINDOW, QROWS):
                at = pl.ds(pl.multiple_of(start + row, 16), QROWS)
                q_part = q_ref[at, cols]
                go_part = go_ref[at, cols]
                inside = rows_inside(QROWS, row, first)
                q_head = jnp.where(mine, q_part, jnp.zeros_like(q_part))
                go_head = jnp.where(mine, go_part, jnp.zeros_like(go_part))
                weights = attend_weights(q_head, k_all, bias, row, inside)
                weight_grad = dot(go_head, v_all, 1, 1)
                product = weights * weight_grad
                score_grad = (
                    product - weights * jnp.sum(product, axis=-1, keepdims=True)
                ).astype(bf16)
                p_ref[row : row + QROWS, :] = weights.astype(bf16)
                s_ref[row : row + QROWS, :] = score_grad
                query_grad = (dot(score_grad, k_all, 1, 0) * HEAD_DIM ** (-0.5)).astype(bf16)
                out_ref[at, cols] = jnp.where(inside & mine, query_grad, out_ref[at, cols])
            q_mine = jnp.where(mine, q_all, jnp.zeros_like(q_all))
            go_mine = jnp.where(mine, go_all, jnp.zeros_like(go_all))
            key_part = dot(q_mine, s_ref[...], 0, 0)
            value_part = dot(go_mine, p_ref[...], 0, 0)
            key_grad = key_part if key_grad is None else key_grad + key_part
            value_grad = value_part if value_grad is None else value_grad + value_part
        key_rows = (key_grad.T * HEAD_DIM ** (-0.5)).astype(bf16)
        value_rows = value_grad.T.astype(bf16)
        out_ref[whole, k_cols] = jnp.where(inside_all, key_rows, out_ref[whole, k_cols])
        out_ref[whole, v_cols] = jnp.where(inside_all, value_rows, out_ref[whole, v_cols])


def qkv_operands(projected, width):
    group_rows = projected.shape[0]
    if width % 128 == 0:
        specs = [
            pl.BlockSpec((group_rows, width), functools.partial(lambda n, i, *_: (0, n), n))
            for n in range(3)
        ]
        return [projected] * 3, specs
    parts = [projected[:, n * width : (n + 1) * width] for n in range(3)]
    return parts, [pl.BlockSpec((group_rows, width), lambda i, *_: (0, 0))] * 3


def attend_call(kernel, projected, extra, out_width, scratch, geometry, mebibytes, name):
    begin, code = geometry
    group_rows = projected.shape[0]
    width = projected.shape[1] // 3
    operands, specs = qkv_operands(projected, width)
    return pl.pallas_call(
        functools.partial(kernel, min(128, width)),
        grid_spec=pltpu.PrefetchScalarGridSpec(
            num_scalar_prefetch=1,
            grid=begin.shape,
            in_specs=[fixed(code.shape)] + specs + [fixed((group_rows, width)) for _ in extra],
            out_specs=fixed((group_rows, out_width)),
            scratch_shapes=scratch,
        ),
        out_shape=jax.ShapeDtypeStruct((group_rows, out_width), bf16),
        compiler_params=pltpu.CompilerParams(vmem_limit_bytes=mebibytes * 1024 * 1024),
        cost_estimate=SMALL,
        name=name,
    )(begin, code, *operands, *extra)


def attend_geometry(segments, live_mask):
    group_rows = segments.shape[0]
    numbers = jnp.arange(group_rows // PATCHES, dtype=jnp.int32)
    positions = jnp.arange(group_rows, dtype=jnp.int32)
    begin = jnp.min(
        jnp.where(segments[None, :] == numbers[:, None], positions[None, :], group_rows - PATCHES),
        axis=1,
    )
    code = jnp.where(live_mask == 1, segments, -1)
    return begin, jnp.broadcast_to(code[:, None], (group_rows, 128))


def plain_call(kernel, out_shape, *operands, grid=(), in_specs=None, out_specs=None, scratch=(), scalars=(), mebibytes=16, name=None):
    params = pltpu.CompilerParams(vmem_limit_bytes=mebibytes * 1024 * 1024)
    if in_specs is None:
        in_specs = [pl.BlockSpec(a.shape, functools.partial(lambda n, *_: (0,) * n, a.ndim)) for a in operands]
    if out_specs is None:
        out_specs = jax.tree.map(
            lambda s: pl.BlockSpec(s.shape, functools.partial(lambda n, *_: (0,) * n, len(s.shape))), out_shape
        )
    return pl.pallas_call(
        kernel,
        grid_spec=pltpu.PrefetchScalarGridSpec(
            num_scalar_prefetch=len(scalars),
            grid=grid,
            in_specs=in_specs,
            out_specs=out_specs,
            scratch_shapes=list(scratch),
        ),
        out_shape=out_shape,
        compiler_params=params,
        cost_estimate=SMALL,
        name=name,
    )(*scalars, *operands)


def shaped(shape, dtype):
    return jax.ShapeDtypeStruct(tuple(shape), dtype)


def row_blocks(rows, *widths):
    return [pl.BlockSpec((rows, w), lambda i, *_: (i, 0)) for w in widths]


def fixed(shape):
    return pl.BlockSpec(tuple(shape), functools.partial(lambda n, *_: (0,) * n, len(shape)))


def pack_kernel(qkv_ref, proj_ref, up_ref, down_ref, qkv_out, up_out, down_out):
    count, _, width = qkv_ref.shape
    for n in range(count):
        qkv_out[:, n * width : (n + 1) * width] = qkv_ref[n].astype(bf16)
    qkv_out[:, count * width :] = proj_ref[...].T.astype(bf16)
    up_out[...] = up_ref[...].astype(bf16)
    down_out[...] = down_ref[...].T.astype(bf16)


def first_kernel(tok_ref, par_ref, low_out):
    normed, _, _ = norm_forward(tok_ref[...], par_ref[0:1, :], par_ref[1:2, :])
    low_out[...] = normed.astype(bf16)


def block_rows(block, slab):
    return pl.ds(pl.multiple_of(block * slab, slab), slab)


def stack_z(pieces, places):
    slab, width = pieces[0].shape

    def kernel(at_ref, *refs):
        for k, ref in enumerate(refs[:-1]):
            refs[-1][block_rows(lax.rem(at_ref[0] + k, N_Z), slab), :] = ref[...]

    return plain_call(
        kernel, shaped((N_Z * slab, width), bf16), *pieces, scalars=(places,), name="stack_z"
    )


def weave(columns, cuts, places):
    n_x = len(columns[0])
    rows, width = columns[0][0].shape
    slab = rows // N_Z
    flat = [half for column in columns for half in column]
    edges = [0, *cuts, width]
    sizes = [stop - start for start, stop in zip(edges[:-1], edges[1:])]

    def kernel(at_ref, *refs):
        outs = refs[len(flat) :]
        for y in range(len(columns)):
            for dx in range(n_x):
                half = refs[y * n_x + dx]
                x = lax.rem(at_ref[1] + dx, n_x)
                for z in range(N_Z):
                    at = block_rows(z * n_x + x, slab)
                    for out, start, size in zip(outs, edges, sizes):
                        out[at, y * size : (y + 1) * size] = half[
                            z * slab : (z + 1) * slab, start : start + size
                        ]

    out = plain_call(
        kernel,
        tuple(shaped((rows * n_x, size * len(columns)), bf16) for size in sizes),
        *flat,
        scalars=(places,),
        mebibytes=24,
        name="weave",
    )
    return out if cuts else out[0]


def proj_kernel(count, n_x, at_ref, *refs):
    blocks, parts = refs[:count], refs[count : 2 * count]
    tok_ref, par_ref, res_out, low_out, turned_out = refs[2 * count :]
    total = tok_ref[...]
    for block, part in zip(blocks, parts):
        total = total + dot(block[...], part[...], 1, 1)
    res_out[...] = total
    normed, _, _ = norm_forward(total, par_ref[2:3, :], par_ref[3:4, :])
    low_out[...] = normed.astype(bf16)
    turned = normed.T.astype(bf16)
    slab = turned.shape[0] // (N_Z * n_x)
    for z in range(N_Z):
        for x in range(n_x):
            dx = lax.rem(x - at_ref[1] + n_x, n_x)
            block = z * n_x + x
            turned_out[block_rows(dx * N_Z + z, slab), :] = turned[block * slab : (block + 1) * slab]


ERF_TOP = (
    -2.72614225801306e-10,
    2.77068142495902e-08,
    -2.10102402082508e-06,
    -5.69250639462346e-05,
    -7.34990630326855e-04,
    -2.95459980854025e-03,
    -1.60960333262415e-02,
)
ERF_LOW = (
    -1.45660718464996e-05,
    -2.13374055278905e-04,
    -1.68282697438203e-03,
    -7.37332916720468e-03,
    -1.42647390514189e-02,
)


def erf(value):
    value = jnp.clip(value, -4.0, 4.0)
    square = value * value
    top = jnp.full_like(square, ERF_TOP[0])
    for number in ERF_TOP[1:]:
        top = top * square + number
    low = jnp.full_like(square, ERF_LOW[0])
    for number in ERF_LOW[1:]:
        low = low * square + number
    inverse = pl.reciprocal(low, approx=True)
    inverse = inverse * (2.0 - low * inverse)
    return value * top * inverse


def up_kernel(low_ref, part_ref, act_out, slope_out):
    hidden = dot(low_ref[...], part_ref[...], 1, 0)
    share = 0.5 * (1.0 + erf(hidden * 0.7071067811865476))
    act_out[...] = (hidden * share).astype(bf16)
    slope_out[...] = share + hidden * jnp.exp(-0.5 * hidden * hidden) * 0.3989422804014327


def up_call(low, part):
    rows, model = low.shape
    width = part.shape[1]
    cols = lambda n: pl.BlockSpec((n, TILE), lambda i, *_: (0, i))
    return plain_call(
        up_kernel,
        (shaped((rows, width), bf16), shaped((rows, width), f32)),
        low,
        part,
        grid=(width // TILE,),
        in_specs=[fixed(low.shape), cols(model)],
        out_specs=(cols(rows), cols(rows)),
        name="up",
    )


def down_kernel(count, *refs):
    base_ref, active, parts = refs[0], refs[1 : 1 + count], refs[1 + count : 1 + 2 * count]
    tea_ref, live_ref, count_ref, grad_out, low_out, turned_out, loss_out = refs[1 + 2 * count :]
    error = base_ref[...] - tea_ref[...]
    for act, part in zip(active, parts):
        error = error + dot(act[...], part[...], 1, 1)
    weighted = live_ref[...] * error
    grad = 2.0 * weighted / count_ref[...]
    grad_out[...] = grad
    low_out[...] = grad.astype(bf16)
    turned_out[...] = grad.T.astype(bf16)
    sums = jnp.sum(weighted * error, axis=0, keepdims=True)
    loss_out[...] = jnp.concatenate([sums, jnp.zeros((7, sums.shape[1]), f32)], axis=0)


def down_call(base, active, parts, teacher, live, live_count):
    rows, model = base.shape
    count = len(active)
    cols = pl.BlockSpec((rows, TILE), lambda i, *_: (0, i))
    return plain_call(
        functools.partial(down_kernel, count),
        (
            shaped(base.shape, f32),
            shaped(base.shape, bf16),
            shaped((model, rows), bf16),
            shaped((8, model), f32),
        ),
        base,
        *active,
        *parts,
        teacher,
        live,
        live_count,
        grid=(model // TILE,),
        in_specs=[cols]
        + [fixed(act.shape) for act in active]
        + [pl.BlockSpec((TILE, part.shape[1]), lambda i, *_: (i, 0)) for part in parts]
        + [cols, fixed(live.shape), fixed((1, 1))],
        out_specs=(
            cols,
            cols,
            pl.BlockSpec((TILE, rows), lambda i, *_: (i, 0)),
            pl.BlockSpec((8, TILE), lambda i, *_: (0, i)),
        ),
        mebibytes=28,
        name="down",
    )


def outer_kernel(splits, adds, *refs):
    piece = dot(refs[0][...], refs[1][...], 1, 0)
    if adds:
        piece = piece + refs[2][...].astype(f32)
    outs = refs[2 + adds :]
    if splits is None:
        outs[0][...] = piece.astype(bf16)
        return
    n_y, n_x, steps = splits
    depth = piece.shape[0] // n_x
    for y in range(n_y):

        @pl.when(pl.program_id(0) // steps == y)
        def _():
            for x in range(n_x):
                outs[y * n_x + x][...] = piece[x * depth : (x + 1) * depth].astype(bf16)


def outer_call(turned, values, received=(), splits=None):
    model, rows = turned.shape
    width = values.shape[1]
    cols = lambda n: pl.BlockSpec((n, TILE), lambda i, *_: (0, i))
    if splits is None:
        shapes, specs = shaped((model, width), bf16), cols(model)
    else:
        n_y, n_x = splits
        steps = width // n_y // TILE
        splits = (n_y, n_x, steps)
        shapes = (shaped((model // n_x, width // n_y), bf16),) * (n_x * n_y)
        specs = tuple(
            pl.BlockSpec(
                (model // n_x, TILE),
                functools.partial(lambda y, i, *_: (0, jnp.clip(i - y * steps, 0, steps - 1)), y),
            )
            for y in range(n_y)
            for _ in range(n_x)
        )
    return plain_call(
        functools.partial(outer_kernel, splits, len(received)),
        shapes,
        turned,
        values,
        *received,
        grid=(width // TILE,),
        in_specs=[fixed(turned.shape), cols(rows)] + [cols(model)] * len(received),
        out_specs=specs,
        name="outer",
    )


def norm_sums(grad, scaled, out_ref, first):
    sums = jnp.concatenate(
        [
            jnp.sum(grad * scaled, axis=0, keepdims=True),
            jnp.sum(grad, axis=0, keepdims=True),
            jnp.zeros((6, grad.shape[1]), f32),
        ],
        axis=0,
    )
    out_ref[...] = jnp.where(first, sums, out_ref[...] + sums)


def middle_kernel(grad_ref, res_ref, gout_ref, par_ref, full_out, low_out, sum_out):
    _, scaled, inverse = norm_forward(res_ref[...], par_ref[2:3, :], par_ref[3:4, :])
    grad = grad_ref[...]
    full = gout_ref[...] + norm_backward(grad, scaled, inverse, par_ref[2:3, :])
    full_out[...] = full
    low_out[...] = full.astype(bf16)
    norm_sums(grad, scaled, sum_out, pl.program_id(0) == 0)


def leave_kernel(count, *refs):
    own_ref, received = refs[0], refs[1 : 1 + count]
    tok_ref, res_ref, par_ref, two_ref, loss_ref, out_ref, sum_out, sum_ref = refs[1 + count :]
    _, scaled, inverse = norm_forward(tok_ref[...], par_ref[0:1, :], par_ref[1:2, :])
    grad = own_ref[...]
    for ref in received:
        grad = grad + ref[...].astype(f32)
    out_ref[...] = res_ref[...] + norm_backward(grad, scaled, inverse, par_ref[0:1, :])
    norm_sums(grad, scaled, sum_ref, pl.program_id(0) == 0)
    sum_out[...] = jnp.concatenate(
        [sum_ref[0:2, :], two_ref[0:2, :], loss_ref[0:1, :], jnp.zeros((3, grad.shape[1]), f32)],
        axis=0,
    )


def split_x_kernel(n_x, at_ref, qkv_ref, proj_ref, *outs):
    width = qkv_ref.shape[1]
    slab = qkv_ref.shape[0] // (N_Z * n_x)
    for dx in range(n_x):
        x = lax.rem(at_ref[1] + dx, n_x)
        for z in range(N_Z):
            at = block_rows(z * n_x + x, slab)
            rows = slice(z * slab, (z + 1) * slab)
            outs[dx][rows, :width] = qkv_ref[at, :]
            outs[dx][rows, width:] = proj_ref[at, :]


def split_z(parts, places):
    rows, width = parts[0].shape
    slab = rows // N_Z

    def kernel(at_ref, *refs):
        for k, out in enumerate(refs[len(parts) :]):
            at = block_rows(lax.rem(at_ref[0] + k, N_Z), slab)
            total = refs[0][at, :].astype(f32)
            for ref in refs[1 : len(parts)]:
                total = total + ref[at, :].astype(f32)
            out[...] = total.astype(out.dtype)

    shapes = (shaped((slab, width), f32),) + (shaped((slab, width), bf16),) * (N_Z - 1)
    return plain_call(kernel, shapes, *parts, scalars=(places,), name="split_z")


def adam_kernel(layout, pieces, *refs):
    grad = refs[0][...]
    for ref in refs[1:pieces]:
        grad = grad + ref[...].astype(f32)
    count = len(layout)
    states = refs[pieces : pieces + 3 * count]
    outs = refs[pieces + 3 * count :]
    for n, (start, size, turned) in enumerate(layout):
        weight, first, second = states[3 * n : 3 * n + 3]
        part = grad[:, start : start + size]
        if turned:
            part = part.T
        if len(weight.shape) == 3:
            depth = size // weight.shape[0]
            for k in range(weight.shape[0]):
                new = adam_step(
                    weight[k], part[:, k * depth : (k + 1) * depth], first[k], second[k], weight_decay, learn_rate
                )
                for out, value in zip(outs[3 * n : 3 * n + 3], new):
                    out[k] = value
        else:
            new = adam_step(weight[...], part, first[...], second[...], weight_decay, learn_rate)
            for out, value in zip(outs[3 * n : 3 * n + 3], new):
                out[...] = value


def adam_call(layout, pieces, *states):
    shapes = tuple(shaped(s.shape, f32) for s in states)
    out = plain_call(
        functools.partial(adam_kernel, layout, len(pieces)), shapes, *pieces, *states, name="adam"
    )
    return [out[3 * n : 3 * n + 3] for n in range(len(layout))]


def tie(*values):
    return lax.optimization_barrier(values)


def local(
    n_x,
    n_y,
    tokens,
    teacher,
    segments,
    live_mask,
    weight_qkv,
    weight_proj,
    weight_up,
    weight_down,
    norm_params,
    first_qkv,
    first_proj,
    first_up,
    first_down,
    first_norms,
    second_qkv,
    second_proj,
    second_up,
    second_down,
    second_norms,
):
    z_at, x_at = lax.axis_index("z"), lax.axis_index("x")
    y_at, core_at = lax.axis_index("y"), lax.axis_index("core")
    rows, model = tokens.shape
    group_rows = segments.shape[0]
    slab = weight_qkv.shape[1]
    width = weight_qkv.shape[2]
    unit = weight_up.shape[1]
    part_rows = min(128, rows)
    sizes = {"z": N_Z, "x": n_x, "y": n_y, "core": N_CORE}
    places = jnp.stack([z_at, x_at]).astype(jnp.int32)
    offsets = [(dc, dy) for dc in range(N_CORE) for dy in range(n_y)]
    other = N_CORE - 1

    def send(value, axis, step):
        size = sizes[axis]
        return lax.ppermute(value, axis, [(i, (i + step) % size) for i in range(size)])

    def send_col(value, dy, dc):
        perm = [
            (y * N_CORE + c, (y + dy) % n_y * N_CORE + (c + dc) % N_CORE)
            for y in range(n_y)
            for c in range(N_CORE)
        ]
        return lax.ppermute(value, ("y", "core"), perm)

    def fetch(value, axis):
        return [value] + [send(value, axis, -k) for k in range(1, sizes[axis])]

    def reduce_all(value, axes):
        for axis in axes:
            step = 1
            while step < sizes[axis]:
                pairs = [(i, i ^ step) for i in range(sizes[axis])]
                value = value + lax.ppermute(value, axis, pairs)
                step *= 2
        return value

    def place(dy, dc):
        return ((y_at + dy) % n_y * N_CORE + (core_at + dc) % N_CORE) * rows

    shard_qkv, shard_up, shard_down = plain_call(
        pack_kernel,
        (
            shaped((slab, 4 * width), bf16),
            shaped((slab, unit), bf16),
            shaped((slab, unit), bf16),
        ),
        weight_qkv,
        weight_proj,
        weight_up,
        weight_down,
        name="pack",
    )
    near_qkv = fetch(shard_qkv, "z")
    shards_down = fetch(shard_down, "y")
    shard_qkv, tokens = tie(shard_qkv, tokens)
    low_one = plain_call(
        first_kernel,
        shaped(tokens.shape, bf16),
        tokens,
        norm_params,
        grid=(rows // part_rows,),
        in_specs=row_blocks(part_rows, model) + [fixed(norm_params.shape)],
        out_specs=row_blocks(part_rows, model)[0],
        name="first",
    )
    blocks_one = fetch(low_one, "y")
    near_qkv, shards_down, shard_up, low_one = tie(near_qkv, shards_down, shard_up, low_one)
    shard_down = jnp.concatenate(shards_down, axis=1)
    full_down = [lax.all_gather(shard_down, ("z", "x"), axis=0, tiled=True)]

    beside_qkv = fetch(stack_z(near_qkv, places), "x")
    near_up = fetch(shard_up, "z")
    blocks_one = blocks_one + [send(block, "core", -1) for block in blocks_one]
    geometry = attend_geometry(segments, live_mask)
    own_live = lax.dynamic_slice_in_dim(
        live_mask, (y_at * N_CORE + core_at) * rows, rows, 0
    ).astype(f32)[:, None]
    group_one = jnp.zeros((group_rows, model), bf16)
    for (dc, dy), block in zip(offsets, blocks_one):
        group_one = lax.dynamic_update_slice_in_dim(group_one, block, place(dy, dc), 0)
    full_qkv, part_proj = weave([beside_qkv], [3 * width], places)
    full_qkv, part_proj, group_one, near_up, geometry, own_live = tie(
        full_qkv, part_proj, group_one, near_up, geometry, own_live
    )

    block_up = stack_z(near_up, places)
    beside_up = fetch(block_up, "x")
    across_up = fetch(block_up, "y")
    full_proj = fetch(part_proj, "y")
    projected = dot(group_one, full_qkv, 1, 0).astype(bf16)
    mixed = attend_call(
        attend_forward_kernel, projected, [], width, [], geometry, 24, "attention_forward"
    )
    mixed, beside_up, across_up, full_proj = tie(mixed, beside_up, across_up, full_proj)

    blocks_mixed = []
    for dc, dy in offsets:
        piece = lax.dynamic_slice_in_dim(mixed, place(-dy, -dc), rows, 0)
        blocks_mixed.append(piece if (dc, dy) == (0, 0) else send_col(piece, -dy, -dc))
    full_proj = full_proj + [send(part, "core", -1) for part in full_proj]
    blocks_mixed, full_proj, beside_up = tie(blocks_mixed, full_proj, beside_up)
    columns_up = [beside_up] + [[across_up[dy]] for dy in range(1, n_y)]
    for dx in range(1, n_x):
        for dy, part in enumerate(fetch(beside_up[dx], "y")[1:], 1):
            columns_up[dy].append(part)
    live_count = reduce_all(jnp.sum(live_mask.astype(f32)), ("z", "x")).reshape(1, 1)
    count = len(offsets)
    residual, low_two, turned_two = plain_call(
        functools.partial(proj_kernel, count, n_x),
        (
            shaped(tokens.shape, f32),
            shaped(tokens.shape, bf16),
            shaped((model, rows), bf16),
        ),
        *blocks_mixed,
        *full_proj,
        tokens,
        norm_params,
        grid=(rows // part_rows,),
        in_specs=row_blocks(part_rows, *([width] * count))
        + [fixed((model, width))] * count
        + row_blocks(part_rows, model)
        + [fixed(norm_params.shape)],
        out_specs=tuple(row_blocks(part_rows, model, model))
        + (pl.BlockSpec((model, part_rows), lambda i, *_: (0, i)),),
        scalars=(places,),
        mebibytes=20,
        name="proj",
    )
    columns_up, full_down, low_two = tie(columns_up, full_down, low_two)
    full_up = [weave(columns_up, [], places)]
    full_up.append(send(full_up[0], "core", -1))
    full_down = [full_down[0], send(full_down[0], "core", -1)]
    active, slope = zip(*[up_call(low_two, part) for part in full_up])
    grad_output, grad_branch, turned_branch, loss_rows = down_call(
        residual, active, full_down, teacher, own_live, live_count
    )

    sent_down = send(outer_call(turned_branch, active[other]), "core", 1)
    grad_hidden = [
        (dot(grad_branch, full_down[dc], 1, 0) * slope[dc]).astype(bf16) for dc in range(N_CORE)
    ]
    sent_up = send(outer_call(turned_two, grad_hidden[other]), "core", 1)
    grad_two = dot(grad_hidden[0], full_up[0], 1, 1) + dot(grad_hidden[1], full_up[1], 1, 1)
    hold_down = outer_call(turned_branch, active[0], (sent_down,))
    reduced_down = lax.psum_scatter(hold_down, ("z", "x"), scatter_dimension=0, tiled=True)
    grad_residual, grad_low, sums_two = plain_call(
        middle_kernel,
        (shaped(tokens.shape, f32), shaped(tokens.shape, bf16), shaped((8, model), f32)),
        grad_two,
        residual,
        grad_output,
        norm_params,
        grid=(rows // part_rows,),
        in_specs=row_blocks(part_rows, model, model, model) + [fixed(norm_params.shape)],
        out_specs=tuple(row_blocks(part_rows, model, model) + [fixed((8, model))]),
        name="middle",
    )
    pieces_attn = [dot(grad_low, part, 1, 0).astype(bf16) for part in full_proj]
    pieces_attn, hold_down, sent_up, grad_low = tie(pieces_attn, hold_down, sent_up, grad_low)

    grad_group = jnp.zeros((group_rows, width), bf16)
    for (dc, dy), piece in zip(offsets, pieces_attn):
        piece = piece if (dc, dy) == (0, 0) else send_col(piece, dy, dc)
        grad_group = lax.dynamic_update_slice_in_dim(grad_group, piece, place(-dy, -dc), 0)
    hold_up = outer_call(turned_two, grad_hidden[0], (sent_up,), splits=(n_y, n_x))
    hold_up = {(dy, dx): hold_up[dy * n_x + dx] for dy in range(n_y) for dx in range(n_x)}
    grad_proj = [dot(grad_low, block, 0, 0).astype(bf16) for block in blocks_mixed]
    grad_group, hold_up, grad_proj = tie(grad_group, hold_up, grad_proj)

    diagonal_up = {
        (dy, dx): send(hold_up[dy, dx], "y", dy) for dy in range(1, n_y) for dx in range(1, n_x)
    }
    direct_up = [send(hold_up[dy, 0], "y", dy) for dy in range(1, n_y)]
    sent_proj = [send(grad_proj[n_y + dy], "core", 1) for dy in range(n_y)]
    grad_projected = attend_call(
        attend_backward_kernel,
        projected,
        [grad_group],
        3 * width,
        [pltpu.VMEM((WINDOW, WINDOW), bf16)] * 2,
        geometry,
        28,
        "attention_backward",
    )
    grad_projected, diagonal_up, direct_up, sent_proj, hold_up = tie(
        grad_projected, diagonal_up, direct_up, sent_proj, hold_up
    )

    parts_up = [hold_up[0, 0]] + direct_up
    for dx in range(1, n_x):
        total = hold_up[0, dx].astype(f32)
        for dy in range(1, n_y):
            total = total + diagonal_up[dy, dx].astype(f32)
        parts_up.append(send(total.astype(bf16), "x", dx))
    hold_proj = [
        (grad_proj[dy].astype(f32) + sent_proj[dy].astype(f32)).astype(bf16) for dy in range(n_y)
    ]
    part_proj = [hold_proj[0]] + [send(hold_proj[k], "y", k) for k in range(1, n_y)]
    grad_qkv = dot(group_one, grad_projected, 0, 0).astype(bf16)
    parts = {
        key: dot(
            lax.dynamic_slice_in_dim(grad_projected, place(key[1], key[0]), rows, 0),
            full_qkv,
            1,
            1,
        )
        for key in reversed(offsets)
    }
    sent_one = [send(parts[other, dy].astype(bf16), "core", 1) for dy in range(n_y)]
    grad_qkv, part_proj, sent_one, parts = tie(grad_qkv, part_proj, sent_one, parts)

    total = part_proj[0].astype(f32)
    for piece in part_proj[1:]:
        total = total + piece.astype(f32)
    halves_qkv = plain_call(
        functools.partial(split_x_kernel, n_x),
        tuple(shaped((model // n_x, 4 * width), bf16) for _ in range(n_x)),
        grad_qkv,
        total.astype(bf16),
        scalars=(places,),
        name="split_x",
    )
    parts_qkv = [halves_qkv[0]] + [send(halves_qkv[dx], "x", dx) for dx in range(1, n_x)]
    parts = [parts[0, dy] + sent_one[dy].astype(f32) for dy in range(n_y)]
    received = [send(parts[k].astype(bf16), "y", k) for k in range(1, n_y)]

    def spread(pieces):
        return [pieces[0]] + [send(pieces[k], "z", k) for k in range(1, N_Z)]

    last_up = spread(split_z(parts_up, places))
    parts_qkv, received, last_up, reduced_down = tie(parts_qkv, received, last_up, reduced_down)

    last_qkv = spread(split_z(parts_qkv, places))
    token_grad, sums = plain_call(
        functools.partial(leave_kernel, len(received)),
        (shaped(tokens.shape, f32), shaped((8, model), f32)),
        parts[0],
        *received,
        tokens,
        grad_residual,
        norm_params,
        sums_two,
        loss_rows,
        grid=(rows // part_rows,),
        in_specs=row_blocks(part_rows, *([model] * (3 + len(received))))
        + [fixed(norm_params.shape), fixed((8, model)), fixed((8, model))],
        out_specs=tuple(row_blocks(part_rows, model) + [fixed((8, model))]),
        scratch=[pltpu.VMEM((8, model), f32)],
        name="leave",
    )
    sums = reduce_all(sums, ("core", "y", "x", "z"))
    loss_sum = jnp.sum(sums[4])
    live_count = live_count[0, 0]
    last_down = [reduced_down[:, :unit].astype(f32)]
    for k in range(1, n_y):
        last_down.append(send(reduced_down[:, k * unit : (k + 1) * unit], "y", k))

    (new_down,) = adam_call(
        [(0, weight_down.shape[0], True)], last_down, weight_down, first_down, second_down
    )
    (new_up,) = adam_call([(0, weight_up.shape[1], False)], last_up, weight_up, first_up, second_up)
    new_qkv, new_proj = adam_call(
        [(0, 3 * width, False), (3 * width, width, True)],
        last_qkv,
        weight_qkv,
        first_qkv,
        second_qkv,
        weight_proj,
        first_proj,
        second_proj,
    )
    new_norms = adam_step(norm_params, sums[:4], first_norms, second_norms, 0.0, norm_rate)
    return (
        loss_sum / live_count,
        token_grad,
        new_qkv[0],
        new_proj[0],
        new_up[0],
        new_down[0],
        new_norms[0],
        new_qkv[1],
        new_proj[1],
        new_up[1],
        new_down[1],
        new_norms[1],
        new_qkv[2],
        new_proj[2],
        new_up[2],
        new_down[2],
        new_norms[2],
    )


def solution(mesh):
    n_x = mesh.shape["row"] // N_Z
    n_y = mesh.shape["col"] // N_CORE
    mesh = jax.sharding.Mesh(
        mesh.devices.reshape(N_Z, n_x, n_y, N_CORE), ("z", "x", "y", "core")
    )
    row, col = ("z", "x"), ("y", "core")
    matrices = (P(None, row, col), P(col, row), P(row, col), P(col, row), P())
    tokens = P(row + col, None)
    return jax.shard_map(
        functools.partial(local, n_x, n_y),
        mesh=mesh,
        in_specs=(tokens, tokens, P(row), P(row)) + matrices * 3,
        out_specs=(P(), tokens) + matrices * 3,
        check_vma=False,
    )
```

```python
import functools

import jax
import jax.numpy as jnp
from jax import lax
from jax.experimental import pallas as pl
from jax.experimental.pallas import tpu as pltpu
from jax.sharding import PartitionSpec as P

HEAD_DIM = 64
PATCHES = 577
STEP = 10
WINDOW = 640
QROWS = 320
TILE = 256
SMALL = pl.CostEstimate(flops=1024, bytes_accessed=1024, transcendentals=0)
N_Z = 4
N_CORE = 2

layer_eps = 1e-06
adam_eps = 1e-08
learn_rate = 0.03
norm_rate = 0.25
moment_decay = 0.5
weight_decay = 0.05

bf16 = jnp.bfloat16
f32 = jnp.float32


def norm_forward(values, gain_row, bias_row):
    average = jnp.mean(values, axis=-1, keepdims=True)
    centred = values - average
    variance = jnp.mean(centred * centred, axis=-1, keepdims=True)
    inverse = lax.rsqrt(variance + layer_eps)
    scaled = centred * inverse
    return (scaled * gain_row + bias_row, scaled, inverse)


def norm_backward(upstream, scaled, inverse, gain_row):
    weighted = upstream * gain_row
    return inverse * (
        weighted
        - jnp.mean(weighted, axis=-1, keepdims=True)
        - scaled * jnp.mean(weighted * scaled, axis=-1, keepdims=True)
    )


def gelu_slope(hidden):
    return (
        0.5 * (1.0 + lax.erf(hidden * 0.7071067811865476))
        + hidden * jnp.exp(-0.5 * hidden * hidden) * 0.3989422804014327
    )


def adam_step(weight, gradient, momentum, variance, decay_rate, rate):
    momentum = moment_decay * momentum + (1.0 - moment_decay) * gradient
    variance = moment_decay * variance + (1.0 - moment_decay) * gradient * gradient
    correction = 1.0 - moment_decay**STEP
    direction = momentum / correction / (jnp.sqrt(variance / correction) + adam_eps)
    return (weight - rate * (direction + decay_rate * weight), momentum, variance)


def dot(left, right, left_dim, right_dim):
    return lax.dot_general(
        left, right, (((left_dim,), (right_dim,)), ((), ())), preferred_element_type=f32
    )


def head_lanes(width, head):
    lanes = lax.broadcasted_iota(jnp.int32, (1, width), 1)
    return (lanes >= head * HEAD_DIM) & (lanes < (head + 1) * HEAD_DIM)


def attend_weights(q_part, k_all, bias, row_start, rows_in):
    scores = dot(q_part, k_all, 1, 1) * HEAD_DIM ** (-0.5)
    rows, window = scores.shape
    row_ids = row_start + lax.broadcasted_iota(jnp.int32, (rows, window), 0)
    col_ids = lax.broadcasted_iota(jnp.int32, (rows, window), 1)
    scores = jnp.where(row_ids == col_ids, scores, scores + bias)
    weights = jnp.exp(scores - jnp.max(scores, axis=-1, keepdims=True))
    totals = jnp.sum(weights, axis=-1, keepdims=True)
    return weights * jnp.where(rows_in, 1.0 / totals, 0.0)


def image_window(begin, code_ref, group_rows):
    image = pl.program_id(0)
    start = jnp.minimum(begin[image] // 16 * 16, group_rows - WINDOW)
    first = begin[image] - start
    start = pl.multiple_of(start, 16)
    code = code_ref[pl.ds(start, WINDOW), :]
    bias = jnp.where(code == image, 0.0, -1e30).astype(f32).T[0:1, :]
    return image, start, first, bias


def rows_inside(rows, row_start, first):
    ids = row_start + lax.broadcasted_iota(jnp.int32, (rows, 1), 0)
    return (ids >= first) & (ids < first + PATCHES)


def attend_forward_kernel(begin, code_ref, *refs):
    image, start, first, bias = image_window(begin, code_ref, refs[0].shape[0])
    out_ref = refs[-1]
    lanes = refs[0].shape[1]

    for tile in range((len(refs) - 1) // 3):
        q_ref, k_ref, v_ref = refs[3 * tile : 3 * tile + 3]
        cols = slice(tile * lanes, (tile + 1) * lanes)

        @pl.when(image == 0)
        def _():
            out_ref[:, cols] = v_ref[...]

        k_all = k_ref[pl.ds(start, WINDOW), :]
        v_all = v_ref[pl.ds(start, WINDOW), :]
        for row in range(0, WINDOW, QROWS):
            at = pl.ds(pl.multiple_of(start + row, 16), QROWS)
            q_part = q_ref[at, :]
            inside = rows_inside(QROWS, row, first)
            mixed = None
            for head in range(lanes // HEAD_DIM):
                mine = head_lanes(lanes, head)
                q_head = jnp.where(mine, q_part, jnp.zeros_like(q_part))
                weights = attend_weights(q_head, k_all, bias, row, inside).astype(bf16)
                part = dot(weights, v_all, 1, 0)
                mixed = part if mixed is None else jnp.where(mine, part, mixed)
            out_ref[at, cols] = jnp.where(inside, mixed.astype(bf16), out_ref[at, cols])


def attend_backward_kernel(begin, code_ref, q_ref, k_ref, v_ref, go_ref, *refs):
    image, start, first, bias = image_window(begin, code_ref, q_ref.shape[0])
    out_ref, p_ref, s_ref = refs[-3:]
    lanes = q_ref.shape[1]

    @pl.when(image == 0)
    def _():
        out_ref[:, : 2 * lanes] = jnp.zeros((out_ref.shape[0], 2 * lanes), bf16)
        out_ref[:, 2 * lanes :] = go_ref[...]

    whole = pl.ds(start, WINDOW)
    inside_all = rows_inside(WINDOW, 0, first)
    q_cols, k_cols, v_cols = [slice(n * lanes, (n + 1) * lanes) for n in range(3)]
    k_all = k_ref[whole, :]
    v_all = v_ref[whole, :]
    q_all = q_ref[whole, :]
    go_all = go_ref[whole, :]
    key_grad = None
    value_grad = None
    for head in range(lanes // HEAD_DIM):
        mine = head_lanes(lanes, head)
        for row in range(0, WINDOW, QROWS):
            at = pl.ds(pl.multiple_of(start + row, 16), QROWS)
            q_part = q_ref[at, :]
            go_part = go_ref[at, :]
            inside = rows_inside(QROWS, row, first)
            q_head = jnp.where(mine, q_part, jnp.zeros_like(q_part))
            go_head = jnp.where(mine, go_part, jnp.zeros_like(go_part))
            weights = attend_weights(q_head, k_all, bias, row, inside)
            weight_grad = dot(go_head, v_all, 1, 1)
            product = weights * weight_grad
            score_grad = (
                product - weights * jnp.sum(product, axis=-1, keepdims=True)
            ).astype(bf16)
            p_ref[row : row + QROWS, :] = weights.astype(bf16)
            s_ref[row : row + QROWS, :] = score_grad
            query_grad = (dot(score_grad, k_all, 1, 0) * HEAD_DIM ** (-0.5)).astype(bf16)
            out_ref[at, q_cols] = jnp.where(inside & mine, query_grad, out_ref[at, q_cols])
        q_mine = jnp.where(mine, q_all, jnp.zeros_like(q_all))
        go_mine = jnp.where(mine, go_all, jnp.zeros_like(go_all))
        key_part = dot(q_mine, s_ref[...], 0, 0)
        value_part = dot(go_mine, p_ref[...], 0, 0)
        key_grad = key_part if key_grad is None else key_grad + key_part
        value_grad = value_part if value_grad is None else value_grad + value_part
    key_rows = (key_grad.T * HEAD_DIM ** (-0.5)).astype(bf16)
    value_rows = value_grad.T.astype(bf16)
    out_ref[whole, k_cols] = jnp.where(inside_all, key_rows, out_ref[whole, k_cols])
    out_ref[whole, v_cols] = jnp.where(inside_all, value_rows, out_ref[whole, v_cols])


def qkv_operands(projected, tile):
    group_rows, total = projected.shape
    lanes = min(128, total // 3)
    if lanes % 128 == 0:
        specs = [
            pl.BlockSpec((group_rows, lanes), functools.partial(lambda n, i, *_: (0, n), 3 * tile + n))
            for n in range(3)
        ]
        return [projected] * 3, specs
    parts = [projected[:, n * lanes : (n + 1) * lanes] for n in range(3)]
    return parts, [fixed((group_rows, lanes))] * 3


def attend_forward(projected, geometry):
    begin, code = geometry
    group_rows, total = projected.shape
    width = total // 3
    operands, specs = [], []
    for tile in range(width // min(128, width)):
        more, places = qkv_operands(projected, tile)
        operands += more
        specs += places
    return plain_call(
        attend_forward_kernel,
        shaped((group_rows, width), bf16),
        code,
        *operands,
        grid=begin.shape,
        in_specs=[fixed(code.shape)] + specs,
        scalars=(begin,),
        mebibytes=24,
        name="attention_forward",
    )


def attend_backward(projected, grad_group, geometry, tile, into):
    begin, code = geometry
    group_rows, total = projected.shape
    lanes = min(128, total // 3)
    operands, specs = qkv_operands(projected, tile)
    return plain_call(
        attend_backward_kernel,
        shaped((group_rows, total), bf16),
        code,
        *operands,
        grad_group,
        grid=begin.shape,
        in_specs=[fixed(code.shape)]
        + specs
        + [pl.BlockSpec((group_rows, lanes), lambda i, *_: (0, tile))],
        out_specs=pl.BlockSpec((group_rows, 3 * lanes), lambda i, *_: (0, tile)),
        scratch=[pltpu.VMEM((WINDOW, WINDOW), bf16)] * 2,
        scalars=(begin,),
        mebibytes=24,
        into=into,
        name="attention_backward",
    )


def attend_geometry(segments, live_mask):
    group_rows = segments.shape[0]
    numbers = jnp.arange(group_rows // PATCHES, dtype=jnp.int32)
    positions = jnp.arange(group_rows, dtype=jnp.int32)
    begin = jnp.min(
        jnp.where(segments[None, :] == numbers[:, None], positions[None, :], group_rows - PATCHES),
        axis=1,
    )
    code = jnp.where(live_mask == 1, segments, -1)
    return begin, jnp.broadcast_to(code[:, None], (group_rows, 128))


def plain_call(kernel, out_shape, *operands, grid=(), in_specs=None, out_specs=None, scratch=(), scalars=(), mebibytes=16, into=(), name=None):
    params = pltpu.CompilerParams(vmem_limit_bytes=mebibytes * 1024 * 1024)
    if in_specs is None:
        in_specs = [pl.BlockSpec(a.shape, functools.partial(lambda n, *_: (0,) * n, a.ndim)) for a in operands]
    in_specs = list(in_specs) + [pl.BlockSpec(memory_space=pl.ANY)] * len(into)
    if out_specs is None:
        out_specs = jax.tree.map(
            lambda s: pl.BlockSpec(s.shape, functools.partial(lambda n, *_: (0,) * n, len(s.shape))), out_shape
        )
    return pl.pallas_call(
        kernel,
        grid_spec=pltpu.PrefetchScalarGridSpec(
            num_scalar_prefetch=len(scalars),
            grid=grid,
            in_specs=in_specs,
            out_specs=out_specs,
            scratch_shapes=list(scratch),
        ),
        out_shape=out_shape,
        input_output_aliases={len(scalars) + len(operands) + n: n for n in range(len(into))},
        compiler_params=params,
        cost_estimate=SMALL,
        name=name,
    )(*scalars, *operands, *into)


def shaped(shape, dtype):
    return jax.ShapeDtypeStruct(tuple(shape), dtype)


def row_blocks(rows, *widths):
    return [pl.BlockSpec((rows, w), lambda i, *_: (i, 0)) for w in widths]


def fixed(shape):
    return pl.BlockSpec(tuple(shape), functools.partial(lambda n, *_: (0,) * n, len(shape)))


def pack_kernel(qkv_ref, proj_ref, up_ref, down_ref, qkv_out, up_out, down_out):
    count, _, width = qkv_ref.shape
    lanes = min(128, width)
    for n in range(count):
        for t in range(width // lanes):
            at = (count * t + n) * lanes
            qkv_out[:, at : at + lanes] = qkv_ref[n][:, t * lanes : (t + 1) * lanes].astype(bf16)
    qkv_out[:, count * width :] = proj_ref[...].T.astype(bf16)
    up_out[...] = up_ref[...].astype(bf16)
    down_out[...] = down_ref[...].T.astype(bf16)


def first_kernel(tok_ref, par_ref, low_out):
    normed, _, _ = norm_forward(tok_ref[...], par_ref[0:1, :], par_ref[1:2, :])
    low_out[...] = normed.astype(bf16)


def block_rows(block, slab):
    return pl.ds(pl.multiple_of(block * slab, slab), slab)


def stack_z(pieces, places):
    slab, width = pieces[0].shape

    def kernel(at_ref, *refs):
        for k, ref in enumerate(refs[:-1]):
            refs[-1][block_rows(lax.rem(at_ref[0] + k, N_Z), slab), :] = ref[...]

    return plain_call(
        kernel, shaped((N_Z * slab, width), bf16), *pieces, scalars=(places,), name="stack_z"
    )


def weave(columns, cuts, places):
    n_x = len(columns[0])
    rows, width = columns[0][0].shape
    slab = rows // N_Z
    flat = [half for column in columns for half in column]
    edges = [0, *cuts, width]
    sizes = [stop - start for start, stop in zip(edges[:-1], edges[1:])]

    def kernel(at_ref, *refs):
        outs = refs[len(flat) :]
        for y in range(len(columns)):
            for dx in range(n_x):
                half = refs[y * n_x + dx]
                x = lax.rem(at_ref[1] + dx, n_x)
                for z in range(N_Z):
                    at = block_rows(z * n_x + x, slab)
                    for out, start, size in zip(outs, edges, sizes):
                        out[at, y * size : (y + 1) * size] = half[
                            z * slab : (z + 1) * slab, start : start + size
                        ]

    out = plain_call(
        kernel,
        tuple(shaped((rows * n_x, size * len(columns)), bf16) for size in sizes),
        *flat,
        scalars=(places,),
        mebibytes=24,
        name="weave",
    )
    return out if cuts else out[0]


def proj_kernel(count, n_x, at_ref, *refs):
    blocks, parts = refs[:count], refs[count : 2 * count]
    tok_ref, par_ref, res_out, low_out, turned_out = refs[2 * count :]
    total = tok_ref[...]
    for block, part in zip(blocks, parts):
        total = total + dot(block[...], part[...], 1, 1)
    res_out[...] = total
    normed, _, _ = norm_forward(total, par_ref[2:3, :], par_ref[3:4, :])
    low_out[...] = normed.astype(bf16)
    turned = normed.T.astype(bf16)
    slab = turned.shape[0] // (N_Z * n_x)
    for z in range(N_Z):
        for x in range(n_x):
            dx = lax.rem(x - at_ref[1] + n_x, n_x)
            block = z * n_x + x
            turned_out[block_rows(dx * N_Z + z, slab), :] = turned[block * slab : (block + 1) * slab]


ERF_TOP = (
    -2.72614225801306e-10,
    2.77068142495902e-08,
    -2.10102402082508e-06,
    -5.69250639462346e-05,
    -7.34990630326855e-04,
    -2.95459980854025e-03,
    -1.60960333262415e-02,
)
ERF_LOW = (
    -1.45660718464996e-05,
    -2.13374055278905e-04,
    -1.68282697438203e-03,
    -7.37332916720468e-03,
    -1.42647390514189e-02,
)


def erf(value):
    value = jnp.clip(value, -4.0, 4.0)
    square = value * value
    top = jnp.full_like(square, ERF_TOP[0])
    for number in ERF_TOP[1:]:
        top = top * square + number
    low = jnp.full_like(square, ERF_LOW[0])
    for number in ERF_LOW[1:]:
        low = low * square + number
    inverse = pl.reciprocal(low, approx=True)
    inverse = inverse * (2.0 - low * inverse)
    return value * top * inverse


def up_kernel(low_ref, part_ref, *refs):
    act_out, slope_out = refs[-2:]
    hidden = dot(low_ref[...], part_ref[...], 1, 0)
    share = 0.5 * (1.0 + erf(hidden * 0.7071067811865476))
    act_out[...] = (hidden * share).astype(bf16)
    slope_out[...] = share + hidden * jnp.exp(-0.5 * hidden * hidden) * 0.3989422804014327


def up_call(low, part, block, blocks, into):
    rows, model = low.shape
    width = part.shape[1]
    steps = width // TILE
    cols = pl.BlockSpec((rows, TILE), lambda i, *_: (0, block * steps + i))
    return plain_call(
        up_kernel,
        (shaped((rows, width * blocks), bf16), shaped((rows, width * blocks), f32)),
        low,
        part,
        grid=(steps,),
        in_specs=[fixed(low.shape), pl.BlockSpec((model, TILE), lambda i, *_: (0, i))],
        out_specs=(cols, cols),
        into=into,
        name="up",
    )


def wide_kernel(count, each, *refs):
    total = None
    for n in range(count):
        for k in range(each):
            part = refs[count + n * each + k]
            size = part.shape[1]
            piece = dot(refs[n][:, k * size : (k + 1) * size], part[...], 1, 1)
            total = piece if total is None else total + piece
    refs[-1][...] = total.astype(refs[-1].dtype)


def wide_call(values, parts):
    rows = values[0].shape[0]
    model = parts[0].shape[0]
    return plain_call(
        functools.partial(wide_kernel, len(values), len(parts) // len(values)),
        shaped((rows, model), f32),
        *values,
        *parts,
        grid=(model // TILE,),
        in_specs=[fixed(value.shape) for value in values]
        + [pl.BlockSpec((TILE, part.shape[1]), lambda i, *_: (i, 0)) for part in parts],
        out_specs=pl.BlockSpec((rows, TILE), lambda i, *_: (0, i)),
        mebibytes=24,
        name="wide",
    )


def spread_kernel(count, low_ref, *refs):
    for part, out in zip(refs[:count], refs[count:]):
        out[...] = dot(low_ref[...], part[...], 1, 0).astype(bf16)


def spread_call(low, parts):
    return plain_call(
        functools.partial(spread_kernel, len(parts)),
        tuple(shaped((low.shape[0], part.shape[1]), bf16) for part in parts),
        low,
        *parts,
        name="spread",
    )


def down_kernel(count, *refs):
    base_ref, active, parts = refs[0], refs[1 : 1 + count], refs[1 + count : 1 + 2 * count]
    tea_ref, live_ref, count_ref, grad_out, low_out, turned_out, loss_out = refs[1 + 2 * count :]
    error = base_ref[...] - tea_ref[...]
    for act, part in zip(active, parts):
        error = error + dot(act[...], part[...], 1, 1)
    weighted = live_ref[...] * error
    grad = 2.0 * weighted / count_ref[...]
    grad_out[...] = grad
    low_out[...] = grad.astype(bf16)
    turned_out[...] = grad.T.astype(bf16)
    sums = jnp.sum(weighted * error, axis=0, keepdims=True)
    loss_out[...] = jnp.concatenate([sums, jnp.zeros((7, sums.shape[1]), f32)], axis=0)


def down_call(base, active, parts, teacher, live, live_count):
    rows, model = base.shape
    count = len(active)
    cols = pl.BlockSpec((rows, TILE), lambda i, *_: (0, i))
    return plain_call(
        functools.partial(down_kernel, count),
        (
            shaped(base.shape, f32),
            shaped(base.shape, bf16),
            shaped((model, rows), bf16),
            shaped((8, model), f32),
        ),
        base,
        *active,
        *parts,
        teacher,
        live,
        live_count,
        grid=(model // TILE,),
        in_specs=[cols]
        + [fixed(act.shape) for act in active]
        + [pl.BlockSpec((TILE, part.shape[1]), lambda i, *_: (i, 0)) for part in parts]
        + [cols, fixed(live.shape), fixed((1, 1))],
        out_specs=(
            cols,
            cols,
            pl.BlockSpec((TILE, rows), lambda i, *_: (i, 0)),
            pl.BlockSpec((8, TILE), lambda i, *_: (0, i)),
        ),
        mebibytes=28,
        name="down",
    )


def outer_kernel(splits, adds, *refs):
    piece = dot(refs[0][...], refs[1][...], 1, 0)
    if adds:
        piece = piece + refs[2][...].astype(f32)
    outs = refs[2 + adds :]
    if splits is None:
        outs[0][...] = piece.astype(bf16)
        return
    n_y, n_x, steps = splits
    depth = piece.shape[0] // n_x
    for y in range(n_y):

        @pl.when(pl.program_id(0) // steps == y)
        def _():
            for x in range(n_x):
                outs[y * n_x + x][...] = piece[x * depth : (x + 1) * depth].astype(bf16)


def outer_call(turned, values, received=(), splits=None):
    model, rows = turned.shape
    width = values.shape[1]
    cols = lambda n: pl.BlockSpec((n, TILE), lambda i, *_: (0, i))
    if splits is None:
        shapes, specs = shaped((model, width), bf16), cols(model)
    else:
        n_y, n_x = splits
        steps = width // n_y // TILE
        splits = (n_y, n_x, steps)
        shapes = (shaped((model // n_x, width // n_y), bf16),) * (n_x * n_y)
        specs = tuple(
            pl.BlockSpec(
                (model // n_x, TILE),
                functools.partial(lambda y, i, *_: (0, jnp.clip(i - y * steps, 0, steps - 1)), y),
            )
            for y in range(n_y)
            for _ in range(n_x)
        )
    return plain_call(
        functools.partial(outer_kernel, splits, len(received)),
        shapes,
        turned,
        values,
        *received,
        grid=(width // TILE,),
        in_specs=[fixed(turned.shape), cols(rows)] + [cols(model)] * len(received),
        out_specs=specs,
        name="outer",
    )


def norm_sums(grad, scaled, out_ref, first):
    sums = jnp.concatenate(
        [
            jnp.sum(grad * scaled, axis=0, keepdims=True),
            jnp.sum(grad, axis=0, keepdims=True),
            jnp.zeros((6, grad.shape[1]), f32),
        ],
        axis=0,
    )
    out_ref[...] = jnp.where(first, sums, out_ref[...] + sums)


def middle_kernel(grad_ref, res_ref, gout_ref, par_ref, full_out, low_out, sum_out):
    _, scaled, inverse = norm_forward(res_ref[...], par_ref[2:3, :], par_ref[3:4, :])
    grad = grad_ref[...]
    full = gout_ref[...] + norm_backward(grad, scaled, inverse, par_ref[2:3, :])
    full_out[...] = full
    low_out[...] = full.astype(bf16)
    norm_sums(grad, scaled, sum_out, pl.program_id(0) == 0)


def leave_kernel(count, *refs):
    own_ref, received = refs[0], refs[1 : 1 + count]
    tok_ref, res_ref, par_ref, two_ref, loss_ref, out_ref, sum_out, sum_ref = refs[1 + count :]
    _, scaled, inverse = norm_forward(tok_ref[...], par_ref[0:1, :], par_ref[1:2, :])
    grad = own_ref[...]
    for ref in received:
        grad = grad + ref[...].astype(f32)
    out_ref[...] = res_ref[...] + norm_backward(grad, scaled, inverse, par_ref[0:1, :])
    norm_sums(grad, scaled, sum_ref, pl.program_id(0) == 0)
    sum_out[...] = jnp.concatenate(
        [sum_ref[0:2, :], two_ref[0:2, :], loss_ref[0:1, :], jnp.zeros((3, grad.shape[1]), f32)],
        axis=0,
    )


def split_x_kernel(n_x, at_ref, qkv_ref, proj_ref, *outs):
    width = qkv_ref.shape[1]
    slab = qkv_ref.shape[0] // (N_Z * n_x)
    for dx in range(n_x):
        x = lax.rem(at_ref[1] + dx, n_x)
        for z in range(N_Z):
            at = block_rows(z * n_x + x, slab)
            rows = slice(z * slab, (z + 1) * slab)
            outs[dx][rows, :width] = qkv_ref[at, :]
            outs[dx][rows, width:] = proj_ref[at, :]


def split_z(parts, places):
    rows, width = parts[0].shape
    slab = rows // N_Z

    def kernel(at_ref, *refs):
        for k, out in enumerate(refs[len(parts) :]):
            at = block_rows(lax.rem(at_ref[0] + k, N_Z), slab)
            total = refs[0][at, :].astype(f32)
            for ref in refs[1 : len(parts)]:
                total = total + ref[at, :].astype(f32)
            out[...] = total.astype(out.dtype)

    shapes = (shaped((slab, width), f32),) + (shaped((slab, width), bf16),) * (N_Z - 1)
    return plain_call(kernel, shapes, *parts, scalars=(places,), name="split_z")


def adam_kernel(layout, pieces, *refs):
    grad = refs[0][...]
    for ref in refs[1:pieces]:
        grad = grad + ref[...].astype(f32)
    count = len(layout)
    states = refs[pieces : pieces + 3 * count]
    outs = refs[pieces + 3 * count :]
    for n, (start, size, turned) in enumerate(layout):
        weight, first, second = states[3 * n : 3 * n + 3]
        part = grad[:, start : start + size]
        if turned:
            part = part.T
        if len(weight.shape) == 3:
            matrices, _, width = weight.shape
            lanes = min(128, width)
            for k in range(matrices):
                own = [
                    part[:, (matrices * t + k) * lanes : (matrices * t + k + 1) * lanes]
                    for t in range(width // lanes)
                ]
                own = own[0] if len(own) == 1 else jnp.concatenate(own, axis=1)
                new = adam_step(weight[k], own, first[k], second[k], weight_decay, learn_rate)
                for out, value in zip(outs[3 * n : 3 * n + 3], new):
                    out[k] = value
        else:
            new = adam_step(weight[...], part, first[...], second[...], weight_decay, learn_rate)
            for out, value in zip(outs[3 * n : 3 * n + 3], new):
                out[...] = value


def adam_call(layout, pieces, *states):
    shapes = tuple(shaped(s.shape, f32) for s in states)
    out = plain_call(
        functools.partial(adam_kernel, layout, len(pieces)), shapes, *pieces, *states, name="adam"
    )
    return [out[3 * n : 3 * n + 3] for n in range(len(layout))]


def tie(*values):
    return lax.optimization_barrier(values)


def local(
    n_x,
    n_y,
    tokens,
    teacher,
    segments,
    live_mask,
    weight_qkv,
    weight_proj,
    weight_up,
    weight_down,
    norm_params,
    first_qkv,
    first_proj,
    first_up,
    first_down,
    first_norms,
    second_qkv,
    second_proj,
    second_up,
    second_down,
    second_norms,
):
    z_at, x_at = lax.axis_index("z"), lax.axis_index("x")
    y_at, core_at = lax.axis_index("y"), lax.axis_index("core")
    rows, model = tokens.shape
    group_rows = segments.shape[0]
    slab = weight_qkv.shape[1]
    width = weight_qkv.shape[2]
    unit = weight_up.shape[1]
    part_rows = min(128, rows)
    sizes = {"z": N_Z, "x": n_x, "y": n_y, "core": N_CORE}
    places = jnp.stack([z_at, x_at]).astype(jnp.int32)
    offsets = [(dc, dy) for dc in range(N_CORE) for dy in range(n_y)]
    other = N_CORE - 1

    def send(value, axis, step):
        size = sizes[axis]
        return lax.ppermute(value, axis, [(i, (i + step) % size) for i in range(size)])

    def send_col(value, dy, dc):
        perm = [
            (y * N_CORE + c, (y + dy) % n_y * N_CORE + (c + dc) % N_CORE)
            for y in range(n_y)
            for c in range(N_CORE)
        ]
        return lax.ppermute(value, ("y", "core"), perm)

    def fetch(value, axis):
        return [value] + [send(value, axis, -k) for k in range(1, sizes[axis])]

    def reduce_all(value, axes):
        for axis in axes:
            step = 1
            while step < sizes[axis]:
                pairs = [(i, i ^ step) for i in range(sizes[axis])]
                value = value + lax.ppermute(value, axis, pairs)
                step *= 2
        return value

    def place(dy, dc):
        return ((y_at + dy) % n_y * N_CORE + (core_at + dc) % N_CORE) * rows

    shard_qkv, shard_up, shard_down = plain_call(
        pack_kernel,
        (
            shaped((slab, 4 * width), bf16),
            shaped((slab, unit), bf16),
            shaped((slab, unit), bf16),
        ),
        weight_qkv,
        weight_proj,
        weight_up,
        weight_down,
        name="pack",
    )
    near_qkv = fetch(shard_qkv, "z")
    shards_down = fetch(shard_down, "y")
    low_one = plain_call(
        first_kernel,
        shaped(tokens.shape, bf16),
        tokens,
        norm_params,
        grid=(rows // part_rows,),
        in_specs=row_blocks(part_rows, model) + [fixed(norm_params.shape)],
        out_specs=row_blocks(part_rows, model)[0],
        name="first",
    )
    blocks_one = fetch(low_one, "y")
    near_qkv, shards_down, shard_up, blocks_one = tie(near_qkv, shards_down, shard_up, blocks_one)

    full_down = [lax.all_gather(jnp.concatenate(shards_down, axis=1), ("z", "x"), axis=0, tiled=True)]
    block_qkv = stack_z(near_qkv, places)
    near_one = jnp.concatenate(blocks_one, axis=0)
    near_one, block_qkv = tie(near_one, block_qkv)
    beside_qkv = fetch(block_qkv, "x")
    near_up = fetch(shard_up, "z")
    far_one = send(near_one, "core", -1)
    geometry = attend_geometry(segments, live_mask)
    own_live = lax.dynamic_slice_in_dim(
        live_mask, (y_at * N_CORE + core_at) * rows, rows, 0
    ).astype(f32)[:, None]
    beside_qkv, near_up, near_one, far_one, geometry, own_live = tie(
        beside_qkv, near_up, near_one, far_one, geometry, own_live
    )

    block_up = stack_z(near_up, places)
    full_qkv, part_proj = weave([beside_qkv], [3 * width], places)
    block_up, part_proj = tie(block_up, part_proj)
    beside_up = fetch(block_up, "x")
    across_up = fetch(block_up, "y")
    full_proj = fetch(part_proj, "y")
    group_one = jnp.zeros((group_rows, model), bf16)
    for n, (dc, dy) in enumerate(offsets):
        block = (far_one if dc else near_one)[dy * rows : (dy + 1) * rows]
        group_one = lax.dynamic_update_slice_in_dim(group_one, block, place(dy, dc), 0)
    projected = dot(group_one, full_qkv, 1, 0).astype(bf16)
    mixed = attend_forward(projected, geometry)
    mixed, beside_up, across_up, full_proj = tie(mixed, beside_up, across_up, full_proj)

    blocks_mixed = []
    for dc, dy in offsets:
        piece = lax.dynamic_slice_in_dim(mixed, place(-dy, -dc), rows, 0)
        blocks_mixed.append(piece if (dc, dy) == (0, 0) else send_col(piece, -dy, -dc))
    full_proj = full_proj + [send(part, "core", -1) for part in full_proj]
    full_up = {(0, 0): weave([beside_up], [], places)}
    blocks_mixed, full_proj, beside_up, across_up, full_up = tie(
        blocks_mixed, full_proj, beside_up, across_up, full_up
    )

    half = block_up.shape[0] // 2
    columns_up = [[across_up[dy]] for dy in range(1, n_y)]
    for dy in range(1, n_y):
        for dx in range(1, n_x):
            upper = send(beside_up[dx][:half], "y", -dy)
            lower = send(across_up[dy][half:], "x", -dx)
            columns_up[dy - 1].append((upper, lower))
    full_up[other, 0] = send(full_up[0, 0], "core", -1)
    count = len(offsets)
    residual, low_two, turned_two = plain_call(
        functools.partial(proj_kernel, count, n_x),
        (
            shaped(tokens.shape, f32),
            shaped(tokens.shape, bf16),
            shaped((model, rows), bf16),
        ),
        *blocks_mixed,
        *full_proj,
        tokens,
        norm_params,
        grid=(rows // part_rows,),
        in_specs=row_blocks(part_rows, *([width] * count))
        + [fixed((model, width))] * count
        + row_blocks(part_rows, model)
        + [fixed(norm_params.shape)],
        out_specs=tuple(row_blocks(part_rows, model, model))
        + (pl.BlockSpec((model, part_rows), lambda i, *_: (0, i)),),
        scalars=(places,),
        mebibytes=20,
        name="proj",
    )
    hidden = [up_call(low_two, full_up[0, 0], 0, n_y, ()), None]
    columns_up, hidden[0], low_two, full_up = tie(columns_up, hidden[0], low_two, full_up)

    for dy in range(1, n_y):
        column = [columns_up[dy - 1][0]] + [
            jnp.concatenate(pair, axis=0) for pair in columns_up[dy - 1][1:]
        ]
        full_up[0, dy] = weave([column], [], places)
        full_up[other, dy] = send(full_up[0, dy], "core", -1)
    hidden[other] = up_call(low_two, full_up[other, 0], 0, n_y, ())
    for dc in range(N_CORE):
        for dy in range(1, n_y):
            hidden[dc] = up_call(low_two, full_up[dc, dy], dy, n_y, hidden[dc])
        if dc == 0:
            hidden[0], full_down = tie(hidden[0], full_down)
            full_down = [full_down[0], send(full_down[0], "core", -1)]
    active, slope = zip(*hidden)
    live_count = reduce_all(jnp.sum(live_mask.astype(f32)), ("z", "x")).reshape(1, 1)
    grad_output, grad_branch, turned_branch, loss_rows = down_call(
        residual, active, full_down, teacher, own_live, live_count
    )

    sent_down = send(outer_call(turned_branch, active[other]), "core", 1)
    grad_hidden = [
        (dot(grad_branch, full_down[dc], 1, 0) * slope[dc]).astype(bf16) for dc in range(N_CORE)
    ]
    grad_two = wide_call(grad_hidden, [full_up[key] for key in offsets])
    grad_residual, grad_low, sums_two = plain_call(
        middle_kernel,
        (shaped(tokens.shape, f32), shaped(tokens.shape, bf16), shaped((8, model), f32)),
        grad_two,
        residual,
        grad_output,
        norm_params,
        grid=(rows // part_rows,),
        in_specs=row_blocks(part_rows, model, model, model) + [fixed(norm_params.shape)],
        out_specs=tuple(row_blocks(part_rows, model, model) + [fixed((8, model))]),
        name="middle",
    )
    pieces_attn = spread_call(grad_low, full_proj)
    pieces_attn, turned_branch, turned_two, grad_low, sent_down = tie(
        pieces_attn, turned_branch, turned_two, grad_low, sent_down
    )

    sent_attn = []
    for (dc, dy), piece in zip(offsets, pieces_attn):
        sent_attn.append(piece if (dc, dy) == (0, 0) else send_col(piece, dy, dc))
    hold_down = outer_call(turned_branch, active[0], (sent_down,))
    sent_up = send(outer_call(turned_two, grad_hidden[other]), "core", 1)
    grad_proj = [dot(grad_low, block, 0, 0).astype(bf16) for block in blocks_mixed]
    grad_group = jnp.zeros((group_rows, width), bf16)
    for (dc, dy), piece in zip(offsets, sent_attn):
        grad_group = lax.dynamic_update_slice_in_dim(grad_group, piece, place(-dy, -dc), 0)
    hold_up = outer_call(turned_two, grad_hidden[0], (sent_up,), splits=(n_y, n_x))
    hold_up = {(dy, dx): hold_up[dy * n_x + dx] for dy in range(n_y) for dx in range(n_x)}
    grad_group, hold_up, grad_proj, hold_down = tie(grad_group, hold_up, grad_proj, hold_down)
    reduced_down = lax.psum_scatter(hold_down, ("z", "x"), scatter_dimension=0, tiled=True)

    diagonal_up = {}
    for dy in range(1, n_y):
        for dx in range(1, n_x):
            upper = send(hold_up[dy, dx][:half], "y", dy)
            lower = send(hold_up[dy, dx][half:], "x", dx)
            diagonal_up[dy, dx] = (upper, lower)
    sent_proj = [send(grad_proj[n_y + dy], "core", 1) for dy in range(n_y)]
    tiles = width // min(128, width)
    grad_projected = attend_backward(projected, grad_group, geometry, 0, ())
    grad_projected, diagonal_up, sent_proj, hold_up = tie(
        grad_projected, diagonal_up, sent_proj, hold_up
    )

    def add_half(base, pieces, upper):
        top, low = base[:half].astype(f32), base[half:].astype(f32)
        for piece in pieces:
            if upper:
                top = top + piece[0].astype(f32)
            else:
                low = low + piece[1].astype(f32)
        return jnp.concatenate([top, low], axis=0).astype(bf16)

    next_x = [
        add_half(hold_up[0, dx], [diagonal_up[dy, dx] for dy in range(1, n_y)], True)
        for dx in range(1, n_x)
    ]
    next_y = [
        add_half(hold_up[dy, 0], [diagonal_up[dy, dx] for dx in range(1, n_x)], False)
        for dy in range(1, n_y)
    ]
    hold_proj = [
        (grad_proj[dy].astype(f32) + sent_proj[dy].astype(f32)).astype(bf16) for dy in range(n_y)
    ]
    next_x, next_y, hold_proj, grad_projected = tie(next_x, next_y, hold_proj, grad_projected)
    parts_up = [hold_up[0, 0]]
    parts_up += [send(part, "x", dx) for dx, part in enumerate(next_x, 1)]
    parts_up += [send(part, "y", dy) for dy, part in enumerate(next_y, 1)]
    part_proj = [hold_proj[0]] + [send(hold_proj[k], "y", k) for k in range(1, n_y)]
    for tile in range(1, tiles):
        grad_projected = attend_backward(
            projected, grad_group, geometry, tile, (grad_projected,)
        )
    grad_projected, parts_up, part_proj = tie(grad_projected, parts_up, part_proj)

    def spread_z(pieces):
        return [pieces[0]] + [send(pieces[k], "z", k) for k in range(1, N_Z)]

    pieces_up = split_z(parts_up, places)
    grad_qkv = dot(group_one, grad_projected, 0, 0).astype(bf16)
    total = part_proj[0].astype(f32)
    for piece in part_proj[1:]:
        total = total + piece.astype(f32)
    halves_qkv = plain_call(
        functools.partial(split_x_kernel, n_x),
        tuple(shaped((model // n_x, 4 * width), bf16) for _ in range(n_x)),
        grad_qkv,
        total.astype(bf16),
        scalars=(places,),
        name="split_x",
    )
    pieces_up, halves_qkv, grad_projected = tie(pieces_up, halves_qkv, grad_projected)
    last_up = spread_z(pieces_up)
    parts_qkv = [halves_qkv[0]] + [send(halves_qkv[dx], "x", dx) for dx in range(1, n_x)]
    parts = {
        key: dot(
            lax.dynamic_slice_in_dim(grad_projected, place(key[1], key[0]), rows, 0),
            full_qkv,
            1,
            1,
        )
        for key in reversed(offsets)
    }
    sent_one = send(
        jnp.concatenate([parts[other, dy].astype(bf16) for dy in range(n_y)], axis=0), "core", 1
    )
    parts = [
        parts[0, dy] + sent_one[dy * rows : (dy + 1) * rows].astype(f32) for dy in range(n_y)
    ]
    sent_parts = [parts[k].astype(bf16) for k in range(1, n_y)]
    parts_qkv, sent_parts, last_up, reduced_down = tie(parts_qkv, sent_parts, last_up, reduced_down)

    last_qkv = spread_z(split_z(parts_qkv, places))
    received = [send(part, "y", k) for k, part in enumerate(sent_parts, 1)]
    last_down = [reduced_down[:, :unit].astype(f32)]
    for k in range(1, n_y):
        last_down.append(send(reduced_down[:, k * unit : (k + 1) * unit], "y", k))
    last_up, received = tie(last_up, received)
    token_grad, sums = plain_call(
        functools.partial(leave_kernel, len(received)),
        (shaped(tokens.shape, f32), shaped((8, model), f32)),
        parts[0],
        *received,
        tokens,
        grad_residual,
        norm_params,
        sums_two,
        loss_rows,
        grid=(rows // part_rows,),
        in_specs=row_blocks(part_rows, *([model] * (3 + len(received))))
        + [fixed(norm_params.shape), fixed((8, model)), fixed((8, model))],
        out_specs=tuple(row_blocks(part_rows, model) + [fixed((8, model))]),
        scratch=[pltpu.VMEM((8, model), f32)],
        name="leave",
    )
    sums = reduce_all(sums, ("core", "y", "x", "z"))
    loss_sum = jnp.sum(sums[4])
    live_count = live_count[0, 0]

    (new_down,) = adam_call(
        [(0, weight_down.shape[0], True)], last_down, weight_down, first_down, second_down
    )
    (new_up,) = adam_call([(0, weight_up.shape[1], False)], last_up, weight_up, first_up, second_up)
    new_qkv, new_proj = adam_call(
        [(0, 3 * width, False), (3 * width, width, True)],
        last_qkv,
        weight_qkv,
        first_qkv,
        second_qkv,
        weight_proj,
        first_proj,
        second_proj,
    )
    new_norms = adam_step(norm_params, sums[:4], first_norms, second_norms, 0.0, norm_rate)
    return (
        loss_sum / live_count,
        token_grad,
        new_qkv[0],
        new_proj[0],
        new_up[0],
        new_down[0],
        new_norms[0],
        new_qkv[1],
        new_proj[1],
        new_up[1],
        new_down[1],
        new_norms[1],
        new_qkv[2],
        new_proj[2],
        new_up[2],
        new_down[2],
        new_norms[2],
    )


def solution(mesh):
    n_x = mesh.shape["row"] // N_Z
    n_y = mesh.shape["col"] // N_CORE
    mesh = jax.sharding.Mesh(
        mesh.devices.reshape(N_Z, n_x, n_y, N_CORE), ("z", "x", "y", "core")
    )
    row, col = ("z", "x"), ("y", "core")
    matrices = (P(None, row, col), P(col, row), P(row, col), P(col, row), P())
    tokens = P(row + col, None)
    return jax.shard_map(
        functools.partial(local, n_x, n_y),
        mesh=mesh,
        in_specs=(tokens, tokens, P(row), P(row)) + matrices * 3,
        out_specs=(P(), tokens) + matrices * 3,
        check_vma=False,
    )
```

```python
import functools

import jax
import jax.numpy as jnp
from jax import lax
from jax.experimental import pallas as pl
from jax.experimental.pallas import tpu as pltpu
from jax.sharding import PartitionSpec as P

HEAD_DIM = 64
PATCHES = 577
STEP = 10
WINDOW = 640
QROWS = 320
TILE = 256
DIGITS = 16
SMALL = pl.CostEstimate(flops=1024, bytes_accessed=1024, transcendentals=0)
N_Z = 4
N_CORE = 2

layer_eps = 1e-06
adam_eps = 1e-08
learn_rate = 0.03
norm_rate = 0.25
moment_decay = 0.5
weight_decay = 0.05

bf16 = jnp.bfloat16
f32 = jnp.float32


def norm_forward(values, gain_row, bias_row):
    average = jnp.mean(values, axis=-1, keepdims=True)
    centred = values - average
    variance = jnp.mean(centred * centred, axis=-1, keepdims=True)
    inverse = lax.rsqrt(variance + layer_eps)
    scaled = centred * inverse
    return (scaled * gain_row + bias_row, scaled, inverse)


def norm_backward(upstream, scaled, inverse, gain_row):
    weighted = upstream * gain_row
    return inverse * (
        weighted
        - jnp.mean(weighted, axis=-1, keepdims=True)
        - scaled * jnp.mean(weighted * scaled, axis=-1, keepdims=True)
    )


def gelu_slope(hidden):
    return (
        0.5 * (1.0 + lax.erf(hidden * 0.7071067811865476))
        + hidden * jnp.exp(-0.5 * hidden * hidden) * 0.3989422804014327
    )


def adam_step(weight, gradient, momentum, variance, decay_rate, rate):
    momentum = moment_decay * momentum + (1.0 - moment_decay) * gradient
    variance = moment_decay * variance + (1.0 - moment_decay) * gradient * gradient
    correction = 1.0 - moment_decay**STEP
    direction = momentum / correction / (jnp.sqrt(variance / correction) + adam_eps)
    return (weight - rate * (direction + decay_rate * weight), momentum, variance)


def dot(left, right, left_dim, right_dim):
    return lax.dot_general(
        left, right, (((left_dim,), (right_dim,)), ((), ())), preferred_element_type=f32
    )


def head_lanes(width, head):
    lanes = lax.broadcasted_iota(jnp.int32, (1, width), 1)
    return (lanes >= head * HEAD_DIM) & (lanes < (head + 1) * HEAD_DIM)


def attend_weights(q_part, k_all, bias, row_start, rows_in):
    scores = dot(q_part, k_all, 1, 1) * HEAD_DIM ** (-0.5)
    rows, window = scores.shape
    row_ids = row_start + lax.broadcasted_iota(jnp.int32, (rows, window), 0)
    col_ids = lax.broadcasted_iota(jnp.int32, (rows, window), 1)
    scores = jnp.where(row_ids == col_ids, scores, scores + bias)
    weights = jnp.exp(scores - jnp.max(scores, axis=-1, keepdims=True))
    totals = jnp.sum(weights, axis=-1, keepdims=True)
    return weights * jnp.where(rows_in, 1.0 / totals, 0.0)


def image_window(begin, code_ref, group_rows):
    image = pl.program_id(0)
    start = jnp.minimum(begin[image] // 16 * 16, group_rows - WINDOW)
    first = begin[image] - start
    start = pl.multiple_of(start, 16)
    code = code_ref[pl.ds(start, WINDOW), :]
    bias = jnp.where(code == image, 0.0, -1e30).astype(f32).T[0:1, :]
    return image, start, first, bias


def rows_inside(rows, row_start, first):
    ids = row_start + lax.broadcasted_iota(jnp.int32, (rows, 1), 0)
    return (ids >= first) & (ids < first + PATCHES)


def attend_forward_kernel(begin, code_ref, *refs):
    image, start, first, bias = image_window(begin, code_ref, refs[0].shape[0])
    out_ref = refs[-1]
    lanes = refs[0].shape[1]

    for tile in range((len(refs) - 1) // 3):
        q_ref, k_ref, v_ref = refs[3 * tile : 3 * tile + 3]
        cols = slice(tile * lanes, (tile + 1) * lanes)

        @pl.when(image == 0)
        def _():
            out_ref[:, cols] = v_ref[...]

        k_all = k_ref[pl.ds(start, WINDOW), :]
        v_all = v_ref[pl.ds(start, WINDOW), :]
        for row in range(0, WINDOW, QROWS):
            at = pl.ds(pl.multiple_of(start + row, 16), QROWS)
            q_part = q_ref[at, :]
            inside = rows_inside(QROWS, row, first)
            mixed = None
            for head in range(lanes // HEAD_DIM):
                mine = head_lanes(lanes, head)
                q_head = jnp.where(mine, q_part, jnp.zeros_like(q_part))
                weights = attend_weights(q_head, k_all, bias, row, inside).astype(bf16)
                part = dot(weights, v_all, 1, 0)
                mixed = part if mixed is None else jnp.where(mine, part, mixed)
            out_ref[at, cols] = jnp.where(inside, mixed.astype(bf16), out_ref[at, cols])


def attend_backward_kernel(blocks, begin, spots, code_ref, q_ref, k_ref, v_ref, *refs):
    image, start, first, bias = image_window(begin, code_ref, q_ref.shape[0])
    out_ref, p_ref, s_ref, go_ref = refs[-4:]
    lanes = q_ref.shape[1]
    rows = refs[0].shape[0]

    @pl.when(image == 0)
    def _():
        for n, block_ref in enumerate(refs[:blocks]):
            go_ref[pl.ds(pl.multiple_of(spots[n], rows), rows), :] = block_ref[...]
        out_ref[:, : 2 * lanes] = jnp.zeros((out_ref.shape[0], 2 * lanes), bf16)
        out_ref[:, 2 * lanes :] = go_ref[...]

    whole = pl.ds(start, WINDOW)
    inside_all = rows_inside(WINDOW, 0, first)
    q_cols, k_cols, v_cols = [slice(n * lanes, (n + 1) * lanes) for n in range(3)]
    k_all = k_ref[whole, :]
    v_all = v_ref[whole, :]
    q_all = q_ref[whole, :]
    go_all = go_ref[whole, :]
    key_grad = None
    value_grad = None
    for head in range(lanes // HEAD_DIM):
        mine = head_lanes(lanes, head)
        for row in range(0, WINDOW, QROWS):
            at = pl.ds(pl.multiple_of(start + row, 16), QROWS)
            q_part = q_ref[at, :]
            go_part = go_ref[at, :]
            inside = rows_inside(QROWS, row, first)
            q_head = jnp.where(mine, q_part, jnp.zeros_like(q_part))
            go_head = jnp.where(mine, go_part, jnp.zeros_like(go_part))
            weights = attend_weights(q_head, k_all, bias, row, inside)
            weight_grad = dot(go_head, v_all, 1, 1)
            product = weights * weight_grad
            score_grad = (
                product - weights * jnp.sum(product, axis=-1, keepdims=True)
            ).astype(bf16)
            p_ref[row : row + QROWS, :] = weights.astype(bf16)
            s_ref[row : row + QROWS, :] = score_grad
            query_grad = (dot(score_grad, k_all, 1, 0) * HEAD_DIM ** (-0.5)).astype(bf16)
            out_ref[at, q_cols] = jnp.where(inside & mine, query_grad, out_ref[at, q_cols])
        q_mine = jnp.where(mine, q_all, jnp.zeros_like(q_all))
        go_mine = jnp.where(mine, go_all, jnp.zeros_like(go_all))
        key_part = dot(q_mine, s_ref[...], 0, 0)
        value_part = dot(go_mine, p_ref[...], 0, 0)
        key_grad = key_part if key_grad is None else key_grad + key_part
        value_grad = value_part if value_grad is None else value_grad + value_part
    key_rows = (key_grad.T * HEAD_DIM ** (-0.5)).astype(bf16)
    value_rows = value_grad.T.astype(bf16)
    out_ref[whole, k_cols] = jnp.where(inside_all, key_rows, out_ref[whole, k_cols])
    out_ref[whole, v_cols] = jnp.where(inside_all, value_rows, out_ref[whole, v_cols])


def qkv_operands(projected, tile):
    group_rows, total = projected.shape
    lanes = min(128, total // 3)
    if lanes % 128 == 0:
        specs = [
            pl.BlockSpec((group_rows, lanes), functools.partial(lambda n, i, *_: (0, n), 3 * tile + n))
            for n in range(3)
        ]
        return [projected] * 3, specs
    parts = [projected[:, n * lanes : (n + 1) * lanes] for n in range(3)]
    return parts, [fixed((group_rows, lanes))] * 3


def attend_forward(projected, geometry):
    begin, code = geometry
    group_rows, total = projected.shape
    width = total // 3
    operands, specs = [], []
    for tile in range(width // min(128, width)):
        more, places = qkv_operands(projected, tile)
        operands += more
        specs += places
    return plain_call(
        attend_forward_kernel,
        shaped((group_rows, width), bf16),
        code,
        *operands,
        grid=begin.shape,
        in_specs=[fixed(code.shape)] + specs,
        scalars=(begin,),
        name="attention_forward",
    )


def attend_backward(projected, go_blocks, spots, geometry, tile, into):
    begin, code = geometry
    group_rows, total = projected.shape
    lanes = min(128, total // 3)
    operands, specs = qkv_operands(projected, tile)
    rows = go_blocks[0].shape[0]
    return plain_call(
        functools.partial(attend_backward_kernel, len(go_blocks)),
        shaped((group_rows, total), bf16),
        code,
        *operands,
        *go_blocks,
        grid=begin.shape,
        in_specs=[fixed(code.shape)]
        + specs
        + [pl.BlockSpec((rows, lanes), lambda i, *_: (0, tile))] * len(go_blocks),
        out_specs=pl.BlockSpec((group_rows, 3 * lanes), lambda i, *_: (0, tile)),
        scratch=[pltpu.VMEM((WINDOW, WINDOW), bf16)] * 2 + [pltpu.VMEM((group_rows, lanes), bf16)],
        scalars=(begin, spots),
        into=into,
        name="attention_backward",
    )


def attend_geometry(segments, live_mask):
    group_rows = segments.shape[0]
    numbers = jnp.arange(group_rows // PATCHES, dtype=jnp.int32)
    positions = jnp.arange(group_rows, dtype=jnp.int32)
    begin = jnp.min(
        jnp.where(segments[None, :] == numbers[:, None], positions[None, :], group_rows - PATCHES),
        axis=1,
    )
    code = jnp.where(live_mask == 1, segments, -1)
    return begin, jnp.broadcast_to(code[:, None], (group_rows, 128))


def plain_call(kernel, out_shape, *operands, grid=(), in_specs=None, out_specs=None, scratch=(), scalars=(), into=(), name=None):
    params = pltpu.CompilerParams(vmem_limit_bytes=60 * 1024 * 1024)
    if in_specs is None:
        in_specs = [pl.BlockSpec(a.shape, functools.partial(lambda n, *_: (0,) * n, a.ndim)) for a in operands]
    in_specs = list(in_specs) + [pl.BlockSpec(memory_space=pl.ANY)] * len(into)
    if out_specs is None:
        out_specs = jax.tree.map(
            lambda s: pl.BlockSpec(s.shape, functools.partial(lambda n, *_: (0,) * n, len(s.shape))), out_shape
        )
    return pl.pallas_call(
        kernel,
        grid_spec=pltpu.PrefetchScalarGridSpec(
            num_scalar_prefetch=len(scalars),
            grid=grid,
            in_specs=in_specs,
            out_specs=out_specs,
            scratch_shapes=list(scratch),
        ),
        out_shape=out_shape,
        input_output_aliases={len(scalars) + len(operands) + n: n for n in range(len(into))},
        compiler_params=params,
        cost_estimate=SMALL,
        name=name,
    )(*scalars, *operands, *into)


def shaped(shape, dtype):
    return jax.ShapeDtypeStruct(tuple(shape), dtype)


def row_blocks(rows, *widths):
    return [pl.BlockSpec((rows, w), lambda i, *_: (i, 0)) for w in widths]


def fixed(shape):
    return pl.BlockSpec(tuple(shape), functools.partial(lambda n, *_: (0,) * n, len(shape)))


def pack_kernel(live_ref, qkv_ref, proj_ref, up_ref, down_ref, qkv_out, up_out, down_out):
    count, slab, width = qkv_ref.shape
    lanes = min(128, width)
    for n in range(count):
        for t in range(width // lanes):
            at = (count * t + n) * lanes
            qkv_out[:, at : at + lanes] = qkv_ref[n][:, t * lanes : (t + 1) * lanes].astype(bf16)
    qkv_out[:, count * width :] = proj_ref[...].T.astype(bf16)
    up_out[:slab, :] = up_ref[...].astype(bf16)
    live = jnp.sum(jnp.sum(live_ref[...].astype(f32), axis=0, keepdims=True), axis=1, keepdims=True)
    high = jnp.floor(live * (1.0 / 256.0))
    middle = jnp.floor(live * (1.0 / 16.0)) - 16.0 * high
    low = live - 256.0 * high - 16.0 * middle
    row = lax.broadcasted_iota(jnp.int32, (DIGITS, up_out.shape[1]), 0)
    digits = jnp.where(row == 0, high, jnp.where(row == 1, middle, jnp.where(row == 2, low, 0.0)))
    up_out[slab:, :] = digits.astype(bf16)
    down_out[...] = down_ref[...].T.astype(bf16)


def first_kernel(tok_ref, par_ref, low_out):
    normed, _, _ = norm_forward(tok_ref[...], par_ref[0:1, :], par_ref[1:2, :])
    low_out[...] = normed.astype(bf16)


def block_rows(block, slab):
    return pl.ds(pl.multiple_of(block * slab, slab), slab)


def stack_z(pieces, slab, places):
    height, width = pieces[0].shape

    def kernel(at_ref, *refs):
        out = refs[-1]
        for k, ref in enumerate(refs[:-1]):
            out[block_rows(lax.rem(at_ref[0] + k, N_Z), slab), :] = ref[:slab, :]
        if height > slab:
            digits = refs[0][slab:, :].astype(f32)
            for ref in refs[1:-1]:
                digits = digits + ref[slab:, :].astype(f32)
            out[N_Z * slab :, :] = digits.astype(bf16)

    return plain_call(
        kernel,
        shaped(((N_Z - 1) * slab + height, width), bf16),
        *pieces,
        scalars=(places,),
        name="stack_z",
    )


def weave(columns, cuts, slab, places):
    n_x = len(columns[0])
    width = columns[0][0].shape[1]
    flat = [half for column in columns for half in column]
    edges = [0, *cuts, width]
    sizes = [stop - start for start, stop in zip(edges[:-1], edges[1:])]

    def kernel(at_ref, *refs):
        outs = refs[len(flat) :]
        for y in range(len(columns)):
            for dx in range(n_x):
                half = refs[y * n_x + dx]
                x = lax.rem(at_ref[1] + dx, n_x)
                for z in range(N_Z):
                    at = block_rows(z * n_x + x, slab)
                    for out, start, size in zip(outs, edges, sizes):
                        out[at, y * size : (y + 1) * size] = half[
                            z * slab : (z + 1) * slab, start : start + size
                        ]

    out = plain_call(
        kernel,
        tuple(shaped((N_Z * n_x * slab, size * len(columns)), bf16) for size in sizes),
        *flat,
        scalars=(places,),
        name="weave",
    )
    return out if cuts else out[0]


def proj_kernel(count, n_x, at_ref, *refs):
    blocks, parts = refs[:count], refs[count : 2 * count]
    tok_ref, par_ref, res_out, low_out, turned_out = refs[2 * count :]
    total = tok_ref[...]
    for block, part in zip(blocks, parts):
        total = total + dot(block[...], part[...], 1, 1)
    res_out[...] = total
    normed, _, _ = norm_forward(total, par_ref[2:3, :], par_ref[3:4, :])
    low_out[...] = normed.astype(bf16)
    turned = normed.T.astype(bf16)
    slab = turned.shape[0] // (N_Z * n_x)
    for z in range(N_Z):
        for x in range(n_x):
            dx = lax.rem(x - at_ref[1] + n_x, n_x)
            block = z * n_x + x
            turned_out[block_rows(dx * N_Z + z, slab), :] = turned[block * slab : (block + 1) * slab]


ERF_TOP = (
    -2.72614225801306e-10,
    2.77068142495902e-08,
    -2.10102402082508e-06,
    -5.69250639462346e-05,
    -7.34990630326855e-04,
    -2.95459980854025e-03,
    -1.60960333262415e-02,
)
ERF_LOW = (
    -1.45660718464996e-05,
    -2.13374055278905e-04,
    -1.68282697438203e-03,
    -7.37332916720468e-03,
    -1.42647390514189e-02,
)


def erf(value):
    value = jnp.clip(value, -4.0, 4.0)
    square = value * value
    top = jnp.full_like(square, ERF_TOP[0])
    for number in ERF_TOP[1:]:
        top = top * square + number
    low = jnp.full_like(square, ERF_LOW[0])
    for number in ERF_LOW[1:]:
        low = low * square + number
    inverse = pl.reciprocal(low, approx=True)
    inverse = inverse * (2.0 - low * inverse)
    return value * top * inverse


def up_kernel(low_ref, part_ref, *refs):
    act_out, slope_out = refs[-2:]
    hidden = dot(low_ref[...], part_ref[...], 1, 0)
    share = 0.5 * (1.0 + erf(hidden * 0.7071067811865476))
    act_out[...] = (hidden * share).astype(bf16)
    slope_out[...] = share + hidden * jnp.exp(-0.5 * hidden * hidden) * 0.3989422804014327


def up_call(low, part, block, blocks, into):
    rows, model = low.shape
    width = part.shape[1]
    steps = width // TILE
    cols = pl.BlockSpec((rows, TILE), lambda i, *_: (0, block * steps + i))
    return plain_call(
        up_kernel,
        (shaped((rows, width * blocks), bf16), shaped((rows, width * blocks), f32)),
        low,
        part,
        grid=(steps,),
        in_specs=[fixed(low.shape), pl.BlockSpec((model, TILE), lambda i, *_: (0, i))],
        out_specs=(cols, cols),
        into=into,
        name="up",
    )


def wide_kernel(count, each, *refs):
    refs[-1][...] = lane_blocks(refs[:count], refs[count:-1], each)


def wide_call(values, parts):
    rows = values[0].shape[0]
    model = parts[0].shape[0]
    return plain_call(
        functools.partial(wide_kernel, len(values), len(parts) // len(values)),
        shaped((rows, model), f32),
        *values,
        *parts,
        grid=(model // TILE,),
        in_specs=[fixed(value.shape) for value in values]
        + [pl.BlockSpec((TILE, part.shape[1]), lambda i, *_: (i, 0)) for part in parts],
        out_specs=pl.BlockSpec((rows, TILE), lambda i, *_: (0, i)),
        name="wide",
    )


def spread_kernel(count, low_ref, *refs):
    for part, out in zip(refs[:count], refs[count:]):
        out[...] = dot(low_ref[...], part[...], 1, 0).astype(bf16)


def spread_call(low, parts):
    return plain_call(
        functools.partial(spread_kernel, len(parts)),
        tuple(shaped((low.shape[0], part.shape[1]), bf16) for part in parts),
        low,
        *parts,
        name="spread",
    )


def lane_blocks(values, parts, each):
    total = None
    for n, part in enumerate(parts):
        size = part.shape[1]
        k = n % each
        piece = dot(values[n // each][:, k * size : (k + 1) * size], part[...], 1, 1)
        total = piece if total is None else total + piece
    return total


def down_kernel(count, each, *refs):
    base_ref, active, parts = refs[0], refs[1 : 1 + count], refs[1 + count : 1 + count + count * each]
    tea_ref, live_ref, count_ref, grad_out, low_out, turned_out, loss_out = refs[
        1 + count + count * each :
    ]
    error = base_ref[...] - tea_ref[...] + lane_blocks(active, parts, each)
    weighted = live_ref[...] * error
    grad = 2.0 * weighted / count_ref[...]
    grad_out[...] = grad
    low_out[...] = grad.astype(bf16)
    turned_out[...] = grad.T.astype(bf16)
    sums = jnp.sum(weighted * error, axis=0, keepdims=True)
    loss_out[...] = jnp.concatenate([sums, jnp.zeros((7, sums.shape[1]), f32)], axis=0)


def down_call(base, active, parts, teacher, live, live_count):
    rows, model = base.shape
    count = len(active)
    cols = pl.BlockSpec((rows, TILE), lambda i, *_: (0, i))
    return plain_call(
        functools.partial(down_kernel, count, len(parts) // count),
        (
            shaped(base.shape, f32),
            shaped(base.shape, bf16),
            shaped((model, rows), bf16),
            shaped((8, model), f32),
        ),
        base,
        *active,
        *parts,
        teacher,
        live,
        live_count,
        grid=(model // TILE,),
        in_specs=[cols]
        + [fixed(act.shape) for act in active]
        + [pl.BlockSpec((TILE, part.shape[1]), lambda i, *_: (i, 0)) for part in parts]
        + [cols, fixed(live.shape), fixed((1, 1))],
        out_specs=(
            cols,
            cols,
            pl.BlockSpec((TILE, rows), lambda i, *_: (i, 0)),
            pl.BlockSpec((8, TILE), lambda i, *_: (0, i)),
        ),
        name="down",
    )


def hidden_kernel(steps, low_ref, slope_ref, *refs):
    out_ref = refs[-1]
    for n, part in enumerate(refs[:-1]):

        @pl.when(pl.program_id(0) // steps == n)
        def _():
            out_ref[...] = (dot(low_ref[...], part[...], 1, 0) * slope_ref[...]).astype(bf16)


def hidden_call(low, slope, parts):
    rows, model = low.shape
    width = slope.shape[1]
    steps = width // len(parts) // TILE
    cols = pl.BlockSpec((rows, TILE), lambda i, *_: (0, i))
    return plain_call(
        functools.partial(hidden_kernel, steps),
        shaped((rows, width), bf16),
        low,
        slope,
        *parts,
        grid=(width // TILE,),
        in_specs=[fixed(low.shape), cols]
        + [
            pl.BlockSpec(
                (model, TILE),
                functools.partial(lambda n, i, *_: (0, jnp.clip(i - n * steps, 0, steps - 1)), n),
            )
            for n in range(len(parts))
        ],
        out_specs=cols,
        name="hidden",
    )


def outer_kernel(splits, adds, *refs):
    piece = dot(refs[0][...], refs[1][...], 1, 0)
    if adds:
        piece = piece + refs[2][...].astype(f32)
    outs = refs[2 + adds :]
    if splits is None:
        outs[0][...] = piece.astype(bf16)
        return
    n_y, n_x, steps = splits
    depth = piece.shape[0] // n_x
    for y in range(n_y):

        @pl.when(pl.program_id(0) // steps == y)
        def _():
            for x in range(n_x):
                outs[y * n_x + x][...] = piece[x * depth : (x + 1) * depth].astype(bf16)


def outer_call(turned, values, received=(), splits=None):
    model, rows = turned.shape
    width = values.shape[1]
    cols = lambda n: pl.BlockSpec((n, TILE), lambda i, *_: (0, i))
    if splits is None:
        shapes, specs = shaped((model, width), bf16), cols(model)
    else:
        n_y, n_x = splits
        steps = width // n_y // TILE
        splits = (n_y, n_x, steps)
        shapes = (shaped((model // n_x, width // n_y), bf16),) * (n_x * n_y)
        specs = tuple(
            pl.BlockSpec(
                (model // n_x, TILE),
                functools.partial(lambda y, i, *_: (0, jnp.clip(i - y * steps, 0, steps - 1)), y),
            )
            for y in range(n_y)
            for _ in range(n_x)
        )
    return plain_call(
        functools.partial(outer_kernel, splits, len(received)),
        shapes,
        turned,
        values,
        *received,
        grid=(width // TILE,),
        in_specs=[fixed(turned.shape), cols(rows)] + [cols(model)] * len(received),
        out_specs=specs,
        name="outer",
    )


def norm_sums(grad, scaled, out_ref, first):
    sums = jnp.concatenate(
        [
            jnp.sum(grad * scaled, axis=0, keepdims=True),
            jnp.sum(grad, axis=0, keepdims=True),
            jnp.zeros((6, grad.shape[1]), f32),
        ],
        axis=0,
    )
    out_ref[...] = jnp.where(first, sums, out_ref[...] + sums)


def middle_kernel(grad_ref, res_ref, gout_ref, par_ref, full_out, low_out, sum_out):
    _, scaled, inverse = norm_forward(res_ref[...], par_ref[2:3, :], par_ref[3:4, :])
    grad = grad_ref[...]
    full = gout_ref[...] + norm_backward(grad, scaled, inverse, par_ref[2:3, :])
    full_out[...] = full
    low_out[...] = full.astype(bf16)
    norm_sums(grad, scaled, sum_out, pl.program_id(0) == 0)


def leave_kernel(count, *refs):
    own_ref, received = refs[0], refs[1 : 1 + count]
    tok_ref, res_ref, par_ref, two_ref, loss_ref, out_ref, sum_out, sum_ref = refs[1 + count :]
    _, scaled, inverse = norm_forward(tok_ref[...], par_ref[0:1, :], par_ref[1:2, :])
    grad = own_ref[...]
    for ref in received:
        grad = grad + ref[...].astype(f32)
    out_ref[...] = res_ref[...] + norm_backward(grad, scaled, inverse, par_ref[0:1, :])
    norm_sums(grad, scaled, sum_ref, pl.program_id(0) == 0)
    sum_out[...] = jnp.concatenate(
        [sum_ref[0:2, :], two_ref[0:2, :], loss_ref[0:1, :], jnp.zeros((3, grad.shape[1]), f32)],
        axis=0,
    )


def split_x_kernel(n_x, at_ref, qkv_ref, proj_ref, *outs):
    width = qkv_ref.shape[1]
    slab = qkv_ref.shape[0] // (N_Z * n_x)
    for dx in range(n_x):
        x = lax.rem(at_ref[1] + dx, n_x)
        for z in range(N_Z):
            at = block_rows(z * n_x + x, slab)
            rows = slice(z * slab, (z + 1) * slab)
            outs[dx][rows, :width] = qkv_ref[at, :]
            outs[dx][rows, width:] = proj_ref[at, :]


def split_z(parts, places):
    rows, width = parts[0].shape
    slab = rows // N_Z

    def kernel(at_ref, *refs):
        for k, out in enumerate(refs[len(parts) :]):
            at = block_rows(lax.rem(at_ref[0] + k, N_Z), slab)
            total = refs[0][at, :].astype(f32)
            for ref in refs[1 : len(parts)]:
                total = total + ref[at, :].astype(f32)
            out[...] = total.astype(out.dtype)

    shapes = (shaped((slab, width), f32),) + (shaped((slab, width), bf16),) * (N_Z - 1)
    return plain_call(kernel, shapes, *parts, scalars=(places,), name="split_z")


def adam_kernel(layout, pieces, *refs):
    grad = refs[0][...]
    for ref in refs[1:pieces]:
        grad = grad + ref[...].astype(f32)
    count = len(layout)
    states = refs[pieces : pieces + 3 * count]
    outs = refs[pieces + 3 * count :]
    for n, (start, size, turned) in enumerate(layout):
        weight, first, second = states[3 * n : 3 * n + 3]
        part = grad[:, start : start + size]
        if turned:
            part = part.T
        if len(weight.shape) == 3:
            matrices, _, width = weight.shape
            lanes = min(128, width)
            for k in range(matrices):
                own = [
                    part[:, (matrices * t + k) * lanes : (matrices * t + k + 1) * lanes]
                    for t in range(width // lanes)
                ]
                own = own[0] if len(own) == 1 else jnp.concatenate(own, axis=1)
                new = adam_step(weight[k], own, first[k], second[k], weight_decay, learn_rate)
                for out, value in zip(outs[3 * n : 3 * n + 3], new):
                    out[k] = value
        else:
            new = adam_step(weight[...], part, first[...], second[...], weight_decay, learn_rate)
            for out, value in zip(outs[3 * n : 3 * n + 3], new):
                out[...] = value


def adam_call(layout, pieces, *states):
    shapes = tuple(shaped(s.shape, f32) for s in states)
    out = plain_call(
        functools.partial(adam_kernel, layout, len(pieces)), shapes, *pieces, *states, name="adam"
    )
    return [out[3 * n : 3 * n + 3] for n in range(len(layout))]


def tie(*values):
    return lax.optimization_barrier(values)


def local(
    n_x,
    n_y,
    tokens,
    teacher,
    segments,
    live_mask,
    weight_qkv,
    weight_proj,
    weight_up,
    weight_down,
    norm_params,
    first_qkv,
    first_proj,
    first_up,
    first_down,
    first_norms,
    second_qkv,
    second_proj,
    second_up,
    second_down,
    second_norms,
):
    z_at, x_at = lax.axis_index("z"), lax.axis_index("x")
    y_at, core_at = lax.axis_index("y"), lax.axis_index("core")
    rows, model = tokens.shape
    group_rows = segments.shape[0]
    slab = weight_qkv.shape[1]
    width = weight_qkv.shape[2]
    unit = weight_up.shape[1]
    part_rows = min(128, rows)
    depth = N_Z * slab
    sizes = {"z": N_Z, "x": n_x, "y": n_y, "core": N_CORE}
    places = jnp.stack([z_at, x_at]).astype(jnp.int32)
    offsets = [(dc, dy) for dc in range(N_CORE) for dy in range(n_y)]
    other = N_CORE - 1

    def send(value, axis, step):
        size = sizes[axis]
        return lax.ppermute(value, axis, [(i, (i + step) % size) for i in range(size)])

    def send_col(value, dy, dc):
        perm = [
            (y * N_CORE + c, (y + dy) % n_y * N_CORE + (c + dc) % N_CORE)
            for y in range(n_y)
            for c in range(N_CORE)
        ]
        return lax.ppermute(value, ("y", "core"), perm)

    def fetch(value, axis):
        return [value] + [send(value, axis, -k) for k in range(1, sizes[axis])]

    def reduce_all(value, axes):
        for axis in axes:
            step = 1
            while step < sizes[axis]:
                pairs = [(i, i ^ step) for i in range(sizes[axis])]
                value = value + lax.ppermute(value, axis, pairs)
                step *= 2
        return value

    def place(dy, dc):
        return ((y_at + dy) % n_y * N_CORE + (core_at + dc) % N_CORE) * rows

    shard_qkv, shard_up, shard_down = plain_call(
        pack_kernel,
        (
            shaped((slab, 4 * width), bf16),
            shaped((slab + DIGITS, unit), bf16),
            shaped((slab, unit), bf16),
        ),
        live_mask.reshape(-1, 128),
        weight_qkv,
        weight_proj,
        weight_up,
        weight_down,
        name="pack",
    )
    near_qkv = fetch(shard_qkv, "z")
    full_down = {(0, 0): lax.all_gather(shard_down, ("z", "x"), axis=0, tiled=True)}
    shards_down = fetch(shard_down, "y")
    low_one = plain_call(
        first_kernel,
        shaped(tokens.shape, bf16),
        tokens,
        norm_params,
        grid=(rows // part_rows,),
        in_specs=row_blocks(part_rows, model) + [fixed(norm_params.shape)],
        out_specs=row_blocks(part_rows, model)[0],
        name="first",
    )
    blocks_one = fetch(low_one, "y")
    near_qkv, shards_down, shard_up, blocks_one = tie(near_qkv, shards_down, shard_up, blocks_one)

    for dy in range(1, n_y):
        full_down[0, dy] = lax.all_gather(shards_down[dy], ("z", "x"), axis=0, tiled=True)
    block_qkv = stack_z(near_qkv, slab, places)
    near_one = jnp.concatenate(blocks_one, axis=0)
    near_one, block_qkv = tie(near_one, block_qkv)
    beside_qkv = fetch(block_qkv, "x")
    near_up = fetch(shard_up, "z")
    far_one = send(near_one, "core", -1)
    geometry = attend_geometry(segments, live_mask)
    own_live = lax.dynamic_slice_in_dim(
        live_mask, (y_at * N_CORE + core_at) * rows, rows, 0
    ).astype(f32)[:, None]
    beside_qkv, near_up, near_one, far_one, geometry, own_live, full_down[0, 0] = tie(
        beside_qkv, near_up, near_one, far_one, geometry, own_live, full_down[0, 0]
    )

    block_up = stack_z(near_up, slab, places)
    full_qkv, part_proj = weave([beside_qkv], [3 * width], slab, places)
    block_up, part_proj = tie(block_up, part_proj)
    beside_up = fetch(block_up, "x")
    across_up = fetch(block_up, "y")
    full_proj = fetch(part_proj, "y")
    full_down[other, 0] = send(full_down[0, 0], "core", -1)
    group_one = jnp.zeros((group_rows, model), bf16)
    for n, (dc, dy) in enumerate(offsets):
        block = (far_one if dc else near_one)[dy * rows : (dy + 1) * rows]
        group_one = lax.dynamic_update_slice_in_dim(group_one, block, place(dy, dc), 0)
    projected = dot(group_one, full_qkv, 1, 0).astype(bf16)
    mixed = attend_forward(projected, geometry)
    mixed, beside_up, across_up, full_proj, full_down[other, 0] = tie(
        mixed, beside_up, across_up, full_proj, full_down[other, 0]
    )

    blocks_mixed = []
    for dc, dy in offsets:
        piece = lax.dynamic_slice_in_dim(mixed, place(-dy, -dc), rows, 0)
        blocks_mixed.append(piece if (dc, dy) == (0, 0) else send_col(piece, -dy, -dc))
    full_proj = full_proj + [send(part, "core", -1) for part in full_proj]
    full_up = {(0, 0): weave([beside_up], [], slab, places)}
    live_count = sum(
        256.0 * part[depth, 0].astype(f32) + 16.0 * part[depth + 1, 0].astype(f32)
        + part[depth + 2, 0].astype(f32)
        for part in beside_up
    ).reshape(1, 1)
    blocks_mixed, full_proj, beside_up, across_up, full_up, full_down, live_count = tie(
        blocks_mixed, full_proj, beside_up, across_up, full_up, full_down, live_count
    )

    half = depth // 2
    columns_up = [[across_up[dy]] for dy in range(1, n_y)]
    for dy in range(1, n_y):
        for dx in range(1, n_x):
            upper = send(beside_up[dx][:half], "y", -dy)
            lower = send(across_up[dy][half:depth], "x", -dx)
            columns_up[dy - 1].append((upper, lower))
    full_up[other, 0] = send(full_up[0, 0], "core", -1)
    for dy in range(1, n_y):
        full_down[other, dy] = send(full_down[0, dy], "core", -1)
    count = len(offsets)
    residual, low_two, turned_two = plain_call(
        functools.partial(proj_kernel, count, n_x),
        (
            shaped(tokens.shape, f32),
            shaped(tokens.shape, bf16),
            shaped((model, rows), bf16),
        ),
        *blocks_mixed,
        *full_proj,
        tokens,
        norm_params,
        grid=(rows // part_rows,),
        in_specs=row_blocks(part_rows, *([width] * count))
        + [fixed((model, width))] * count
        + row_blocks(part_rows, model)
        + [fixed(norm_params.shape)],
        out_specs=tuple(row_blocks(part_rows, model, model))
        + (pl.BlockSpec((model, part_rows), lambda i, *_: (0, i)),),
        scalars=(places,),
        name="proj",
    )
    hidden = [up_call(low_two, full_up[0, 0], 0, n_y, ()), None]
    columns_up, hidden[0], low_two, full_up, full_down = tie(
        columns_up, hidden[0], low_two, full_up, full_down
    )

    for dy in range(1, n_y):
        column = [columns_up[dy - 1][0]] + [
            jnp.concatenate(pair, axis=0) for pair in columns_up[dy - 1][1:]
        ]
        full_up[0, dy] = weave([column], [], slab, places)
        full_up[other, dy] = send(full_up[0, dy], "core", -1)
    hidden[other] = up_call(low_two, full_up[other, 0], 0, n_y, ())
    for dc in range(N_CORE):
        for dy in range(1, n_y):
            hidden[dc] = up_call(low_two, full_up[dc, dy], dy, n_y, hidden[dc])
    active, slope = zip(*hidden)
    full_down = [[full_down[dc, dy] for dy in range(n_y)] for dc in range(N_CORE)]
    grad_output, grad_branch, turned_branch, loss_rows = down_call(
        residual, active, sum(full_down, []), teacher, own_live, live_count
    )

    grad_hidden = [
        hidden_call(grad_branch, slope[dc], full_down[dc]) for dc in range(N_CORE)
    ]
    grad_two = wide_call(grad_hidden, [full_up[key] for key in offsets])
    grad_residual, grad_low, sums_two = plain_call(
        middle_kernel,
        (shaped(tokens.shape, f32), shaped(tokens.shape, bf16), shaped((8, model), f32)),
        grad_two,
        residual,
        grad_output,
        norm_params,
        grid=(rows // part_rows,),
        in_specs=row_blocks(part_rows, model, model, model) + [fixed(norm_params.shape)],
        out_specs=tuple(row_blocks(part_rows, model, model) + [fixed((8, model))]),
        name="middle",
    )
    pieces_attn = spread_call(grad_low, full_proj)
    pieces_attn, turned_branch, turned_two, grad_low = tie(
        pieces_attn, turned_branch, turned_two, grad_low
    )

    sent_attn = [
        piece if key == (0, 0) else send_col(piece, key[1], key[0])
        for key, piece in zip(offsets, pieces_attn)
    ]
    spots = jnp.stack([place(-dy, -dc) for dc, dy in offsets]).astype(jnp.int32)
    sent_down = send(outer_call(turned_branch, active[other]), "core", 1)
    sent_up = send(outer_call(turned_two, grad_hidden[other]), "core", 1)
    sent_attn, sent_down, turned_branch = tie(sent_attn, sent_down, turned_branch)
    hold_down = outer_call(turned_branch, active[0], (sent_down,))
    hold_up = outer_call(turned_two, grad_hidden[0], (sent_up,), splits=(n_y, n_x))
    hold_up = {(dy, dx): hold_up[dy * n_x + dx] for dy in range(n_y) for dx in range(n_x)}
    sent_attn, hold_up, hold_down, grad_low = tie(sent_attn, hold_up, hold_down, grad_low)
    reduced_down = lax.psum_scatter(hold_down, ("z", "x"), scatter_dimension=0, tiled=True)

    diagonal_up = {}
    for dy in range(1, n_y):
        for dx in range(1, n_x):
            upper = send(hold_up[dy, dx][:half], "y", dy)
            lower = send(hold_up[dy, dx][half:], "x", dx)
            diagonal_up[dy, dx] = (upper, lower)
    tiles = width // min(128, width)
    grad_projected = attend_backward(projected, sent_attn, spots, geometry, 0, ())
    grad_projected, diagonal_up, hold_up, grad_low = tie(
        grad_projected, diagonal_up, hold_up, grad_low
    )

    def add_half(base, pieces, upper):
        top, low = base[:half].astype(f32), base[half:].astype(f32)
        for piece in pieces:
            if upper:
                top = top + piece[0].astype(f32)
            else:
                low = low + piece[1].astype(f32)
        return jnp.concatenate([top, low], axis=0).astype(bf16)

    next_x = [
        add_half(hold_up[0, dx], [diagonal_up[dy, dx] for dy in range(1, n_y)], True)
        for dx in range(1, n_x)
    ]
    next_y = [
        add_half(hold_up[dy, 0], [diagonal_up[dy, dx] for dx in range(1, n_x)], False)
        for dy in range(1, n_y)
    ]
    grad_proj = [dot(grad_low, block, 0, 0).astype(bf16) for block in blocks_mixed]
    next_x, next_y, grad_proj, grad_projected = tie(next_x, next_y, grad_proj, grad_projected)
    parts_up = [hold_up[0, 0]]
    parts_up += [send(part, "x", dx) for dx, part in enumerate(next_x, 1)]
    parts_up += [send(part, "y", dy) for dy, part in enumerate(next_y, 1)]
    sent_proj = [send(grad_proj[n_y + dy], "core", 1) for dy in range(n_y)]
    for tile in range(1, tiles):
        grad_projected = attend_backward(
            projected, sent_attn, spots, geometry, tile, (grad_projected,)
        )
    grad_projected, sent_proj = tie(grad_projected, sent_proj)
    hold_proj = [
        (grad_proj[dy].astype(f32) + sent_proj[dy].astype(f32)).astype(bf16) for dy in range(n_y)
    ]
    part_proj = [hold_proj[0]] + [send(hold_proj[k], "y", k) for k in range(1, n_y)]
    parts = {
        key: dot(
            lax.dynamic_slice_in_dim(grad_projected, place(key[1], key[0]), rows, 0),
            full_qkv,
            1,
            1,
        )
        for key in reversed(offsets)
    }
    sent_one = send(
        jnp.concatenate([parts[other, dy].astype(bf16) for dy in range(n_y)], axis=0), "core", 1
    )
    grad_qkv = dot(group_one, grad_projected, 0, 0).astype(bf16)
    parts_up, part_proj, sent_one, grad_qkv, parts = tie(
        parts_up, part_proj, sent_one, grad_qkv, parts
    )

    def spread_z(pieces):
        return [pieces[0]] + [send(pieces[k], "z", k) for k in range(1, N_Z)]

    pieces_up = split_z(parts_up, places)
    total = part_proj[0].astype(f32)
    for piece in part_proj[1:]:
        total = total + piece.astype(f32)
    halves_qkv = plain_call(
        functools.partial(split_x_kernel, n_x),
        tuple(shaped((model // n_x, 4 * width), bf16) for _ in range(n_x)),
        grad_qkv,
        total.astype(bf16),
        scalars=(places,),
        name="split_x",
    )
    parts = [
        parts[0, dy] + sent_one[dy * rows : (dy + 1) * rows].astype(f32) for dy in range(n_y)
    ]
    sent_parts = [parts[k].astype(bf16) for k in range(1, n_y)]
    pieces_up, halves_qkv, sent_parts = tie(pieces_up, halves_qkv, sent_parts)
    last_up = spread_z(pieces_up)
    parts_qkv = [halves_qkv[0]] + [send(halves_qkv[dx], "x", dx) for dx in range(1, n_x)]
    received = [send(part, "y", k) for k, part in enumerate(sent_parts, 1)]
    parts_qkv, received, last_up = tie(parts_qkv, received, last_up)

    last_qkv = spread_z(split_z(parts_qkv, places))
    last_down = [reduced_down[:, :unit].astype(f32)]
    for k in range(1, n_y):
        last_down.append(send(reduced_down[:, k * unit : (k + 1) * unit], "y", k))
    token_grad, sums = plain_call(
        functools.partial(leave_kernel, len(received)),
        (shaped(tokens.shape, f32), shaped((8, model), f32)),
        parts[0],
        *received,
        tokens,
        grad_residual,
        norm_params,
        sums_two,
        loss_rows,
        grid=(rows // part_rows,),
        in_specs=row_blocks(part_rows, *([model] * (3 + len(received))))
        + [fixed(norm_params.shape), fixed((8, model)), fixed((8, model))],
        out_specs=tuple(row_blocks(part_rows, model) + [fixed((8, model))]),
        scratch=[pltpu.VMEM((8, model), f32)],
        name="leave",
    )
    sums = reduce_all(sums, ("core", "y", "x", "z"))
    loss_sum = jnp.sum(sums[4])
    live_count = live_count[0, 0]

    (new_down,) = adam_call(
        [(0, weight_down.shape[0], True)], last_down, weight_down, first_down, second_down
    )
    (new_up,) = adam_call([(0, weight_up.shape[1], False)], last_up, weight_up, first_up, second_up)
    new_qkv, new_proj = adam_call(
        [(0, 3 * width, False), (3 * width, width, True)],
        last_qkv,
        weight_qkv,
        first_qkv,
        second_qkv,
        weight_proj,
        first_proj,
        second_proj,
    )
    new_norms = adam_step(norm_params, sums[:4], first_norms, second_norms, 0.0, norm_rate)
    return (
        loss_sum / live_count,
        token_grad,
        new_qkv[0],
        new_proj[0],
        new_up[0],
        new_down[0],
        new_norms[0],
        new_qkv[1],
        new_proj[1],
        new_up[1],
        new_down[1],
        new_norms[1],
        new_qkv[2],
        new_proj[2],
        new_up[2],
        new_down[2],
        new_norms[2],
    )


def solution(mesh):
    n_x = mesh.shape["row"] // N_Z
    n_y = mesh.shape["col"] // N_CORE
    mesh = jax.sharding.Mesh(
        mesh.devices.reshape(N_Z, n_x, n_y, N_CORE), ("z", "x", "y", "core")
    )
    row, col = ("z", "x"), ("y", "core")
    matrices = (P(None, row, col), P(col, row), P(row, col), P(col, row), P())
    tokens = P(row + col, None)
    return jax.shard_map(
        functools.partial(local, n_x, n_y),
        mesh=mesh,
        in_specs=(tokens, tokens, P(row), P(row)) + matrices * 3,
        out_specs=(P(), tokens) + matrices * 3,
        check_vma=False,
    )
```

```python
import functools

import jax
import jax.numpy as jnp
from jax import lax
from jax.experimental import pallas as pl
from jax.experimental.pallas import tpu as pltpu
from jax.sharding import PartitionSpec as P

HEAD_DIM = 64
PATCHES = 577
STEP = 10
WINDOW = 640
QROWS = 320
TILE = 256
DIGITS = 16
SMALL = pl.CostEstimate(flops=1024, bytes_accessed=1024, transcendentals=0)
N_Z = 4
N_CORE = 2

layer_eps = 1e-06
adam_eps = 1e-08
learn_rate = 0.03
norm_rate = 0.25
moment_decay = 0.5
weight_decay = 0.05

bf16 = jnp.bfloat16
f32 = jnp.float32


def norm_forward(values, gain_row, bias_row):
    average = jnp.mean(values, axis=-1, keepdims=True)
    centred = values - average
    variance = jnp.mean(centred * centred, axis=-1, keepdims=True)
    inverse = lax.rsqrt(variance + layer_eps)
    scaled = centred * inverse
    return (scaled * gain_row + bias_row, scaled, inverse)


def norm_backward(upstream, scaled, inverse, gain_row):
    weighted = upstream * gain_row
    return inverse * (
        weighted
        - jnp.mean(weighted, axis=-1, keepdims=True)
        - scaled * jnp.mean(weighted * scaled, axis=-1, keepdims=True)
    )


def gelu_slope(hidden):
    return (
        0.5 * (1.0 + lax.erf(hidden * 0.7071067811865476))
        + hidden * jnp.exp(-0.5 * hidden * hidden) * 0.3989422804014327
    )


def adam_step(weight, gradient, momentum, variance, decay_rate, rate):
    momentum = moment_decay * momentum + (1.0 - moment_decay) * gradient
    variance = moment_decay * variance + (1.0 - moment_decay) * gradient * gradient
    correction = 1.0 - moment_decay**STEP
    direction = momentum / correction / (jnp.sqrt(variance / correction) + adam_eps)
    return (weight - rate * (direction + decay_rate * weight), momentum, variance)


def dot(left, right, left_dim, right_dim):
    return lax.dot_general(
        left, right, (((left_dim,), (right_dim,)), ((), ())), preferred_element_type=f32
    )


def head_lanes(width, head):
    lanes = lax.broadcasted_iota(jnp.int32, (1, width), 1)
    return (lanes >= head * HEAD_DIM) & (lanes < (head + 1) * HEAD_DIM)


def attend_weights(q_part, k_all, bias, row_start, rows_in):
    scores = dot(q_part, k_all, 1, 1) * HEAD_DIM ** (-0.5)
    rows, window = scores.shape
    row_ids = row_start + lax.broadcasted_iota(jnp.int32, (rows, window), 0)
    col_ids = lax.broadcasted_iota(jnp.int32, (rows, window), 1)
    scores = jnp.where(row_ids == col_ids, scores, scores + bias)
    weights = jnp.exp(scores - jnp.max(scores, axis=-1, keepdims=True))
    totals = jnp.sum(weights, axis=-1, keepdims=True)
    return weights * jnp.where(rows_in, 1.0 / totals, 0.0)


def image_window(begin, code_ref, group_rows):
    image = pl.program_id(0)
    start = jnp.minimum(begin[image] // 16 * 16, group_rows - WINDOW)
    first = begin[image] - start
    start = pl.multiple_of(start, 16)
    code = code_ref[pl.ds(start, WINDOW), :]
    bias = jnp.where(code == image, 0.0, -1e30).astype(f32).T[0:1, :]
    return image, start, first, bias


def rows_inside(rows, row_start, first):
    ids = row_start + lax.broadcasted_iota(jnp.int32, (rows, 1), 0)
    return (ids >= first) & (ids < first + PATCHES)


def attend_forward_kernel(begin, code_ref, *refs):
    image, start, first, bias = image_window(begin, code_ref, refs[0].shape[0])
    out_ref = refs[-1]
    lanes = refs[0].shape[1]

    for tile in range((len(refs) - 1) // 3):
        q_ref, k_ref, v_ref = refs[3 * tile : 3 * tile + 3]
        cols = slice(tile * lanes, (tile + 1) * lanes)

        @pl.when(image == 0)
        def _():
            out_ref[:, cols] = v_ref[...]

        k_all = k_ref[pl.ds(start, WINDOW), :]
        v_all = v_ref[pl.ds(start, WINDOW), :]
        for row in range(0, WINDOW, QROWS):
            at = pl.ds(pl.multiple_of(start + row, 16), QROWS)
            q_part = q_ref[at, :]
            inside = rows_inside(QROWS, row, first)
            mixed = None
            for head in range(lanes // HEAD_DIM):
                mine = head_lanes(lanes, head)
                q_head = jnp.where(mine, q_part, jnp.zeros_like(q_part))
                weights = attend_weights(q_head, k_all, bias, row, inside).astype(bf16)
                part = dot(weights, v_all, 1, 0)
                mixed = part if mixed is None else jnp.where(mine, part, mixed)
            out_ref[at, cols] = jnp.where(inside, mixed.astype(bf16), out_ref[at, cols])


def attend_backward_kernel(blocks, begin, spots, code_ref, q_ref, k_ref, v_ref, *refs):
    image, start, first, bias = image_window(begin, code_ref, q_ref.shape[0])
    out_ref, p_ref, s_ref, go_ref = refs[-4:]
    lanes = q_ref.shape[1]
    rows = refs[0].shape[0]

    @pl.when(image == 0)
    def _():
        for n, block_ref in enumerate(refs[:blocks]):
            go_ref[pl.ds(pl.multiple_of(spots[n], rows), rows), :] = block_ref[...]
        out_ref[:, : 2 * lanes] = jnp.zeros((out_ref.shape[0], 2 * lanes), bf16)
        out_ref[:, 2 * lanes :] = go_ref[...]

    whole = pl.ds(start, WINDOW)
    inside_all = rows_inside(WINDOW, 0, first)
    q_cols, k_cols, v_cols = [slice(n * lanes, (n + 1) * lanes) for n in range(3)]
    k_all = k_ref[whole, :]
    v_all = v_ref[whole, :]
    q_all = q_ref[whole, :]
    go_all = go_ref[whole, :]
    key_grad = None
    value_grad = None
    for head in range(lanes // HEAD_DIM):
        mine = head_lanes(lanes, head)
        for row in range(0, WINDOW, QROWS):
            at = pl.ds(pl.multiple_of(start + row, 16), QROWS)
            q_part = q_ref[at, :]
            go_part = go_ref[at, :]
            inside = rows_inside(QROWS, row, first)
            q_head = jnp.where(mine, q_part, jnp.zeros_like(q_part))
            go_head = jnp.where(mine, go_part, jnp.zeros_like(go_part))
            weights = attend_weights(q_head, k_all, bias, row, inside)
            weight_grad = dot(go_head, v_all, 1, 1)
            product = weights * weight_grad
            score_grad = (
                product - weights * jnp.sum(product, axis=-1, keepdims=True)
            ).astype(bf16)
            p_ref[row : row + QROWS, :] = weights.astype(bf16)
            s_ref[row : row + QROWS, :] = score_grad
            query_grad = (dot(score_grad, k_all, 1, 0) * HEAD_DIM ** (-0.5)).astype(bf16)
            out_ref[at, q_cols] = jnp.where(inside & mine, query_grad, out_ref[at, q_cols])
        q_mine = jnp.where(mine, q_all, jnp.zeros_like(q_all))
        go_mine = jnp.where(mine, go_all, jnp.zeros_like(go_all))
        key_part = dot(q_mine, s_ref[...], 0, 0)
        value_part = dot(go_mine, p_ref[...], 0, 0)
        key_grad = key_part if key_grad is None else key_grad + key_part
        value_grad = value_part if value_grad is None else value_grad + value_part
    key_rows = (key_grad.T * HEAD_DIM ** (-0.5)).astype(bf16)
    value_rows = value_grad.T.astype(bf16)
    out_ref[whole, k_cols] = jnp.where(inside_all, key_rows, out_ref[whole, k_cols])
    out_ref[whole, v_cols] = jnp.where(inside_all, value_rows, out_ref[whole, v_cols])


def qkv_operands(projected, tile):
    group_rows, total = projected.shape
    lanes = min(128, total // 3)
    if lanes % 128 == 0:
        specs = [
            pl.BlockSpec((group_rows, lanes), functools.partial(lambda n, i, *_: (0, n), 3 * tile + n))
            for n in range(3)
        ]
        return [projected] * 3, specs
    parts = [projected[:, n * lanes : (n + 1) * lanes] for n in range(3)]
    return parts, [fixed((group_rows, lanes))] * 3


def attend_forward(projected, geometry):
    begin, code = geometry
    group_rows, total = projected.shape
    width = total // 3
    operands, specs = [], []
    for tile in range(width // min(128, width)):
        more, places = qkv_operands(projected, tile)
        operands += more
        specs += places
    return plain_call(
        attend_forward_kernel,
        shaped((group_rows, width), bf16),
        code,
        *operands,
        grid=begin.shape,
        in_specs=[fixed(code.shape)] + specs,
        scalars=(begin,),
        mebibytes=20,
        name="attention_forward",
    )


def attend_backward(projected, go_blocks, spots, geometry, tile, into):
    begin, code = geometry
    group_rows, total = projected.shape
    lanes = min(128, total // 3)
    operands, specs = qkv_operands(projected, tile)
    rows = go_blocks[0].shape[0]
    return plain_call(
        functools.partial(attend_backward_kernel, len(go_blocks)),
        shaped((group_rows, total), bf16),
        code,
        *operands,
        *go_blocks,
        grid=begin.shape,
        in_specs=[fixed(code.shape)]
        + specs
        + [pl.BlockSpec((rows, lanes), lambda i, *_: (0, tile))] * len(go_blocks),
        out_specs=pl.BlockSpec((group_rows, 3 * lanes), lambda i, *_: (0, tile)),
        scratch=[pltpu.VMEM((WINDOW, WINDOW), bf16)] * 2 + [pltpu.VMEM((group_rows, lanes), bf16)],
        scalars=(begin, spots),
        into=into,
        mebibytes=20,
        name="attention_backward",
    )


def attend_geometry(segments, live_mask):
    group_rows = segments.shape[0]
    numbers = jnp.arange(group_rows // PATCHES, dtype=jnp.int32)
    positions = jnp.arange(group_rows, dtype=jnp.int32)
    begin = jnp.min(
        jnp.where(segments[None, :] == numbers[:, None], positions[None, :], group_rows - PATCHES),
        axis=1,
    )
    code = jnp.where(live_mask == 1, segments, -1)
    return begin, jnp.broadcast_to(code[:, None], (group_rows, 128))


def plain_call(kernel, out_shape, *operands, grid=(), in_specs=None, out_specs=None, scratch=(), scalars=(), into=(), mebibytes=16, name=None):
    params = pltpu.CompilerParams(vmem_limit_bytes=mebibytes * 1024 * 1024)
    if in_specs is None:
        in_specs = [pl.BlockSpec(a.shape, functools.partial(lambda n, *_: (0,) * n, a.ndim)) for a in operands]
    in_specs = list(in_specs) + [pl.BlockSpec(memory_space=pl.ANY)] * len(into)
    if out_specs is None:
        out_specs = jax.tree.map(
            lambda s: pl.BlockSpec(s.shape, functools.partial(lambda n, *_: (0,) * n, len(s.shape))), out_shape
        )
    return pl.pallas_call(
        kernel,
        grid_spec=pltpu.PrefetchScalarGridSpec(
            num_scalar_prefetch=len(scalars),
            grid=grid,
            in_specs=in_specs,
            out_specs=out_specs,
            scratch_shapes=list(scratch),
        ),
        out_shape=out_shape,
        input_output_aliases={len(scalars) + len(operands) + n: n for n in range(len(into))},
        compiler_params=params,
        cost_estimate=SMALL,
        name=name,
    )(*scalars, *operands, *into)


def shaped(shape, dtype):
    return jax.ShapeDtypeStruct(tuple(shape), dtype)


def row_blocks(rows, *widths):
    return [pl.BlockSpec((rows, w), lambda i, *_: (i, 0)) for w in widths]


def fixed(shape):
    return pl.BlockSpec(tuple(shape), functools.partial(lambda n, *_: (0,) * n, len(shape)))


def pack_kernel(live_ref, qkv_ref, proj_ref, up_ref, down_ref, qkv_out, up_out, down_out):
    count, slab, width = qkv_ref.shape
    lanes = min(128, width)
    for n in range(count):
        for t in range(width // lanes):
            at = (count * t + n) * lanes
            qkv_out[:, at : at + lanes] = qkv_ref[n][:, t * lanes : (t + 1) * lanes].astype(bf16)
    qkv_out[:, count * width :] = proj_ref[...].T.astype(bf16)
    up_out[:slab, :] = up_ref[...].astype(bf16)
    live = jnp.sum(jnp.sum(live_ref[...].astype(f32), axis=0, keepdims=True), axis=1, keepdims=True)
    high = jnp.floor(live * (1.0 / 256.0))
    middle = jnp.floor(live * (1.0 / 16.0)) - 16.0 * high
    low = live - 256.0 * high - 16.0 * middle
    row = lax.broadcasted_iota(jnp.int32, (DIGITS, up_out.shape[1]), 0)
    digits = jnp.where(row == 0, high, jnp.where(row == 1, middle, jnp.where(row == 2, low, 0.0)))
    up_out[slab:, :] = digits.astype(bf16)
    down_out[...] = down_ref[...].T.astype(bf16)


def first_kernel(tok_ref, par_ref, low_out):
    normed, _, _ = norm_forward(tok_ref[...], par_ref[0:1, :], par_ref[1:2, :])
    low_out[...] = normed.astype(bf16)


def block_rows(block, slab):
    return pl.ds(pl.multiple_of(block * slab, slab), slab)


def stack_z(pieces, slab, places):
    height, width = pieces[0].shape

    def kernel(at_ref, *refs):
        out = refs[-1]
        for k, ref in enumerate(refs[:-1]):
            out[block_rows(lax.rem(at_ref[0] + k, N_Z), slab), :] = ref[:slab, :]
        if height > slab:
            digits = refs[0][slab:, :].astype(f32)
            for ref in refs[1:-1]:
                digits = digits + ref[slab:, :].astype(f32)
            out[N_Z * slab :, :] = digits.astype(bf16)

    return plain_call(
        kernel,
        shaped(((N_Z - 1) * slab + height, width), bf16),
        *pieces,
        scalars=(places,),
        mebibytes=6,
        name="stack_z",
    )


def weave(columns, cuts, slab, places):
    n_x = len(columns[0])
    width = columns[0][0].shape[1]
    flat = [half for column in columns for half in column]
    edges = [0, *cuts, width]
    sizes = [stop - start for start, stop in zip(edges[:-1], edges[1:])]

    def kernel(at_ref, *refs):
        outs = refs[len(flat) :]
        for y in range(len(columns)):
            for dx in range(n_x):
                half = refs[y * n_x + dx]
                x = lax.rem(at_ref[1] + dx, n_x)
                for z in range(N_Z):
                    at = block_rows(z * n_x + x, slab)
                    for out, start, size in zip(outs, edges, sizes):
                        out[at, y * size : (y + 1) * size] = half[
                            z * slab : (z + 1) * slab, start : start + size
                        ]

    out = plain_call(
        kernel,
        tuple(shaped((N_Z * n_x * slab, size * len(columns)), bf16) for size in sizes),
        *flat,
        scalars=(places,),
        mebibytes=12,
        name="weave",
    )
    return out if cuts else out[0]


def proj_kernel(count, n_x, at_ref, *refs):
    blocks, parts = refs[:count], refs[count : 2 * count]
    tok_ref, par_ref, res_out, low_out, turned_out = refs[2 * count :]
    total = tok_ref[...]
    for block, part in zip(blocks, parts):
        total = total + dot(block[...], part[...], 1, 1)
    res_out[...] = total
    normed, _, _ = norm_forward(total, par_ref[2:3, :], par_ref[3:4, :])
    low_out[...] = normed.astype(bf16)
    turned = normed.T.astype(bf16)
    slab = turned.shape[0] // (N_Z * n_x)
    for z in range(N_Z):
        for x in range(n_x):
            dx = lax.rem(x - at_ref[1] + n_x, n_x)
            block = z * n_x + x
            turned_out[block_rows(dx * N_Z + z, slab), :] = turned[block * slab : (block + 1) * slab]


ERF_TOP = (
    -2.72614225801306e-10,
    2.77068142495902e-08,
    -2.10102402082508e-06,
    -5.69250639462346e-05,
    -7.34990630326855e-04,
    -2.95459980854025e-03,
    -1.60960333262415e-02,
)
ERF_LOW = (
    -1.45660718464996e-05,
    -2.13374055278905e-04,
    -1.68282697438203e-03,
    -7.37332916720468e-03,
    -1.42647390514189e-02,
)


def erf(value):
    value = jnp.clip(value, -4.0, 4.0)
    square = value * value
    top = jnp.full_like(square, ERF_TOP[0])
    for number in ERF_TOP[1:]:
        top = top * square + number
    low = jnp.full_like(square, ERF_LOW[0])
    for number in ERF_LOW[1:]:
        low = low * square + number
    inverse = pl.reciprocal(low, approx=True)
    inverse = inverse * (2.0 - low * inverse)
    return value * top * inverse


def up_kernel(low_ref, part_ref, *refs):
    act_out, slope_out = refs[-2:]
    hidden = dot(low_ref[...], part_ref[...], 1, 0)
    share = 0.5 * (1.0 + erf(hidden * 0.7071067811865476))
    act_out[...] = (hidden * share).astype(bf16)
    slope_out[...] = share + hidden * jnp.exp(-0.5 * hidden * hidden) * 0.3989422804014327


def up_call(low, part, block, blocks, into):
    rows, model = low.shape
    width = part.shape[1]
    steps = width // TILE
    cols = pl.BlockSpec((rows, TILE), lambda i, *_: (0, block * steps + i))
    return plain_call(
        up_kernel,
        (shaped((rows, width * blocks), bf16), shaped((rows, width * blocks), f32)),
        low,
        part,
        grid=(steps,),
        in_specs=[fixed(low.shape), pl.BlockSpec((model, TILE), lambda i, *_: (0, i))],
        out_specs=(cols, cols),
        into=into,
        mebibytes=14,
        name="up",
    )


def wide_kernel(count, each, *refs):
    refs[-1][...] = lane_blocks(refs[:count], refs[count:-1], each)


def wide_call(values, parts):
    rows = values[0].shape[0]
    model = parts[0].shape[0]
    return plain_call(
        functools.partial(wide_kernel, len(values), len(parts) // len(values)),
        shaped((rows, model), f32),
        *values,
        *parts,
        grid=(model // TILE,),
        in_specs=[fixed(value.shape) for value in values]
        + [pl.BlockSpec((TILE, part.shape[1]), lambda i, *_: (i, 0)) for part in parts],
        out_specs=pl.BlockSpec((rows, TILE), lambda i, *_: (0, i)),
        mebibytes=20,
        name="wide",
    )


def spread_kernel(count, low_ref, *refs):
    for part, out in zip(refs[:count], refs[count:]):
        out[...] = dot(low_ref[...], part[...], 1, 0).astype(bf16)


def spread_call(low, parts):
    return plain_call(
        functools.partial(spread_kernel, len(parts)),
        tuple(shaped((low.shape[0], part.shape[1]), bf16) for part in parts),
        low,
        *parts,
        mebibytes=12,
        name="spread",
    )


def lane_blocks(values, parts, each):
    total = None
    for n, part in enumerate(parts):
        size = part.shape[1]
        k = n % each
        piece = dot(values[n // each][:, k * size : (k + 1) * size], part[...], 1, 1)
        total = piece if total is None else total + piece
    return total


def down_kernel(count, each, *refs):
    base_ref, active, parts = refs[0], refs[1 : 1 + count], refs[1 + count : 1 + count + count * each]
    tea_ref, live_ref, count_ref, grad_out, low_out, turned_out, loss_out = refs[
        1 + count + count * each :
    ]
    error = base_ref[...] - tea_ref[...] + lane_blocks(active, parts, each)
    weighted = live_ref[...] * error
    grad = 2.0 * weighted / count_ref[...]
    grad_out[...] = grad
    low_out[...] = grad.astype(bf16)
    turned_out[...] = grad.T.astype(bf16)
    sums = jnp.sum(weighted * error, axis=0, keepdims=True)
    loss_out[...] = jnp.concatenate([sums, jnp.zeros((7, sums.shape[1]), f32)], axis=0)


def down_call(base, active, parts, teacher, live, live_count):
    rows, model = base.shape
    count = len(active)
    cols = pl.BlockSpec((rows, TILE), lambda i, *_: (0, i))
    return plain_call(
        functools.partial(down_kernel, count, len(parts) // count),
        (
            shaped(base.shape, f32),
            shaped(base.shape, bf16),
            shaped((model, rows), bf16),
            shaped((8, model), f32),
        ),
        base,
        *active,
        *parts,
        teacher,
        live,
        live_count,
        grid=(model // TILE,),
        in_specs=[cols]
        + [fixed(act.shape) for act in active]
        + [pl.BlockSpec((TILE, part.shape[1]), lambda i, *_: (i, 0)) for part in parts]
        + [cols, fixed(live.shape), fixed((1, 1))],
        out_specs=(
            cols,
            cols,
            pl.BlockSpec((TILE, rows), lambda i, *_: (i, 0)),
            pl.BlockSpec((8, TILE), lambda i, *_: (0, i)),
        ),
        mebibytes=24,
        name="down",
    )


def hidden_kernel(steps, low_ref, slope_ref, *refs):
    out_ref = refs[-1]
    for n, part in enumerate(refs[:-1]):

        @pl.when(pl.program_id(0) // steps == n)
        def _():
            out_ref[...] = (dot(low_ref[...], part[...], 1, 0) * slope_ref[...]).astype(bf16)


def hidden_call(low, slope, parts):
    rows, model = low.shape
    width = slope.shape[1]
    steps = width // len(parts) // TILE
    cols = pl.BlockSpec((rows, TILE), lambda i, *_: (0, i))
    return plain_call(
        functools.partial(hidden_kernel, steps),
        shaped((rows, width), bf16),
        low,
        slope,
        *parts,
        grid=(width // TILE,),
        in_specs=[fixed(low.shape), cols]
        + [
            pl.BlockSpec(
                (model, TILE),
                functools.partial(lambda n, i, *_: (0, jnp.clip(i - n * steps, 0, steps - 1)), n),
            )
            for n in range(len(parts))
        ],
        out_specs=cols,
        mebibytes=14,
        name="hidden",
    )


def outer_kernel(splits, adds, *refs):
    piece = dot(refs[0][...], refs[1][...], 1, 0)
    if adds:
        piece = piece + refs[2][...].astype(f32)
    outs = refs[2 + adds :]
    if splits is None:
        outs[0][...] = piece.astype(bf16)
        return
    n_y, n_x, steps = splits
    depth = piece.shape[0] // n_x
    for y in range(n_y):

        @pl.when(pl.program_id(0) // steps == y)
        def _():
            for x in range(n_x):
                outs[y * n_x + x][...] = piece[x * depth : (x + 1) * depth].astype(bf16)


def outer_call(turned, values, received=(), splits=None):
    model, rows = turned.shape
    width = values.shape[1]
    cols = lambda n: pl.BlockSpec((n, TILE), lambda i, *_: (0, i))
    if splits is None:
        shapes, specs = shaped((model, width), bf16), cols(model)
    else:
        n_y, n_x = splits
        steps = width // n_y // TILE
        splits = (n_y, n_x, steps)
        shapes = (shaped((model // n_x, width // n_y), bf16),) * (n_x * n_y)
        specs = tuple(
            pl.BlockSpec(
                (model // n_x, TILE),
                functools.partial(lambda y, i, *_: (0, jnp.clip(i - y * steps, 0, steps - 1)), y),
            )
            for y in range(n_y)
            for _ in range(n_x)
        )
    return plain_call(
        functools.partial(outer_kernel, splits, len(received)),
        shapes,
        turned,
        values,
        *received,
        grid=(width // TILE,),
        in_specs=[fixed(turned.shape), cols(rows)] + [cols(model)] * len(received),
        out_specs=specs,
        mebibytes=14,
        name="outer",
    )


def norm_sums(grad, scaled, out_ref, first):
    sums = jnp.concatenate(
        [
            jnp.sum(grad * scaled, axis=0, keepdims=True),
            jnp.sum(grad, axis=0, keepdims=True),
            jnp.zeros((6, grad.shape[1]), f32),
        ],
        axis=0,
    )
    out_ref[...] = jnp.where(first, sums, out_ref[...] + sums)


def middle_kernel(grad_ref, res_ref, gout_ref, par_ref, full_out, low_out, sum_out):
    _, scaled, inverse = norm_forward(res_ref[...], par_ref[2:3, :], par_ref[3:4, :])
    grad = grad_ref[...]
    full = gout_ref[...] + norm_backward(grad, scaled, inverse, par_ref[2:3, :])
    full_out[...] = full
    low_out[...] = full.astype(bf16)
    norm_sums(grad, scaled, sum_out, pl.program_id(0) == 0)


def leave_kernel(count, *refs):
    own_ref, received = refs[0], refs[1 : 1 + count]
    tok_ref, res_ref, par_ref, two_ref, loss_ref, out_ref, sum_out, sum_ref = refs[1 + count :]
    _, scaled, inverse = norm_forward(tok_ref[...], par_ref[0:1, :], par_ref[1:2, :])
    grad = own_ref[...]
    for ref in received:
        grad = grad + ref[...].astype(f32)
    out_ref[...] = res_ref[...] + norm_backward(grad, scaled, inverse, par_ref[0:1, :])
    norm_sums(grad, scaled, sum_ref, pl.program_id(0) == 0)
    sum_out[...] = jnp.concatenate(
        [sum_ref[0:2, :], two_ref[0:2, :], loss_ref[0:1, :], jnp.zeros((3, grad.shape[1]), f32)],
        axis=0,
    )


def split_x(parts, n_x, places):
    model = parts[0].shape[0]
    slab = model // (N_Z * n_x)
    total = sum(part.shape[1] for part in parts)

    def kernel(at_ref, *refs):
        outs = refs[len(parts) :]
        for dx in range(n_x):
            x = lax.rem(at_ref[1] + dx, n_x)
            for z in range(N_Z):
                at = block_rows(z * n_x + x, slab)
                lane = 0
                for ref in refs[: len(parts)]:
                    size = ref.shape[1]
                    outs[dx][z * slab : (z + 1) * slab, lane : lane + size] = ref[at, :]
                    lane += size

    return plain_call(
        kernel,
        tuple(shaped((model // n_x, total), bf16) for _ in range(n_x)),
        *parts,
        scalars=(places,),
        mebibytes=10,
        name="split_x",
    )


def sum_in_order(pieces, spots):
    def kernel(spot_ref, *refs):
        out, held = refs[-2:]
        for n, ref in enumerate(refs[:-2]):
            held[spot_ref[n]] = ref[...]
        total = held[0]
        for n in range(1, len(pieces)):
            total = total + held[n]
        out[...] = total

    return plain_call(
        kernel,
        shaped(pieces[0].shape, f32),
        *pieces,
        scalars=(spots,),
        scratch=[pltpu.VMEM((len(pieces),) + pieces[0].shape, f32)],
        mebibytes=6,
        name="sum_in_order",
    )


def split_z(parts, places):
    rows, width = parts[0].shape
    slab = rows // N_Z

    def kernel(at_ref, *refs):
        for k, out in enumerate(refs[len(parts) :]):
            at = block_rows(lax.rem(at_ref[0] + k, N_Z), slab)
            total = refs[0][at, :].astype(f32)
            for ref in refs[1 : len(parts)]:
                total = total + ref[at, :].astype(f32)
            out[...] = total.astype(out.dtype)

    shapes = (shaped((slab, width), f32),) + (shaped((slab, width), bf16),) * (N_Z - 1)
    return plain_call(kernel, shapes, *parts, scalars=(places,), mebibytes=8, name="split_z")


def adam_kernel(layout, pieces, *refs):
    grad = refs[0][...]
    for ref in refs[1:pieces]:
        grad = grad + ref[...].astype(f32)
    count = len(layout)
    states = refs[pieces : pieces + 3 * count]
    outs = refs[pieces + 3 * count :]
    for n, (start, size, turned) in enumerate(layout):
        weight, first, second = states[3 * n : 3 * n + 3]
        if len(weight.shape) == 3:
            matrices = weight.shape[0]
            lanes = size // matrices
            for k in range(matrices):
                own = [grad[:, at + k * lanes : at + (k + 1) * lanes] for at in start]
                own = own[0] if len(own) == 1 else jnp.concatenate(own, axis=1)
                new = adam_step(weight[k], own, first[k], second[k], weight_decay, learn_rate)
                for out, value in zip(outs[3 * n : 3 * n + 3], new):
                    out[k] = value
        else:
            part = grad[:, start : start + size]
            if turned:
                part = part.T
            new = adam_step(weight[...], part, first[...], second[...], weight_decay, learn_rate)
            for out, value in zip(outs[3 * n : 3 * n + 3], new):
                out[...] = value


def adam_call(layout, pieces, *states):
    shapes = tuple(shaped(s.shape, f32) for s in states)
    out = plain_call(
        functools.partial(adam_kernel, layout, len(pieces)), shapes, *pieces, *states, mebibytes=14, name="adam"
    )
    return [out[3 * n : 3 * n + 3] for n in range(len(layout))]


def tie(*values):
    return lax.optimization_barrier(values)


def local(
    n_x,
    n_y,
    tokens,
    teacher,
    segments,
    live_mask,
    weight_qkv,
    weight_proj,
    weight_up,
    weight_down,
    norm_params,
    first_qkv,
    first_proj,
    first_up,
    first_down,
    first_norms,
    second_qkv,
    second_proj,
    second_up,
    second_down,
    second_norms,
):
    z_at, x_at = lax.axis_index("z"), lax.axis_index("x")
    y_at, core_at = lax.axis_index("y"), lax.axis_index("core")
    rows, model = tokens.shape
    group_rows = segments.shape[0]
    slab = weight_qkv.shape[1]
    width = weight_qkv.shape[2]
    unit = weight_up.shape[1]
    part_rows = min(128, rows)
    depth = N_Z * slab
    sizes = {"z": N_Z, "x": n_x, "y": n_y, "core": N_CORE}
    places = jnp.stack([z_at, x_at]).astype(jnp.int32)
    offsets = [(dc, dy) for dc in range(N_CORE) for dy in range(n_y)]
    other = N_CORE - 1

    def send(value, axis, step):
        size = sizes[axis]
        return lax.ppermute(value, axis, [(i, (i + step) % size) for i in range(size)])

    def send_col(value, dy, dc):
        perm = [
            (y * N_CORE + c, (y + dy) % n_y * N_CORE + (c + dc) % N_CORE)
            for y in range(n_y)
            for c in range(N_CORE)
        ]
        return lax.ppermute(value, ("y", "core"), perm)

    def fetch(value, axis):
        return [value] + [send(value, axis, -k) for k in range(1, sizes[axis])]

    def place(dy, dc):
        return ((y_at + dy) % n_y * N_CORE + (core_at + dc) % N_CORE) * rows

    shard_qkv, shard_up, shard_down = plain_call(
        pack_kernel,
        (
            shaped((slab, 4 * width), bf16),
            shaped((slab + DIGITS, unit), bf16),
            shaped((slab, unit), bf16),
        ),
        live_mask.reshape(-1, 128),
        weight_qkv,
        weight_proj,
        weight_up,
        weight_down,
        mebibytes=8,
        name="pack",
    )
    near_qkv = fetch(shard_qkv, "z")
    full_down = {(0, 0): lax.all_gather(shard_down, ("z", "x"), axis=0, tiled=True)}
    shards_down = fetch(shard_down, "y")
    low_one = plain_call(
        first_kernel,
        shaped(tokens.shape, bf16),
        tokens,
        norm_params,
        grid=(rows // part_rows,),
        in_specs=row_blocks(part_rows, model) + [fixed(norm_params.shape)],
        out_specs=row_blocks(part_rows, model)[0],
        mebibytes=8,
        name="first",
    )
    blocks_one = fetch(low_one, "y")
    near_qkv, shards_down, shard_up, blocks_one = tie(near_qkv, shards_down, shard_up, blocks_one)

    for dy in range(1, n_y):
        full_down[0, dy] = lax.all_gather(shards_down[dy], ("z", "x"), axis=0, tiled=True)
    block_qkv = stack_z(near_qkv, slab, places)
    near_one = jnp.concatenate(blocks_one, axis=0)
    near_one, block_qkv = tie(near_one, block_qkv)
    beside_qkv = fetch(block_qkv, "x")
    near_up = fetch(shard_up, "z")
    far_one = send(near_one, "core", -1)
    geometry = attend_geometry(segments, live_mask)
    own_live = lax.dynamic_slice_in_dim(
        live_mask, (y_at * N_CORE + core_at) * rows, rows, 0
    ).astype(f32)[:, None]
    beside_qkv, near_up, near_one, far_one, geometry, own_live, full_down[0, 0] = tie(
        beside_qkv, near_up, near_one, far_one, geometry, own_live, full_down[0, 0]
    )

    block_up = stack_z(near_up, slab, places)
    full_qkv, part_proj = weave([beside_qkv], [3 * width], slab, places)
    block_up, part_proj = tie(block_up, part_proj)
    beside_up = fetch(block_up, "x")
    across_up = fetch(block_up, "y")
    full_proj = fetch(part_proj, "y")
    full_down[other, 0] = send(full_down[0, 0], "core", -1)
    group_one = jnp.zeros((group_rows, model), bf16)
    for n, (dc, dy) in enumerate(offsets):
        block = (far_one if dc else near_one)[dy * rows : (dy + 1) * rows]
        group_one = lax.dynamic_update_slice_in_dim(group_one, block, place(dy, dc), 0)
    projected = dot(group_one, full_qkv, 1, 0).astype(bf16)
    mixed = attend_forward(projected, geometry)
    mixed, beside_up, across_up, full_proj, full_down[other, 0] = tie(
        mixed, beside_up, across_up, full_proj, full_down[other, 0]
    )

    blocks_mixed = []
    for dc, dy in offsets:
        piece = lax.dynamic_slice_in_dim(mixed, place(-dy, -dc), rows, 0)
        blocks_mixed.append(piece if (dc, dy) == (0, 0) else send_col(piece, -dy, -dc))
    full_proj = full_proj + [send(part, "core", -1) for part in full_proj]
    full_up = {(0, 0): weave([beside_up], [], slab, places)}
    live_count = sum(
        256.0 * part[depth, 0].astype(f32) + 16.0 * part[depth + 1, 0].astype(f32)
        + part[depth + 2, 0].astype(f32)
        for part in beside_up
    ).reshape(1, 1)
    blocks_mixed, full_proj, beside_up, across_up, full_up, full_down, live_count = tie(
        blocks_mixed, full_proj, beside_up, across_up, full_up, full_down, live_count
    )

    columns_up = [[across_up[dy]] for dy in range(1, n_y)]
    for dx in range(1, n_x):
        for dy, part in enumerate(fetch(beside_up[dx], "y")[1:], 1):
            columns_up[dy - 1].append(part)
    full_up[other, 0] = send(full_up[0, 0], "core", -1)
    for dy in range(1, n_y):
        full_down[other, dy] = send(full_down[0, dy], "core", -1)
    count = len(offsets)
    residual, low_two, turned_two = plain_call(
        functools.partial(proj_kernel, count, n_x),
        (
            shaped(tokens.shape, f32),
            shaped(tokens.shape, bf16),
            shaped((model, rows), bf16),
        ),
        *blocks_mixed,
        *full_proj,
        tokens,
        norm_params,
        grid=(rows // part_rows,),
        in_specs=row_blocks(part_rows, *([width] * count))
        + [fixed((model, width))] * count
        + row_blocks(part_rows, model)
        + [fixed(norm_params.shape)],
        out_specs=tuple(row_blocks(part_rows, model, model))
        + (pl.BlockSpec((model, part_rows), lambda i, *_: (0, i)),),
        scalars=(places,),
        mebibytes=16,
        name="proj",
    )
    hidden = [up_call(low_two, full_up[0, 0], 0, n_y, ()), None]
    columns_up, hidden[0], low_two, full_up, full_down = tie(
        columns_up, hidden[0], low_two, full_up, full_down
    )

    for dy in range(1, n_y):
        full_up[0, dy] = weave([columns_up[dy - 1]], [], slab, places)
        full_up[other, dy] = send(full_up[0, dy], "core", -1)
    hidden[other] = up_call(low_two, full_up[other, 0], 0, n_y, ())
    for dc in range(N_CORE):
        for dy in range(1, n_y):
            hidden[dc] = up_call(low_two, full_up[dc, dy], dy, n_y, hidden[dc])
    active, slope = zip(*hidden)
    full_down = [[full_down[dc, dy] for dy in range(n_y)] for dc in range(N_CORE)]
    grad_output, grad_branch, turned_branch, loss_rows = down_call(
        residual, active, sum(full_down, []), teacher, own_live, live_count
    )

    half = depth // 2
    sent_down = send(outer_call(turned_branch, active[other]), "core", 1)
    grad_hidden = [hidden_call(grad_branch, slope[dc], full_down[dc]) for dc in range(N_CORE)]
    grad_hidden, sent_down = tie(grad_hidden, sent_down)
    hold_down = outer_call(turned_branch, active[0], (sent_down,), splits=(n_y, 1))
    grad_hidden, hold_down = tie(grad_hidden, hold_down)
    reduced_down = [
        lax.psum_scatter(part, ("z", "x"), scatter_dimension=0, tiled=True) for part in hold_down
    ]

    grad_two = wide_call(grad_hidden, [full_up[key] for key in offsets])
    grad_residual, grad_low, sums_two = plain_call(
        middle_kernel,
        (shaped(tokens.shape, f32), shaped(tokens.shape, bf16), shaped((8, model), f32)),
        grad_two,
        residual,
        grad_output,
        norm_params,
        grid=(rows // part_rows,),
        in_specs=row_blocks(part_rows, model, model, model) + [fixed(norm_params.shape)],
        out_specs=tuple(row_blocks(part_rows, model, model) + [fixed((8, model))]),
        mebibytes=14,
        name="middle",
    )
    pieces_attn = spread_call(grad_low, full_proj)
    pieces_attn, turned_two, grad_low = tie(pieces_attn, turned_two, grad_low)

    sent_attn = [
        piece if key == (0, 0) else send_col(piece, key[1], key[0])
        for key, piece in zip(offsets, pieces_attn)
    ]
    spots = jnp.stack([place(-dy, -dc) for dc, dy in offsets]).astype(jnp.int32)
    far_up = outer_call(turned_two, grad_hidden[other])
    grad_proj = [dot(grad_low, block, 0, 0).astype(bf16) for block in blocks_mixed]
    sent_attn, far_up, grad_proj = tie(sent_attn, far_up, grad_proj)

    sent_up = send(far_up, "core", 1)
    sent_proj = [send(grad_proj[n_y + dy], "core", 1) for dy in range(n_y)]
    sent_up, sent_proj = tie(sent_up, sent_proj)
    hold_up = outer_call(turned_two, grad_hidden[0], (sent_up,), splits=(n_y, n_x))
    hold_up = {(dy, dx): hold_up[dy * n_x + dx] for dy in range(n_y) for dx in range(n_x)}
    hold_proj = [
        (grad_proj[dy].astype(f32) + sent_proj[dy].astype(f32)).astype(bf16) for dy in range(n_y)
    ]
    sent_attn, hold_up, hold_proj, reduced_down[1:] = tie(
        sent_attn, hold_up, hold_proj, reduced_down[1:]
    )

    diagonal_up = {}
    for dy in range(1, n_y):
        for dx in range(1, n_x):
            upper = send(hold_up[dy, dx][:half], "y", dy)
            lower = send(hold_up[dy, dx][half:], "x", dx)
            diagonal_up[dy, dx] = (upper, lower)
    part_proj = [hold_proj[0]] + [send(hold_proj[k], "y", k) for k in range(1, n_y)]
    lanes = 3 * min(128, width)
    tiles = 3 * width // lanes
    grad_projected = attend_backward(projected, sent_attn, spots, geometry, 0, ())
    grad_projected, diagonal_up, hold_up, part_proj = tie(
        grad_projected, diagonal_up, hold_up, part_proj
    )

    def add_half(base, pieces, upper):
        top, low = base[:half].astype(f32), base[half:].astype(f32)
        for piece in pieces:
            if upper:
                top = top + piece[0].astype(f32)
            else:
                low = low + piece[1].astype(f32)
        return jnp.concatenate([top, low], axis=0).astype(bf16)

    def grad_tile(tile):
        cols = slice(tile * lanes, (tile + 1) * lanes)
        return dot(group_one, grad_projected[:, cols], 0, 0).astype(bf16)

    next_x = [
        add_half(hold_up[0, dx], [diagonal_up[dy, dx] for dy in range(1, n_y)], True)
        for dx in range(1, n_x)
    ]
    next_y = [
        add_half(hold_up[dy, 0], [diagonal_up[dy, dx] for dx in range(1, n_x)], False)
        for dy in range(1, n_y)
    ]
    total = part_proj[0].astype(f32)
    for piece in part_proj[1:]:
        total = total + piece.astype(f32)
    halves = [split_x([grad_tile(0), total.astype(bf16)], n_x, places)]
    next_x, next_y, halves, grad_projected = tie(next_x, next_y, halves, grad_projected)
    parts_up = [hold_up[0, 0]]
    parts_up += [send(part, "x", dx) for dx, part in enumerate(next_x, 1)]
    parts_up += [send(part, "y", dy) for dy, part in enumerate(next_y, 1)]
    parts_qkv = [[halves[0][0]] + [send(halves[0][dx], "x", dx) for dx in range(1, n_x)]]
    for tile in range(1, tiles):
        grad_projected = attend_backward(
            projected, sent_attn, spots, geometry, tile, (grad_projected,)
        )
    grad_projected, parts_up, parts_qkv, reduced_down[0] = tie(
        grad_projected, parts_up, parts_qkv, reduced_down[0]
    )

    parts = {
        key: dot(
            lax.dynamic_slice_in_dim(grad_projected, place(key[1], key[0]), rows, 0),
            full_qkv,
            1,
            1,
        )
        for key in reversed(offsets)
    }
    far_one = jnp.concatenate([parts[other, dy].astype(bf16) for dy in range(n_y)], axis=0)
    far_one, parts_up, grad_projected = tie(far_one, parts_up, grad_projected)
    sent_one = send(far_one, "core", 1)
    if tiles > 1:
        tile_grads = [grad_tile(tile) for tile in range(1, tiles)]
        halves.append(split_x(tile_grads, n_x, places))
    pieces_up = split_z(parts_up, places)
    pieces_up, halves, sent_one, parts = tie(pieces_up, halves, sent_one, parts)

    def spread_z(pieces):
        return [pieces[0]] + [send(pieces[k], "z", k) for k in range(1, N_Z)]

    parts = [
        parts[0, dy] + sent_one[dy * rows : (dy + 1) * rows].astype(f32) for dy in range(n_y)
    ]
    sent_parts = [parts[k].astype(bf16) for k in range(1, n_y)]
    last_up = spread_z(pieces_up)
    received = [send(part, "y", k) for k, part in enumerate(sent_parts, 1)]
    for part in halves[1:]:
        parts_qkv.append([part[0]] + [send(part[dx], "x", dx) for dx in range(1, n_x)])
    parts_qkv, received, last_up = tie(parts_qkv, received, last_up)

    pieces_qkv = [split_z(part, places) for part in parts_qkv]
    pieces_qkv = [
        jnp.concatenate([pieces[k] for pieces in pieces_qkv], axis=1) for k in range(N_Z)
    ]
    last_qkv = spread_z(pieces_qkv)
    last_down = [reduced_down[0].astype(f32)]
    for k in range(1, n_y):
        last_down.append(send(reduced_down[k], "y", k))
    token_grad, sums = plain_call(
        functools.partial(leave_kernel, len(received)),
        (shaped(tokens.shape, f32), shaped((8, model), f32)),
        parts[0],
        *received,
        tokens,
        grad_residual,
        norm_params,
        sums_two,
        loss_rows,
        grid=(rows // part_rows,),
        in_specs=row_blocks(part_rows, *([model] * (3 + len(received))))
        + [fixed(norm_params.shape), fixed((8, model)), fixed((8, model))],
        out_specs=tuple(row_blocks(part_rows, model) + [fixed((8, model))]),
        scratch=[pltpu.VMEM((8, model), f32)],
        mebibytes=14,
        name="leave",
    )
    around = [(y_at + dy) % n_y * N_CORE + (core_at + dc) % N_CORE for dc, dy in offsets]
    sums = sum_in_order(
        [sums] + [send_col(sums, -dy, -dc) for dc, dy in offsets[1:]],
        jnp.stack(around).astype(jnp.int32),
    )
    for axis, at in (("x", x_at), ("z", z_at)):
        around = jnp.stack([(at + k) % sizes[axis] for k in range(sizes[axis])])
        sums = sum_in_order(fetch(sums, axis), around.astype(jnp.int32))
    loss_sum = jnp.sum(sums[4])
    live_count = live_count[0, 0]

    (new_down,) = adam_call(
        [(0, weight_down.shape[0], True)], last_down, weight_down, first_down, second_down
    )
    (new_up,) = adam_call([(0, weight_up.shape[1], False)], last_up, weight_up, first_up, second_up)
    starts = [0] + [width + tile * lanes for tile in range(1, tiles)]
    new_qkv, new_proj = adam_call(
        [(starts, lanes, False), (lanes, width, True)],
        last_qkv,
        weight_qkv,
        first_qkv,
        second_qkv,
        weight_proj,
        first_proj,
        second_proj,
    )
    new_norms = adam_step(norm_params, sums[:4], first_norms, second_norms, 0.0, norm_rate)
    return (
        loss_sum / live_count,
        token_grad,
        new_qkv[0],
        new_proj[0],
        new_up[0],
        new_down[0],
        new_norms[0],
        new_qkv[1],
        new_proj[1],
        new_up[1],
        new_down[1],
        new_norms[1],
        new_qkv[2],
        new_proj[2],
        new_up[2],
        new_down[2],
        new_norms[2],
    )


def solution(mesh):
    n_x = mesh.shape["row"] // N_Z
    n_y = mesh.shape["col"] // N_CORE
    mesh = jax.sharding.Mesh(
        mesh.devices.reshape(N_Z, n_x, n_y, N_CORE), ("z", "x", "y", "core")
    )
    row, col = ("z", "x"), ("y", "core")
    matrices = (P(None, row, col), P(col, row), P(row, col), P(col, row), P())
    tokens = P(row + col, None)
    return jax.shard_map(
        functools.partial(local, n_x, n_y),
        mesh=mesh,
        in_specs=(tokens, tokens, P(row), P(row)) + matrices * 3,
        out_specs=(P(), tokens) + matrices * 3,
        check_vma=False,
    )
```

```python
import functools

import jax
import jax.numpy as jnp
from jax import lax
from jax.experimental import pallas as pl
from jax.experimental.pallas import tpu as pltpu
from jax.sharding import PartitionSpec as P

HEAD_DIM = 64
PATCHES = 577
STEP = 10
WINDOW = 640
QROWS = 320
TILE = 256
DIGITS = 16
SMALL = pl.CostEstimate(flops=1024, bytes_accessed=1024, transcendentals=0)
N_Z = 4
N_CORE = 2

layer_eps = 1e-06
adam_eps = 1e-08
learn_rate = 0.03
norm_rate = 0.25
moment_decay = 0.5
weight_decay = 0.05

bf16 = jnp.bfloat16
f32 = jnp.float32


def norm_forward(values, gain_row, bias_row):
    average = jnp.mean(values, axis=-1, keepdims=True)
    centred = values - average
    variance = jnp.mean(centred * centred, axis=-1, keepdims=True)
    inverse = lax.rsqrt(variance + layer_eps)
    scaled = centred * inverse
    return (scaled * gain_row + bias_row, scaled, inverse)


def norm_backward(upstream, scaled, inverse, gain_row):
    weighted = upstream * gain_row
    return inverse * (
        weighted
        - jnp.mean(weighted, axis=-1, keepdims=True)
        - scaled * jnp.mean(weighted * scaled, axis=-1, keepdims=True)
    )


def gelu_slope(hidden):
    return (
        0.5 * (1.0 + lax.erf(hidden * 0.7071067811865476))
        + hidden * jnp.exp(-0.5 * hidden * hidden) * 0.3989422804014327
    )


def adam_step(weight, gradient, momentum, variance, decay_rate, rate):
    momentum = moment_decay * momentum + (1.0 - moment_decay) * gradient
    variance = moment_decay * variance + (1.0 - moment_decay) * gradient * gradient
    correction = 1.0 - moment_decay**STEP
    direction = momentum / correction / (jnp.sqrt(variance / correction) + adam_eps)
    return (weight - rate * (direction + decay_rate * weight), momentum, variance)


def dot(left, right, left_dim, right_dim):
    return lax.dot_general(
        left, right, (((left_dim,), (right_dim,)), ((), ())), preferred_element_type=f32
    )


def head_lanes(width, head):
    lanes = lax.broadcasted_iota(jnp.int32, (1, width), 1)
    return (lanes >= head * HEAD_DIM) & (lanes < (head + 1) * HEAD_DIM)


def attend_weights(q_part, k_all, bias, row_start, rows_in):
    scores = dot(q_part, k_all, 1, 1) * HEAD_DIM ** (-0.5)
    rows, window = scores.shape
    row_ids = row_start + lax.broadcasted_iota(jnp.int32, (rows, window), 0)
    col_ids = lax.broadcasted_iota(jnp.int32, (rows, window), 1)
    scores = jnp.where(row_ids == col_ids, scores, scores + bias)
    weights = jnp.exp(scores - jnp.max(scores, axis=-1, keepdims=True))
    totals = jnp.sum(weights, axis=-1, keepdims=True)
    return weights * jnp.where(rows_in, 1.0 / totals, 0.0)


def image_window(begin, code_ref, group_rows):
    image = pl.program_id(0)
    start = jnp.minimum(begin[image] // 16 * 16, group_rows - WINDOW)
    first = begin[image] - start
    start = pl.multiple_of(start, 16)
    code = code_ref[pl.ds(start, WINDOW), :]
    bias = jnp.where(code == image, 0.0, -1e30).astype(f32).T[0:1, :]
    return image, start, first, bias


def rows_inside(rows, row_start, first):
    ids = row_start + lax.broadcasted_iota(jnp.int32, (rows, 1), 0)
    return (ids >= first) & (ids < first + PATCHES)


def attend_forward_kernel(begin, code_ref, *refs):
    image, start, first, bias = image_window(begin, code_ref, refs[0].shape[0])
    out_ref = refs[-1]
    lanes = refs[0].shape[1]

    for tile in range((len(refs) - 1) // 3):
        q_ref, k_ref, v_ref = refs[3 * tile : 3 * tile + 3]
        cols = slice(tile * lanes, (tile + 1) * lanes)

        @pl.when(image == 0)
        def _():
            out_ref[:, cols] = v_ref[...]

        k_all = k_ref[pl.ds(start, WINDOW), :]
        v_all = v_ref[pl.ds(start, WINDOW), :]
        for row in range(0, WINDOW, QROWS):
            at = pl.ds(pl.multiple_of(start + row, 16), QROWS)
            q_part = q_ref[at, :]
            inside = rows_inside(QROWS, row, first)
            mixed = None
            for head in range(lanes // HEAD_DIM):
                mine = head_lanes(lanes, head)
                q_head = jnp.where(mine, q_part, jnp.zeros_like(q_part))
                weights = attend_weights(q_head, k_all, bias, row, inside).astype(bf16)
                part = dot(weights, v_all, 1, 0)
                mixed = part if mixed is None else jnp.where(mine, part, mixed)
            out_ref[at, cols] = jnp.where(inside, mixed.astype(bf16), out_ref[at, cols])


def attend_backward_kernel(blocks, begin, spots, code_ref, q_ref, k_ref, v_ref, *refs):
    image, start, first, bias = image_window(begin, code_ref, q_ref.shape[0])
    out_ref, p_ref, s_ref, go_ref = refs[-4:]
    lanes = q_ref.shape[1]
    rows = refs[0].shape[0]

    @pl.when(image == 0)
    def _():
        for n, block_ref in enumerate(refs[:blocks]):
            go_ref[pl.ds(pl.multiple_of(spots[n], rows), rows), :] = block_ref[...]
        out_ref[:, : 2 * lanes] = jnp.zeros((out_ref.shape[0], 2 * lanes), bf16)
        out_ref[:, 2 * lanes :] = go_ref[...]

    whole = pl.ds(start, WINDOW)
    inside_all = rows_inside(WINDOW, 0, first)
    q_cols, k_cols, v_cols = [slice(n * lanes, (n + 1) * lanes) for n in range(3)]
    k_all = k_ref[whole, :]
    v_all = v_ref[whole, :]
    q_all = q_ref[whole, :]
    go_all = go_ref[whole, :]
    key_grad = None
    value_grad = None
    for head in range(lanes // HEAD_DIM):
        mine = head_lanes(lanes, head)
        for row in range(0, WINDOW, QROWS):
            at = pl.ds(pl.multiple_of(start + row, 16), QROWS)
            q_part = q_ref[at, :]
            go_part = go_ref[at, :]
            inside = rows_inside(QROWS, row, first)
            q_head = jnp.where(mine, q_part, jnp.zeros_like(q_part))
            go_head = jnp.where(mine, go_part, jnp.zeros_like(go_part))
            weights = attend_weights(q_head, k_all, bias, row, inside)
            weight_grad = dot(go_head, v_all, 1, 1)
            product = weights * weight_grad
            score_grad = (
                product - weights * jnp.sum(product, axis=-1, keepdims=True)
            ).astype(bf16)
            p_ref[row : row + QROWS, :] = weights.astype(bf16)
            s_ref[row : row + QROWS, :] = score_grad
            query_grad = (dot(score_grad, k_all, 1, 0) * HEAD_DIM ** (-0.5)).astype(bf16)
            out_ref[at, q_cols] = jnp.where(inside & mine, query_grad, out_ref[at, q_cols])
        q_mine = jnp.where(mine, q_all, jnp.zeros_like(q_all))
        go_mine = jnp.where(mine, go_all, jnp.zeros_like(go_all))
        key_part = dot(q_mine, s_ref[...], 0, 0)
        value_part = dot(go_mine, p_ref[...], 0, 0)
        key_grad = key_part if key_grad is None else key_grad + key_part
        value_grad = value_part if value_grad is None else value_grad + value_part
    key_rows = (key_grad.T * HEAD_DIM ** (-0.5)).astype(bf16)
    value_rows = value_grad.T.astype(bf16)
    out_ref[whole, k_cols] = jnp.where(inside_all, key_rows, out_ref[whole, k_cols])
    out_ref[whole, v_cols] = jnp.where(inside_all, value_rows, out_ref[whole, v_cols])


def qkv_operands(projected, tile):
    group_rows, total = projected.shape
    lanes = min(128, total // 3)
    if lanes % 128 == 0:
        specs = [
            pl.BlockSpec((group_rows, lanes), functools.partial(lambda n, i, *_: (0, n), 3 * tile + n))
            for n in range(3)
        ]
        return [projected] * 3, specs
    parts = [projected[:, n * lanes : (n + 1) * lanes] for n in range(3)]
    return parts, [fixed((group_rows, lanes))] * 3


def attend_forward(projected, geometry):
    begin, code = geometry
    group_rows, total = projected.shape
    width = total // 3
    operands, specs = [], []
    for tile in range(width // min(128, width)):
        more, places = qkv_operands(projected, tile)
        operands += more
        specs += places
    return plain_call(
        attend_forward_kernel,
        shaped((group_rows, width), bf16),
        code,
        *operands,
        grid=begin.shape,
        in_specs=[fixed(code.shape)] + specs,
        scalars=(begin,),
        mebibytes=20,
        name="attention_forward",
    )


def attend_backward(projected, go_blocks, spots, geometry, tile, into):
    begin, code = geometry
    group_rows, total = projected.shape
    lanes = min(128, total // 3)
    operands, specs = qkv_operands(projected, tile)
    rows = go_blocks[0].shape[0]
    return plain_call(
        functools.partial(attend_backward_kernel, len(go_blocks)),
        shaped((group_rows, total), bf16),
        code,
        *operands,
        *go_blocks,
        grid=begin.shape,
        in_specs=[fixed(code.shape)]
        + specs
        + [pl.BlockSpec((rows, lanes), lambda i, *_: (0, tile))] * len(go_blocks),
        out_specs=pl.BlockSpec((group_rows, 3 * lanes), lambda i, *_: (0, tile)),
        scratch=[pltpu.VMEM((WINDOW, WINDOW), bf16)] * 2 + [pltpu.VMEM((group_rows, lanes), bf16)],
        scalars=(begin, spots),
        into=into,
        mebibytes=20,
        name="attention_backward",
    )


def attend_geometry(segments, live_mask):
    group_rows = segments.shape[0]
    numbers = jnp.arange(group_rows // PATCHES, dtype=jnp.int32)
    positions = jnp.arange(group_rows, dtype=jnp.int32)
    begin = jnp.min(
        jnp.where(segments[None, :] == numbers[:, None], positions[None, :], group_rows - PATCHES),
        axis=1,
    )
    code = jnp.where(live_mask == 1, segments, -1)
    return begin, jnp.broadcast_to(code[:, None], (group_rows, 128))


def plain_call(kernel, out_shape, *operands, grid=(), in_specs=None, out_specs=None, scratch=(), scalars=(), into=(), mebibytes=16, name=None):
    params = pltpu.CompilerParams(vmem_limit_bytes=mebibytes * 1024 * 1024)
    if in_specs is None:
        in_specs = [pl.BlockSpec(a.shape, functools.partial(lambda n, *_: (0,) * n, a.ndim)) for a in operands]
    in_specs = list(in_specs) + [pl.BlockSpec(memory_space=pl.ANY)] * len(into)
    if out_specs is None:
        out_specs = jax.tree.map(
            lambda s: pl.BlockSpec(s.shape, functools.partial(lambda n, *_: (0,) * n, len(s.shape))), out_shape
        )
    return pl.pallas_call(
        kernel,
        grid_spec=pltpu.PrefetchScalarGridSpec(
            num_scalar_prefetch=len(scalars),
            grid=grid,
            in_specs=in_specs,
            out_specs=out_specs,
            scratch_shapes=list(scratch),
        ),
        out_shape=out_shape,
        input_output_aliases={len(scalars) + len(operands) + n: n for n in range(len(into))},
        compiler_params=params,
        cost_estimate=SMALL,
        name=name,
    )(*scalars, *operands, *into)


def shaped(shape, dtype):
    return jax.ShapeDtypeStruct(tuple(shape), dtype)


def row_blocks(rows, *widths):
    return [pl.BlockSpec((rows, w), lambda i, *_: (i, 0)) for w in widths]


def fixed(shape):
    return pl.BlockSpec(tuple(shape), functools.partial(lambda n, *_: (0,) * n, len(shape)))


def pack_kernel(live_ref, qkv_ref, proj_ref, up_ref, down_ref, qkv_out, up_out, down_out):
    count, slab, width = qkv_ref.shape
    lanes = min(128, width)
    for n in range(count):
        for t in range(width // lanes):
            at = (count * t + n) * lanes
            qkv_out[:, at : at + lanes] = qkv_ref[n][:, t * lanes : (t + 1) * lanes].astype(bf16)
    qkv_out[:, count * width :] = proj_ref[...].T.astype(bf16)
    up_out[:slab, :] = up_ref[...].astype(bf16)
    live = jnp.sum(jnp.sum(live_ref[...].astype(f32), axis=0, keepdims=True), axis=1, keepdims=True)
    high = jnp.floor(live * (1.0 / 256.0))
    middle = jnp.floor(live * (1.0 / 16.0)) - 16.0 * high
    low = live - 256.0 * high - 16.0 * middle
    row = lax.broadcasted_iota(jnp.int32, (DIGITS, up_out.shape[1]), 0)
    digits = jnp.where(row == 0, high, jnp.where(row == 1, middle, jnp.where(row == 2, low, 0.0)))
    up_out[slab:, :] = digits.astype(bf16)
    down_out[...] = down_ref[...].T.astype(bf16)


def first_kernel(tok_ref, par_ref, low_out):
    normed, _, _ = norm_forward(tok_ref[...], par_ref[0:1, :], par_ref[1:2, :])
    low_out[...] = normed.astype(bf16)


def block_rows(block, slab):
    return pl.ds(pl.multiple_of(block * slab, slab), slab)


def stack_z(pieces, slab, places):
    height, width = pieces[0].shape

    def kernel(at_ref, *refs):
        out = refs[-1]
        for k, ref in enumerate(refs[:-1]):
            out[block_rows(lax.rem(at_ref[0] + k, N_Z), slab), :] = ref[:slab, :]
        if height > slab:
            digits = refs[0][slab:, :].astype(f32)
            for ref in refs[1:-1]:
                digits = digits + ref[slab:, :].astype(f32)
            out[N_Z * slab :, :] = digits.astype(bf16)

    return plain_call(
        kernel,
        shaped(((N_Z - 1) * slab + height, width), bf16),
        *pieces,
        scalars=(places,),
        mebibytes=6,
        name="stack_z",
    )


def weave(columns, cuts, slab, places):
    n_x = len(columns[0])
    width = columns[0][0].shape[1]
    flat = [half for column in columns for half in column]
    edges = [0, *cuts, width]
    sizes = [stop - start for start, stop in zip(edges[:-1], edges[1:])]

    def kernel(at_ref, *refs):
        outs = refs[len(flat) :]
        for y in range(len(columns)):
            for dx in range(n_x):
                half = refs[y * n_x + dx]
                x = lax.rem(at_ref[1] + dx, n_x)
                for z in range(N_Z):
                    at = block_rows(z * n_x + x, slab)
                    for out, start, size in zip(outs, edges, sizes):
                        out[at, y * size : (y + 1) * size] = half[
                            z * slab : (z + 1) * slab, start : start + size
                        ]

    out = plain_call(
        kernel,
        tuple(shaped((N_Z * n_x * slab, size * len(columns)), bf16) for size in sizes),
        *flat,
        scalars=(places,),
        mebibytes=12,
        name="weave",
    )
    return out if cuts else out[0]


def proj_kernel(count, each, *refs):
    blocks, parts = refs[:count], refs[count : count + count // each]
    tok_ref, par_ref, res_out, low_out = refs[count + count // each :]
    total = tok_ref[...]
    for n, block in enumerate(blocks):
        size = block.shape[1]
        part = parts[n // each][:, n % each * size : (n % each + 1) * size]
        total = total + dot(block[...], part, 1, 1)
    res_out[...] = total
    normed, _, _ = norm_forward(total, par_ref[2:3, :], par_ref[3:4, :])
    low_out[...] = normed.astype(bf16)


ERF_TOP = (
    -2.72614225801306e-10,
    2.77068142495902e-08,
    -2.10102402082508e-06,
    -5.69250639462346e-05,
    -7.34990630326855e-04,
    -2.95459980854025e-03,
    -1.60960333262415e-02,
)
ERF_LOW = (
    -1.45660718464996e-05,
    -2.13374055278905e-04,
    -1.68282697438203e-03,
    -7.37332916720468e-03,
    -1.42647390514189e-02,
)


def erf(value):
    value = jnp.clip(value, -4.0, 4.0)
    square = value * value
    top = jnp.full_like(square, ERF_TOP[0])
    for number in ERF_TOP[1:]:
        top = top * square + number
    low = jnp.full_like(square, ERF_LOW[0])
    for number in ERF_LOW[1:]:
        low = low * square + number
    inverse = pl.reciprocal(low, approx=True)
    inverse = inverse * (2.0 - low * inverse)
    return value * top * inverse


def up_kernel(count, low_ref, *refs):
    outs = refs[-2 * count :]
    for n, part in enumerate(refs[:count]):
        hidden = dot(low_ref[...], part[...], 1, 0)
        share = 0.5 * (1.0 + erf(hidden * 0.7071067811865476))
        outs[2 * n][...] = (hidden * share).astype(bf16)
        slope = share + hidden * jnp.exp(-0.5 * hidden * hidden) * 0.3989422804014327
        outs[2 * n + 1][...] = slope.astype(bf16)


def up_call(low, parts, rows_all, spot, into):
    rows, model = low.shape
    width = parts[0].shape[1]
    cols = pl.BlockSpec((rows, TILE), lambda i, *_: (spot, i))
    return plain_call(
        functools.partial(up_kernel, len(parts)),
        (shaped((rows_all, width), bf16),) * (2 * len(parts)),
        low,
        *parts,
        grid=(width // TILE,),
        in_specs=[fixed(low.shape)] + [pl.BlockSpec((model, TILE), lambda i, *_: (0, i))] * len(parts),
        out_specs=(cols,) * (2 * len(parts)),
        into=into,
        mebibytes=14,
        name="up",
    )


def hidden_kernel(count, low_ref, *refs):
    outs = refs[-count:]
    for n in range(count):
        slope, part = refs[n], refs[count + n]
        outs[n][...] = (dot(low_ref[...], part[...], 1, 0) * slope[...].astype(f32)).astype(bf16)


def hidden_call(low, slopes, parts, spot, into):
    rows, model = low.shape
    width = parts[0].shape[1]
    cols = pl.BlockSpec((rows, TILE), lambda i, *_: (spot, i))
    return plain_call(
        functools.partial(hidden_kernel, len(parts)),
        tuple(shaped(slope.shape, bf16) for slope in slopes),
        low,
        *slopes,
        *parts,
        grid=(width // TILE,),
        in_specs=[fixed(low.shape)]
        + [cols] * len(parts)
        + [pl.BlockSpec((model, TILE), lambda i, *_: (0, i))] * len(parts),
        out_specs=(cols,) * len(parts),
        into=into,
        mebibytes=14,
        name="hidden",
    )


def wide_kernel(count, *refs):
    total = dot(refs[0][...], refs[count][...], 1, 1)
    for n in range(1, count):
        total = total + dot(refs[n][...], refs[count + n][...], 1, 1)
    refs[-1][...] = total.astype(refs[-1].dtype)


def wide_call(values, parts, rows, spot, kind):
    model, width = parts[0].shape
    return plain_call(
        functools.partial(wide_kernel, len(values)),
        shaped((rows, model), kind),
        *values,
        *parts,
        grid=(model // TILE,),
        in_specs=[pl.BlockSpec((rows, width), lambda i, *_: (spot, 0))] * len(values)
        + [pl.BlockSpec((TILE, width), lambda i, *_: (i, 0))] * len(parts),
        out_specs=pl.BlockSpec((rows, TILE), lambda i, *_: (0, i)),
        mebibytes=14,
        name="wide",
    )


def loss_kernel(count, *refs):
    res_ref, tea_ref, own_ref = refs[:3]
    live_ref, count_ref, grad_out, low_out, loss_out = refs[3 + count :]
    error = res_ref[...] - tea_ref[...] + own_ref[...]
    for ref in refs[3 : 3 + count]:
        error = error + ref[...].astype(f32)
    weighted = live_ref[...] * error
    grad = 2.0 * weighted / count_ref[...]
    grad_out[...] = grad
    low_out[...] = grad.astype(bf16)
    sums = jnp.sum(weighted * error, axis=0, keepdims=True)
    sums = jnp.concatenate([sums, jnp.zeros((7, sums.shape[1]), f32)], axis=0)
    loss_out[...] = jnp.where(pl.program_id(0) == 0, sums, loss_out[...] + sums)


def spread_kernel(each, low_ref, *refs):
    parts = len(refs) // (each + 1)
    for n, out in enumerate(refs[parts:]):
        size = out.shape[1]
        part = refs[n // each][:, n % each * size : (n % each + 1) * size]
        out[...] = dot(low_ref[...], part, 1, 0).astype(bf16)


def spread_call(low, parts, each):
    size = parts[0].shape[1] // each
    return plain_call(
        functools.partial(spread_kernel, each),
        tuple(shaped((low.shape[0], size), bf16) for _ in range(each * len(parts))),
        low,
        *parts,
        mebibytes=12,
        name="spread",
    )


def norm_sums(grad, scaled, out_ref, first):
    sums = jnp.concatenate(
        [
            jnp.sum(grad * scaled, axis=0, keepdims=True),
            jnp.sum(grad, axis=0, keepdims=True),
            jnp.zeros((6, grad.shape[1]), f32),
        ],
        axis=0,
    )
    out_ref[...] = jnp.where(first, sums, out_ref[...] + sums)


def middle_kernel(count, *refs):
    grad_ref, received = refs[0], refs[1 : 1 + count]
    res_ref, gout_ref, par_ref, full_out, low_out, sum_out = refs[1 + count :]
    _, scaled, inverse = norm_forward(res_ref[...], par_ref[2:3, :], par_ref[3:4, :])
    grad = grad_ref[...]
    for ref in received:
        grad = grad + ref[...].astype(f32)
    full = gout_ref[...] + norm_backward(grad, scaled, inverse, par_ref[2:3, :])
    full_out[...] = full
    low_out[...] = full.astype(bf16)
    norm_sums(grad, scaled, sum_out, pl.program_id(0) == 0)


def leave_kernel(count, *refs):
    own_ref, received = refs[0], refs[1 : 1 + count]
    tok_ref, res_ref, par_ref, two_ref, loss_ref, out_ref, sum_out, sum_ref = refs[1 + count :]
    _, scaled, inverse = norm_forward(tok_ref[...], par_ref[0:1, :], par_ref[1:2, :])
    grad = own_ref[...]
    for ref in received:
        grad = grad + ref[...].astype(f32)
    out_ref[...] = res_ref[...] + norm_backward(grad, scaled, inverse, par_ref[0:1, :])
    norm_sums(grad, scaled, sum_ref, pl.program_id(0) == 0)
    sum_out[...] = jnp.concatenate(
        [sum_ref[0:2, :], two_ref[0:2, :], loss_ref[0:1, :], jnp.zeros((3, grad.shape[1]), f32)],
        axis=0,
    )


def split_x(parts, n_x, places):
    model = parts[0].shape[0]
    slab = model // (N_Z * n_x)
    total = sum(part.shape[1] for part in parts)

    def kernel(at_ref, *refs):
        outs = refs[len(parts) :]
        for dx in range(n_x):
            x = lax.rem(at_ref[1] + dx, n_x)
            for z in range(N_Z):
                at = block_rows(z * n_x + x, slab)
                lane = 0
                for ref in refs[: len(parts)]:
                    size = ref.shape[1]
                    outs[dx][z * slab : (z + 1) * slab, lane : lane + size] = ref[at, :]
                    lane += size

    return plain_call(
        kernel,
        tuple(shaped((model // n_x, total), bf16) for _ in range(n_x)),
        *parts,
        scalars=(places,),
        mebibytes=10,
        name="split_x",
    )


def sum_in_order(pieces, spots):
    def kernel(spot_ref, *refs):
        out, held = refs[-2:]
        for n, ref in enumerate(refs[:-2]):
            held[spot_ref[n]] = ref[...]
        total = held[0]
        for n in range(1, len(pieces)):
            total = total + held[n]
        out[...] = total

    return plain_call(
        kernel,
        shaped(pieces[0].shape, f32),
        *pieces,
        scalars=(spots,),
        scratch=[pltpu.VMEM((len(pieces),) + pieces[0].shape, f32)],
        mebibytes=6,
        name="sum_in_order",
    )


def split_z(parts, places):
    rows, width = parts[0].shape
    slab = rows // N_Z

    def kernel(at_ref, *refs):
        for k, out in enumerate(refs[len(parts) :]):
            at = block_rows(lax.rem(at_ref[0] + k, N_Z), slab)
            total = refs[0][at, :].astype(f32)
            for ref in refs[1 : len(parts)]:
                total = total + ref[at, :].astype(f32)
            out[...] = total.astype(out.dtype)

    shapes = (shaped((slab, width), f32),) + (shaped((slab, width), bf16),) * (N_Z - 1)
    return plain_call(kernel, shapes, *parts, scalars=(places,), mebibytes=8, name="split_z")


def adam_kernel(layout, counts, *refs):
    grads = []
    for count in counts:
        grad = refs[0][...].astype(f32)
        for ref in refs[1:count]:
            grad = grad + ref[...].astype(f32)
        grads.append(grad)
        refs = refs[count:]
    count = len(layout)
    states, outs = refs[: 3 * count], refs[3 * count :]
    for n, (source, start, size, turned) in enumerate(layout):
        weight, first, second = states[3 * n : 3 * n + 3]
        if len(weight.shape) == 3:
            matrices = weight.shape[0]
            lanes = size // matrices
            for k in range(matrices):
                own = [
                    grads[at][:, lane + k * lanes : lane + (k + 1) * lanes] for at, lane in start
                ]
                own = own[0] if len(own) == 1 else jnp.concatenate(own, axis=1)
                new = adam_step(weight[k], own, first[k], second[k], weight_decay, learn_rate)
                for out, value in zip(outs[3 * n : 3 * n + 3], new):
                    out[k] = value
        else:
            part = grads[source][:, start : start + size]
            if turned:
                part = part.T
            new = adam_step(weight[...], part, first[...], second[...], weight_decay, learn_rate)
            for out, value in zip(outs[3 * n : 3 * n + 3], new):
                out[...] = value


def adam_call(groups, layout, *states):
    shapes = tuple(shaped(s.shape, f32) for s in states)
    out = plain_call(
        functools.partial(adam_kernel, layout, [len(group) for group in groups]),
        shapes,
        *[piece for group in groups for piece in group],
        *states,
        mebibytes=16,
        name="adam",
    )
    return [out[3 * n : 3 * n + 3] for n in range(len(layout))]


def tie(*values):
    return lax.optimization_barrier(values)


def local(
    n_x,
    n_y,
    tokens,
    teacher,
    segments,
    live_mask,
    weight_qkv,
    weight_proj,
    weight_up,
    weight_down,
    norm_params,
    first_qkv,
    first_proj,
    first_up,
    first_down,
    first_norms,
    second_qkv,
    second_proj,
    second_up,
    second_down,
    second_norms,
):
    z_at, x_at = lax.axis_index("z"), lax.axis_index("x")
    y_at, core_at = lax.axis_index("y"), lax.axis_index("core")
    rows, model = tokens.shape
    group_rows = segments.shape[0]
    slab = weight_qkv.shape[1]
    width = weight_qkv.shape[2]
    unit = weight_up.shape[1]
    part_rows = min(128, rows)
    depth = N_Z * slab
    sizes = {"z": N_Z, "x": n_x, "y": n_y, "core": N_CORE}
    places = jnp.stack([z_at, x_at]).astype(jnp.int32)
    offsets = [(dc, dy) for dc in range(N_CORE) for dy in range(n_y)]
    other = N_CORE - 1

    def send(value, axis, step):
        size = sizes[axis]
        return lax.ppermute(value, axis, [(i, (i + step) % size) for i in range(size)])

    def send_col(value, dy, dc):
        perm = [
            (y * N_CORE + c, (y + dy) % n_y * N_CORE + (c + dc) % N_CORE)
            for y in range(n_y)
            for c in range(N_CORE)
        ]
        return lax.ppermute(value, ("y", "core"), perm)

    def fetch(value, axis):
        return [value] + [send(value, axis, -k) for k in range(1, sizes[axis])]

    def place(dy, dc):
        return ((y_at + dy) % n_y * N_CORE + (core_at + dc) % N_CORE) * rows

    shard_qkv, shard_up, shard_down = plain_call(
        pack_kernel,
        (
            shaped((slab, 4 * width), bf16),
            shaped((slab + DIGITS, unit), bf16),
            shaped((slab, unit), bf16),
        ),
        live_mask.reshape(-1, 128),
        weight_qkv,
        weight_proj,
        weight_up,
        weight_down,
        mebibytes=8,
        name="pack",
    )
    near_qkv = fetch(shard_qkv, "z")
    low_one = plain_call(
        first_kernel,
        shaped(tokens.shape, bf16),
        tokens,
        norm_params,
        grid=(rows // part_rows,),
        in_specs=row_blocks(part_rows, model) + [fixed(norm_params.shape)],
        out_specs=row_blocks(part_rows, model)[0],
        mebibytes=8,
        name="first",
    )
    blocks_one = fetch(low_one, "y")
    near_qkv, shard_down, shard_up, blocks_one = tie(near_qkv, shard_down, shard_up, blocks_one)

    block_qkv = stack_z(near_qkv, slab, places)
    near_one = jnp.concatenate(blocks_one, axis=0)
    near_one, block_qkv = tie(near_one, block_qkv)
    beside_qkv = fetch(block_qkv, "x")
    near_up = fetch(shard_up, "z")
    far_one = send(near_one, "core", -1)
    geometry = attend_geometry(segments, live_mask)
    own_live = lax.dynamic_slice_in_dim(
        live_mask, (y_at * N_CORE + core_at) * rows, rows, 0
    ).astype(f32)[:, None]
    beside_qkv, near_up, near_one, far_one, geometry, own_live, shard_down = tie(
        beside_qkv, near_up, near_one, far_one, geometry, own_live, shard_down
    )

    block_up = stack_z(near_up, slab, places)
    full_qkv, part_proj = weave([beside_qkv], [3 * width], slab, places)
    block_up, part_proj = tie(block_up, part_proj)
    beside_up = fetch(block_up, "x")
    near_down = fetch(shard_down, "z")
    full_proj = fetch(part_proj, "y")
    group_one = jnp.zeros((group_rows, model), bf16)
    for dc, dy in offsets:
        block = (far_one if dc else near_one)[dy * rows : (dy + 1) * rows]
        group_one = lax.dynamic_update_slice_in_dim(group_one, block, place(dy, dc), 0)
    projected = dot(group_one, full_qkv, 1, 0).astype(bf16)
    mixed = attend_forward(projected, geometry)
    mixed, beside_up, near_down, full_proj = tie(mixed, beside_up, near_down, full_proj)

    blocks_mixed = []
    for dc, dy in offsets:
        piece = lax.dynamic_slice_in_dim(mixed, place(-dy, -dc), rows, 0)
        blocks_mixed.append(piece if (dc, dy) == (0, 0) else send_col(piece, -dy, -dc))
    full_proj = [jnp.concatenate(full_proj, axis=1)]
    full_proj.append(send(full_proj[0], "core", -1))
    beside_down = fetch(stack_z(near_down, slab, places), "x")
    full_up = [weave([beside_up], [], slab, places)]
    live_count = sum(
        256.0 * part[depth, 0].astype(f32) + 16.0 * part[depth + 1, 0].astype(f32)
        + part[depth + 2, 0].astype(f32)
        for part in beside_up
    ).reshape(1, 1)
    blocks_mixed, full_proj, full_up, live_count = tie(
        blocks_mixed, full_proj, full_up, live_count
    )
    full_up.append(send(full_up[0], "core", -1))
    count = len(offsets)
    residual, low_two = plain_call(
        functools.partial(proj_kernel, count, n_y),
        (shaped(tokens.shape, f32), shaped(tokens.shape, bf16)),
        *blocks_mixed,
        *full_proj,
        tokens,
        norm_params,
        grid=(rows // part_rows,),
        in_specs=row_blocks(part_rows, *([width] * count))
        + [fixed(part.shape) for part in full_proj]
        + row_blocks(part_rows, model)
        + [fixed(norm_params.shape)],
        out_specs=tuple(row_blocks(part_rows, model, model)),
        mebibytes=16,
        name="proj",
    )
    low_two, full_up, beside_down = tie(low_two, full_up, beside_down)

    chunk = min(256, rows)
    chunks = range(rows // chunk)
    neighbours = range(1, n_y)
    rows_all = n_y * rows

    def cross(value, n, back):
        piece = value[n * chunk : (n + 1) * chunk]
        return {dy: send(piece, "y", dy if back else -dy) for dy in neighbours}

    def spot_of(dy, n):
        return (dy * rows) // chunk + n

    low_far = {0: cross(low_two, 0, False)}
    full_down = [weave([beside_down], [], slab, places)]
    full_down.append(send(full_down[0], "core", -1))
    hidden = up_call(low_two, full_up, rows_all, 0, ())
    low_far[0], hidden, full_down, low_two = tie(low_far[0], hidden, full_down, low_two)
    far_out = {}
    for n in chunks:
        if n + 1 in chunks:
            low_far[n + 1] = cross(low_two, n + 1, False)
        for dy in neighbours:
            hidden = up_call(low_far[n][dy], full_up, rows_all, spot_of(dy, n), hidden)
        outs = {
            dy: wide_call(hidden[::2], full_down, chunk, spot_of(dy, n), bf16) for dy in neighbours
        }
        if n + 1 in chunks:
            outs, hidden, low_far[n + 1] = tie(outs, hidden, low_far[n + 1])
        else:
            outs, hidden = tie(outs, hidden)
        if n:
            far_out[n - 1] = tie(far_out[n - 1], outs)[0]
        far_out[n] = {dy: send(outs[dy], "y", -dy) for dy in neighbours}
    own_out = wide_call(hidden[::2], full_down, rows, 0, f32)
    own_out, far_out = tie(own_out, far_out)
    far_out = [
        jnp.concatenate([far_out[n][dy] for n in chunks], axis=0) for dy in neighbours
    ]
    grad_output, grad_branch, loss_rows = plain_call(
        functools.partial(loss_kernel, len(far_out)),
        (shaped(tokens.shape, f32), shaped(tokens.shape, bf16), shaped((8, model), f32)),
        residual,
        teacher,
        own_out,
        *far_out,
        own_live,
        live_count,
        grid=(rows // part_rows,),
        in_specs=row_blocks(part_rows, *([model] * (3 + len(far_out))), 1) + [fixed((1, 1))],
        out_specs=tuple(row_blocks(part_rows, model, model) + [fixed((8, model))]),
        mebibytes=14,
        name="loss",
    )
    active, slope = hidden[::2], hidden[1::2]

    grad_far = {0: cross(grad_branch, 0, False)}
    grad_hidden = hidden_call(grad_branch, slope, full_down, 0, ())
    own_two = wide_call(grad_hidden, full_up, rows, 0, f32)
    grad_far[0], grad_hidden, own_two, grad_branch = tie(
        grad_far[0], grad_hidden, own_two, grad_branch
    )
    far_two = {}
    for n in chunks:
        if n + 1 in chunks:
            grad_far[n + 1] = cross(grad_branch, n + 1, False)
        for dy in neighbours:
            grad_hidden = hidden_call(
                grad_far[n][dy], slope, full_down, spot_of(dy, n), grad_hidden
            )
        outs = {
            dy: wide_call(grad_hidden, full_up, chunk, spot_of(dy, n), bf16) for dy in neighbours
        }
        if n + 1 in chunks:
            outs, grad_hidden, grad_far[n + 1] = tie(outs, grad_hidden, grad_far[n + 1])
        else:
            outs, grad_hidden = tie(outs, grad_hidden)
        if n:
            far_two[n - 1] = tie(far_two[n - 1], outs)[0]
        far_two[n] = {dy: send(outs[dy], "y", -dy) for dy in neighbours}

    def gather_rows(own, far):
        return jnp.concatenate([own] + [far[n][dy] for dy in neighbours for n in chunks], axis=0)

    grad_all = gather_rows(grad_branch, grad_far)
    low_all = gather_rows(low_two, low_far)
    far_down = dot(grad_all, active[other], 0, 0).astype(bf16)
    far_up = dot(low_all, grad_hidden[other], 0, 0).astype(bf16)
    far_two, far_down, far_up = tie(far_two, far_down, far_up)
    far_two = [
        jnp.concatenate([far_two[n][dy] for n in chunks], axis=0) for dy in neighbours
    ]
    grad_residual, grad_low, sums_two = plain_call(
        functools.partial(middle_kernel, len(far_two)),
        (shaped(tokens.shape, f32), shaped(tokens.shape, bf16), shaped((8, model), f32)),
        own_two,
        *far_two,
        residual,
        grad_output,
        norm_params,
        grid=(rows // part_rows,),
        in_specs=row_blocks(part_rows, *([model] * (3 + len(far_two)))) + [fixed(norm_params.shape)],
        out_specs=tuple(row_blocks(part_rows, model, model) + [fixed((8, model))]),
        mebibytes=14,
        name="middle",
    )
    pieces_attn = spread_call(grad_low, full_proj, n_y)
    pieces_attn, far_down, far_up, grad_low = tie(pieces_attn, far_down, far_up, grad_low)

    sent_attn = [
        piece if key == (0, 0) else send_col(piece, key[1], key[0])
        for key, piece in zip(offsets, pieces_attn)
    ]
    spots = jnp.stack([place(-dy, -dc) for dc, dy in offsets]).astype(jnp.int32)
    grad_proj = [dot(grad_low, block, 0, 0).astype(bf16) for block in blocks_mixed]
    sent_attn, grad_proj, far_down, far_up, grad_all, low_all = tie(
        sent_attn, grad_proj, far_down, far_up, grad_all, low_all
    )

    lanes = 3 * min(128, width)
    tiles = 3 * width // lanes
    sent_down, sent_up = send(far_down, "core", 1), send(far_up, "core", 1)
    sent_proj = send(jnp.concatenate(grad_proj[n_y:], axis=1), "core", 1)
    hold_down, hold_up = dot(grad_all, active[0], 0, 0), dot(low_all, grad_hidden[0], 0, 0)
    grad_projected = attend_backward(projected, sent_attn, spots, geometry, 0, ())
    grad_projected, sent_down, sent_up, sent_proj, hold_down, hold_up = tie(
        grad_projected, sent_down, sent_up, sent_proj, hold_down, hold_up
    )
    hold = jnp.concatenate(
        [
            (hold_down + sent_down.astype(f32)).astype(bf16),
            (hold_up + sent_up.astype(f32)).astype(bf16),
        ],
        axis=1,
    )

    def grad_tile(tile):
        cols = slice(tile * lanes, (tile + 1) * lanes)
        return dot(group_one, grad_projected[:, cols], 0, 0).astype(bf16)

    hold_proj = [
        (
            grad_proj[dy].astype(f32) + sent_proj[:, dy * width : (dy + 1) * width].astype(f32)
        ).astype(bf16)
        for dy in range(n_y)
    ]
    halves = []
    if tiles > 1:
        halves.append(split_x([grad_tile(0)], n_x, places))
    halves, hold_proj, grad_projected, hold = tie(halves, hold_proj, grad_projected, hold)
    reduced = lax.psum_scatter(hold, ("z", "x"), scatter_dimension=0, tiled=True)
    parts_qkv = [
        [part[0]] + [send(part[dx], "x", dx) for dx in range(1, n_x)] for part in halves
    ]
    part_proj = [hold_proj[0]] + [send(hold_proj[k], "y", k) for k in range(1, n_y)]
    for tile in range(1, tiles):
        grad_projected = attend_backward(
            projected, sent_attn, spots, geometry, tile, (grad_projected,)
        )
    grad_projected, parts_qkv, part_proj = tie(grad_projected, parts_qkv, part_proj)

    parts = {
        key: dot(
            lax.dynamic_slice_in_dim(grad_projected, place(key[1], key[0]), rows, 0),
            full_qkv,
            1,
            1,
        )
        for key in reversed(offsets)
    }
    far_one = jnp.concatenate([parts[other, dy].astype(bf16) for dy in range(n_y)], axis=0)
    far_one, grad_projected = tie(far_one, grad_projected)
    sent_one = send(far_one, "core", 1)
    total = part_proj[0].astype(f32)
    for piece in part_proj[1:]:
        total = total + piece.astype(f32)
    tile_grads = [grad_tile(tile) for tile in range(min(1, tiles - 1), tiles)]
    last_half = split_x([total.astype(bf16)] + tile_grads, n_x, places)
    last_half, sent_one, parts = tie(last_half, sent_one, parts)

    def spread_z(pieces):
        return [pieces[0]] + [send(pieces[k], "z", k) for k in range(1, N_Z)]

    parts = [
        parts[0, dy] + sent_one[dy * rows : (dy + 1) * rows].astype(f32) for dy in range(n_y)
    ]
    sent_parts = [parts[k].astype(bf16) for k in range(1, n_y)]
    received = [send(part, "y", k) for k, part in enumerate(sent_parts, 1)]
    parts_qkv.append([last_half[0]] + [send(last_half[dx], "x", dx) for dx in range(1, n_x)])
    early = [spread_z(split_z(part, places)) for part in parts_qkv[:-1]]
    parts_qkv, received, early = tie(parts_qkv, received, early)

    last_qkv = spread_z(split_z(parts_qkv[-1], places))
    last_qkv, reduced = tie(last_qkv, reduced)
    token_grad, sums = plain_call(
        functools.partial(leave_kernel, len(received)),
        (shaped(tokens.shape, f32), shaped((8, model), f32)),
        parts[0],
        *received,
        tokens,
        grad_residual,
        norm_params,
        sums_two,
        loss_rows,
        grid=(rows // part_rows,),
        in_specs=row_blocks(part_rows, *([model] * (3 + len(received))))
        + [fixed(norm_params.shape), fixed((8, model)), fixed((8, model))],
        out_specs=tuple(row_blocks(part_rows, model) + [fixed((8, model))]),
        scratch=[pltpu.VMEM((8, model), f32)],
        mebibytes=14,
        name="leave",
    )
    around = [(y_at + dy) % n_y * N_CORE + (core_at + dc) % N_CORE for dc, dy in offsets]
    sums = sum_in_order(
        [sums] + [send_col(sums, -dy, -dc) for dc, dy in offsets[1:]],
        jnp.stack(around).astype(jnp.int32),
    )
    for axis, at in (("x", x_at), ("z", z_at)):
        around = jnp.stack([(at + k) % sizes[axis] for k in range(sizes[axis])])
        sums = sum_in_order(fetch(sums, axis), around.astype(jnp.int32))
    loss_sum = jnp.sum(sums[4])
    live_count = live_count[0, 0]

    new_down, new_up = adam_call(
        [[reduced]],
        [(0, 0, unit, True), (0, unit, unit, False)],
        weight_down,
        first_down,
        second_down,
        weight_up,
        first_up,
        second_up,
    )
    last = len(early)
    starts = [(n, 0) for n in range(last)]
    starts += [(last, width + n * lanes) for n in range(tiles - last)]
    new_qkv, new_proj = adam_call(
        early + [last_qkv],
        [(last, starts, lanes, False), (last, 0, width, True)],
        weight_qkv,
        first_qkv,
        second_qkv,
        weight_proj,
        first_proj,
        second_proj,
    )
    new_norms = adam_step(norm_params, sums[:4], first_norms, second_norms, 0.0, norm_rate)
    return (
        loss_sum / live_count,
        token_grad,
        new_qkv[0],
        new_proj[0],
        new_up[0],
        new_down[0],
        new_norms[0],
        new_qkv[1],
        new_proj[1],
        new_up[1],
        new_down[1],
        new_norms[1],
        new_qkv[2],
        new_proj[2],
        new_up[2],
        new_down[2],
        new_norms[2],
    )


def solution(mesh):
    n_x = mesh.shape["row"] // N_Z
    n_y = mesh.shape["col"] // N_CORE
    mesh = jax.sharding.Mesh(
        mesh.devices.reshape(N_Z, n_x, n_y, N_CORE), ("z", "x", "y", "core")
    )
    row, col = ("z", "x"), ("y", "core")
    matrices = (P(None, row, col), P(col, row), P(row, col), P(col, row), P())
    tokens = P(row + col, None)
    return jax.shard_map(
        functools.partial(local, n_x, n_y),
        mesh=mesh,
        in_specs=(tokens, tokens, P(row), P(row)) + matrices * 3,
        out_specs=(P(), tokens) + matrices * 3,
        check_vma=False,
    )
```

```python
import functools

import jax
import jax.numpy as jnp
from jax import lax
from jax.experimental import pallas as pl
from jax.experimental.pallas import tpu as pltpu
from jax.sharding import PartitionSpec as P

HEAD_DIM = 64
PATCHES = 577
STEP = 10
WINDOW = 640
QROWS = 320
TILE = 256
DIGITS = 16
SMALL = pl.CostEstimate(flops=1024, bytes_accessed=1024, transcendentals=0)
N_Z = 4
N_CORE = 2

layer_eps = 1e-06
adam_eps = 1e-08
learn_rate = 0.03
norm_rate = 0.25
moment_decay = 0.5
weight_decay = 0.05

bf16 = jnp.bfloat16
f32 = jnp.float32


def norm_forward(values, gain_row, bias_row):
    average = jnp.mean(values, axis=-1, keepdims=True)
    centred = values - average
    variance = jnp.mean(centred * centred, axis=-1, keepdims=True)
    inverse = lax.rsqrt(variance + layer_eps)
    scaled = centred * inverse
    return (scaled * gain_row + bias_row, scaled, inverse)


def norm_backward(upstream, scaled, inverse, gain_row):
    weighted = upstream * gain_row
    return inverse * (
        weighted
        - jnp.mean(weighted, axis=-1, keepdims=True)
        - scaled * jnp.mean(weighted * scaled, axis=-1, keepdims=True)
    )


def gelu_slope(hidden):
    return (
        0.5 * (1.0 + lax.erf(hidden * 0.7071067811865476))
        + hidden * jnp.exp(-0.5 * hidden * hidden) * 0.3989422804014327
    )


def adam_step(weight, gradient, momentum, variance, decay_rate, rate):
    momentum = moment_decay * momentum + (1.0 - moment_decay) * gradient
    variance = moment_decay * variance + (1.0 - moment_decay) * gradient * gradient
    correction = 1.0 - moment_decay**STEP
    direction = momentum / correction / (jnp.sqrt(variance / correction) + adam_eps)
    return (weight - rate * (direction + decay_rate * weight), momentum, variance)


def dot(left, right, left_dim, right_dim):
    return lax.dot_general(
        left, right, (((left_dim,), (right_dim,)), ((), ())), preferred_element_type=f32
    )


def head_lanes(width, head):
    lanes = lax.broadcasted_iota(jnp.int32, (1, width), 1)
    return (lanes >= head * HEAD_DIM) & (lanes < (head + 1) * HEAD_DIM)


def attend_weights(q_part, k_all, bias, row_start, rows_in):
    scores = dot(q_part, k_all, 1, 1) * HEAD_DIM ** (-0.5)
    rows, window = scores.shape
    row_ids = row_start + lax.broadcasted_iota(jnp.int32, (rows, window), 0)
    col_ids = lax.broadcasted_iota(jnp.int32, (rows, window), 1)
    scores = jnp.where(row_ids == col_ids, scores, scores + bias)
    weights = jnp.exp(scores - jnp.max(scores, axis=-1, keepdims=True))
    totals = jnp.sum(weights, axis=-1, keepdims=True)
    return weights * jnp.where(rows_in, 1.0 / totals, 0.0)


def image_window(begin, code_ref, group_rows):
    image = pl.program_id(0)
    start = jnp.minimum(begin[image] // 16 * 16, group_rows - WINDOW)
    first = begin[image] - start
    start = pl.multiple_of(start, 16)
    code = code_ref[pl.ds(start, WINDOW), :]
    bias = jnp.where(code == image, 0.0, -1e30).astype(f32).T[0:1, :]
    return image, start, first, bias


def rows_inside(rows, row_start, first):
    ids = row_start + lax.broadcasted_iota(jnp.int32, (rows, 1), 0)
    return (ids >= first) & (ids < first + PATCHES)


def attend_forward_kernel(begin, code_ref, *refs):
    image, start, first, bias = image_window(begin, code_ref, refs[0].shape[0])
    out_ref = refs[-1]
    lanes = refs[0].shape[1]

    for tile in range((len(refs) - 1) // 3):
        q_ref, k_ref, v_ref = refs[3 * tile : 3 * tile + 3]
        cols = slice(tile * lanes, (tile + 1) * lanes)

        @pl.when(image == 0)
        def _():
            out_ref[:, cols] = v_ref[...]

        k_all = k_ref[pl.ds(start, WINDOW), :]
        v_all = v_ref[pl.ds(start, WINDOW), :]
        for row in range(0, WINDOW, QROWS):
            at = pl.ds(pl.multiple_of(start + row, 16), QROWS)
            q_part = q_ref[at, :]
            inside = rows_inside(QROWS, row, first)
            mixed = None
            for head in range(lanes // HEAD_DIM):
                mine = head_lanes(lanes, head)
                q_head = jnp.where(mine, q_part, jnp.zeros_like(q_part))
                weights = attend_weights(q_head, k_all, bias, row, inside).astype(bf16)
                part = dot(weights, v_all, 1, 0)
                mixed = part if mixed is None else jnp.where(mine, part, mixed)
            out_ref[at, cols] = jnp.where(inside, mixed.astype(bf16), out_ref[at, cols])


def attend_backward_kernel(blocks, begin, spots, code_ref, q_ref, k_ref, v_ref, *refs):
    image, start, first, bias = image_window(begin, code_ref, q_ref.shape[0])
    out_ref, p_ref, s_ref, go_ref = refs[-4:]
    lanes = q_ref.shape[1]
    rows = refs[0].shape[0]

    @pl.when(image == 0)
    def _():
        for n, block_ref in enumerate(refs[:blocks]):
            go_ref[pl.ds(pl.multiple_of(spots[n], rows), rows), :] = block_ref[...]
        out_ref[:, : 2 * lanes] = jnp.zeros((out_ref.shape[0], 2 * lanes), bf16)
        out_ref[:, 2 * lanes :] = go_ref[...]

    whole = pl.ds(start, WINDOW)
    inside_all = rows_inside(WINDOW, 0, first)
    q_cols, k_cols, v_cols = [slice(n * lanes, (n + 1) * lanes) for n in range(3)]
    k_all = k_ref[whole, :]
    v_all = v_ref[whole, :]
    q_all = q_ref[whole, :]
    go_all = go_ref[whole, :]
    key_grad = None
    value_grad = None
    for head in range(lanes // HEAD_DIM):
        mine = head_lanes(lanes, head)
        for row in range(0, WINDOW, QROWS):
            at = pl.ds(pl.multiple_of(start + row, 16), QROWS)
            q_part = q_ref[at, :]
            go_part = go_ref[at, :]
            inside = rows_inside(QROWS, row, first)
            q_head = jnp.where(mine, q_part, jnp.zeros_like(q_part))
            go_head = jnp.where(mine, go_part, jnp.zeros_like(go_part))
            weights = attend_weights(q_head, k_all, bias, row, inside)
            weight_grad = dot(go_head, v_all, 1, 1)
            product = weights * weight_grad
            score_grad = (
                product - weights * jnp.sum(product, axis=-1, keepdims=True)
            ).astype(bf16)
            p_ref[row : row + QROWS, :] = weights.astype(bf16)
            s_ref[row : row + QROWS, :] = score_grad
            query_grad = (dot(score_grad, k_all, 1, 0) * HEAD_DIM ** (-0.5)).astype(bf16)
            out_ref[at, q_cols] = jnp.where(inside & mine, query_grad, out_ref[at, q_cols])
        q_mine = jnp.where(mine, q_all, jnp.zeros_like(q_all))
        go_mine = jnp.where(mine, go_all, jnp.zeros_like(go_all))
        key_part = dot(q_mine, s_ref[...], 0, 0)
        value_part = dot(go_mine, p_ref[...], 0, 0)
        key_grad = key_part if key_grad is None else key_grad + key_part
        value_grad = value_part if value_grad is None else value_grad + value_part
    key_rows = (key_grad.T * HEAD_DIM ** (-0.5)).astype(bf16)
    value_rows = value_grad.T.astype(bf16)
    out_ref[whole, k_cols] = jnp.where(inside_all, key_rows, out_ref[whole, k_cols])
    out_ref[whole, v_cols] = jnp.where(inside_all, value_rows, out_ref[whole, v_cols])


def qkv_operands(projected, tile):
    group_rows, total = projected.shape
    lanes = min(128, total // 3)
    if lanes % 128 == 0:
        specs = [
            pl.BlockSpec((group_rows, lanes), functools.partial(lambda n, i, *_: (0, n), 3 * tile + n))
            for n in range(3)
        ]
        return [projected] * 3, specs
    parts = [projected[:, n * lanes : (n + 1) * lanes] for n in range(3)]
    return parts, [fixed((group_rows, lanes))] * 3


def attend_forward(projected, geometry):
    begin, code = geometry
    group_rows, total = projected.shape
    width = total // 3
    operands, specs = [], []
    for tile in range(width // min(128, width)):
        more, places = qkv_operands(projected, tile)
        operands += more
        specs += places
    return plain_call(
        attend_forward_kernel,
        shaped((group_rows, width), bf16),
        code,
        *operands,
        grid=begin.shape,
        in_specs=[fixed(code.shape)] + specs,
        scalars=(begin,),
        mebibytes=20,
        name="attention_forward",
    )


def attend_backward(projected, go_blocks, spots, geometry, tile, into):
    begin, code = geometry
    group_rows, total = projected.shape
    lanes = min(128, total // 3)
    operands, specs = qkv_operands(projected, tile)
    rows = go_blocks[0].shape[0]
    return plain_call(
        functools.partial(attend_backward_kernel, len(go_blocks)),
        shaped((group_rows, total), bf16),
        code,
        *operands,
        *go_blocks,
        grid=begin.shape,
        in_specs=[fixed(code.shape)]
        + specs
        + [fixed((rows, lanes))] * len(go_blocks),
        out_specs=pl.BlockSpec((group_rows, 3 * lanes), lambda i, *_: (0, tile)),
        scratch=[pltpu.VMEM((WINDOW, WINDOW), bf16)] * 2 + [pltpu.VMEM((group_rows, lanes), bf16)],
        scalars=(begin, spots),
        into=into,
        mebibytes=20,
        name="attention_backward",
    )


def attend_geometry(segments, live_mask):
    group_rows = segments.shape[0]
    numbers = jnp.arange(group_rows // PATCHES, dtype=jnp.int32)
    positions = jnp.arange(group_rows, dtype=jnp.int32)
    begin = jnp.min(
        jnp.where(segments[None, :] == numbers[:, None], positions[None, :], group_rows - PATCHES),
        axis=1,
    )
    code = jnp.where(live_mask == 1, segments, -1)
    return begin, jnp.broadcast_to(code[:, None], (group_rows, 128))


def plain_call(kernel, out_shape, *operands, grid=(), in_specs=None, out_specs=None, scratch=(), scalars=(), into=(), mebibytes=16, name=None):
    params = pltpu.CompilerParams(vmem_limit_bytes=mebibytes * 1024 * 1024)
    if in_specs is None:
        in_specs = [pl.BlockSpec(a.shape, functools.partial(lambda n, *_: (0,) * n, a.ndim)) for a in operands]
    in_specs = list(in_specs) + [pl.BlockSpec(memory_space=pl.ANY)] * len(into)
    if out_specs is None:
        out_specs = jax.tree.map(
            lambda s: pl.BlockSpec(s.shape, functools.partial(lambda n, *_: (0,) * n, len(s.shape))), out_shape
        )
    return pl.pallas_call(
        kernel,
        grid_spec=pltpu.PrefetchScalarGridSpec(
            num_scalar_prefetch=len(scalars),
            grid=grid,
            in_specs=in_specs,
            out_specs=out_specs,
            scratch_shapes=list(scratch),
        ),
        out_shape=out_shape,
        input_output_aliases={len(scalars) + len(operands) + n: n for n in range(len(into))},
        compiler_params=params,
        cost_estimate=SMALL,
        name=name,
    )(*scalars, *operands, *into)


def shaped(shape, dtype):
    return jax.ShapeDtypeStruct(tuple(shape), dtype)


def row_blocks(rows, *widths):
    return [pl.BlockSpec((rows, w), lambda i, *_: (i, 0)) for w in widths]


def fixed(shape):
    return pl.BlockSpec(tuple(shape), functools.partial(lambda n, *_: (0,) * n, len(shape)))


def pack_kernel(live_ref, qkv_ref, proj_ref, up_ref, down_ref, qkv_out, up_out, down_out):
    count, slab, width = qkv_ref.shape
    lanes = min(128, width)
    for n in range(count):
        for t in range(width // lanes):
            at = (count * t + n) * lanes
            qkv_out[:, at : at + lanes] = qkv_ref[n][:, t * lanes : (t + 1) * lanes].astype(bf16)
    qkv_out[:, count * width :] = proj_ref[...].T.astype(bf16)
    up_out[:slab, :] = up_ref[...].astype(bf16)
    live = jnp.sum(jnp.sum(live_ref[...].astype(f32), axis=0, keepdims=True), axis=1, keepdims=True)
    high = jnp.floor(live * (1.0 / 256.0))
    middle = jnp.floor(live * (1.0 / 16.0)) - 16.0 * high
    low = live - 256.0 * high - 16.0 * middle
    row = lax.broadcasted_iota(jnp.int32, (DIGITS, up_out.shape[1]), 0)
    digits = jnp.where(row == 0, high, jnp.where(row == 1, middle, jnp.where(row == 2, low, 0.0)))
    up_out[slab:, :] = digits.astype(bf16)
    down_out[...] = down_ref[...].T.astype(bf16)


def first_kernel(tok_ref, par_ref, low_out):
    normed, _, _ = norm_forward(tok_ref[...], par_ref[0:1, :], par_ref[1:2, :])
    low_out[...] = normed.astype(bf16)


def block_rows(block, slab):
    return pl.ds(pl.multiple_of(block * slab, slab), slab)


def stack_z(pieces, slab, places):
    height, width = pieces[0].shape

    def kernel(at_ref, *refs):
        out = refs[-1]
        for k, ref in enumerate(refs[:-1]):
            out[block_rows(lax.rem(at_ref[0] + k, N_Z), slab), :] = ref[:slab, :]
        if height > slab:
            digits = refs[0][slab:, :].astype(f32)
            for ref in refs[1:-1]:
                digits = digits + ref[slab:, :].astype(f32)
            out[N_Z * slab :, :] = digits.astype(bf16)

    return plain_call(
        kernel,
        shaped(((N_Z - 1) * slab + height, width), bf16),
        *pieces,
        scalars=(places,),
        mebibytes=6,
        name="stack_z",
    )


def weave(columns, cuts, slab, places):
    n_x = len(columns[0])
    width = columns[0][0].shape[1]
    flat = [half for column in columns for half in column]
    edges = [0, *cuts, width]
    sizes = [stop - start for start, stop in zip(edges[:-1], edges[1:])]

    def kernel(at_ref, *refs):
        outs = refs[len(flat) :]
        for y in range(len(columns)):
            for dx in range(n_x):
                half = refs[y * n_x + dx]
                x = lax.rem(at_ref[1] + dx, n_x)
                for z in range(N_Z):
                    at = block_rows(z * n_x + x, slab)
                    for out, start, size in zip(outs, edges, sizes):
                        out[at, y * size : (y + 1) * size] = half[
                            z * slab : (z + 1) * slab, start : start + size
                        ]

    out = plain_call(
        kernel,
        tuple(shaped((N_Z * n_x * slab, size * len(columns)), bf16) for size in sizes),
        *flat,
        scalars=(places,),
        mebibytes=12,
        name="weave",
    )
    return out if cuts else out[0]


def proj_kernel(count, each, *refs):
    blocks, parts = refs[:count], refs[count : count + count // each]
    tok_ref, par_ref, res_out, low_out = refs[count + count // each :]
    total = tok_ref[...]
    for n, block in enumerate(blocks):
        size = block.shape[1]
        part = parts[n // each][:, n % each * size : (n % each + 1) * size]
        total = total + dot(block[...], part, 1, 1)
    res_out[...] = total
    normed, _, _ = norm_forward(total, par_ref[2:3, :], par_ref[3:4, :])
    low_out[...] = normed.astype(bf16)


ERF_TOP = (
    -2.72614225801306e-10,
    2.77068142495902e-08,
    -2.10102402082508e-06,
    -5.69250639462346e-05,
    -7.34990630326855e-04,
    -2.95459980854025e-03,
    -1.60960333262415e-02,
)
ERF_LOW = (
    -1.45660718464996e-05,
    -2.13374055278905e-04,
    -1.68282697438203e-03,
    -7.37332916720468e-03,
    -1.42647390514189e-02,
)


def erf(value):
    value = jnp.clip(value, -4.0, 4.0)
    square = value * value
    top = jnp.full_like(square, ERF_TOP[0])
    for number in ERF_TOP[1:]:
        top = top * square + number
    low = jnp.full_like(square, ERF_LOW[0])
    for number in ERF_LOW[1:]:
        low = low * square + number
    inverse = pl.reciprocal(low, approx=True)
    inverse = inverse * (2.0 - low * inverse)
    return value * top * inverse


def up_kernel(count, low_ref, *refs):
    outs = refs[-2 * count :]
    for n, part in enumerate(refs[:count]):
        hidden = dot(low_ref[...], part[...], 1, 0)
        share = 0.5 * (1.0 + erf(hidden * 0.7071067811865476))
        outs[2 * n][...] = (hidden * share).astype(bf16)
        slope = share + hidden * jnp.exp(-0.5 * hidden * hidden) * 0.3989422804014327
        outs[2 * n + 1][...] = slope.astype(bf16)


def up_call(low, parts, rows_all, spot, into):
    rows, model = low.shape
    width = parts[0].shape[1]
    cols = pl.BlockSpec((rows, TILE), lambda i, *_: (spot, i))
    return plain_call(
        functools.partial(up_kernel, len(parts)),
        (shaped((rows_all, width), bf16),) * (2 * len(parts)),
        low,
        *parts,
        grid=(width // TILE,),
        in_specs=[fixed(low.shape)] + [pl.BlockSpec((model, TILE), lambda i, *_: (0, i))] * len(parts),
        out_specs=(cols,) * (2 * len(parts)),
        into=into,
        mebibytes=14,
        name="up",
    )


def hidden_kernel(count, low_ref, *refs):
    outs = refs[-count:]
    for n in range(count):
        slope, part = refs[n], refs[count + n]
        outs[n][...] = (dot(low_ref[...], part[...], 1, 0) * slope[...].astype(f32)).astype(bf16)


def hidden_call(low, slopes, parts, spot, into):
    rows, model = low.shape
    width = parts[0].shape[1]
    cols = pl.BlockSpec((rows, TILE), lambda i, *_: (spot, i))
    return plain_call(
        functools.partial(hidden_kernel, len(parts)),
        tuple(shaped(slope.shape, bf16) for slope in slopes),
        low,
        *slopes,
        *parts,
        grid=(width // TILE,),
        in_specs=[fixed(low.shape)]
        + [cols] * len(parts)
        + [pl.BlockSpec((model, TILE), lambda i, *_: (0, i))] * len(parts),
        out_specs=(cols,) * len(parts),
        into=into,
        mebibytes=14,
        name="hidden",
    )


def wide_kernel(count, *refs):
    total = dot(refs[0][...], refs[count][...], 1, 1)
    for n in range(1, count):
        total = total + dot(refs[n][...], refs[count + n][...], 1, 1)
    refs[-1][...] = total.astype(refs[-1].dtype)


def wide_call(values, parts, rows, spot, kind):
    model, width = parts[0].shape
    return plain_call(
        functools.partial(wide_kernel, len(values)),
        shaped((rows, model), kind),
        *values,
        *parts,
        grid=(model // TILE,),
        in_specs=[pl.BlockSpec((rows, width), lambda i, *_: (spot, 0))] * len(values)
        + [pl.BlockSpec((TILE, width), lambda i, *_: (i, 0))] * len(parts),
        out_specs=pl.BlockSpec((rows, TILE), lambda i, *_: (0, i)),
        mebibytes=14,
        name="wide",
    )


def loss_kernel(count, *refs):
    res_ref, tea_ref, own_ref = refs[:3]
    live_ref, count_ref, grad_out, low_out, loss_out = refs[3 + count :]
    error = res_ref[...] - tea_ref[...] + own_ref[...]
    for ref in refs[3 : 3 + count]:
        error = error + ref[...].astype(f32)
    weighted = live_ref[...] * error
    grad = 2.0 * weighted / count_ref[...]
    grad_out[...] = grad
    low_out[...] = grad.astype(bf16)
    sums = jnp.sum(weighted * error, axis=0, keepdims=True)
    sums = jnp.concatenate([sums, jnp.zeros((7, sums.shape[1]), f32)], axis=0)
    loss_out[...] = jnp.where(pl.program_id(0) == 0, sums, loss_out[...] + sums)


def spread_kernel(count, low_ref, *refs):
    outs = refs[count:]
    tiles = len(outs) // count
    for n, part in enumerate(refs[:count]):
        piece = dot(low_ref[...], part[...], 1, 0).astype(bf16)
        lanes = piece.shape[1] // tiles
        for tile in range(tiles):
            outs[tile * count + n][...] = piece[:, tile * lanes : (tile + 1) * lanes]


def spread_call(low, parts):
    width = parts[0].shape[1]
    lanes = min(128, width)
    count = len(parts)
    out = plain_call(
        functools.partial(spread_kernel, count),
        tuple(shaped((low.shape[0], lanes), bf16) for _ in range(count * (width // lanes))),
        low,
        *parts,
        mebibytes=12,
        name="spread",
    )
    return [out[n : n + count] for n in range(0, len(out), count)]


def norm_sums(grad, scaled, out_ref, first):
    sums = jnp.concatenate(
        [
            jnp.sum(grad * scaled, axis=0, keepdims=True),
            jnp.sum(grad, axis=0, keepdims=True),
            jnp.zeros((6, grad.shape[1]), f32),
        ],
        axis=0,
    )
    out_ref[...] = jnp.where(first, sums, out_ref[...] + sums)


def middle_kernel(count, *refs):
    grad_ref, received = refs[0], refs[1 : 1 + count]
    res_ref, gout_ref, par_ref, full_out, low_out, sum_out = refs[1 + count :]
    _, scaled, inverse = norm_forward(res_ref[...], par_ref[2:3, :], par_ref[3:4, :])
    grad = grad_ref[...]
    for ref in received:
        grad = grad + ref[...].astype(f32)
    full = gout_ref[...] + norm_backward(grad, scaled, inverse, par_ref[2:3, :])
    full_out[...] = full
    low_out[...] = full.astype(bf16)
    norm_sums(grad, scaled, sum_out, pl.program_id(0) == 0)


def leave_kernel(count, *refs):
    own_ref, received = refs[0], refs[1 : 1 + count]
    tok_ref, res_ref, par_ref, two_ref, loss_ref, out_ref, sum_out, sum_ref = refs[1 + count :]
    _, scaled, inverse = norm_forward(tok_ref[...], par_ref[0:1, :], par_ref[1:2, :])
    grad = own_ref[...]
    for ref in received:
        grad = grad + ref[...].astype(f32)
    out_ref[...] = res_ref[...] + norm_backward(grad, scaled, inverse, par_ref[0:1, :])
    norm_sums(grad, scaled, sum_ref, pl.program_id(0) == 0)
    sum_out[...] = jnp.concatenate(
        [sum_ref[0:2, :], two_ref[0:2, :], loss_ref[0:1, :], jnp.zeros((3, grad.shape[1]), f32)],
        axis=0,
    )


def split_x(parts, n_x, places):
    model = parts[0].shape[0]
    slab = model // (N_Z * n_x)
    total = sum(part.shape[1] for part in parts)

    def kernel(at_ref, *refs):
        outs = refs[len(parts) :]
        for dx in range(n_x):
            x = lax.rem(at_ref[1] + dx, n_x)
            for z in range(N_Z):
                at = block_rows(z * n_x + x, slab)
                lane = 0
                for ref in refs[: len(parts)]:
                    size = ref.shape[1]
                    outs[dx][z * slab : (z + 1) * slab, lane : lane + size] = ref[at, :]
                    lane += size

    return plain_call(
        kernel,
        tuple(shaped((model // n_x, total), bf16) for _ in range(n_x)),
        *parts,
        scalars=(places,),
        mebibytes=10,
        name="split_x",
    )


def sum_in_order(pieces, spots):
    def kernel(spot_ref, *refs):
        out, held = refs[-2:]
        for n, ref in enumerate(refs[:-2]):
            held[spot_ref[n]] = ref[...]
        total = held[0]
        for n in range(1, len(pieces)):
            total = total + held[n]
        out[...] = total

    return plain_call(
        kernel,
        shaped(pieces[0].shape, f32),
        *pieces,
        scalars=(spots,),
        scratch=[pltpu.VMEM((len(pieces),) + pieces[0].shape, f32)],
        mebibytes=6,
        name="sum_in_order",
    )


def split_z(parts, places):
    rows, width = parts[0].shape
    slab = rows // N_Z

    def kernel(at_ref, *refs):
        for k, out in enumerate(refs[len(parts) :]):
            at = block_rows(lax.rem(at_ref[0] + k, N_Z), slab)
            total = refs[0][at, :].astype(f32)
            for ref in refs[1 : len(parts)]:
                total = total + ref[at, :].astype(f32)
            out[...] = total.astype(out.dtype)

    shapes = (shaped((slab, width), f32),) + (shaped((slab, width), bf16),) * (N_Z - 1)
    return plain_call(kernel, shapes, *parts, scalars=(places,), mebibytes=8, name="split_z")


def adam_kernel(layout, counts, *refs):
    grads = []
    for count in counts:
        grad = refs[0][...].astype(f32)
        for ref in refs[1:count]:
            grad = grad + ref[...].astype(f32)
        grads.append(grad)
        refs = refs[count:]
    count = len(layout)
    states, outs = refs[: 3 * count], refs[3 * count :]
    for n, (source, start, size, turned) in enumerate(layout):
        weight, first, second = states[3 * n : 3 * n + 3]
        if len(weight.shape) == 3:
            matrices = weight.shape[0]
            lanes = size // matrices
            for k in range(matrices):
                own = [
                    grads[at][:, lane + k * lanes : lane + (k + 1) * lanes] for at, lane in start
                ]
                own = own[0] if len(own) == 1 else jnp.concatenate(own, axis=1)
                new = adam_step(weight[k], own, first[k], second[k], weight_decay, learn_rate)
                for out, value in zip(outs[3 * n : 3 * n + 3], new):
                    out[k] = value
        else:
            part = grads[source][:, start : start + size]
            if turned:
                part = part.T
            new = adam_step(weight[...], part, first[...], second[...], weight_decay, learn_rate)
            for out, value in zip(outs[3 * n : 3 * n + 3], new):
                out[...] = value


def adam_call(groups, layout, *states):
    shapes = tuple(shaped(s.shape, f32) for s in states)
    out = plain_call(
        functools.partial(adam_kernel, layout, [len(group) for group in groups]),
        shapes,
        *[piece for group in groups for piece in group],
        *states,
        mebibytes=16,
        name="adam",
    )
    return [out[3 * n : 3 * n + 3] for n in range(len(layout))]


def tie(*values):
    return lax.optimization_barrier(values)


def local(
    n_x,
    n_y,
    tokens,
    teacher,
    segments,
    live_mask,
    weight_qkv,
    weight_proj,
    weight_up,
    weight_down,
    norm_params,
    first_qkv,
    first_proj,
    first_up,
    first_down,
    first_norms,
    second_qkv,
    second_proj,
    second_up,
    second_down,
    second_norms,
):
    z_at, x_at = lax.axis_index("z"), lax.axis_index("x")
    y_at, core_at = lax.axis_index("y"), lax.axis_index("core")
    rows, model = tokens.shape
    group_rows = segments.shape[0]
    slab = weight_qkv.shape[1]
    width = weight_qkv.shape[2]
    unit = weight_up.shape[1]
    part_rows = min(128, rows)
    depth = N_Z * slab
    sizes = {"z": N_Z, "x": n_x, "y": n_y, "core": N_CORE}
    places = jnp.stack([z_at, x_at]).astype(jnp.int32)
    offsets = [(dc, dy) for dc in range(N_CORE) for dy in range(n_y)]
    other = N_CORE - 1

    def send(value, axis, step):
        size = sizes[axis]
        return lax.ppermute(value, axis, [(i, (i + step) % size) for i in range(size)])

    def send_col(value, dy, dc):
        perm = [
            (y * N_CORE + c, (y + dy) % n_y * N_CORE + (c + dc) % N_CORE)
            for y in range(n_y)
            for c in range(N_CORE)
        ]
        return lax.ppermute(value, ("y", "core"), perm)

    def fetch(value, axis):
        return [value] + [send(value, axis, -k) for k in range(1, sizes[axis])]

    def place(dy, dc):
        return ((y_at + dy) % n_y * N_CORE + (core_at + dc) % N_CORE) * rows

    shard_qkv, shard_up, shard_down = plain_call(
        pack_kernel,
        (
            shaped((slab, 4 * width), bf16),
            shaped((slab + DIGITS, unit), bf16),
            shaped((slab, unit), bf16),
        ),
        live_mask.reshape(-1, 128),
        weight_qkv,
        weight_proj,
        weight_up,
        weight_down,
        mebibytes=8,
        name="pack",
    )
    near_qkv = fetch(shard_qkv, "z")
    low_one = plain_call(
        first_kernel,
        shaped(tokens.shape, bf16),
        tokens,
        norm_params,
        grid=(rows // part_rows,),
        in_specs=row_blocks(part_rows, model) + [fixed(norm_params.shape)],
        out_specs=row_blocks(part_rows, model)[0],
        mebibytes=8,
        name="first",
    )
    blocks_one = fetch(low_one, "y")
    near_qkv, shard_down, shard_up, blocks_one = tie(near_qkv, shard_down, shard_up, blocks_one)

    block_qkv = stack_z(near_qkv, slab, places)
    near_one = jnp.concatenate(blocks_one, axis=0)
    near_one, block_qkv = tie(near_one, block_qkv)
    beside_qkv = fetch(block_qkv, "x")
    near_up = fetch(shard_up, "z")
    far_one = send(near_one, "core", -1)
    geometry = attend_geometry(segments, live_mask)
    own_live = lax.dynamic_slice_in_dim(
        live_mask, (y_at * N_CORE + core_at) * rows, rows, 0
    ).astype(f32)[:, None]
    group_one = jnp.zeros((group_rows, model), bf16)
    for dc, dy in offsets:
        block = (far_one if dc else near_one)[dy * rows : (dy + 1) * rows]
        group_one = lax.dynamic_update_slice_in_dim(group_one, block, place(dy, dc), 0)
    beside_qkv, near_up, group_one, geometry, own_live, shard_down = tie(
        beside_qkv, near_up, group_one, geometry, own_live, shard_down
    )

    block_up = stack_z(near_up, slab, places)
    full_qkv, part_proj = weave([beside_qkv], [3 * width], slab, places)
    block_up, part_proj = tie(block_up, part_proj)
    beside_up = fetch(block_up, "x")
    near_down = fetch(shard_down, "z")
    full_proj = fetch(part_proj, "y")
    projected = dot(group_one, full_qkv, 1, 0).astype(bf16)
    mixed = attend_forward(projected, geometry)
    mixed, beside_up, near_down, full_proj = tie(mixed, beside_up, near_down, full_proj)

    blocks_mixed = []
    for dc, dy in offsets:
        piece = lax.dynamic_slice_in_dim(mixed, place(-dy, -dc), rows, 0)
        blocks_mixed.append(piece if (dc, dy) == (0, 0) else send_col(piece, -dy, -dc))
    full_proj = full_proj + [send(part, "core", -1) for part in full_proj]
    block_down = stack_z(near_down, slab, places)
    full_up = [weave([beside_up], [], slab, places)]
    live_count = sum(
        256.0 * part[depth, 0].astype(f32) + 16.0 * part[depth + 1, 0].astype(f32)
        + part[depth + 2, 0].astype(f32)
        for part in beside_up
    ).reshape(1, 1)
    blocks_mixed, full_proj, full_up, live_count, block_down = tie(
        blocks_mixed, full_proj, full_up, live_count, block_down
    )
    beside_down = fetch(block_down, "x")
    full_up.append(send(full_up[0], "core", -1))
    count = len(offsets)
    residual, low_two = plain_call(
        functools.partial(proj_kernel, count, 1),
        (shaped(tokens.shape, f32), shaped(tokens.shape, bf16)),
        *blocks_mixed,
        *full_proj,
        tokens,
        norm_params,
        grid=(rows // part_rows,),
        in_specs=row_blocks(part_rows, *([width] * count))
        + [fixed(part.shape) for part in full_proj]
        + row_blocks(part_rows, model)
        + [fixed(norm_params.shape)],
        out_specs=tuple(row_blocks(part_rows, model, model)),
        mebibytes=16,
        name="proj",
    )
    low_two, full_up = tie(low_two, full_up)

    chunk = min(256, rows)
    chunks = range(rows // chunk)
    neighbours = range(1, n_y)
    rows_all = n_y * rows

    def cross(value, n, back):
        piece = value[n * chunk : (n + 1) * chunk]
        return {dy: send(piece, "y", dy if back else -dy) for dy in neighbours}

    def spot_of(dy, n):
        return (dy * rows) // chunk + n

    low_far = {0: cross(low_two, 0, False)}
    hidden = up_call(low_two, full_up, rows_all, 0, ())
    low_far[0], hidden, beside_down, low_two = tie(low_far[0], hidden, beside_down, low_two)
    full_down = [weave([beside_down], [], slab, places)]
    full_down.append(send(full_down[0], "core", -1))
    far_out = {}
    for n in chunks:
        if n + 1 in chunks:
            low_far[n + 1] = cross(low_two, n + 1, False)
        for dy in neighbours:
            hidden = up_call(low_far[n][dy], full_up, rows_all, spot_of(dy, n), hidden)
        outs = {
            dy: wide_call(hidden[::2], full_down, chunk, spot_of(dy, n), bf16) for dy in neighbours
        }
        if n + 1 in chunks:
            outs, hidden, low_far[n + 1] = tie(outs, hidden, low_far[n + 1])
        else:
            outs, hidden = tie(outs, hidden)
        if n:
            far_out[n - 1] = tie(far_out[n - 1], outs)[0]
        far_out[n] = {dy: send(outs[dy], "y", -dy) for dy in neighbours}
    own_out = wide_call(hidden[::2], full_down, rows, 0, f32)
    own_out, far_out = tie(own_out, far_out)
    far_out = [
        jnp.concatenate([far_out[n][dy] for n in chunks], axis=0) for dy in neighbours
    ]
    grad_output, grad_branch, loss_rows = plain_call(
        functools.partial(loss_kernel, len(far_out)),
        (shaped(tokens.shape, f32), shaped(tokens.shape, bf16), shaped((8, model), f32)),
        residual,
        teacher,
        own_out,
        *far_out,
        own_live,
        live_count,
        grid=(rows // part_rows,),
        in_specs=row_blocks(part_rows, *([model] * (3 + len(far_out))), 1) + [fixed((1, 1))],
        out_specs=tuple(row_blocks(part_rows, model, model) + [fixed((8, model))]),
        mebibytes=14,
        name="loss",
    )
    active, slope = hidden[::2], hidden[1::2]

    grad_far = {0: cross(grad_branch, 0, False)}
    grad_hidden = hidden_call(grad_branch, slope, full_down, 0, ())
    own_two = wide_call(grad_hidden, full_up, rows, 0, f32)
    grad_far[0], grad_hidden, own_two, grad_branch = tie(
        grad_far[0], grad_hidden, own_two, grad_branch
    )
    def gather_rows(own, far):
        return jnp.concatenate([own] + [far[n][dy] for dy in neighbours for n in chunks], axis=0)

    far_two = {}
    for n in chunks:
        if n + 1 in chunks:
            grad_far[n + 1] = cross(grad_branch, n + 1, False)
        else:
            grad_all = gather_rows(grad_branch, grad_far)
            far_down = dot(grad_all, active[other], 0, 0).astype(bf16)
            far_down, grad_hidden, grad_far[n] = tie(far_down, grad_hidden, grad_far[n])
            sent_down = send(far_down, "core", 1)
        for dy in neighbours:
            grad_hidden = hidden_call(
                grad_far[n][dy], slope, full_down, spot_of(dy, n), grad_hidden
            )
        outs = {
            dy: wide_call(grad_hidden, full_up, chunk, spot_of(dy, n), bf16) for dy in neighbours
        }
        if n + 1 in chunks:
            outs, grad_hidden, grad_far[n + 1] = tie(outs, grad_hidden, grad_far[n + 1])
        else:
            outs, grad_hidden, sent_down, grad_all = tie(outs, grad_hidden, sent_down, grad_all)
        if n:
            far_two[n - 1] = tie(far_two[n - 1], outs)[0]
        far_two[n] = {dy: send(outs[dy], "y", -dy) for dy in neighbours}

    low_all = gather_rows(low_two, low_far)
    hold_down = (dot(grad_all, active[0], 0, 0) + sent_down.astype(f32)).astype(bf16)
    halves_down = split_x([hold_down], n_x, places)
    far_up = dot(low_all, grad_hidden[other], 0, 0).astype(bf16)
    far_two, halves_down, far_up, low_all = tie(far_two, halves_down, far_up, low_all)
    far_two = [
        jnp.concatenate([far_two[n][dy] for n in chunks], axis=0) for dy in neighbours
    ]
    grad_residual, grad_low, sums_two = plain_call(
        functools.partial(middle_kernel, len(far_two)),
        (shaped(tokens.shape, f32), shaped(tokens.shape, bf16), shaped((8, model), f32)),
        own_two,
        *far_two,
        residual,
        grad_output,
        norm_params,
        grid=(rows // part_rows,),
        in_specs=row_blocks(part_rows, *([model] * (3 + len(far_two)))) + [fixed(norm_params.shape)],
        out_specs=tuple(row_blocks(part_rows, model, model) + [fixed((8, model))]),
        mebibytes=14,
        name="middle",
    )
    pieces_attn = spread_call(grad_low, full_proj)
    pieces_attn, far_up, halves_down, grad_low, low_all = tie(
        pieces_attn, far_up, halves_down, grad_low, low_all
    )

    def send_back(pieces):
        return [
            piece if key == (0, 0) else send_col(piece, key[1], key[0])
            for key, piece in zip(offsets, pieces)
        ]

    def hop_x(halves):
        return [halves[0]] + [send(halves[dx], "x", dx) for dx in range(1, n_x)]

    def spread_z(pieces):
        return [pieces[0]] + [send(pieces[k], "z", k) for k in range(1, N_Z)]

    lanes = 3 * min(128, width)
    tiles = 3 * width // lanes
    spots = jnp.stack([place(-dy, -dc) for dc, dy in offsets]).astype(jnp.int32)
    sent_attn = send_back(pieces_attn[0])
    parts_down = hop_x(halves_down)
    sent_up = send(far_up, "core", 1)
    sent_attn, low_all = tie(sent_attn, low_all)

    sent_later = [send_back(pieces) for pieces in pieces_attn[1:]]
    grad_projected = attend_backward(projected, sent_attn, spots, geometry, 0, ())
    grad_projected, sent_later, sent_up, parts_down, grad_low = tie(
        grad_projected, sent_later, sent_up, parts_down, grad_low
    )

    hold_up = (dot(low_all, grad_hidden[0], 0, 0) + sent_up.astype(f32)).astype(bf16)
    halves_up = split_x([hold_up], n_x, places)
    pieces_down = split_z(parts_down, places)
    grad_projected, halves_up, pieces_down, grad_low = tie(
        grad_projected, halves_up, pieces_down, grad_low
    )
    parts_up = hop_x(halves_up)
    last_down = spread_z(pieces_down)
    for tile in range(1, tiles):
        grad_projected = attend_backward(
            projected, sent_later[tile - 1], spots, geometry, tile, (grad_projected,)
        )
    grad_proj = [dot(grad_low, block, 0, 0).astype(bf16) for block in blocks_mixed]
    far_proj = jnp.concatenate(grad_proj[n_y:], axis=1)
    grad_projected, parts_up, last_down, far_proj, grad_proj = tie(
        grad_projected, parts_up, last_down, far_proj, grad_proj
    )

    sent_proj = send(far_proj, "core", 1)
    parts = {
        key: dot(
            lax.dynamic_slice_in_dim(grad_projected, place(key[1], key[0]), rows, 0),
            full_qkv,
            1,
            1,
        )
        for key in reversed(offsets)
    }
    far_one = jnp.concatenate([parts[other, dy].astype(bf16) for dy in range(n_y)], axis=0)
    far_one, sent_proj, grad_projected = tie(far_one, sent_proj, grad_projected)
    sent_one = send(far_one, "core", 1)
    hold_proj = [
        (
            grad_proj[dy].astype(f32) + sent_proj[:, dy * width : (dy + 1) * width].astype(f32)
        ).astype(bf16)
        for dy in range(n_y)
    ]
    part_proj = [hold_proj[0]] + [send(hold_proj[k], "y", k) for k in range(1, n_y)]
    grad_qkv = dot(group_one, grad_projected, 0, 0).astype(bf16)
    pieces_up = split_z(parts_up, places)
    pieces_up, grad_qkv, sent_one, parts, part_proj = tie(
        pieces_up, grad_qkv, sent_one, parts, part_proj
    )

    total = part_proj[0].astype(f32)
    for piece in part_proj[1:]:
        total = total + piece.astype(f32)
    halves_qkv = split_x([grad_qkv, total.astype(bf16)], n_x, places)
    parts = [
        parts[0, dy] + sent_one[dy * rows : (dy + 1) * rows].astype(f32) for dy in range(n_y)
    ]
    sent_parts = [parts[k].astype(bf16) for k in range(1, n_y)]
    halves_qkv, sent_parts, pieces_up = tie(halves_qkv, sent_parts, pieces_up)
    received = [send(part, "y", k) for k, part in enumerate(sent_parts, 1)]
    parts_qkv = hop_x(halves_qkv)
    last_up = spread_z(pieces_up)
    parts_qkv, received, last_up = tie(parts_qkv, received, last_up)

    pieces_qkv = split_z(parts_qkv, places)
    pieces_qkv, received = tie(pieces_qkv, received)
    last_qkv = spread_z(pieces_qkv)
    token_grad, sums = plain_call(
        functools.partial(leave_kernel, len(received)),
        (shaped(tokens.shape, f32), shaped((8, model), f32)),
        parts[0],
        *received,
        tokens,
        grad_residual,
        norm_params,
        sums_two,
        loss_rows,
        grid=(rows // part_rows,),
        in_specs=row_blocks(part_rows, *([model] * (3 + len(received))))
        + [fixed(norm_params.shape), fixed((8, model)), fixed((8, model))],
        out_specs=tuple(row_blocks(part_rows, model) + [fixed((8, model))]),
        scratch=[pltpu.VMEM((8, model), f32)],
        mebibytes=14,
        name="leave",
    )
    for axis in ("core", "y"):
        step = 1
        while step < sizes[axis]:
            pairs = [(i, i ^ step) for i in range(sizes[axis])]
            sums = sums + lax.ppermute(sums, axis, pairs)
            step *= 2
    sums, token_grad, last_qkv = tie(sums, token_grad, last_qkv)
    for axis, at in (("x", x_at), ("z", z_at)):
        around = jnp.stack([(at + k) % sizes[axis] for k in range(sizes[axis])])
        sums = sum_in_order(fetch(sums, axis), around.astype(jnp.int32))
    loss_sum = jnp.sum(sums[4])
    live_count = live_count[0, 0]

    (new_down,) = adam_call(
        [last_down], [(0, 0, unit, True)], weight_down, first_down, second_down
    )
    (new_up,) = adam_call([last_up], [(0, 0, unit, False)], weight_up, first_up, second_up)
    new_qkv, new_proj = adam_call(
        [last_qkv],
        [(0, [(0, n * lanes) for n in range(tiles)], lanes, False), (0, 3 * width, width, True)],
        weight_qkv,
        first_qkv,
        second_qkv,
        weight_proj,
        first_proj,
        second_proj,
    )
    new_norms = adam_step(norm_params, sums[:4], first_norms, second_norms, 0.0, norm_rate)
    return (
        loss_sum / live_count,
        token_grad,
        new_qkv[0],
        new_proj[0],
        new_up[0],
        new_down[0],
        new_norms[0],
        new_qkv[1],
        new_proj[1],
        new_up[1],
        new_down[1],
        new_norms[1],
        new_qkv[2],
        new_proj[2],
        new_up[2],
        new_down[2],
        new_norms[2],
    )


def solution(mesh):
    n_x = mesh.shape["row"] // N_Z
    n_y = mesh.shape["col"] // N_CORE
    mesh = jax.sharding.Mesh(
        mesh.devices.reshape(N_Z, n_x, n_y, N_CORE), ("z", "x", "y", "core")
    )
    row, col = ("z", "x"), ("y", "core")
    matrices = (P(None, row, col), P(col, row), P(row, col), P(col, row), P())
    tokens = P(row + col, None)
    return jax.shard_map(
        functools.partial(local, n_x, n_y),
        mesh=mesh,
        in_specs=(tokens, tokens, P(row), P(row)) + matrices * 3,
        out_specs=(P(), tokens) + matrices * 3,
        check_vma=False,
    )
```

```python
import functools

import jax
import jax.numpy as jnp
from jax import lax
from jax.experimental import pallas as pl
from jax.experimental.pallas import tpu as pltpu
from jax.sharding import PartitionSpec as P

HEAD_DIM = 64
PATCHES = 577
STEP = 10
WINDOW = 640
QROWS = 320
TILE = 256
DIGITS = 16
SMALL = pl.CostEstimate(flops=1024, bytes_accessed=1024, transcendentals=0)
N_Z = 4
N_CORE = 2

layer_eps = 1e-06
adam_eps = 1e-08
learn_rate = 0.03
norm_rate = 0.25
moment_decay = 0.5
weight_decay = 0.05

bf16 = jnp.bfloat16
f32 = jnp.float32


def norm_forward(values, gain_row, bias_row):
    average = jnp.mean(values, axis=-1, keepdims=True)
    centred = values - average
    variance = jnp.mean(centred * centred, axis=-1, keepdims=True)
    inverse = lax.rsqrt(variance + layer_eps)
    scaled = centred * inverse
    return (scaled * gain_row + bias_row, scaled, inverse)


def norm_backward(upstream, scaled, inverse, gain_row):
    weighted = upstream * gain_row
    return inverse * (
        weighted
        - jnp.mean(weighted, axis=-1, keepdims=True)
        - scaled * jnp.mean(weighted * scaled, axis=-1, keepdims=True)
    )


def gelu_slope(hidden):
    return (
        0.5 * (1.0 + lax.erf(hidden * 0.7071067811865476))
        + hidden * jnp.exp(-0.5 * hidden * hidden) * 0.3989422804014327
    )


def adam_step(weight, gradient, momentum, variance, decay_rate, rate):
    momentum = moment_decay * momentum + (1.0 - moment_decay) * gradient
    variance = moment_decay * variance + (1.0 - moment_decay) * gradient * gradient
    correction = 1.0 - moment_decay**STEP
    direction = momentum / correction / (jnp.sqrt(variance / correction) + adam_eps)
    return (weight - rate * (direction + decay_rate * weight), momentum, variance)


def dot(left, right, left_dim, right_dim):
    return lax.dot_general(
        left, right, (((left_dim,), (right_dim,)), ((), ())), preferred_element_type=f32
    )


def head_lanes(width, head):
    lanes = lax.broadcasted_iota(jnp.int32, (1, width), 1)
    return (lanes >= head * HEAD_DIM) & (lanes < (head + 1) * HEAD_DIM)


def attend_weights(q_part, k_all, bias, row_start, rows_in):
    scores = dot(q_part, k_all, 1, 1) * HEAD_DIM ** (-0.5)
    rows, window = scores.shape
    row_ids = row_start + lax.broadcasted_iota(jnp.int32, (rows, window), 0)
    col_ids = lax.broadcasted_iota(jnp.int32, (rows, window), 1)
    scores = jnp.where(row_ids == col_ids, scores, scores + bias)
    weights = jnp.exp(scores - jnp.max(scores, axis=-1, keepdims=True))
    totals = jnp.sum(weights, axis=-1, keepdims=True)
    return weights * jnp.where(rows_in, 1.0 / totals, 0.0)


def image_window(begin, code_ref, group_rows):
    image = pl.program_id(0)
    start = jnp.minimum(begin[image] // 16 * 16, group_rows - WINDOW)
    first = begin[image] - start
    start = pl.multiple_of(start, 16)
    code = code_ref[pl.ds(start, WINDOW), :]
    bias = jnp.where(code == image, 0.0, -1e30).astype(f32).T[0:1, :]
    return image, start, first, bias


def rows_inside(rows, row_start, first):
    ids = row_start + lax.broadcasted_iota(jnp.int32, (rows, 1), 0)
    return (ids >= first) & (ids < first + PATCHES)


def attend_forward_kernel(blocks, begin, spots, code_ref, *refs):
    image, start, first, bias = image_window(begin, code_ref, refs[0].shape[0])
    out_ref = refs[-1]
    lanes = refs[0].shape[1]

    for tile in range((len(refs) - 1 - blocks) // 3):
        q_ref, k_ref, v_ref = refs[3 * tile : 3 * tile + 3]
        cols = slice(tile * lanes, (tile + 1) * lanes)

        @pl.when(image == 0)
        def _():
            out_ref[:, cols] = v_ref[...]

        k_all = k_ref[pl.ds(start, WINDOW), :]
        v_all = v_ref[pl.ds(start, WINDOW), :]
        for row in range(0, WINDOW, QROWS):
            at = pl.ds(pl.multiple_of(start + row, 16), QROWS)
            q_part = q_ref[at, :]
            inside = rows_inside(QROWS, row, first)
            mixed = None
            for head in range(lanes // HEAD_DIM):
                mine = head_lanes(lanes, head)
                q_head = jnp.where(mine, q_part, jnp.zeros_like(q_part))
                weights = attend_weights(q_head, k_all, bias, row, inside).astype(bf16)
                part = dot(weights, v_all, 1, 0)
                mixed = part if mixed is None else jnp.where(mine, part, mixed)
            out_ref[at, cols] = jnp.where(inside, mixed.astype(bf16), out_ref[at, cols])

    @pl.when(image == pl.num_programs(0) - 1)
    def _():
        for n, block in enumerate(refs[-1 - blocks : -1]):
            rows = block.shape[0]
            block[...] = out_ref[pl.ds(pl.multiple_of(spots[n], rows), rows), :]


def attend_backward_kernel(blocks, begin, spots, code_ref, q_ref, k_ref, v_ref, *refs):
    image, start, first, bias = image_window(begin, code_ref, q_ref.shape[0])
    out_ref, p_ref, s_ref, go_ref = refs[-4:]
    lanes = q_ref.shape[1]
    rows = refs[0].shape[0]

    @pl.when(image == 0)
    def _():
        for n, block_ref in enumerate(refs[:blocks]):
            go_ref[pl.ds(pl.multiple_of(spots[n], rows), rows), :] = block_ref[...]
        out_ref[:, : 2 * lanes] = jnp.zeros((out_ref.shape[0], 2 * lanes), bf16)
        out_ref[:, 2 * lanes :] = go_ref[...]

    whole = pl.ds(start, WINDOW)
    inside_all = rows_inside(WINDOW, 0, first)
    q_cols, k_cols, v_cols = [slice(n * lanes, (n + 1) * lanes) for n in range(3)]
    k_all = k_ref[whole, :]
    v_all = v_ref[whole, :]
    q_all = q_ref[whole, :]
    go_all = go_ref[whole, :]
    key_grad = None
    value_grad = None
    for head in range(lanes // HEAD_DIM):
        mine = head_lanes(lanes, head)
        for row in range(0, WINDOW, QROWS):
            at = pl.ds(pl.multiple_of(start + row, 16), QROWS)
            q_part = q_ref[at, :]
            go_part = go_ref[at, :]
            inside = rows_inside(QROWS, row, first)
            q_head = jnp.where(mine, q_part, jnp.zeros_like(q_part))
            go_head = jnp.where(mine, go_part, jnp.zeros_like(go_part))
            weights = attend_weights(q_head, k_all, bias, row, inside)
            weight_grad = dot(go_head, v_all, 1, 1)
            product = weights * weight_grad
            score_grad = (
                product - weights * jnp.sum(product, axis=-1, keepdims=True)
            ).astype(bf16)
            p_ref[row : row + QROWS, :] = weights.astype(bf16)
            s_ref[row : row + QROWS, :] = score_grad
            query_grad = (dot(score_grad, k_all, 1, 0) * HEAD_DIM ** (-0.5)).astype(bf16)
            out_ref[at, q_cols] = jnp.where(inside & mine, query_grad, out_ref[at, q_cols])
        q_mine = jnp.where(mine, q_all, jnp.zeros_like(q_all))
        go_mine = jnp.where(mine, go_all, jnp.zeros_like(go_all))
        key_part = dot(q_mine, s_ref[...], 0, 0)
        value_part = dot(go_mine, p_ref[...], 0, 0)
        key_grad = key_part if key_grad is None else key_grad + key_part
        value_grad = value_part if value_grad is None else value_grad + value_part
    key_rows = (key_grad.T * HEAD_DIM ** (-0.5)).astype(bf16)
    value_rows = value_grad.T.astype(bf16)
    out_ref[whole, k_cols] = jnp.where(inside_all, key_rows, out_ref[whole, k_cols])
    out_ref[whole, v_cols] = jnp.where(inside_all, value_rows, out_ref[whole, v_cols])


def qkv_operands(projected, tile):
    group_rows, total = projected.shape
    lanes = min(128, total // 3)
    if lanes % 128 == 0:
        specs = [
            pl.BlockSpec((group_rows, lanes), functools.partial(lambda n, i, *_: (0, n), 3 * tile + n))
            for n in range(3)
        ]
        return [projected] * 3, specs
    parts = [projected[:, n * lanes : (n + 1) * lanes] for n in range(3)]
    return parts, [fixed((group_rows, lanes))] * 3


def attend_forward(projected, geometry, spots, rows):
    begin, code = geometry
    group_rows, total = projected.shape
    width = total // 3
    blocks = group_rows // rows
    operands, specs = [], []
    for tile in range(width // min(128, width)):
        more, places = qkv_operands(projected, tile)
        operands += more
        specs += places
    return plain_call(
        functools.partial(attend_forward_kernel, blocks),
        (shaped((rows, width), bf16),) * blocks,
        code,
        *operands,
        grid=begin.shape,
        in_specs=[fixed(code.shape)] + specs,
        scratch=[pltpu.VMEM((group_rows, width), bf16)],
        scalars=(begin, spots),
        mebibytes=20,
        name="attention_forward",
    )


def attend_backward(projected, go_blocks, spots, geometry, tile, into):
    begin, code = geometry
    group_rows, total = projected.shape
    lanes = min(128, total // 3)
    operands, specs = qkv_operands(projected, tile)
    rows = go_blocks[0].shape[0]
    return plain_call(
        functools.partial(attend_backward_kernel, len(go_blocks)),
        shaped((group_rows, total), bf16),
        code,
        *operands,
        *go_blocks,
        grid=begin.shape,
        in_specs=[fixed(code.shape)]
        + specs
        + [fixed((rows, lanes))] * len(go_blocks),
        out_specs=pl.BlockSpec((group_rows, 3 * lanes), lambda i, *_: (0, tile)),
        scratch=[pltpu.VMEM((WINDOW, WINDOW), bf16)] * 2 + [pltpu.VMEM((group_rows, lanes), bf16)],
        scalars=(begin, spots),
        into=into,
        mebibytes=20,
        name="attention_backward",
    )


def attend_geometry(segments, live_mask):
    group_rows = segments.shape[0]
    numbers = jnp.arange(group_rows // PATCHES, dtype=jnp.int32)
    positions = jnp.arange(group_rows, dtype=jnp.int32)
    begin = jnp.min(
        jnp.where(segments[None, :] == numbers[:, None], positions[None, :], group_rows - PATCHES),
        axis=1,
    )
    code = jnp.where(live_mask == 1, segments, -1)
    return begin, jnp.broadcast_to(code[:, None], (group_rows, 128))


def plain_call(kernel, out_shape, *operands, grid=(), in_specs=None, out_specs=None, scratch=(), scalars=(), into=(), mebibytes=16, name=None):
    params = pltpu.CompilerParams(vmem_limit_bytes=mebibytes * 1024 * 1024)
    if in_specs is None:
        in_specs = [pl.BlockSpec(a.shape, functools.partial(lambda n, *_: (0,) * n, a.ndim)) for a in operands]
    in_specs = list(in_specs) + [pl.BlockSpec(memory_space=pl.ANY)] * len(into)
    if out_specs is None:
        out_specs = jax.tree.map(
            lambda s: pl.BlockSpec(s.shape, functools.partial(lambda n, *_: (0,) * n, len(s.shape))), out_shape
        )
    return pl.pallas_call(
        kernel,
        grid_spec=pltpu.PrefetchScalarGridSpec(
            num_scalar_prefetch=len(scalars),
            grid=grid,
            in_specs=in_specs,
            out_specs=out_specs,
            scratch_shapes=list(scratch),
        ),
        out_shape=out_shape,
        input_output_aliases={len(scalars) + len(operands) + n: n for n in range(len(into))},
        compiler_params=params,
        cost_estimate=SMALL,
        name=name,
    )(*scalars, *operands, *into)


def shaped(shape, dtype):
    return jax.ShapeDtypeStruct(tuple(shape), dtype)


def row_blocks(rows, *widths):
    return [pl.BlockSpec((rows, w), lambda i, *_: (i, 0)) for w in widths]


def fixed(shape):
    return pl.BlockSpec(tuple(shape), functools.partial(lambda n, *_: (0,) * n, len(shape)))


def pack_kernel(live_ref, qkv_ref, proj_ref, up_ref, down_ref, qkv_out, up_out, down_out):
    count, slab, width = qkv_ref.shape
    lanes = min(128, width)
    for n in range(count):
        for t in range(width // lanes):
            at = (count * t + n) * lanes
            qkv_out[:, at : at + lanes] = qkv_ref[n][:, t * lanes : (t + 1) * lanes].astype(bf16)
    qkv_out[:, count * width :] = proj_ref[...].T.astype(bf16)
    up_out[:slab, :] = up_ref[...].astype(bf16)
    live = jnp.sum(jnp.sum(live_ref[...].astype(f32), axis=0, keepdims=True), axis=1, keepdims=True)
    high = jnp.floor(live * (1.0 / 256.0))
    middle = jnp.floor(live * (1.0 / 16.0)) - 16.0 * high
    low = live - 256.0 * high - 16.0 * middle
    row = lax.broadcasted_iota(jnp.int32, (DIGITS, up_out.shape[1]), 0)
    digits = jnp.where(row == 0, high, jnp.where(row == 1, middle, jnp.where(row == 2, low, 0.0)))
    up_out[slab:, :] = digits.astype(bf16)
    down_out[...] = down_ref[...].T.astype(bf16)


def first_kernel(tok_ref, par_ref, low_out):
    normed, _, _ = norm_forward(tok_ref[...], par_ref[0:1, :], par_ref[1:2, :])
    low_out[...] = normed.astype(bf16)


def place_blocks(blocks, spots):
    rows, width = blocks[0].shape

    def kernel(spot_ref, *refs):
        for n, ref in enumerate(refs[:-1]):
            refs[-1][pl.ds(pl.multiple_of(spot_ref[n], rows), rows), :] = ref[...]

    return plain_call(
        kernel,
        shaped((rows * len(blocks), width), bf16),
        *blocks,
        scalars=(spots,),
        mebibytes=20,
        name="place_blocks",
    )


def block_rows(block, slab):
    return pl.ds(pl.multiple_of(block * slab, slab), slab)


def stack_z(pieces, slab, places):
    height, width = pieces[0].shape

    def kernel(at_ref, *refs):
        out = refs[-1]
        for k, ref in enumerate(refs[:-1]):
            out[block_rows(lax.rem(at_ref[0] + k, N_Z), slab), :] = ref[:slab, :]
        if height > slab:
            digits = refs[0][slab:, :].astype(f32)
            for ref in refs[1:-1]:
                digits = digits + ref[slab:, :].astype(f32)
            out[N_Z * slab :, :] = digits.astype(bf16)

    return plain_call(
        kernel,
        shaped(((N_Z - 1) * slab + height, width), bf16),
        *pieces,
        scalars=(places,),
        mebibytes=6,
        name="stack_z",
    )


def weave(columns, cuts, slab, places):
    n_x = len(columns[0])
    width = columns[0][0].shape[1]
    flat = [half for column in columns for half in column]
    edges = [0, *cuts, width]
    sizes = [stop - start for start, stop in zip(edges[:-1], edges[1:])]

    def kernel(at_ref, *refs):
        outs = refs[len(flat) :]
        for y in range(len(columns)):
            for dx in range(n_x):
                half = refs[y * n_x + dx]
                x = lax.rem(at_ref[1] + dx, n_x)
                for z in range(N_Z):
                    at = block_rows(z * n_x + x, slab)
                    for out, start, size in zip(outs, edges, sizes):
                        out[at, y * size : (y + 1) * size] = half[
                            z * slab : (z + 1) * slab, start : start + size
                        ]

    out = plain_call(
        kernel,
        tuple(shaped((N_Z * n_x * slab, size * len(columns)), bf16) for size in sizes),
        *flat,
        scalars=(places,),
        mebibytes=12,
        name="weave",
    )
    return out if cuts else out[0]


def proj_kernel(count, each, *refs):
    blocks, parts = refs[:count], refs[count : count + count // each]
    tok_ref, par_ref, res_out, low_out = refs[count + count // each :]
    total = tok_ref[...]
    for n, block in enumerate(blocks):
        size = block.shape[1]
        part = parts[n // each][:, n % each * size : (n % each + 1) * size]
        total = total + dot(block[...], part, 1, 1)
    res_out[...] = total
    normed, _, _ = norm_forward(total, par_ref[2:3, :], par_ref[3:4, :])
    low_out[...] = normed.astype(bf16)


ERF_TOP = (
    -2.72614225801306e-10,
    2.77068142495902e-08,
    -2.10102402082508e-06,
    -5.69250639462346e-05,
    -7.34990630326855e-04,
    -2.95459980854025e-03,
    -1.60960333262415e-02,
)
ERF_LOW = (
    -1.45660718464996e-05,
    -2.13374055278905e-04,
    -1.68282697438203e-03,
    -7.37332916720468e-03,
    -1.42647390514189e-02,
)


def erf(value):
    value = jnp.clip(value, -4.0, 4.0)
    square = value * value
    top = jnp.full_like(square, ERF_TOP[0])
    for number in ERF_TOP[1:]:
        top = top * square + number
    low = jnp.full_like(square, ERF_LOW[0])
    for number in ERF_LOW[1:]:
        low = low * square + number
    inverse = pl.reciprocal(low, approx=True)
    inverse = inverse * (2.0 - low * inverse)
    return value * top * inverse


def up_kernel(count, low_ref, *refs):
    outs = refs[-2 * count :]
    for n, part in enumerate(refs[:count]):
        hidden = dot(low_ref[...], part[...], 1, 0)
        share = 0.5 * (1.0 + erf(hidden * 0.7071067811865476))
        outs[2 * n][...] = (hidden * share).astype(bf16)
        slope = share + hidden * jnp.exp(-0.5 * hidden * hidden) * 0.3989422804014327
        outs[2 * n + 1][...] = slope.astype(bf16)


def up_call(low, parts, rows_all, spot, into):
    rows, model = low.shape
    width = parts[0].shape[1]
    cols = pl.BlockSpec((rows, TILE), lambda i, *_: (spot, i))
    return plain_call(
        functools.partial(up_kernel, len(parts)),
        (shaped((rows_all, width), bf16),) * (2 * len(parts)),
        low,
        *parts,
        grid=(width // TILE,),
        in_specs=[fixed(low.shape)] + [pl.BlockSpec((model, TILE), lambda i, *_: (0, i))] * len(parts),
        out_specs=(cols,) * (2 * len(parts)),
        into=into,
        mebibytes=14,
        name="up",
    )


def hidden_kernel(count, low_ref, *refs):
    outs = refs[-count:]
    for n in range(count):
        slope, part = refs[n], refs[count + n]
        outs[n][...] = (dot(low_ref[...], part[...], 1, 0) * slope[...].astype(f32)).astype(bf16)


def hidden_call(low, slopes, parts, spot, into):
    rows, model = low.shape
    width = parts[0].shape[1]
    cols = pl.BlockSpec((rows, TILE), lambda i, *_: (spot, i))
    return plain_call(
        functools.partial(hidden_kernel, len(parts)),
        tuple(shaped(slope.shape, bf16) for slope in slopes),
        low,
        *slopes,
        *parts,
        grid=(width // TILE,),
        in_specs=[fixed(low.shape)]
        + [cols] * len(parts)
        + [pl.BlockSpec((model, TILE), lambda i, *_: (0, i))] * len(parts),
        out_specs=(cols,) * len(parts),
        into=into,
        mebibytes=14,
        name="hidden",
    )


def wide_kernel(count, *refs):
    total = dot(refs[0][...], refs[count][...], 1, 1)
    for n in range(1, count):
        total = total + dot(refs[n][...], refs[count + n][...], 1, 1)
    refs[-1][...] = total.astype(refs[-1].dtype)


def wide_call(values, parts, rows, spot, kind):
    model, width = parts[0].shape
    return plain_call(
        functools.partial(wide_kernel, len(values)),
        shaped((rows, model), kind),
        *values,
        *parts,
        grid=(model // TILE,),
        in_specs=[pl.BlockSpec((rows, width), lambda i, *_: (spot, 0))] * len(values)
        + [pl.BlockSpec((TILE, width), lambda i, *_: (i, 0))] * len(parts),
        out_specs=pl.BlockSpec((rows, TILE), lambda i, *_: (0, i)),
        mebibytes=14,
        name="wide",
    )


def loss_kernel(chunks, each, *refs):
    res_ref, tea_ref, own_ref = refs[:3]
    received = refs[3 : 3 + chunks * each]
    live_ref, count_ref, grad_out, low_out, loss_out, far_ref = refs[3 + chunks * each :]
    add_received(received, each, far_ref)
    error = res_ref[...] - tea_ref[...] + own_ref[...] + far_ref[...]
    weighted = live_ref[...] * error
    grad = 2.0 * weighted / count_ref[...]
    grad_out[...] = grad
    low_out[...] = grad.astype(bf16)
    sums = jnp.sum(weighted * error, axis=0, keepdims=True)
    sums = jnp.concatenate([sums, jnp.zeros((7, sums.shape[1]), f32)], axis=0)
    loss_out[...] = jnp.where(pl.program_id(0) == 0, sums, loss_out[...] + sums)


def add_received(received, each, far_ref):
    for n in range(len(received) // each):

        @pl.when(pl.program_id(0) == n)
        def _():
            total = received[n * each][...].astype(f32)
            for ref in received[n * each + 1 : (n + 1) * each]:
                total = total + ref[...].astype(f32)
            far_ref[...] = total


def spread_kernel(count, low_ref, *refs):
    outs = refs[count:]
    tiles = len(outs) // count
    for n, part in enumerate(refs[:count]):
        piece = dot(low_ref[...], part[...], 1, 0).astype(bf16)
        lanes = piece.shape[1] // tiles
        for tile in range(tiles):
            outs[tile * count + n][...] = piece[:, tile * lanes : (tile + 1) * lanes]


def spread_call(low, parts):
    width = parts[0].shape[1]
    lanes = min(128, width)
    count = len(parts)
    out = plain_call(
        functools.partial(spread_kernel, count),
        tuple(shaped((low.shape[0], lanes), bf16) for _ in range(count * (width // lanes))),
        low,
        *parts,
        mebibytes=12,
        name="spread",
    )
    return [out[n : n + count] for n in range(0, len(out), count)]


def norm_sums(grad, scaled, out_ref, first):
    sums = jnp.concatenate(
        [
            jnp.sum(grad * scaled, axis=0, keepdims=True),
            jnp.sum(grad, axis=0, keepdims=True),
            jnp.zeros((6, grad.shape[1]), f32),
        ],
        axis=0,
    )
    out_ref[...] = jnp.where(first, sums, out_ref[...] + sums)


def middle_kernel(chunks, each, *refs):
    grad_ref, received = refs[0], refs[1 : 1 + chunks * each]
    res_ref, gout_ref, par_ref, full_out, low_out, sum_out, far_ref = refs[1 + chunks * each :]
    add_received(received, each, far_ref)
    _, scaled, inverse = norm_forward(res_ref[...], par_ref[2:3, :], par_ref[3:4, :])
    grad = grad_ref[...] + far_ref[...]
    full = gout_ref[...] + norm_backward(grad, scaled, inverse, par_ref[2:3, :])
    full_out[...] = full
    low_out[...] = full.astype(bf16)
    norm_sums(grad, scaled, sum_out, pl.program_id(0) == 0)


def leave_kernel(count, *refs):
    own_ref, received = refs[0], refs[1 : 1 + count]
    tok_ref, res_ref, par_ref, two_ref, loss_ref, out_ref, sum_out, sum_ref = refs[1 + count :]
    _, scaled, inverse = norm_forward(tok_ref[...], par_ref[0:1, :], par_ref[1:2, :])
    grad = own_ref[...]
    for ref in received:
        grad = grad + ref[...].astype(f32)
    out_ref[...] = res_ref[...] + norm_backward(grad, scaled, inverse, par_ref[0:1, :])
    norm_sums(grad, scaled, sum_ref, pl.program_id(0) == 0)
    sum_out[...] = jnp.concatenate(
        [sum_ref[0:2, :], two_ref[0:2, :], loss_ref[0:1, :], jnp.zeros((3, grad.shape[1]), f32)],
        axis=0,
    )


def split_x(parts, n_x, places):
    model = parts[0].shape[0]
    slab = model // (N_Z * n_x)
    total = sum(part.shape[1] for part in parts)

    def kernel(at_ref, *refs):
        outs = refs[len(parts) :]
        for dx in range(n_x):
            x = lax.rem(at_ref[1] + dx, n_x)
            for z in range(N_Z):
                at = block_rows(z * n_x + x, slab)
                lane = 0
                for ref in refs[: len(parts)]:
                    size = ref.shape[1]
                    outs[dx][z * slab : (z + 1) * slab, lane : lane + size] = ref[at, :]
                    lane += size

    return plain_call(
        kernel,
        tuple(shaped((model // n_x, total), bf16) for _ in range(n_x)),
        *parts,
        scalars=(places,),
        mebibytes=10,
        name="split_x",
    )


def split_z(parts, places):
    rows, width = parts[0].shape
    slab = rows // N_Z

    def kernel(at_ref, *refs):
        for k, out in enumerate(refs[len(parts) :]):
            at = block_rows(lax.rem(at_ref[0] + k, N_Z), slab)
            total = refs[0][at, :].astype(f32)
            for ref in refs[1 : len(parts)]:
                total = total + ref[at, :].astype(f32)
            out[...] = total.astype(out.dtype)

    shapes = (shaped((slab, width), f32),) + (shaped((slab, width), bf16),) * (N_Z - 1)
    return plain_call(kernel, shapes, *parts, scalars=(places,), mebibytes=8, name="split_z")


def adam_kernel(layout, counts, *refs):
    grads = []
    for count in counts:
        grad = refs[0][...].astype(f32)
        for ref in refs[1:count]:
            grad = grad + ref[...].astype(f32)
        grads.append(grad)
        refs = refs[count:]
    count = len(layout)
    states, outs = refs[: 3 * count], refs[3 * count :]
    for n, (source, start, size, turned) in enumerate(layout):
        weight, first, second = states[3 * n : 3 * n + 3]
        if len(weight.shape) == 3:
            matrices = weight.shape[0]
            lanes = size // matrices
            for k in range(matrices):
                own = [
                    grads[at][:, lane + k * lanes : lane + (k + 1) * lanes] for at, lane in start
                ]
                own = own[0] if len(own) == 1 else jnp.concatenate(own, axis=1)
                new = adam_step(weight[k], own, first[k], second[k], weight_decay, learn_rate)
                for out, value in zip(outs[3 * n : 3 * n + 3], new):
                    out[k] = value
        else:
            part = grads[source][:, start : start + size]
            if turned:
                part = part.T
            new = adam_step(weight[...], part, first[...], second[...], weight_decay, learn_rate)
            for out, value in zip(outs[3 * n : 3 * n + 3], new):
                out[...] = value


def adam_call(groups, layout, *states):
    shapes = tuple(shaped(s.shape, f32) for s in states)
    out = plain_call(
        functools.partial(adam_kernel, layout, [len(group) for group in groups]),
        shapes,
        *[piece for group in groups for piece in group],
        *states,
        mebibytes=16,
        name="adam",
    )
    return [out[3 * n : 3 * n + 3] for n in range(len(layout))]


def tie(*values):
    return lax.optimization_barrier(values)


def local(
    n_x,
    n_y,
    tokens,
    teacher,
    segments,
    live_mask,
    weight_qkv,
    weight_proj,
    weight_up,
    weight_down,
    norm_params,
    first_qkv,
    first_proj,
    first_up,
    first_down,
    first_norms,
    second_qkv,
    second_proj,
    second_up,
    second_down,
    second_norms,
):
    z_at, x_at = lax.axis_index("z"), lax.axis_index("x")
    y_at, core_at = lax.axis_index("y"), lax.axis_index("core")
    rows, model = tokens.shape
    group_rows = segments.shape[0]
    slab = weight_qkv.shape[1]
    width = weight_qkv.shape[2]
    unit = weight_up.shape[1]
    part_rows = min(128, rows)
    wide_rows = min(256, rows)
    depth = N_Z * slab
    sizes = {"z": N_Z, "x": n_x, "y": n_y, "core": N_CORE}
    places = jnp.stack([z_at, x_at]).astype(jnp.int32)
    offsets = [(dc, dy) for dc in range(N_CORE) for dy in range(n_y)]
    other = N_CORE - 1

    def send(value, axis, step):
        size = sizes[axis]
        return lax.ppermute(value, axis, [(i, (i + step) % size) for i in range(size)])

    def send_col(value, dy, dc):
        perm = [
            (y * N_CORE + c, (y + dy) % n_y * N_CORE + (c + dc) % N_CORE)
            for y in range(n_y)
            for c in range(N_CORE)
        ]
        return lax.ppermute(value, ("y", "core"), perm)

    def fetch(value, axis):
        return [value] + [send(value, axis, -k) for k in range(1, sizes[axis])]

    def place(dy, dc):
        return ((y_at + dy) % n_y * N_CORE + (core_at + dc) % N_CORE) * rows

    shard_qkv, shard_up, shard_down = plain_call(
        pack_kernel,
        (
            shaped((slab, 4 * width), bf16),
            shaped((slab + DIGITS, unit), bf16),
            shaped((slab, unit), bf16),
        ),
        live_mask.reshape(-1, 128),
        weight_qkv,
        weight_proj,
        weight_up,
        weight_down,
        mebibytes=8,
        name="pack",
    )
    near_qkv = fetch(shard_qkv, "z")
    low_one = plain_call(
        first_kernel,
        shaped(tokens.shape, bf16),
        tokens,
        norm_params,
        grid=(rows // part_rows,),
        in_specs=row_blocks(part_rows, model) + [fixed(norm_params.shape)],
        out_specs=row_blocks(part_rows, model)[0],
        mebibytes=8,
        name="first",
    )
    blocks_one = fetch(low_one, "y") + [send(low_one, "core", -1)]
    near_qkv, shard_down, shard_up, blocks_one[n_y] = tie(
        near_qkv, shard_down, shard_up, blocks_one[n_y]
    )

    beside_qkv = fetch(stack_z(near_qkv, slab, places), "x")
    blocks_one, shard_up = tie(blocks_one, shard_up)
    near_up = fetch(shard_up, "z")
    blocks_one = blocks_one + [send(block, "core", -1) for block in blocks_one[1:n_y]]
    spots_here = jnp.stack([place(dy, dc) for dc, dy in offsets]).astype(jnp.int32)
    spots = jnp.stack([place(-dy, -dc) for dc, dy in offsets]).astype(jnp.int32)
    group_one = place_blocks(blocks_one, spots_here)
    geometry = attend_geometry(segments, live_mask)
    own_live = lax.dynamic_slice_in_dim(
        live_mask, (y_at * N_CORE + core_at) * rows, rows, 0
    ).astype(f32)[:, None]
    beside_qkv, near_up, group_one, geometry, own_live, shard_down, spots = tie(
        beside_qkv, near_up, group_one, geometry, own_live, shard_down, spots
    )

    block_up = stack_z(near_up, slab, places)
    full_qkv, part_proj = weave([beside_qkv], [3 * width], slab, places)
    block_up, part_proj = tie(block_up, part_proj)
    beside_up = fetch(block_up, "x")
    near_down = fetch(shard_down, "z")
    full_proj = fetch(part_proj, "y")
    projected = dot(group_one, full_qkv, 1, 0).astype(bf16)
    mixed = attend_forward(projected, geometry, spots, rows)
    mixed, beside_up, near_down, full_proj = tie(mixed, beside_up, near_down, full_proj)

    blocks_mixed = [
        piece if key == (0, 0) else send_col(piece, -key[1], -key[0])
        for key, piece in zip(offsets, mixed)
    ]
    full_proj = full_proj + [send(part, "core", -1) for part in full_proj]
    block_down = stack_z(near_down, slab, places)
    full_up = [weave([beside_up], [], slab, places)]
    live_count = sum(
        256.0 * part[depth, 0].astype(f32) + 16.0 * part[depth + 1, 0].astype(f32)
        + part[depth + 2, 0].astype(f32)
        for part in beside_up
    ).reshape(1, 1)
    blocks_mixed, full_proj, full_up, live_count = tie(
        blocks_mixed, full_proj, full_up, live_count
    )
    beside_down = fetch(block_down, "x")
    full_up.append(send(full_up[0], "core", -1))
    count = len(offsets)
    residual, low_two = plain_call(
        functools.partial(proj_kernel, count, 1),
        (shaped(tokens.shape, f32), shaped(tokens.shape, bf16)),
        *blocks_mixed,
        *full_proj,
        tokens,
        norm_params,
        grid=(rows // wide_rows,),
        in_specs=row_blocks(wide_rows, *([width] * count))
        + [fixed(part.shape) for part in full_proj]
        + row_blocks(wide_rows, model)
        + [fixed(norm_params.shape)],
        out_specs=tuple(row_blocks(wide_rows, model, model)),
        mebibytes=18,
        name="proj",
    )
    low_two, full_up = tie(low_two, full_up)

    chunk = min(256, rows)
    chunks = range(rows // chunk)
    neighbours = range(1, n_y)
    rows_all = n_y * rows

    def cross(value, n, back):
        piece = value[n * chunk : (n + 1) * chunk]
        return {dy: send(piece, "y", dy if back else -dy) for dy in neighbours}

    def spot_of(dy, n):
        return (dy * rows) // chunk + n

    low_far = {0: cross(low_two, 0, False)}
    hidden = up_call(low_two, full_up, rows_all, 0, ())
    low_far[0], hidden, low_two, beside_down = tie(low_far[0], hidden, low_two, beside_down)
    full_down = [weave([beside_down], [], slab, places)]
    full_down.append(send(full_down[0], "core", -1))
    far_out = {}
    for n in chunks:
        if n + 1 in chunks:
            low_far[n + 1] = cross(low_two, n + 1, False)
        for dy in neighbours:
            hidden = up_call(low_far[n][dy], full_up, rows_all, spot_of(dy, n), hidden)
        outs = {
            dy: wide_call(hidden[::2], full_down, chunk, spot_of(dy, n), bf16) for dy in neighbours
        }
        if n + 1 in chunks:
            outs, hidden, low_far[n + 1] = tie(outs, hidden, low_far[n + 1])
        else:
            outs, hidden = tie(outs, hidden)
        if n:
            far_out[n - 1] = tie(far_out[n - 1], outs)[0]
        far_out[n] = {dy: send(outs[dy], "y", -dy) for dy in neighbours}
    own_out = wide_call(hidden[::2], full_down, rows, 0, f32)
    own_out, far_out = tie(own_out, far_out)
    far_out = [far_out[n][dy] for n in chunks for dy in neighbours]
    each = len(neighbours)
    grad_output, grad_branch, loss_rows = plain_call(
        functools.partial(loss_kernel, len(chunks), each),
        (shaped(tokens.shape, f32), shaped(tokens.shape, bf16), shaped((8, model), f32)),
        residual,
        teacher,
        own_out,
        *far_out,
        own_live,
        live_count,
        grid=(len(chunks),),
        in_specs=row_blocks(chunk, model, model, model)
        + [fixed((chunk, model))] * len(far_out)
        + row_blocks(chunk, 1)
        + [fixed((1, 1))],
        out_specs=tuple(row_blocks(chunk, model, model) + [fixed((8, model))]),
        scratch=[pltpu.VMEM((chunk, model), f32)],
        mebibytes=20,
        name="loss",
    )
    active, slope = hidden[::2], hidden[1::2]

    grad_far = {0: cross(grad_branch, 0, False)}
    grad_hidden = hidden_call(grad_branch, slope, full_down, 0, ())
    own_two = wide_call(grad_hidden, full_up, rows, 0, f32)
    grad_far[0], grad_hidden, own_two, grad_branch = tie(
        grad_far[0], grad_hidden, own_two, grad_branch
    )
    def gather_rows(own, far):
        return jnp.concatenate([own] + [far[n][dy] for dy in neighbours for n in chunks], axis=0)

    far_two = {}
    for n in chunks:
        if n + 1 in chunks:
            grad_far[n + 1] = cross(grad_branch, n + 1, False)
        for dy in neighbours:
            grad_hidden = hidden_call(
                grad_far[n][dy], slope, full_down, spot_of(dy, n), grad_hidden
            )
        outs = {
            dy: wide_call(grad_hidden, full_up, chunk, spot_of(dy, n), bf16) for dy in neighbours
        }
        if n + 1 in chunks:
            outs, grad_hidden, grad_far[n + 1] = tie(outs, grad_hidden, grad_far[n + 1])
        else:
            grad_all = gather_rows(grad_branch, grad_far)
            far_down = dot(grad_all, active[other], 0, 0).astype(bf16)
            outs, grad_hidden, grad_all, far_down, far_two = tie(
                outs, grad_hidden, grad_all, far_down, far_two
            )
        far_two[n] = {dy: send(outs[dy], "y", -dy) for dy in neighbours}

    low_all = gather_rows(low_two, low_far)
    far_up = dot(low_all, grad_hidden[other], 0, 0).astype(bf16)
    sent_down, sent_up = send(far_down, "core", 1), send(far_up, "core", 1)
    hold_down = (dot(grad_all, active[0], 0, 0) + sent_down.astype(f32)).astype(bf16)
    halves_down = split_x([hold_down], n_x, places)
    hold_up = (dot(low_all, grad_hidden[0], 0, 0) + sent_up.astype(f32)).astype(bf16)
    halves_up = split_x([hold_up], n_x, places)
    far_two, halves_down, halves_up = tie(far_two, halves_down, halves_up)
    far_two = [far_two[n][dy] for n in chunks for dy in neighbours]
    grad_residual, grad_low, sums_two = plain_call(
        functools.partial(middle_kernel, len(chunks), each),
        (shaped(tokens.shape, f32), shaped(tokens.shape, bf16), shaped((8, model), f32)),
        own_two,
        *far_two,
        residual,
        grad_output,
        norm_params,
        grid=(len(chunks),),
        in_specs=row_blocks(chunk, model)
        + [fixed((chunk, model))] * len(far_two)
        + row_blocks(chunk, model, model)
        + [fixed(norm_params.shape)],
        out_specs=tuple(row_blocks(chunk, model, model) + [fixed((8, model))]),
        scratch=[pltpu.VMEM((chunk, model), f32)],
        mebibytes=20,
        name="middle",
    )
    pieces_attn = spread_call(grad_low, full_proj)
    pieces_attn, halves_down, halves_up, grad_low = tie(
        pieces_attn, halves_down, halves_up, grad_low
    )

    def send_back(pieces):
        return [
            piece if key == (0, 0) else send_col(piece, key[1], key[0])
            for key, piece in zip(offsets, pieces)
        ]

    def hop_x(halves):
        return [halves[0]] + [send(halves[dx], "x", dx) for dx in range(1, n_x)]

    def spread_z(pieces):
        return [pieces[0]] + [send(pieces[k], "z", k) for k in range(1, N_Z)]

    lanes = 3 * min(128, width)
    tiles = 3 * width // lanes
    sent_attn = send_back(pieces_attn[0])
    parts_down = hop_x(halves_down)
    grad_proj = [dot(grad_low, block, 0, 0).astype(bf16) for block in blocks_mixed]
    far_proj = jnp.concatenate(grad_proj[n_y:], axis=1)
    sent_attn, far_proj, grad_proj = tie(sent_attn, far_proj, grad_proj)

    sent_later = [send_back(pieces) for pieces in pieces_attn[1:]]
    sent_proj = send(far_proj, "core", 1)
    grad_projected = attend_backward(projected, sent_attn, spots, geometry, 0, ())
    grad_projected, sent_later, sent_proj, parts_down, halves_up = tie(
        grad_projected, sent_later, sent_proj, parts_down, halves_up
    )

    hold_proj = [
        (
            grad_proj[dy].astype(f32) + sent_proj[:, dy * width : (dy + 1) * width].astype(f32)
        ).astype(bf16)
        for dy in range(n_y)
    ]
    pieces_down = split_z(parts_down, places)
    grad_projected, pieces_down, hold_proj, halves_up = tie(
        grad_projected, pieces_down, hold_proj, halves_up
    )
    parts_up = hop_x(halves_up)
    last_down = spread_z(pieces_down)
    part_proj = [hold_proj[0]] + [send(hold_proj[k], "y", k) for k in range(1, n_y)]
    for tile in range(1, tiles):
        grad_projected = attend_backward(
            projected, sent_later[tile - 1], spots, geometry, tile, (grad_projected,)
        )
    grad_projected, parts_up, last_down, part_proj = tie(
        grad_projected, parts_up, last_down, part_proj
    )

    parts = {
        key: dot(
            lax.dynamic_slice_in_dim(grad_projected, place(key[1], key[0]), rows, 0),
            full_qkv,
            1,
            1,
        )
        for key in reversed(offsets)
    }
    far_one = jnp.concatenate([parts[other, dy].astype(bf16) for dy in range(n_y)], axis=0)
    far_one, grad_projected = tie(far_one, grad_projected)
    sent_one = send(far_one, "core", 1)
    grad_qkv = dot(group_one, grad_projected, 0, 0).astype(bf16)
    total = part_proj[0].astype(f32)
    for piece in part_proj[1:]:
        total = total + piece.astype(f32)
    halves_qkv = split_x([grad_qkv, total.astype(bf16)], n_x, places)
    pieces_up = split_z(parts_up, places)
    halves_qkv, sent_one, parts, pieces_up = tie(halves_qkv, sent_one, parts, pieces_up)

    parts = [
        parts[0, dy] + sent_one[dy * rows : (dy + 1) * rows].astype(f32) for dy in range(n_y)
    ]
    sent_parts = [parts[k].astype(bf16) for k in range(1, n_y)]
    halves_qkv, sent_parts, pieces_up = tie(halves_qkv, sent_parts, pieces_up)
    received = [send(part, "y", k) for k, part in enumerate(sent_parts, 1)]
    parts_qkv = hop_x(halves_qkv)
    last_up = spread_z(pieces_up)
    parts_qkv, received, last_up = tie(parts_qkv, received, last_up)

    pieces_qkv = split_z(parts_qkv, places)
    pieces_qkv, received = tie(pieces_qkv, received)
    last_qkv = spread_z(pieces_qkv)
    token_grad, sums = plain_call(
        functools.partial(leave_kernel, len(received)),
        (shaped(tokens.shape, f32), shaped((8, model), f32)),
        parts[0],
        *received,
        tokens,
        grad_residual,
        norm_params,
        sums_two,
        loss_rows,
        grid=(rows // part_rows,),
        in_specs=row_blocks(part_rows, *([model] * (3 + len(received))))
        + [fixed(norm_params.shape), fixed((8, model)), fixed((8, model))],
        out_specs=tuple(row_blocks(part_rows, model) + [fixed((8, model))]),
        scratch=[pltpu.VMEM((8, model), f32)],
        mebibytes=14,
        name="leave",
    )
    for axis in ("core", "y", "x", "z"):
        step = 1
        while step < sizes[axis]:
            pairs = [(i, i ^ step) for i in range(sizes[axis])]
            sums = sums + lax.ppermute(sums, axis, pairs)
            step *= 2
    sums, last_qkv = tie(sums, last_qkv)
    loss_sum = jnp.sum(sums[4])
    live_count = live_count[0, 0]

    (new_down,) = adam_call(
        [last_down], [(0, 0, unit, True)], weight_down, first_down, second_down
    )
    (new_up,) = adam_call([last_up], [(0, 0, unit, False)], weight_up, first_up, second_up)
    new_qkv, new_proj = adam_call(
        [last_qkv],
        [(0, [(0, n * lanes) for n in range(tiles)], lanes, False), (0, 3 * width, width, True)],
        weight_qkv,
        first_qkv,
        second_qkv,
        weight_proj,
        first_proj,
        second_proj,
    )
    new_norms = adam_step(norm_params, sums[:4], first_norms, second_norms, 0.0, norm_rate)
    return (
        loss_sum / live_count,
        token_grad,
        new_qkv[0],
        new_proj[0],
        new_up[0],
        new_down[0],
        new_norms[0],
        new_qkv[1],
        new_proj[1],
        new_up[1],
        new_down[1],
        new_norms[1],
        new_qkv[2],
        new_proj[2],
        new_up[2],
        new_down[2],
        new_norms[2],
    )


def solution(mesh):
    n_x = mesh.shape["row"] // N_Z
    n_y = mesh.shape["col"] // N_CORE
    mesh = jax.sharding.Mesh(
        mesh.devices.reshape(N_Z, n_x, n_y, N_CORE), ("z", "x", "y", "core")
    )
    row, col = ("z", "x"), ("y", "core")
    matrices = (P(None, row, col), P(col, row), P(row, col), P(col, row), P())
    tokens = P(row + col, None)
    return jax.shard_map(
        functools.partial(local, n_x, n_y),
        mesh=mesh,
        in_specs=(tokens, tokens, P(row), P(row)) + matrices * 3,
        out_specs=(P(), tokens) + matrices * 3,
        check_vma=False,
    )
```

```python
import functools

import jax
import jax.numpy as jnp
from jax import lax
from jax.experimental import pallas as pl
from jax.experimental.pallas import tpu as pltpu
from jax.sharding import PartitionSpec as P

HEAD_DIM = 64
PATCHES = 577
STEP = 10
WINDOW = 640
QROWS = 320
TILE = 256
DIGITS = 16
SMALL = pl.CostEstimate(flops=1024, bytes_accessed=1024, transcendentals=0)
N_Z = 4
N_CORE = 2

layer_eps = 1e-06
adam_eps = 1e-08
learn_rate = 0.03
norm_rate = 0.25
moment_decay = 0.5
weight_decay = 0.05

bf16 = jnp.bfloat16
f32 = jnp.float32


def norm_forward(values, gain_row, bias_row):
    average = jnp.mean(values, axis=-1, keepdims=True)
    centred = values - average
    variance = jnp.mean(centred * centred, axis=-1, keepdims=True)
    inverse = lax.rsqrt(variance + layer_eps)
    scaled = centred * inverse
    return (scaled * gain_row + bias_row, scaled, inverse)


def norm_backward(upstream, scaled, inverse, gain_row):
    weighted = upstream * gain_row
    return inverse * (
        weighted
        - jnp.mean(weighted, axis=-1, keepdims=True)
        - scaled * jnp.mean(weighted * scaled, axis=-1, keepdims=True)
    )


def gelu_slope(hidden):
    return (
        0.5 * (1.0 + lax.erf(hidden * 0.7071067811865476))
        + hidden * jnp.exp(-0.5 * hidden * hidden) * 0.3989422804014327
    )


def adam_step(weight, gradient, momentum, variance, decay_rate, rate):
    momentum = moment_decay * momentum + (1.0 - moment_decay) * gradient
    variance = moment_decay * variance + (1.0 - moment_decay) * gradient * gradient
    correction = 1.0 - moment_decay**STEP
    direction = momentum / correction / (jnp.sqrt(variance / correction) + adam_eps)
    return (weight - rate * (direction + decay_rate * weight), momentum, variance)


def dot(left, right, left_dim, right_dim):
    return lax.dot_general(
        left, right, (((left_dim,), (right_dim,)), ((), ())), preferred_element_type=f32
    )


def head_lanes(width, head):
    lanes = lax.broadcasted_iota(jnp.int32, (1, width), 1)
    return (lanes >= head * HEAD_DIM) & (lanes < (head + 1) * HEAD_DIM)


def attend_scores(q_part, k_all, mask):
    scores = dot(q_part, k_all, 1, 1) + mask
    weights = jnp.exp(scores - jnp.max(scores, axis=-1, keepdims=True))
    return weights, jnp.sum(weights, axis=-1, keepdims=True)


def image_window(begin, code_ref, mask_ref, group_rows):
    image = pl.program_id(0)
    start = jnp.minimum(begin[image] // 16 * 16, group_rows - WINDOW)
    first = begin[image] - start
    start = pl.multiple_of(start, 16)
    code = code_ref[pl.ds(start, WINDOW), :]
    bias = jnp.where(code == image, 0.0, -1e30).astype(f32).T[0:1, :]
    for row in range(0, WINDOW, 128):
        rows = row + lax.broadcasted_iota(jnp.int32, (128, WINDOW), 0)
        cols = lax.broadcasted_iota(jnp.int32, (128, WINDOW), 1)
        mask_ref[row : row + 128, :] = jnp.where(rows == cols, 0.0, bias)
    return image, start, first


def rows_inside(rows, row_start, first):
    ids = row_start + lax.broadcasted_iota(jnp.int32, (rows, 1), 0)
    return (ids >= first) & (ids < first + PATCHES)


def attend_forward_kernel(blocks, begin, spots, code_ref, *refs):
    out_ref, mask_ref = refs[-2:]
    image, start, first = image_window(begin, code_ref, mask_ref, refs[0].shape[0])
    lanes = refs[0].shape[1]

    for tile in range((len(refs) - 2 - blocks) // 3):
        q_ref, k_ref, v_ref = refs[3 * tile : 3 * tile + 3]
        cols = slice(tile * lanes, (tile + 1) * lanes)

        @pl.when(image == 0)
        def _():
            out_ref[:, cols] = v_ref[...]

        k_all = k_ref[pl.ds(start, WINDOW), :]
        v_all = v_ref[pl.ds(start, WINDOW), :]
        for row in range(0, WINDOW, QROWS):
            at = pl.ds(pl.multiple_of(start + row, 16), QROWS)
            q_part = q_ref[at, :] * jnp.asarray(HEAD_DIM ** (-0.5), bf16)
            inside = rows_inside(QROWS, row, first)
            mixed = None
            for head in range(lanes // HEAD_DIM):
                mine = head_lanes(lanes, head)
                q_head = jnp.where(mine, q_part, jnp.zeros_like(q_part))
                weights, totals = attend_scores(q_head, k_all, mask_ref[row : row + QROWS, :])
                part = dot(weights.astype(bf16), v_all, 1, 0) * (1.0 / totals)
                mixed = part if mixed is None else jnp.where(mine, part, mixed)
            out_ref[at, cols] = jnp.where(inside, mixed.astype(bf16), out_ref[at, cols])

    @pl.when(image == pl.num_programs(0) - 1)
    def _():
        for n, block in enumerate(refs[-2 - blocks : -2]):
            rows = block.shape[0]
            block[...] = out_ref[pl.ds(pl.multiple_of(spots[n], rows), rows), :]


def attend_backward_kernel(blocks, begin, spots, code_ref, *refs):
    out_ref, p_ref, s_ref, go_ref, mask_ref = refs[-5:]
    go_blocks, refs = refs[-5 - blocks : -5], refs[: -5 - blocks]
    image, start, first = image_window(begin, code_ref, mask_ref, refs[0].shape[0])
    lanes = refs[0].shape[1]
    rows = go_blocks[0].shape[0]
    whole = pl.ds(start, WINDOW)
    inside_all = rows_inside(WINDOW, 0, first)

    @pl.when(image == 0)
    def _():
        for n, block_ref in enumerate(go_blocks):
            go_ref[pl.ds(pl.multiple_of(spots[n], rows), rows), :] = block_ref[...]

    for tile in range(len(refs) // 3):
        q_ref, k_ref, v_ref = refs[3 * tile : 3 * tile + 3]
        cols = slice(tile * lanes, (tile + 1) * lanes)
        base = 3 * tile * lanes
        q_cols, k_cols, v_cols = [
            slice(base + n * lanes, base + (n + 1) * lanes) for n in range(3)
        ]

        @pl.when(image == 0)
        def _():
            out_ref[:, base : base + 2 * lanes] = jnp.zeros((out_ref.shape[0], 2 * lanes), bf16)
            out_ref[:, v_cols] = go_ref[:, cols]

        k_all = k_ref[whole, :]
        v_all = v_ref[whole, :]
        q_all = q_ref[whole, :] * jnp.asarray(HEAD_DIM ** (-0.5), bf16)
        go_all = go_ref[whole, cols]
        key_grad = None
        value_grad = None
        for head in range(lanes // HEAD_DIM):
            mine = head_lanes(lanes, head)
            q_mine = jnp.where(mine, q_all, jnp.zeros_like(q_all))
            go_mine = jnp.where(mine, go_all, jnp.zeros_like(go_all))
            for row in range(0, WINDOW, QROWS):
                part = slice(row, row + QROWS)
                at = pl.ds(pl.multiple_of(start + row, 16), QROWS)
                inside = rows_inside(QROWS, row, first)
                weights, totals = attend_scores(q_mine[part], k_all, mask_ref[part, :])
                weights = weights * jnp.where(inside, 1.0 / totals, 0.0)
                weight_grad = dot(go_mine[part], v_all, 1, 1)
                product = weights * weight_grad
                score_grad = (
                    product - weights * jnp.sum(product, axis=-1, keepdims=True)
                ).astype(bf16)
                p_ref[part, :] = weights.astype(bf16)
                s_ref[part, :] = score_grad
                query_grad = (dot(score_grad, k_all, 1, 0) * HEAD_DIM ** (-0.5)).astype(bf16)
                out_ref[at, q_cols] = jnp.where(inside & mine, query_grad, out_ref[at, q_cols])
            key_part = dot(q_mine, s_ref[...], 0, 0)
            value_part = dot(go_mine, p_ref[...], 0, 0)
            key_grad = key_part if key_grad is None else key_grad + key_part
            value_grad = value_part if value_grad is None else value_grad + value_part
        key_rows = key_grad.T.astype(bf16)
        value_rows = value_grad.T.astype(bf16)
        out_ref[whole, k_cols] = jnp.where(inside_all, key_rows, out_ref[whole, k_cols])
        out_ref[whole, v_cols] = jnp.where(inside_all, value_rows, out_ref[whole, v_cols])


def qkv_operands(projected, tile):
    group_rows, total = projected.shape
    lanes = min(128, total // 3)
    if lanes % 128 == 0:
        specs = [
            pl.BlockSpec((group_rows, lanes), functools.partial(lambda n, i, *_: (0, n), 3 * tile + n))
            for n in range(3)
        ]
        return [projected] * 3, specs
    parts = [projected[:, n * lanes : (n + 1) * lanes] for n in range(3)]
    return parts, [fixed((group_rows, lanes))] * 3


def all_operands(projected):
    width = projected.shape[1] // 3
    operands, specs = [], []
    for tile in range(width // min(128, width)):
        more, places = qkv_operands(projected, tile)
        operands += more
        specs += places
    return operands, specs


def attend_forward(projected, geometry, spots, rows):
    begin, code = geometry
    group_rows, total = projected.shape
    width = total // 3
    blocks = group_rows // rows
    operands, specs = all_operands(projected)
    return plain_call(
        functools.partial(attend_forward_kernel, blocks),
        (shaped((rows, width), bf16),) * blocks,
        code,
        *operands,
        grid=begin.shape,
        in_specs=[fixed(code.shape)] + specs,
        scratch=[pltpu.VMEM((group_rows, width), bf16), pltpu.VMEM((WINDOW, WINDOW), f32)],
        scalars=(begin, spots),
        mebibytes=20,
        name="attention_forward",
    )


def attend_backward(projected, go_blocks, spots, geometry):
    begin, code = geometry
    group_rows, total = projected.shape
    operands, specs = all_operands(projected)
    return plain_call(
        functools.partial(attend_backward_kernel, len(go_blocks)),
        shaped((group_rows, total), bf16),
        code,
        *operands,
        *go_blocks,
        grid=begin.shape,
        in_specs=[fixed(code.shape)] + specs + [fixed(block.shape) for block in go_blocks],
        scratch=[pltpu.VMEM((WINDOW, WINDOW), bf16)] * 2
        + [pltpu.VMEM((group_rows, total // 3), bf16), pltpu.VMEM((WINDOW, WINDOW), f32)],
        scalars=(begin, spots),
        mebibytes=28,
        name="attention_backward",
    )


def attend_geometry(segments, live_mask):
    group_rows = segments.shape[0]
    numbers = jnp.arange(group_rows // PATCHES, dtype=jnp.int32)
    positions = jnp.arange(group_rows, dtype=jnp.int32)
    begin = jnp.min(
        jnp.where(segments[None, :] == numbers[:, None], positions[None, :], group_rows - PATCHES),
        axis=1,
    )
    code = jnp.where(live_mask == 1, segments, -1)
    return begin, jnp.broadcast_to(code[:, None], (group_rows, 128))


def plain_call(kernel, out_shape, *operands, grid=(), in_specs=None, out_specs=None, scratch=(), scalars=(), into=(), mebibytes=16, name=None):
    params = pltpu.CompilerParams(vmem_limit_bytes=mebibytes * 1024 * 1024)
    if in_specs is None:
        in_specs = [pl.BlockSpec(a.shape, functools.partial(lambda n, *_: (0,) * n, a.ndim)) for a in operands]
    in_specs = list(in_specs) + [pl.BlockSpec(memory_space=pl.ANY)] * len(into)
    if out_specs is None:
        out_specs = jax.tree.map(
            lambda s: pl.BlockSpec(s.shape, functools.partial(lambda n, *_: (0,) * n, len(s.shape))), out_shape
        )
    return pl.pallas_call(
        kernel,
        grid_spec=pltpu.PrefetchScalarGridSpec(
            num_scalar_prefetch=len(scalars),
            grid=grid,
            in_specs=in_specs,
            out_specs=out_specs,
            scratch_shapes=list(scratch),
        ),
        out_shape=out_shape,
        input_output_aliases={len(scalars) + len(operands) + n: n for n in range(len(into))},
        compiler_params=params,
        cost_estimate=SMALL,
        name=name,
    )(*scalars, *operands, *into)


def shaped(shape, dtype):
    return jax.ShapeDtypeStruct(tuple(shape), dtype)


def row_blocks(rows, *widths):
    return [pl.BlockSpec((rows, w), lambda i, *_: (i, 0)) for w in widths]


def fixed(shape):
    return pl.BlockSpec(tuple(shape), functools.partial(lambda n, *_: (0,) * n, len(shape)))


def pack_kernel(live_ref, qkv_ref, proj_ref, up_ref, down_ref, qkv_out, up_out, down_out):
    count, slab, width = qkv_ref.shape
    lanes = min(128, width)
    for n in range(count):
        for t in range(width // lanes):
            at = (count * t + n) * lanes
            qkv_out[:, at : at + lanes] = qkv_ref[n][:, t * lanes : (t + 1) * lanes].astype(bf16)
    qkv_out[:, count * width :] = proj_ref[...].T.astype(bf16)
    up_out[:slab, :] = up_ref[...].astype(bf16)
    live = jnp.sum(jnp.sum(live_ref[...].astype(f32), axis=0, keepdims=True), axis=1, keepdims=True)
    high = jnp.floor(live * (1.0 / 256.0))
    middle = jnp.floor(live * (1.0 / 16.0)) - 16.0 * high
    low = live - 256.0 * high - 16.0 * middle
    row = lax.broadcasted_iota(jnp.int32, (DIGITS, up_out.shape[1]), 0)
    digits = jnp.where(row == 0, high, jnp.where(row == 1, middle, jnp.where(row == 2, low, 0.0)))
    up_out[slab:, :] = digits.astype(bf16)
    down_out[...] = down_ref[...].T.astype(bf16)


def first_kernel(tok_ref, par_ref, low_out):
    normed, _, _ = norm_forward(tok_ref[...], par_ref[0:1, :], par_ref[1:2, :])
    low_out[...] = normed.astype(bf16)


def place_blocks(blocks, spots):
    rows, width = blocks[0].shape

    def kernel(spot_ref, *refs):
        for n, ref in enumerate(refs[:-1]):
            refs[-1][pl.ds(pl.multiple_of(spot_ref[n], rows), rows), :] = ref[...]

    return plain_call(
        kernel,
        shaped((rows * len(blocks), width), bf16),
        *blocks,
        scalars=(spots,),
        mebibytes=20,
        name="place_blocks",
    )


def block_rows(block, slab):
    return pl.ds(pl.multiple_of(block * slab, slab), slab)


def stack_z(pieces, slab, places):
    height, width = pieces[0].shape

    def kernel(at_ref, *refs):
        out = refs[-1]
        for k, ref in enumerate(refs[:-1]):
            out[block_rows(lax.rem(at_ref[0] + k, N_Z), slab), :] = ref[:slab, :]
        if height > slab:
            digits = refs[0][slab:, :].astype(f32)
            for ref in refs[1:-1]:
                digits = digits + ref[slab:, :].astype(f32)
            out[N_Z * slab :, :] = digits.astype(bf16)

    return plain_call(
        kernel,
        shaped(((N_Z - 1) * slab + height, width), bf16),
        *pieces,
        scalars=(places,),
        mebibytes=6,
        name="stack_z",
    )


def weave(columns, cuts, slab, places):
    n_x = len(columns[0])
    width = columns[0][0].shape[1]
    flat = [half for column in columns for half in column]
    edges = [0, *cuts, width]
    sizes = [stop - start for start, stop in zip(edges[:-1], edges[1:])]

    def kernel(at_ref, *refs):
        outs = refs[len(flat) :]
        for y in range(len(columns)):
            for dx in range(n_x):
                half = refs[y * n_x + dx]
                x = lax.rem(at_ref[1] + dx, n_x)
                for z in range(N_Z):
                    at = block_rows(z * n_x + x, slab)
                    for out, start, size in zip(outs, edges, sizes):
                        out[at, y * size : (y + 1) * size] = half[
                            z * slab : (z + 1) * slab, start : start + size
                        ]

    out = plain_call(
        kernel,
        tuple(shaped((N_Z * n_x * slab, size * len(columns)), bf16) for size in sizes),
        *flat,
        scalars=(places,),
        mebibytes=12,
        name="weave",
    )
    return out if cuts else out[0]


def proj_kernel(count, each, *refs):
    blocks, parts = refs[:count], refs[count : count + count // each]
    tok_ref, par_ref, res_out, low_out = refs[count + count // each :]
    total = tok_ref[...]
    for n, block in enumerate(blocks):
        size = block.shape[1]
        part = parts[n // each][:, n % each * size : (n % each + 1) * size]
        total = total + dot(block[...], part, 1, 1)
    res_out[...] = total
    normed, _, _ = norm_forward(total, par_ref[2:3, :], par_ref[3:4, :])
    low_out[...] = normed.astype(bf16)


ERF_TOP = (
    -2.72614225801306e-10,
    2.77068142495902e-08,
    -2.10102402082508e-06,
    -5.69250639462346e-05,
    -7.34990630326855e-04,
    -2.95459980854025e-03,
    -1.60960333262415e-02,
)
ERF_LOW = (
    -1.45660718464996e-05,
    -2.13374055278905e-04,
    -1.68282697438203e-03,
    -7.37332916720468e-03,
    -1.42647390514189e-02,
)


def erf(value):
    value = jnp.clip(value, -4.0, 4.0)
    square = value * value
    top = jnp.full_like(square, ERF_TOP[0])
    for number in ERF_TOP[1:]:
        top = top * square + number
    low = jnp.full_like(square, ERF_LOW[0])
    for number in ERF_LOW[1:]:
        low = low * square + number
    inverse = pl.reciprocal(low, approx=True)
    inverse = inverse * (2.0 - low * inverse)
    return value * top * inverse


def up_kernel(count, low_ref, *refs):
    outs = refs[-2 * count :]
    for n, part in enumerate(refs[:count]):
        hidden = dot(low_ref[...], part[...], 1, 0)
        share = 0.5 * (1.0 + erf(hidden * 0.7071067811865476))
        outs[2 * n][...] = (hidden * share).astype(bf16)
        slope = share + hidden * jnp.exp(-0.5 * hidden * hidden) * 0.3989422804014327
        outs[2 * n + 1][...] = slope.astype(bf16)


def up_call(low, parts, rows_all, spot, into):
    rows, model = low.shape
    width = parts[0].shape[1]
    cols = pl.BlockSpec((rows, TILE), lambda i, *_: (spot, i))
    return plain_call(
        functools.partial(up_kernel, len(parts)),
        (shaped((rows_all, width), bf16),) * (2 * len(parts)),
        low,
        *parts,
        grid=(width // TILE,),
        in_specs=[fixed(low.shape)] + [pl.BlockSpec((model, TILE), lambda i, *_: (0, i))] * len(parts),
        out_specs=(cols,) * (2 * len(parts)),
        into=into,
        mebibytes=14,
        name="up",
    )


def hidden_kernel(count, low_ref, *refs):
    outs = refs[-count:]
    for n in range(count):
        slope, part = refs[n], refs[count + n]
        outs[n][...] = (dot(low_ref[...], part[...], 1, 0) * slope[...].astype(f32)).astype(bf16)


def hidden_call(low, slopes, parts, spot, into):
    rows, model = low.shape
    width = parts[0].shape[1]
    cols = pl.BlockSpec((rows, TILE), lambda i, *_: (spot, i))
    return plain_call(
        functools.partial(hidden_kernel, len(parts)),
        tuple(shaped(slope.shape, bf16) for slope in slopes),
        low,
        *slopes,
        *parts,
        grid=(width // TILE,),
        in_specs=[fixed(low.shape)]
        + [cols] * len(parts)
        + [pl.BlockSpec((model, TILE), lambda i, *_: (0, i))] * len(parts),
        out_specs=(cols,) * len(parts),
        into=into,
        mebibytes=14,
        name="hidden",
    )


def wide_kernel(count, *refs):
    total = dot(refs[0][...], refs[count][...], 1, 1)
    for n in range(1, count):
        total = total + dot(refs[n][...], refs[count + n][...], 1, 1)
    refs[-1][...] = total.astype(refs[-1].dtype)


def wide_call(values, parts, rows, spot, kind):
    model, width = parts[0].shape
    return plain_call(
        functools.partial(wide_kernel, len(values)),
        shaped((rows, model), kind),
        *values,
        *parts,
        grid=(model // TILE,),
        in_specs=[pl.BlockSpec((rows, width), lambda i, *_: (spot, 0))] * len(values)
        + [pl.BlockSpec((TILE, width), lambda i, *_: (i, 0))] * len(parts),
        out_specs=pl.BlockSpec((rows, TILE), lambda i, *_: (0, i)),
        mebibytes=14,
        name="wide",
    )


def loss_kernel(chunks, each, *refs):
    res_ref, tea_ref, own_ref = refs[:3]
    received = refs[3 : 3 + chunks * each]
    live_ref, count_ref, grad_out, low_out, loss_out, far_ref = refs[3 + chunks * each :]
    add_received(received, each, far_ref)
    error = res_ref[...] - tea_ref[...] + own_ref[...] + far_ref[...]
    weighted = live_ref[...] * error
    grad = 2.0 * weighted / count_ref[...]
    grad_out[...] = grad
    low_out[...] = grad.astype(bf16)
    sums = jnp.sum(weighted * error, axis=0, keepdims=True)
    sums = jnp.concatenate([sums, jnp.zeros((7, sums.shape[1]), f32)], axis=0)
    loss_out[...] = jnp.where(pl.program_id(0) == 0, sums, loss_out[...] + sums)


def add_received(received, each, far_ref):
    for n in range(len(received) // each):

        @pl.when(pl.program_id(0) == n)
        def _():
            total = received[n * each][...].astype(f32)
            for ref in received[n * each + 1 : (n + 1) * each]:
                total = total + ref[...].astype(f32)
            far_ref[...] = total


def spread_kernel(count, low_ref, *refs):
    for part, out in zip(refs[:count], refs[count:]):
        out[...] = dot(low_ref[...], part[...], 1, 0).astype(bf16)


def spread_call(low, parts):
    return plain_call(
        functools.partial(spread_kernel, len(parts)),
        tuple(shaped((low.shape[0], part.shape[1]), bf16) for part in parts),
        low,
        *parts,
        mebibytes=12,
        name="spread",
    )


def unproject_kernel(half, spots, grad_ref, part_ref, far_out, near_out):
    piece = dot(grad_ref[...], part_ref[...], 1, 1)

    @pl.when(pl.program_id(0) < half)
    def _():
        far_out[...] = piece.astype(bf16)

    @pl.when(pl.program_id(0) >= half)
    def _():
        near_out[...] = piece


def unproject_call(grads, part, blocks, rows):
    half = len(blocks) // 2
    model, width = part.shape
    return plain_call(
        functools.partial(unproject_kernel, half),
        (shaped((half * rows, model), bf16), shaped((half * rows, model), f32)),
        grads,
        part,
        grid=(len(blocks),),
        in_specs=[
            pl.BlockSpec((rows, width), lambda i, spots: (spots[i], 0)),
            fixed(part.shape),
        ],
        out_specs=(
            pl.BlockSpec((rows, model), lambda i, spots: (jnp.minimum(i, half - 1), 0)),
            pl.BlockSpec((rows, model), lambda i, spots: (jnp.maximum(i - half, 0), 0)),
        ),
        scalars=(jnp.stack(blocks).astype(jnp.int32),),
        mebibytes=20,
        name="unproject",
    )


def norm_sums(grad, scaled, out_ref, first):
    sums = jnp.concatenate(
        [
            jnp.sum(grad * scaled, axis=0, keepdims=True),
            jnp.sum(grad, axis=0, keepdims=True),
            jnp.zeros((6, grad.shape[1]), f32),
        ],
        axis=0,
    )
    out_ref[...] = jnp.where(first, sums, out_ref[...] + sums)


def middle_kernel(chunks, each, *refs):
    grad_ref, received = refs[0], refs[1 : 1 + chunks * each]
    res_ref, gout_ref, par_ref, full_out, low_out, sum_out, far_ref = refs[1 + chunks * each :]
    add_received(received, each, far_ref)
    _, scaled, inverse = norm_forward(res_ref[...], par_ref[2:3, :], par_ref[3:4, :])
    grad = grad_ref[...] + far_ref[...]
    full = gout_ref[...] + norm_backward(grad, scaled, inverse, par_ref[2:3, :])
    full_out[...] = full
    low_out[...] = full.astype(bf16)
    norm_sums(grad, scaled, sum_out, pl.program_id(0) == 0)


def leave_kernel(count, *refs):
    own_ref, received = refs[0], refs[1 : 1 + count]
    tok_ref, res_ref, par_ref, two_ref, loss_ref, out_ref, sum_out, sum_ref = refs[1 + count :]
    _, scaled, inverse = norm_forward(tok_ref[...], par_ref[0:1, :], par_ref[1:2, :])
    grad = own_ref[...]
    for ref in received:
        grad = grad + ref[...].astype(f32)
    out_ref[...] = res_ref[...] + norm_backward(grad, scaled, inverse, par_ref[0:1, :])
    norm_sums(grad, scaled, sum_ref, pl.program_id(0) == 0)
    sum_out[...] = jnp.concatenate(
        [sum_ref[0:2, :], two_ref[0:2, :], loss_ref[0:1, :], jnp.zeros((3, grad.shape[1]), f32)],
        axis=0,
    )


def split_x(parts, n_x, places):
    model = parts[0][0].shape[0]
    slab = model // (N_Z * n_x)
    total = sum(part[0].shape[1] for part in parts)
    flat = [piece for part in parts for piece in part]

    def kernel(at_ref, *refs):
        outs = refs[len(flat) :]
        for dx in range(n_x):
            x = lax.rem(at_ref[1] + dx, n_x)
            for z in range(N_Z):
                at = block_rows(z * n_x + x, slab)
                lane = 0
                used = 0
                for part in parts:
                    value = refs[used][at, :]
                    size = value.shape[1]
                    if len(part) > 1:
                        value = value.astype(f32)
                        for ref in refs[used + 1 : used + len(part)]:
                            value = value + ref[at, :].astype(f32)
                        value = value.astype(bf16)
                    outs[dx][z * slab : (z + 1) * slab, lane : lane + size] = value
                    lane += size
                    used += len(part)

    return plain_call(
        kernel,
        tuple(shaped((model // n_x, total), bf16) for _ in range(n_x)),
        *flat,
        scalars=(places,),
        mebibytes=12,
        name="split_x",
    )


def split_z(parts, places):
    rows, width = parts[0].shape
    slab = rows // N_Z

    def kernel(at_ref, *refs):
        for k, out in enumerate(refs[len(parts) :]):
            at = block_rows(lax.rem(at_ref[0] + k, N_Z), slab)
            total = refs[0][at, :].astype(f32)
            for ref in refs[1 : len(parts)]:
                total = total + ref[at, :].astype(f32)
            out[...] = total.astype(out.dtype)

    shapes = (shaped((slab, width), f32),) + (shaped((slab, width), bf16),) * (N_Z - 1)
    return plain_call(kernel, shapes, *parts, scalars=(places,), mebibytes=8, name="split_z")


def adam_kernel(layout, counts, *refs):
    grads = []
    for count in counts:
        grad = refs[0][...].astype(f32)
        for ref in refs[1:count]:
            grad = grad + ref[...].astype(f32)
        grads.append(grad)
        refs = refs[count:]
    count = len(layout)
    states, outs = refs[: 3 * count], refs[3 * count :]
    for n, (source, start, size, turned) in enumerate(layout):
        weight, first, second = states[3 * n : 3 * n + 3]
        if len(weight.shape) == 3:
            matrices = weight.shape[0]
            lanes = size // matrices
            for k in range(matrices):
                own = [
                    grads[at][:, lane + k * lanes : lane + (k + 1) * lanes] for at, lane in start
                ]
                own = own[0] if len(own) == 1 else jnp.concatenate(own, axis=1)
                new = adam_step(weight[k], own, first[k], second[k], weight_decay, learn_rate)
                for out, value in zip(outs[3 * n : 3 * n + 3], new):
                    out[k] = value
        else:
            part = grads[source][:, start : start + size]
            if turned:
                part = part.T
            new = adam_step(weight[...], part, first[...], second[...], weight_decay, learn_rate)
            for out, value in zip(outs[3 * n : 3 * n + 3], new):
                out[...] = value


def adam_call(groups, layout, *states):
    shapes = tuple(shaped(s.shape, f32) for s in states)
    out = plain_call(
        functools.partial(adam_kernel, layout, [len(group) for group in groups]),
        shapes,
        *[piece for group in groups for piece in group],
        *states,
        mebibytes=16,
        name="adam",
    )
    return [out[3 * n : 3 * n + 3] for n in range(len(layout))]


def tie(*values):
    return lax.optimization_barrier(values)


def local(
    n_x,
    n_y,
    tokens,
    teacher,
    segments,
    live_mask,
    weight_qkv,
    weight_proj,
    weight_up,
    weight_down,
    norm_params,
    first_qkv,
    first_proj,
    first_up,
    first_down,
    first_norms,
    second_qkv,
    second_proj,
    second_up,
    second_down,
    second_norms,
):
    z_at, x_at = lax.axis_index("z"), lax.axis_index("x")
    y_at, core_at = lax.axis_index("y"), lax.axis_index("core")
    rows, model = tokens.shape
    group_rows = segments.shape[0]
    slab = weight_qkv.shape[1]
    width = weight_qkv.shape[2]
    unit = weight_up.shape[1]
    part_rows = min(128, rows)
    wide_rows = min(256, rows)
    depth = N_Z * slab
    sizes = {"z": N_Z, "x": n_x, "y": n_y, "core": N_CORE}
    places = jnp.stack([z_at, x_at]).astype(jnp.int32)
    offsets = [(dc, dy) for dc in range(N_CORE) for dy in range(n_y)]
    other = N_CORE - 1

    def send(value, axis, step):
        size = sizes[axis]
        return lax.ppermute(value, axis, [(i, (i + step) % size) for i in range(size)])

    def send_col(value, dy, dc):
        perm = [
            (y * N_CORE + c, (y + dy) % n_y * N_CORE + (c + dc) % N_CORE)
            for y in range(n_y)
            for c in range(N_CORE)
        ]
        return lax.ppermute(value, ("y", "core"), perm)

    def fetch(value, axis):
        return [value] + [send(value, axis, -k) for k in range(1, sizes[axis])]

    def place(dy, dc):
        return ((y_at + dy) % n_y * N_CORE + (core_at + dc) % N_CORE) * rows

    shard_qkv, shard_up, shard_down = plain_call(
        pack_kernel,
        (
            shaped((slab, 4 * width), bf16),
            shaped((slab + DIGITS, unit), bf16),
            shaped((slab, unit), bf16),
        ),
        live_mask.reshape(-1, 128),
        weight_qkv,
        weight_proj,
        weight_up,
        weight_down,
        mebibytes=8,
        name="pack",
    )
    near_qkv = fetch(shard_qkv, "z")
    low_one = plain_call(
        first_kernel,
        shaped(tokens.shape, bf16),
        tokens,
        norm_params,
        grid=(rows // part_rows,),
        in_specs=row_blocks(part_rows, model) + [fixed(norm_params.shape)],
        out_specs=row_blocks(part_rows, model)[0],
        mebibytes=8,
        name="first",
    )
    blocks_one = fetch(low_one, "y") + [send(low_one, "core", -1)]
    near_qkv, shard_down, shard_up, blocks_one[n_y] = tie(
        near_qkv, shard_down, shard_up, blocks_one[n_y]
    )

    beside_qkv = fetch(stack_z(near_qkv, slab, places), "x")
    blocks_one, shard_up = tie(blocks_one, shard_up)
    near_up = fetch(shard_up, "z")
    blocks_one = blocks_one + [send(block, "core", -1) for block in blocks_one[1:n_y]]
    spots_here = jnp.stack([place(dy, dc) for dc, dy in offsets]).astype(jnp.int32)
    spots = jnp.stack([place(-dy, -dc) for dc, dy in offsets]).astype(jnp.int32)
    group_one = place_blocks(blocks_one, spots_here)
    geometry = attend_geometry(segments, live_mask)
    own_live = lax.dynamic_slice_in_dim(
        live_mask, (y_at * N_CORE + core_at) * rows, rows, 0
    ).astype(f32)[:, None]
    beside_qkv, near_up, group_one, geometry, own_live, shard_down, spots = tie(
        beside_qkv, near_up, group_one, geometry, own_live, shard_down, spots
    )

    block_up = stack_z(near_up, slab, places)
    full_qkv, part_proj = weave([beside_qkv], [3 * width], slab, places)
    block_up, part_proj = tie(block_up, part_proj)
    beside_up = fetch(block_up, "x")
    near_down = fetch(shard_down, "z")
    full_proj = fetch(part_proj, "y")
    projected = dot(group_one, full_qkv, 1, 0).astype(bf16)
    mixed = attend_forward(projected, geometry, spots, rows)
    mixed, beside_up, near_down, full_proj = tie(mixed, beside_up, near_down, full_proj)

    blocks_mixed = [
        piece if key == (0, 0) else send_col(piece, -key[1], -key[0])
        for key, piece in zip(offsets, mixed)
    ]
    full_proj = full_proj + [send(part, "core", -1) for part in full_proj]
    block_down = stack_z(near_down, slab, places)
    full_up = [weave([beside_up], [], slab, places)]
    live_count = sum(
        256.0 * part[depth, 0].astype(f32) + 16.0 * part[depth + 1, 0].astype(f32)
        + part[depth + 2, 0].astype(f32)
        for part in beside_up
    ).reshape(1, 1)
    beside_down = fetch(block_down, "x")
    blocks_mixed, full_proj, full_up, live_count = tie(
        blocks_mixed, full_proj, full_up, live_count
    )
    full_up.append(send(full_up[0], "core", -1))
    count = len(offsets)
    residual, low_two = plain_call(
        functools.partial(proj_kernel, count, 1),
        (shaped(tokens.shape, f32), shaped(tokens.shape, bf16)),
        *blocks_mixed,
        *full_proj,
        tokens,
        norm_params,
        grid=(rows // wide_rows,),
        in_specs=row_blocks(wide_rows, *([width] * count))
        + [fixed(part.shape) for part in full_proj]
        + row_blocks(wide_rows, model)
        + [fixed(norm_params.shape)],
        out_specs=tuple(row_blocks(wide_rows, model, model)),
        mebibytes=18,
        name="proj",
    )
    low_two, full_up = tie(low_two, full_up)

    chunk = min(256, rows)
    chunks = range(rows // chunk)
    neighbours = range(1, n_y)
    rows_all = n_y * rows

    def cross(value, n, back):
        piece = value[n * chunk : (n + 1) * chunk]
        return {dy: send(piece, "y", dy if back else -dy) for dy in neighbours}

    def spot_of(dy, n):
        return (dy * rows) // chunk + n

    low_far = {0: cross(low_two, 0, False)}
    hidden = up_call(low_two, full_up, rows_all, 0, ())
    low_far[0], hidden, low_two, beside_down = tie(low_far[0], hidden, low_two, beside_down)
    full_down = [weave([beside_down], [], slab, places)]
    full_down.append(send(full_down[0], "core", -1))
    far_out = {}
    for n in chunks:
        if n + 1 in chunks:
            low_far[n + 1] = cross(low_two, n + 1, False)
        for dy in neighbours:
            hidden = up_call(low_far[n][dy], full_up, rows_all, spot_of(dy, n), hidden)
        outs = {
            dy: wide_call(hidden[::2], full_down, chunk, spot_of(dy, n), bf16) for dy in neighbours
        }
        if n + 1 in chunks:
            outs, hidden, low_far[n + 1] = tie(outs, hidden, low_far[n + 1])
        else:
            outs, hidden = tie(outs, hidden)
        if n:
            far_out[n - 1] = tie(far_out[n - 1], outs)[0]
        far_out[n] = {dy: send(outs[dy], "y", -dy) for dy in neighbours}
    own_out = wide_call(hidden[::2], full_down, rows, 0, f32)
    own_out, far_out = tie(own_out, far_out)
    far_out = [far_out[n][dy] for n in chunks for dy in neighbours]
    each = len(neighbours)
    grad_output, grad_branch, loss_rows = plain_call(
        functools.partial(loss_kernel, len(chunks), each),
        (shaped(tokens.shape, f32), shaped(tokens.shape, bf16), shaped((8, model), f32)),
        residual,
        teacher,
        own_out,
        *far_out,
        own_live,
        live_count,
        grid=(len(chunks),),
        in_specs=row_blocks(chunk, model, model, model)
        + [fixed((chunk, model))] * len(far_out)
        + row_blocks(chunk, 1)
        + [fixed((1, 1))],
        out_specs=tuple(row_blocks(chunk, model, model) + [fixed((8, model))]),
        scratch=[pltpu.VMEM((chunk, model), f32)],
        mebibytes=20,
        name="loss",
    )
    active, slope = hidden[::2], hidden[1::2]

    def gather_rows(own, far):
        return jnp.concatenate([own] + [far[n][dy] for dy in neighbours for n in chunks], axis=0)

    low_all = gather_rows(low_two, low_far)
    grad_branch, low_all = tie(grad_branch, low_all)

    grad_far = {0: cross(grad_branch, 0, False)}
    grad_hidden = hidden_call(grad_branch, slope, full_down, 0, ())
    own_two = wide_call(grad_hidden, full_up, rows, 0, f32)
    grad_far[0], grad_hidden, own_two, grad_branch = tie(
        grad_far[0], grad_hidden, own_two, grad_branch
    )
    far_two = {}
    for n in chunks:
        if n + 1 in chunks:
            grad_far[n + 1] = cross(grad_branch, n + 1, False)
        for dy in neighbours:
            grad_hidden = hidden_call(
                grad_far[n][dy], slope, full_down, spot_of(dy, n), grad_hidden
            )
        outs = {
            dy: wide_call(grad_hidden, full_up, chunk, spot_of(dy, n), bf16) for dy in neighbours
        }
        if n + 1 in chunks:
            outs, grad_hidden, grad_far[n + 1] = tie(outs, grad_hidden, grad_far[n + 1])
        else:
            grad_all = gather_rows(grad_branch, grad_far)
            far_down = dot(grad_all, active[other], 0, 0).astype(bf16)
            outs, grad_hidden, grad_all, far_down, far_two = tie(
                outs, grad_hidden, grad_all, far_down, far_two
            )
        far_two[n] = {dy: send(outs[dy], "y", -dy) for dy in neighbours}

    def send_back(pieces):
        return [
            piece if key == (0, 0) else send_col(piece, key[1], key[0])
            for key, piece in zip(offsets, pieces)
        ]

    def hop_x(halves):
        return [halves[0]] + [send(halves[dx], "x", dx) for dx in range(1, n_x)]

    def spread_z(pieces):
        return [pieces[0]] + [send(pieces[k], "z", k) for k in range(1, N_Z)]

    far_up = dot(low_all, grad_hidden[other], 0, 0).astype(bf16)
    sent_down, sent_up = send(far_down, "core", 1), send(far_up, "core", 1)
    hold_down = (dot(grad_all, active[0], 0, 0) + sent_down.astype(f32)).astype(bf16)
    halves_down = split_x([[hold_down]], n_x, places)
    hold_up = (dot(low_all, grad_hidden[0], 0, 0) + sent_up.astype(f32)).astype(bf16)
    halves_up = split_x([[hold_up]], n_x, places)
    parts_down = hop_x(halves_down)
    far_two, hold_down, halves_up = tie(far_two, hold_down, halves_up)
    far_two = [far_two[n][dy] for n in chunks for dy in neighbours]
    grad_residual, grad_low, sums_two = plain_call(
        functools.partial(middle_kernel, len(chunks), each),
        (shaped(tokens.shape, f32), shaped(tokens.shape, bf16), shaped((8, model), f32)),
        own_two,
        *far_two,
        residual,
        grad_output,
        norm_params,
        grid=(len(chunks),),
        in_specs=row_blocks(chunk, model)
        + [fixed((chunk, model))] * len(far_two)
        + row_blocks(chunk, model, model)
        + [fixed(norm_params.shape)],
        out_specs=tuple(row_blocks(chunk, model, model) + [fixed((8, model))]),
        scratch=[pltpu.VMEM((chunk, model), f32)],
        mebibytes=20,
        name="middle",
    )
    pieces_attn = spread_call(grad_low, full_proj)
    pieces_attn, halves_up, grad_low = tie(pieces_attn, halves_up, grad_low)

    sent_attn = send_back(pieces_attn)
    grad_proj = [dot(grad_low, block, 0, 0).astype(bf16) for block in blocks_mixed]
    sent_proj = send(jnp.concatenate(grad_proj[n_y:], axis=1), "core", 1)
    sent_attn, sent_proj, grad_proj = tie(sent_attn, sent_proj, grad_proj)

    hold_proj = [
        (
            grad_proj[dy].astype(f32) + sent_proj[:, dy * width : (dy + 1) * width].astype(f32)
        ).astype(bf16)
        for dy in range(n_y)
    ]
    sent_attn, hold_proj, halves_up = tie(sent_attn, hold_proj, halves_up)
    part_proj = [hold_proj[0]] + [send(hold_proj[k], "y", k) for k in range(1, n_y)]
    grad_projected = attend_backward(projected, sent_attn, spots, geometry)
    grad_projected, parts_down, part_proj, halves_up = tie(
        grad_projected, parts_down, part_proj, halves_up
    )

    parts_up = hop_x(halves_up)
    last_down = spread_z(split_z(parts_down, places))
    far_one, near_one = unproject_call(
        grad_projected,
        full_qkv,
        [place(dy, dc) // rows for dc in reversed(range(N_CORE)) for dy in range(n_y)],
        rows,
    )
    far_one, grad_projected = tie(far_one, grad_projected)
    sent_one = send(far_one, "core", 1)
    grad_qkv = dot(group_one, grad_projected, 0, 0).astype(bf16)
    halves_qkv = split_x([[grad_qkv], part_proj], n_x, places)
    halves_qkv, sent_one, near_one, parts_up, last_down = tie(
        halves_qkv, sent_one, near_one, parts_up, last_down
    )
    pieces_up = split_z(parts_up, places)
    parts = [
        near_one[dy * rows : (dy + 1) * rows] + sent_one[dy * rows : (dy + 1) * rows].astype(f32)
        for dy in range(n_y)
    ]
    sent_parts = [parts[k].astype(bf16) for k in range(1, n_y)]
    halves_qkv, sent_parts, pieces_up = tie(halves_qkv, sent_parts, pieces_up)

    received = [send(part, "y", k) for k, part in enumerate(sent_parts, 1)]
    parts_qkv = hop_x(halves_qkv)
    last_up = spread_z(pieces_up)
    parts_qkv, received, last_up = tie(parts_qkv, received, last_up)

    pieces_qkv = split_z(parts_qkv, places)
    pieces_qkv, received = tie(pieces_qkv, received)
    last_qkv = spread_z(pieces_qkv)
    token_grad, sums = plain_call(
        functools.partial(leave_kernel, len(received)),
        (shaped(tokens.shape, f32), shaped((8, model), f32)),
        parts[0],
        *received,
        tokens,
        grad_residual,
        norm_params,
        sums_two,
        loss_rows,
        grid=(rows // part_rows,),
        in_specs=row_blocks(part_rows, *([model] * (3 + len(received))))
        + [fixed(norm_params.shape), fixed((8, model)), fixed((8, model))],
        out_specs=tuple(row_blocks(part_rows, model) + [fixed((8, model))]),
        scratch=[pltpu.VMEM((8, model), f32)],
        mebibytes=14,
        name="leave",
    )
    for axis in ("core", "y", "x", "z"):
        step = 1
        while step < sizes[axis]:
            pairs = [(i, i ^ step) for i in range(sizes[axis])]
            sums = sums + lax.ppermute(sums, axis, pairs)
            step *= 2
    sums, last_qkv = tie(sums, last_qkv)
    loss_sum = jnp.sum(sums[4])
    live_count = live_count[0, 0]

    (new_down,) = adam_call(
        [last_down], [(0, 0, unit, True)], weight_down, first_down, second_down
    )
    (new_up,) = adam_call([last_up], [(0, 0, unit, False)], weight_up, first_up, second_up)
    lanes = min(128, width)
    new_qkv, new_proj = adam_call(
        [last_qkv],
        [
            (0, [(0, 3 * at) for at in range(0, width, lanes)], 3 * lanes, False),
            (0, 3 * width, width, True),
        ],
        weight_qkv,
        first_qkv,
        second_qkv,
        weight_proj,
        first_proj,
        second_proj,
    )
    new_norms = adam_step(norm_params, sums[:4], first_norms, second_norms, 0.0, norm_rate)
    return (
        loss_sum / live_count,
        token_grad,
        new_qkv[0],
        new_proj[0],
        new_up[0],
        new_down[0],
        new_norms[0],
        new_qkv[1],
        new_proj[1],
        new_up[1],
        new_down[1],
        new_norms[1],
        new_qkv[2],
        new_proj[2],
        new_up[2],
        new_down[2],
        new_norms[2],
    )


def solution(mesh):
    n_x = mesh.shape["row"] // N_Z
    n_y = mesh.shape["col"] // N_CORE
    mesh = jax.sharding.Mesh(
        mesh.devices.reshape(N_Z, n_x, n_y, N_CORE), ("z", "x", "y", "core")
    )
    row, col = ("z", "x"), ("y", "core")
    matrices = (P(None, row, col), P(col, row), P(row, col), P(col, row), P())
    tokens = P(row + col, None)
    return jax.shard_map(
        functools.partial(local, n_x, n_y),
        mesh=mesh,
        in_specs=(tokens, tokens, P(row), P(row)) + matrices * 3,
        out_specs=(P(), tokens) + matrices * 3,
        check_vma=False,
    )
```

```python
import functools

import jax
import jax.numpy as jnp
from jax import lax
from jax.experimental import pallas as pl
from jax.experimental.pallas import tpu as pltpu
from jax.sharding import PartitionSpec as P

HEAD_DIM = 64
PATCHES = 577
STEP = 10
WINDOW = 640
QROWS = 320
TILE = 256
DIGITS = 16
SMALL = pl.CostEstimate(flops=1024, bytes_accessed=1024, transcendentals=0)
N_Z = 4
N_CORE = 2

layer_eps = 1e-06
adam_eps = 1e-08
learn_rate = 0.03
norm_rate = 0.25
moment_decay = 0.5
weight_decay = 0.05

bf16 = jnp.bfloat16
f32 = jnp.float32


def norm_forward(values, gain_row, bias_row):
    average = jnp.mean(values, axis=-1, keepdims=True)
    centred = values - average
    variance = jnp.mean(centred * centred, axis=-1, keepdims=True)
    inverse = lax.rsqrt(variance + layer_eps)
    scaled = centred * inverse
    return (scaled * gain_row + bias_row, scaled, inverse)


def norm_backward(upstream, scaled, inverse, gain_row):
    weighted = upstream * gain_row
    return inverse * (
        weighted
        - jnp.mean(weighted, axis=-1, keepdims=True)
        - scaled * jnp.mean(weighted * scaled, axis=-1, keepdims=True)
    )


def gelu_slope(hidden):
    return (
        0.5 * (1.0 + lax.erf(hidden * 0.7071067811865476))
        + hidden * jnp.exp(-0.5 * hidden * hidden) * 0.3989422804014327
    )


def adam_step(weight, gradient, momentum, variance, decay_rate, rate):
    momentum = moment_decay * momentum + (1.0 - moment_decay) * gradient
    variance = moment_decay * variance + (1.0 - moment_decay) * gradient * gradient
    correction = 1.0 - moment_decay**STEP
    direction = momentum / correction / (jnp.sqrt(variance / correction) + adam_eps)
    return (weight - rate * (direction + decay_rate * weight), momentum, variance)


def dot(left, right, left_dim, right_dim):
    return lax.dot_general(
        left, right, (((left_dim,), (right_dim,)), ((), ())), preferred_element_type=f32
    )


def head_lanes(width, head):
    lanes = lax.broadcasted_iota(jnp.int32, (1, width), 1)
    return (lanes >= head * HEAD_DIM) & (lanes < (head + 1) * HEAD_DIM)


def attend_scores(q_part, k_all, mask):
    scores = dot(q_part, k_all, 1, 1) + mask
    weights = jnp.exp(scores - jnp.max(scores, axis=-1, keepdims=True))
    return weights, jnp.sum(weights, axis=-1, keepdims=True)


def image_window(begin, group_rows):
    image = pl.program_id(0)
    start = jnp.minimum(begin[image] // 16 * 16, group_rows - WINDOW)
    first = begin[image] - start
    return image, pl.multiple_of(start, 16), first


def fill_mask(bias, mask_ref):
    for row in range(0, WINDOW, 128):
        rows = row + lax.broadcasted_iota(jnp.int32, (128, WINDOW), 0)
        cols = lax.broadcasted_iota(jnp.int32, (128, WINDOW), 1)
        mask_ref[row : row + 128, :] = jnp.where(rows == cols, 0.0, bias)


def rows_inside(rows, row_start, first):
    ids = row_start + lax.broadcasted_iota(jnp.int32, (rows, 1), 0)
    return (ids >= first) & (ids < first + PATCHES)


def attend_forward_kernel(blocks, begin, spots, code_ref, *refs):
    bias_out, out_ref, mask_ref = refs[-3:]
    image, start, first = image_window(begin, refs[0].shape[0])
    code = code_ref[pl.ds(start, WINDOW), :]
    bias = jnp.where(code == image, 0.0, -1e30).astype(f32).T
    bias_out[0] = bias[0:8, :]
    fill_mask(bias[0:1, :], mask_ref)
    lanes = refs[0].shape[1]

    for tile in range((len(refs) - 3 - blocks) // 3):
        q_ref, k_ref, v_ref = refs[3 * tile : 3 * tile + 3]
        cols = slice(tile * lanes, (tile + 1) * lanes)

        @pl.when(image == 0)
        def _():
            out_ref[:, cols] = v_ref[...]

        k_all = k_ref[pl.ds(start, WINDOW), :]
        v_all = v_ref[pl.ds(start, WINDOW), :]
        for row in range(0, WINDOW, QROWS):
            at = pl.ds(pl.multiple_of(start + row, 16), QROWS)
            q_part = q_ref[at, :] * jnp.asarray(HEAD_DIM ** (-0.5), bf16)
            inside = rows_inside(QROWS, row, first)
            mixed = None
            for head in range(lanes // HEAD_DIM):
                mine = head_lanes(lanes, head)
                q_head = jnp.where(mine, q_part, jnp.zeros_like(q_part))
                weights, totals = attend_scores(q_head, k_all, mask_ref[row : row + QROWS, :])
                part = dot(weights.astype(bf16), v_all, 1, 0) * (1.0 / totals)
                mixed = part if mixed is None else jnp.where(mine, part, mixed)
            out_ref[at, cols] = jnp.where(inside, mixed.astype(bf16), out_ref[at, cols])

    @pl.when(image == pl.num_programs(0) - 1)
    def _():
        for n, block in enumerate(refs[-3 - blocks : -3]):
            rows = block.shape[0]
            block[...] = out_ref[pl.ds(pl.multiple_of(spots[n], rows), rows), :]


def attend_backward_kernel(blocks, begin, spots, bias_ref, *refs):
    out_ref, p_ref, s_ref, go_ref, mask_ref = refs[-5:]
    go_blocks, refs = refs[3 : 3 + blocks], refs[:3]
    image, start, first = image_window(begin, refs[0].shape[0])
    fill_mask(bias_ref[0, 0:1, :], mask_ref)
    lanes = refs[0].shape[1]
    rows = go_blocks[0].shape[0]
    whole = pl.ds(start, WINDOW)
    inside_all = rows_inside(WINDOW, 0, first)

    @pl.when(image == 0)
    def _():
        for n, block_ref in enumerate(go_blocks):
            go_ref[pl.ds(pl.multiple_of(spots[n], rows), rows), :] = block_ref[...]

    for tile in range(len(refs) // 3):
        q_ref, k_ref, v_ref = refs[3 * tile : 3 * tile + 3]
        cols = slice(tile * lanes, (tile + 1) * lanes)
        base = 3 * tile * lanes
        q_cols, k_cols, v_cols = [
            slice(base + n * lanes, base + (n + 1) * lanes) for n in range(3)
        ]

        @pl.when(image == 0)
        def _():
            out_ref[:, base : base + 2 * lanes] = jnp.zeros((out_ref.shape[0], 2 * lanes), bf16)
            out_ref[:, v_cols] = go_ref[:, cols]

        k_all = k_ref[whole, :]
        v_all = v_ref[whole, :]
        q_all = q_ref[whole, :] * jnp.asarray(HEAD_DIM ** (-0.5), bf16)
        go_all = go_ref[whole, cols]
        key_grad = None
        value_grad = None
        for head in range(lanes // HEAD_DIM):
            mine = head_lanes(lanes, head)
            q_mine = jnp.where(mine, q_all, jnp.zeros_like(q_all))
            go_mine = jnp.where(mine, go_all, jnp.zeros_like(go_all))
            for row in range(0, WINDOW, QROWS):
                part = slice(row, row + QROWS)
                at = pl.ds(pl.multiple_of(start + row, 16), QROWS)
                inside = rows_inside(QROWS, row, first)
                weights, totals = attend_scores(q_mine[part], k_all, mask_ref[part, :])
                weights = weights * jnp.where(inside, 1.0 / totals, 0.0)
                weight_grad = dot(go_mine[part], v_all, 1, 1)
                product = weights * weight_grad
                score_grad = (
                    product - weights * jnp.sum(product, axis=-1, keepdims=True)
                ).astype(bf16)
                p_ref[part, :] = weights.astype(bf16)
                s_ref[part, :] = score_grad
                query_grad = (dot(score_grad, k_all, 1, 0) * HEAD_DIM ** (-0.5)).astype(bf16)
                out_ref[at, q_cols] = jnp.where(inside & mine, query_grad, out_ref[at, q_cols])
            key_part = dot(q_mine, s_ref[...], 0, 0)
            value_part = dot(go_mine, p_ref[...], 0, 0)
            key_grad = key_part if key_grad is None else key_grad + key_part
            value_grad = value_part if value_grad is None else value_grad + value_part
        key_rows = key_grad.T.astype(bf16)
        value_rows = value_grad.T.astype(bf16)
        out_ref[whole, k_cols] = jnp.where(inside_all, key_rows, out_ref[whole, k_cols])
        out_ref[whole, v_cols] = jnp.where(inside_all, value_rows, out_ref[whole, v_cols])


def qkv_operands(projected, tile):
    group_rows, total = projected.shape
    lanes = min(128, total // 3)
    if lanes % 128 == 0:
        specs = [
            pl.BlockSpec((group_rows, lanes), functools.partial(lambda n, i, *_: (0, n), 3 * tile + n))
            for n in range(3)
        ]
        return [projected] * 3, specs
    parts = [projected[:, n * lanes : (n + 1) * lanes] for n in range(3)]
    return parts, [fixed((group_rows, lanes))] * 3


def all_operands(projected):
    width = projected.shape[1] // 3
    operands, specs = [], []
    for tile in range(width // min(128, width)):
        more, places = qkv_operands(projected, tile)
        operands += more
        specs += places
    return operands, specs


def attend_forward(projected, geometry, spots, rows):
    begin, code = geometry
    group_rows, total = projected.shape
    width = total // 3
    blocks = group_rows // rows
    images = begin.shape[0]
    operands, specs = all_operands(projected)
    out = plain_call(
        functools.partial(attend_forward_kernel, blocks),
        (shaped((rows, width), bf16),) * blocks + (shaped((images, 8, WINDOW), f32),),
        code,
        *operands,
        grid=begin.shape,
        in_specs=[fixed(code.shape)] + specs,
        out_specs=(fixed((rows, width)),) * blocks
        + (pl.BlockSpec((1, 8, WINDOW), lambda i, *_: (i, 0, 0)),),
        scratch=[pltpu.VMEM((group_rows, width), bf16), pltpu.VMEM((WINDOW, WINDOW), f32)],
        scalars=(begin, spots),
        mebibytes=20,
        name="attention_forward",
    )
    return out[:blocks], out[blocks]


def attend_backward(projected, go_blocks, spots, begin, bias, tile, into):
    group_rows, total = projected.shape
    lanes = min(128, total // 3)
    operands, specs = qkv_operands(projected, tile)
    return plain_call(
        functools.partial(attend_backward_kernel, len(go_blocks)),
        shaped((group_rows, total), bf16),
        bias,
        *operands,
        *go_blocks,
        grid=begin.shape,
        in_specs=[pl.BlockSpec((1, 8, WINDOW), lambda i, *_: (i, 0, 0))]
        + specs
        + [fixed(block.shape) for block in go_blocks],
        out_specs=pl.BlockSpec((group_rows, 3 * lanes), lambda i, *_: (0, tile)),
        scratch=[pltpu.VMEM((WINDOW, WINDOW), bf16)] * 2
        + [pltpu.VMEM((group_rows, lanes), bf16), pltpu.VMEM((WINDOW, WINDOW), f32)],
        scalars=(begin, spots),
        into=into,
        mebibytes=20,
        name="attention_backward",
    )


def attend_geometry(segments, live_mask):
    group_rows = segments.shape[0]
    numbers = jnp.arange(group_rows // PATCHES, dtype=jnp.int32)
    positions = jnp.arange(group_rows, dtype=jnp.int32)
    begin = jnp.min(
        jnp.where(segments[None, :] == numbers[:, None], positions[None, :], group_rows - PATCHES),
        axis=1,
    )
    code = jnp.where(live_mask == 1, segments, -1)
    return begin, jnp.broadcast_to(code[:, None], (group_rows, 128))


def plain_call(kernel, out_shape, *operands, grid=(), in_specs=None, out_specs=None, scratch=(), scalars=(), into=(), mebibytes=16, name=None):
    params = pltpu.CompilerParams(vmem_limit_bytes=mebibytes * 1024 * 1024)
    if in_specs is None:
        in_specs = [pl.BlockSpec(a.shape, functools.partial(lambda n, *_: (0,) * n, a.ndim)) for a in operands]
    in_specs = list(in_specs) + [pl.BlockSpec(memory_space=pl.ANY)] * len(into)
    if out_specs is None:
        out_specs = jax.tree.map(
            lambda s: pl.BlockSpec(s.shape, functools.partial(lambda n, *_: (0,) * n, len(s.shape))), out_shape
        )
    return pl.pallas_call(
        kernel,
        grid_spec=pltpu.PrefetchScalarGridSpec(
            num_scalar_prefetch=len(scalars),
            grid=grid,
            in_specs=in_specs,
            out_specs=out_specs,
            scratch_shapes=list(scratch),
        ),
        out_shape=out_shape,
        input_output_aliases={len(scalars) + len(operands) + n: n for n in range(len(into))},
        compiler_params=params,
        cost_estimate=SMALL,
        name=name,
    )(*scalars, *operands, *into)


def shaped(shape, dtype):
    return jax.ShapeDtypeStruct(tuple(shape), dtype)


def row_blocks(rows, *widths):
    return [pl.BlockSpec((rows, w), lambda i, *_: (i, 0)) for w in widths]


def fixed(shape):
    return pl.BlockSpec(tuple(shape), functools.partial(lambda n, *_: (0,) * n, len(shape)))


def pack_kernel(live_ref, qkv_ref, proj_ref, up_ref, down_ref, qkv_out, up_out, down_out):
    count, slab, width = qkv_ref.shape
    lanes = min(128, width)
    for n in range(count):
        for t in range(width // lanes):
            at = (count * t + n) * lanes
            qkv_out[:, at : at + lanes] = qkv_ref[n][:, t * lanes : (t + 1) * lanes].astype(bf16)
    qkv_out[:, count * width :] = proj_ref[...].T.astype(bf16)
    up_out[:slab, :] = up_ref[...].astype(bf16)
    live = jnp.sum(jnp.sum(live_ref[...].astype(f32), axis=0, keepdims=True), axis=1, keepdims=True)
    high = jnp.floor(live * (1.0 / 256.0))
    middle = jnp.floor(live * (1.0 / 16.0)) - 16.0 * high
    low = live - 256.0 * high - 16.0 * middle
    row = lax.broadcasted_iota(jnp.int32, (DIGITS, up_out.shape[1]), 0)
    digits = jnp.where(row == 0, high, jnp.where(row == 1, middle, jnp.where(row == 2, low, 0.0)))
    up_out[slab:, :] = digits.astype(bf16)
    down_out[...] = down_ref[...].T.astype(bf16)


def first_kernel(tok_ref, par_ref, low_out):
    normed, _, _ = norm_forward(tok_ref[...], par_ref[0:1, :], par_ref[1:2, :])
    low_out[...] = normed.astype(bf16)


def place_blocks(blocks, spots):
    rows, width = blocks[0].shape

    def kernel(spot_ref, *refs):
        for n, ref in enumerate(refs[:-1]):
            refs[-1][pl.ds(pl.multiple_of(spot_ref[n], rows), rows), :] = ref[...]

    return plain_call(
        kernel,
        shaped((rows * len(blocks), width), bf16),
        *blocks,
        scalars=(spots,),
        mebibytes=20,
        name="place_blocks",
    )


def block_rows(block, slab):
    return pl.ds(pl.multiple_of(block * slab, slab), slab)


def stack_z(pieces, slab, places, count=1):
    height, width = pieces[0].shape
    extra = height - slab
    shapes = (shaped((N_Z * slab // count + extra, width), bf16),) * count

    def kernel(at_ref, *refs):
        held = refs[-1]
        for k, ref in enumerate(refs[:N_Z]):
            held[block_rows(lax.rem(at_ref[0] + N_Z - k, N_Z), slab), :] = ref[:slab, :]
        for n, out in enumerate(refs[N_Z:-1]):
            rows = N_Z * slab // count
            out[:rows, :] = held[n * rows : (n + 1) * rows, :]
            if extra:
                digits = refs[0][slab:, :].astype(f32)
                for ref in refs[1:N_Z]:
                    digits = digits + ref[slab:, :].astype(f32)
                out[rows:, :] = digits.astype(bf16)

    out = plain_call(
        kernel,
        shapes,
        *pieces,
        scalars=(places,),
        scratch=[pltpu.VMEM((N_Z * slab, width), bf16)],
        mebibytes=8,
        name="stack_z",
    )
    return out if count > 1 else out[0]


def weave(columns, cuts, slab, places):
    n_x = len(columns[0])
    width = columns[0][0][0].shape[1]
    flat = [piece for column in columns for half in column for piece in half]
    edges = [0, *cuts, width]
    sizes = [stop - start for start, stop in zip(edges[:-1], edges[1:])]

    def kernel(at_ref, *refs):
        outs = refs[len(flat) :]
        used = 0
        for y, column in enumerate(columns):
            for dx, half in enumerate(column):
                x = lax.rem(at_ref[1] + dx, n_x)
                share = N_Z // len(half)
                for z in range(N_Z):
                    piece = refs[used + z // share]
                    at = block_rows(z * n_x + x, slab)
                    row = z % share * slab
                    for out, start, size in zip(outs, edges, sizes):
                        out[at, y * size : (y + 1) * size] = piece[
                            row : row + slab, start : start + size
                        ]
                used += len(half)

    out = plain_call(
        kernel,
        tuple(shaped((N_Z * n_x * slab, size * len(columns)), bf16) for size in sizes),
        *flat,
        scalars=(places,),
        mebibytes=12,
        name="weave",
    )
    return out if cuts else out[0]


def proj_kernel(count, each, *refs):
    blocks, parts = refs[:count], refs[count : count + count // each]
    tok_ref, par_ref, res_out, low_out = refs[count + count // each :]
    total = tok_ref[...]
    for n, block in enumerate(blocks):
        size = block.shape[1]
        part = parts[n // each][:, n % each * size : (n % each + 1) * size]
        total = total + dot(block[...], part, 1, 1)
    res_out[...] = total
    normed, _, _ = norm_forward(total, par_ref[2:3, :], par_ref[3:4, :])
    low_out[...] = normed.astype(bf16)


ERF_TOP = (
    -2.72614225801306e-10,
    2.77068142495902e-08,
    -2.10102402082508e-06,
    -5.69250639462346e-05,
    -7.34990630326855e-04,
    -2.95459980854025e-03,
    -1.60960333262415e-02,
)
ERF_LOW = (
    -1.45660718464996e-05,
    -2.13374055278905e-04,
    -1.68282697438203e-03,
    -7.37332916720468e-03,
    -1.42647390514189e-02,
)


def erf(value):
    value = jnp.clip(value, -4.0, 4.0)
    square = value * value
    top = jnp.full_like(square, ERF_TOP[0])
    for number in ERF_TOP[1:]:
        top = top * square + number
    low = jnp.full_like(square, ERF_LOW[0])
    for number in ERF_LOW[1:]:
        low = low * square + number
    inverse = pl.reciprocal(low, approx=True)
    inverse = inverse * (2.0 - low * inverse)
    return value * top * inverse


def up_kernel(count, low_ref, *refs):
    outs = refs[-2 * count :]
    for n, part in enumerate(refs[:count]):
        hidden = dot(low_ref[...], part[...], 1, 0)
        share = 0.5 * (1.0 + erf(hidden * 0.7071067811865476))
        outs[2 * n][...] = (hidden * share).astype(bf16)
        slope = share + hidden * jnp.exp(-0.5 * hidden * hidden) * 0.3989422804014327
        outs[2 * n + 1][...] = slope.astype(bf16)


def up_call(low, parts, rows_all, spot, into):
    rows, model = low.shape
    width = parts[0].shape[1]
    cols = pl.BlockSpec((rows, TILE), lambda i, *_: (spot, i))
    return plain_call(
        functools.partial(up_kernel, len(parts)),
        (shaped((rows_all, width), bf16),) * (2 * len(parts)),
        low,
        *parts,
        grid=(width // TILE,),
        in_specs=[fixed(low.shape)] + [pl.BlockSpec((model, TILE), lambda i, *_: (0, i))] * len(parts),
        out_specs=(cols,) * (2 * len(parts)),
        into=into,
        mebibytes=14,
        name="up",
    )


def hidden_kernel(count, low_ref, *refs):
    outs = refs[-count:]
    for n in range(count):
        slope, part = refs[n], refs[count + n]
        outs[n][...] = (dot(low_ref[...], part[...], 1, 0) * slope[...].astype(f32)).astype(bf16)


def hidden_call(low, slopes, parts, spot, into):
    rows, model = low.shape
    width = parts[0].shape[1]
    cols = pl.BlockSpec((rows, TILE), lambda i, *_: (spot, i))
    return plain_call(
        functools.partial(hidden_kernel, len(parts)),
        tuple(shaped(slope.shape, bf16) for slope in slopes),
        low,
        *slopes,
        *parts,
        grid=(width // TILE,),
        in_specs=[fixed(low.shape)]
        + [cols] * len(parts)
        + [pl.BlockSpec((model, TILE), lambda i, *_: (0, i))] * len(parts),
        out_specs=(cols,) * len(parts),
        into=into,
        mebibytes=14,
        name="hidden",
    )


def wide_kernel(count, *refs):
    total = dot(refs[0][...], refs[count][...], 1, 1)
    for n in range(1, count):
        total = total + dot(refs[n][...], refs[count + n][...], 1, 1)
    refs[-1][...] = total.astype(refs[-1].dtype)


def wide_call(values, parts, rows, spot, kind):
    model, width = parts[0].shape
    return plain_call(
        functools.partial(wide_kernel, len(values)),
        shaped((rows, model), kind),
        *values,
        *parts,
        grid=(model // TILE,),
        in_specs=[pl.BlockSpec((rows, width), lambda i, *_: (spot, 0))] * len(values)
        + [pl.BlockSpec((TILE, width), lambda i, *_: (i, 0))] * len(parts),
        out_specs=pl.BlockSpec((rows, TILE), lambda i, *_: (0, i)),
        mebibytes=14,
        name="wide",
    )


def loss_kernel(chunks, each, *refs):
    res_ref, tea_ref, own_ref = refs[:3]
    received = refs[3 : 3 + chunks * each]
    live_ref, count_ref, grad_out, low_out, loss_out, far_ref = refs[3 + chunks * each :]
    add_received(received, each, far_ref)
    error = res_ref[...] - tea_ref[...] + own_ref[...] + far_ref[...]
    weighted = live_ref[...] * error
    grad = 2.0 * weighted / count_ref[...]
    grad_out[...] = grad
    low_out[...] = grad.astype(bf16)
    sums = jnp.sum(weighted * error, axis=0, keepdims=True)
    sums = jnp.concatenate([sums, jnp.zeros((7, sums.shape[1]), f32)], axis=0)
    loss_out[...] = jnp.where(pl.program_id(0) == 0, sums, loss_out[...] + sums)


def add_received(received, each, far_ref):
    for n in range(len(received) // each):

        @pl.when(pl.program_id(0) == n)
        def _():
            total = received[n * each][...].astype(f32)
            for ref in received[n * each + 1 : (n + 1) * each]:
                total = total + ref[...].astype(f32)
            far_ref[...] = total


def beside_call(parts):
    rows, width = parts[0].shape

    def kernel(*refs):
        for n, ref in enumerate(refs[:-1]):
            refs[-1][:, n * width : (n + 1) * width] = ref[...]

    return plain_call(
        kernel, shaped((rows, width * len(parts)), bf16), *parts, mebibytes=8, name="beside"
    )


def spread_kernel(each, tiles, low_ref, *refs):
    count = len(refs) // (1 + each * tiles)
    outs = refs[count:]
    for n in range(count * each):
        size = refs[0].shape[1] // each
        part = refs[n // each][:, n % each * size : (n % each + 1) * size]
        piece = dot(low_ref[...], part, 1, 0).astype(bf16)
        lanes = size // tiles
        for tile in range(tiles):
            outs[tile * count * each + n][...] = piece[:, tile * lanes : (tile + 1) * lanes]


def spread_call(low, parts, each):
    width = parts[0].shape[1] // each
    lanes = min(128, width)
    count = len(parts) * each
    out = plain_call(
        functools.partial(spread_kernel, each, width // lanes),
        tuple(shaped((low.shape[0], lanes), bf16) for _ in range(count * (width // lanes))),
        low,
        *parts,
        mebibytes=12,
        name="spread",
    )
    return [out[n : n + count] for n in range(0, len(out), count)]


def norm_sums(grad, scaled, out_ref, first):
    sums = jnp.concatenate(
        [
            jnp.sum(grad * scaled, axis=0, keepdims=True),
            jnp.sum(grad, axis=0, keepdims=True),
            jnp.zeros((6, grad.shape[1]), f32),
        ],
        axis=0,
    )
    out_ref[...] = jnp.where(first, sums, out_ref[...] + sums)


def middle_kernel(chunks, each, *refs):
    grad_ref, received = refs[0], refs[1 : 1 + chunks * each]
    res_ref, gout_ref, par_ref, full_out, low_out, sum_out, far_ref = refs[1 + chunks * each :]
    add_received(received, each, far_ref)
    _, scaled, inverse = norm_forward(res_ref[...], par_ref[2:3, :], par_ref[3:4, :])
    grad = grad_ref[...] + far_ref[...]
    full = gout_ref[...] + norm_backward(grad, scaled, inverse, par_ref[2:3, :])
    full_out[...] = full
    low_out[...] = full.astype(bf16)
    norm_sums(grad, scaled, sum_out, pl.program_id(0) == 0)


def leave_kernel(count, *refs):
    own_ref, received = refs[0], refs[1 : 1 + count]
    tok_ref, res_ref, par_ref, two_ref, loss_ref, out_ref, sum_out, sum_ref = refs[1 + count :]
    _, scaled, inverse = norm_forward(tok_ref[...], par_ref[0:1, :], par_ref[1:2, :])
    grad = own_ref[...]
    for ref in received:
        grad = grad + ref[...].astype(f32)
    out_ref[...] = res_ref[...] + norm_backward(grad, scaled, inverse, par_ref[0:1, :])
    norm_sums(grad, scaled, sum_ref, pl.program_id(0) == 0)
    sum_out[...] = jnp.concatenate(
        [sum_ref[0:2, :], two_ref[0:2, :], loss_ref[0:1, :], jnp.zeros((3, grad.shape[1]), f32)],
        axis=0,
    )


def split_x(parts, n_x, places):
    model = parts[0][0].shape[0]
    slab = model // (N_Z * n_x)
    total = sum(part[0].shape[1] for part in parts)
    flat = [piece for part in parts for piece in part]

    def kernel(at_ref, *refs):
        outs = refs[len(flat) :]
        for dx in range(n_x):
            x = lax.rem(at_ref[1] + dx, n_x)
            for z in range(N_Z):
                at = block_rows(z * n_x + x, slab)
                lane = 0
                used = 0
                for part in parts:
                    value = refs[used][at, :]
                    size = value.shape[1]
                    if len(part) > 1:
                        value = value.astype(f32)
                        for ref in refs[used + 1 : used + len(part)]:
                            value = value + ref[at, :].astype(f32)
                        value = value.astype(bf16)
                    outs[dx][z * slab : (z + 1) * slab, lane : lane + size] = value
                    lane += size
                    used += len(part)

    return plain_call(
        kernel,
        tuple(shaped((model // n_x, total), bf16) for _ in range(n_x)),
        *flat,
        scalars=(places,),
        mebibytes=12,
        name="split_x",
    )


def split_z(parts, places):
    rows, width = parts[0].shape
    slab = rows // N_Z

    def kernel(at_ref, *refs):
        for k, out in enumerate(refs[len(parts) :]):
            at = block_rows(lax.rem(at_ref[0] + k, N_Z), slab)
            total = refs[0][at, :].astype(f32)
            for ref in refs[1 : len(parts)]:
                total = total + ref[at, :].astype(f32)
            out[...] = total.astype(out.dtype)

    shapes = (shaped((slab, width), f32),) + (shaped((slab, width), bf16),) * (N_Z - 1)
    return plain_call(kernel, shapes, *parts, scalars=(places,), mebibytes=8, name="split_z")


def adam_kernel(layout, counts, *refs):
    grads = []
    for count in counts:
        grad = refs[0][...].astype(f32)
        for ref in refs[1:count]:
            grad = grad + ref[...].astype(f32)
        grads.append(grad)
        refs = refs[count:]
    count = len(layout)
    states, outs = refs[: 3 * count], refs[3 * count :]
    for n, (source, start, size, turned) in enumerate(layout):
        weight, first, second = states[3 * n : 3 * n + 3]
        if len(weight.shape) == 3:
            matrices = weight.shape[0]
            lanes = size // matrices
            for k in range(matrices):
                own = [
                    grads[at][:, lane + k * lanes : lane + (k + 1) * lanes] for at, lane in start
                ]
                own = own[0] if len(own) == 1 else jnp.concatenate(own, axis=1)
                new = adam_step(weight[k], own, first[k], second[k], weight_decay, learn_rate)
                for out, value in zip(outs[3 * n : 3 * n + 3], new):
                    out[k] = value
        else:
            part = grads[source][:, start : start + size]
            if turned:
                part = part.T
            new = adam_step(weight[...], part, first[...], second[...], weight_decay, learn_rate)
            for out, value in zip(outs[3 * n : 3 * n + 3], new):
                out[...] = value


def adam_call(groups, layout, *states):
    shapes = tuple(shaped(s.shape, f32) for s in states)
    out = plain_call(
        functools.partial(adam_kernel, layout, [len(group) for group in groups]),
        shapes,
        *[piece for group in groups for piece in group],
        *states,
        mebibytes=16,
        name="adam",
    )
    return [out[3 * n : 3 * n + 3] for n in range(len(layout))]


def tie(*values):
    return lax.optimization_barrier(values)


def local(
    n_x,
    n_y,
    tokens,
    teacher,
    segments,
    live_mask,
    weight_qkv,
    weight_proj,
    weight_up,
    weight_down,
    norm_params,
    first_qkv,
    first_proj,
    first_up,
    first_down,
    first_norms,
    second_qkv,
    second_proj,
    second_up,
    second_down,
    second_norms,
):
    z_at, x_at = lax.axis_index("z"), lax.axis_index("x")
    y_at, core_at = lax.axis_index("y"), lax.axis_index("core")
    rows, model = tokens.shape
    group_rows = segments.shape[0]
    slab = weight_qkv.shape[1]
    width = weight_qkv.shape[2]
    unit = weight_up.shape[1]
    part_rows = min(128, rows)
    wide_rows = min(256, rows)
    depth = N_Z * slab
    sizes = {"z": N_Z, "x": n_x, "y": n_y, "core": N_CORE}
    places = jnp.stack([z_at, x_at]).astype(jnp.int32)
    offsets = [(dc, dy) for dc in range(N_CORE) for dy in range(n_y)]
    other = N_CORE - 1

    def send(value, axis, step):
        size = sizes[axis]
        return lax.ppermute(value, axis, [(i, (i + step) % size) for i in range(size)])

    def send_col(value, dy, dc):
        perm = [
            (y * N_CORE + c, (y + dy) % n_y * N_CORE + (c + dc) % N_CORE)
            for y in range(n_y)
            for c in range(N_CORE)
        ]
        return lax.ppermute(value, ("y", "core"), perm)

    def fetch(value, axis):
        return [value] + [send(value, axis, -k) for k in range(1, sizes[axis])]

    def fetch_z(value):
        return [value] + [send(value, "z", k) for k in range(1, N_Z)]

    def place(dy, dc):
        return ((y_at + dy) % n_y * N_CORE + (core_at + dc) % N_CORE) * rows

    shard_qkv, shard_up, shard_down = plain_call(
        pack_kernel,
        (
            shaped((slab, 4 * width), bf16),
            shaped((slab + DIGITS, unit), bf16),
            shaped((slab, unit), bf16),
        ),
        live_mask.reshape(-1, 128),
        weight_qkv,
        weight_proj,
        weight_up,
        weight_down,
        mebibytes=8,
        name="pack",
    )
    near_qkv = fetch_z(shard_qkv)
    low_one = plain_call(
        first_kernel,
        shaped(tokens.shape, bf16),
        tokens,
        norm_params,
        grid=(rows // part_rows,),
        in_specs=row_blocks(part_rows, model) + [fixed(norm_params.shape)],
        out_specs=row_blocks(part_rows, model)[0],
        mebibytes=8,
        name="first",
    )
    blocks_one = fetch(low_one, "y") + [send(low_one, "core", -1)]
    near_qkv, shard_down, shard_up, blocks_one[n_y] = tie(
        near_qkv, shard_down, shard_up, blocks_one[n_y]
    )

    beside_qkv = fetch(stack_z(near_qkv, slab, places), "x")
    blocks_one, shard_up = tie(blocks_one, shard_up)
    near_up = fetch_z(shard_up)
    blocks_one = blocks_one + [send(block, "core", -1) for block in blocks_one[1:n_y]]
    spots_here = jnp.stack([place(dy, dc) for dc, dy in offsets]).astype(jnp.int32)
    spots = jnp.stack([place(-dy, -dc) for dc, dy in offsets]).astype(jnp.int32)
    group_one = place_blocks(blocks_one, spots_here)
    geometry = attend_geometry(segments, live_mask)
    own_live = lax.dynamic_slice_in_dim(
        live_mask, (y_at * N_CORE + core_at) * rows, rows, 0
    ).astype(f32)[:, None]
    beside_qkv, near_up, group_one, geometry, own_live, shard_down, spots = tie(
        beside_qkv, near_up, group_one, geometry, own_live, shard_down, spots
    )

    block_up = stack_z(near_up, slab, places)
    full_qkv, part_proj = weave([[[part] for part in beside_qkv]], [3 * width], slab, places)
    block_up, part_proj = tie(block_up, part_proj)
    beside_up = fetch(block_up, "x")
    near_down = fetch_z(shard_down)
    full_proj = fetch(part_proj, "y")
    projected = dot(group_one, full_qkv, 1, 0).astype(bf16)
    mixed, bias = attend_forward(projected, geometry, spots, rows)
    mixed, beside_up, near_down, full_proj = tie(mixed, beside_up, near_down, full_proj)

    blocks_mixed = [
        piece if key == (0, 0) else send_col(piece, -key[1], -key[0])
        for key, piece in zip(offsets, mixed)
    ]
    full_proj = [beside_call(full_proj)]
    full_proj.append(send(full_proj[0], "core", -1))
    blocks_down = stack_z(near_down, slab, places, 2)
    beside_down = [fetch(blocks_down[0], "x")]
    full_up = [weave([[[part] for part in beside_up]], [], slab, places)]
    live_count = sum(
        256.0 * part[depth, 0].astype(f32) + 16.0 * part[depth + 1, 0].astype(f32)
        + part[depth + 2, 0].astype(f32)
        for part in beside_up
    ).reshape(1, 1)
    blocks_mixed, full_proj, full_up, live_count, beside_down, blocks_down = tie(
        blocks_mixed, full_proj, full_up, live_count, beside_down, blocks_down
    )
    beside_down.append(fetch(blocks_down[1], "x"))
    full_up.append(send(full_up[0], "core", -1))
    count = len(offsets)
    residual, low_two = plain_call(
        functools.partial(proj_kernel, count, n_y),
        (shaped(tokens.shape, f32), shaped(tokens.shape, bf16)),
        *blocks_mixed,
        *full_proj,
        tokens,
        norm_params,
        grid=(rows // wide_rows,),
        in_specs=row_blocks(wide_rows, *([width] * count))
        + [fixed(part.shape) for part in full_proj]
        + row_blocks(wide_rows, model)
        + [fixed(norm_params.shape)],
        out_specs=tuple(row_blocks(wide_rows, model, model)),
        mebibytes=18,
        name="proj",
    )
    low_two, full_up = tie(low_two, full_up)

    chunk = min(256, rows)
    chunks = range(rows // chunk)
    neighbours = range(1, n_y)
    rows_all = n_y * rows

    def cross(value, n, back):
        piece = value[n * chunk : (n + 1) * chunk]
        return {dy: send(piece, "y", dy if back else -dy) for dy in neighbours}

    def spot_of(dy, n):
        return (dy * rows) // chunk + n

    low_far = {0: cross(low_two, 0, False)}
    hidden = up_call(low_two, full_up, rows_all, 0, ())
    low_far[0], hidden, low_two, beside_down = tie(low_far[0], hidden, low_two, beside_down)
    full_down = [weave([list(zip(*beside_down))], [], slab, places)]
    full_down.append(send(full_down[0], "core", -1))
    far_out = {}
    for n in chunks:
        if n + 1 in chunks:
            low_far[n + 1] = cross(low_two, n + 1, False)
        for dy in neighbours:
            hidden = up_call(low_far[n][dy], full_up, rows_all, spot_of(dy, n), hidden)
        outs = {
            dy: wide_call(hidden[::2], full_down, chunk, spot_of(dy, n), bf16) for dy in neighbours
        }
        if n + 1 in chunks:
            outs, hidden, low_far[n + 1] = tie(outs, hidden, low_far[n + 1])
        else:
            outs, hidden = tie(outs, hidden)
        if n:
            far_out[n - 1] = tie(far_out[n - 1], outs)[0]
        far_out[n] = {dy: send(outs[dy], "y", -dy) for dy in neighbours}
    own_out = wide_call(hidden[::2], full_down, rows, 0, f32)
    own_out, far_out = tie(own_out, far_out)
    far_out = [far_out[n][dy] for n in chunks for dy in neighbours]
    each = len(neighbours)
    grad_output, grad_branch, loss_rows = plain_call(
        functools.partial(loss_kernel, len(chunks), each),
        (shaped(tokens.shape, f32), shaped(tokens.shape, bf16), shaped((8, model), f32)),
        residual,
        teacher,
        own_out,
        *far_out,
        own_live,
        live_count,
        grid=(len(chunks),),
        in_specs=row_blocks(chunk, model, model, model)
        + [fixed((chunk, model))] * len(far_out)
        + row_blocks(chunk, 1)
        + [fixed((1, 1))],
        out_specs=tuple(row_blocks(chunk, model, model) + [fixed((8, model))]),
        scratch=[pltpu.VMEM((chunk, model), f32)],
        mebibytes=20,
        name="loss",
    )
    active, slope = hidden[::2], hidden[1::2]

    grad_far = {0: cross(grad_branch, 0, False)}
    grad_hidden = hidden_call(grad_branch, slope, full_down, 0, ())
    own_two = wide_call(grad_hidden, full_up, rows, 0, f32)
    grad_far[0], grad_hidden, own_two, grad_branch = tie(
        grad_far[0], grad_hidden, own_two, grad_branch
    )
    def gather_rows(own, far):
        return jnp.concatenate([own] + [far[n][dy] for dy in neighbours for n in chunks], axis=0)

    far_two = {}
    for n in chunks:
        if n + 1 in chunks:
            grad_far[n + 1] = cross(grad_branch, n + 1, False)
        for dy in neighbours:
            grad_hidden = hidden_call(
                grad_far[n][dy], slope, full_down, spot_of(dy, n), grad_hidden
            )
        outs = {
            dy: wide_call(grad_hidden, full_up, chunk, spot_of(dy, n), bf16) for dy in neighbours
        }
        if n + 1 in chunks:
            outs, grad_hidden, grad_far[n + 1] = tie(outs, grad_hidden, grad_far[n + 1])
        else:
            grad_all = gather_rows(grad_branch, grad_far)
            far_down = dot(grad_all, active[other], 0, 0).astype(bf16)
            outs, grad_hidden, grad_all, far_down, far_two = tie(
                outs, grad_hidden, grad_all, far_down, far_two
            )
        far_two[n] = {dy: send(outs[dy], "y", -dy) for dy in neighbours}

    low_all = gather_rows(low_two, low_far)
    far_up = dot(low_all, grad_hidden[other], 0, 0).astype(bf16)
    sent_down, sent_up = send(far_down, "core", 1), send(far_up, "core", 1)
    hold_down = (dot(grad_all, active[0], 0, 0) + sent_down.astype(f32)).astype(bf16)
    halves_down = split_x([[hold_down]], n_x, places)
    hold_up = (dot(low_all, grad_hidden[0], 0, 0) + sent_up.astype(f32)).astype(bf16)
    halves_up = split_x([[hold_up]], n_x, places)
    far_two, halves_down, halves_up = tie(far_two, halves_down, halves_up)
    far_two = [far_two[n][dy] for n in chunks for dy in neighbours]
    grad_residual, grad_low, sums_two = plain_call(
        functools.partial(middle_kernel, len(chunks), each),
        (shaped(tokens.shape, f32), shaped(tokens.shape, bf16), shaped((8, model), f32)),
        own_two,
        *far_two,
        residual,
        grad_output,
        norm_params,
        grid=(len(chunks),),
        in_specs=row_blocks(chunk, model)
        + [fixed((chunk, model))] * len(far_two)
        + row_blocks(chunk, model, model)
        + [fixed(norm_params.shape)],
        out_specs=tuple(row_blocks(chunk, model, model) + [fixed((8, model))]),
        scratch=[pltpu.VMEM((chunk, model), f32)],
        mebibytes=20,
        name="middle",
    )
    pieces_attn = spread_call(grad_low, full_proj, n_y)
    pieces_attn, halves_down, halves_up, grad_low = tie(
        pieces_attn, halves_down, halves_up, grad_low
    )

    def send_back(pieces):
        return [
            piece if key == (0, 0) else send_col(piece, key[1], key[0])
            for key, piece in zip(offsets, pieces)
        ]

    def hop_x(halves):
        return [halves[0]] + [send(halves[dx], "x", dx) for dx in range(1, n_x)]

    def spread_z(pieces):
        return [pieces[0]] + [send(pieces[k], "z", k) for k in range(1, N_Z)]

    lanes = 3 * min(128, width)
    tiles = 3 * width // lanes
    sent_attn = send_back(pieces_attn[0])
    parts_down = hop_x(halves_down)
    grad_proj = [dot(grad_low, block, 0, 0).astype(bf16) for block in blocks_mixed]
    far_proj = jnp.concatenate(grad_proj[n_y:], axis=1)
    sent_attn, far_proj, grad_proj = tie(sent_attn, far_proj, grad_proj)

    sent_later = [send_back(pieces) for pieces in pieces_attn[1:]]
    sent_proj = send(far_proj, "core", 1)
    grad_projected = attend_backward(projected, sent_attn, spots, geometry[0], bias, 0, ())
    grad_projected, sent_later, sent_proj, parts_down, halves_up = tie(
        grad_projected, sent_later, sent_proj, parts_down, halves_up
    )

    hold_proj = [
        (
            grad_proj[dy].astype(f32) + sent_proj[:, dy * width : (dy + 1) * width].astype(f32)
        ).astype(bf16)
        for dy in range(n_y)
    ]
    pieces_down = split_z(parts_down, places)
    grad_projected, pieces_down, hold_proj, halves_up = tie(
        grad_projected, pieces_down, hold_proj, halves_up
    )
    parts_up = hop_x(halves_up)
    last_down = spread_z(pieces_down)
    part_proj = [hold_proj[0]] + [send(hold_proj[k], "y", k) for k in range(1, n_y)]
    for tile in range(1, tiles):
        grad_projected = attend_backward(
            projected, sent_later[tile - 1], spots, geometry[0], bias, tile, (grad_projected,)
        )
    grad_projected, parts_up, last_down, part_proj = tie(
        grad_projected, parts_up, last_down, part_proj
    )

    parts = {
        key: dot(
            lax.dynamic_slice_in_dim(grad_projected, place(key[1], key[0]), rows, 0),
            full_qkv,
            1,
            1,
        )
        for key in reversed(offsets)
    }
    far_one = jnp.concatenate([parts[other, dy].astype(bf16) for dy in range(n_y)], axis=0)
    far_one, grad_projected = tie(far_one, grad_projected)
    sent_one = send(far_one, "core", 1)
    grad_qkv = dot(group_one, grad_projected, 0, 0).astype(bf16)
    halves_qkv = split_x([[grad_qkv], part_proj], n_x, places)
    pieces_up = split_z(parts_up, places)
    halves_qkv, sent_one, parts, pieces_up = tie(halves_qkv, sent_one, parts, pieces_up)

    parts = [
        parts[0, dy] + sent_one[dy * rows : (dy + 1) * rows].astype(f32) for dy in range(n_y)
    ]
    sent_parts = [parts[k].astype(bf16) for k in range(1, n_y)]
    halves_qkv, sent_parts, pieces_up = tie(halves_qkv, sent_parts, pieces_up)
    received = [send(part, "y", k) for k, part in enumerate(sent_parts, 1)]
    parts_qkv = hop_x(halves_qkv)
    last_up = spread_z(pieces_up)
    (new_down,) = adam_call(
        [last_down], [(0, 0, unit, True)], weight_down, first_down, second_down
    )
    parts_qkv, received, last_up, new_down = tie(parts_qkv, received, last_up, new_down)

    pieces_qkv = split_z(parts_qkv, places)
    pieces_qkv, received = tie(pieces_qkv, received)
    last_qkv = spread_z(pieces_qkv)
    token_grad, sums = plain_call(
        functools.partial(leave_kernel, len(received)),
        (shaped(tokens.shape, f32), shaped((8, model), f32)),
        parts[0],
        *received,
        tokens,
        grad_residual,
        norm_params,
        sums_two,
        loss_rows,
        grid=(rows // part_rows,),
        in_specs=row_blocks(part_rows, *([model] * (3 + len(received))))
        + [fixed(norm_params.shape), fixed((8, model)), fixed((8, model))],
        out_specs=tuple(row_blocks(part_rows, model) + [fixed((8, model))]),
        scratch=[pltpu.VMEM((8, model), f32)],
        mebibytes=14,
        name="leave",
    )
    for axis in ("core", "y", "x", "z"):
        step = 1
        while step < sizes[axis]:
            pairs = [(i, i ^ step) for i in range(sizes[axis])]
            sums = sums + lax.ppermute(sums, axis, pairs)
            step *= 2
    (new_up,) = adam_call([last_up], [(0, 0, unit, False)], weight_up, first_up, second_up)
    sums, last_qkv, new_up = tie(sums, last_qkv, new_up)
    loss_sum = jnp.sum(sums[4])
    live_count = live_count[0, 0]

    new_qkv, new_proj = adam_call(
        [last_qkv],
        [(0, [(0, n * lanes) for n in range(tiles)], lanes, False), (0, 3 * width, width, True)],
        weight_qkv,
        first_qkv,
        second_qkv,
        weight_proj,
        first_proj,
        second_proj,
    )
    new_norms = adam_step(norm_params, sums[:4], first_norms, second_norms, 0.0, norm_rate)
    return (
        loss_sum / live_count,
        token_grad,
        new_qkv[0],
        new_proj[0],
        new_up[0],
        new_down[0],
        new_norms[0],
        new_qkv[1],
        new_proj[1],
        new_up[1],
        new_down[1],
        new_norms[1],
        new_qkv[2],
        new_proj[2],
        new_up[2],
        new_down[2],
        new_norms[2],
    )


def solution(mesh):
    n_x = mesh.shape["row"] // N_Z
    n_y = mesh.shape["col"] // N_CORE
    mesh = jax.sharding.Mesh(
        mesh.devices.reshape(N_Z, n_x, n_y, N_CORE), ("z", "x", "y", "core")
    )
    row, col = ("z", "x"), ("y", "core")
    matrices = (P(None, row, col), P(col, row), P(row, col), P(col, row), P())
    tokens = P(row + col, None)
    return jax.shard_map(
        functools.partial(local, n_x, n_y),
        mesh=mesh,
        in_specs=(tokens, tokens, P(row), P(row)) + matrices * 3,
        out_specs=(P(), tokens) + matrices * 3,
        check_vma=False,
    )
```

```python
import functools

import jax
import jax.numpy as jnp
from jax import lax
from jax.experimental import pallas as pl
from jax.experimental.pallas import tpu as pltpu
from jax.sharding import PartitionSpec as P

HEAD_DIM = 64
PATCHES = 577
STEP = 10
WINDOW = 640
QROWS = 320
TILE = 256
DIGITS = 16
SMALL = pl.CostEstimate(flops=1024, bytes_accessed=1024, transcendentals=0)
N_Z = 4
N_CORE = 2

layer_eps = 1e-06
adam_eps = 1e-08
learn_rate = 0.03
norm_rate = 0.25
moment_decay = 0.5
weight_decay = 0.05

bf16 = jnp.bfloat16
f32 = jnp.float32


def norm_forward(values, gain_row, bias_row):
    average = jnp.mean(values, axis=-1, keepdims=True)
    centred = values - average
    variance = jnp.mean(centred * centred, axis=-1, keepdims=True)
    inverse = lax.rsqrt(variance + layer_eps)
    scaled = centred * inverse
    return (scaled * gain_row + bias_row, scaled, inverse)


def norm_backward(upstream, scaled, inverse, gain_row):
    weighted = upstream * gain_row
    return inverse * (
        weighted
        - jnp.mean(weighted, axis=-1, keepdims=True)
        - scaled * jnp.mean(weighted * scaled, axis=-1, keepdims=True)
    )


def gelu_slope(hidden):
    return (
        0.5 * (1.0 + lax.erf(hidden * 0.7071067811865476))
        + hidden * jnp.exp(-0.5 * hidden * hidden) * 0.3989422804014327
    )


def adam_step(weight, gradient, momentum, variance, decay_rate, rate):
    momentum = moment_decay * momentum + (1.0 - moment_decay) * gradient
    variance = moment_decay * variance + (1.0 - moment_decay) * gradient * gradient
    correction = 1.0 - moment_decay**STEP
    direction = momentum / correction / (jnp.sqrt(variance / correction) + adam_eps)
    return (weight - rate * (direction + decay_rate * weight), momentum, variance)


def dot(left, right, left_dim, right_dim):
    return lax.dot_general(
        left, right, (((left_dim,), (right_dim,)), ((), ())), preferred_element_type=f32
    )


def head_lanes(width, head):
    lanes = lax.broadcasted_iota(jnp.int32, (1, width), 1)
    return (lanes >= head * HEAD_DIM) & (lanes < (head + 1) * HEAD_DIM)


def attend_scores(q_part, k_all, mask):
    scores = dot(q_part, k_all, 1, 1) + mask
    weights = jnp.exp(scores - jnp.max(scores, axis=-1, keepdims=True))
    return weights, jnp.sum(weights, axis=-1, keepdims=True)


def image_window(begin, group_rows):
    image = pl.program_id(0)
    start = jnp.minimum(begin[image] // 16 * 16, group_rows - WINDOW)
    first = begin[image] - start
    return image, pl.multiple_of(start, 16), first


def fill_mask(bias, mask_ref):
    for row in range(0, WINDOW, 128):
        rows = row + lax.broadcasted_iota(jnp.int32, (128, WINDOW), 0)
        cols = lax.broadcasted_iota(jnp.int32, (128, WINDOW), 1)
        mask_ref[row : row + 128, :] = jnp.where(rows == cols, 0.0, bias)


def rows_inside(rows, row_start, first):
    ids = row_start + lax.broadcasted_iota(jnp.int32, (rows, 1), 0)
    return (ids >= first) & (ids < first + PATCHES)


def attend_forward_kernel(blocks, begin, spots, code_ref, *refs):
    bias_out, out_ref, mask_ref = refs[-3:]
    image, start, first = image_window(begin, refs[0].shape[0])
    code = code_ref[pl.ds(start, WINDOW), :]
    bias = jnp.where(code == image, 0.0, -1e30).astype(f32).T
    bias_out[0] = bias[0:8, :]
    fill_mask(bias[0:1, :], mask_ref)
    lanes = refs[0].shape[1]

    for tile in range((len(refs) - 3 - blocks) // 3):
        q_ref, k_ref, v_ref = refs[3 * tile : 3 * tile + 3]
        cols = slice(tile * lanes, (tile + 1) * lanes)

        @pl.when(image == 0)
        def _():
            out_ref[:, cols] = v_ref[...]

        k_all = k_ref[pl.ds(start, WINDOW), :]
        v_all = v_ref[pl.ds(start, WINDOW), :]
        for row in range(0, WINDOW, QROWS):
            at = pl.ds(pl.multiple_of(start + row, 16), QROWS)
            q_part = q_ref[at, :] * jnp.asarray(HEAD_DIM ** (-0.5), bf16)
            inside = rows_inside(QROWS, row, first)
            mixed = None
            for head in range(lanes // HEAD_DIM):
                mine = head_lanes(lanes, head)
                q_head = jnp.where(mine, q_part, jnp.zeros_like(q_part))
                weights, totals = attend_scores(q_head, k_all, mask_ref[row : row + QROWS, :])
                part = dot(weights.astype(bf16), v_all, 1, 0) * (1.0 / totals)
                mixed = part if mixed is None else jnp.where(mine, part, mixed)
            out_ref[at, cols] = jnp.where(inside, mixed.astype(bf16), out_ref[at, cols])

    @pl.when(image == pl.num_programs(0) - 1)
    def _():
        for n, block in enumerate(refs[-3 - blocks : -3]):
            rows = block.shape[0]
            block[...] = out_ref[pl.ds(pl.multiple_of(spots[n], rows), rows), :]


def attend_backward_kernel(blocks, begin, spots, bias_ref, *refs):
    out_ref, p_ref, s_ref, go_ref, mask_ref = refs[-5:]
    go_blocks, refs = refs[3 : 3 + blocks], refs[:3]
    image, start, first = image_window(begin, refs[0].shape[0])
    fill_mask(bias_ref[0, 0:1, :], mask_ref)
    lanes = refs[0].shape[1]
    rows = go_blocks[0].shape[0]
    whole = pl.ds(start, WINDOW)
    inside_all = rows_inside(WINDOW, 0, first)

    @pl.when(image == 0)
    def _():
        for n, block_ref in enumerate(go_blocks):
            go_ref[pl.ds(pl.multiple_of(spots[n], rows), rows), :] = block_ref[...]

    for tile in range(len(refs) // 3):
        q_ref, k_ref, v_ref = refs[3 * tile : 3 * tile + 3]
        cols = slice(tile * lanes, (tile + 1) * lanes)
        base = 3 * tile * lanes
        q_cols, k_cols, v_cols = [
            slice(base + n * lanes, base + (n + 1) * lanes) for n in range(3)
        ]

        @pl.when(image == 0)
        def _():
            out_ref[:, base : base + 2 * lanes] = jnp.zeros((out_ref.shape[0], 2 * lanes), bf16)
            out_ref[:, v_cols] = go_ref[:, cols]

        k_all = k_ref[whole, :]
        v_all = v_ref[whole, :]
        q_all = q_ref[whole, :] * jnp.asarray(HEAD_DIM ** (-0.5), bf16)
        go_all = go_ref[whole, cols]
        key_grad = None
        value_grad = None
        for head in range(lanes // HEAD_DIM):
            mine = head_lanes(lanes, head)
            q_mine = jnp.where(mine, q_all, jnp.zeros_like(q_all))
            go_mine = jnp.where(mine, go_all, jnp.zeros_like(go_all))
            for row in range(0, WINDOW, QROWS):
                part = slice(row, row + QROWS)
                at = pl.ds(pl.multiple_of(start + row, 16), QROWS)
                inside = rows_inside(QROWS, row, first)
                weights, totals = attend_scores(q_mine[part], k_all, mask_ref[part, :])
                weights = weights * jnp.where(inside, 1.0 / totals, 0.0)
                weight_grad = dot(go_mine[part], v_all, 1, 1)
                product = weights * weight_grad
                score_grad = (
                    product - weights * jnp.sum(product, axis=-1, keepdims=True)
                ).astype(bf16)
                p_ref[part, :] = weights.astype(bf16)
                s_ref[part, :] = score_grad
                query_grad = (dot(score_grad, k_all, 1, 0) * HEAD_DIM ** (-0.5)).astype(bf16)
                out_ref[at, q_cols] = jnp.where(inside & mine, query_grad, out_ref[at, q_cols])
            key_part = dot(q_mine, s_ref[...], 0, 0)
            value_part = dot(go_mine, p_ref[...], 0, 0)
            key_grad = key_part if key_grad is None else key_grad + key_part
            value_grad = value_part if value_grad is None else value_grad + value_part
        key_rows = key_grad.T.astype(bf16)
        value_rows = value_grad.T.astype(bf16)
        out_ref[whole, k_cols] = jnp.where(inside_all, key_rows, out_ref[whole, k_cols])
        out_ref[whole, v_cols] = jnp.where(inside_all, value_rows, out_ref[whole, v_cols])


def qkv_operands(projected, tile):
    group_rows, total = projected.shape
    lanes = min(128, total // 3)
    if lanes % 128 == 0:
        specs = [
            pl.BlockSpec((group_rows, lanes), functools.partial(lambda n, i, *_: (0, n), 3 * tile + n))
            for n in range(3)
        ]
        return [projected] * 3, specs
    parts = [projected[:, n * lanes : (n + 1) * lanes] for n in range(3)]
    return parts, [fixed((group_rows, lanes))] * 3


def all_operands(projected):
    width = projected.shape[1] // 3
    operands, specs = [], []
    for tile in range(width // min(128, width)):
        more, places = qkv_operands(projected, tile)
        operands += more
        specs += places
    return operands, specs


def attend_forward(projected, geometry, spots, rows):
    begin, code = geometry
    group_rows, total = projected.shape
    width = total // 3
    blocks = group_rows // rows
    images = begin.shape[0]
    operands, specs = all_operands(projected)
    out = plain_call(
        functools.partial(attend_forward_kernel, blocks),
        (shaped((rows, width), bf16),) * blocks + (shaped((images, 8, WINDOW), f32),),
        code,
        *operands,
        grid=begin.shape,
        in_specs=[fixed(code.shape)] + specs,
        out_specs=(fixed((rows, width)),) * blocks
        + (pl.BlockSpec((1, 8, WINDOW), lambda i, *_: (i, 0, 0)),),
        scratch=[pltpu.VMEM((group_rows, width), bf16), pltpu.VMEM((WINDOW, WINDOW), f32)],
        scalars=(begin, spots),
        mebibytes=20,
        name="attention_forward",
    )
    return out[:blocks], out[blocks]


def attend_backward(projected, go_blocks, spots, begin, bias, tile, into):
    group_rows, total = projected.shape
    lanes = min(128, total // 3)
    operands, specs = qkv_operands(projected, tile)
    return plain_call(
        functools.partial(attend_backward_kernel, len(go_blocks)),
        shaped((group_rows, total), bf16),
        bias,
        *operands,
        *go_blocks,
        grid=begin.shape,
        in_specs=[pl.BlockSpec((1, 8, WINDOW), lambda i, *_: (i, 0, 0))]
        + specs
        + [fixed(block.shape) for block in go_blocks],
        out_specs=pl.BlockSpec((group_rows, 3 * lanes), lambda i, *_: (0, tile)),
        scratch=[pltpu.VMEM((WINDOW, WINDOW), bf16)] * 2
        + [pltpu.VMEM((group_rows, lanes), bf16), pltpu.VMEM((WINDOW, WINDOW), f32)],
        scalars=(begin, spots),
        into=into,
        mebibytes=16,
        name="attention_backward",
    )


def attend_geometry(segments, live_mask):
    group_rows = segments.shape[0]
    numbers = jnp.arange(group_rows // PATCHES, dtype=jnp.int32)
    positions = jnp.arange(group_rows, dtype=jnp.int32)
    begin = jnp.min(
        jnp.where(segments[None, :] == numbers[:, None], positions[None, :], group_rows - PATCHES),
        axis=1,
    )
    code = jnp.where(live_mask == 1, segments, -1)
    return begin, jnp.broadcast_to(code[:, None], (group_rows, 128))


def plain_call(kernel, out_shape, *operands, grid=(), in_specs=None, out_specs=None, scratch=(), scalars=(), into=(), mebibytes=16, name=None):
    params = pltpu.CompilerParams(vmem_limit_bytes=mebibytes * 1024 * 1024)
    if in_specs is None:
        in_specs = [pl.BlockSpec(a.shape, functools.partial(lambda n, *_: (0,) * n, a.ndim)) for a in operands]
    in_specs = list(in_specs) + [pl.BlockSpec(memory_space=pl.ANY)] * len(into)
    if out_specs is None:
        out_specs = jax.tree.map(
            lambda s: pl.BlockSpec(s.shape, functools.partial(lambda n, *_: (0,) * n, len(s.shape))), out_shape
        )
    return pl.pallas_call(
        kernel,
        grid_spec=pltpu.PrefetchScalarGridSpec(
            num_scalar_prefetch=len(scalars),
            grid=grid,
            in_specs=in_specs,
            out_specs=out_specs,
            scratch_shapes=list(scratch),
        ),
        out_shape=out_shape,
        input_output_aliases={len(scalars) + len(operands) + n: n for n in range(len(into))},
        compiler_params=params,
        cost_estimate=SMALL,
        name=name,
    )(*scalars, *operands, *into)


def shaped(shape, dtype):
    return jax.ShapeDtypeStruct(tuple(shape), dtype)


def row_blocks(rows, *widths):
    return [pl.BlockSpec((rows, w), lambda i, *_: (i, 0)) for w in widths]


def fixed(shape):
    return pl.BlockSpec(tuple(shape), functools.partial(lambda n, *_: (0,) * n, len(shape)))


def pack_kernel(live_ref, qkv_ref, proj_ref, up_ref, down_ref, qkv_out, up_out, down_out):
    count, slab, width = qkv_ref.shape
    lanes = min(128, width)
    for n in range(count):
        for t in range(width // lanes):
            at = (count * t + n) * lanes
            qkv_out[:, at : at + lanes] = qkv_ref[n][:, t * lanes : (t + 1) * lanes].astype(bf16)
    qkv_out[:, count * width :] = proj_ref[...].T.astype(bf16)
    up_out[:slab, :] = up_ref[...].astype(bf16)
    live = jnp.sum(jnp.sum(live_ref[...].astype(f32), axis=0, keepdims=True), axis=1, keepdims=True)
    high = jnp.floor(live * (1.0 / 256.0))
    middle = jnp.floor(live * (1.0 / 16.0)) - 16.0 * high
    low = live - 256.0 * high - 16.0 * middle
    row = lax.broadcasted_iota(jnp.int32, (DIGITS, up_out.shape[1]), 0)
    digits = jnp.where(row == 0, high, jnp.where(row == 1, middle, jnp.where(row == 2, low, 0.0)))
    up_out[slab:, :] = digits.astype(bf16)
    down_out[...] = down_ref[...].T.astype(bf16)


def first_kernel(tok_ref, par_ref, low_out):
    normed, _, _ = norm_forward(tok_ref[...], par_ref[0:1, :], par_ref[1:2, :])
    low_out[...] = normed.astype(bf16)


def place_blocks(blocks, spots):
    rows, width = blocks[0].shape

    def kernel(spot_ref, *refs):
        for n, ref in enumerate(refs[:-1]):
            refs[-1][pl.ds(pl.multiple_of(spot_ref[n], rows), rows), :] = ref[...]

    return plain_call(
        kernel,
        shaped((rows * len(blocks), width), bf16),
        *blocks,
        scalars=(spots,),
        mebibytes=20,
        name="place_blocks",
    )


def block_rows(block, slab):
    return pl.ds(pl.multiple_of(block * slab, slab), slab)


def stack_z(pieces, slab, places, count=1):
    height, width = pieces[0].shape
    extra = height - slab
    shapes = (shaped((N_Z * slab // count + extra, width), bf16),) * count

    def kernel(at_ref, *refs):
        held = refs[-1]
        for k, ref in enumerate(refs[:N_Z]):
            held[block_rows(lax.rem(at_ref[0] + N_Z - k, N_Z), slab), :] = ref[:slab, :]
        for n, out in enumerate(refs[N_Z:-1]):
            rows = N_Z * slab // count
            out[:rows, :] = held[n * rows : (n + 1) * rows, :]
            if extra:
                digits = refs[0][slab:, :].astype(f32)
                for ref in refs[1:N_Z]:
                    digits = digits + ref[slab:, :].astype(f32)
                out[rows:, :] = digits.astype(bf16)

    out = plain_call(
        kernel,
        shapes,
        *pieces,
        scalars=(places,),
        scratch=[pltpu.VMEM((N_Z * slab, width), bf16)],
        mebibytes=8,
        name="stack_z",
    )
    return out if count > 1 else out[0]


def weave(columns, cuts, slab, places):
    n_x = len(columns[0])
    width = columns[0][0][0].shape[1]
    flat = [piece for column in columns for half in column for piece in half]
    edges = [0, *cuts, width]
    sizes = [stop - start for start, stop in zip(edges[:-1], edges[1:])]

    def kernel(at_ref, *refs):
        outs = refs[len(flat) :]
        used = 0
        for y, column in enumerate(columns):
            for dx, half in enumerate(column):
                x = lax.rem(at_ref[1] + dx, n_x)
                share = N_Z // len(half)
                for z in range(N_Z):
                    piece = refs[used + z // share]
                    at = block_rows(z * n_x + x, slab)
                    row = z % share * slab
                    for out, start, size in zip(outs, edges, sizes):
                        out[at, y * size : (y + 1) * size] = piece[
                            row : row + slab, start : start + size
                        ]
                used += len(half)

    out = plain_call(
        kernel,
        tuple(shaped((N_Z * n_x * slab, size * len(columns)), bf16) for size in sizes),
        *flat,
        scalars=(places,),
        mebibytes=12,
        name="weave",
    )
    return out if cuts else out[0]


def proj_kernel(count, each, *refs):
    blocks, parts = refs[:count], refs[count : count + count // each]
    tok_ref, par_ref, res_out, low_out = refs[count + count // each :]
    total = tok_ref[...]
    for n, block in enumerate(blocks):
        size = block.shape[1]
        part = parts[n // each][:, n % each * size : (n % each + 1) * size]
        total = total + dot(block[...], part, 1, 1)
    res_out[...] = total
    normed, _, _ = norm_forward(total, par_ref[2:3, :], par_ref[3:4, :])
    low_out[...] = normed.astype(bf16)


ERF_TOP = (
    -2.72614225801306e-10,
    2.77068142495902e-08,
    -2.10102402082508e-06,
    -5.69250639462346e-05,
    -7.34990630326855e-04,
    -2.95459980854025e-03,
    -1.60960333262415e-02,
)
ERF_LOW = (
    -1.45660718464996e-05,
    -2.13374055278905e-04,
    -1.68282697438203e-03,
    -7.37332916720468e-03,
    -1.42647390514189e-02,
)


def erf(value):
    value = jnp.clip(value, -4.0, 4.0)
    square = value * value
    top = jnp.full_like(square, ERF_TOP[0])
    for number in ERF_TOP[1:]:
        top = top * square + number
    low = jnp.full_like(square, ERF_LOW[0])
    for number in ERF_LOW[1:]:
        low = low * square + number
    inverse = pl.reciprocal(low, approx=True)
    inverse = inverse * (2.0 - low * inverse)
    return value * top * inverse


def up_kernel(count, low_ref, *refs):
    outs = refs[-2 * count :]
    for n, part in enumerate(refs[:count]):
        hidden = dot(low_ref[...], part[...], 1, 0)
        share = 0.5 * (1.0 + erf(hidden * 0.7071067811865476))
        outs[2 * n][...] = (hidden * share).astype(bf16)
        slope = share + hidden * jnp.exp(-0.5 * hidden * hidden) * 0.3989422804014327
        outs[2 * n + 1][...] = slope.astype(bf16)


def up_call(low, parts, rows_all, spot, into):
    rows, model = low.shape
    width = parts[0].shape[1]
    cols = pl.BlockSpec((rows, TILE), lambda i, *_: (spot, i))
    return plain_call(
        functools.partial(up_kernel, len(parts)),
        (shaped((rows_all, width), bf16),) * (2 * len(parts)),
        low,
        *parts,
        grid=(width // TILE,),
        in_specs=[fixed(low.shape)] + [pl.BlockSpec((model, TILE), lambda i, *_: (0, i))] * len(parts),
        out_specs=(cols,) * (2 * len(parts)),
        into=into,
        mebibytes=14,
        name="up",
    )


def hidden_kernel(count, low_ref, *refs):
    outs = refs[-count:]
    for n in range(count):
        slope, part = refs[n], refs[count + n]
        outs[n][...] = (dot(low_ref[...], part[...], 1, 0) * slope[...].astype(f32)).astype(bf16)


def hidden_call(low, slopes, parts, spot, into):
    rows, model = low.shape
    width = parts[0].shape[1]
    cols = pl.BlockSpec((rows, TILE), lambda i, *_: (spot, i))
    return plain_call(
        functools.partial(hidden_kernel, len(parts)),
        tuple(shaped(slope.shape, bf16) for slope in slopes),
        low,
        *slopes,
        *parts,
        grid=(width // TILE,),
        in_specs=[fixed(low.shape)]
        + [cols] * len(parts)
        + [pl.BlockSpec((model, TILE), lambda i, *_: (0, i))] * len(parts),
        out_specs=(cols,) * len(parts),
        into=into,
        mebibytes=14,
        name="hidden",
    )


def wide_kernel(count, *refs):
    total = dot(refs[0][...], refs[count][...], 1, 1)
    for n in range(1, count):
        total = total + dot(refs[n][...], refs[count + n][...], 1, 1)
    refs[-1][...] = total.astype(refs[-1].dtype)


def wide_call(values, parts, rows, spot, kind):
    model, width = parts[0].shape
    return plain_call(
        functools.partial(wide_kernel, len(values)),
        shaped((rows, model), kind),
        *values,
        *parts,
        grid=(model // TILE,),
        in_specs=[pl.BlockSpec((rows, width), lambda i, *_: (spot, 0))] * len(values)
        + [pl.BlockSpec((TILE, width), lambda i, *_: (i, 0))] * len(parts),
        out_specs=pl.BlockSpec((rows, TILE), lambda i, *_: (0, i)),
        mebibytes=14,
        name="wide",
    )


def loss_kernel(chunks, each, *refs):
    res_ref, tea_ref, own_ref = refs[:3]
    received = refs[3 : 3 + chunks * each]
    live_ref, count_ref, grad_out, low_out, loss_out, far_ref = refs[3 + chunks * each :]
    add_received(received, each, far_ref)
    error = res_ref[...] - tea_ref[...] + own_ref[...] + far_ref[...]
    weighted = live_ref[...] * error
    grad = 2.0 * weighted / count_ref[...]
    grad_out[...] = grad
    low_out[...] = grad.astype(bf16)
    sums = jnp.sum(weighted * error, axis=0, keepdims=True)
    sums = jnp.concatenate([sums, jnp.zeros((7, sums.shape[1]), f32)], axis=0)
    loss_out[...] = jnp.where(pl.program_id(0) == 0, sums, loss_out[...] + sums)


def add_received(received, each, far_ref):
    for n in range(len(received) // each):

        @pl.when(pl.program_id(0) == n)
        def _():
            total = received[n * each][...].astype(f32)
            for ref in received[n * each + 1 : (n + 1) * each]:
                total = total + ref[...].astype(f32)
            far_ref[...] = total


def beside_call(parts):
    rows, width = parts[0].shape

    def kernel(*refs):
        for n, ref in enumerate(refs[:-1]):
            refs[-1][:, n * width : (n + 1) * width] = ref[...]

    return plain_call(
        kernel, shaped((rows, width * len(parts)), bf16), *parts, mebibytes=8, name="beside"
    )


def spread_kernel(each, tiles, low_ref, *refs):
    count = len(refs) // (1 + each * tiles)
    outs = refs[count:]
    for n in range(count * each):
        size = refs[0].shape[1] // each
        part = refs[n // each][:, n % each * size : (n % each + 1) * size]
        piece = dot(low_ref[...], part, 1, 0).astype(bf16)
        lanes = size // tiles
        for tile in range(tiles):
            outs[tile * count * each + n][...] = piece[:, tile * lanes : (tile + 1) * lanes]


def spread_call(low, parts, each):
    width = parts[0].shape[1] // each
    lanes = min(128, width)
    count = len(parts) * each
    out = plain_call(
        functools.partial(spread_kernel, each, width // lanes),
        tuple(shaped((low.shape[0], lanes), bf16) for _ in range(count * (width // lanes))),
        low,
        *parts,
        mebibytes=12,
        name="spread",
    )
    return [out[n : n + count] for n in range(0, len(out), count)]


def unproject_kernel(half, spots, grad_ref, part_ref, far_out, near_out):
    piece = dot(grad_ref[...], part_ref[...], 1, 1)

    @pl.when(pl.program_id(0) < half)
    def _():
        far_out[...] = piece.astype(bf16)

    @pl.when(pl.program_id(0) >= half)
    def _():
        near_out[...] = piece


def unproject_call(grads, part, blocks, rows):
    half = len(blocks) // 2
    model, width = part.shape
    return plain_call(
        functools.partial(unproject_kernel, half),
        (shaped((half * rows, model), bf16), shaped((half * rows, model), f32)),
        grads,
        part,
        grid=(len(blocks),),
        in_specs=[
            pl.BlockSpec((rows, width), lambda i, spots: (spots[i], 0)),
            fixed(part.shape),
        ],
        out_specs=(
            pl.BlockSpec((rows, model), lambda i, spots: (jnp.minimum(i, half - 1), 0)),
            pl.BlockSpec((rows, model), lambda i, spots: (jnp.maximum(i - half, 0), 0)),
        ),
        scalars=(jnp.stack(blocks).astype(jnp.int32),),
        mebibytes=16,
        name="unproject",
    )


def outer_proj_kernel(half, low_ref, *refs):
    blocks, (far_out, *near) = refs[: 2 * half], refs[2 * half :]
    turned = low_ref[...].astype(f32).T.astype(bf16)
    width = blocks[0].shape[1]
    for n in range(half):
        far_out[:, n * width : (n + 1) * width] = dot(turned, blocks[half + n][...], 1, 0).astype(bf16)
        near[n][...] = dot(turned, blocks[n][...], 1, 0).astype(bf16)


def outer_proj_call(low, blocks):
    model = low.shape[1]
    width = blocks[0].shape[1]
    half = len(blocks) // 2
    out = plain_call(
        functools.partial(outer_proj_kernel, half),
        (shaped((model, half * width), bf16),) + (shaped((model, width), bf16),) * half,
        low,
        *blocks,
        mebibytes=14,
        name="outer_proj",
    )
    return out[0], out[1:]


def add_lanes(own, received):
    width = own[0].shape[1]

    def kernel(*refs):
        got = refs[len(own)]
        for n, ref in enumerate(refs[: len(own)]):
            other = got[:, n * width : (n + 1) * width].astype(f32)
            refs[len(own) + 1 + n][...] = (ref[...].astype(f32) + other).astype(bf16)

    return plain_call(
        kernel,
        tuple(shaped(part.shape, bf16) for part in own),
        *own,
        received,
        mebibytes=8,
        name="add_lanes",
    )


def norm_sums(grad, scaled, out_ref, first):
    sums = jnp.concatenate(
        [
            jnp.sum(grad * scaled, axis=0, keepdims=True),
            jnp.sum(grad, axis=0, keepdims=True),
            jnp.zeros((6, grad.shape[1]), f32),
        ],
        axis=0,
    )
    out_ref[...] = jnp.where(first, sums, out_ref[...] + sums)


def middle_kernel(chunks, each, *refs):
    grad_ref, received = refs[0], refs[1 : 1 + chunks * each]
    res_ref, gout_ref, par_ref, full_out, low_out, sum_out, far_ref = refs[1 + chunks * each :]
    add_received(received, each, far_ref)
    _, scaled, inverse = norm_forward(res_ref[...], par_ref[2:3, :], par_ref[3:4, :])
    grad = grad_ref[...] + far_ref[...]
    full = gout_ref[...] + norm_backward(grad, scaled, inverse, par_ref[2:3, :])
    full_out[...] = full
    low_out[...] = full.astype(bf16)
    norm_sums(grad, scaled, sum_out, pl.program_id(0) == 0)


def leave_kernel(count, *refs):
    own_ref, received = refs[0], refs[1 : 1 + count]
    tok_ref, res_ref, par_ref, two_ref, loss_ref, out_ref, sum_out, sum_ref = refs[1 + count :]
    _, scaled, inverse = norm_forward(tok_ref[...], par_ref[0:1, :], par_ref[1:2, :])
    grad = own_ref[...]
    for ref in received:
        grad = grad + ref[...].astype(f32)
    out_ref[...] = res_ref[...] + norm_backward(grad, scaled, inverse, par_ref[0:1, :])
    norm_sums(grad, scaled, sum_ref, pl.program_id(0) == 0)
    sum_out[...] = jnp.concatenate(
        [sum_ref[0:2, :], two_ref[0:2, :], loss_ref[0:1, :], jnp.zeros((3, grad.shape[1]), f32)],
        axis=0,
    )


def split_x(parts, n_x, places):
    model = parts[0][0].shape[0]
    slab = model // (N_Z * n_x)
    total = sum(part[0].shape[1] for part in parts)
    flat = [piece for part in parts for piece in part]

    def kernel(at_ref, *refs):
        outs = refs[len(flat) :]
        for dx in range(n_x):
            x = lax.rem(at_ref[1] + dx, n_x)
            for z in range(N_Z):
                at = block_rows(z * n_x + x, slab)
                lane = 0
                used = 0
                for part in parts:
                    value = refs[used][at, :]
                    size = value.shape[1]
                    if len(part) > 1:
                        value = value.astype(f32)
                        for ref in refs[used + 1 : used + len(part)]:
                            value = value + ref[at, :].astype(f32)
                        value = value.astype(bf16)
                    outs[dx][z * slab : (z + 1) * slab, lane : lane + size] = value
                    lane += size
                    used += len(part)

    return plain_call(
        kernel,
        tuple(shaped((model // n_x, total), bf16) for _ in range(n_x)),
        *flat,
        scalars=(places,),
        mebibytes=12,
        name="split_x",
    )


def split_z(parts, places):
    rows, width = parts[0].shape
    slab = rows // N_Z

    def kernel(at_ref, *refs):
        for k, out in enumerate(refs[len(parts) :]):
            at = block_rows(lax.rem(at_ref[0] + k, N_Z), slab)
            total = refs[0][at, :].astype(f32)
            for ref in refs[1 : len(parts)]:
                total = total + ref[at, :].astype(f32)
            out[...] = total.astype(out.dtype)

    shapes = (shaped((slab, width), f32),) + (shaped((slab, width), bf16),) * (N_Z - 1)
    return plain_call(kernel, shapes, *parts, scalars=(places,), mebibytes=8, name="split_z")


def adam_kernel(layout, counts, *refs):
    grads = []
    for count in counts:
        grad = refs[0][...].astype(f32)
        for ref in refs[1:count]:
            grad = grad + ref[...].astype(f32)
        grads.append(grad)
        refs = refs[count:]
    count = len(layout)
    states, outs = refs[: 3 * count], refs[3 * count :]
    for n, (source, start, size, turned) in enumerate(layout):
        weight, first, second = states[3 * n : 3 * n + 3]
        if len(weight.shape) == 3:
            matrices = weight.shape[0]
            lanes = size // matrices
            for k in range(matrices):
                own = [
                    grads[at][:, lane + k * lanes : lane + (k + 1) * lanes] for at, lane in start
                ]
                own = own[0] if len(own) == 1 else jnp.concatenate(own, axis=1)
                new = adam_step(weight[k], own, first[k], second[k], weight_decay, learn_rate)
                for out, value in zip(outs[3 * n : 3 * n + 3], new):
                    out[k] = value
        else:
            part = grads[source][:, start : start + size]
            if turned:
                part = part.T
            new = adam_step(weight[...], part, first[...], second[...], weight_decay, learn_rate)
            for out, value in zip(outs[3 * n : 3 * n + 3], new):
                out[...] = value


def adam_call(groups, layout, *states):
    shapes = tuple(shaped(s.shape, f32) for s in states)
    out = plain_call(
        functools.partial(adam_kernel, layout, [len(group) for group in groups]),
        shapes,
        *[piece for group in groups for piece in group],
        *states,
        mebibytes=16,
        name="adam",
    )
    return [out[3 * n : 3 * n + 3] for n in range(len(layout))]


def tie(*values):
    return lax.optimization_barrier(values)


def local(
    n_x,
    n_y,
    tokens,
    teacher,
    segments,
    live_mask,
    weight_qkv,
    weight_proj,
    weight_up,
    weight_down,
    norm_params,
    first_qkv,
    first_proj,
    first_up,
    first_down,
    first_norms,
    second_qkv,
    second_proj,
    second_up,
    second_down,
    second_norms,
):
    z_at, x_at = lax.axis_index("z"), lax.axis_index("x")
    y_at, core_at = lax.axis_index("y"), lax.axis_index("core")
    rows, model = tokens.shape
    group_rows = segments.shape[0]
    slab = weight_qkv.shape[1]
    width = weight_qkv.shape[2]
    unit = weight_up.shape[1]
    part_rows = min(128, rows)
    wide_rows = min(256, rows)
    depth = N_Z * slab
    sizes = {"z": N_Z, "x": n_x, "y": n_y, "core": N_CORE}
    places = jnp.stack([z_at, x_at]).astype(jnp.int32)
    offsets = [(dc, dy) for dc in range(N_CORE) for dy in range(n_y)]
    other = N_CORE - 1

    def send(value, axis, step):
        size = sizes[axis]
        return lax.ppermute(value, axis, [(i, (i + step) % size) for i in range(size)])

    def send_col(value, dy, dc):
        perm = [
            (y * N_CORE + c, (y + dy) % n_y * N_CORE + (c + dc) % N_CORE)
            for y in range(n_y)
            for c in range(N_CORE)
        ]
        return lax.ppermute(value, ("y", "core"), perm)

    def fetch(value, axis):
        return [value] + [send(value, axis, -k) for k in range(1, sizes[axis])]

    def fetch_z(value):
        return [value] + [send(value, "z", k) for k in range(1, N_Z)]

    def place(dy, dc):
        return ((y_at + dy) % n_y * N_CORE + (core_at + dc) % N_CORE) * rows

    shard_qkv, shard_up, shard_down = plain_call(
        pack_kernel,
        (
            shaped((slab, 4 * width), bf16),
            shaped((slab + DIGITS, unit), bf16),
            shaped((slab, unit), bf16),
        ),
        live_mask.reshape(-1, 128),
        weight_qkv,
        weight_proj,
        weight_up,
        weight_down,
        mebibytes=8,
        name="pack",
    )
    near_qkv = fetch_z(shard_qkv)
    low_one = plain_call(
        first_kernel,
        shaped(tokens.shape, bf16),
        tokens,
        norm_params,
        grid=(rows // part_rows,),
        in_specs=row_blocks(part_rows, model) + [fixed(norm_params.shape)],
        out_specs=row_blocks(part_rows, model)[0],
        mebibytes=8,
        name="first",
    )
    blocks_one = fetch(low_one, "y") + [send(low_one, "core", -1)]
    block_qkv = stack_z(near_qkv, slab, places)
    geometry = attend_geometry(segments, live_mask)
    own_live = lax.dynamic_slice_in_dim(
        live_mask, (y_at * N_CORE + core_at) * rows, rows, 0
    ).astype(f32)[:, None]
    spots_here = jnp.stack([place(dy, dc) for dc, dy in offsets]).astype(jnp.int32)
    spots = jnp.stack([place(-dy, -dc) for dc, dy in offsets]).astype(jnp.int32)
    block_qkv, shard_down, shard_up, blocks_one[n_y], geometry, own_live, spots_here, spots = tie(
        block_qkv, shard_down, shard_up, blocks_one[n_y], geometry, own_live, spots_here, spots
    )

    beside_qkv = fetch(block_qkv, "x")
    blocks_one, shard_up = tie(blocks_one, shard_up)
    near_up = fetch_z(shard_up)
    blocks_one = blocks_one + [send(block, "core", -1) for block in blocks_one[1:n_y]]
    group_one = place_blocks(blocks_one, spots_here)
    beside_qkv, near_up, group_one, shard_down = tie(beside_qkv, near_up, group_one, shard_down)

    block_up = stack_z(near_up, slab, places)
    full_qkv, part_proj = weave([[[part] for part in beside_qkv]], [3 * width], slab, places)
    block_up, part_proj = tie(block_up, part_proj)
    beside_up = fetch(block_up, "x")
    near_down = fetch_z(shard_down)
    full_proj = fetch(part_proj, "y")
    projected = dot(group_one, full_qkv, 1, 0).astype(bf16)
    mixed, bias = attend_forward(projected, geometry, spots, rows)
    mixed, beside_up, near_down, full_proj = tie(mixed, beside_up, near_down, full_proj)

    blocks_mixed = [
        piece if key == (0, 0) else send_col(piece, -key[1], -key[0])
        for key, piece in zip(offsets, mixed)
    ]
    full_proj = [beside_call(full_proj)]
    full_proj.append(send(full_proj[0], "core", -1))
    blocks_down = stack_z(near_down, slab, places, 2)
    beside_down = [fetch(blocks_down[0], "x")]
    full_up = [weave([[[part] for part in beside_up]], [], slab, places)]
    live_count = sum(
        256.0 * part[depth, 0].astype(f32) + 16.0 * part[depth + 1, 0].astype(f32)
        + part[depth + 2, 0].astype(f32)
        for part in beside_up
    ).reshape(1, 1)
    blocks_mixed, full_proj, full_up, live_count, beside_down, blocks_down = tie(
        blocks_mixed, full_proj, full_up, live_count, beside_down, blocks_down
    )
    beside_down.append(fetch(blocks_down[1], "x"))
    full_up.append(send(full_up[0], "core", -1))
    count = len(offsets)
    residual, low_two = plain_call(
        functools.partial(proj_kernel, count, n_y),
        (shaped(tokens.shape, f32), shaped(tokens.shape, bf16)),
        *blocks_mixed,
        *full_proj,
        tokens,
        norm_params,
        grid=(rows // wide_rows,),
        in_specs=row_blocks(wide_rows, *([width] * count))
        + [fixed(part.shape) for part in full_proj]
        + row_blocks(wide_rows, model)
        + [fixed(norm_params.shape)],
        out_specs=tuple(row_blocks(wide_rows, model, model)),
        mebibytes=18,
        name="proj",
    )
    low_two, full_up = tie(low_two, full_up)

    chunk = min(256, rows)
    chunks = range(rows // chunk)
    neighbours = range(1, n_y)
    rows_all = n_y * rows

    def cross(value, n, back):
        piece = value[n * chunk : (n + 1) * chunk]
        return {dy: send(piece, "y", dy if back else -dy) for dy in neighbours}

    def spot_of(dy, n):
        return (dy * rows) // chunk + n

    low_far = {0: cross(low_two, 0, False)}
    hidden = up_call(low_two, full_up, rows_all, 0, ())
    low_far[0], hidden, low_two, beside_down = tie(low_far[0], hidden, low_two, beside_down)
    full_down = [weave([list(zip(*beside_down))], [], slab, places)]
    full_down.append(send(full_down[0], "core", -1))
    far_out = {}
    for n in chunks:
        if n + 1 in chunks:
            low_far[n + 1] = cross(low_two, n + 1, False)
        for dy in neighbours:
            hidden = up_call(low_far[n][dy], full_up, rows_all, spot_of(dy, n), hidden)
        outs = {
            dy: wide_call(hidden[::2], full_down, chunk, spot_of(dy, n), bf16) for dy in neighbours
        }
        if n + 1 in chunks:
            outs, hidden, low_far[n + 1] = tie(outs, hidden, low_far[n + 1])
        else:
            outs, hidden = tie(outs, hidden)
        if n:
            far_out[n - 1] = tie(far_out[n - 1], outs)[0]
        far_out[n] = {dy: send(outs[dy], "y", -dy) for dy in neighbours}
    own_out = wide_call(hidden[::2], full_down, rows, 0, f32)
    own_out, far_out = tie(own_out, far_out)
    far_out = [far_out[n][dy] for n in chunks for dy in neighbours]
    each = len(neighbours)
    grad_output, grad_branch, loss_rows = plain_call(
        functools.partial(loss_kernel, len(chunks), each),
        (shaped(tokens.shape, f32), shaped(tokens.shape, bf16), shaped((8, model), f32)),
        residual,
        teacher,
        own_out,
        *far_out,
        own_live,
        live_count,
        grid=(len(chunks),),
        in_specs=row_blocks(chunk, model, model, model)
        + [fixed((chunk, model))] * len(far_out)
        + row_blocks(chunk, 1)
        + [fixed((1, 1))],
        out_specs=tuple(row_blocks(chunk, model, model) + [fixed((8, model))]),
        scratch=[pltpu.VMEM((chunk, model), f32)],
        mebibytes=20,
        name="loss",
    )
    active, slope = hidden[::2], hidden[1::2]

    grad_far = {0: cross(grad_branch, 0, False)}
    grad_hidden = hidden_call(grad_branch, slope, full_down, 0, ())
    own_two = wide_call(grad_hidden, full_up, rows, 0, f32)
    grad_far[0], grad_hidden, own_two, grad_branch = tie(
        grad_far[0], grad_hidden, own_two, grad_branch
    )
    def gather_rows(own, far):
        return jnp.concatenate([own] + [far[n][dy] for dy in neighbours for n in chunks], axis=0)

    far_two = {}
    for n in chunks:
        if n + 1 in chunks:
            grad_far[n + 1] = cross(grad_branch, n + 1, False)
        for dy in neighbours:
            grad_hidden = hidden_call(
                grad_far[n][dy], slope, full_down, spot_of(dy, n), grad_hidden
            )
        outs = {
            dy: wide_call(grad_hidden, full_up, chunk, spot_of(dy, n), bf16) for dy in neighbours
        }
        if n + 1 in chunks:
            outs, grad_hidden, grad_far[n + 1] = tie(outs, grad_hidden, grad_far[n + 1])
        else:
            grad_all = gather_rows(grad_branch, grad_far)
            far_down = dot(grad_all, active[other], 0, 0).astype(bf16)
            outs, grad_hidden, grad_all, far_down, far_two = tie(
                outs, grad_hidden, grad_all, far_down, far_two
            )
        far_two[n] = {dy: send(outs[dy], "y", -dy) for dy in neighbours}

    low_all = gather_rows(low_two, low_far)
    far_up = dot(low_all, grad_hidden[other], 0, 0).astype(bf16)
    sent_down, sent_up = send(far_down, "core", 1), send(far_up, "core", 1)
    hold_down = (dot(grad_all, active[0], 0, 0) + sent_down.astype(f32)).astype(bf16)
    halves_down = split_x([[hold_down]], n_x, places)
    hold_up = (dot(low_all, grad_hidden[0], 0, 0) + sent_up.astype(f32)).astype(bf16)
    halves_up = split_x([[hold_up]], n_x, places)
    far_two, halves_down, halves_up = tie(far_two, halves_down, halves_up)
    far_two = [far_two[n][dy] for n in chunks for dy in neighbours]
    grad_residual, grad_low, sums_two = plain_call(
        functools.partial(middle_kernel, len(chunks), each),
        (shaped(tokens.shape, f32), shaped(tokens.shape, bf16), shaped((8, model), f32)),
        own_two,
        *far_two,
        residual,
        grad_output,
        norm_params,
        grid=(len(chunks),),
        in_specs=row_blocks(chunk, model)
        + [fixed((chunk, model))] * len(far_two)
        + row_blocks(chunk, model, model)
        + [fixed(norm_params.shape)],
        out_specs=tuple(row_blocks(chunk, model, model) + [fixed((8, model))]),
        scratch=[pltpu.VMEM((chunk, model), f32)],
        mebibytes=20,
        name="middle",
    )
    pieces_attn = spread_call(grad_low, full_proj, n_y)
    pieces_attn, halves_down, halves_up, grad_low = tie(
        pieces_attn, halves_down, halves_up, grad_low
    )

    def send_back(pieces):
        return [
            piece if key == (0, 0) else send_col(piece, key[1], key[0])
            for key, piece in zip(offsets, pieces)
        ]

    def hop_x(halves):
        return [halves[0]] + [send(halves[dx], "x", dx) for dx in range(1, n_x)]

    def spread_z(pieces):
        return [pieces[0]] + [send(pieces[k], "z", k) for k in range(1, N_Z)]

    lanes = 3 * min(128, width)
    tiles = 3 * width // lanes
    sent_attn = send_back(pieces_attn[0])
    parts_down = hop_x(halves_down)
    far_proj, grad_proj = outer_proj_call(grad_low, blocks_mixed)
    sent_attn, far_proj, grad_proj = tie(sent_attn, far_proj, grad_proj)

    sent_later = [send_back(pieces) for pieces in pieces_attn[1:]]
    sent_proj = send(far_proj, "core", 1)
    grad_projected = attend_backward(projected, sent_attn, spots, geometry[0], bias, 0, ())
    grad_projected, sent_later, sent_proj, parts_down, halves_up = tie(
        grad_projected, sent_later, sent_proj, parts_down, halves_up
    )

    hold_proj = add_lanes(grad_proj, sent_proj)
    pieces_down = split_z(parts_down, places)
    grad_projected, pieces_down, hold_proj, halves_up = tie(
        grad_projected, pieces_down, hold_proj, halves_up
    )
    parts_up = hop_x(halves_up)
    last_down = spread_z(pieces_down)
    part_proj = [hold_proj[0]] + [send(hold_proj[k], "y", k) for k in range(1, n_y)]
    for tile in range(1, tiles):
        grad_projected = attend_backward(
            projected, sent_later[tile - 1], spots, geometry[0], bias, tile, (grad_projected,)
        )
    grad_projected, parts_up, last_down, part_proj = tie(
        grad_projected, parts_up, last_down, part_proj
    )

    far_one, near_one = unproject_call(
        grad_projected,
        full_qkv,
        [place(dy, dc) // rows for dc in reversed(range(N_CORE)) for dy in range(n_y)],
        rows,
    )
    far_one, grad_projected = tie(far_one, grad_projected)
    sent_one = send(far_one, "core", 1)
    grad_qkv = dot(group_one, grad_projected, 0, 0).astype(bf16)
    halves_qkv = split_x([[grad_qkv], part_proj], n_x, places)
    pieces_up = split_z(parts_up, places)
    halves_qkv, sent_one, near_one, pieces_up = tie(halves_qkv, sent_one, near_one, pieces_up)

    parts = [
        near_one[dy * rows : (dy + 1) * rows] + sent_one[dy * rows : (dy + 1) * rows].astype(f32)
        for dy in range(n_y)
    ]
    sent_parts = [parts[k].astype(bf16) for k in range(1, n_y)]
    halves_qkv, sent_parts, pieces_up = tie(halves_qkv, sent_parts, pieces_up)
    received = [send(part, "y", k) for k, part in enumerate(sent_parts, 1)]
    parts_qkv = hop_x(halves_qkv)
    last_up = spread_z(pieces_up)
    (new_down,) = adam_call(
        [last_down], [(0, 0, unit, True)], weight_down, first_down, second_down
    )
    parts_qkv, received, last_up, new_down = tie(parts_qkv, received, last_up, new_down)

    pieces_qkv = split_z(parts_qkv, places)
    token_grad, sums = plain_call(
        functools.partial(leave_kernel, len(received)),
        (shaped(tokens.shape, f32), shaped((8, model), f32)),
        parts[0],
        *received,
        tokens,
        grad_residual,
        norm_params,
        sums_two,
        loss_rows,
        grid=(rows // part_rows,),
        in_specs=row_blocks(part_rows, *([model] * (3 + len(received))))
        + [fixed(norm_params.shape), fixed((8, model)), fixed((8, model))],
        out_specs=tuple(row_blocks(part_rows, model) + [fixed((8, model))]),
        scratch=[pltpu.VMEM((8, model), f32)],
        mebibytes=14,
        name="leave",
    )
    sums, token_grad, pieces_qkv = tie(sums, token_grad, pieces_qkv)
    last_qkv = spread_z(pieces_qkv)
    for axis in ("core", "y", "x", "z"):
        step = 1
        while step < sizes[axis]:
            pairs = [(i, i ^ step) for i in range(sizes[axis])]
            sums = sums + lax.ppermute(sums, axis, pairs)
            step *= 2
    (new_up,) = adam_call([last_up], [(0, 0, unit, False)], weight_up, first_up, second_up)
    sums, last_qkv, new_up = tie(sums, last_qkv, new_up)
    loss_sum = jnp.sum(sums[4])
    live_count = live_count[0, 0]

    new_qkv, new_proj = adam_call(
        [last_qkv],
        [(0, [(0, n * lanes) for n in range(tiles)], lanes, False), (0, 3 * width, width, True)],
        weight_qkv,
        first_qkv,
        second_qkv,
        weight_proj,
        first_proj,
        second_proj,
    )
    new_norms = adam_step(norm_params, sums[:4], first_norms, second_norms, 0.0, norm_rate)
    return (
        loss_sum / live_count,
        token_grad,
        new_qkv[0],
        new_proj[0],
        new_up[0],
        new_down[0],
        new_norms[0],
        new_qkv[1],
        new_proj[1],
        new_up[1],
        new_down[1],
        new_norms[1],
        new_qkv[2],
        new_proj[2],
        new_up[2],
        new_down[2],
        new_norms[2],
    )


def solution(mesh):
    n_x = mesh.shape["row"] // N_Z
    n_y = mesh.shape["col"] // N_CORE
    mesh = jax.sharding.Mesh(
        mesh.devices.reshape(N_Z, n_x, n_y, N_CORE), ("z", "x", "y", "core")
    )
    row, col = ("z", "x"), ("y", "core")
    matrices = (P(None, row, col), P(col, row), P(row, col), P(col, row), P())
    tokens = P(row + col, None)
    return jax.shard_map(
        functools.partial(local, n_x, n_y),
        mesh=mesh,
        in_specs=(tokens, tokens, P(row), P(row)) + matrices * 3,
        out_specs=(P(), tokens) + matrices * 3,
        check_vma=False,
    )
```

```python
import functools

import jax
import jax.numpy as jnp
from jax import lax
from jax.experimental import pallas as pl
from jax.experimental.pallas import tpu as pltpu
from jax.sharding import PartitionSpec as P

HEAD_DIM = 64
PATCHES = 577
STEP = 10
WINDOW = 640
QROWS = 320
TILE = 256
DIGITS = 16
SMALL = pl.CostEstimate(flops=1024, bytes_accessed=1024, transcendentals=0)
N_Z = 4
N_CORE = 2

layer_eps = 1e-06
adam_eps = 1e-08
learn_rate = 0.03
norm_rate = 0.25
moment_decay = 0.5
weight_decay = 0.05

bf16 = jnp.bfloat16
f32 = jnp.float32


def norm_forward(values, gain_row, bias_row):
    average = jnp.mean(values, axis=-1, keepdims=True)
    centred = values - average
    variance = jnp.mean(centred * centred, axis=-1, keepdims=True)
    inverse = lax.rsqrt(variance + layer_eps)
    scaled = centred * inverse
    return (scaled * gain_row + bias_row, scaled, inverse)


def norm_backward(upstream, scaled, inverse, gain_row):
    weighted = upstream * gain_row
    return inverse * (
        weighted
        - jnp.mean(weighted, axis=-1, keepdims=True)
        - scaled * jnp.mean(weighted * scaled, axis=-1, keepdims=True)
    )


def gelu_slope(hidden):
    return (
        0.5 * (1.0 + lax.erf(hidden * 0.7071067811865476))
        + hidden * jnp.exp(-0.5 * hidden * hidden) * 0.3989422804014327
    )


def adam_step(weight, gradient, momentum, variance, decay_rate, rate):
    momentum = moment_decay * momentum + (1.0 - moment_decay) * gradient
    variance = moment_decay * variance + (1.0 - moment_decay) * gradient * gradient
    correction = 1.0 - moment_decay**STEP
    direction = momentum / correction / (jnp.sqrt(variance / correction) + adam_eps)
    return (weight - rate * (direction + decay_rate * weight), momentum, variance)


def dot(left, right, left_dim, right_dim):
    return lax.dot_general(
        left, right, (((left_dim,), (right_dim,)), ((), ())), preferred_element_type=f32
    )


def head_lanes(width, head):
    lanes = lax.broadcasted_iota(jnp.int32, (1, width), 1)
    return (lanes >= head * HEAD_DIM) & (lanes < (head + 1) * HEAD_DIM)


def attend_scores(q_part, k_all, mask):
    scores = dot(q_part, k_all, 1, 1) + mask
    weights = jnp.exp(scores - jnp.max(scores, axis=-1, keepdims=True))
    return weights, jnp.sum(weights, axis=-1, keepdims=True)


def image_window(begin, group_rows):
    image = pl.program_id(0)
    start = jnp.minimum(begin[image] // 16 * 16, group_rows - WINDOW)
    first = begin[image] - start
    return image, pl.multiple_of(start, 16), first


def fill_mask(bias, mask_ref):
    for row in range(0, WINDOW, 128):
        rows = row + lax.broadcasted_iota(jnp.int32, (128, WINDOW), 0)
        cols = lax.broadcasted_iota(jnp.int32, (128, WINDOW), 1)
        mask_ref[row : row + 128, :] = jnp.where(rows == cols, 0.0, bias)


def rows_inside(rows, row_start, first):
    ids = row_start + lax.broadcasted_iota(jnp.int32, (rows, 1), 0)
    return (ids >= first) & (ids < first + PATCHES)


def attend_forward_kernel(blocks, begin, spots, code_ref, *refs):
    bias_out, out_ref, mask_ref = refs[-3:]
    image, start, first = image_window(begin, refs[0].shape[0])
    code = code_ref[pl.ds(start, WINDOW), :]
    bias = jnp.where(code == image, 0.0, -1e30).astype(f32).T
    bias_out[0] = bias[0:8, :]
    fill_mask(bias[0:1, :], mask_ref)
    lanes = refs[0].shape[1]

    for tile in range((len(refs) - 3 - blocks) // 3):
        q_ref, k_ref, v_ref = refs[3 * tile : 3 * tile + 3]
        cols = slice(tile * lanes, (tile + 1) * lanes)

        @pl.when(image == 0)
        def _():
            out_ref[:, cols] = v_ref[...]

        k_all = k_ref[pl.ds(start, WINDOW), :]
        v_all = v_ref[pl.ds(start, WINDOW), :]
        for row in range(0, WINDOW, QROWS):
            at = pl.ds(pl.multiple_of(start + row, 16), QROWS)
            q_part = q_ref[at, :] * jnp.asarray(HEAD_DIM ** (-0.5), bf16)
            inside = rows_inside(QROWS, row, first)
            mixed = None
            for head in range(lanes // HEAD_DIM):
                mine = head_lanes(lanes, head)
                q_head = jnp.where(mine, q_part, jnp.zeros_like(q_part))
                weights, totals = attend_scores(q_head, k_all, mask_ref[row : row + QROWS, :])
                part = dot(weights.astype(bf16), v_all, 1, 0) * (1.0 / totals)
                mixed = part if mixed is None else jnp.where(mine, part, mixed)
            out_ref[at, cols] = jnp.where(inside, mixed.astype(bf16), out_ref[at, cols])

    @pl.when(image == pl.num_programs(0) - 1)
    def _():
        for n, block in enumerate(refs[-3 - blocks : -3]):
            rows = block.shape[0]
            block[...] = out_ref[pl.ds(pl.multiple_of(spots[n], rows), rows), :]


def attend_backward_kernel(blocks, begin, spots, bias_ref, *refs):
    out_ref, p_ref, s_ref, go_ref, mask_ref = refs[-5:]
    go_blocks, refs = refs[3 : 3 + blocks], refs[:3]
    image, start, first = image_window(begin, refs[0].shape[0])
    fill_mask(bias_ref[0, 0:1, :], mask_ref)
    lanes = refs[0].shape[1]
    rows = go_blocks[0].shape[0]
    whole = pl.ds(start, WINDOW)
    inside_all = rows_inside(WINDOW, 0, first)

    @pl.when(image == 0)
    def _():
        for n, block_ref in enumerate(go_blocks):
            go_ref[pl.ds(pl.multiple_of(spots[n], rows), rows), :] = block_ref[...]

    for tile in range(len(refs) // 3):
        q_ref, k_ref, v_ref = refs[3 * tile : 3 * tile + 3]
        cols = slice(tile * lanes, (tile + 1) * lanes)
        base = 3 * tile * lanes
        q_cols, k_cols, v_cols = [
            slice(base + n * lanes, base + (n + 1) * lanes) for n in range(3)
        ]

        @pl.when(image == 0)
        def _():
            out_ref[:, base : base + 2 * lanes] = jnp.zeros((out_ref.shape[0], 2 * lanes), bf16)
            out_ref[:, v_cols] = go_ref[:, cols]

        k_all = k_ref[whole, :]
        v_all = v_ref[whole, :]
        q_all = q_ref[whole, :] * jnp.asarray(HEAD_DIM ** (-0.5), bf16)
        go_all = go_ref[whole, cols]
        key_grad = None
        value_grad = None
        for head in range(lanes // HEAD_DIM):
            mine = head_lanes(lanes, head)
            q_mine = jnp.where(mine, q_all, jnp.zeros_like(q_all))
            go_mine = jnp.where(mine, go_all, jnp.zeros_like(go_all))
            for row in range(0, WINDOW, QROWS):
                part = slice(row, row + QROWS)
                at = pl.ds(pl.multiple_of(start + row, 16), QROWS)
                inside = rows_inside(QROWS, row, first)
                weights, totals = attend_scores(q_mine[part], k_all, mask_ref[part, :])
                weights = weights * jnp.where(inside, 1.0 / totals, 0.0)
                weight_grad = dot(go_mine[part], v_all, 1, 1)
                product = weights * weight_grad
                score_grad = (
                    product - weights * jnp.sum(product, axis=-1, keepdims=True)
                ).astype(bf16)
                p_ref[part, :] = weights.astype(bf16)
                s_ref[part, :] = score_grad
                query_grad = (dot(score_grad, k_all, 1, 0) * HEAD_DIM ** (-0.5)).astype(bf16)
                out_ref[at, q_cols] = jnp.where(inside & mine, query_grad, out_ref[at, q_cols])
            key_part = dot(q_mine, s_ref[...], 0, 0)
            value_part = dot(go_mine, p_ref[...], 0, 0)
            key_grad = key_part if key_grad is None else key_grad + key_part
            value_grad = value_part if value_grad is None else value_grad + value_part
        key_rows = key_grad.T.astype(bf16)
        value_rows = value_grad.T.astype(bf16)
        out_ref[whole, k_cols] = jnp.where(inside_all, key_rows, out_ref[whole, k_cols])
        out_ref[whole, v_cols] = jnp.where(inside_all, value_rows, out_ref[whole, v_cols])


def qkv_operands(projected, tile):
    group_rows, total = projected.shape
    lanes = min(128, total // 3)
    if lanes % 128 == 0:
        specs = [
            pl.BlockSpec((group_rows, lanes), functools.partial(lambda n, i, *_: (0, n), 3 * tile + n))
            for n in range(3)
        ]
        return [projected] * 3, specs
    parts = [projected[:, n * lanes : (n + 1) * lanes] for n in range(3)]
    return parts, [fixed((group_rows, lanes))] * 3


def all_operands(projected):
    width = projected.shape[1] // 3
    operands, specs = [], []
    for tile in range(width // min(128, width)):
        more, places = qkv_operands(projected, tile)
        operands += more
        specs += places
    return operands, specs


def attend_forward(projected, geometry, spots, rows):
    begin, code = geometry
    group_rows, total = projected.shape
    width = total // 3
    blocks = group_rows // rows
    images = begin.shape[0]
    operands, specs = all_operands(projected)
    out = plain_call(
        functools.partial(attend_forward_kernel, blocks),
        (shaped((rows, width), bf16),) * blocks + (shaped((images, 8, WINDOW), f32),),
        code,
        *operands,
        grid=begin.shape,
        in_specs=[fixed(code.shape)] + specs,
        out_specs=(fixed((rows, width)),) * blocks
        + (pl.BlockSpec((1, 8, WINDOW), lambda i, *_: (i, 0, 0)),),
        scratch=[pltpu.VMEM((group_rows, width), bf16), pltpu.VMEM((WINDOW, WINDOW), f32)],
        scalars=(begin, spots),
        mebibytes=20,
        name="attention_forward",
    )
    return out[:blocks], out[blocks]


def attend_backward(projected, go_blocks, spots, begin, bias, tile, into):
    group_rows, total = projected.shape
    lanes = min(128, total // 3)
    operands, specs = qkv_operands(projected, tile)
    return plain_call(
        functools.partial(attend_backward_kernel, len(go_blocks)),
        shaped((group_rows, total), bf16),
        bias,
        *operands,
        *go_blocks,
        grid=begin.shape,
        in_specs=[pl.BlockSpec((1, 8, WINDOW), lambda i, *_: (i, 0, 0))]
        + specs
        + [fixed(block.shape) for block in go_blocks],
        out_specs=pl.BlockSpec((group_rows, 3 * lanes), lambda i, *_: (0, tile)),
        scratch=[pltpu.VMEM((WINDOW, WINDOW), bf16)] * 2
        + [pltpu.VMEM((group_rows, lanes), bf16), pltpu.VMEM((WINDOW, WINDOW), f32)],
        scalars=(begin, spots),
        into=into,
        mebibytes=56 if into else 16,
        name="attention_backward",
    )


def attend_geometry(segments, live_mask):
    group_rows = segments.shape[0]
    numbers = jnp.arange(group_rows // PATCHES, dtype=jnp.int32)
    positions = jnp.arange(group_rows, dtype=jnp.int32)
    begin = jnp.min(
        jnp.where(segments[None, :] == numbers[:, None], positions[None, :], group_rows - PATCHES),
        axis=1,
    )
    code = jnp.where(live_mask == 1, segments, -1)
    return begin, jnp.broadcast_to(code[:, None], (group_rows, 128))


def plain_call(kernel, out_shape, *operands, grid=(), in_specs=None, out_specs=None, scratch=(), scalars=(), into=(), mebibytes=16, name=None):
    params = pltpu.CompilerParams(vmem_limit_bytes=mebibytes * 1024 * 1024)
    if in_specs is None:
        in_specs = [pl.BlockSpec(a.shape, functools.partial(lambda n, *_: (0,) * n, a.ndim)) for a in operands]
    in_specs = list(in_specs) + [pl.BlockSpec(memory_space=pl.ANY)] * len(into)
    if out_specs is None:
        out_specs = jax.tree.map(
            lambda s: pl.BlockSpec(s.shape, functools.partial(lambda n, *_: (0,) * n, len(s.shape))), out_shape
        )
    return pl.pallas_call(
        kernel,
        grid_spec=pltpu.PrefetchScalarGridSpec(
            num_scalar_prefetch=len(scalars),
            grid=grid,
            in_specs=in_specs,
            out_specs=out_specs,
            scratch_shapes=list(scratch),
        ),
        out_shape=out_shape,
        input_output_aliases={len(scalars) + len(operands) + n: n for n in range(len(into))},
        compiler_params=params,
        cost_estimate=SMALL,
        name=name,
    )(*scalars, *operands, *into)


def shaped(shape, dtype):
    return jax.ShapeDtypeStruct(tuple(shape), dtype)


def row_blocks(rows, *widths):
    return [pl.BlockSpec((rows, w), lambda i, *_: (i, 0)) for w in widths]


def fixed(shape):
    return pl.BlockSpec(tuple(shape), functools.partial(lambda n, *_: (0,) * n, len(shape)))


def pack_kernel(live_ref, qkv_ref, proj_ref, up_ref, down_ref, qkv_out, up_out, down_out):
    count, slab, width = qkv_ref.shape
    lanes = min(128, width)
    for n in range(count):
        for t in range(width // lanes):
            at = (count * t + n) * lanes
            qkv_out[:, at : at + lanes] = qkv_ref[n][:, t * lanes : (t + 1) * lanes].astype(bf16)
    qkv_out[:, count * width :] = proj_ref[...].T.astype(bf16)
    up_out[:slab, :] = up_ref[...].astype(bf16)
    live = jnp.sum(jnp.sum(live_ref[...].astype(f32), axis=0, keepdims=True), axis=1, keepdims=True)
    high = jnp.floor(live * (1.0 / 256.0))
    middle = jnp.floor(live * (1.0 / 16.0)) - 16.0 * high
    low = live - 256.0 * high - 16.0 * middle
    row = lax.broadcasted_iota(jnp.int32, (DIGITS, up_out.shape[1]), 0)
    digits = jnp.where(row == 0, high, jnp.where(row == 1, middle, jnp.where(row == 2, low, 0.0)))
    up_out[slab:, :] = digits.astype(bf16)
    down_out[...] = down_ref[...].T.astype(bf16)


def first_kernel(tok_ref, par_ref, low_out):
    normed, _, _ = norm_forward(tok_ref[...], par_ref[0:1, :], par_ref[1:2, :])
    low_out[...] = normed.astype(bf16)


def place_blocks(blocks, spots):
    rows, width = blocks[0].shape

    def kernel(spot_ref, *refs):
        for n, ref in enumerate(refs[:-1]):
            refs[-1][pl.ds(pl.multiple_of(spot_ref[n], rows), rows), :] = ref[...]

    return plain_call(
        kernel,
        shaped((rows * len(blocks), width), bf16),
        *blocks,
        scalars=(spots,),
        mebibytes=20,
        name="place_blocks",
    )


def block_rows(block, slab):
    return pl.ds(pl.multiple_of(block * slab, slab), slab)


def stack_z(pieces, slab, places, count=1):
    height, width = pieces[0].shape
    extra = height - slab
    shapes = (shaped((N_Z * slab // count + extra, width), bf16),) * count

    def kernel(at_ref, *refs):
        held = refs[-1]
        for k, ref in enumerate(refs[:N_Z]):
            held[block_rows(lax.rem(at_ref[0] + N_Z - k, N_Z), slab), :] = ref[:slab, :]
        for n, out in enumerate(refs[N_Z:-1]):
            rows = N_Z * slab // count
            out[:rows, :] = held[n * rows : (n + 1) * rows, :]
            if extra:
                digits = refs[0][slab:, :].astype(f32)
                for ref in refs[1:N_Z]:
                    digits = digits + ref[slab:, :].astype(f32)
                out[rows:, :] = digits.astype(bf16)

    out = plain_call(
        kernel,
        shapes,
        *pieces,
        scalars=(places,),
        scratch=[pltpu.VMEM((N_Z * slab, width), bf16)],
        mebibytes=8,
        name="stack_z",
    )
    return out if count > 1 else out[0]


def weave(columns, cuts, slab, places):
    n_x = len(columns[0])
    width = columns[0][0][0].shape[1]
    flat = [piece for column in columns for half in column for piece in half]
    edges = [0, *cuts, width]
    sizes = [stop - start for start, stop in zip(edges[:-1], edges[1:])]

    def kernel(at_ref, *refs):
        outs = refs[len(flat) :]
        used = 0
        for y, column in enumerate(columns):
            for dx, half in enumerate(column):
                x = lax.rem(at_ref[1] + dx, n_x)
                share = N_Z // len(half)
                for z in range(N_Z):
                    piece = refs[used + z // share]
                    at = block_rows(z * n_x + x, slab)
                    row = z % share * slab
                    for out, start, size in zip(outs, edges, sizes):
                        out[at, y * size : (y + 1) * size] = piece[
                            row : row + slab, start : start + size
                        ]
                used += len(half)

    out = plain_call(
        kernel,
        tuple(shaped((N_Z * n_x * slab, size * len(columns)), bf16) for size in sizes),
        *flat,
        scalars=(places,),
        mebibytes=12,
        name="weave",
    )
    return out if cuts else out[0]


def proj_kernel(count, each, *refs):
    blocks, parts = refs[:count], refs[count : count + count // each]
    tok_ref, par_ref, res_out, low_out = refs[count + count // each :]
    total = tok_ref[...]
    for n, block in enumerate(blocks):
        size = block.shape[1]
        part = parts[n // each][:, n % each * size : (n % each + 1) * size]
        total = total + dot(block[...], part, 1, 1)
    res_out[...] = total
    normed, _, _ = norm_forward(total, par_ref[2:3, :], par_ref[3:4, :])
    low_out[...] = normed.astype(bf16)


ERF_TOP = (
    -2.72614225801306e-10,
    2.77068142495902e-08,
    -2.10102402082508e-06,
    -5.69250639462346e-05,
    -7.34990630326855e-04,
    -2.95459980854025e-03,
    -1.60960333262415e-02,
)
ERF_LOW = (
    -1.45660718464996e-05,
    -2.13374055278905e-04,
    -1.68282697438203e-03,
    -7.37332916720468e-03,
    -1.42647390514189e-02,
)


def erf(value):
    value = jnp.clip(value, -4.0, 4.0)
    square = value * value
    top = jnp.full_like(square, ERF_TOP[0])
    for number in ERF_TOP[1:]:
        top = top * square + number
    low = jnp.full_like(square, ERF_LOW[0])
    for number in ERF_LOW[1:]:
        low = low * square + number
    inverse = pl.reciprocal(low, approx=True)
    inverse = inverse * (2.0 - low * inverse)
    return value * top * inverse


def up_kernel(count, low_ref, *refs):
    outs = refs[-2 * count :]
    for n, part in enumerate(refs[:count]):
        hidden = dot(low_ref[...], part[...], 1, 0)
        share = 0.5 * (1.0 + erf(hidden * 0.7071067811865476))
        outs[2 * n][...] = (hidden * share).astype(bf16)
        slope = share + hidden * jnp.exp(-0.5 * hidden * hidden) * 0.3989422804014327
        outs[2 * n + 1][...] = slope.astype(bf16)


def up_call(low, parts, rows_all, spot, into):
    rows, model = low.shape
    width = parts[0].shape[1]
    cols = pl.BlockSpec((rows, TILE), lambda i, *_: (spot, i))
    return plain_call(
        functools.partial(up_kernel, len(parts)),
        (shaped((rows_all, width), bf16),) * (2 * len(parts)),
        low,
        *parts,
        grid=(width // TILE,),
        in_specs=[fixed(low.shape)] + [pl.BlockSpec((model, TILE), lambda i, *_: (0, i))] * len(parts),
        out_specs=(cols,) * (2 * len(parts)),
        into=into,
        mebibytes=14,
        name="up",
    )


def hidden_kernel(count, low_ref, *refs):
    outs = refs[-count:]
    for n in range(count):
        slope, part = refs[n], refs[count + n]
        outs[n][...] = (dot(low_ref[...], part[...], 1, 0) * slope[...].astype(f32)).astype(bf16)


def hidden_call(low, slopes, parts, spot, into):
    rows, model = low.shape
    width = parts[0].shape[1]
    cols = pl.BlockSpec((rows, TILE), lambda i, *_: (spot, i))
    return plain_call(
        functools.partial(hidden_kernel, len(parts)),
        tuple(shaped(slope.shape, bf16) for slope in slopes),
        low,
        *slopes,
        *parts,
        grid=(width // TILE,),
        in_specs=[fixed(low.shape)]
        + [cols] * len(parts)
        + [pl.BlockSpec((model, TILE), lambda i, *_: (0, i))] * len(parts),
        out_specs=(cols,) * len(parts),
        into=into,
        mebibytes=14,
        name="hidden",
    )


def wide_kernel(count, *refs):
    total = dot(refs[0][...], refs[count][...], 1, 1)
    for n in range(1, count):
        total = total + dot(refs[n][...], refs[count + n][...], 1, 1)
    refs[-1][...] = total.astype(refs[-1].dtype)


def wide_call(values, parts, rows, spot, kind):
    model, width = parts[0].shape
    return plain_call(
        functools.partial(wide_kernel, len(values)),
        shaped((rows, model), kind),
        *values,
        *parts,
        grid=(model // TILE,),
        in_specs=[pl.BlockSpec((rows, width), lambda i, *_: (spot, 0))] * len(values)
        + [pl.BlockSpec((TILE, width), lambda i, *_: (i, 0))] * len(parts),
        out_specs=pl.BlockSpec((rows, TILE), lambda i, *_: (0, i)),
        mebibytes=14,
        name="wide",
    )


def loss_kernel(chunks, each, *refs):
    res_ref, tea_ref, own_ref = refs[:3]
    received = refs[3 : 3 + chunks * each]
    live_ref, count_ref, grad_out, low_out, loss_out, far_ref = refs[3 + chunks * each :]
    add_received(received, each, far_ref)
    error = res_ref[...] - tea_ref[...] + own_ref[...] + far_ref[...]
    weighted = live_ref[...] * error
    grad = 2.0 * weighted / count_ref[...]
    grad_out[...] = grad
    low_out[...] = grad.astype(bf16)
    sums = jnp.sum(weighted * error, axis=0, keepdims=True)
    sums = jnp.concatenate([sums, jnp.zeros((7, sums.shape[1]), f32)], axis=0)
    loss_out[...] = jnp.where(pl.program_id(0) == 0, sums, loss_out[...] + sums)


def add_received(received, each, far_ref):
    for n in range(len(received) // each):

        @pl.when(pl.program_id(0) == n)
        def _():
            total = received[n * each][...].astype(f32)
            for ref in received[n * each + 1 : (n + 1) * each]:
                total = total + ref[...].astype(f32)
            far_ref[...] = total


def beside_call(parts):
    rows, width = parts[0].shape

    def kernel(*refs):
        for n, ref in enumerate(refs[:-1]):
            refs[-1][:, n * width : (n + 1) * width] = ref[...]

    return plain_call(
        kernel, shaped((rows, width * len(parts)), bf16), *parts, mebibytes=8, name="beside"
    )


def spread_kernel(each, tiles, low_ref, *refs):
    count = len(refs) // (1 + each * tiles)
    outs = refs[count:]
    for n in range(count * each):
        size = refs[0].shape[1] // each
        part = refs[n // each][:, n % each * size : (n % each + 1) * size]
        piece = dot(low_ref[...], part, 1, 0).astype(bf16)
        lanes = size // tiles
        for tile in range(tiles):
            outs[tile * count * each + n][...] = piece[:, tile * lanes : (tile + 1) * lanes]


def spread_call(low, parts, each):
    width = parts[0].shape[1] // each
    lanes = min(128, width)
    count = len(parts) * each
    out = plain_call(
        functools.partial(spread_kernel, each, width // lanes),
        tuple(shaped((low.shape[0], lanes), bf16) for _ in range(count * (width // lanes))),
        low,
        *parts,
        mebibytes=12,
        name="spread",
    )
    return [out[n : n + count] for n in range(0, len(out), count)]


def unproject_kernel(half, spots, grad_ref, part_ref, far_out, near_out):
    piece = dot(grad_ref[...], part_ref[...], 1, 1)

    @pl.when(pl.program_id(0) < half)
    def _():
        far_out[...] = piece.astype(bf16)

    @pl.when(pl.program_id(0) >= half)
    def _():
        near_out[...] = piece


def unproject_call(grads, part, blocks, rows):
    half = len(blocks) // 2
    model, width = part.shape
    return plain_call(
        functools.partial(unproject_kernel, half),
        (shaped((half * rows, model), bf16), shaped((half * rows, model), f32)),
        grads,
        part,
        grid=(len(blocks),),
        in_specs=[
            pl.BlockSpec((rows, width), lambda i, spots: (spots[i], 0)),
            fixed(part.shape),
        ],
        out_specs=(
            pl.BlockSpec((rows, model), lambda i, spots: (jnp.minimum(i, half - 1), 0)),
            pl.BlockSpec((rows, model), lambda i, spots: (jnp.maximum(i - half, 0), 0)),
        ),
        scalars=(jnp.stack(blocks).astype(jnp.int32),),
        mebibytes=48,
        name="unproject",
    )


def outer_proj_kernel(half, low_ref, *refs):
    blocks, (far_out, *near) = refs[: 2 * half], refs[2 * half :]
    turned = low_ref[...].astype(f32).T.astype(bf16)
    width = blocks[0].shape[1]
    for n in range(half):
        far_out[:, n * width : (n + 1) * width] = dot(turned, blocks[half + n][...], 1, 0).astype(bf16)
        near[n][...] = dot(turned, blocks[n][...], 1, 0).astype(bf16)


def outer_proj_call(low, blocks):
    model = low.shape[1]
    width = blocks[0].shape[1]
    half = len(blocks) // 2
    out = plain_call(
        functools.partial(outer_proj_kernel, half),
        (shaped((model, half * width), bf16),) + (shaped((model, width), bf16),) * half,
        low,
        *blocks,
        mebibytes=14,
        name="outer_proj",
    )
    return out[0], out[1:]


def add_lanes(own, received):
    width = own[0].shape[1]

    def kernel(*refs):
        got = refs[len(own)]
        for n, ref in enumerate(refs[: len(own)]):
            other = got[:, n * width : (n + 1) * width].astype(f32)
            refs[len(own) + 1 + n][...] = (ref[...].astype(f32) + other).astype(bf16)

    return plain_call(
        kernel,
        tuple(shaped(part.shape, bf16) for part in own),
        *own,
        received,
        mebibytes=8,
        name="add_lanes",
    )


def norm_sums(grad, scaled, out_ref, first):
    sums = jnp.concatenate(
        [
            jnp.sum(grad * scaled, axis=0, keepdims=True),
            jnp.sum(grad, axis=0, keepdims=True),
            jnp.zeros((6, grad.shape[1]), f32),
        ],
        axis=0,
    )
    out_ref[...] = jnp.where(first, sums, out_ref[...] + sums)


def middle_kernel(chunks, each, *refs):
    grad_ref, received = refs[0], refs[1 : 1 + chunks * each]
    res_ref, gout_ref, par_ref, full_out, low_out, sum_out, far_ref = refs[1 + chunks * each :]
    add_received(received, each, far_ref)
    _, scaled, inverse = norm_forward(res_ref[...], par_ref[2:3, :], par_ref[3:4, :])
    grad = grad_ref[...] + far_ref[...]
    full = gout_ref[...] + norm_backward(grad, scaled, inverse, par_ref[2:3, :])
    full_out[...] = full
    low_out[...] = full.astype(bf16)
    norm_sums(grad, scaled, sum_out, pl.program_id(0) == 0)


def leave_kernel(count, *refs):
    own_ref, received = refs[0], refs[1 : 1 + count]
    tok_ref, res_ref, par_ref, two_ref, loss_ref, out_ref, sum_out, sum_ref = refs[1 + count :]
    _, scaled, inverse = norm_forward(tok_ref[...], par_ref[0:1, :], par_ref[1:2, :])
    grad = own_ref[...]
    for ref in received:
        grad = grad + ref[...].astype(f32)
    out_ref[...] = res_ref[...] + norm_backward(grad, scaled, inverse, par_ref[0:1, :])
    norm_sums(grad, scaled, sum_ref, pl.program_id(0) == 0)
    sum_out[...] = jnp.concatenate(
        [sum_ref[0:2, :], two_ref[0:2, :], loss_ref[0:1, :], jnp.zeros((3, grad.shape[1]), f32)],
        axis=0,
    )


def split_x(parts, n_x, places):
    model = parts[0][0].shape[0]
    slab = model // (N_Z * n_x)
    total = sum(part[0].shape[1] for part in parts)
    flat = [piece for part in parts for piece in part]

    def kernel(at_ref, *refs):
        outs = refs[len(flat) :]
        for dx in range(n_x):
            x = lax.rem(at_ref[1] + dx, n_x)
            for z in range(N_Z):
                at = block_rows(z * n_x + x, slab)
                lane = 0
                used = 0
                for part in parts:
                    value = refs[used][at, :]
                    size = value.shape[1]
                    if len(part) > 1:
                        value = value.astype(f32)
                        for ref in refs[used + 1 : used + len(part)]:
                            value = value + ref[at, :].astype(f32)
                        value = value.astype(bf16)
                    outs[dx][z * slab : (z + 1) * slab, lane : lane + size] = value
                    lane += size
                    used += len(part)

    return plain_call(
        kernel,
        tuple(shaped((model // n_x, total), bf16) for _ in range(n_x)),
        *flat,
        scalars=(places,),
        mebibytes=12,
        name="split_x",
    )


def split_z(parts, places):
    rows, width = parts[0].shape
    slab = rows // N_Z

    def kernel(at_ref, *refs):
        for k, out in enumerate(refs[len(parts) :]):
            at = block_rows(lax.rem(at_ref[0] + k, N_Z), slab)
            total = refs[0][at, :].astype(f32)
            for ref in refs[1 : len(parts)]:
                total = total + ref[at, :].astype(f32)
            out[...] = total.astype(out.dtype)

    shapes = (shaped((slab, width), f32),) + (shaped((slab, width), bf16),) * (N_Z - 1)
    return plain_call(kernel, shapes, *parts, scalars=(places,), mebibytes=8, name="split_z")


def adam_kernel(layout, counts, *refs):
    grads = []
    for count in counts:
        grad = refs[0][...].astype(f32)
        for ref in refs[1:count]:
            grad = grad + ref[...].astype(f32)
        grads.append(grad)
        refs = refs[count:]
    count = len(layout)
    states, outs = refs[: 3 * count], refs[3 * count :]
    for n, (source, start, size, turned) in enumerate(layout):
        weight, first, second = states[3 * n : 3 * n + 3]
        if len(weight.shape) == 3:
            matrices = weight.shape[0]
            lanes = size // matrices
            for k in range(matrices):
                own = [
                    grads[at][:, lane + k * lanes : lane + (k + 1) * lanes] for at, lane in start
                ]
                own = own[0] if len(own) == 1 else jnp.concatenate(own, axis=1)
                new = adam_step(weight[k], own, first[k], second[k], weight_decay, learn_rate)
                for out, value in zip(outs[3 * n : 3 * n + 3], new):
                    out[k] = value
        else:
            part = grads[source][:, start : start + size]
            if turned:
                part = part.T
            new = adam_step(weight[...], part, first[...], second[...], weight_decay, learn_rate)
            for out, value in zip(outs[3 * n : 3 * n + 3], new):
                out[...] = value


def adam_call(groups, layout, *states):
    shapes = tuple(shaped(s.shape, f32) for s in states)
    out = plain_call(
        functools.partial(adam_kernel, layout, [len(group) for group in groups]),
        shapes,
        *[piece for group in groups for piece in group],
        *states,
        mebibytes=16,
        name="adam",
    )
    return [out[3 * n : 3 * n + 3] for n in range(len(layout))]


def tie(*values):
    return lax.optimization_barrier(values)


def local(
    n_x,
    n_y,
    tokens,
    teacher,
    segments,
    live_mask,
    weight_qkv,
    weight_proj,
    weight_up,
    weight_down,
    norm_params,
    first_qkv,
    first_proj,
    first_up,
    first_down,
    first_norms,
    second_qkv,
    second_proj,
    second_up,
    second_down,
    second_norms,
):
    z_at, x_at = lax.axis_index("z"), lax.axis_index("x")
    y_at, core_at = lax.axis_index("y"), lax.axis_index("core")
    rows, model = tokens.shape
    group_rows = segments.shape[0]
    slab = weight_qkv.shape[1]
    width = weight_qkv.shape[2]
    unit = weight_up.shape[1]
    part_rows = min(128, rows)
    wide_rows = min(256, rows)
    depth = N_Z * slab
    sizes = {"z": N_Z, "x": n_x, "y": n_y, "core": N_CORE}
    places = jnp.stack([z_at, x_at]).astype(jnp.int32)
    offsets = [(dc, dy) for dc in range(N_CORE) for dy in range(n_y)]
    other = N_CORE - 1

    def send(value, axis, step):
        size = sizes[axis]
        return lax.ppermute(value, axis, [(i, (i + step) % size) for i in range(size)])

    def send_col(value, dy, dc):
        perm = [
            (y * N_CORE + c, (y + dy) % n_y * N_CORE + (c + dc) % N_CORE)
            for y in range(n_y)
            for c in range(N_CORE)
        ]
        return lax.ppermute(value, ("y", "core"), perm)

    def fetch(value, axis):
        return [value] + [send(value, axis, -k) for k in range(1, sizes[axis])]

    def fetch_z(value):
        return [value] + [send(value, "z", k) for k in range(1, N_Z)]

    def place(dy, dc):
        return ((y_at + dy) % n_y * N_CORE + (core_at + dc) % N_CORE) * rows

    shard_qkv, shard_up, shard_down = plain_call(
        pack_kernel,
        (
            shaped((slab, 4 * width), bf16),
            shaped((slab + DIGITS, unit), bf16),
            shaped((slab, unit), bf16),
        ),
        live_mask.reshape(-1, 128),
        weight_qkv,
        weight_proj,
        weight_up,
        weight_down,
        mebibytes=8,
        name="pack",
    )
    near_qkv = fetch_z(shard_qkv)
    low_one = plain_call(
        first_kernel,
        shaped(tokens.shape, bf16),
        tokens,
        norm_params,
        grid=(rows // part_rows,),
        in_specs=row_blocks(part_rows, model) + [fixed(norm_params.shape)],
        out_specs=row_blocks(part_rows, model)[0],
        mebibytes=8,
        name="first",
    )
    blocks_one = fetch(low_one, "y") + [send(low_one, "core", -1)]
    block_qkv = stack_z(near_qkv, slab, places)
    geometry = attend_geometry(segments, live_mask)
    own_live = lax.dynamic_slice_in_dim(
        live_mask, (y_at * N_CORE + core_at) * rows, rows, 0
    ).astype(f32)[:, None]
    spots_here = jnp.stack([place(dy, dc) for dc, dy in offsets]).astype(jnp.int32)
    spots = jnp.stack([place(-dy, -dc) for dc, dy in offsets]).astype(jnp.int32)
    block_qkv, shard_down, shard_up, blocks_one[n_y], geometry, own_live, spots_here, spots = tie(
        block_qkv, shard_down, shard_up, blocks_one[n_y], geometry, own_live, spots_here, spots
    )

    beside_qkv = fetch(block_qkv, "x")
    blocks_one, shard_up = tie(blocks_one, shard_up)
    near_up = fetch_z(shard_up)
    blocks_one = blocks_one + [send(block, "core", -1) for block in blocks_one[1:n_y]]
    group_one = place_blocks(blocks_one, spots_here)
    beside_qkv, near_up, group_one, shard_down = tie(beside_qkv, near_up, group_one, shard_down)

    block_up = stack_z(near_up, slab, places)
    full_qkv, part_proj = weave([[[part] for part in beside_qkv]], [3 * width], slab, places)
    block_up, part_proj = tie(block_up, part_proj)
    beside_up = fetch(block_up, "x")
    near_down = fetch_z(shard_down)
    full_proj = fetch(part_proj, "y")
    projected = dot(group_one, full_qkv, 1, 0).astype(bf16)
    mixed, bias = attend_forward(projected, geometry, spots, rows)
    mixed, beside_up, near_down, full_proj = tie(mixed, beside_up, near_down, full_proj)

    blocks_mixed = [
        piece if key == (0, 0) else send_col(piece, -key[1], -key[0])
        for key, piece in zip(offsets, mixed)
    ]
    full_proj = [beside_call(full_proj)]
    full_proj.append(send(full_proj[0], "core", -1))
    blocks_down = stack_z(near_down, slab, places, 2)
    beside_down = [fetch(blocks_down[0], "x")]
    full_up = [weave([[[part] for part in beside_up]], [], slab, places)]
    live_count = sum(
        256.0 * part[depth, 0].astype(f32) + 16.0 * part[depth + 1, 0].astype(f32)
        + part[depth + 2, 0].astype(f32)
        for part in beside_up
    ).reshape(1, 1)
    blocks_mixed, full_proj, full_up, live_count, beside_down, blocks_down = tie(
        blocks_mixed, full_proj, full_up, live_count, beside_down, blocks_down
    )
    beside_down.append(fetch(blocks_down[1], "x"))
    full_up.append(send(full_up[0], "core", -1))
    count = len(offsets)
    residual, low_two = plain_call(
        functools.partial(proj_kernel, count, n_y),
        (shaped(tokens.shape, f32), shaped(tokens.shape, bf16)),
        *blocks_mixed,
        *full_proj,
        tokens,
        norm_params,
        grid=(rows // wide_rows,),
        in_specs=row_blocks(wide_rows, *([width] * count))
        + [fixed(part.shape) for part in full_proj]
        + row_blocks(wide_rows, model)
        + [fixed(norm_params.shape)],
        out_specs=tuple(row_blocks(wide_rows, model, model)),
        mebibytes=18,
        name="proj",
    )
    low_two, full_up = tie(low_two, full_up)

    chunk = min(256, rows)
    chunks = range(rows // chunk)
    neighbours = range(1, n_y)
    rows_all = n_y * rows

    def cross(value, n, back):
        piece = value[n * chunk : (n + 1) * chunk]
        return {dy: send(piece, "y", dy if back else -dy) for dy in neighbours}

    def spot_of(dy, n):
        return (dy * rows) // chunk + n

    low_far = {0: cross(low_two, 0, False)}
    hidden = up_call(low_two, full_up, rows_all, 0, ())
    low_far[0], hidden, low_two, beside_down = tie(low_far[0], hidden, low_two, beside_down)
    full_down = [weave([list(zip(*beside_down))], [], slab, places)]
    full_down.append(send(full_down[0], "core", -1))
    far_out = {}
    for n in chunks:
        if n + 1 in chunks:
            low_far[n + 1] = cross(low_two, n + 1, False)
        for dy in neighbours:
            hidden = up_call(low_far[n][dy], full_up, rows_all, spot_of(dy, n), hidden)
        outs = {
            dy: wide_call(hidden[::2], full_down, chunk, spot_of(dy, n), bf16) for dy in neighbours
        }
        if n + 1 in chunks:
            outs, hidden, low_far[n + 1] = tie(outs, hidden, low_far[n + 1])
        else:
            outs, hidden = tie(outs, hidden)
        if n:
            far_out[n - 1] = tie(far_out[n - 1], outs)[0]
        far_out[n] = {dy: send(outs[dy], "y", -dy) for dy in neighbours}
    own_out = wide_call(hidden[::2], full_down, rows, 0, f32)
    own_out, far_out = tie(own_out, far_out)
    far_out = [far_out[n][dy] for n in chunks for dy in neighbours]
    each = len(neighbours)
    grad_output, grad_branch, loss_rows = plain_call(
        functools.partial(loss_kernel, len(chunks), each),
        (shaped(tokens.shape, f32), shaped(tokens.shape, bf16), shaped((8, model), f32)),
        residual,
        teacher,
        own_out,
        *far_out,
        own_live,
        live_count,
        grid=(len(chunks),),
        in_specs=row_blocks(chunk, model, model, model)
        + [fixed((chunk, model))] * len(far_out)
        + row_blocks(chunk, 1)
        + [fixed((1, 1))],
        out_specs=tuple(row_blocks(chunk, model, model) + [fixed((8, model))]),
        scratch=[pltpu.VMEM((chunk, model), f32)],
        mebibytes=20,
        name="loss",
    )
    active, slope = hidden[::2], hidden[1::2]

    grad_far = {0: cross(grad_branch, 0, False)}
    grad_hidden = hidden_call(grad_branch, slope, full_down, 0, ())
    own_two = wide_call(grad_hidden, full_up, rows, 0, f32)
    grad_far[0], grad_hidden, own_two, grad_branch = tie(
        grad_far[0], grad_hidden, own_two, grad_branch
    )
    def gather_rows(own, far):
        return jnp.concatenate([own] + [far[n][dy] for dy in neighbours for n in chunks], axis=0)

    far_two = {}
    for n in chunks:
        if n + 1 in chunks:
            grad_far[n + 1] = cross(grad_branch, n + 1, False)
        for dy in neighbours:
            grad_hidden = hidden_call(
                grad_far[n][dy], slope, full_down, spot_of(dy, n), grad_hidden
            )
        outs = {
            dy: wide_call(grad_hidden, full_up, chunk, spot_of(dy, n), bf16) for dy in neighbours
        }
        if n + 1 in chunks:
            outs, grad_hidden, grad_far[n + 1] = tie(outs, grad_hidden, grad_far[n + 1])
        else:
            grad_all = gather_rows(grad_branch, grad_far)
            far_down = dot(grad_all, active[other], 0, 0).astype(bf16)
            outs, grad_hidden, grad_all, far_down, far_two = tie(
                outs, grad_hidden, grad_all, far_down, far_two
            )
        far_two[n] = {dy: send(outs[dy], "y", -dy) for dy in neighbours}

    low_all = gather_rows(low_two, low_far)
    far_up = dot(low_all, grad_hidden[other], 0, 0).astype(bf16)
    sent_down, sent_up = send(far_down, "core", 1), send(far_up, "core", 1)
    hold_down = (dot(grad_all, active[0], 0, 0) + sent_down.astype(f32)).astype(bf16)
    halves_down = split_x([[hold_down]], n_x, places)
    hold_up = (dot(low_all, grad_hidden[0], 0, 0) + sent_up.astype(f32)).astype(bf16)
    halves_up = split_x([[hold_up]], n_x, places)
    far_two, halves_down, halves_up = tie(far_two, halves_down, halves_up)
    far_two = [far_two[n][dy] for n in chunks for dy in neighbours]
    grad_residual, grad_low, sums_two = plain_call(
        functools.partial(middle_kernel, len(chunks), each),
        (shaped(tokens.shape, f32), shaped(tokens.shape, bf16), shaped((8, model), f32)),
        own_two,
        *far_two,
        residual,
        grad_output,
        norm_params,
        grid=(len(chunks),),
        in_specs=row_blocks(chunk, model)
        + [fixed((chunk, model))] * len(far_two)
        + row_blocks(chunk, model, model)
        + [fixed(norm_params.shape)],
        out_specs=tuple(row_blocks(chunk, model, model) + [fixed((8, model))]),
        scratch=[pltpu.VMEM((chunk, model), f32)],
        mebibytes=20,
        name="middle",
    )
    pieces_attn = spread_call(grad_low, full_proj, n_y)
    pieces_attn, halves_down, halves_up, grad_low = tie(
        pieces_attn, halves_down, halves_up, grad_low
    )

    def send_back(pieces):
        return [
            piece if key == (0, 0) else send_col(piece, key[1], key[0])
            for key, piece in zip(offsets, pieces)
        ]

    def hop_x(halves):
        return [halves[0]] + [send(halves[dx], "x", dx) for dx in range(1, n_x)]

    def spread_z(pieces):
        return [pieces[0]] + [send(pieces[k], "z", k) for k in range(1, N_Z)]

    lanes = 3 * min(128, width)
    tiles = 3 * width // lanes
    sent_attn = send_back(pieces_attn[0])
    parts_down = hop_x(halves_down)
    far_proj, grad_proj = outer_proj_call(grad_low, blocks_mixed)
    sent_attn, far_proj, grad_proj = tie(sent_attn, far_proj, grad_proj)

    sent_later = [send_back(pieces) for pieces in pieces_attn[1:]]
    sent_proj = send(far_proj, "core", 1)
    grad_projected = attend_backward(projected, sent_attn, spots, geometry[0], bias, 0, ())
    grad_projected, sent_later, sent_proj, parts_down, halves_up = tie(
        grad_projected, sent_later, sent_proj, parts_down, halves_up
    )

    hold_proj = add_lanes(grad_proj, sent_proj)
    pieces_down = split_z(parts_down, places)
    grad_projected, pieces_down, hold_proj, halves_up = tie(
        grad_projected, pieces_down, hold_proj, halves_up
    )
    parts_up = hop_x(halves_up)
    last_down = spread_z(pieces_down)
    part_proj = [hold_proj[0]] + [send(hold_proj[k], "y", k) for k in range(1, n_y)]
    for tile in range(1, tiles):
        grad_projected = attend_backward(
            projected, sent_later[tile - 1], spots, geometry[0], bias, tile, (grad_projected,)
        )
    grad_projected, parts_up, last_down, part_proj = tie(
        grad_projected, parts_up, last_down, part_proj
    )

    far_one, near_one = unproject_call(
        grad_projected,
        full_qkv,
        [place(dy, dc) // rows for dc in reversed(range(N_CORE)) for dy in range(n_y)],
        rows,
    )
    far_one, grad_projected = tie(far_one, grad_projected)
    sent_one = send(far_one, "core", 1)
    grad_qkv = dot(group_one, grad_projected, 0, 0).astype(bf16)
    halves_qkv = split_x([[grad_qkv], part_proj], n_x, places)
    pieces_up = split_z(parts_up, places)
    halves_qkv, sent_one, near_one, pieces_up = tie(halves_qkv, sent_one, near_one, pieces_up)

    parts = [
        near_one[dy * rows : (dy + 1) * rows] + sent_one[dy * rows : (dy + 1) * rows].astype(f32)
        for dy in range(n_y)
    ]
    sent_parts = [parts[k].astype(bf16) for k in range(1, n_y)]
    halves_qkv, sent_parts, pieces_up = tie(halves_qkv, sent_parts, pieces_up)
    received = [send(part, "y", k) for k, part in enumerate(sent_parts, 1)]
    parts_qkv = hop_x(halves_qkv)
    last_up = spread_z(pieces_up)
    (new_down,) = adam_call(
        [last_down], [(0, 0, unit, True)], weight_down, first_down, second_down
    )
    parts_qkv, received, last_up, new_down = tie(parts_qkv, received, last_up, new_down)

    pieces_qkv = split_z(parts_qkv, places)
    token_grad, sums = plain_call(
        functools.partial(leave_kernel, len(received)),
        (shaped(tokens.shape, f32), shaped((8, model), f32)),
        parts[0],
        *received,
        tokens,
        grad_residual,
        norm_params,
        sums_two,
        loss_rows,
        grid=(rows // part_rows,),
        in_specs=row_blocks(part_rows, *([model] * (3 + len(received))))
        + [fixed(norm_params.shape), fixed((8, model)), fixed((8, model))],
        out_specs=tuple(row_blocks(part_rows, model) + [fixed((8, model))]),
        scratch=[pltpu.VMEM((8, model), f32)],
        mebibytes=14,
        name="leave",
    )
    sums, token_grad, pieces_qkv = tie(sums, token_grad, pieces_qkv)
    last_qkv = spread_z(pieces_qkv)
    for axis in ("z", "x", "y", "core"):
        step = 1
        while step < sizes[axis]:
            pairs = [(i, i ^ step) for i in range(sizes[axis])]
            sums = sums + lax.ppermute(sums, axis, pairs)
            step *= 2
    (new_up,) = adam_call([last_up], [(0, 0, unit, False)], weight_up, first_up, second_up)
    sums, last_qkv, new_up = tie(sums, last_qkv, new_up)
    loss_sum = jnp.sum(sums[4])
    live_count = live_count[0, 0]

    new_qkv, new_proj = adam_call(
        [last_qkv],
        [(0, [(0, n * lanes) for n in range(tiles)], lanes, False), (0, 3 * width, width, True)],
        weight_qkv,
        first_qkv,
        second_qkv,
        weight_proj,
        first_proj,
        second_proj,
    )
    new_norms = adam_step(norm_params, sums[:4], first_norms, second_norms, 0.0, norm_rate)
    return (
        loss_sum / live_count,
        token_grad,
        new_qkv[0],
        new_proj[0],
        new_up[0],
        new_down[0],
        new_norms[0],
        new_qkv[1],
        new_proj[1],
        new_up[1],
        new_down[1],
        new_norms[1],
        new_qkv[2],
        new_proj[2],
        new_up[2],
        new_down[2],
        new_norms[2],
    )


def solution(mesh):
    n_x = mesh.shape["row"] // N_Z
    n_y = mesh.shape["col"] // N_CORE
    mesh = jax.sharding.Mesh(
        mesh.devices.reshape(N_Z, n_x, n_y, N_CORE), ("z", "x", "y", "core")
    )
    row, col = ("z", "x"), ("y", "core")
    matrices = (P(None, row, col), P(col, row), P(row, col), P(col, row), P())
    tokens = P(row + col, None)
    return jax.shard_map(
        functools.partial(local, n_x, n_y),
        mesh=mesh,
        in_specs=(tokens, tokens, P(row), P(row)) + matrices * 3,
        out_specs=(P(), tokens) + matrices * 3,
        check_vma=False,
    )
```

```python
import functools

import jax
import jax.numpy as jnp
from jax import lax
from jax.experimental import pallas as pl
from jax.experimental.pallas import tpu as pltpu
from jax.sharding import PartitionSpec as P

HEAD_DIM = 64
PATCHES = 577
STEP = 10
WINDOW = 640
QROWS = 320
TILE = 256
DIGITS = 16
SMALL = pl.CostEstimate(flops=1024, bytes_accessed=1024, transcendentals=0)
N_Z = 4
N_CORE = 2

layer_eps = 1e-06
adam_eps = 1e-08
learn_rate = 0.03
norm_rate = 0.25
moment_decay = 0.5
weight_decay = 0.05

bf16 = jnp.bfloat16
f32 = jnp.float32


def norm_forward(values, gain_row, bias_row):
    average = jnp.mean(values, axis=-1, keepdims=True)
    centred = values - average
    variance = jnp.mean(centred * centred, axis=-1, keepdims=True)
    inverse = lax.rsqrt(variance + layer_eps)
    scaled = centred * inverse
    return (scaled * gain_row + bias_row, scaled, inverse)


def norm_backward(upstream, scaled, inverse, gain_row):
    weighted = upstream * gain_row
    return inverse * (
        weighted
        - jnp.mean(weighted, axis=-1, keepdims=True)
        - scaled * jnp.mean(weighted * scaled, axis=-1, keepdims=True)
    )


def gelu_slope(hidden):
    return (
        0.5 * (1.0 + lax.erf(hidden * 0.7071067811865476))
        + hidden * jnp.exp(-0.5 * hidden * hidden) * 0.3989422804014327
    )


def adam_step(weight, gradient, momentum, variance, decay_rate, rate):
    momentum = moment_decay * momentum + (1.0 - moment_decay) * gradient
    variance = moment_decay * variance + (1.0 - moment_decay) * gradient * gradient
    correction = 1.0 - moment_decay**STEP
    direction = momentum / correction / (jnp.sqrt(variance / correction) + adam_eps)
    return (weight - rate * (direction + decay_rate * weight), momentum, variance)


def dot(left, right, left_dim, right_dim):
    return lax.dot_general(
        left, right, (((left_dim,), (right_dim,)), ((), ())), preferred_element_type=f32
    )


def head_lanes(width, head):
    lanes = lax.broadcasted_iota(jnp.int32, (1, width), 1)
    return (lanes >= head * HEAD_DIM) & (lanes < (head + 1) * HEAD_DIM)


def attend_scores(q_part, k_all, mask):
    scores = dot(q_part, k_all, 1, 1) + mask
    weights = jnp.exp(scores - jnp.max(scores, axis=-1, keepdims=True))
    return weights, jnp.sum(weights, axis=-1, keepdims=True)


def image_window(begin, group_rows):
    image = pl.program_id(0)
    start = jnp.minimum(begin[image] // 16 * 16, group_rows - WINDOW)
    first = begin[image] - start
    return image, pl.multiple_of(start, 16), first


def fill_mask(bias, mask_ref):
    for row in range(0, WINDOW, 128):
        rows = row + lax.broadcasted_iota(jnp.int32, (128, WINDOW), 0)
        cols = lax.broadcasted_iota(jnp.int32, (128, WINDOW), 1)
        mask_ref[row : row + 128, :] = jnp.where(rows == cols, 0.0, bias)


def rows_inside(rows, row_start, first):
    ids = row_start + lax.broadcasted_iota(jnp.int32, (rows, 1), 0)
    return (ids >= first) & (ids < first + PATCHES)


def attend_forward_kernel(blocks, begin, spots, code_ref, *refs):
    bias_out, out_ref, mask_ref = refs[-3:]
    image, start, first = image_window(begin, refs[0].shape[0])
    code = code_ref[pl.ds(start, WINDOW), :]
    bias = jnp.where(code == image, 0.0, -1e30).astype(f32).T
    bias_out[0] = bias[0:8, :]
    fill_mask(bias[0:1, :], mask_ref)
    lanes = refs[0].shape[1]

    for tile in range((len(refs) - 3 - blocks) // 3):
        q_ref, k_ref, v_ref = refs[3 * tile : 3 * tile + 3]
        cols = slice(tile * lanes, (tile + 1) * lanes)

        @pl.when(image == 0)
        def _():
            out_ref[:, cols] = v_ref[...]

        k_all = k_ref[pl.ds(start, WINDOW), :]
        v_all = v_ref[pl.ds(start, WINDOW), :]
        for row in range(0, WINDOW, QROWS):
            at = pl.ds(pl.multiple_of(start + row, 16), QROWS)
            q_part = q_ref[at, :] * jnp.asarray(HEAD_DIM ** (-0.5), bf16)
            inside = rows_inside(QROWS, row, first)
            mixed = None
            for head in range(lanes // HEAD_DIM):
                mine = head_lanes(lanes, head)
                q_head = jnp.where(mine, q_part, jnp.zeros_like(q_part))
                weights, totals = attend_scores(q_head, k_all, mask_ref[row : row + QROWS, :])
                part = dot(weights.astype(bf16), v_all, 1, 0) * (1.0 / totals)
                mixed = part if mixed is None else jnp.where(mine, part, mixed)
            out_ref[at, cols] = jnp.where(inside, mixed.astype(bf16), out_ref[at, cols])

    @pl.when(image == pl.num_programs(0) - 1)
    def _():
        each = spots.shape[0] // blocks
        for n, block in enumerate(refs[-3 - blocks : -3]):
            rows = block.shape[0] // each
            for k in range(each):
                there = pl.ds(pl.multiple_of(spots[n * each + k], rows), rows)
                block[k * rows : (k + 1) * rows, :] = out_ref[there, :]


def attend_backward_kernel(blocks, begin, spots, bias_ref, *refs):
    out_ref, p_ref, s_ref, go_ref, mask_ref = refs[-5:]
    go_blocks, refs = refs[3 : 3 + blocks], refs[:3]
    image, start, first = image_window(begin, refs[0].shape[0])
    fill_mask(bias_ref[0, 0:1, :], mask_ref)
    lanes = refs[0].shape[1]
    rows = go_blocks[0].shape[0]
    whole = pl.ds(start, WINDOW)
    inside_all = rows_inside(WINDOW, 0, first)

    @pl.when(image == 0)
    def _():
        for n, block_ref in enumerate(go_blocks):
            go_ref[pl.ds(pl.multiple_of(spots[n], rows), rows), :] = block_ref[...]

    for tile in range(len(refs) // 3):
        q_ref, k_ref, v_ref = refs[3 * tile : 3 * tile + 3]
        cols = slice(tile * lanes, (tile + 1) * lanes)
        base = 3 * tile * lanes
        q_cols, k_cols, v_cols = [
            slice(base + n * lanes, base + (n + 1) * lanes) for n in range(3)
        ]

        @pl.when(image == 0)
        def _():
            out_ref[:, base : base + 2 * lanes] = jnp.zeros((out_ref.shape[0], 2 * lanes), bf16)
            out_ref[:, v_cols] = go_ref[:, cols]

        k_all = k_ref[whole, :]
        v_all = v_ref[whole, :]
        q_all = q_ref[whole, :] * jnp.asarray(HEAD_DIM ** (-0.5), bf16)
        go_all = go_ref[whole, cols]
        key_grad = None
        value_grad = None
        for head in range(lanes // HEAD_DIM):
            mine = head_lanes(lanes, head)
            q_mine = jnp.where(mine, q_all, jnp.zeros_like(q_all))
            go_mine = jnp.where(mine, go_all, jnp.zeros_like(go_all))
            for row in range(0, WINDOW, QROWS):
                part = slice(row, row + QROWS)
                at = pl.ds(pl.multiple_of(start + row, 16), QROWS)
                inside = rows_inside(QROWS, row, first)
                weights, totals = attend_scores(q_mine[part], k_all, mask_ref[part, :])
                weights = weights * jnp.where(inside, 1.0 / totals, 0.0)
                weight_grad = dot(go_mine[part], v_all, 1, 1)
                product = weights * weight_grad
                score_grad = (
                    product - weights * jnp.sum(product, axis=-1, keepdims=True)
                ).astype(bf16)
                p_ref[part, :] = weights.astype(bf16)
                s_ref[part, :] = score_grad
                query_grad = (dot(score_grad, k_all, 1, 0) * HEAD_DIM ** (-0.5)).astype(bf16)
                out_ref[at, q_cols] = jnp.where(inside & mine, query_grad, out_ref[at, q_cols])
            key_part = dot(q_mine, s_ref[...], 0, 0)
            value_part = dot(go_mine, p_ref[...], 0, 0)
            key_grad = key_part if key_grad is None else key_grad + key_part
            value_grad = value_part if value_grad is None else value_grad + value_part
        key_rows = key_grad.T.astype(bf16)
        value_rows = value_grad.T.astype(bf16)
        out_ref[whole, k_cols] = jnp.where(inside_all, key_rows, out_ref[whole, k_cols])
        out_ref[whole, v_cols] = jnp.where(inside_all, value_rows, out_ref[whole, v_cols])


def qkv_operands(projected, tile):
    group_rows, total = projected.shape
    lanes = min(128, total // 3)
    if lanes % 128 == 0:
        specs = [
            pl.BlockSpec((group_rows, lanes), functools.partial(lambda n, i, *_: (0, n), 3 * tile + n))
            for n in range(3)
        ]
        return [projected] * 3, specs
    parts = [projected[:, n * lanes : (n + 1) * lanes] for n in range(3)]
    return parts, [fixed((group_rows, lanes))] * 3


def all_operands(projected):
    width = projected.shape[1] // 3
    operands, specs = [], []
    for tile in range(width // min(128, width)):
        more, places = qkv_operands(projected, tile)
        operands += more
        specs += places
    return operands, specs


def attend_forward(projected, geometry, spots, rows):
    begin, code = geometry
    group_rows, total = projected.shape
    width = total // 3
    blocks = group_rows // rows
    images = begin.shape[0]
    operands, specs = all_operands(projected)
    out = plain_call(
        functools.partial(attend_forward_kernel, blocks),
        (shaped((rows, width), bf16),) * blocks + (shaped((images, 8, WINDOW), f32),),
        code,
        *operands,
        grid=begin.shape,
        in_specs=[fixed(code.shape)] + specs,
        out_specs=(fixed((rows, width)),) * blocks
        + (pl.BlockSpec((1, 8, WINDOW), lambda i, *_: (i, 0, 0)),),
        scratch=[pltpu.VMEM((group_rows, width), bf16), pltpu.VMEM((WINDOW, WINDOW), f32)],
        scalars=(begin, spots),
        mebibytes=20,
        name="attention_forward",
    )
    return out[:blocks], out[blocks]


def attend_backward(projected, go_blocks, spots, begin, bias, tile, into):
    group_rows, total = projected.shape
    lanes = min(128, total // 3)
    operands, specs = qkv_operands(projected, tile)
    return plain_call(
        functools.partial(attend_backward_kernel, len(go_blocks)),
        shaped((group_rows, total), bf16),
        bias,
        *operands,
        *go_blocks,
        grid=begin.shape,
        in_specs=[pl.BlockSpec((1, 8, WINDOW), lambda i, *_: (i, 0, 0))]
        + specs
        + [fixed(block.shape) for block in go_blocks],
        out_specs=pl.BlockSpec((group_rows, 3 * lanes), lambda i, *_: (0, tile)),
        scratch=[pltpu.VMEM((WINDOW, WINDOW), bf16)] * 2
        + [pltpu.VMEM((group_rows, lanes), bf16), pltpu.VMEM((WINDOW, WINDOW), f32)],
        scalars=(begin, spots),
        into=into,
        mebibytes=56 if into else 16,
        name="attention_backward",
    )


def attend_geometry(segments, live_mask):
    group_rows = segments.shape[0]
    numbers = jnp.arange(group_rows // PATCHES, dtype=jnp.int32)
    positions = jnp.arange(group_rows, dtype=jnp.int32)
    begin = jnp.min(
        jnp.where(segments[None, :] == numbers[:, None], positions[None, :], group_rows - PATCHES),
        axis=1,
    )
    code = jnp.where(live_mask == 1, segments, -1)
    return begin, jnp.broadcast_to(code[:, None], (group_rows, 128))


def plain_call(kernel, out_shape, *operands, grid=(), in_specs=None, out_specs=None, scratch=(), scalars=(), into=(), mebibytes=16, name=None):
    params = pltpu.CompilerParams(vmem_limit_bytes=mebibytes * 1024 * 1024)
    if in_specs is None:
        in_specs = [pl.BlockSpec(a.shape, functools.partial(lambda n, *_: (0,) * n, a.ndim)) for a in operands]
    in_specs = list(in_specs) + [pl.BlockSpec(memory_space=pl.ANY)] * len(into)
    if out_specs is None:
        out_specs = jax.tree.map(
            lambda s: pl.BlockSpec(s.shape, functools.partial(lambda n, *_: (0,) * n, len(s.shape))), out_shape
        )
    return pl.pallas_call(
        kernel,
        grid_spec=pltpu.PrefetchScalarGridSpec(
            num_scalar_prefetch=len(scalars),
            grid=grid,
            in_specs=in_specs,
            out_specs=out_specs,
            scratch_shapes=list(scratch),
        ),
        out_shape=out_shape,
        input_output_aliases={len(scalars) + len(operands) + n: n for n in range(len(into))},
        compiler_params=params,
        cost_estimate=SMALL,
        name=name,
    )(*scalars, *operands, *into)


def shaped(shape, dtype):
    return jax.ShapeDtypeStruct(tuple(shape), dtype)


def row_blocks(rows, *widths):
    return [pl.BlockSpec((rows, w), lambda i, *_: (i, 0)) for w in widths]


def fixed(shape):
    return pl.BlockSpec(tuple(shape), functools.partial(lambda n, *_: (0,) * n, len(shape)))


def pack_kernel(live_ref, qkv_ref, proj_ref, up_ref, down_ref, qkv_out, up_out, down_out):
    count, slab, width = qkv_ref.shape
    lanes = min(128, width)
    for n in range(count):
        for t in range(width // lanes):
            at = (count * t + n) * lanes
            qkv_out[:, at : at + lanes] = qkv_ref[n][:, t * lanes : (t + 1) * lanes].astype(bf16)
    qkv_out[:, count * width :] = proj_ref[...].T.astype(bf16)
    up_out[:slab, :] = up_ref[...].astype(bf16)
    live = jnp.sum(jnp.sum(live_ref[...].astype(f32), axis=0, keepdims=True), axis=1, keepdims=True)
    high = jnp.floor(live * (1.0 / 256.0))
    middle = jnp.floor(live * (1.0 / 16.0)) - 16.0 * high
    low = live - 256.0 * high - 16.0 * middle
    row = lax.broadcasted_iota(jnp.int32, (DIGITS, up_out.shape[1]), 0)
    digits = jnp.where(row == 0, high, jnp.where(row == 1, middle, jnp.where(row == 2, low, 0.0)))
    up_out[slab:, :] = digits.astype(bf16)
    down_out[...] = down_ref[...].T.astype(bf16)


def first_kernel(tok_ref, par_ref, low_out):
    normed, _, _ = norm_forward(tok_ref[...], par_ref[0:1, :], par_ref[1:2, :])
    low_out[...] = normed.astype(bf16)


def place_blocks(blocks, spots, unit=256):
    width = blocks[0].shape[1]

    def kernel(spot_ref, *refs):
        for n, ref in enumerate(refs[:-1]):
            refs[-1][pl.ds(pl.multiple_of(spot_ref[n], unit), ref.shape[0]), :] = ref[...]

    return plain_call(
        kernel,
        shaped((sum(block.shape[0] for block in blocks), width), blocks[0].dtype),
        *blocks,
        scalars=(spots,),
        mebibytes=20,
        name="place_blocks",
    )


def block_rows(block, slab):
    return pl.ds(pl.multiple_of(block * slab, slab), slab)


def stack_z(pieces, slab, places, count=1):
    height, width = pieces[0].shape
    extra = height - slab
    shapes = (shaped((N_Z * slab // count + extra, width), bf16),) * count

    def kernel(at_ref, *refs):
        held = refs[-1]
        for k, ref in enumerate(refs[:N_Z]):
            held[block_rows(lax.rem(at_ref[0] + N_Z - k, N_Z), slab), :] = ref[:slab, :]
        for n, out in enumerate(refs[N_Z:-1]):
            rows = N_Z * slab // count
            out[:rows, :] = held[n * rows : (n + 1) * rows, :]
            if extra:
                digits = refs[0][slab:, :].astype(f32)
                for ref in refs[1:N_Z]:
                    digits = digits + ref[slab:, :].astype(f32)
                out[rows:, :] = digits.astype(bf16)

    out = plain_call(
        kernel,
        shapes,
        *pieces,
        scalars=(places,),
        scratch=[pltpu.VMEM((N_Z * slab, width), bf16)],
        mebibytes=8,
        name="stack_z",
    )
    return out if count > 1 else out[0]


def weave(columns, cuts, slab, places):
    n_x = len(columns[0])
    width = columns[0][0][0].shape[1]
    flat = [piece for column in columns for half in column for piece in half]
    edges = [0, *cuts, width]
    sizes = [stop - start for start, stop in zip(edges[:-1], edges[1:])]

    def kernel(at_ref, *refs):
        outs = refs[len(flat) :]
        used = 0
        for y, column in enumerate(columns):
            for dx, half in enumerate(column):
                x = lax.rem(at_ref[1] + dx, n_x)
                share = N_Z // len(half)
                for z in range(N_Z):
                    piece = refs[used + z // share]
                    at = block_rows(z * n_x + x, slab)
                    row = z % share * slab
                    for out, start, size in zip(outs, edges, sizes):
                        out[at, y * size : (y + 1) * size] = piece[
                            row : row + slab, start : start + size
                        ]
                used += len(half)

    out = plain_call(
        kernel,
        tuple(shaped((N_Z * n_x * slab, size * len(columns)), bf16) for size in sizes),
        *flat,
        scalars=(places,),
        mebibytes=12,
        name="weave",
    )
    return out if cuts else out[0]


def proj_kernel(count, each, *refs):
    blocks, parts = refs[:count], refs[count : count + count // each]
    tok_ref, par_ref, res_out, low_out = refs[count + count // each :]
    total = tok_ref[...]
    for n, block in enumerate(blocks):
        size = block.shape[1]
        part = parts[n // each][:, n % each * size : (n % each + 1) * size]
        total = total + dot(block[...], part, 1, 1)
    res_out[...] = total
    normed, _, _ = norm_forward(total, par_ref[2:3, :], par_ref[3:4, :])
    low_out[...] = normed.astype(bf16)


ERF_TOP = (
    -2.72614225801306e-10,
    2.77068142495902e-08,
    -2.10102402082508e-06,
    -5.69250639462346e-05,
    -7.34990630326855e-04,
    -2.95459980854025e-03,
    -1.60960333262415e-02,
)
ERF_LOW = (
    -1.45660718464996e-05,
    -2.13374055278905e-04,
    -1.68282697438203e-03,
    -7.37332916720468e-03,
    -1.42647390514189e-02,
)


def erf(value):
    value = jnp.clip(value, -4.0, 4.0)
    square = value * value
    top = jnp.full_like(square, ERF_TOP[0])
    for number in ERF_TOP[1:]:
        top = top * square + number
    low = jnp.full_like(square, ERF_LOW[0])
    for number in ERF_LOW[1:]:
        low = low * square + number
    inverse = pl.reciprocal(low, approx=True)
    inverse = inverse * (2.0 - low * inverse)
    return value * top * inverse


def up_kernel(count, _, low_ref, *refs):
    outs = refs[-2 * count :]
    for n, part in enumerate(refs[:count]):
        hidden = dot(low_ref[...], part[...], 1, 0)
        share = 0.5 * (1.0 + erf(hidden * 0.7071067811865476))
        outs[2 * n][...] = (hidden * share).astype(bf16)
        slope = share + hidden * jnp.exp(-0.5 * hidden * hidden) * 0.3989422804014327
        outs[2 * n + 1][...] = slope.astype(bf16)


def up_call(low, parts, rows, spot, into):
    rows_all, model = low.shape
    width = parts[0].shape[1]
    cols = pl.BlockSpec((rows, TILE), lambda i, at: (at[0], i))
    return plain_call(
        functools.partial(up_kernel, len(parts)),
        (shaped((rows_all, width), bf16),) * (2 * len(parts)),
        low,
        *parts,
        grid=(width // TILE,),
        in_specs=[pl.BlockSpec((rows, model), lambda i, at: (at[0], 0))]
        + [pl.BlockSpec((model, TILE), lambda i, at: (0, i))] * len(parts),
        out_specs=(cols,) * (2 * len(parts)),
        scalars=(spot,),
        into=into,
        mebibytes=14,
        name="up",
    )


def hidden_kernel(count, _, low_ref, *refs):
    outs = refs[-count:]
    for n in range(count):
        slope, part = refs[n], refs[count + n]
        outs[n][...] = (dot(low_ref[...], part[...], 1, 0) * slope[...].astype(f32)).astype(bf16)


def hidden_call(low, slopes, parts, spot, into):
    rows, model = low.shape
    width = parts[0].shape[1]
    cols = pl.BlockSpec((rows, TILE), lambda i, at: (at[0], i))
    return plain_call(
        functools.partial(hidden_kernel, len(parts)),
        tuple(shaped(slope.shape, bf16) for slope in slopes),
        low,
        *slopes,
        *parts,
        grid=(width // TILE,),
        in_specs=[fixed(low.shape)]
        + [cols] * len(parts)
        + [pl.BlockSpec((model, TILE), lambda i, at: (0, i))] * len(parts),
        out_specs=(cols,) * len(parts),
        scalars=(spot,),
        into=into,
        mebibytes=14,
        name="hidden",
    )


def wide_kernel(count, _, *refs):
    total = dot(refs[0][...], refs[count][...], 1, 1)
    for n in range(1, count):
        total = total + dot(refs[n][...], refs[count + n][...], 1, 1)
    refs[-1][...] = total.astype(refs[-1].dtype)


def wide_call(values, parts, rows, spot, kind):
    model, width = parts[0].shape
    return plain_call(
        functools.partial(wide_kernel, len(values)),
        shaped((rows, model), kind),
        *values,
        *parts,
        grid=(model // TILE,),
        in_specs=[pl.BlockSpec((rows, width), lambda i, at: (at[0], 0))] * len(values)
        + [pl.BlockSpec((TILE, width), lambda i, at: (i, 0))] * len(parts),
        out_specs=pl.BlockSpec((rows, TILE), lambda i, at: (0, i)),
        scalars=(spot,),
        mebibytes=14,
        name="wide",
    )


def loss_kernel(chunks, each, _, *refs):
    res_ref, tea_ref, own_ref = refs[:3]
    received = refs[3 : 3 + chunks * each]
    live_ref, count_ref, grad_out, low_out, loss_out, far_ref = refs[3 + chunks * each :]
    add_received(received, each, far_ref)
    error = res_ref[...] - tea_ref[...] + own_ref[...] + far_ref[...]
    weighted = live_ref[...] * error
    grad = 2.0 * weighted / count_ref[...]
    grad_out[...] = grad
    low_out[...] = grad.astype(bf16)
    sums = jnp.sum(weighted * error, axis=0, keepdims=True)
    sums = jnp.concatenate([sums, jnp.zeros((7, sums.shape[1]), f32)], axis=0)
    loss_out[...] = jnp.where(pl.program_id(0) == 0, sums, loss_out[...] + sums)


def add_received(received, each, far_ref):
    for n in range(len(received) // each):

        @pl.when(pl.program_id(0) == n)
        def _():
            total = received[n * each][...].astype(f32)
            for ref in received[n * each + 1 : (n + 1) * each]:
                total = total + ref[...].astype(f32)
            far_ref[...] = total


def beside_call(parts):
    rows, width = parts[0].shape

    def kernel(*refs):
        for n, ref in enumerate(refs[:-1]):
            refs[-1][:, n * width : (n + 1) * width] = ref[...]

    return plain_call(
        kernel, shaped((rows, width * len(parts)), bf16), *parts, mebibytes=8, name="beside"
    )


def spread_kernel(each, tiles, low_ref, *refs):
    count = len(refs) // (1 + each * tiles)
    outs = refs[count:]
    for n in range(count * each):
        size = refs[0].shape[1] // each
        part = refs[n // each][:, n % each * size : (n % each + 1) * size]
        piece = dot(low_ref[...], part, 1, 0).astype(bf16)
        lanes = size // tiles
        for tile in range(tiles):
            outs[tile * count * each + n][...] = piece[:, tile * lanes : (tile + 1) * lanes]


def spread_call(low, parts, each):
    width = parts[0].shape[1] // each
    lanes = min(128, width)
    count = len(parts) * each
    out = plain_call(
        functools.partial(spread_kernel, each, width // lanes),
        tuple(shaped((low.shape[0], lanes), bf16) for _ in range(count * (width // lanes))),
        low,
        *parts,
        mebibytes=12,
        name="spread",
    )
    return [out[n : n + count] for n in range(0, len(out), count)]


def unproject_kernel(half, spots, grad_ref, part_ref, far_out, near_out):
    piece = dot(grad_ref[...], part_ref[...], 1, 1)

    @pl.when(pl.program_id(0) < half)
    def _():
        far_out[...] = piece.astype(bf16)

    @pl.when(pl.program_id(0) >= half)
    def _():
        near_out[...] = piece


def unproject_call(grads, part, blocks, rows):
    half = len(blocks) // 2
    model, width = part.shape
    return plain_call(
        functools.partial(unproject_kernel, half),
        (shaped((half * rows, model), bf16), shaped((half * rows, model), f32)),
        grads,
        part,
        grid=(len(blocks),),
        in_specs=[
            pl.BlockSpec((rows, width), lambda i, spots: (spots[i], 0)),
            fixed(part.shape),
        ],
        out_specs=(
            pl.BlockSpec((rows, model), lambda i, spots: (jnp.minimum(i, half - 1), 0)),
            pl.BlockSpec((rows, model), lambda i, spots: (jnp.maximum(i - half, 0), 0)),
        ),
        scalars=(jnp.stack(blocks).astype(jnp.int32),),
        mebibytes=48,
        name="unproject",
    )


def outer_proj_kernel(half, _, low_ref, *refs):
    blocks, (far_out, *near) = refs[: 2 * half], refs[2 * half :]
    turned = low_ref[...].astype(f32).T.astype(bf16)
    width = blocks[0].shape[1]
    for n in range(half):
        far_out[:, n * width : (n + 1) * width] = dot(turned, blocks[half + n][...], 1, 0).astype(bf16)
        near[n][...] = dot(turned, blocks[n][...], 1, 0).astype(bf16)


def outer_proj_call(low, blocks, spot):
    rows, model = low.shape
    width = blocks[0].shape[1]
    half = len(blocks) // 2
    own = pl.BlockSpec((rows, width), lambda i, at: (at[0], 0))
    out = plain_call(
        functools.partial(outer_proj_kernel, half),
        (shaped((model, half * width), bf16),) + (shaped((model, width), bf16),) * half,
        low,
        *blocks,
        grid=(1,),
        in_specs=[fixed(low.shape)] + [own] * len(blocks),
        scalars=(spot,),
        mebibytes=14,
        name="outer_proj",
    )
    return out[0], out[1:]


def add_lanes(own, received):
    width = own[0].shape[1]

    def kernel(*refs):
        got = refs[len(own)]
        for n, ref in enumerate(refs[: len(own)]):
            other = got[:, n * width : (n + 1) * width].astype(f32)
            refs[len(own) + 1 + n][...] = (ref[...].astype(f32) + other).astype(bf16)

    return plain_call(
        kernel,
        tuple(shaped(part.shape, bf16) for part in own),
        *own,
        received,
        mebibytes=8,
        name="add_lanes",
    )


def norm_sums(grad, scaled, out_ref, first):
    sums = jnp.concatenate(
        [
            jnp.sum(grad * scaled, axis=0, keepdims=True),
            jnp.sum(grad, axis=0, keepdims=True),
            jnp.zeros((6, grad.shape[1]), f32),
        ],
        axis=0,
    )
    out_ref[...] = jnp.where(first, sums, out_ref[...] + sums)


def middle_kernel(chunks, each, _, *refs):
    grad_ref, received = refs[0], refs[1 : 1 + chunks * each]
    res_ref, gout_ref, par_ref, full_out, low_out, sum_out, far_ref = refs[1 + chunks * each :]
    add_received(received, each, far_ref)
    _, scaled, inverse = norm_forward(res_ref[...], par_ref[2:3, :], par_ref[3:4, :])
    grad = grad_ref[...] + far_ref[...]
    full = gout_ref[...] + norm_backward(grad, scaled, inverse, par_ref[2:3, :])
    full_out[...] = full
    low_out[...] = full.astype(bf16)
    norm_sums(grad, scaled, sum_out, pl.program_id(0) == 0)


def leave_kernel(count, *refs):
    own_ref, received = refs[0], refs[1 : 1 + count]
    tok_ref, res_ref, par_ref, two_ref, loss_ref, out_ref, sum_out, sum_ref = refs[1 + count :]
    _, scaled, inverse = norm_forward(tok_ref[...], par_ref[0:1, :], par_ref[1:2, :])
    grad = own_ref[...]
    for ref in received:
        grad = grad + ref[...].astype(f32)
    out_ref[...] = res_ref[...] + norm_backward(grad, scaled, inverse, par_ref[0:1, :])
    norm_sums(grad, scaled, sum_ref, pl.program_id(0) == 0)
    sum_out[...] = jnp.concatenate(
        [sum_ref[0:2, :], two_ref[0:2, :], loss_ref[0:1, :], jnp.zeros((3, grad.shape[1]), f32)],
        axis=0,
    )


def split_x(parts, n_x, places):
    model = parts[0][0].shape[0]
    slab = model // (N_Z * n_x)
    total = sum(part[0].shape[1] for part in parts)
    flat = [piece for part in parts for piece in part]

    def kernel(at_ref, *refs):
        outs = refs[len(flat) :]
        for dx in range(n_x):
            x = lax.rem(at_ref[1] + dx, n_x)
            for z in range(N_Z):
                at = block_rows(z * n_x + x, slab)
                lane = 0
                used = 0
                for part in parts:
                    value = refs[used][at, :]
                    size = value.shape[1]
                    if len(part) > 1:
                        value = value.astype(f32)
                        for ref in refs[used + 1 : used + len(part)]:
                            value = value + ref[at, :].astype(f32)
                        value = value.astype(bf16)
                    outs[dx][z * slab : (z + 1) * slab, lane : lane + size] = value
                    lane += size
                    used += len(part)

    return plain_call(
        kernel,
        tuple(shaped((model // n_x, total), bf16) for _ in range(n_x)),
        *flat,
        scalars=(places,),
        mebibytes=12,
        name="split_x",
    )


def split_z(parts, places):
    rows, width = parts[0].shape
    slab = rows // N_Z

    def kernel(at_ref, *refs):
        for k, out in enumerate(refs[len(parts) :]):
            at = block_rows(lax.rem(at_ref[0] + k, N_Z), slab)
            total = refs[0][at, :].astype(f32)
            for ref in refs[1 : len(parts)]:
                total = total + ref[at, :].astype(f32)
            out[...] = total.astype(out.dtype)

    shapes = (shaped((slab, width), f32),) + (shaped((slab, width), bf16),) * (N_Z - 1)
    return plain_call(kernel, shapes, *parts, scalars=(places,), mebibytes=8, name="split_z")


def adam_kernel(layout, counts, *refs):
    grads = []
    for count in counts:
        grad = refs[0][...].astype(f32)
        for ref in refs[1:count]:
            grad = grad + ref[...].astype(f32)
        grads.append(grad)
        refs = refs[count:]
    count = len(layout)
    states, outs = refs[: 3 * count], refs[3 * count :]
    for n, (source, start, size, turned) in enumerate(layout):
        weight, first, second = states[3 * n : 3 * n + 3]
        if len(weight.shape) == 3:
            matrices = weight.shape[0]
            lanes = size // matrices
            for k in range(matrices):
                own = [
                    grads[at][:, lane + k * lanes : lane + (k + 1) * lanes] for at, lane in start
                ]
                own = own[0] if len(own) == 1 else jnp.concatenate(own, axis=1)
                new = adam_step(weight[k], own, first[k], second[k], weight_decay, learn_rate)
                for out, value in zip(outs[3 * n : 3 * n + 3], new):
                    out[k] = value
        else:
            part = grads[source][:, start : start + size]
            if turned:
                part = part.T
            new = adam_step(weight[...], part, first[...], second[...], weight_decay, learn_rate)
            for out, value in zip(outs[3 * n : 3 * n + 3], new):
                out[...] = value


def adam_call(groups, layout, *states):
    shapes = tuple(shaped(s.shape, f32) for s in states)
    out = plain_call(
        functools.partial(adam_kernel, layout, [len(group) for group in groups]),
        shapes,
        *[piece for group in groups for piece in group],
        *states,
        mebibytes=16,
        name="adam",
    )
    return [out[3 * n : 3 * n + 3] for n in range(len(layout))]


def tie(*values):
    return lax.optimization_barrier(values)


def local(
    n_x,
    n_y,
    tokens,
    teacher,
    segments,
    live_mask,
    weight_qkv,
    weight_proj,
    weight_up,
    weight_down,
    norm_params,
    first_qkv,
    first_proj,
    first_up,
    first_down,
    first_norms,
    second_qkv,
    second_proj,
    second_up,
    second_down,
    second_norms,
):
    z_at, x_at = lax.axis_index("z"), lax.axis_index("x")
    y_at, core_at = lax.axis_index("y"), lax.axis_index("core")
    rows, model = tokens.shape
    group_rows = segments.shape[0]
    slab = weight_qkv.shape[1]
    width = weight_qkv.shape[2]
    unit = weight_up.shape[1]
    part_rows = min(128, rows)
    wide_rows = min(256, rows)
    depth = N_Z * slab
    sizes = {"z": N_Z, "x": n_x, "y": n_y, "core": N_CORE}
    places = jnp.stack([z_at, x_at]).astype(jnp.int32)
    offsets = [(dc, dy) for dc in range(N_CORE) for dy in range(n_y)]
    other = N_CORE - 1

    def send(value, axis, step):
        size = sizes[axis]
        return lax.ppermute(value, axis, [(i, (i + step) % size) for i in range(size)])

    def send_col(value, dy, dc):
        perm = [
            (y * N_CORE + c, (y + dy) % n_y * N_CORE + (c + dc) % N_CORE)
            for y in range(n_y)
            for c in range(N_CORE)
        ]
        return lax.ppermute(value, ("y", "core"), perm)

    def fetch(value, axis):
        return [value] + [send(value, axis, -k) for k in range(1, sizes[axis])]

    def fetch_z(value):
        return [value] + [send(value, "z", k) for k in range(1, N_Z)]

    def place(dy, dc):
        return ((y_at + dy) % n_y * N_CORE + (core_at + dc) % N_CORE) * rows

    shard_qkv, shard_up, shard_down = plain_call(
        pack_kernel,
        (
            shaped((slab, 4 * width), bf16),
            shaped((slab + DIGITS, unit), bf16),
            shaped((slab, unit), bf16),
        ),
        live_mask.reshape(-1, 128),
        weight_qkv,
        weight_proj,
        weight_up,
        weight_down,
        mebibytes=8,
        name="pack",
    )
    near_qkv = fetch_z(shard_qkv)
    def first_norm(values):
        return plain_call(
            first_kernel,
            shaped(values.shape, bf16),
            values,
            norm_params,
            grid=(rows // part_rows,),
            in_specs=row_blocks(part_rows, model) + [fixed(norm_params.shape)],
            out_specs=row_blocks(part_rows, model)[0],
            mebibytes=8,
            name="first",
        )

    low_one = first_norm(tokens)
    tokens_all = fetch(tokens, "y")
    far_one = send(low_one, "core", -1)
    block_qkv = stack_z(near_qkv, slab, places)
    geometry = attend_geometry(segments, live_mask)
    own_live = lax.dynamic_slice_in_dim(
        live_mask, (y_at * N_CORE + core_at) * rows, rows, 0
    ).astype(f32)[:, None]
    spots_here = jnp.stack([place(dy, dc) for dc, dy in offsets]).astype(jnp.int32)
    spots = jnp.stack([place(-dy, -dc) for dc, dy in offsets]).astype(jnp.int32)
    col_spots = jnp.stack([(y_at + dy) % n_y for dy in range(n_y)]).astype(jnp.int32) * rows
    block_qkv, shard_down, shard_up, far_one, geometry, own_live, spots_here, spots, col_spots = tie(
        block_qkv, shard_down, shard_up, far_one, geometry, own_live, spots_here, spots, col_spots
    )

    beside_qkv = fetch(block_qkv, "x")
    near_up = fetch_z(shard_up)
    beside_qkv, near_up, shard_down, tokens_all = tie(
        beside_qkv, near_up, shard_down, tokens_all
    )

    block_up = stack_z(near_up, slab, places)
    full_qkv, part_proj = weave([[[part] for part in beside_qkv]], [3 * width], slab, places)
    blocks_one = [low_one] + [first_norm(part) for part in tokens_all[1:]]
    blocks_one, block_up, part_proj = tie(blocks_one, block_up, part_proj)
    blocks_one = blocks_one + [far_one] + [send(part, "core", -1) for part in blocks_one[1:]]
    group_one = place_blocks(blocks_one, spots_here)
    tokens_all = place_blocks(tokens_all, col_spots)
    beside_up = fetch(block_up, "x")
    near_down = fetch_z(shard_down)
    full_proj = fetch(part_proj, "y")
    projected = dot(group_one, full_qkv, 1, 0).astype(bf16)
    col_places = [
        (dy * N_CORE + (core_at + dc) % N_CORE) * rows for dc in range(N_CORE) for dy in range(n_y)
    ]
    mixed, bias = attend_forward(
        projected, geometry, jnp.stack(col_places).astype(jnp.int32), n_y * rows
    )
    mixed, beside_up, near_down, full_proj = tie(mixed, beside_up, near_down, full_proj)

    blocks_mixed = [
        mixed[0] if key == (0, 0) else send_col(mixed[key[0]], -key[1], -key[0])
        for key in offsets
    ]
    full_proj = [beside_call(full_proj)]
    full_proj.append(send(full_proj[0], "core", -1))
    beside_down = fetch(stack_z(near_down, slab, places), "x")
    full_up = [weave([[[part] for part in beside_up]], [], slab, places)]
    live_count = sum(
        256.0 * part[depth, 0].astype(f32) + 16.0 * part[depth + 1, 0].astype(f32)
        + part[depth + 2, 0].astype(f32)
        for part in beside_up
    ).reshape(1, 1)
    blocks_mixed, full_proj, full_up, live_count, beside_down, tokens_all = tie(
        blocks_mixed, full_proj, full_up, live_count, beside_down, tokens_all
    )
    full_up.append(send(full_up[0], "core", -1))
    full_down = [weave([[[part] for part in beside_down]], [], slab, places)]
    full_down.append(send(full_down[0], "core", -1))
    count = len(offsets)
    rows_all = n_y * rows
    residual, low_all = plain_call(
        functools.partial(proj_kernel, count, n_y),
        (shaped((rows_all, model), f32), shaped((rows_all, model), bf16)),
        *blocks_mixed,
        *full_proj,
        tokens_all,
        norm_params,
        grid=(rows_all // wide_rows,),
        in_specs=row_blocks(wide_rows, *([width] * count))
        + [fixed(part.shape) for part in full_proj]
        + row_blocks(wide_rows, model)
        + [fixed(norm_params.shape)],
        out_specs=tuple(row_blocks(wide_rows, model, model)),
        mebibytes=18,
        name="proj",
    )

    chunk = min(256, rows)
    chunks = range(rows // chunk)
    neighbours = range(1, n_y)
    each = len(neighbours)

    def spot_of(dy, n):
        return ((y_at + dy) % n_y * (rows // chunk) + n).reshape(1).astype(jnp.int32)

    own_spot = y_at.reshape(1).astype(jnp.int32)
    own_chunks = spot_of(0, 0)

    def cross(value, n):
        piece = value[n * chunk : (n + 1) * chunk]
        return {dy: send(piece, "y", -dy) for dy in neighbours}

    hidden = ()
    far_out = {}
    for n in chunks:
        for dy in neighbours:
            hidden = up_call(low_all, full_up, chunk, spot_of(dy, n), hidden)
        outs = {
            dy: wide_call(hidden[::2], full_down, chunk, spot_of(dy, n), bf16) for dy in neighbours
        }
        outs, hidden = tie(outs, hidden)
        far_out[n] = {dy: send(outs[dy], "y", dy) for dy in neighbours}
    hidden = up_call(low_all, full_up, rows, own_spot, hidden)
    own_out = wide_call(hidden[::2], full_down, rows, own_spot, f32)
    own_out, far_out, hidden = tie(own_out, far_out, hidden)
    far_out = [far_out[n][dy] for n in chunks for dy in neighbours]
    grad_output, grad_branch, loss_rows = plain_call(
        functools.partial(loss_kernel, len(chunks), each),
        (shaped(tokens.shape, f32), shaped(tokens.shape, bf16), shaped((8, model), f32)),
        residual,
        teacher,
        own_out,
        *far_out,
        own_live,
        live_count,
        grid=(len(chunks),),
        in_specs=[pl.BlockSpec((chunk, model), lambda i, at: (at[0] + i, 0))]
        + row_blocks(chunk, model, model)
        + [fixed((chunk, model))] * len(far_out)
        + row_blocks(chunk, 1)
        + [fixed((1, 1))],
        out_specs=tuple(row_blocks(chunk, model, model) + [fixed((8, model))]),
        scratch=[pltpu.VMEM((chunk, model), f32)],
        scalars=(own_chunks,),
        mebibytes=20,
        name="loss",
    )
    active, slope = hidden[::2], hidden[1::2]

    grad_far = {0: cross(grad_branch, 0)}
    grad_hidden = hidden_call(grad_branch, slope, full_down, own_spot, ())
    own_two = wide_call(grad_hidden, full_up, rows, own_spot, f32)
    grad_far[0], grad_hidden, own_two, grad_branch = tie(
        grad_far[0], grad_hidden, own_two, grad_branch
    )
    grad_spots = [y_at * rows] + [
        (y_at + dy) % n_y * rows + n * chunk for dy in neighbours for n in chunks
    ]
    far_two = {}
    for n in chunks:
        if n + 1 in chunks:
            grad_far[n + 1] = cross(grad_branch, n + 1)
        for dy in neighbours:
            grad_hidden = hidden_call(
                grad_far[n][dy], slope, full_down, spot_of(dy, n), grad_hidden
            )
        outs = {
            dy: wide_call(grad_hidden, full_up, chunk, spot_of(dy, n), bf16) for dy in neighbours
        }
        if n + 1 in chunks:
            outs, grad_hidden, grad_far[n + 1] = tie(outs, grad_hidden, grad_far[n + 1])
        else:
            grad_all = place_blocks(
                [grad_branch] + [grad_far[k][dy] for dy in neighbours for k in chunks],
                jnp.stack(grad_spots).astype(jnp.int32),
                chunk,
            )
            far_down = dot(grad_all, active[other], 0, 0).astype(bf16)
            outs, grad_hidden, grad_all, far_down, far_two = tie(
                outs, grad_hidden, grad_all, far_down, far_two
            )
        far_two[n] = {dy: send(outs[dy], "y", dy) for dy in neighbours}

    far_up = dot(low_all, grad_hidden[other], 0, 0).astype(bf16)
    sent_down, sent_up = send(far_down, "core", 1), send(far_up, "core", 1)
    hold_down = (dot(grad_all, active[0], 0, 0) + sent_down.astype(f32)).astype(bf16)
    halves_down = split_x([[hold_down]], n_x, places)
    hold_up = (dot(low_all, grad_hidden[0], 0, 0) + sent_up.astype(f32)).astype(bf16)
    halves_up = split_x([[hold_up]], n_x, places)
    far_two, halves_down, halves_up = tie(far_two, halves_down, halves_up)
    far_two = [far_two[n][dy] for n in chunks for dy in neighbours]
    grad_residual, grad_low, sums_two = plain_call(
        functools.partial(middle_kernel, len(chunks), each),
        (shaped(tokens.shape, f32), shaped(tokens.shape, bf16), shaped((8, model), f32)),
        own_two,
        *far_two,
        residual,
        grad_output,
        norm_params,
        grid=(len(chunks),),
        in_specs=row_blocks(chunk, model)
        + [fixed((chunk, model))] * len(far_two)
        + [pl.BlockSpec((chunk, model), lambda i, at: (at[0] + i, 0))]
        + row_blocks(chunk, model)
        + [fixed(norm_params.shape)],
        out_specs=tuple(row_blocks(chunk, model, model) + [fixed((8, model))]),
        scratch=[pltpu.VMEM((chunk, model), f32)],
        scalars=(own_chunks,),
        mebibytes=20,
        name="middle",
    )
    pieces_attn = spread_call(grad_low, full_proj, n_y)
    pieces_attn, halves_down, halves_up, grad_low = tie(
        pieces_attn, halves_down, halves_up, grad_low
    )

    def send_back(pieces):
        return [
            piece if key == (0, 0) else send_col(piece, key[1], key[0])
            for key, piece in zip(offsets, pieces)
        ]

    def hop_x(halves):
        return [halves[0]] + [send(halves[dx], "x", dx) for dx in range(1, n_x)]

    def spread_z(pieces):
        return [pieces[0]] + [send(pieces[k], "z", k) for k in range(1, N_Z)]

    lanes = 3 * min(128, width)
    tiles = 3 * width // lanes
    sent_attn = send_back(pieces_attn[0])
    parts_down = hop_x(halves_down)
    far_proj, grad_proj = outer_proj_call(grad_low, blocks_mixed, own_spot)
    sent_attn, far_proj, grad_proj = tie(sent_attn, far_proj, grad_proj)

    sent_later = [send_back(pieces) for pieces in pieces_attn[1:]]
    sent_proj = send(far_proj, "core", 1)
    grad_projected = attend_backward(projected, sent_attn, spots, geometry[0], bias, 0, ())
    grad_projected, sent_later, sent_proj, parts_down, halves_up = tie(
        grad_projected, sent_later, sent_proj, parts_down, halves_up
    )

    hold_proj = add_lanes(grad_proj, sent_proj)
    pieces_down = split_z(parts_down, places)
    grad_projected, pieces_down, hold_proj, halves_up = tie(
        grad_projected, pieces_down, hold_proj, halves_up
    )
    parts_up = hop_x(halves_up)
    last_down = spread_z(pieces_down)
    part_proj = [hold_proj[0]] + [send(hold_proj[k], "y", k) for k in range(1, n_y)]
    for tile in range(1, tiles):
        grad_projected = attend_backward(
            projected, sent_later[tile - 1], spots, geometry[0], bias, tile, (grad_projected,)
        )
    grad_projected, parts_up, last_down, part_proj = tie(
        grad_projected, parts_up, last_down, part_proj
    )

    far_one, near_one = unproject_call(
        grad_projected,
        full_qkv,
        [place(dy, dc) // rows for dc in reversed(range(N_CORE)) for dy in range(n_y)],
        rows,
    )
    far_one, grad_projected = tie(far_one, grad_projected)
    sent_one = send(far_one, "core", 1)
    grad_qkv = dot(group_one, grad_projected, 0, 0).astype(bf16)
    halves_qkv = split_x([[grad_qkv], part_proj], n_x, places)
    pieces_up = split_z(parts_up, places)
    halves_qkv, sent_one, near_one, pieces_up = tie(halves_qkv, sent_one, near_one, pieces_up)

    parts = [
        near_one[dy * rows : (dy + 1) * rows] + sent_one[dy * rows : (dy + 1) * rows].astype(f32)
        for dy in range(n_y)
    ]
    sent_parts = [parts[k].astype(bf16) for k in range(1, n_y)]
    halves_qkv, sent_parts, pieces_up = tie(halves_qkv, sent_parts, pieces_up)
    received = [send(part, "y", k) for k, part in enumerate(sent_parts, 1)]
    parts_qkv = hop_x(halves_qkv)
    last_up = spread_z(pieces_up)
    (new_down,) = adam_call(
        [last_down], [(0, 0, unit, True)], weight_down, first_down, second_down
    )
    parts_qkv, received, last_up, new_down = tie(parts_qkv, received, last_up, new_down)

    pieces_qkv = split_z(parts_qkv, places)
    token_grad, sums = plain_call(
        functools.partial(leave_kernel, len(received)),
        (shaped(tokens.shape, f32), shaped((8, model), f32)),
        parts[0],
        *received,
        tokens,
        grad_residual,
        norm_params,
        sums_two,
        loss_rows,
        grid=(rows // part_rows,),
        in_specs=row_blocks(part_rows, *([model] * (3 + len(received))))
        + [fixed(norm_params.shape), fixed((8, model)), fixed((8, model))],
        out_specs=tuple(row_blocks(part_rows, model) + [fixed((8, model))]),
        scratch=[pltpu.VMEM((8, model), f32)],
        mebibytes=14,
        name="leave",
    )
    sums, token_grad, pieces_qkv = tie(sums, token_grad, pieces_qkv)
    last_qkv = spread_z(pieces_qkv)
    for axis in ("core", "y", "x", "z"):
        step = 1
        while step < sizes[axis]:
            pairs = [(i, i ^ step) for i in range(sizes[axis])]
            sums = sums + lax.ppermute(sums, axis, pairs)
            step *= 2
    (new_up,) = adam_call([last_up], [(0, 0, unit, False)], weight_up, first_up, second_up)
    sums, last_qkv, new_up = tie(sums, last_qkv, new_up)
    loss_sum = jnp.sum(sums[4])
    live_count = live_count[0, 0]

    new_qkv, new_proj = adam_call(
        [last_qkv],
        [(0, [(0, n * lanes) for n in range(tiles)], lanes, False), (0, 3 * width, width, True)],
        weight_qkv,
        first_qkv,
        second_qkv,
        weight_proj,
        first_proj,
        second_proj,
    )
    new_norms = adam_step(norm_params, sums[:4], first_norms, second_norms, 0.0, norm_rate)
    return (
        loss_sum / live_count,
        token_grad,
        new_qkv[0],
        new_proj[0],
        new_up[0],
        new_down[0],
        new_norms[0],
        new_qkv[1],
        new_proj[1],
        new_up[1],
        new_down[1],
        new_norms[1],
        new_qkv[2],
        new_proj[2],
        new_up[2],
        new_down[2],
        new_norms[2],
    )


def solution(mesh):
    n_x = mesh.shape["row"] // N_Z
    n_y = mesh.shape["col"] // N_CORE
    mesh = jax.sharding.Mesh(
        mesh.devices.reshape(N_Z, n_x, n_y, N_CORE), ("z", "x", "y", "core")
    )
    row, col = ("z", "x"), ("y", "core")
    matrices = (P(None, row, col), P(col, row), P(row, col), P(col, row), P())
    tokens = P(row + col, None)
    return jax.shard_map(
        functools.partial(local, n_x, n_y),
        mesh=mesh,
        in_specs=(tokens, tokens, P(row), P(row)) + matrices * 3,
        out_specs=(P(), tokens) + matrices * 3,
        check_vma=False,
    )
```

```python
import functools

import jax
import jax.numpy as jnp
from jax import lax
from jax.experimental import pallas as pl
from jax.experimental.pallas import tpu as pltpu
from jax.sharding import PartitionSpec as P

HEAD_DIM = 64
PATCHES = 577
STEP = 10
WINDOW = 640
QROWS = 320
TILE = 256
DIGITS = 16
SMALL = pl.CostEstimate(flops=1024, bytes_accessed=1024, transcendentals=0)
N_Z = 4
N_CORE = 2

layer_eps = 1e-06
adam_eps = 1e-08
learn_rate = 0.03
norm_rate = 0.25
moment_decay = 0.5
weight_decay = 0.05

bf16 = jnp.bfloat16
f32 = jnp.float32


def norm_forward(values, gain_row, bias_row):
    average = jnp.mean(values, axis=-1, keepdims=True)
    centred = values - average
    variance = jnp.mean(centred * centred, axis=-1, keepdims=True)
    inverse = lax.rsqrt(variance + layer_eps)
    scaled = centred * inverse
    return (scaled * gain_row + bias_row, scaled, inverse)


def norm_backward(upstream, scaled, inverse, gain_row):
    weighted = upstream * gain_row
    return inverse * (
        weighted
        - jnp.mean(weighted, axis=-1, keepdims=True)
        - scaled * jnp.mean(weighted * scaled, axis=-1, keepdims=True)
    )


def gelu_slope(hidden):
    return (
        0.5 * (1.0 + lax.erf(hidden * 0.7071067811865476))
        + hidden * jnp.exp(-0.5 * hidden * hidden) * 0.3989422804014327
    )


def adam_step(weight, gradient, momentum, variance, decay_rate, rate):
    momentum = moment_decay * momentum + (1.0 - moment_decay) * gradient
    variance = moment_decay * variance + (1.0 - moment_decay) * gradient * gradient
    correction = 1.0 - moment_decay**STEP
    direction = momentum / correction / (jnp.sqrt(variance / correction) + adam_eps)
    return (weight - rate * (direction + decay_rate * weight), momentum, variance)


def dot(left, right, left_dim, right_dim):
    return lax.dot_general(
        left, right, (((left_dim,), (right_dim,)), ((), ())), preferred_element_type=f32
    )


def head_lanes(width, head):
    lanes = lax.broadcasted_iota(jnp.int32, (1, width), 1)
    return (lanes >= head * HEAD_DIM) & (lanes < (head + 1) * HEAD_DIM)


def attend_scores(q_part, k_all, mask):
    scores = dot(q_part, k_all, 1, 1) + mask
    weights = jnp.exp(scores - jnp.max(scores, axis=-1, keepdims=True))
    return weights, jnp.sum(weights, axis=-1, keepdims=True)


def image_window(begin, group_rows):
    image = pl.program_id(0)
    start = jnp.minimum(begin[image] // 16 * 16, group_rows - WINDOW)
    first = begin[image] - start
    return image, pl.multiple_of(start, 16), first


def fill_mask(bias, mask_ref):
    for row in range(0, WINDOW, 128):
        rows = row + lax.broadcasted_iota(jnp.int32, (128, WINDOW), 0)
        cols = lax.broadcasted_iota(jnp.int32, (128, WINDOW), 1)
        mask_ref[row : row + 128, :] = jnp.where(rows == cols, 0.0, bias)


def rows_inside(rows, row_start, first):
    ids = row_start + lax.broadcasted_iota(jnp.int32, (rows, 1), 0)
    return (ids >= first) & (ids < first + PATCHES)


def attend_forward_kernel(blocks, begin, spots, code_ref, *refs):
    bias_out, out_ref, mask_ref = refs[-3:]
    image, start, first = image_window(begin, refs[0].shape[0])
    code = code_ref[pl.ds(start, WINDOW), :]
    bias = jnp.where(code == image, 0.0, -1e30).astype(f32).T
    bias_out[0] = bias[0:8, :]
    fill_mask(bias[0:1, :], mask_ref)
    lanes = refs[0].shape[1]

    for tile in range((len(refs) - 3 - blocks) // 3):
        q_ref, k_ref, v_ref = refs[3 * tile : 3 * tile + 3]
        cols = slice(tile * lanes, (tile + 1) * lanes)

        @pl.when(image == 0)
        def _():
            out_ref[:, cols] = v_ref[...]

        k_all = k_ref[pl.ds(start, WINDOW), :]
        v_all = v_ref[pl.ds(start, WINDOW), :]
        for row in range(0, WINDOW, QROWS):
            at = pl.ds(pl.multiple_of(start + row, 16), QROWS)
            q_part = q_ref[at, :] * jnp.asarray(HEAD_DIM ** (-0.5), bf16)
            inside = rows_inside(QROWS, row, first)
            mixed = None
            for head in range(lanes // HEAD_DIM):
                mine = head_lanes(lanes, head)
                q_head = jnp.where(mine, q_part, jnp.zeros_like(q_part))
                weights, totals = attend_scores(q_head, k_all, mask_ref[row : row + QROWS, :])
                part = dot(weights.astype(bf16), v_all, 1, 0) * (1.0 / totals)
                mixed = part if mixed is None else jnp.where(mine, part, mixed)
            out_ref[at, cols] = jnp.where(inside, mixed.astype(bf16), out_ref[at, cols])

    @pl.when(image == pl.num_programs(0) - 1)
    def _():
        for n, block in enumerate(refs[-3 - blocks : -3]):
            rows = block.shape[0]
            block[...] = out_ref[pl.ds(pl.multiple_of(spots[n], rows), rows), :]


def attend_backward_kernel(blocks, begin, spots, bias_ref, *refs):
    out_ref, p_ref, s_ref, go_ref, mask_ref = refs[-5:]
    go_blocks, refs = refs[3 : 3 + blocks], refs[:3]
    image, start, first = image_window(begin, refs[0].shape[0])
    fill_mask(bias_ref[0, 0:1, :], mask_ref)
    lanes = refs[0].shape[1]
    rows = go_blocks[0].shape[0]
    whole = pl.ds(start, WINDOW)
    inside_all = rows_inside(WINDOW, 0, first)

    @pl.when(image == 0)
    def _():
        for n, block_ref in enumerate(go_blocks):
            go_ref[pl.ds(pl.multiple_of(spots[n], rows), rows), :] = block_ref[...]

    for tile in range(len(refs) // 3):
        q_ref, k_ref, v_ref = refs[3 * tile : 3 * tile + 3]
        cols = slice(tile * lanes, (tile + 1) * lanes)
        base = 3 * tile * lanes
        q_cols, k_cols, v_cols = [
            slice(base + n * lanes, base + (n + 1) * lanes) for n in range(3)
        ]

        @pl.when(image == 0)
        def _():
            out_ref[:, base : base + 2 * lanes] = jnp.zeros((out_ref.shape[0], 2 * lanes), bf16)
            out_ref[:, v_cols] = go_ref[:, cols]

        k_all = k_ref[whole, :]
        v_all = v_ref[whole, :]
        q_all = q_ref[whole, :] * jnp.asarray(HEAD_DIM ** (-0.5), bf16)
        go_all = go_ref[whole, cols]
        key_grad = None
        value_grad = None
        for head in range(lanes // HEAD_DIM):
            mine = head_lanes(lanes, head)
            q_mine = jnp.where(mine, q_all, jnp.zeros_like(q_all))
            go_mine = jnp.where(mine, go_all, jnp.zeros_like(go_all))
            for row in range(0, WINDOW, QROWS):
                part = slice(row, row + QROWS)
                at = pl.ds(pl.multiple_of(start + row, 16), QROWS)
                inside = rows_inside(QROWS, row, first)
                weights, totals = attend_scores(q_mine[part], k_all, mask_ref[part, :])
                weights = weights * jnp.where(inside, 1.0 / totals, 0.0)
                weight_grad = dot(go_mine[part], v_all, 1, 1)
                product = weights * weight_grad
                score_grad = (
                    product - weights * jnp.sum(product, axis=-1, keepdims=True)
                ).astype(bf16)
                p_ref[part, :] = weights.astype(bf16)
                s_ref[part, :] = score_grad
                query_grad = (dot(score_grad, k_all, 1, 0) * HEAD_DIM ** (-0.5)).astype(bf16)
                out_ref[at, q_cols] = jnp.where(inside & mine, query_grad, out_ref[at, q_cols])
            key_part = dot(q_mine, s_ref[...], 0, 0)
            value_part = dot(go_mine, p_ref[...], 0, 0)
            key_grad = key_part if key_grad is None else key_grad + key_part
            value_grad = value_part if value_grad is None else value_grad + value_part
        key_rows = key_grad.T.astype(bf16)
        value_rows = value_grad.T.astype(bf16)
        out_ref[whole, k_cols] = jnp.where(inside_all, key_rows, out_ref[whole, k_cols])
        out_ref[whole, v_cols] = jnp.where(inside_all, value_rows, out_ref[whole, v_cols])


def qkv_operands(projected, tile):
    group_rows, total = projected.shape
    lanes = min(128, total // 3)
    if lanes % 128 == 0:
        specs = [
            pl.BlockSpec((group_rows, lanes), functools.partial(lambda n, i, *_: (0, n), 3 * tile + n))
            for n in range(3)
        ]
        return [projected] * 3, specs
    parts = [projected[:, n * lanes : (n + 1) * lanes] for n in range(3)]
    return parts, [fixed((group_rows, lanes))] * 3


def all_operands(projected):
    width = projected.shape[1] // 3
    operands, specs = [], []
    for tile in range(width // min(128, width)):
        more, places = qkv_operands(projected, tile)
        operands += more
        specs += places
    return operands, specs


def attend_forward(projected, geometry, spots, rows):
    begin, code = geometry
    group_rows, total = projected.shape
    width = total // 3
    blocks = group_rows // rows
    images = begin.shape[0]
    operands, specs = all_operands(projected)
    out = plain_call(
        functools.partial(attend_forward_kernel, blocks),
        (shaped((rows, width), bf16),) * blocks + (shaped((images, 8, WINDOW), f32),),
        code,
        *operands,
        grid=begin.shape,
        in_specs=[fixed(code.shape)] + specs,
        out_specs=(fixed((rows, width)),) * blocks
        + (pl.BlockSpec((1, 8, WINDOW), lambda i, *_: (i, 0, 0)),),
        scratch=[pltpu.VMEM((group_rows, width), bf16), pltpu.VMEM((WINDOW, WINDOW), f32)],
        scalars=(begin, spots),
        mebibytes=20,
        name="attention_forward",
    )
    return out[:blocks], out[blocks]


def attend_backward(projected, go_blocks, spots, begin, bias, tile, into):
    group_rows, total = projected.shape
    lanes = min(128, total // 3)
    operands, specs = qkv_operands(projected, tile)
    return plain_call(
        functools.partial(attend_backward_kernel, len(go_blocks)),
        shaped((group_rows, total), bf16),
        bias,
        *operands,
        *go_blocks,
        grid=begin.shape,
        in_specs=[pl.BlockSpec((1, 8, WINDOW), lambda i, *_: (i, 0, 0))]
        + specs
        + [fixed(block.shape) for block in go_blocks],
        out_specs=pl.BlockSpec((group_rows, 3 * lanes), lambda i, *_: (0, tile)),
        scratch=[pltpu.VMEM((WINDOW, WINDOW), bf16)] * 2
        + [pltpu.VMEM((group_rows, lanes), bf16), pltpu.VMEM((WINDOW, WINDOW), f32)],
        scalars=(begin, spots),
        into=into,
        mebibytes=56 if into else 16,
        name="attention_backward",
    )


def attend_geometry(segments, live_mask):
    group_rows = segments.shape[0]
    numbers = jnp.arange(group_rows // PATCHES, dtype=jnp.int32)
    positions = jnp.arange(group_rows, dtype=jnp.int32)
    begin = jnp.min(
        jnp.where(segments[None, :] == numbers[:, None], positions[None, :], group_rows - PATCHES),
        axis=1,
    )
    code = jnp.where(live_mask == 1, segments, -1)
    return begin, jnp.broadcast_to(code[:, None], (group_rows, 128))


def plain_call(kernel, out_shape, *operands, grid=(), in_specs=None, out_specs=None, scratch=(), scalars=(), into=(), mebibytes=16, name=None):
    params = pltpu.CompilerParams(vmem_limit_bytes=mebibytes * 1024 * 1024)
    if in_specs is None:
        in_specs = [pl.BlockSpec(a.shape, functools.partial(lambda n, *_: (0,) * n, a.ndim)) for a in operands]
    in_specs = list(in_specs) + [pl.BlockSpec(memory_space=pl.ANY)] * len(into)
    if out_specs is None:
        out_specs = jax.tree.map(
            lambda s: pl.BlockSpec(s.shape, functools.partial(lambda n, *_: (0,) * n, len(s.shape))), out_shape
        )
    return pl.pallas_call(
        kernel,
        grid_spec=pltpu.PrefetchScalarGridSpec(
            num_scalar_prefetch=len(scalars),
            grid=grid,
            in_specs=in_specs,
            out_specs=out_specs,
            scratch_shapes=list(scratch),
        ),
        out_shape=out_shape,
        input_output_aliases={len(scalars) + len(operands) + n: n for n in range(len(into))},
        compiler_params=params,
        cost_estimate=SMALL,
        name=name,
    )(*scalars, *operands, *into)


def shaped(shape, dtype):
    return jax.ShapeDtypeStruct(tuple(shape), dtype)


def row_blocks(rows, *widths):
    return [pl.BlockSpec((rows, w), lambda i, *_: (i, 0)) for w in widths]


def fixed(shape):
    return pl.BlockSpec(tuple(shape), functools.partial(lambda n, *_: (0,) * n, len(shape)))


def pack_kernel(live_ref, qkv_ref, proj_ref, up_ref, down_ref, qkv_out, up_out, down_out):
    count, slab, width = qkv_ref.shape
    lanes = min(128, width)
    for n in range(count):
        for t in range(width // lanes):
            at = (count * t + n) * lanes
            qkv_out[:, at : at + lanes] = qkv_ref[n][:, t * lanes : (t + 1) * lanes].astype(bf16)
    qkv_out[:, count * width :] = proj_ref[...].T.astype(bf16)
    up_out[:slab, :] = up_ref[...].astype(bf16)
    live = jnp.sum(jnp.sum(live_ref[...].astype(f32), axis=0, keepdims=True), axis=1, keepdims=True)
    high = jnp.floor(live * (1.0 / 256.0))
    middle = jnp.floor(live * (1.0 / 16.0)) - 16.0 * high
    low = live - 256.0 * high - 16.0 * middle
    row = lax.broadcasted_iota(jnp.int32, (DIGITS, up_out.shape[1]), 0)
    digits = jnp.where(row == 0, high, jnp.where(row == 1, middle, jnp.where(row == 2, low, 0.0)))
    up_out[slab:, :] = digits.astype(bf16)
    down_out[...] = down_ref[...].T.astype(bf16)


def first_kernel(tok_ref, par_ref, low_out):
    normed, _, _ = norm_forward(tok_ref[...], par_ref[0:1, :], par_ref[1:2, :])
    low_out[...] = normed.astype(bf16)


def place_blocks(blocks, spots):
    rows, width = blocks[0].shape

    def kernel(spot_ref, *refs):
        for n, ref in enumerate(refs[:-1]):
            refs[-1][pl.ds(pl.multiple_of(spot_ref[n], rows), rows), :] = ref[...]

    return plain_call(
        kernel,
        shaped((rows * len(blocks), width), bf16),
        *blocks,
        scalars=(spots,),
        mebibytes=20,
        name="place_blocks",
    )


def block_rows(block, slab):
    return pl.ds(pl.multiple_of(block * slab, slab), slab)


def stack_z(pieces, slab, places, count=1):
    height, width = pieces[0].shape
    extra = height - slab
    shapes = (shaped((N_Z * slab // count + extra, width), bf16),) * count

    def kernel(at_ref, *refs):
        held = refs[-1]
        for k, ref in enumerate(refs[:N_Z]):
            held[block_rows(lax.rem(at_ref[0] + N_Z - k, N_Z), slab), :] = ref[:slab, :]
        for n, out in enumerate(refs[N_Z:-1]):
            rows = N_Z * slab // count
            out[:rows, :] = held[n * rows : (n + 1) * rows, :]
            if extra:
                digits = refs[0][slab:, :].astype(f32)
                for ref in refs[1:N_Z]:
                    digits = digits + ref[slab:, :].astype(f32)
                out[rows:, :] = digits.astype(bf16)

    out = plain_call(
        kernel,
        shapes,
        *pieces,
        scalars=(places,),
        scratch=[pltpu.VMEM((N_Z * slab, width), bf16)],
        mebibytes=8,
        name="stack_z",
    )
    return out if count > 1 else out[0]


def weave(columns, cuts, slab, places):
    n_x = len(columns[0])
    width = columns[0][0][0].shape[1]
    flat = [piece for column in columns for half in column for piece in half]
    edges = [0, *cuts, width]
    sizes = [stop - start for start, stop in zip(edges[:-1], edges[1:])]

    def kernel(at_ref, *refs):
        outs = refs[len(flat) :]
        used = 0
        for y, column in enumerate(columns):
            for dx, half in enumerate(column):
                x = lax.rem(at_ref[1] + dx, n_x)
                share = N_Z // len(half)
                for z in range(N_Z):
                    piece = refs[used + z // share]
                    at = block_rows(z * n_x + x, slab)
                    row = z % share * slab
                    for out, start, size in zip(outs, edges, sizes):
                        out[at, y * size : (y + 1) * size] = piece[
                            row : row + slab, start : start + size
                        ]
                used += len(half)

    out = plain_call(
        kernel,
        tuple(shaped((N_Z * n_x * slab, size * len(columns)), bf16) for size in sizes),
        *flat,
        scalars=(places,),
        mebibytes=12,
        name="weave",
    )
    return out if cuts else out[0]


def proj_kernel(count, each, *refs):
    blocks, parts = refs[:count], refs[count : count + count // each]
    tok_ref, par_ref, res_out, low_out = refs[count + count // each :]
    total = tok_ref[...]
    for n, block in enumerate(blocks):
        size = block.shape[1]
        part = parts[n // each][:, n % each * size : (n % each + 1) * size]
        total = total + dot(block[...], part, 1, 1)
    res_out[...] = total
    normed, _, _ = norm_forward(total, par_ref[2:3, :], par_ref[3:4, :])
    low_out[...] = normed.astype(bf16)


ERF_TOP = (
    -2.72614225801306e-10,
    2.77068142495902e-08,
    -2.10102402082508e-06,
    -5.69250639462346e-05,
    -7.34990630326855e-04,
    -2.95459980854025e-03,
    -1.60960333262415e-02,
)
ERF_LOW = (
    -1.45660718464996e-05,
    -2.13374055278905e-04,
    -1.68282697438203e-03,
    -7.37332916720468e-03,
    -1.42647390514189e-02,
)


def erf(value):
    value = jnp.clip(value, -4.0, 4.0)
    square = value * value
    top = jnp.full_like(square, ERF_TOP[0])
    for number in ERF_TOP[1:]:
        top = top * square + number
    low = jnp.full_like(square, ERF_LOW[0])
    for number in ERF_LOW[1:]:
        low = low * square + number
    inverse = pl.reciprocal(low, approx=True)
    inverse = inverse * (2.0 - low * inverse)
    return value * top * inverse


def up_kernel(count, low_ref, *refs):
    outs = refs[-2 * count :]
    for n, part in enumerate(refs[:count]):
        hidden = dot(low_ref[...], part[...], 1, 0)
        share = 0.5 * (1.0 + erf(hidden * 0.7071067811865476))
        outs[2 * n][...] = (hidden * share).astype(bf16)
        slope = share + hidden * jnp.exp(-0.5 * hidden * hidden) * 0.3989422804014327
        outs[2 * n + 1][...] = slope.astype(bf16)


def up_call(low, parts, rows_all, spot, into):
    rows, model = low.shape
    width = parts[0].shape[1]
    cols = pl.BlockSpec((rows, TILE), lambda i, *_: (spot, i))
    return plain_call(
        functools.partial(up_kernel, len(parts)),
        (shaped((rows_all, width), bf16),) * (2 * len(parts)),
        low,
        *parts,
        grid=(width // TILE,),
        in_specs=[fixed(low.shape)] + [pl.BlockSpec((model, TILE), lambda i, *_: (0, i))] * len(parts),
        out_specs=(cols,) * (2 * len(parts)),
        into=into,
        mebibytes=14,
        name="up",
    )


def hidden_kernel(count, low_ref, *refs):
    outs = refs[-count:]
    for n in range(count):
        slope, part = refs[n], refs[count + n]
        outs[n][...] = (dot(low_ref[...], part[...], 1, 0) * slope[...].astype(f32)).astype(bf16)


def hidden_call(low, slopes, parts, spot, into):
    rows, model = low.shape
    width = parts[0].shape[1]
    cols = pl.BlockSpec((rows, TILE), lambda i, *_: (spot, i))
    return plain_call(
        functools.partial(hidden_kernel, len(parts)),
        tuple(shaped(slope.shape, bf16) for slope in slopes),
        low,
        *slopes,
        *parts,
        grid=(width // TILE,),
        in_specs=[fixed(low.shape)]
        + [cols] * len(parts)
        + [pl.BlockSpec((model, TILE), lambda i, *_: (0, i))] * len(parts),
        out_specs=(cols,) * len(parts),
        into=into,
        mebibytes=14,
        name="hidden",
    )


def wide_kernel(count, *refs):
    total = dot(refs[0][...], refs[count][...], 1, 1)
    for n in range(1, count):
        total = total + dot(refs[n][...], refs[count + n][...], 1, 1)
    refs[-1][...] = total.astype(refs[-1].dtype)


def wide_call(values, parts, rows, spot, kind):
    model, width = parts[0].shape
    return plain_call(
        functools.partial(wide_kernel, len(values)),
        shaped((rows, model), kind),
        *values,
        *parts,
        grid=(model // TILE,),
        in_specs=[pl.BlockSpec((rows, width), lambda i, *_: (spot, 0))] * len(values)
        + [pl.BlockSpec((TILE, width), lambda i, *_: (i, 0))] * len(parts),
        out_specs=pl.BlockSpec((rows, TILE), lambda i, *_: (0, i)),
        mebibytes=14,
        name="wide",
    )


def loss_kernel(chunks, each, *refs):
    res_ref, tea_ref, own_ref = refs[:3]
    received = refs[3 : 3 + chunks * each]
    live_ref, count_ref, grad_out, low_out, loss_out, far_ref = refs[3 + chunks * each :]
    add_received(received, each, far_ref)
    error = res_ref[...] - tea_ref[...] + own_ref[...] + far_ref[...]
    weighted = live_ref[...] * error
    grad = 2.0 * weighted / count_ref[...]
    grad_out[...] = grad
    low_out[...] = grad.astype(bf16)
    sums = jnp.sum(weighted * error, axis=0, keepdims=True)
    sums = jnp.concatenate([sums, jnp.zeros((7, sums.shape[1]), f32)], axis=0)
    loss_out[...] = jnp.where(pl.program_id(0) == 0, sums, loss_out[...] + sums)


def add_received(received, each, far_ref):
    for n in range(len(received) // each):

        @pl.when(pl.program_id(0) == n)
        def _():
            total = received[n * each][...].astype(f32)
            for ref in received[n * each + 1 : (n + 1) * each]:
                total = total + ref[...].astype(f32)
            far_ref[...] = total


def beside_call(parts):
    rows, width = parts[0].shape

    def kernel(*refs):
        for n, ref in enumerate(refs[:-1]):
            refs[-1][:, n * width : (n + 1) * width] = ref[...]

    return plain_call(
        kernel, shaped((rows, width * len(parts)), bf16), *parts, mebibytes=8, name="beside"
    )


def spread_kernel(each, tiles, low_ref, *refs):
    count = len(refs) // (1 + each * tiles)
    outs = refs[count:]
    for n in range(count * each):
        size = refs[0].shape[1] // each
        part = refs[n // each][:, n % each * size : (n % each + 1) * size]
        piece = dot(low_ref[...], part, 1, 0).astype(bf16)
        lanes = size // tiles
        for tile in range(tiles):
            outs[tile * count * each + n][...] = piece[:, tile * lanes : (tile + 1) * lanes]


def spread_call(low, parts, each):
    width = parts[0].shape[1] // each
    lanes = min(128, width)
    count = len(parts) * each
    out = plain_call(
        functools.partial(spread_kernel, each, width // lanes),
        tuple(shaped((low.shape[0], lanes), bf16) for _ in range(count * (width // lanes))),
        low,
        *parts,
        mebibytes=12,
        name="spread",
    )
    return [out[n : n + count] for n in range(0, len(out), count)]


def unproject_kernel(half, spots, grad_ref, part_ref, far_out, near_out):
    piece = dot(grad_ref[...], part_ref[...], 1, 1)

    @pl.when(pl.program_id(0) < half)
    def _():
        far_out[...] = piece.astype(bf16)

    @pl.when(pl.program_id(0) >= half)
    def _():
        near_out[...] = piece


def unproject_call(grads, part, blocks, rows):
    half = len(blocks) // 2
    model, width = part.shape
    return plain_call(
        functools.partial(unproject_kernel, half),
        (shaped((half * rows, model), bf16), shaped((half * rows, model), f32)),
        grads,
        part,
        grid=(len(blocks),),
        in_specs=[
            pl.BlockSpec((rows, width), lambda i, spots: (spots[i], 0)),
            fixed(part.shape),
        ],
        out_specs=(
            pl.BlockSpec((rows, model), lambda i, spots: (jnp.minimum(i, half - 1), 0)),
            pl.BlockSpec((rows, model), lambda i, spots: (jnp.maximum(i - half, 0), 0)),
        ),
        scalars=(jnp.stack(blocks).astype(jnp.int32),),
        mebibytes=48,
        name="unproject",
    )


def outer_proj_kernel(half, low_ref, *refs):
    blocks, (far_out, *near) = refs[: 2 * half], refs[2 * half :]
    turned = low_ref[...].astype(f32).T.astype(bf16)
    width = blocks[0].shape[1]
    for n in range(half):
        far_out[:, n * width : (n + 1) * width] = dot(turned, blocks[half + n][...], 1, 0).astype(bf16)
        near[n][...] = dot(turned, blocks[n][...], 1, 0).astype(bf16)


def outer_proj_call(low, blocks):
    model = low.shape[1]
    width = blocks[0].shape[1]
    half = len(blocks) // 2
    out = plain_call(
        functools.partial(outer_proj_kernel, half),
        (shaped((model, half * width), bf16),) + (shaped((model, width), bf16),) * half,
        low,
        *blocks,
        mebibytes=14,
        name="outer_proj",
    )
    return out[0], out[1:]


def add_lanes(own, received):
    width = own[0].shape[1]

    def kernel(*refs):
        got = refs[len(own)]
        for n, ref in enumerate(refs[: len(own)]):
            other = got[:, n * width : (n + 1) * width].astype(f32)
            refs[len(own) + 1 + n][...] = (ref[...].astype(f32) + other).astype(bf16)

    return plain_call(
        kernel,
        tuple(shaped(part.shape, bf16) for part in own),
        *own,
        received,
        mebibytes=8,
        name="add_lanes",
    )


def norm_sums(grad, scaled, out_ref, first):
    sums = jnp.concatenate(
        [
            jnp.sum(grad * scaled, axis=0, keepdims=True),
            jnp.sum(grad, axis=0, keepdims=True),
            jnp.zeros((6, grad.shape[1]), f32),
        ],
        axis=0,
    )
    out_ref[...] = jnp.where(first, sums, out_ref[...] + sums)


def middle_kernel(chunks, each, *refs):
    grad_ref, received = refs[0], refs[1 : 1 + chunks * each]
    res_ref, gout_ref, par_ref, full_out, low_out, sum_out, far_ref = refs[1 + chunks * each :]
    add_received(received, each, far_ref)
    _, scaled, inverse = norm_forward(res_ref[...], par_ref[2:3, :], par_ref[3:4, :])
    grad = grad_ref[...] + far_ref[...]
    full = gout_ref[...] + norm_backward(grad, scaled, inverse, par_ref[2:3, :])
    full_out[...] = full
    low_out[...] = full.astype(bf16)
    norm_sums(grad, scaled, sum_out, pl.program_id(0) == 0)


def leave_kernel(count, *refs):
    own_ref, received = refs[0], refs[1 : 1 + count]
    tok_ref, res_ref, par_ref, two_ref, loss_ref, out_ref, sum_out, sum_ref = refs[1 + count :]
    _, scaled, inverse = norm_forward(tok_ref[...], par_ref[0:1, :], par_ref[1:2, :])
    grad = own_ref[...]
    for ref in received:
        grad = grad + ref[...].astype(f32)
    out_ref[...] = res_ref[...] + norm_backward(grad, scaled, inverse, par_ref[0:1, :])
    norm_sums(grad, scaled, sum_ref, pl.program_id(0) == 0)
    sum_out[...] = jnp.concatenate(
        [sum_ref[0:2, :], two_ref[0:2, :], loss_ref[0:1, :], jnp.zeros((3, grad.shape[1]), f32)],
        axis=0,
    )


def split_x(parts, n_x, places):
    model = parts[0][0].shape[0]
    slab = model // (N_Z * n_x)
    total = sum(part[0].shape[1] for part in parts)
    flat = [piece for part in parts for piece in part]

    def kernel(at_ref, *refs):
        outs = refs[len(flat) :]
        for dx in range(n_x):
            x = lax.rem(at_ref[1] + dx, n_x)
            for z in range(N_Z):
                at = block_rows(z * n_x + x, slab)
                lane = 0
                used = 0
                for part in parts:
                    value = refs[used][at, :]
                    size = value.shape[1]
                    if len(part) > 1:
                        value = value.astype(f32)
                        for ref in refs[used + 1 : used + len(part)]:
                            value = value + ref[at, :].astype(f32)
                        value = value.astype(bf16)
                    outs[dx][z * slab : (z + 1) * slab, lane : lane + size] = value
                    lane += size
                    used += len(part)

    return plain_call(
        kernel,
        tuple(shaped((model // n_x, total), bf16) for _ in range(n_x)),
        *flat,
        scalars=(places,),
        mebibytes=12,
        name="split_x",
    )


def split_z(parts, places):
    rows, width = parts[0].shape
    slab = rows // N_Z

    def kernel(at_ref, *refs):
        for k, out in enumerate(refs[len(parts) :]):
            at = block_rows(lax.rem(at_ref[0] + k, N_Z), slab)
            total = refs[0][at, :].astype(f32)
            for ref in refs[1 : len(parts)]:
                total = total + ref[at, :].astype(f32)
            out[...] = total.astype(out.dtype)

    shapes = (shaped((slab, width), f32),) + (shaped((slab, width), bf16),) * (N_Z - 1)
    return plain_call(kernel, shapes, *parts, scalars=(places,), mebibytes=8, name="split_z")


def adam_kernel(layout, counts, *refs):
    grads = []
    for count in counts:
        grad = refs[0][...].astype(f32)
        for ref in refs[1:count]:
            grad = grad + ref[...].astype(f32)
        grads.append(grad)
        refs = refs[count:]
    count = len(layout)
    states, outs = refs[: 3 * count], refs[3 * count :]
    for n, (source, start, size, turned) in enumerate(layout):
        weight, first, second = states[3 * n : 3 * n + 3]
        if len(weight.shape) == 3:
            matrices = weight.shape[0]
            lanes = size // matrices
            for k in range(matrices):
                own = [
                    grads[at][:, lane + k * lanes : lane + (k + 1) * lanes] for at, lane in start
                ]
                own = own[0] if len(own) == 1 else jnp.concatenate(own, axis=1)
                new = adam_step(weight[k], own, first[k], second[k], weight_decay, learn_rate)
                for out, value in zip(outs[3 * n : 3 * n + 3], new):
                    out[k] = value
        else:
            part = grads[source][:, start : start + size]
            if turned:
                part = part.T
            new = adam_step(weight[...], part, first[...], second[...], weight_decay, learn_rate)
            for out, value in zip(outs[3 * n : 3 * n + 3], new):
                out[...] = value


def adam_call(groups, layout, *states):
    shapes = tuple(shaped(s.shape, f32) for s in states)
    out = plain_call(
        functools.partial(adam_kernel, layout, [len(group) for group in groups]),
        shapes,
        *[piece for group in groups for piece in group],
        *states,
        mebibytes=16,
        name="adam",
    )
    return [out[3 * n : 3 * n + 3] for n in range(len(layout))]


def tie(*values):
    return lax.optimization_barrier(values)


def local(
    n_x,
    n_y,
    tokens,
    teacher,
    segments,
    live_mask,
    weight_qkv,
    weight_proj,
    weight_up,
    weight_down,
    norm_params,
    first_qkv,
    first_proj,
    first_up,
    first_down,
    first_norms,
    second_qkv,
    second_proj,
    second_up,
    second_down,
    second_norms,
):
    z_at, x_at = lax.axis_index("z"), lax.axis_index("x")
    y_at, core_at = lax.axis_index("y"), lax.axis_index("core")
    rows, model = tokens.shape
    group_rows = segments.shape[0]
    slab = weight_qkv.shape[1]
    width = weight_qkv.shape[2]
    unit = weight_up.shape[1]
    part_rows = min(128, rows)
    wide_rows = min(256, rows)
    depth = N_Z * slab
    sizes = {"z": N_Z, "x": n_x, "y": n_y, "core": N_CORE}
    places = jnp.stack([z_at, x_at]).astype(jnp.int32)
    offsets = [(dc, dy) for dc in range(N_CORE) for dy in range(n_y)]
    other = N_CORE - 1

    def send(value, axis, step):
        size = sizes[axis]
        return lax.ppermute(value, axis, [(i, (i + step) % size) for i in range(size)])

    def send_col(value, dy, dc):
        perm = [
            (y * N_CORE + c, (y + dy) % n_y * N_CORE + (c + dc) % N_CORE)
            for y in range(n_y)
            for c in range(N_CORE)
        ]
        return lax.ppermute(value, ("y", "core"), perm)

    def fetch(value, axis):
        return [value] + [send(value, axis, -k) for k in range(1, sizes[axis])]

    def fetch_z(value):
        return [value] + [send(value, "z", k) for k in range(1, N_Z)]

    def place(dy, dc):
        return ((y_at + dy) % n_y * N_CORE + (core_at + dc) % N_CORE) * rows

    shard_qkv, shard_up, shard_down = plain_call(
        pack_kernel,
        (
            shaped((slab, 4 * width), bf16),
            shaped((slab + DIGITS, unit), bf16),
            shaped((slab, unit), bf16),
        ),
        live_mask.reshape(-1, 128),
        weight_qkv,
        weight_proj,
        weight_up,
        weight_down,
        mebibytes=8,
        name="pack",
    )
    near_qkv = fetch_z(shard_qkv)
    block_qkv = stack_z(near_qkv, slab, places)
    geometry = attend_geometry(segments, live_mask)
    own_live = lax.dynamic_slice_in_dim(
        live_mask, (y_at * N_CORE + core_at) * rows, rows, 0
    ).astype(f32)[:, None]
    spots_here = jnp.stack([place(dy, dc) for dc, dy in offsets]).astype(jnp.int32)
    spots = jnp.stack([place(-dy, -dc) for dc, dy in offsets]).astype(jnp.int32)
    block_qkv, shard_down, shard_up, tokens, geometry, own_live, spots_here, spots = tie(
        block_qkv, shard_down, shard_up, tokens, geometry, own_live, spots_here, spots
    )

    beside_qkv = fetch(block_qkv, "x")
    near_up = fetch_z(shard_up)
    low_one = plain_call(
        first_kernel,
        shaped(tokens.shape, bf16),
        tokens,
        norm_params,
        grid=(rows // part_rows,),
        in_specs=row_blocks(part_rows, model) + [fixed(norm_params.shape)],
        out_specs=row_blocks(part_rows, model)[0],
        mebibytes=8,
        name="first",
    )
    blocks_one = fetch(low_one, "y")
    beside_qkv, near_up, blocks_one, shard_down = tie(beside_qkv, near_up, blocks_one, shard_down)

    block_up = stack_z(near_up, slab, places)
    full_qkv, part_proj = weave([[[part] for part in beside_qkv]], [3 * width], slab, places)
    block_up, part_proj, blocks_one = tie(block_up, part_proj, blocks_one)
    blocks_one = blocks_one + [send(block, "core", -1) for block in blocks_one]
    group_one = place_blocks(blocks_one, spots_here)
    beside_up = fetch(block_up, "x")
    near_down = fetch_z(shard_down)
    full_proj = fetch(part_proj, "y")
    projected = dot(group_one, full_qkv, 1, 0).astype(bf16)
    mixed, bias = attend_forward(projected, geometry, spots, rows)
    mixed, beside_up, near_down, full_proj = tie(mixed, beside_up, near_down, full_proj)

    blocks_mixed = [
        piece if key == (0, 0) else send_col(piece, -key[1], -key[0])
        for key, piece in zip(offsets, mixed)
    ]
    full_proj = [beside_call(full_proj)]
    full_proj.append(send(full_proj[0], "core", -1))
    blocks_down = stack_z(near_down, slab, places, 2)
    beside_down = [fetch(blocks_down[0], "x")]
    full_up = [weave([[[part] for part in beside_up]], [], slab, places)]
    live_count = sum(
        256.0 * part[depth, 0].astype(f32) + 16.0 * part[depth + 1, 0].astype(f32)
        + part[depth + 2, 0].astype(f32)
        for part in beside_up
    ).reshape(1, 1)
    blocks_mixed, full_proj, full_up, live_count, beside_down, blocks_down = tie(
        blocks_mixed, full_proj, full_up, live_count, beside_down, blocks_down
    )
    beside_down.append(fetch(blocks_down[1], "x"))
    full_up.append(send(full_up[0], "core", -1))
    count = len(offsets)
    residual, low_two = plain_call(
        functools.partial(proj_kernel, count, n_y),
        (shaped(tokens.shape, f32), shaped(tokens.shape, bf16)),
        *blocks_mixed,
        *full_proj,
        tokens,
        norm_params,
        grid=(rows // wide_rows,),
        in_specs=row_blocks(wide_rows, *([width] * count))
        + [fixed(part.shape) for part in full_proj]
        + row_blocks(wide_rows, model)
        + [fixed(norm_params.shape)],
        out_specs=tuple(row_blocks(wide_rows, model, model)),
        mebibytes=18,
        name="proj",
    )
    low_two, full_up = tie(low_two, full_up)

    chunk = min(256, rows)
    chunks = range(rows // chunk)
    neighbours = range(1, n_y)
    rows_all = n_y * rows

    def cross(value, n):
        piece = value[n * chunk : (n + 1) * chunk]
        return {dy: send(piece, "y", -dy) for dy in neighbours}

    def spot_of(dy, n):
        return (dy * rows) // chunk + n

    low_far = {0: cross(low_two, 0)}
    hidden = up_call(low_two, full_up, rows_all, 0, ())
    low_far[0], hidden, low_two, beside_down = tie(low_far[0], hidden, low_two, beside_down)
    full_down = [weave([list(zip(*beside_down))], [], slab, places)]
    full_down.append(send(full_down[0], "core", -1))
    far_out = {}
    for n in chunks:
        if n + 1 in chunks:
            low_far[n + 1] = cross(low_two, n + 1)
        for dy in neighbours:
            hidden = up_call(low_far[n][dy], full_up, rows_all, spot_of(dy, n), hidden)
        outs = {
            dy: wide_call(hidden[::2], full_down, chunk, spot_of(dy, n), bf16) for dy in neighbours
        }
        if n + 1 in chunks:
            outs, hidden, low_far[n + 1] = tie(outs, hidden, low_far[n + 1])
        else:
            outs, hidden = tie(outs, hidden)
        if n:
            far_out[n - 1] = tie(far_out[n - 1], outs)[0]
        far_out[n] = {dy: send(outs[dy], "y", dy) for dy in neighbours}
    own_out = wide_call(hidden[::2], full_down, rows, 0, f32)
    own_out, far_out = tie(own_out, far_out)
    far_out = [far_out[n][dy] for n in chunks for dy in neighbours]
    each = len(neighbours)
    grad_output, grad_branch, loss_rows = plain_call(
        functools.partial(loss_kernel, len(chunks), each),
        (shaped(tokens.shape, f32), shaped(tokens.shape, bf16), shaped((8, model), f32)),
        residual,
        teacher,
        own_out,
        *far_out,
        own_live,
        live_count,
        grid=(len(chunks),),
        in_specs=row_blocks(chunk, model, model, model)
        + [fixed((chunk, model))] * len(far_out)
        + row_blocks(chunk, 1)
        + [fixed((1, 1))],
        out_specs=tuple(row_blocks(chunk, model, model) + [fixed((8, model))]),
        scratch=[pltpu.VMEM((chunk, model), f32)],
        mebibytes=20,
        name="loss",
    )
    active, slope = hidden[::2], hidden[1::2]

    grad_far = {0: cross(grad_branch, 0)}
    grad_hidden = hidden_call(grad_branch, slope, full_down, 0, ())
    own_two = wide_call(grad_hidden, full_up, rows, 0, f32)
    grad_far[0], grad_hidden, own_two, grad_branch = tie(
        grad_far[0], grad_hidden, own_two, grad_branch
    )
    def gather_rows(own, far):
        return jnp.concatenate([own] + [far[n][dy] for dy in neighbours for n in chunks], axis=0)

    far_two = {}
    for n in chunks:
        if n + 1 in chunks:
            grad_far[n + 1] = cross(grad_branch, n + 1)
        for dy in neighbours:
            grad_hidden = hidden_call(
                grad_far[n][dy], slope, full_down, spot_of(dy, n), grad_hidden
            )
        outs = {
            dy: wide_call(grad_hidden, full_up, chunk, spot_of(dy, n), bf16) for dy in neighbours
        }
        if n + 1 in chunks:
            outs, grad_hidden, grad_far[n + 1] = tie(outs, grad_hidden, grad_far[n + 1])
        else:
            grad_all = gather_rows(grad_branch, grad_far)
            far_down = dot(grad_all, active[other], 0, 0).astype(bf16)
            outs, grad_hidden, grad_all, far_down, far_two = tie(
                outs, grad_hidden, grad_all, far_down, far_two
            )
        far_two[n] = {dy: send(outs[dy], "y", dy) for dy in neighbours}

    low_all = gather_rows(low_two, low_far)
    far_up = dot(low_all, grad_hidden[other], 0, 0).astype(bf16)
    sent_down, sent_up = send(far_down, "core", 1), send(far_up, "core", 1)
    hold_down = (dot(grad_all, active[0], 0, 0) + sent_down.astype(f32)).astype(bf16)
    halves_down = split_x([[hold_down]], n_x, places)
    hold_up = (dot(low_all, grad_hidden[0], 0, 0) + sent_up.astype(f32)).astype(bf16)
    halves_up = split_x([[hold_up]], n_x, places)
    far_two, halves_down, halves_up = tie(far_two, halves_down, halves_up)
    far_two = [far_two[n][dy] for n in chunks for dy in neighbours]
    grad_residual, grad_low, sums_two = plain_call(
        functools.partial(middle_kernel, len(chunks), each),
        (shaped(tokens.shape, f32), shaped(tokens.shape, bf16), shaped((8, model), f32)),
        own_two,
        *far_two,
        residual,
        grad_output,
        norm_params,
        grid=(len(chunks),),
        in_specs=row_blocks(chunk, model)
        + [fixed((chunk, model))] * len(far_two)
        + row_blocks(chunk, model, model)
        + [fixed(norm_params.shape)],
        out_specs=tuple(row_blocks(chunk, model, model) + [fixed((8, model))]),
        scratch=[pltpu.VMEM((chunk, model), f32)],
        mebibytes=20,
        name="middle",
    )
    pieces_attn = spread_call(grad_low, full_proj, n_y)
    pieces_attn, halves_down, halves_up, grad_low = tie(
        pieces_attn, halves_down, halves_up, grad_low
    )

    def send_back(pieces):
        return [
            piece if key == (0, 0) else send_col(piece, key[1], key[0])
            for key, piece in zip(offsets, pieces)
        ]

    def hop_x(halves):
        return [halves[0]] + [send(halves[dx], "x", dx) for dx in range(1, n_x)]

    def spread_z(pieces):
        return [pieces[0]] + [send(pieces[k], "z", k) for k in range(1, N_Z)]

    lanes = 3 * min(128, width)
    tiles = 3 * width // lanes
    sent_attn = send_back(pieces_attn[0])
    parts_down = hop_x(halves_down)
    far_proj, grad_proj = outer_proj_call(grad_low, blocks_mixed)
    sent_attn, far_proj, grad_proj = tie(sent_attn, far_proj, grad_proj)

    sent_later = [send_back(pieces) for pieces in pieces_attn[1:]]
    sent_proj = send(far_proj, "core", 1)
    grad_projected = attend_backward(projected, sent_attn, spots, geometry[0], bias, 0, ())
    grad_projected, sent_later, sent_proj, parts_down, halves_up = tie(
        grad_projected, sent_later, sent_proj, parts_down, halves_up
    )

    hold_proj = add_lanes(grad_proj, sent_proj)
    pieces_down = split_z(parts_down, places)
    grad_projected, pieces_down, hold_proj, halves_up = tie(
        grad_projected, pieces_down, hold_proj, halves_up
    )
    parts_up = hop_x(halves_up)
    last_down = spread_z(pieces_down)
    part_proj = [hold_proj[0]] + [send(hold_proj[k], "y", k) for k in range(1, n_y)]
    for tile in range(1, tiles):
        grad_projected = attend_backward(
            projected, sent_later[tile - 1], spots, geometry[0], bias, tile, (grad_projected,)
        )
    grad_projected, parts_up, last_down, part_proj = tie(
        grad_projected, parts_up, last_down, part_proj
    )

    far_one, near_one = unproject_call(
        grad_projected,
        full_qkv,
        [place(dy, dc) // rows for dc in reversed(range(N_CORE)) for dy in range(n_y)],
        rows,
    )
    far_one, grad_projected = tie(far_one, grad_projected)
    sent_one = send(far_one, "core", 1)
    grad_qkv = dot(group_one, grad_projected, 0, 0).astype(bf16)
    halves_qkv = split_x([[grad_qkv], part_proj], n_x, places)
    pieces_up = split_z(parts_up, places)
    halves_qkv, sent_one, near_one, pieces_up = tie(halves_qkv, sent_one, near_one, pieces_up)

    parts = [
        near_one[dy * rows : (dy + 1) * rows] + sent_one[dy * rows : (dy + 1) * rows].astype(f32)
        for dy in range(n_y)
    ]
    sent_parts = [parts[k].astype(bf16) for k in range(1, n_y)]
    halves_qkv, sent_parts, pieces_up = tie(halves_qkv, sent_parts, pieces_up)
    received = [send(part, "y", k) for k, part in enumerate(sent_parts, 1)]
    parts_qkv = hop_x(halves_qkv)
    last_up = spread_z(pieces_up)
    (new_down,) = adam_call(
        [last_down], [(0, 0, unit, True)], weight_down, first_down, second_down
    )
    parts_qkv, received, last_up, new_down = tie(parts_qkv, received, last_up, new_down)

    pieces_qkv = split_z(parts_qkv, places)
    token_grad, sums = plain_call(
        functools.partial(leave_kernel, len(received)),
        (shaped(tokens.shape, f32), shaped((8, model), f32)),
        parts[0],
        *received,
        tokens,
        grad_residual,
        norm_params,
        sums_two,
        loss_rows,
        grid=(rows // part_rows,),
        in_specs=row_blocks(part_rows, *([model] * (3 + len(received))))
        + [fixed(norm_params.shape), fixed((8, model)), fixed((8, model))],
        out_specs=tuple(row_blocks(part_rows, model) + [fixed((8, model))]),
        scratch=[pltpu.VMEM((8, model), f32)],
        mebibytes=14,
        name="leave",
    )
    sums, token_grad, pieces_qkv = tie(sums, token_grad, pieces_qkv)
    last_qkv = spread_z(pieces_qkv)
    for axis in ("core", "y", "x", "z"):
        step = 1
        while step < sizes[axis]:
            pairs = [(i, i ^ step) for i in range(sizes[axis])]
            sums = sums + lax.ppermute(sums, axis, pairs)
            step *= 2
    (new_up,) = adam_call([last_up], [(0, 0, unit, False)], weight_up, first_up, second_up)
    sums, last_qkv, new_up = tie(sums, last_qkv, new_up)
    loss_sum = jnp.sum(sums[4])
    live_count = live_count[0, 0]

    new_qkv, new_proj = adam_call(
        [last_qkv],
        [(0, [(0, n * lanes) for n in range(tiles)], lanes, False), (0, 3 * width, width, True)],
        weight_qkv,
        first_qkv,
        second_qkv,
        weight_proj,
        first_proj,
        second_proj,
    )
    new_norms = adam_step(norm_params, sums[:4], first_norms, second_norms, 0.0, norm_rate)
    return (
        loss_sum / live_count,
        token_grad,
        new_qkv[0],
        new_proj[0],
        new_up[0],
        new_down[0],
        new_norms[0],
        new_qkv[1],
        new_proj[1],
        new_up[1],
        new_down[1],
        new_norms[1],
        new_qkv[2],
        new_proj[2],
        new_up[2],
        new_down[2],
        new_norms[2],
    )


def solution(mesh):
    n_x = mesh.shape["row"] // N_Z
    n_y = mesh.shape["col"] // N_CORE
    mesh = jax.sharding.Mesh(
        mesh.devices.reshape(N_Z, n_x, n_y, N_CORE), ("z", "x", "y", "core")
    )
    row, col = ("z", "x"), ("y", "core")
    matrices = (P(None, row, col), P(col, row), P(row, col), P(col, row), P())
    tokens = P(row + col, None)
    return jax.shard_map(
        functools.partial(local, n_x, n_y),
        mesh=mesh,
        in_specs=(tokens, tokens, P(row), P(row)) + matrices * 3,
        out_specs=(P(), tokens) + matrices * 3,
        check_vma=False,
    )
```

```python
import functools

import jax
import jax.numpy as jnp
from jax import lax
from jax.experimental import pallas as pl
from jax.experimental.pallas import tpu as pltpu
from jax.sharding import PartitionSpec as P

HEAD_DIM = 64
PATCHES = 577
STEP = 10
WINDOW = 640
QROWS = 320
TILE = 256
DIGITS = 16
SMALL = pl.CostEstimate(flops=1024, bytes_accessed=1024, transcendentals=0)
N_Z = 4
N_CORE = 2

layer_eps = 1e-06
adam_eps = 1e-08
learn_rate = 0.03
norm_rate = 0.25
moment_decay = 0.5
weight_decay = 0.05

bf16 = jnp.bfloat16
f32 = jnp.float32


def norm_forward(values, gain_row, bias_row):
    average = jnp.mean(values, axis=-1, keepdims=True)
    centred = values - average
    variance = jnp.mean(centred * centred, axis=-1, keepdims=True)
    inverse = lax.rsqrt(variance + layer_eps)
    scaled = centred * inverse
    return (scaled * gain_row + bias_row, scaled, inverse)


def norm_backward(upstream, scaled, inverse, gain_row):
    weighted = upstream * gain_row
    return inverse * (
        weighted
        - jnp.mean(weighted, axis=-1, keepdims=True)
        - scaled * jnp.mean(weighted * scaled, axis=-1, keepdims=True)
    )


def gelu_slope(hidden):
    return (
        0.5 * (1.0 + lax.erf(hidden * 0.7071067811865476))
        + hidden * jnp.exp(-0.5 * hidden * hidden) * 0.3989422804014327
    )


def adam_step(weight, gradient, momentum, variance, decay_rate, rate):
    momentum = moment_decay * momentum + (1.0 - moment_decay) * gradient
    variance = moment_decay * variance + (1.0 - moment_decay) * gradient * gradient
    correction = 1.0 - moment_decay**STEP
    direction = momentum / correction / (jnp.sqrt(variance / correction) + adam_eps)
    return (weight - rate * (direction + decay_rate * weight), momentum, variance)


def dot(left, right, left_dim, right_dim):
    return lax.dot_general(
        left, right, (((left_dim,), (right_dim,)), ((), ())), preferred_element_type=f32
    )


def head_lanes(width, head):
    lanes = lax.broadcasted_iota(jnp.int32, (1, width), 1)
    return (lanes >= head * HEAD_DIM) & (lanes < (head + 1) * HEAD_DIM)


def attend_scores(q_part, k_all, mask):
    scores = dot(q_part, k_all, 1, 1) + mask
    weights = jnp.exp(scores - jnp.max(scores, axis=-1, keepdims=True))
    return weights, jnp.sum(weights, axis=-1, keepdims=True)


def image_window(begin, group_rows):
    image = pl.program_id(0)
    start = jnp.minimum(begin[image] // 16 * 16, group_rows - WINDOW)
    first = begin[image] - start
    return image, pl.multiple_of(start, 16), first


def fill_mask(bias, mask_ref):
    for row in range(0, WINDOW, 128):
        rows = row + lax.broadcasted_iota(jnp.int32, (128, WINDOW), 0)
        cols = lax.broadcasted_iota(jnp.int32, (128, WINDOW), 1)
        mask_ref[row : row + 128, :] = jnp.where(rows == cols, 0.0, bias)


def rows_inside(rows, row_start, first):
    ids = row_start + lax.broadcasted_iota(jnp.int32, (rows, 1), 0)
    return (ids >= first) & (ids < first + PATCHES)


def attend_forward_kernel(blocks, begin, spots, code_ref, *refs):
    bias_out, out_ref, mask_ref = refs[-3:]
    image, start, first = image_window(begin, refs[0].shape[0])
    code = code_ref[pl.ds(start, WINDOW), :]
    bias = jnp.where(code == image, 0.0, -1e30).astype(f32).T
    bias_out[0] = bias[0:8, :]
    fill_mask(bias[0:1, :], mask_ref)
    lanes = refs[0].shape[1]

    for tile in range((len(refs) - 3 - blocks) // 3):
        q_ref, k_ref, v_ref = refs[3 * tile : 3 * tile + 3]
        cols = slice(tile * lanes, (tile + 1) * lanes)

        @pl.when(image == 0)
        def _():
            out_ref[:, cols] = v_ref[...]

        k_all = k_ref[pl.ds(start, WINDOW), :]
        v_all = v_ref[pl.ds(start, WINDOW), :]
        for row in range(0, WINDOW, QROWS):
            at = pl.ds(pl.multiple_of(start + row, 16), QROWS)
            q_part = q_ref[at, :] * jnp.asarray(HEAD_DIM ** (-0.5), bf16)
            inside = rows_inside(QROWS, row, first)
            mixed = None
            for head in range(lanes // HEAD_DIM):
                mine = head_lanes(lanes, head)
                q_head = jnp.where(mine, q_part, jnp.zeros_like(q_part))
                weights, totals = attend_scores(q_head, k_all, mask_ref[row : row + QROWS, :])
                part = dot(weights.astype(bf16), v_all, 1, 0) * (1.0 / totals)
                mixed = part if mixed is None else jnp.where(mine, part, mixed)
            out_ref[at, cols] = jnp.where(inside, mixed.astype(bf16), out_ref[at, cols])

    @pl.when(image == pl.num_programs(0) - 1)
    def _():
        for n, block in enumerate(refs[-3 - blocks : -3]):
            rows = block.shape[0]
            block[...] = out_ref[pl.ds(pl.multiple_of(spots[n], rows), rows), :]


def attend_backward_kernel(blocks, begin, spots, bias_ref, *refs):
    out_ref, p_ref, s_ref, go_ref, mask_ref = refs[-5:]
    go_blocks, refs = refs[3 : 3 + blocks], refs[:3]
    image, start, first = image_window(begin, refs[0].shape[0])
    fill_mask(bias_ref[0, 0:1, :], mask_ref)
    lanes = refs[0].shape[1]
    rows = go_blocks[0].shape[0]
    whole = pl.ds(start, WINDOW)
    inside_all = rows_inside(WINDOW, 0, first)

    @pl.when(image == 0)
    def _():
        for n, block_ref in enumerate(go_blocks):
            go_ref[pl.ds(pl.multiple_of(spots[n], rows), rows), :] = block_ref[...]

    for tile in range(len(refs) // 3):
        q_ref, k_ref, v_ref = refs[3 * tile : 3 * tile + 3]
        cols = slice(tile * lanes, (tile + 1) * lanes)
        base = 3 * tile * lanes
        q_cols, k_cols, v_cols = [
            slice(base + n * lanes, base + (n + 1) * lanes) for n in range(3)
        ]

        @pl.when(image == 0)
        def _():
            out_ref[:, base : base + 2 * lanes] = jnp.zeros((out_ref.shape[0], 2 * lanes), bf16)
            out_ref[:, v_cols] = go_ref[:, cols]

        k_all = k_ref[whole, :]
        v_all = v_ref[whole, :]
        q_all = q_ref[whole, :] * jnp.asarray(HEAD_DIM ** (-0.5), bf16)
        go_all = go_ref[whole, cols]
        key_grad = None
        value_grad = None
        for head in range(lanes // HEAD_DIM):
            mine = head_lanes(lanes, head)
            q_mine = jnp.where(mine, q_all, jnp.zeros_like(q_all))
            go_mine = jnp.where(mine, go_all, jnp.zeros_like(go_all))
            for row in range(0, WINDOW, QROWS):
                part = slice(row, row + QROWS)
                at = pl.ds(pl.multiple_of(start + row, 16), QROWS)
                inside = rows_inside(QROWS, row, first)
                weights, totals = attend_scores(q_mine[part], k_all, mask_ref[part, :])
                weights = weights * jnp.where(inside, 1.0 / totals, 0.0)
                weight_grad = dot(go_mine[part], v_all, 1, 1)
                product = weights * weight_grad
                score_grad = (
                    product - weights * jnp.sum(product, axis=-1, keepdims=True)
                ).astype(bf16)
                p_ref[part, :] = weights.astype(bf16)
                s_ref[part, :] = score_grad
                query_grad = (dot(score_grad, k_all, 1, 0) * HEAD_DIM ** (-0.5)).astype(bf16)
                out_ref[at, q_cols] = jnp.where(inside & mine, query_grad, out_ref[at, q_cols])
            key_part = dot(q_mine, s_ref[...], 0, 0)
            value_part = dot(go_mine, p_ref[...], 0, 0)
            key_grad = key_part if key_grad is None else key_grad + key_part
            value_grad = value_part if value_grad is None else value_grad + value_part
        key_rows = key_grad.T.astype(bf16)
        value_rows = value_grad.T.astype(bf16)
        out_ref[whole, k_cols] = jnp.where(inside_all, key_rows, out_ref[whole, k_cols])
        out_ref[whole, v_cols] = jnp.where(inside_all, value_rows, out_ref[whole, v_cols])


def qkv_operands(projected, tile):
    group_rows, total = projected.shape
    lanes = min(128, total // 3)
    if lanes % 128 == 0:
        specs = [
            pl.BlockSpec((group_rows, lanes), functools.partial(lambda n, i, *_: (0, n), 3 * tile + n))
            for n in range(3)
        ]
        return [projected] * 3, specs
    parts = [projected[:, n * lanes : (n + 1) * lanes] for n in range(3)]
    return parts, [fixed((group_rows, lanes))] * 3


def all_operands(projected):
    width = projected.shape[1] // 3
    operands, specs = [], []
    for tile in range(width // min(128, width)):
        more, places = qkv_operands(projected, tile)
        operands += more
        specs += places
    return operands, specs


def attend_forward(projected, geometry, spots, rows):
    begin, code = geometry
    group_rows, total = projected.shape
    width = total // 3
    blocks = group_rows // rows
    images = begin.shape[0]
    operands, specs = all_operands(projected)
    out = plain_call(
        functools.partial(attend_forward_kernel, blocks),
        (shaped((rows, width), bf16),) * blocks + (shaped((images, 8, WINDOW), f32),),
        code,
        *operands,
        grid=begin.shape,
        in_specs=[fixed(code.shape)] + specs,
        out_specs=(fixed((rows, width)),) * blocks
        + (pl.BlockSpec((1, 8, WINDOW), lambda i, *_: (i, 0, 0)),),
        scratch=[pltpu.VMEM((group_rows, width), bf16), pltpu.VMEM((WINDOW, WINDOW), f32)],
        scalars=(begin, spots),
        mebibytes=20,
        name="attention_forward",
    )
    return out[:blocks], out[blocks]


def attend_backward(projected, go_blocks, spots, begin, bias, tile, into):
    group_rows, total = projected.shape
    lanes = min(128, total // 3)
    operands, specs = qkv_operands(projected, tile)
    return plain_call(
        functools.partial(attend_backward_kernel, len(go_blocks)),
        shaped((group_rows, total), bf16),
        bias,
        *operands,
        *go_blocks,
        grid=begin.shape,
        in_specs=[pl.BlockSpec((1, 8, WINDOW), lambda i, *_: (i, 0, 0))]
        + specs
        + [fixed(block.shape) for block in go_blocks],
        out_specs=pl.BlockSpec((group_rows, 3 * lanes), lambda i, *_: (0, tile)),
        scratch=[pltpu.VMEM((WINDOW, WINDOW), bf16)] * 2
        + [pltpu.VMEM((group_rows, lanes), bf16), pltpu.VMEM((WINDOW, WINDOW), f32)],
        scalars=(begin, spots),
        into=into,
        mebibytes=56 if into else 16,
        name="attention_backward",
    )


def attend_geometry(segments, live_mask):
    group_rows = segments.shape[0]
    numbers = jnp.arange(group_rows // PATCHES, dtype=jnp.int32)
    positions = jnp.arange(group_rows, dtype=jnp.int32)
    begin = jnp.min(
        jnp.where(segments[None, :] == numbers[:, None], positions[None, :], group_rows - PATCHES),
        axis=1,
    )
    code = jnp.where(live_mask == 1, segments, -1)
    return begin, jnp.broadcast_to(code[:, None], (group_rows, 128))


def plain_call(kernel, out_shape, *operands, grid=(), in_specs=None, out_specs=None, scratch=(), scalars=(), into=(), mebibytes=16, name=None):
    params = pltpu.CompilerParams(vmem_limit_bytes=mebibytes * 1024 * 1024)
    if in_specs is None:
        in_specs = [pl.BlockSpec(a.shape, functools.partial(lambda n, *_: (0,) * n, a.ndim)) for a in operands]
    in_specs = list(in_specs) + [pl.BlockSpec(memory_space=pl.ANY)] * len(into)
    if out_specs is None:
        out_specs = jax.tree.map(
            lambda s: pl.BlockSpec(s.shape, functools.partial(lambda n, *_: (0,) * n, len(s.shape))), out_shape
        )
    return pl.pallas_call(
        kernel,
        grid_spec=pltpu.PrefetchScalarGridSpec(
            num_scalar_prefetch=len(scalars),
            grid=grid,
            in_specs=in_specs,
            out_specs=out_specs,
            scratch_shapes=list(scratch),
        ),
        out_shape=out_shape,
        input_output_aliases={len(scalars) + len(operands) + n: n for n in range(len(into))},
        compiler_params=params,
        cost_estimate=SMALL,
        name=name,
    )(*scalars, *operands, *into)


def shaped(shape, dtype):
    return jax.ShapeDtypeStruct(tuple(shape), dtype)


def row_blocks(rows, *widths):
    return [pl.BlockSpec((rows, w), lambda i, *_: (i, 0)) for w in widths]


def fixed(shape):
    return pl.BlockSpec(tuple(shape), functools.partial(lambda n, *_: (0,) * n, len(shape)))


def pack_kernel(live_ref, qkv_ref, proj_ref, up_ref, down_ref, qkv_out, up_out, down_out):
    count, slab, width = qkv_ref.shape
    lanes = min(128, width)
    for n in range(count):
        for t in range(width // lanes):
            at = (count * t + n) * lanes
            qkv_out[:, at : at + lanes] = qkv_ref[n][:, t * lanes : (t + 1) * lanes].astype(bf16)
    qkv_out[:, count * width :] = proj_ref[...].T.astype(bf16)
    up_out[:slab, :] = up_ref[...].astype(bf16)
    live = jnp.sum(jnp.sum(live_ref[...].astype(f32), axis=0, keepdims=True), axis=1, keepdims=True)
    high = jnp.floor(live * (1.0 / 256.0))
    middle = jnp.floor(live * (1.0 / 16.0)) - 16.0 * high
    low = live - 256.0 * high - 16.0 * middle
    row = lax.broadcasted_iota(jnp.int32, (DIGITS, up_out.shape[1]), 0)
    digits = jnp.where(row == 0, high, jnp.where(row == 1, middle, jnp.where(row == 2, low, 0.0)))
    up_out[slab:, :] = digits.astype(bf16)
    down_out[...] = down_ref[...].T.astype(bf16)


def first_kernel(tok_ref, par_ref, low_out):
    normed, _, _ = norm_forward(tok_ref[...], par_ref[0:1, :], par_ref[1:2, :])
    low_out[...] = normed.astype(bf16)


def place_blocks(blocks, spots):
    rows, width = blocks[0].shape

    def kernel(spot_ref, *refs):
        for n, ref in enumerate(refs[:-1]):
            refs[-1][pl.ds(pl.multiple_of(spot_ref[n], rows), rows), :] = ref[...]

    return plain_call(
        kernel,
        shaped((rows * len(blocks), width), bf16),
        *blocks,
        scalars=(spots,),
        mebibytes=20,
        name="place_blocks",
    )


def block_rows(block, slab):
    return pl.ds(pl.multiple_of(block * slab, slab), slab)


def stack_z(pieces, slab, places, count=1):
    height, width = pieces[0].shape
    extra = height - slab
    shapes = (shaped((N_Z * slab // count + extra, width), bf16),) * count

    def kernel(at_ref, *refs):
        held = refs[-1]
        for k, ref in enumerate(refs[:N_Z]):
            held[block_rows(lax.rem(at_ref[0] + N_Z - k, N_Z), slab), :] = ref[:slab, :]
        for n, out in enumerate(refs[N_Z:-1]):
            rows = N_Z * slab // count
            out[:rows, :] = held[n * rows : (n + 1) * rows, :]
            if extra:
                digits = refs[0][slab:, :].astype(f32)
                for ref in refs[1:N_Z]:
                    digits = digits + ref[slab:, :].astype(f32)
                out[rows:, :] = digits.astype(bf16)

    out = plain_call(
        kernel,
        shapes,
        *pieces,
        scalars=(places,),
        scratch=[pltpu.VMEM((N_Z * slab, width), bf16)],
        mebibytes=8,
        name="stack_z",
    )
    return out if count > 1 else out[0]


def weave(columns, cuts, slab, places):
    n_x = len(columns[0])
    width = columns[0][0][0].shape[1]
    flat = [piece for column in columns for half in column for piece in half]
    edges = [0, *cuts, width]
    sizes = [stop - start for start, stop in zip(edges[:-1], edges[1:])]

    def kernel(at_ref, *refs):
        outs = refs[len(flat) :]
        used = 0
        for y, column in enumerate(columns):
            for dx, half in enumerate(column):
                x = lax.rem(at_ref[1] + dx, n_x)
                share = N_Z // len(half)
                for z in range(N_Z):
                    piece = refs[used + z // share]
                    at = block_rows(z * n_x + x, slab)
                    row = z % share * slab
                    for out, start, size in zip(outs, edges, sizes):
                        out[at, y * size : (y + 1) * size] = piece[
                            row : row + slab, start : start + size
                        ]
                used += len(half)

    out = plain_call(
        kernel,
        tuple(shaped((N_Z * n_x * slab, size * len(columns)), bf16) for size in sizes),
        *flat,
        scalars=(places,),
        mebibytes=12,
        name="weave",
    )
    return out if cuts else out[0]


def proj_kernel(count, each, *refs):
    blocks, parts = refs[:count], refs[count : count + count // each]
    tok_ref, par_ref, res_out, low_out = refs[count + count // each :]
    total = tok_ref[...]
    for n, block in enumerate(blocks):
        size = block.shape[1]
        part = parts[n // each][:, n % each * size : (n % each + 1) * size]
        total = total + dot(block[...], part, 1, 1)
    res_out[...] = total
    normed, _, _ = norm_forward(total, par_ref[2:3, :], par_ref[3:4, :])
    low_out[...] = normed.astype(bf16)


ERF_TOP = (
    -2.72614225801306e-10,
    2.77068142495902e-08,
    -2.10102402082508e-06,
    -5.69250639462346e-05,
    -7.34990630326855e-04,
    -2.95459980854025e-03,
    -1.60960333262415e-02,
)
ERF_LOW = (
    -1.45660718464996e-05,
    -2.13374055278905e-04,
    -1.68282697438203e-03,
    -7.37332916720468e-03,
    -1.42647390514189e-02,
)


def erf(value):
    value = jnp.clip(value, -4.0, 4.0)
    square = value * value
    top = jnp.full_like(square, ERF_TOP[0])
    for number in ERF_TOP[1:]:
        top = top * square + number
    low = jnp.full_like(square, ERF_LOW[0])
    for number in ERF_LOW[1:]:
        low = low * square + number
    inverse = pl.reciprocal(low, approx=True)
    inverse = inverse * (2.0 - low * inverse)
    return value * top * inverse


def up_kernel(count, low_ref, *refs):
    outs = refs[-2 * count :]
    for n, part in enumerate(refs[:count]):
        hidden = dot(low_ref[...], part[...], 1, 0)
        share = 0.5 * (1.0 + erf(hidden * 0.7071067811865476))
        outs[2 * n][...] = (hidden * share).astype(bf16)
        slope = share + hidden * jnp.exp(-0.5 * hidden * hidden) * 0.3989422804014327
        outs[2 * n + 1][...] = slope.astype(bf16)


def up_call(low, parts, rows_all, spot, into):
    rows, model = low.shape
    width = parts[0].shape[1]
    cols = pl.BlockSpec((rows, TILE), lambda i, *_: (spot, i))
    return plain_call(
        functools.partial(up_kernel, len(parts)),
        (shaped((rows_all, width), bf16),) * (2 * len(parts)),
        low,
        *parts,
        grid=(width // TILE,),
        in_specs=[fixed(low.shape)] + [pl.BlockSpec((model, TILE), lambda i, *_: (0, i))] * len(parts),
        out_specs=(cols,) * (2 * len(parts)),
        into=into,
        mebibytes=14,
        name="up",
    )


def hidden_kernel(count, low_ref, *refs):
    outs = refs[-count:]
    for n in range(count):
        slope, part = refs[n], refs[count + n]
        outs[n][...] = (dot(low_ref[...], part[...], 1, 0) * slope[...].astype(f32)).astype(bf16)


def hidden_call(low, slopes, parts, spot, into):
    rows, model = low.shape
    width = parts[0].shape[1]
    cols = pl.BlockSpec((rows, TILE), lambda i, *_: (spot, i))
    return plain_call(
        functools.partial(hidden_kernel, len(parts)),
        tuple(shaped(slope.shape, bf16) for slope in slopes),
        low,
        *slopes,
        *parts,
        grid=(width // TILE,),
        in_specs=[fixed(low.shape)]
        + [cols] * len(parts)
        + [pl.BlockSpec((model, TILE), lambda i, *_: (0, i))] * len(parts),
        out_specs=(cols,) * len(parts),
        into=into,
        mebibytes=14,
        name="hidden",
    )


def wide_kernel(count, *refs):
    total = dot(refs[0][...], refs[count][...], 1, 1)
    for n in range(1, count):
        total = total + dot(refs[n][...], refs[count + n][...], 1, 1)
    refs[-1][...] = total.astype(refs[-1].dtype)


def wide_call(values, parts, rows, spot, kind):
    model, width = parts[0].shape
    return plain_call(
        functools.partial(wide_kernel, len(values)),
        shaped((rows, model), kind),
        *values,
        *parts,
        grid=(model // TILE,),
        in_specs=[pl.BlockSpec((rows, width), lambda i, *_: (spot, 0))] * len(values)
        + [pl.BlockSpec((TILE, width), lambda i, *_: (i, 0))] * len(parts),
        out_specs=pl.BlockSpec((rows, TILE), lambda i, *_: (0, i)),
        mebibytes=14,
        name="wide",
    )


def loss_kernel(each, *refs):
    error = refs[0][...] - refs[1][...] + refs[2][...]
    for ref in refs[3 : 3 + each]:
        error = error + ref[...].astype(f32)
    live_ref, count_ref, grad_out, low_out, loss_out = refs[3 + each :]
    weighted = live_ref[...] * error
    grad = 2.0 * weighted / count_ref[...]
    grad_out[...] = grad
    low_out[...] = grad.astype(bf16)
    sums = jnp.sum(weighted * error, axis=0, keepdims=True)
    sums = jnp.concatenate([sums, jnp.zeros((7, sums.shape[1]), f32)], axis=0)
    loss_out[...] = jnp.where(pl.program_id(0) == 0, sums, loss_out[...] + sums)


def loss_call(residual, teacher, own_out, received, live, live_count, n):
    rows, model = received[0].shape
    step = min(128, rows)
    steps = rows // step
    mine = lambda width: pl.BlockSpec((step, width), lambda i: (n * steps + i, 0))
    return plain_call(
        functools.partial(loss_kernel, len(received)),
        (shaped((rows, model), f32), shaped((rows, model), bf16), shaped((8, model), f32)),
        residual,
        teacher,
        own_out,
        *received,
        live,
        live_count,
        grid=(steps,),
        in_specs=[mine(model)] * 3 + row_blocks(step, *([model] * len(received))) + [mine(1), fixed((1, 1))],
        out_specs=tuple(row_blocks(step, model, model) + [fixed((8, model))]),
        mebibytes=14,
        name="loss",
    )


def add_received(received, each, far_ref):
    for n in range(len(received) // each):

        @pl.when(pl.program_id(0) == n)
        def _():
            total = received[n * each][...].astype(f32)
            for ref in received[n * each + 1 : (n + 1) * each]:
                total = total + ref[...].astype(f32)
            far_ref[...] = total


def beside_call(parts):
    rows, width = parts[0].shape

    def kernel(*refs):
        for n, ref in enumerate(refs[:-1]):
            refs[-1][:, n * width : (n + 1) * width] = ref[...]

    return plain_call(
        kernel, shaped((rows, width * len(parts)), bf16), *parts, mebibytes=8, name="beside"
    )


def spread_kernel(each, tiles, low_ref, *refs):
    count = len(refs) // (1 + each * tiles)
    outs = refs[count:]
    for n in range(count * each):
        size = refs[0].shape[1] // each
        part = refs[n // each][:, n % each * size : (n % each + 1) * size]
        piece = dot(low_ref[...], part, 1, 0).astype(bf16)
        lanes = size // tiles
        for tile in range(tiles):
            outs[tile * count * each + n][...] = piece[:, tile * lanes : (tile + 1) * lanes]


def spread_call(low, parts, each):
    width = parts[0].shape[1] // each
    lanes = min(128, width)
    count = len(parts) * each
    out = plain_call(
        functools.partial(spread_kernel, each, width // lanes),
        tuple(shaped((low.shape[0], lanes), bf16) for _ in range(count * (width // lanes))),
        low,
        *parts,
        mebibytes=12,
        name="spread",
    )
    return [out[n : n + count] for n in range(0, len(out), count)]


def unproject_kernel(half, spots, grad_ref, part_ref, far_out, near_out):
    piece = dot(grad_ref[...], part_ref[...], 1, 1)

    @pl.when(pl.program_id(0) < half)
    def _():
        far_out[...] = piece.astype(bf16)

    @pl.when(pl.program_id(0) >= half)
    def _():
        near_out[...] = piece


def unproject_call(grads, part, blocks, rows):
    half = len(blocks) // 2
    model, width = part.shape
    return plain_call(
        functools.partial(unproject_kernel, half),
        (shaped((half * rows, model), bf16), shaped((half * rows, model), f32)),
        grads,
        part,
        grid=(len(blocks),),
        in_specs=[
            pl.BlockSpec((rows, width), lambda i, spots: (spots[i], 0)),
            fixed(part.shape),
        ],
        out_specs=(
            pl.BlockSpec((rows, model), lambda i, spots: (jnp.minimum(i, half - 1), 0)),
            pl.BlockSpec((rows, model), lambda i, spots: (jnp.maximum(i - half, 0), 0)),
        ),
        scalars=(jnp.stack(blocks).astype(jnp.int32),),
        mebibytes=48,
        name="unproject",
    )


def outer_proj_kernel(half, low_ref, *refs):
    blocks, (far_out, *near) = refs[: 2 * half], refs[2 * half :]
    turned = low_ref[...].astype(f32).T.astype(bf16)
    width = blocks[0].shape[1]
    for n in range(half):
        far_out[:, n * width : (n + 1) * width] = dot(turned, blocks[half + n][...], 1, 0).astype(bf16)
        near[n][...] = dot(turned, blocks[n][...], 1, 0).astype(bf16)


def outer_proj_call(low, blocks):
    model = low.shape[1]
    width = blocks[0].shape[1]
    half = len(blocks) // 2
    out = plain_call(
        functools.partial(outer_proj_kernel, half),
        (shaped((model, half * width), bf16),) + (shaped((model, width), bf16),) * half,
        low,
        *blocks,
        mebibytes=14,
        name="outer_proj",
    )
    return out[0], out[1:]


def add_lanes(own, received):
    width = own[0].shape[1]

    def kernel(*refs):
        got = refs[len(own)]
        for n, ref in enumerate(refs[: len(own)]):
            other = got[:, n * width : (n + 1) * width].astype(f32)
            refs[len(own) + 1 + n][...] = (ref[...].astype(f32) + other).astype(bf16)

    return plain_call(
        kernel,
        tuple(shaped(part.shape, bf16) for part in own),
        *own,
        received,
        mebibytes=8,
        name="add_lanes",
    )


def norm_sums(grad, scaled, out_ref, first):
    sums = jnp.concatenate(
        [
            jnp.sum(grad * scaled, axis=0, keepdims=True),
            jnp.sum(grad, axis=0, keepdims=True),
            jnp.zeros((6, grad.shape[1]), f32),
        ],
        axis=0,
    )
    out_ref[...] = jnp.where(first, sums, out_ref[...] + sums)


def middle_kernel(chunks, each, *refs):
    grad_ref, received = refs[0], refs[1 : 1 + chunks * each]
    res_ref, *gouts = refs[1 + chunks * each : 2 + chunks * each + chunks]
    par_ref, full_out, low_out, sum_out, far_ref, gout_ref = refs[2 + chunks * each + chunks :]
    add_received(received, each, far_ref)
    add_received(gouts, 1, gout_ref)
    _, scaled, inverse = norm_forward(res_ref[...], par_ref[2:3, :], par_ref[3:4, :])
    grad = grad_ref[...] + far_ref[...]
    full = gout_ref[...] + norm_backward(grad, scaled, inverse, par_ref[2:3, :])
    full_out[...] = full
    low_out[...] = full.astype(bf16)
    norm_sums(grad, scaled, sum_out, pl.program_id(0) == 0)


def leave_kernel(count, *refs):
    own_ref, received = refs[0], refs[1 : 1 + count]
    tok_ref, res_ref, par_ref, two_ref, loss_ref, out_ref, sum_out, sum_ref = refs[1 + count :]
    _, scaled, inverse = norm_forward(tok_ref[...], par_ref[0:1, :], par_ref[1:2, :])
    grad = own_ref[...]
    for ref in received:
        grad = grad + ref[...].astype(f32)
    out_ref[...] = res_ref[...] + norm_backward(grad, scaled, inverse, par_ref[0:1, :])
    norm_sums(grad, scaled, sum_ref, pl.program_id(0) == 0)
    sum_out[...] = jnp.concatenate(
        [sum_ref[0:2, :], two_ref[0:2, :], loss_ref[0:1, :], jnp.zeros((3, grad.shape[1]), f32)],
        axis=0,
    )


def split_x(parts, n_x, places):
    model = parts[0][0].shape[0]
    slab = model // (N_Z * n_x)
    total = sum(part[0].shape[1] for part in parts)
    flat = [piece for part in parts for piece in part]

    def kernel(at_ref, *refs):
        outs = refs[len(flat) :]
        for dx in range(n_x):
            x = lax.rem(at_ref[1] + dx, n_x)
            for z in range(N_Z):
                at = block_rows(z * n_x + x, slab)
                lane = 0
                used = 0
                for part in parts:
                    value = refs[used][at, :]
                    size = value.shape[1]
                    if len(part) > 1:
                        value = value.astype(f32)
                        for ref in refs[used + 1 : used + len(part)]:
                            value = value + ref[at, :].astype(f32)
                        value = value.astype(bf16)
                    outs[dx][z * slab : (z + 1) * slab, lane : lane + size] = value
                    lane += size
                    used += len(part)

    return plain_call(
        kernel,
        tuple(shaped((model // n_x, total), bf16) for _ in range(n_x)),
        *flat,
        scalars=(places,),
        mebibytes=12,
        name="split_x",
    )


def split_z(parts, places):
    rows, width = parts[0].shape
    slab = rows // N_Z

    def kernel(at_ref, *refs):
        for k, out in enumerate(refs[len(parts) :]):
            at = block_rows(lax.rem(at_ref[0] + k, N_Z), slab)
            total = refs[0][at, :].astype(f32)
            for ref in refs[1 : len(parts)]:
                total = total + ref[at, :].astype(f32)
            out[...] = total.astype(out.dtype)

    shapes = (shaped((slab, width), f32),) + (shaped((slab, width), bf16),) * (N_Z - 1)
    return plain_call(kernel, shapes, *parts, scalars=(places,), mebibytes=8, name="split_z")


def adam_kernel(layout, counts, *refs):
    grads = []
    for count in counts:
        grad = refs[0][...].astype(f32)
        for ref in refs[1:count]:
            grad = grad + ref[...].astype(f32)
        grads.append(grad)
        refs = refs[count:]
    count = len(layout)
    states, outs = refs[: 3 * count], refs[3 * count :]
    for n, (source, start, size, turned) in enumerate(layout):
        weight, first, second = states[3 * n : 3 * n + 3]
        if len(weight.shape) == 3:
            matrices = weight.shape[0]
            lanes = size // matrices
            for k in range(matrices):
                own = [
                    grads[at][:, lane + k * lanes : lane + (k + 1) * lanes] for at, lane in start
                ]
                own = own[0] if len(own) == 1 else jnp.concatenate(own, axis=1)
                new = adam_step(weight[k], own, first[k], second[k], weight_decay, learn_rate)
                for out, value in zip(outs[3 * n : 3 * n + 3], new):
                    out[k] = value
        else:
            part = grads[source][:, start : start + size]
            if turned:
                part = part.T
            new = adam_step(weight[...], part, first[...], second[...], weight_decay, learn_rate)
            for out, value in zip(outs[3 * n : 3 * n + 3], new):
                out[...] = value


def adam_call(groups, layout, *states):
    shapes = tuple(shaped(s.shape, f32) for s in states)
    out = plain_call(
        functools.partial(adam_kernel, layout, [len(group) for group in groups]),
        shapes,
        *[piece for group in groups for piece in group],
        *states,
        mebibytes=16,
        name="adam",
    )
    return [out[3 * n : 3 * n + 3] for n in range(len(layout))]


def tie(*values):
    return lax.optimization_barrier(values)


def local(
    n_x,
    n_y,
    tokens,
    teacher,
    segments,
    live_mask,
    weight_qkv,
    weight_proj,
    weight_up,
    weight_down,
    norm_params,
    first_qkv,
    first_proj,
    first_up,
    first_down,
    first_norms,
    second_qkv,
    second_proj,
    second_up,
    second_down,
    second_norms,
):
    z_at, x_at = lax.axis_index("z"), lax.axis_index("x")
    y_at, core_at = lax.axis_index("y"), lax.axis_index("core")
    rows, model = tokens.shape
    group_rows = segments.shape[0]
    slab = weight_qkv.shape[1]
    width = weight_qkv.shape[2]
    unit = weight_up.shape[1]
    part_rows = min(128, rows)
    wide_rows = min(256, rows)
    depth = N_Z * slab
    sizes = {"z": N_Z, "x": n_x, "y": n_y, "core": N_CORE}
    places = jnp.stack([z_at, x_at]).astype(jnp.int32)
    offsets = [(dc, dy) for dc in range(N_CORE) for dy in range(n_y)]
    other = N_CORE - 1

    def send(value, axis, step):
        size = sizes[axis]
        return lax.ppermute(value, axis, [(i, (i + step) % size) for i in range(size)])

    def send_col(value, dy, dc):
        perm = [
            (y * N_CORE + c, (y + dy) % n_y * N_CORE + (c + dc) % N_CORE)
            for y in range(n_y)
            for c in range(N_CORE)
        ]
        return lax.ppermute(value, ("y", "core"), perm)

    def fetch(value, axis):
        return [value] + [send(value, axis, -k) for k in range(1, sizes[axis])]

    def fetch_z(value):
        return [value] + [send(value, "z", k) for k in range(1, N_Z)]

    def place(dy, dc):
        return ((y_at + dy) % n_y * N_CORE + (core_at + dc) % N_CORE) * rows

    shard_qkv, shard_up, shard_down = plain_call(
        pack_kernel,
        (
            shaped((slab, 4 * width), bf16),
            shaped((slab + DIGITS, unit), bf16),
            shaped((slab, unit), bf16),
        ),
        live_mask.reshape(-1, 128),
        weight_qkv,
        weight_proj,
        weight_up,
        weight_down,
        mebibytes=56,
        name="pack",
    )
    near_qkv = fetch_z(shard_qkv)
    block_qkv = stack_z(near_qkv, slab, places)
    geometry = attend_geometry(segments, live_mask)
    own_live = lax.dynamic_slice_in_dim(
        live_mask, (y_at * N_CORE + core_at) * rows, rows, 0
    ).astype(f32)[:, None]
    spots_here = jnp.stack([place(dy, dc) for dc, dy in offsets]).astype(jnp.int32)
    spots = jnp.stack([place(-dy, -dc) for dc, dy in offsets]).astype(jnp.int32)
    block_qkv, shard_down, shard_up, tokens, geometry, own_live, spots_here, spots = tie(
        block_qkv, shard_down, shard_up, tokens, geometry, own_live, spots_here, spots
    )

    beside_qkv = fetch(block_qkv, "x")
    near_up = fetch_z(shard_up)
    low_one = plain_call(
        first_kernel,
        shaped(tokens.shape, bf16),
        tokens,
        norm_params,
        grid=(rows // part_rows,),
        in_specs=row_blocks(part_rows, model) + [fixed(norm_params.shape)],
        out_specs=row_blocks(part_rows, model)[0],
        mebibytes=8,
        name="first",
    )
    blocks_one = fetch(low_one, "y")
    beside_qkv, near_up, blocks_one, shard_down = tie(beside_qkv, near_up, blocks_one, shard_down)

    block_up = stack_z(near_up, slab, places)
    full_qkv, part_proj = weave([[[part] for part in beside_qkv]], [3 * width], slab, places)
    block_up, part_proj, blocks_one = tie(block_up, part_proj, blocks_one)
    blocks_one = blocks_one + [send(block, "core", -1) for block in blocks_one]
    group_one = place_blocks(blocks_one, spots_here)
    beside_up = fetch(block_up, "x")
    near_down = fetch_z(shard_down)
    full_proj = fetch(part_proj, "y")
    projected = dot(group_one, full_qkv, 1, 0).astype(bf16)
    mixed, bias = attend_forward(projected, geometry, spots, rows)
    mixed, beside_up, near_down, full_proj = tie(mixed, beside_up, near_down, full_proj)

    blocks_mixed = [
        piece if key == (0, 0) else send_col(piece, -key[1], -key[0])
        for key, piece in zip(offsets, mixed)
    ]
    full_proj = [beside_call(full_proj)]
    full_proj.append(send(full_proj[0], "core", -1))
    blocks_down = stack_z(near_down, slab, places, 2)
    beside_down = [fetch(blocks_down[0], "x")]
    full_up = [weave([[[part] for part in beside_up]], [], slab, places)]
    live_count = sum(
        256.0 * part[depth, 0].astype(f32) + 16.0 * part[depth + 1, 0].astype(f32)
        + part[depth + 2, 0].astype(f32)
        for part in beside_up
    ).reshape(1, 1)
    blocks_mixed, full_proj, full_up, live_count, beside_down, blocks_down = tie(
        blocks_mixed, full_proj, full_up, live_count, beside_down, blocks_down
    )
    beside_down.append(fetch(blocks_down[1], "x"))
    full_up.append(send(full_up[0], "core", -1))
    count = len(offsets)
    residual, low_two = plain_call(
        functools.partial(proj_kernel, count, n_y),
        (shaped(tokens.shape, f32), shaped(tokens.shape, bf16)),
        *blocks_mixed,
        *full_proj,
        tokens,
        norm_params,
        grid=(rows // wide_rows,),
        in_specs=row_blocks(wide_rows, *([width] * count))
        + [fixed(part.shape) for part in full_proj]
        + row_blocks(wide_rows, model)
        + [fixed(norm_params.shape)],
        out_specs=tuple(row_blocks(wide_rows, model, model)),
        mebibytes=18,
        name="proj",
    )
    low_two, full_up = tie(low_two, full_up)

    chunk = min(256, rows)
    chunks = range(rows // chunk)
    neighbours = range(1, n_y)
    rows_all = n_y * rows

    def cross(value, n):
        piece = value[n * chunk : (n + 1) * chunk]
        return {dy: send(piece, "y", -dy) for dy in neighbours}

    def spot_of(dy, n):
        return (dy * rows) // chunk + n

    low_far = {0: cross(low_two, 0)}
    hidden = up_call(low_two, full_up, rows_all, 0, ())
    low_far[0], hidden, low_two, beside_down = tie(low_far[0], hidden, low_two, beside_down)
    full_down = [weave([list(zip(*beside_down))], [], slab, places)]
    full_down.append(send(full_down[0], "core", -1))
    far_out = {}
    for n in chunks:
        if n + 1 in chunks:
            low_far[n + 1] = cross(low_two, n + 1)
        for dy in neighbours:
            hidden = up_call(low_far[n][dy], full_up, rows_all, spot_of(dy, n), hidden)
        outs = {
            dy: wide_call(hidden[::2], full_down, chunk, spot_of(dy, n), bf16) for dy in neighbours
        }
        if n == 0:
            own_out = wide_call(hidden[::2], full_down, rows, 0, f32)
            outs, own_out = tie(outs, own_out)
        if n + 1 in chunks:
            outs, hidden, low_far[n + 1] = tie(outs, hidden, low_far[n + 1])
        else:
            outs, hidden = tie(outs, hidden)
        if n:
            far_out[n - 1] = tie(far_out[n - 1], outs)[0]
        far_out[n] = {dy: send(outs[dy], "y", dy) for dy in neighbours}
    each = len(neighbours)
    active, slope = hidden[::2], hidden[1::2]
    grad_output, grad_branch, loss_rows, grad_far = [], [], [], {}
    for n in chunks:
        received = list(far_out[n].values())
        grad, low, sums = loss_call(
            residual, teacher, own_out, received, own_live, live_count, n
        )
        grad_output.append(grad)
        grad_branch.append(low)
        loss_rows.append(sums)
        grad_far[n] = {dy: send(low, "y", -dy) for dy in neighbours}
        if n + 1 in chunks:
            far_out[n + 1], grad_far[n], grad_branch[n] = tie(
                far_out[n + 1], grad_far[n], grad_branch[n]
            )
    loss_rows = sum(loss_rows)

    def gather_rows(own, far):
        return jnp.concatenate(own + [far[n][dy] for dy in neighbours for n in chunks], axis=0)

    low_all = gather_rows([low_two], low_far)
    grad_hidden = ()
    far_two = {}
    for n in chunks:
        for dy in neighbours:
            grad_hidden = hidden_call(
                grad_far[n][dy], slope, full_down, spot_of(dy, n), grad_hidden
            )
        outs = {
            dy: wide_call(grad_hidden, full_up, chunk, spot_of(dy, n), bf16) for dy in neighbours
        }
        if n == 0:
            for k in chunks:
                grad_hidden = hidden_call(grad_branch[k], slope, full_down, k, grad_hidden)
            own_two = wide_call(grad_hidden, full_up, rows, 0, f32)
            outs, own_two = tie(outs, own_two)
        if n + 1 in chunks:
            outs, grad_hidden, grad_far[n + 1] = tie(outs, grad_hidden, grad_far[n + 1])
        else:
            grad_all = gather_rows(grad_branch, grad_far)
            far_down = dot(grad_all, active[other], 0, 0).astype(bf16)
            far_up = dot(low_all, grad_hidden[other], 0, 0).astype(bf16)
            outs, grad_hidden, grad_all, far_down, far_up, far_two = tie(
                outs, grad_hidden, grad_all, far_down, far_up, far_two
            )
        far_two[n] = {dy: send(outs[dy], "y", dy) for dy in neighbours}

    sent_down, sent_up = send(far_down, "core", 1), send(far_up, "core", 1)
    hold_down = (dot(grad_all, active[0], 0, 0) + sent_down.astype(f32)).astype(bf16)
    halves_down = split_x([[hold_down]], n_x, places)
    hold_up = (dot(low_all, grad_hidden[0], 0, 0) + sent_up.astype(f32)).astype(bf16)
    halves_up = split_x([[hold_up]], n_x, places)
    far_two, halves_down, halves_up = tie(far_two, halves_down, halves_up)
    far_two = [far_two[n][dy] for n in chunks for dy in neighbours]
    grad_residual, grad_low, sums_two = plain_call(
        functools.partial(middle_kernel, len(chunks), each),
        (shaped(tokens.shape, f32), shaped(tokens.shape, bf16), shaped((8, model), f32)),
        own_two,
        *far_two,
        residual,
        *grad_output,
        norm_params,
        grid=(len(chunks),),
        in_specs=row_blocks(chunk, model)
        + [fixed((chunk, model))] * len(far_two)
        + row_blocks(chunk, model)
        + [fixed((chunk, model))] * len(chunks)
        + [fixed(norm_params.shape)],
        out_specs=tuple(row_blocks(chunk, model, model) + [fixed((8, model))]),
        scratch=[pltpu.VMEM((chunk, model), f32)] * 2,
        mebibytes=20,
        name="middle",
    )
    pieces_attn = spread_call(grad_low, full_proj, n_y)
    pieces_attn, halves_down, halves_up, grad_low = tie(
        pieces_attn, halves_down, halves_up, grad_low
    )

    def send_back(pieces):
        return [
            piece if key == (0, 0) else send_col(piece, key[1], key[0])
            for key, piece in zip(offsets, pieces)
        ]

    def hop_x(halves):
        return [halves[0]] + [send(halves[dx], "x", dx) for dx in range(1, n_x)]

    def spread_z(pieces):
        return [pieces[0]] + [send(pieces[k], "z", k) for k in range(1, N_Z)]

    lanes = 3 * min(128, width)
    tiles = 3 * width // lanes
    sent_attn = send_back(pieces_attn[0])
    parts_down = hop_x(halves_down)
    far_proj, grad_proj = outer_proj_call(grad_low, blocks_mixed)
    sent_attn, far_proj, grad_proj = tie(sent_attn, far_proj, grad_proj)

    sent_later = [send_back(pieces) for pieces in pieces_attn[1:]]
    sent_proj = send(far_proj, "core", 1)
    grad_projected = attend_backward(projected, sent_attn, spots, geometry[0], bias, 0, ())
    grad_projected, sent_later, sent_proj, parts_down, halves_up = tie(
        grad_projected, sent_later, sent_proj, parts_down, halves_up
    )

    hold_proj = add_lanes(grad_proj, sent_proj)
    pieces_down = split_z(parts_down, places)
    grad_projected, pieces_down, hold_proj, halves_up = tie(
        grad_projected, pieces_down, hold_proj, halves_up
    )
    parts_up = hop_x(halves_up)
    last_down = spread_z(pieces_down)
    part_proj = [hold_proj[0]] + [send(hold_proj[k], "y", k) for k in range(1, n_y)]
    for tile in range(1, tiles):
        grad_projected = attend_backward(
            projected, sent_later[tile - 1], spots, geometry[0], bias, tile, (grad_projected,)
        )
    grad_projected, parts_up, last_down, part_proj = tie(
        grad_projected, parts_up, last_down, part_proj
    )

    far_one, near_one = unproject_call(
        grad_projected,
        full_qkv,
        [place(dy, dc) // rows for dc in reversed(range(N_CORE)) for dy in range(n_y)],
        rows,
    )
    far_one, grad_projected = tie(far_one, grad_projected)
    sent_one = send(far_one, "core", 1)
    grad_qkv = dot(group_one, grad_projected, 0, 0).astype(bf16)
    halves_qkv = split_x([[grad_qkv], part_proj], n_x, places)
    pieces_up = split_z(parts_up, places)
    halves_qkv, sent_one, near_one, pieces_up = tie(halves_qkv, sent_one, near_one, pieces_up)

    parts = [
        near_one[dy * rows : (dy + 1) * rows] + sent_one[dy * rows : (dy + 1) * rows].astype(f32)
        for dy in range(n_y)
    ]
    sent_parts = [parts[k].astype(bf16) for k in range(1, n_y)]
    halves_qkv, sent_parts, pieces_up = tie(halves_qkv, sent_parts, pieces_up)
    received = [send(part, "y", k) for k, part in enumerate(sent_parts, 1)]
    parts_qkv = hop_x(halves_qkv)
    last_up = spread_z(pieces_up)
    (new_down,) = adam_call(
        [last_down], [(0, 0, unit, True)], weight_down, first_down, second_down
    )
    parts_qkv, received, last_up, new_down = tie(parts_qkv, received, last_up, new_down)

    pieces_qkv = split_z(parts_qkv, places)
    token_grad, sums = plain_call(
        functools.partial(leave_kernel, len(received)),
        (shaped(tokens.shape, f32), shaped((8, model), f32)),
        parts[0],
        *received,
        tokens,
        grad_residual,
        norm_params,
        sums_two,
        loss_rows,
        grid=(rows // part_rows,),
        in_specs=row_blocks(part_rows, *([model] * (3 + len(received))))
        + [fixed(norm_params.shape), fixed((8, model)), fixed((8, model))],
        out_specs=tuple(row_blocks(part_rows, model) + [fixed((8, model))]),
        scratch=[pltpu.VMEM((8, model), f32)],
        mebibytes=14,
        name="leave",
    )
    sums, token_grad, pieces_qkv = tie(sums, token_grad, pieces_qkv)
    last_qkv = spread_z(pieces_qkv)
    for axis in ("core", "y", "x", "z"):
        step = 1
        while step < sizes[axis]:
            pairs = [(i, i ^ step) for i in range(sizes[axis])]
            sums = sums + lax.ppermute(sums, axis, pairs)
            step *= 2
    (new_up,) = adam_call([last_up], [(0, 0, unit, False)], weight_up, first_up, second_up)
    sums, last_qkv, new_up = tie(sums, last_qkv, new_up)
    loss_sum = jnp.sum(sums[4])
    live_count = live_count[0, 0]

    new_qkv, new_proj = adam_call(
        [last_qkv],
        [(0, [(0, n * lanes) for n in range(tiles)], lanes, False), (0, 3 * width, width, True)],
        weight_qkv,
        first_qkv,
        second_qkv,
        weight_proj,
        first_proj,
        second_proj,
    )
    new_norms = adam_step(norm_params, sums[:4], first_norms, second_norms, 0.0, norm_rate)
    return (
        loss_sum / live_count,
        token_grad,
        new_qkv[0],
        new_proj[0],
        new_up[0],
        new_down[0],
        new_norms[0],
        new_qkv[1],
        new_proj[1],
        new_up[1],
        new_down[1],
        new_norms[1],
        new_qkv[2],
        new_proj[2],
        new_up[2],
        new_down[2],
        new_norms[2],
    )


def solution(mesh):
    n_x = mesh.shape["row"] // N_Z
    n_y = mesh.shape["col"] // N_CORE
    mesh = jax.sharding.Mesh(
        mesh.devices.reshape(N_Z, n_x, n_y, N_CORE), ("z", "x", "y", "core")
    )
    row, col = ("z", "x"), ("y", "core")
    matrices = (P(None, row, col), P(col, row), P(row, col), P(col, row), P())
    tokens = P(row + col, None)
    return jax.shard_map(
        functools.partial(local, n_x, n_y),
        mesh=mesh,
        in_specs=(tokens, tokens, P(row), P(row)) + matrices * 3,
        out_specs=(P(), tokens) + matrices * 3,
        check_vma=False,
    )
```

```python
import functools

import jax
import jax.numpy as jnp
from jax import lax
from jax.experimental import pallas as pl
from jax.experimental.pallas import tpu as pltpu
from jax.sharding import PartitionSpec as P

HEAD_DIM = 64
PATCHES = 577
STEP = 10
WINDOW = 640
QROWS = 320
TILE = 256
DIGITS = 16
SMALL = pl.CostEstimate(flops=1024, bytes_accessed=1024, transcendentals=0)
N_Z = 4
N_CORE = 2

layer_eps = 1e-06
adam_eps = 1e-08
learn_rate = 0.03
norm_rate = 0.25
moment_decay = 0.5
weight_decay = 0.05

bf16 = jnp.bfloat16
f32 = jnp.float32


def norm_forward(values, gain_row, bias_row):
    average = jnp.mean(values, axis=-1, keepdims=True)
    centred = values - average
    variance = jnp.mean(centred * centred, axis=-1, keepdims=True)
    inverse = lax.rsqrt(variance + layer_eps)
    scaled = centred * inverse
    return (scaled * gain_row + bias_row, scaled, inverse)


def norm_backward(upstream, scaled, inverse, gain_row):
    weighted = upstream * gain_row
    return inverse * (
        weighted
        - jnp.mean(weighted, axis=-1, keepdims=True)
        - scaled * jnp.mean(weighted * scaled, axis=-1, keepdims=True)
    )


def gelu_slope(hidden):
    return (
        0.5 * (1.0 + lax.erf(hidden * 0.7071067811865476))
        + hidden * jnp.exp(-0.5 * hidden * hidden) * 0.3989422804014327
    )


def adam_step(weight, gradient, momentum, variance, decay_rate, rate):
    momentum = moment_decay * momentum + (1.0 - moment_decay) * gradient
    variance = moment_decay * variance + (1.0 - moment_decay) * gradient * gradient
    correction = 1.0 - moment_decay**STEP
    direction = momentum / correction / (jnp.sqrt(variance / correction) + adam_eps)
    return (weight - rate * (direction + decay_rate * weight), momentum, variance)


def dot(left, right, left_dim, right_dim):
    return lax.dot_general(
        left, right, (((left_dim,), (right_dim,)), ((), ())), preferred_element_type=f32
    )


def head_lanes(width, head):
    lanes = lax.broadcasted_iota(jnp.int32, (1, width), 1)
    return (lanes >= head * HEAD_DIM) & (lanes < (head + 1) * HEAD_DIM)


def attend_scores(q_part, k_all, mask):
    scores = dot(q_part, k_all, 1, 1) + mask
    weights = jnp.exp(scores - jnp.max(scores, axis=-1, keepdims=True))
    return weights, jnp.sum(weights, axis=-1, keepdims=True)


def image_window(begin, group_rows):
    image = pl.program_id(0)
    start = jnp.minimum(begin[image] // 16 * 16, group_rows - WINDOW)
    first = begin[image] - start
    return image, pl.multiple_of(start, 16), first


def fill_mask(bias, mask_ref):
    for row in range(0, WINDOW, 128):
        rows = row + lax.broadcasted_iota(jnp.int32, (128, WINDOW), 0)
        cols = lax.broadcasted_iota(jnp.int32, (128, WINDOW), 1)
        mask_ref[row : row + 128, :] = jnp.where(rows == cols, 0.0, bias)


def rows_inside(rows, row_start, first):
    ids = row_start + lax.broadcasted_iota(jnp.int32, (rows, 1), 0)
    return (ids >= first) & (ids < first + PATCHES)


def attend_forward_kernel(blocks, begin, spots, code_ref, *refs):
    bias_out, out_ref, mask_ref = refs[-3:]
    image, start, first = image_window(begin, refs[0].shape[0])
    code = code_ref[pl.ds(start, WINDOW), :]
    bias = jnp.where(code == image, 0.0, -1e30).astype(f32).T
    bias_out[0] = bias[0:8, :]
    fill_mask(bias[0:1, :], mask_ref)
    lanes = refs[0].shape[1]

    for tile in range((len(refs) - 3 - blocks) // 3):
        q_ref, k_ref, v_ref = refs[3 * tile : 3 * tile + 3]
        cols = slice(tile * lanes, (tile + 1) * lanes)

        @pl.when(image == 0)
        def _():
            out_ref[:, cols] = v_ref[...]

        k_all = k_ref[pl.ds(start, WINDOW), :]
        v_all = v_ref[pl.ds(start, WINDOW), :]
        for row in range(0, WINDOW, QROWS):
            at = pl.ds(pl.multiple_of(start + row, 16), QROWS)
            q_part = q_ref[at, :] * jnp.asarray(HEAD_DIM ** (-0.5), bf16)
            inside = rows_inside(QROWS, row, first)
            mixed = None
            for head in range(lanes // HEAD_DIM):
                mine = head_lanes(lanes, head)
                q_head = jnp.where(mine, q_part, jnp.zeros_like(q_part))
                weights, totals = attend_scores(q_head, k_all, mask_ref[row : row + QROWS, :])
                part = dot(weights.astype(bf16), v_all, 1, 0) * (1.0 / totals)
                mixed = part if mixed is None else jnp.where(mine, part, mixed)
            out_ref[at, cols] = jnp.where(inside, mixed.astype(bf16), out_ref[at, cols])

    @pl.when(image == pl.num_programs(0) - 1)
    def _():
        for n, block in enumerate(refs[-3 - blocks : -3]):
            rows = block.shape[0]
            block[...] = out_ref[pl.ds(pl.multiple_of(spots[n], rows), rows), :]


def attend_backward_kernel(blocks, begin, spots, bias_ref, *refs):
    out_ref, p_ref, s_ref, go_ref, mask_ref = refs[-5:]
    go_blocks, refs = refs[3 : 3 + blocks], refs[:3]
    image, start, first = image_window(begin, refs[0].shape[0])
    fill_mask(bias_ref[0, 0:1, :], mask_ref)
    lanes = refs[0].shape[1]
    rows = go_blocks[0].shape[0]
    whole = pl.ds(start, WINDOW)
    inside_all = rows_inside(WINDOW, 0, first)

    @pl.when(image == 0)
    def _():
        for n, block_ref in enumerate(go_blocks):
            go_ref[pl.ds(pl.multiple_of(spots[n], rows), rows), :] = block_ref[...]

    for tile in range(len(refs) // 3):
        q_ref, k_ref, v_ref = refs[3 * tile : 3 * tile + 3]
        cols = slice(tile * lanes, (tile + 1) * lanes)
        base = 3 * tile * lanes
        q_cols, k_cols, v_cols = [
            slice(base + n * lanes, base + (n + 1) * lanes) for n in range(3)
        ]

        @pl.when(image == 0)
        def _():
            out_ref[:, base : base + 2 * lanes] = jnp.zeros((out_ref.shape[0], 2 * lanes), bf16)
            out_ref[:, v_cols] = go_ref[:, cols]

        k_all = k_ref[whole, :]
        v_all = v_ref[whole, :]
        q_all = q_ref[whole, :] * jnp.asarray(HEAD_DIM ** (-0.5), bf16)
        go_all = go_ref[whole, cols]
        key_grad = None
        value_grad = None
        for head in range(lanes // HEAD_DIM):
            mine = head_lanes(lanes, head)
            q_mine = jnp.where(mine, q_all, jnp.zeros_like(q_all))
            go_mine = jnp.where(mine, go_all, jnp.zeros_like(go_all))
            for row in range(0, WINDOW, QROWS):
                part = slice(row, row + QROWS)
                at = pl.ds(pl.multiple_of(start + row, 16), QROWS)
                inside = rows_inside(QROWS, row, first)
                weights, totals = attend_scores(q_mine[part], k_all, mask_ref[part, :])
                weights = weights * jnp.where(inside, 1.0 / totals, 0.0)
                weight_grad = dot(go_mine[part], v_all, 1, 1)
                product = weights * weight_grad
                score_grad = (
                    product - weights * jnp.sum(product, axis=-1, keepdims=True)
                ).astype(bf16)
                p_ref[part, :] = weights.astype(bf16)
                s_ref[part, :] = score_grad
                query_grad = (dot(score_grad, k_all, 1, 0) * HEAD_DIM ** (-0.5)).astype(bf16)
                out_ref[at, q_cols] = jnp.where(inside & mine, query_grad, out_ref[at, q_cols])
            key_part = dot(q_mine, s_ref[...], 0, 0)
            value_part = dot(go_mine, p_ref[...], 0, 0)
            key_grad = key_part if key_grad is None else key_grad + key_part
            value_grad = value_part if value_grad is None else value_grad + value_part
        key_rows = key_grad.T.astype(bf16)
        value_rows = value_grad.T.astype(bf16)
        out_ref[whole, k_cols] = jnp.where(inside_all, key_rows, out_ref[whole, k_cols])
        out_ref[whole, v_cols] = jnp.where(inside_all, value_rows, out_ref[whole, v_cols])


def qkv_operands(projected, tile):
    group_rows, total = projected.shape
    lanes = min(128, total // 3)
    if lanes % 128 == 0:
        specs = [
            pl.BlockSpec((group_rows, lanes), functools.partial(lambda n, i, *_: (0, n), 3 * tile + n))
            for n in range(3)
        ]
        return [projected] * 3, specs
    parts = [projected[:, n * lanes : (n + 1) * lanes] for n in range(3)]
    return parts, [fixed((group_rows, lanes))] * 3


def all_operands(projected):
    width = projected.shape[1] // 3
    operands, specs = [], []
    for tile in range(width // min(128, width)):
        more, places = qkv_operands(projected, tile)
        operands += more
        specs += places
    return operands, specs


def attend_forward(projected, geometry, spots, rows):
    begin, code = geometry
    group_rows, total = projected.shape
    width = total // 3
    blocks = group_rows // rows
    images = begin.shape[0]
    operands, specs = all_operands(projected)
    out = plain_call(
        functools.partial(attend_forward_kernel, blocks),
        (shaped((rows, width), bf16),) * blocks + (shaped((images, 8, WINDOW), f32),),
        code,
        *operands,
        grid=begin.shape,
        in_specs=[fixed(code.shape)] + specs,
        out_specs=(fixed((rows, width)),) * blocks
        + (pl.BlockSpec((1, 8, WINDOW), lambda i, *_: (i, 0, 0)),),
        scratch=[pltpu.VMEM((group_rows, width), bf16), pltpu.VMEM((WINDOW, WINDOW), f32)],
        scalars=(begin, spots),
        mebibytes=20,
        name="attention_forward",
    )
    return out[:blocks], out[blocks]


def attend_backward(projected, go_blocks, spots, begin, bias, tile, into):
    group_rows, total = projected.shape
    lanes = min(128, total // 3)
    operands, specs = qkv_operands(projected, tile)
    return plain_call(
        functools.partial(attend_backward_kernel, len(go_blocks)),
        shaped((group_rows, total), bf16),
        bias,
        *operands,
        *go_blocks,
        grid=begin.shape,
        in_specs=[pl.BlockSpec((1, 8, WINDOW), lambda i, *_: (i, 0, 0))]
        + specs
        + [fixed(block.shape) for block in go_blocks],
        out_specs=pl.BlockSpec((group_rows, 3 * lanes), lambda i, *_: (0, tile)),
        scratch=[pltpu.VMEM((WINDOW, WINDOW), bf16)] * 2
        + [pltpu.VMEM((group_rows, lanes), bf16), pltpu.VMEM((WINDOW, WINDOW), f32)],
        scalars=(begin, spots),
        into=into,
        mebibytes=56 if into else 16,
        name="attention_backward",
    )


def attend_geometry(segments, live_mask):
    group_rows = segments.shape[0]
    numbers = jnp.arange(group_rows // PATCHES, dtype=jnp.int32)
    positions = jnp.arange(group_rows, dtype=jnp.int32)
    begin = jnp.min(
        jnp.where(segments[None, :] == numbers[:, None], positions[None, :], group_rows - PATCHES),
        axis=1,
    )
    code = jnp.where(live_mask == 1, segments, -1)
    return begin, jnp.broadcast_to(code[:, None], (group_rows, 128))


def plain_call(kernel, out_shape, *operands, grid=(), in_specs=None, out_specs=None, scratch=(), scalars=(), into=(), mebibytes=16, name=None):
    params = pltpu.CompilerParams(vmem_limit_bytes=mebibytes * 1024 * 1024)
    if in_specs is None:
        in_specs = [pl.BlockSpec(a.shape, functools.partial(lambda n, *_: (0,) * n, a.ndim)) for a in operands]
    in_specs = list(in_specs) + [pl.BlockSpec(memory_space=pl.ANY)] * len(into)
    if out_specs is None:
        out_specs = jax.tree.map(
            lambda s: pl.BlockSpec(s.shape, functools.partial(lambda n, *_: (0,) * n, len(s.shape))), out_shape
        )
    return pl.pallas_call(
        kernel,
        grid_spec=pltpu.PrefetchScalarGridSpec(
            num_scalar_prefetch=len(scalars),
            grid=grid,
            in_specs=in_specs,
            out_specs=out_specs,
            scratch_shapes=list(scratch),
        ),
        out_shape=out_shape,
        input_output_aliases={len(scalars) + len(operands) + n: n for n in range(len(into))},
        compiler_params=params,
        cost_estimate=SMALL,
        name=name,
    )(*scalars, *operands, *into)


def shaped(shape, dtype):
    return jax.ShapeDtypeStruct(tuple(shape), dtype)


def row_blocks(rows, *widths):
    return [pl.BlockSpec((rows, w), lambda i, *_: (i, 0)) for w in widths]


def fixed(shape):
    return pl.BlockSpec(tuple(shape), functools.partial(lambda n, *_: (0,) * n, len(shape)))


def pack_kernel(live_ref, qkv_ref, proj_ref, up_ref, down_ref, qkv_out, up_out, down_out):
    count, slab, width = qkv_ref.shape
    lanes = min(128, width)
    for n in range(count):
        for t in range(width // lanes):
            at = (count * t + n) * lanes
            qkv_out[:, at : at + lanes] = qkv_ref[n][:, t * lanes : (t + 1) * lanes].astype(bf16)
    qkv_out[:, count * width :] = proj_ref[...].T.astype(bf16)
    up_out[:slab, :] = up_ref[...].astype(bf16)
    live = jnp.sum(jnp.sum(live_ref[...].astype(f32), axis=0, keepdims=True), axis=1, keepdims=True)
    high = jnp.floor(live * (1.0 / 256.0))
    middle = jnp.floor(live * (1.0 / 16.0)) - 16.0 * high
    low = live - 256.0 * high - 16.0 * middle
    row = lax.broadcasted_iota(jnp.int32, (DIGITS, up_out.shape[1]), 0)
    digits = jnp.where(row == 0, high, jnp.where(row == 1, middle, jnp.where(row == 2, low, 0.0)))
    up_out[slab:, :] = digits.astype(bf16)
    down_out[...] = down_ref[...].T.astype(bf16)


def first_kernel(tok_ref, par_ref, low_out):
    normed, _, _ = norm_forward(tok_ref[...], par_ref[0:1, :], par_ref[1:2, :])
    low_out[...] = normed.astype(bf16)


def place_blocks(blocks, spots):
    rows, width = blocks[0].shape

    def kernel(spot_ref, *refs):
        for n, ref in enumerate(refs[:-1]):
            refs[-1][pl.ds(pl.multiple_of(spot_ref[n], rows), rows), :] = ref[...]

    return plain_call(
        kernel,
        shaped((rows * len(blocks), width), bf16),
        *blocks,
        scalars=(spots,),
        mebibytes=20,
        name="place_blocks",
    )


def block_rows(block, slab):
    return pl.ds(pl.multiple_of(block * slab, slab), slab)


def stack_z(pieces, slab, places, count=1):
    height, width = pieces[0].shape
    extra = height - slab
    shapes = (shaped((N_Z * slab // count + extra, width), bf16),) * count

    def kernel(at_ref, *refs):
        held = refs[-1]
        for k, ref in enumerate(refs[:N_Z]):
            held[block_rows(lax.rem(at_ref[0] + N_Z - k, N_Z), slab), :] = ref[:slab, :]
        for n, out in enumerate(refs[N_Z:-1]):
            rows = N_Z * slab // count
            out[:rows, :] = held[n * rows : (n + 1) * rows, :]
            if extra:
                digits = refs[0][slab:, :].astype(f32)
                for ref in refs[1:N_Z]:
                    digits = digits + ref[slab:, :].astype(f32)
                out[rows:, :] = digits.astype(bf16)

    out = plain_call(
        kernel,
        shapes,
        *pieces,
        scalars=(places,),
        scratch=[pltpu.VMEM((N_Z * slab, width), bf16)],
        mebibytes=8,
        name="stack_z",
    )
    return out if count > 1 else out[0]


def weave(columns, cuts, slab, places):
    n_x = len(columns[0])
    width = columns[0][0][0].shape[1]
    flat = [piece for column in columns for half in column for piece in half]
    edges = [0, *cuts, width]
    sizes = [stop - start for start, stop in zip(edges[:-1], edges[1:])]

    def kernel(at_ref, *refs):
        outs = refs[len(flat) :]
        used = 0
        for y, column in enumerate(columns):
            for dx, half in enumerate(column):
                x = lax.rem(at_ref[1] + dx, n_x)
                share = N_Z // len(half)
                for z in range(N_Z):
                    piece = refs[used + z // share]
                    at = block_rows(z * n_x + x, slab)
                    row = z % share * slab
                    for out, start, size in zip(outs, edges, sizes):
                        out[at, y * size : (y + 1) * size] = piece[
                            row : row + slab, start : start + size
                        ]
                used += len(half)

    out = plain_call(
        kernel,
        tuple(shaped((N_Z * n_x * slab, size * len(columns)), bf16) for size in sizes),
        *flat,
        scalars=(places,),
        mebibytes=12,
        name="weave",
    )
    return out if cuts else out[0]


def proj_kernel(count, each, *refs):
    blocks, parts = refs[:count], refs[count : count + count // each]
    tok_ref, par_ref, res_out, low_out = refs[count + count // each :]
    total = tok_ref[...]
    for n, block in enumerate(blocks):
        size = block.shape[1]
        part = parts[n // each][:, n % each * size : (n % each + 1) * size]
        total = total + dot(block[...], part, 1, 1)
    res_out[...] = total
    normed, _, _ = norm_forward(total, par_ref[2:3, :], par_ref[3:4, :])
    low_out[...] = normed.astype(bf16)


ERF_TOP = (
    -2.72614225801306e-10,
    2.77068142495902e-08,
    -2.10102402082508e-06,
    -5.69250639462346e-05,
    -7.34990630326855e-04,
    -2.95459980854025e-03,
    -1.60960333262415e-02,
)
ERF_LOW = (
    -1.45660718464996e-05,
    -2.13374055278905e-04,
    -1.68282697438203e-03,
    -7.37332916720468e-03,
    -1.42647390514189e-02,
)


def erf(value):
    value = jnp.clip(value, -4.0, 4.0)
    square = value * value
    top = jnp.full_like(square, ERF_TOP[0])
    for number in ERF_TOP[1:]:
        top = top * square + number
    low = jnp.full_like(square, ERF_LOW[0])
    for number in ERF_LOW[1:]:
        low = low * square + number
    inverse = pl.reciprocal(low, approx=True)
    inverse = inverse * (2.0 - low * inverse)
    return value * top * inverse


def up_kernel(count, low_ref, *refs):
    outs = refs[-2 * count :]
    for n, part in enumerate(refs[:count]):
        hidden = dot(low_ref[...], part[...], 1, 0)
        share = 0.5 * (1.0 + erf(hidden * 0.7071067811865476))
        outs[2 * n][...] = (hidden * share).astype(bf16)
        slope = share + hidden * jnp.exp(-0.5 * hidden * hidden) * 0.3989422804014327
        outs[2 * n + 1][...] = slope.astype(bf16)


def up_call(low, parts, rows_all, spot, into):
    rows, model = low.shape
    width = parts[0].shape[1]
    cols = pl.BlockSpec((rows, TILE), lambda i, *_: (spot, i))
    return plain_call(
        functools.partial(up_kernel, len(parts)),
        (shaped((rows_all, width), bf16),) * (2 * len(parts)),
        low,
        *parts,
        grid=(width // TILE,),
        in_specs=[fixed(low.shape)] + [pl.BlockSpec((model, TILE), lambda i, *_: (0, i))] * len(parts),
        out_specs=(cols,) * (2 * len(parts)),
        into=into,
        mebibytes=14,
        name="up",
    )


def hidden_kernel(count, low_ref, *refs):
    outs = refs[-count:]
    for n in range(count):
        slope, part = refs[n], refs[count + n]
        outs[n][...] = (dot(low_ref[...], part[...], 1, 0) * slope[...].astype(f32)).astype(bf16)


def hidden_call(low, slopes, parts, spot, into):
    rows, model = low.shape
    width = parts[0].shape[1]
    cols = pl.BlockSpec((rows, TILE), lambda i, *_: (spot, i))
    return plain_call(
        functools.partial(hidden_kernel, len(parts)),
        tuple(shaped(slope.shape, bf16) for slope in slopes),
        low,
        *slopes,
        *parts,
        grid=(width // TILE,),
        in_specs=[fixed(low.shape)]
        + [cols] * len(parts)
        + [pl.BlockSpec((model, TILE), lambda i, *_: (0, i))] * len(parts),
        out_specs=(cols,) * len(parts),
        into=into,
        mebibytes=14,
        name="hidden",
    )


def wide_kernel(count, *refs):
    total = dot(refs[0][...], refs[count][...], 1, 1)
    for n in range(1, count):
        total = total + dot(refs[n][...], refs[count + n][...], 1, 1)
    refs[-1][...] = total.astype(refs[-1].dtype)


def wide_call(values, parts, rows, spot, kind):
    model, width = parts[0].shape
    return plain_call(
        functools.partial(wide_kernel, len(values)),
        shaped((rows, model), kind),
        *values,
        *parts,
        grid=(model // TILE,),
        in_specs=[pl.BlockSpec((rows, width), lambda i, *_: (spot, 0))] * len(values)
        + [pl.BlockSpec((TILE, width), lambda i, *_: (i, 0))] * len(parts),
        out_specs=pl.BlockSpec((rows, TILE), lambda i, *_: (0, i)),
        mebibytes=14,
        name="wide",
    )


def loss_kernel(chunks, each, *refs):
    res_ref, tea_ref, own_ref = refs[:3]
    received = refs[3 : 3 + chunks * each]
    live_ref, count_ref, grad_out, low_out, loss_out, far_ref = refs[3 + chunks * each :]
    add_received(received, each, far_ref)
    error = res_ref[...] - tea_ref[...] + own_ref[...] + far_ref[...]
    weighted = live_ref[...] * error
    grad = 2.0 * weighted / count_ref[...]
    grad_out[...] = grad
    low_out[...] = grad.astype(bf16)
    sums = jnp.sum(weighted * error, axis=0, keepdims=True)
    sums = jnp.concatenate([sums, jnp.zeros((7, sums.shape[1]), f32)], axis=0)
    loss_out[...] = jnp.where(pl.program_id(0) == 0, sums, loss_out[...] + sums)


def add_received(received, each, far_ref):
    for n in range(len(received) // each):

        @pl.when(pl.program_id(0) == n)
        def _():
            total = received[n * each][...].astype(f32)
            for ref in received[n * each + 1 : (n + 1) * each]:
                total = total + ref[...].astype(f32)
            far_ref[...] = total


def beside_call(parts):
    rows, width = parts[0].shape

    def kernel(*refs):
        for n, ref in enumerate(refs[:-1]):
            refs[-1][:, n * width : (n + 1) * width] = ref[...]

    return plain_call(
        kernel, shaped((rows, width * len(parts)), bf16), *parts, mebibytes=8, name="beside"
    )


def spread_kernel(each, tiles, low_ref, *refs):
    count = len(refs) // (1 + each * tiles)
    outs = refs[count:]
    for n in range(count * each):
        size = refs[0].shape[1] // each
        part = refs[n // each][:, n % each * size : (n % each + 1) * size]
        piece = dot(low_ref[...], part, 1, 0).astype(bf16)
        lanes = size // tiles
        for tile in range(tiles):
            outs[tile * count * each + n][...] = piece[:, tile * lanes : (tile + 1) * lanes]


def spread_call(low, parts, each):
    width = parts[0].shape[1] // each
    lanes = min(128, width)
    count = len(parts) * each
    out = plain_call(
        functools.partial(spread_kernel, each, width // lanes),
        tuple(shaped((low.shape[0], lanes), bf16) for _ in range(count * (width // lanes))),
        low,
        *parts,
        mebibytes=12,
        name="spread",
    )
    return [out[n : n + count] for n in range(0, len(out), count)]


def unproject_kernel(half, spots, grad_ref, part_ref, far_out, near_out):
    piece = dot(grad_ref[...], part_ref[...], 1, 1)

    @pl.when(pl.program_id(0) < half)
    def _():
        far_out[...] = piece.astype(bf16)

    @pl.when(pl.program_id(0) >= half)
    def _():
        near_out[...] = piece.astype(bf16)


def unproject_call(grads, part, blocks, rows):
    half = len(blocks) // 2
    model, width = part.shape
    return plain_call(
        functools.partial(unproject_kernel, half),
        (shaped((half * rows, model), bf16),) * 2,
        grads,
        part,
        grid=(len(blocks),),
        in_specs=[
            pl.BlockSpec((rows, width), lambda i, spots: (spots[i], 0)),
            fixed(part.shape),
        ],
        out_specs=(
            pl.BlockSpec((rows, model), lambda i, spots: (jnp.minimum(i, half - 1), 0)),
            pl.BlockSpec((rows, model), lambda i, spots: (jnp.maximum(i - half, 0), 0)),
        ),
        scalars=(jnp.stack(blocks).astype(jnp.int32),),
        mebibytes=48,
        name="unproject",
    )


def outer_proj_kernel(half, low_ref, *refs):
    blocks, (far_out, *near) = refs[: 2 * half], refs[2 * half :]
    turned = low_ref[...].astype(f32).T.astype(bf16)
    width = blocks[0].shape[1]
    for n in range(half):
        far_out[:, n * width : (n + 1) * width] = dot(turned, blocks[half + n][...], 1, 0).astype(bf16)
        near[n][...] = dot(turned, blocks[n][...], 1, 0).astype(bf16)


def outer_proj_call(low, blocks):
    model = low.shape[1]
    width = blocks[0].shape[1]
    half = len(blocks) // 2
    out = plain_call(
        functools.partial(outer_proj_kernel, half),
        (shaped((model, half * width), bf16),) + (shaped((model, width), bf16),) * half,
        low,
        *blocks,
        mebibytes=14,
        name="outer_proj",
    )
    return out[0], out[1:]


def add_lanes(own, received):
    width = own[0].shape[1]

    def kernel(*refs):
        got = refs[len(own)]
        for n, ref in enumerate(refs[: len(own)]):
            other = got[:, n * width : (n + 1) * width].astype(f32)
            refs[len(own) + 1 + n][...] = (ref[...].astype(f32) + other).astype(bf16)

    return plain_call(
        kernel,
        tuple(shaped(part.shape, bf16) for part in own),
        *own,
        received,
        mebibytes=8,
        name="add_lanes",
    )


def norm_sums(grad, scaled, out_ref, first):
    sums = jnp.concatenate(
        [
            jnp.sum(grad * scaled, axis=0, keepdims=True),
            jnp.sum(grad, axis=0, keepdims=True),
            jnp.zeros((6, grad.shape[1]), f32),
        ],
        axis=0,
    )
    out_ref[...] = jnp.where(first, sums, out_ref[...] + sums)


def middle_kernel(chunks, each, *refs):
    grad_ref, received = refs[0], refs[1 : 1 + chunks * each]
    res_ref, gout_ref, par_ref, full_out, low_out, sum_out, far_ref = refs[1 + chunks * each :]
    add_received(received, each, far_ref)
    _, scaled, inverse = norm_forward(res_ref[...], par_ref[2:3, :], par_ref[3:4, :])
    grad = grad_ref[...] + far_ref[...]
    full = gout_ref[...] + norm_backward(grad, scaled, inverse, par_ref[2:3, :])
    full_out[...] = full
    low_out[...] = full.astype(bf16)
    norm_sums(grad, scaled, sum_out, pl.program_id(0) == 0)


def leave_kernel(count, *refs):
    own_ref, received = refs[0], refs[1 : 1 + count]
    tok_ref, res_ref, par_ref, two_ref, loss_ref, out_ref, sum_out, sum_ref = refs[1 + count :]
    _, scaled, inverse = norm_forward(tok_ref[...], par_ref[0:1, :], par_ref[1:2, :])
    grad = own_ref[...]
    for ref in received:
        grad = grad + ref[...].astype(f32)
    out_ref[...] = res_ref[...] + norm_backward(grad, scaled, inverse, par_ref[0:1, :])
    norm_sums(grad, scaled, sum_ref, pl.program_id(0) == 0)
    sum_out[...] = jnp.concatenate(
        [sum_ref[0:2, :], two_ref[0:2, :], loss_ref[0:1, :], jnp.zeros((3, grad.shape[1]), f32)],
        axis=0,
    )


def split_x(parts, n_x, places):
    model = parts[0][0].shape[0]
    slab = model // (N_Z * n_x)
    total = sum(part[0].shape[1] for part in parts)
    flat = [piece for part in parts for piece in part]

    def kernel(at_ref, *refs):
        outs = refs[len(flat) :]
        for dx in range(n_x):
            x = lax.rem(at_ref[1] + dx, n_x)
            for z in range(N_Z):
                at = block_rows(z * n_x + x, slab)
                lane = 0
                used = 0
                for part in parts:
                    value = refs[used][at, :]
                    size = value.shape[1]
                    if len(part) > 1:
                        value = value.astype(f32)
                        for ref in refs[used + 1 : used + len(part)]:
                            value = value + ref[at, :].astype(f32)
                        value = value.astype(bf16)
                    outs[dx][z * slab : (z + 1) * slab, lane : lane + size] = value
                    lane += size
                    used += len(part)

    return plain_call(
        kernel,
        tuple(shaped((model // n_x, total), bf16) for _ in range(n_x)),
        *flat,
        scalars=(places,),
        mebibytes=12,
        name="split_x",
    )


def split_z(parts, places):
    rows, width = parts[0].shape
    slab = rows // N_Z

    def kernel(at_ref, *refs):
        for k, out in enumerate(refs[len(parts) :]):
            at = block_rows(lax.rem(at_ref[0] + k, N_Z), slab)
            total = refs[0][at, :].astype(f32)
            for ref in refs[1 : len(parts)]:
                total = total + ref[at, :].astype(f32)
            out[...] = total.astype(out.dtype)

    shapes = (shaped((slab, width), f32),) + (shaped((slab, width), bf16),) * (N_Z - 1)
    return plain_call(kernel, shapes, *parts, scalars=(places,), mebibytes=8, name="split_z")


def adam_kernel(layout, counts, *refs):
    grads = []
    for count in counts:
        grad = refs[0][...].astype(f32)
        for ref in refs[1:count]:
            grad = grad + ref[...].astype(f32)
        grads.append(grad)
        refs = refs[count:]
    count = len(layout)
    states, outs = refs[: 3 * count], refs[3 * count :]
    for n, (source, start, size, turned) in enumerate(layout):
        weight, first, second = states[3 * n : 3 * n + 3]
        if len(weight.shape) == 3:
            matrices = weight.shape[0]
            lanes = size // matrices
            for k in range(matrices):
                own = [
                    grads[at][:, lane + k * lanes : lane + (k + 1) * lanes] for at, lane in start
                ]
                own = own[0] if len(own) == 1 else jnp.concatenate(own, axis=1)
                new = adam_step(weight[k], own, first[k], second[k], weight_decay, learn_rate)
                for out, value in zip(outs[3 * n : 3 * n + 3], new):
                    out[k] = value
        else:
            part = grads[source][:, start : start + size]
            if turned:
                part = part.T
            new = adam_step(weight[...], part, first[...], second[...], weight_decay, learn_rate)
            for out, value in zip(outs[3 * n : 3 * n + 3], new):
                out[...] = value


def adam_call(groups, layout, *states):
    shapes = tuple(shaped(s.shape, f32) for s in states)
    out = plain_call(
        functools.partial(adam_kernel, layout, [len(group) for group in groups]),
        shapes,
        *[piece for group in groups for piece in group],
        *states,
        mebibytes=16,
        name="adam",
    )
    return [out[3 * n : 3 * n + 3] for n in range(len(layout))]


def tie(*values):
    return lax.optimization_barrier(values)


def local(
    n_x,
    n_y,
    tokens,
    teacher,
    segments,
    live_mask,
    weight_qkv,
    weight_proj,
    weight_up,
    weight_down,
    norm_params,
    first_qkv,
    first_proj,
    first_up,
    first_down,
    first_norms,
    second_qkv,
    second_proj,
    second_up,
    second_down,
    second_norms,
):
    z_at, x_at = lax.axis_index("z"), lax.axis_index("x")
    y_at, core_at = lax.axis_index("y"), lax.axis_index("core")
    rows, model = tokens.shape
    group_rows = segments.shape[0]
    slab = weight_qkv.shape[1]
    width = weight_qkv.shape[2]
    unit = weight_up.shape[1]
    part_rows = min(128, rows)
    wide_rows = min(256, rows)
    depth = N_Z * slab
    sizes = {"z": N_Z, "x": n_x, "y": n_y, "core": N_CORE}
    places = jnp.stack([z_at, x_at]).astype(jnp.int32)
    offsets = [(dc, dy) for dc in range(N_CORE) for dy in range(n_y)]
    other = N_CORE - 1

    def send(value, axis, step):
        size = sizes[axis]
        return lax.ppermute(value, axis, [(i, (i + step) % size) for i in range(size)])

    def send_col(value, dy, dc):
        perm = [
            (y * N_CORE + c, (y + dy) % n_y * N_CORE + (c + dc) % N_CORE)
            for y in range(n_y)
            for c in range(N_CORE)
        ]
        return lax.ppermute(value, ("y", "core"), perm)

    def fetch(value, axis):
        return [value] + [send(value, axis, -k) for k in range(1, sizes[axis])]

    def fetch_z(value):
        return [value] + [send(value, "z", k) for k in range(1, N_Z)]

    def place(dy, dc):
        return ((y_at + dy) % n_y * N_CORE + (core_at + dc) % N_CORE) * rows

    shard_qkv, shard_up, shard_down = plain_call(
        pack_kernel,
        (
            shaped((slab, 4 * width), bf16),
            shaped((slab + DIGITS, unit), bf16),
            shaped((slab, unit), bf16),
        ),
        live_mask.reshape(-1, 128),
        weight_qkv,
        weight_proj,
        weight_up,
        weight_down,
        mebibytes=56,
        name="pack",
    )
    near_qkv = fetch_z(shard_qkv)
    block_qkv = stack_z(near_qkv, slab, places)
    geometry = attend_geometry(segments, live_mask)
    own_live = lax.dynamic_slice_in_dim(
        live_mask, (y_at * N_CORE + core_at) * rows, rows, 0
    ).astype(f32)[:, None]
    spots_here = jnp.stack([place(dy, dc) for dc, dy in offsets]).astype(jnp.int32)
    spots = jnp.stack([place(-dy, -dc) for dc, dy in offsets]).astype(jnp.int32)
    block_qkv, shard_down, shard_up, tokens, geometry, own_live, spots_here, spots = tie(
        block_qkv, shard_down, shard_up, tokens, geometry, own_live, spots_here, spots
    )

    beside_qkv = fetch(block_qkv, "x")
    near_up = fetch_z(shard_up)
    low_one = plain_call(
        first_kernel,
        shaped(tokens.shape, bf16),
        tokens,
        norm_params,
        grid=(rows // part_rows,),
        in_specs=row_blocks(part_rows, model) + [fixed(norm_params.shape)],
        out_specs=row_blocks(part_rows, model)[0],
        mebibytes=8,
        name="first",
    )
    blocks_one = fetch(low_one, "y")
    beside_qkv, near_up, blocks_one, shard_down = tie(beside_qkv, near_up, blocks_one, shard_down)

    block_up = stack_z(near_up, slab, places)
    full_qkv, part_proj = weave([[[part] for part in beside_qkv]], [3 * width], slab, places)
    block_up, part_proj, blocks_one = tie(block_up, part_proj, blocks_one)
    blocks_one = blocks_one + [send(block, "core", -1) for block in blocks_one]
    group_one = place_blocks(blocks_one, spots_here)
    beside_up = fetch(block_up, "x")
    near_down = fetch_z(shard_down)
    full_proj = fetch(part_proj, "y")
    projected = dot(group_one, full_qkv, 1, 0).astype(bf16)
    mixed, bias = attend_forward(projected, geometry, spots, rows)
    mixed, beside_up, near_down, full_proj = tie(mixed, beside_up, near_down, full_proj)

    blocks_mixed = [
        piece if key == (0, 0) else send_col(piece, -key[1], -key[0])
        for key, piece in zip(offsets, mixed)
    ]
    full_proj = [beside_call(full_proj)]
    full_proj.append(send(full_proj[0], "core", -1))
    blocks_down = stack_z(near_down, slab, places, 2)
    beside_down = [fetch(blocks_down[0], "x")]
    full_up = [weave([[[part] for part in beside_up]], [], slab, places)]
    live_count = sum(
        256.0 * part[depth, 0].astype(f32) + 16.0 * part[depth + 1, 0].astype(f32)
        + part[depth + 2, 0].astype(f32)
        for part in beside_up
    ).reshape(1, 1)
    blocks_mixed, full_proj, full_up, live_count, beside_down, blocks_down = tie(
        blocks_mixed, full_proj, full_up, live_count, beside_down, blocks_down
    )
    beside_down.append(fetch(blocks_down[1], "x"))
    full_up.append(send(full_up[0], "core", -1))
    count = len(offsets)
    residual, low_two = plain_call(
        functools.partial(proj_kernel, count, n_y),
        (shaped(tokens.shape, f32), shaped(tokens.shape, bf16)),
        *blocks_mixed,
        *full_proj,
        tokens,
        norm_params,
        grid=(rows // wide_rows,),
        in_specs=row_blocks(wide_rows, *([width] * count))
        + [fixed(part.shape) for part in full_proj]
        + row_blocks(wide_rows, model)
        + [fixed(norm_params.shape)],
        out_specs=tuple(row_blocks(wide_rows, model, model)),
        mebibytes=18,
        name="proj",
    )
    low_two, full_up = tie(low_two, full_up)

    chunk = min(256, rows)
    chunks = range(rows // chunk)
    neighbours = range(1, n_y)
    rows_all = n_y * rows

    def cross(value, n):
        piece = value[n * chunk : (n + 1) * chunk]
        return {dy: send(piece, "y", -dy) for dy in neighbours}

    def spot_of(dy, n):
        return (dy * rows) // chunk + n

    low_far = {0: cross(low_two, 0)}
    hidden = up_call(low_two, full_up, rows_all, 0, ())
    low_far[0], hidden, low_two, beside_down = tie(low_far[0], hidden, low_two, beside_down)
    full_down = [weave([list(zip(*beside_down))], [], slab, places)]
    full_down.append(send(full_down[0], "core", -1))
    far_out = {}
    for n in chunks:
        if n + 1 in chunks:
            low_far[n + 1] = cross(low_two, n + 1)
        for dy in neighbours:
            hidden = up_call(low_far[n][dy], full_up, rows_all, spot_of(dy, n), hidden)
        outs = {
            dy: wide_call(hidden[::2], full_down, chunk, spot_of(dy, n), bf16) for dy in neighbours
        }
        if n + 1 in chunks:
            outs, hidden, low_far[n + 1] = tie(outs, hidden, low_far[n + 1])
        else:
            outs, hidden = tie(outs, hidden)
        if n:
            far_out[n - 1] = tie(far_out[n - 1], outs)[0]
        far_out[n] = {dy: send(outs[dy], "y", dy) for dy in neighbours}
    own_out = wide_call(hidden[::2], full_down, rows, 0, f32)
    own_out, far_out = tie(own_out, far_out)
    far_out = [far_out[n][dy] for n in chunks for dy in neighbours]
    each = len(neighbours)
    grad_output, grad_branch, loss_rows = plain_call(
        functools.partial(loss_kernel, len(chunks), each),
        (shaped(tokens.shape, f32), shaped(tokens.shape, bf16), shaped((8, model), f32)),
        residual,
        teacher,
        own_out,
        *far_out,
        own_live,
        live_count,
        grid=(len(chunks),),
        in_specs=row_blocks(chunk, model, model, model)
        + [fixed((chunk, model))] * len(far_out)
        + row_blocks(chunk, 1)
        + [fixed((1, 1))],
        out_specs=tuple(row_blocks(chunk, model, model) + [fixed((8, model))]),
        scratch=[pltpu.VMEM((chunk, model), f32)],
        mebibytes=20,
        name="loss",
    )
    active, slope = hidden[::2], hidden[1::2]

    grad_far = {0: cross(grad_branch, 0)}
    grad_hidden = hidden_call(grad_branch, slope, full_down, 0, ())
    own_two = wide_call(grad_hidden, full_up, rows, 0, f32)
    grad_far[0], grad_hidden, own_two, grad_branch = tie(
        grad_far[0], grad_hidden, own_two, grad_branch
    )
    def gather_rows(own, far):
        return jnp.concatenate([own] + [far[n][dy] for dy in neighbours for n in chunks], axis=0)

    far_two = {}
    for n in chunks:
        if n + 1 in chunks:
            grad_far[n + 1] = cross(grad_branch, n + 1)
        for dy in neighbours:
            grad_hidden = hidden_call(
                grad_far[n][dy], slope, full_down, spot_of(dy, n), grad_hidden
            )
        outs = {
            dy: wide_call(grad_hidden, full_up, chunk, spot_of(dy, n), bf16) for dy in neighbours
        }
        if n + 1 in chunks:
            outs, grad_hidden, grad_far[n + 1] = tie(outs, grad_hidden, grad_far[n + 1])
        else:
            grad_all = gather_rows(grad_branch, grad_far)
            far_down = dot(grad_all, active[other], 0, 0).astype(bf16)
            outs, grad_hidden, grad_all, far_down, far_two = tie(
                outs, grad_hidden, grad_all, far_down, far_two
            )
        far_two[n] = {dy: send(outs[dy], "y", dy) for dy in neighbours}

    low_all = gather_rows(low_two, low_far)
    far_up = dot(low_all, grad_hidden[other], 0, 0).astype(bf16)
    sent_down, sent_up = send(far_down, "core", 1), send(far_up, "core", 1)
    hold_down = (dot(grad_all, active[0], 0, 0) + sent_down.astype(f32)).astype(bf16)
    halves_down = split_x([[hold_down]], n_x, places)
    hold_up = (dot(low_all, grad_hidden[0], 0, 0) + sent_up.astype(f32)).astype(bf16)
    halves_up = split_x([[hold_up]], n_x, places)
    far_two, halves_down, halves_up = tie(far_two, halves_down, halves_up)
    far_two = [far_two[n][dy] for n in chunks for dy in neighbours]
    grad_residual, grad_low, sums_two = plain_call(
        functools.partial(middle_kernel, len(chunks), each),
        (shaped(tokens.shape, f32), shaped(tokens.shape, bf16), shaped((8, model), f32)),
        own_two,
        *far_two,
        residual,
        grad_output,
        norm_params,
        grid=(len(chunks),),
        in_specs=row_blocks(chunk, model)
        + [fixed((chunk, model))] * len(far_two)
        + row_blocks(chunk, model, model)
        + [fixed(norm_params.shape)],
        out_specs=tuple(row_blocks(chunk, model, model) + [fixed((8, model))]),
        scratch=[pltpu.VMEM((chunk, model), f32)],
        mebibytes=20,
        name="middle",
    )
    pieces_attn = spread_call(grad_low, full_proj, n_y)
    pieces_attn, halves_down, halves_up, grad_low = tie(
        pieces_attn, halves_down, halves_up, grad_low
    )

    def send_back(pieces):
        return [
            piece if key == (0, 0) else send_col(piece, key[1], key[0])
            for key, piece in zip(offsets, pieces)
        ]

    def hop_x(halves):
        return [halves[0]] + [send(halves[dx], "x", dx) for dx in range(1, n_x)]

    def spread_z(pieces):
        return [pieces[0]] + [send(pieces[k], "z", k) for k in range(1, N_Z)]

    lanes = 3 * min(128, width)
    tiles = 3 * width // lanes
    sent_attn = send_back(pieces_attn[0])
    parts_down = hop_x(halves_down)
    far_proj, grad_proj = outer_proj_call(grad_low, blocks_mixed)
    sent_attn, far_proj, grad_proj = tie(sent_attn, far_proj, grad_proj)

    sent_later = [send_back(pieces) for pieces in pieces_attn[1:]]
    sent_proj = send(far_proj, "core", 1)
    grad_projected = attend_backward(projected, sent_attn, spots, geometry[0], bias, 0, ())
    grad_projected, sent_later, sent_proj, parts_down, halves_up = tie(
        grad_projected, sent_later, sent_proj, parts_down, halves_up
    )

    hold_proj = add_lanes(grad_proj, sent_proj)
    pieces_down = split_z(parts_down, places)
    grad_projected, pieces_down, hold_proj, halves_up = tie(
        grad_projected, pieces_down, hold_proj, halves_up
    )
    parts_up = hop_x(halves_up)
    last_down = spread_z(pieces_down)
    part_proj = [hold_proj[0]] + [send(hold_proj[k], "y", k) for k in range(1, n_y)]
    for tile in range(1, tiles):
        grad_projected = attend_backward(
            projected, sent_later[tile - 1], spots, geometry[0], bias, tile, (grad_projected,)
        )
    grad_projected, parts_up, last_down, part_proj = tie(
        grad_projected, parts_up, last_down, part_proj
    )

    far_one, near_one = unproject_call(
        grad_projected,
        full_qkv,
        [place(dy, dc) // rows for dc in reversed(range(N_CORE)) for dy in range(n_y)],
        rows,
    )
    far_one, grad_projected = tie(far_one, grad_projected)
    sent_one = send(far_one, "core", 1)
    grad_qkv = dot(group_one, grad_projected, 0, 0).astype(bf16)
    halves_qkv = split_x([[grad_qkv], part_proj], n_x, places)
    pieces_up = split_z(parts_up, places)
    halves_qkv, sent_one, near_one, pieces_up = tie(halves_qkv, sent_one, near_one, pieces_up)

    parts = [
        near_one[dy * rows : (dy + 1) * rows].astype(f32)
        + sent_one[dy * rows : (dy + 1) * rows].astype(f32)
        for dy in range(n_y)
    ]
    sent_parts = [parts[k].astype(bf16) for k in range(1, n_y)]
    halves_qkv, sent_parts, pieces_up = tie(halves_qkv, sent_parts, pieces_up)
    received = [send(part, "y", k) for k, part in enumerate(sent_parts, 1)]
    parts_qkv = hop_x(halves_qkv)
    last_up = spread_z(pieces_up)
    (new_down,) = adam_call(
        [last_down], [(0, 0, unit, True)], weight_down, first_down, second_down
    )
    parts_qkv, received, last_up, new_down = tie(parts_qkv, received, last_up, new_down)

    pieces_qkv = split_z(parts_qkv, places)
    token_grad, sums = plain_call(
        functools.partial(leave_kernel, len(received)),
        (shaped(tokens.shape, f32), shaped((8, model), f32)),
        parts[0],
        *received,
        tokens,
        grad_residual,
        norm_params,
        sums_two,
        loss_rows,
        grid=(rows // part_rows,),
        in_specs=row_blocks(part_rows, *([model] * (3 + len(received))))
        + [fixed(norm_params.shape), fixed((8, model)), fixed((8, model))],
        out_specs=tuple(row_blocks(part_rows, model) + [fixed((8, model))]),
        scratch=[pltpu.VMEM((8, model), f32)],
        mebibytes=14,
        name="leave",
    )
    sums, token_grad, pieces_qkv = tie(sums, token_grad, pieces_qkv)
    last_qkv = spread_z(pieces_qkv)
    for axis in ("core", "y", "x", "z"):
        step = 1
        while step < sizes[axis]:
            pairs = [(i, i ^ step) for i in range(sizes[axis])]
            sums = sums + lax.ppermute(sums, axis, pairs)
            step *= 2
    (new_up,) = adam_call([last_up], [(0, 0, unit, False)], weight_up, first_up, second_up)
    sums, last_qkv, new_up = tie(sums, last_qkv, new_up)
    loss_sum = jnp.sum(sums[4])
    live_count = live_count[0, 0]

    new_qkv, new_proj = adam_call(
        [last_qkv],
        [(0, [(0, n * lanes) for n in range(tiles)], lanes, False), (0, 3 * width, width, True)],
        weight_qkv,
        first_qkv,
        second_qkv,
        weight_proj,
        first_proj,
        second_proj,
    )
    new_norms = adam_step(norm_params, sums[:4], first_norms, second_norms, 0.0, norm_rate)
    return (
        loss_sum / live_count,
        token_grad,
        new_qkv[0],
        new_proj[0],
        new_up[0],
        new_down[0],
        new_norms[0],
        new_qkv[1],
        new_proj[1],
        new_up[1],
        new_down[1],
        new_norms[1],
        new_qkv[2],
        new_proj[2],
        new_up[2],
        new_down[2],
        new_norms[2],
    )


def solution(mesh):
    n_x = mesh.shape["row"] // N_Z
    n_y = mesh.shape["col"] // N_CORE
    mesh = jax.sharding.Mesh(
        mesh.devices.reshape(N_Z, n_x, n_y, N_CORE), ("z", "x", "y", "core")
    )
    row, col = ("z", "x"), ("y", "core")
    matrices = (P(None, row, col), P(col, row), P(row, col), P(col, row), P())
    tokens = P(row + col, None)
    return jax.shard_map(
        functools.partial(local, n_x, n_y),
        mesh=mesh,
        in_specs=(tokens, tokens, P(row), P(row)) + matrices * 3,
        out_specs=(P(), tokens) + matrices * 3,
        check_vma=False,
    )
```

```python
import functools

import jax
import jax.numpy as jnp
from jax import lax
from jax.experimental import pallas as pl
from jax.experimental.pallas import tpu as pltpu
from jax.sharding import PartitionSpec as P

HEAD_DIM = 64
PATCHES = 577
STEP = 10
WINDOW = 640
QROWS = 320
TILE = 256
DIGITS = 16
SMALL = pl.CostEstimate(flops=1024, bytes_accessed=1024, transcendentals=0)
N_Z = 4
N_CORE = 2

layer_eps = 1e-06
adam_eps = 1e-08
learn_rate = 0.03
norm_rate = 0.25
moment_decay = 0.5
weight_decay = 0.05

bf16 = jnp.bfloat16
f32 = jnp.float32


def norm_forward(values, gain_row, bias_row):
    average = jnp.mean(values, axis=-1, keepdims=True)
    centred = values - average
    variance = jnp.mean(centred * centred, axis=-1, keepdims=True)
    inverse = lax.rsqrt(variance + layer_eps)
    scaled = centred * inverse
    return (scaled * gain_row + bias_row, scaled, inverse)


def norm_backward(upstream, scaled, inverse, gain_row):
    weighted = upstream * gain_row
    return inverse * (
        weighted
        - jnp.mean(weighted, axis=-1, keepdims=True)
        - scaled * jnp.mean(weighted * scaled, axis=-1, keepdims=True)
    )


def gelu_slope(hidden):
    return (
        0.5 * (1.0 + lax.erf(hidden * 0.7071067811865476))
        + hidden * jnp.exp(-0.5 * hidden * hidden) * 0.3989422804014327
    )


def adam_step(weight, gradient, momentum, variance, decay_rate, rate):
    momentum = moment_decay * momentum + (1.0 - moment_decay) * gradient
    variance = moment_decay * variance + (1.0 - moment_decay) * gradient * gradient
    correction = 1.0 - moment_decay**STEP
    direction = momentum / correction / (jnp.sqrt(variance / correction) + adam_eps)
    return (weight - rate * (direction + decay_rate * weight), momentum, variance)


def dot(left, right, left_dim, right_dim):
    return lax.dot_general(
        left, right, (((left_dim,), (right_dim,)), ((), ())), preferred_element_type=f32
    )


def head_lanes(width, head):
    lanes = lax.broadcasted_iota(jnp.int32, (1, width), 1)
    return (lanes >= head * HEAD_DIM) & (lanes < (head + 1) * HEAD_DIM)


def attend_scores(q_part, k_all, mask):
    scores = dot(q_part, k_all, 1, 1) + mask
    weights = jnp.exp(scores - jnp.max(scores, axis=-1, keepdims=True))
    return weights, jnp.sum(weights, axis=-1, keepdims=True)


def image_window(begin, group_rows):
    image = pl.program_id(0)
    start = jnp.minimum(begin[image] // 16 * 16, group_rows - WINDOW)
    first = begin[image] - start
    return image, pl.multiple_of(start, 16), first


def fill_mask(bias, mask_ref):
    for row in range(0, WINDOW, 128):
        rows = row + lax.broadcasted_iota(jnp.int32, (128, WINDOW), 0)
        cols = lax.broadcasted_iota(jnp.int32, (128, WINDOW), 1)
        mask_ref[row : row + 128, :] = jnp.where(rows == cols, 0.0, bias)


def rows_inside(rows, row_start, first):
    ids = row_start + lax.broadcasted_iota(jnp.int32, (rows, 1), 0)
    return (ids >= first) & (ids < first + PATCHES)


def attend_forward_kernel(blocks, begin, spots, code_ref, *refs):
    bias_out, out_ref, mask_ref = refs[-3:]
    image, start, first = image_window(begin, refs[0].shape[0])
    code = code_ref[pl.ds(start, WINDOW), :]
    bias = jnp.where(code == image, 0.0, -1e30).astype(f32).T
    bias_out[0] = bias[0:8, :]
    fill_mask(bias[0:1, :], mask_ref)
    lanes = refs[0].shape[1]

    for tile in range((len(refs) - 3 - blocks) // 3):
        q_ref, k_ref, v_ref = refs[3 * tile : 3 * tile + 3]
        cols = slice(tile * lanes, (tile + 1) * lanes)

        @pl.when(image == 0)
        def _():
            out_ref[:, cols] = v_ref[...]

        k_all = k_ref[pl.ds(start, WINDOW), :]
        v_all = v_ref[pl.ds(start, WINDOW), :]
        for row in range(0, WINDOW, QROWS):
            at = pl.ds(pl.multiple_of(start + row, 16), QROWS)
            q_part = q_ref[at, :] * jnp.asarray(HEAD_DIM ** (-0.5), bf16)
            inside = rows_inside(QROWS, row, first)
            mixed = None
            for head in range(lanes // HEAD_DIM):
                mine = head_lanes(lanes, head)
                q_head = jnp.where(mine, q_part, jnp.zeros_like(q_part))
                weights, totals = attend_scores(q_head, k_all, mask_ref[row : row + QROWS, :])
                part = dot(weights.astype(bf16), v_all, 1, 0) * (1.0 / totals)
                mixed = part if mixed is None else jnp.where(mine, part, mixed)
            out_ref[at, cols] = jnp.where(inside, mixed.astype(bf16), out_ref[at, cols])

    @pl.when(image == pl.num_programs(0) - 1)
    def _():
        for n, block in enumerate(refs[-3 - blocks : -3]):
            rows = block.shape[0]
            block[...] = out_ref[pl.ds(pl.multiple_of(spots[n], rows), rows), :]


def attend_backward_kernel(blocks, begin, spots, bias_ref, *refs):
    out_ref, p_ref, s_ref, go_ref, mask_ref = refs[-5:]
    go_blocks, refs = refs[3 : 3 + blocks], refs[:3]
    image, start, first = image_window(begin, refs[0].shape[0])
    fill_mask(bias_ref[0, 0:1, :], mask_ref)
    lanes = refs[0].shape[1]
    rows = go_blocks[0].shape[0]
    whole = pl.ds(start, WINDOW)
    inside_all = rows_inside(WINDOW, 0, first)

    @pl.when(image == 0)
    def _():
        for n, block_ref in enumerate(go_blocks):
            go_ref[pl.ds(pl.multiple_of(spots[n], rows), rows), :] = block_ref[...]

    for tile in range(len(refs) // 3):
        q_ref, k_ref, v_ref = refs[3 * tile : 3 * tile + 3]
        cols = slice(tile * lanes, (tile + 1) * lanes)
        base = 3 * tile * lanes
        q_cols, k_cols, v_cols = [
            slice(base + n * lanes, base + (n + 1) * lanes) for n in range(3)
        ]

        @pl.when(image == 0)
        def _():
            out_ref[:, base : base + 2 * lanes] = jnp.zeros((out_ref.shape[0], 2 * lanes), bf16)
            out_ref[:, v_cols] = go_ref[:, cols]

        k_all = k_ref[whole, :]
        v_all = v_ref[whole, :]
        q_all = q_ref[whole, :] * jnp.asarray(HEAD_DIM ** (-0.5), bf16)
        go_all = go_ref[whole, cols]
        key_grad = None
        value_grad = None
        for head in range(lanes // HEAD_DIM):
            mine = head_lanes(lanes, head)
            q_mine = jnp.where(mine, q_all, jnp.zeros_like(q_all))
            go_mine = jnp.where(mine, go_all, jnp.zeros_like(go_all))
            for row in range(0, WINDOW, QROWS):
                part = slice(row, row + QROWS)
                at = pl.ds(pl.multiple_of(start + row, 16), QROWS)
                inside = rows_inside(QROWS, row, first)
                weights, totals = attend_scores(q_mine[part], k_all, mask_ref[part, :])
                weights = weights * jnp.where(inside, 1.0 / totals, 0.0)
                weight_grad = dot(go_mine[part], v_all, 1, 1)
                product = weights * weight_grad
                score_grad = (
                    product - weights * jnp.sum(product, axis=-1, keepdims=True)
                ).astype(bf16)
                p_ref[part, :] = weights.astype(bf16)
                s_ref[part, :] = score_grad
                query_grad = (dot(score_grad, k_all, 1, 0) * HEAD_DIM ** (-0.5)).astype(bf16)
                out_ref[at, q_cols] = jnp.where(inside & mine, query_grad, out_ref[at, q_cols])
            key_part = dot(q_mine, s_ref[...], 0, 0)
            value_part = dot(go_mine, p_ref[...], 0, 0)
            key_grad = key_part if key_grad is None else key_grad + key_part
            value_grad = value_part if value_grad is None else value_grad + value_part
        key_rows = key_grad.T.astype(bf16)
        value_rows = value_grad.T.astype(bf16)
        out_ref[whole, k_cols] = jnp.where(inside_all, key_rows, out_ref[whole, k_cols])
        out_ref[whole, v_cols] = jnp.where(inside_all, value_rows, out_ref[whole, v_cols])


def qkv_operands(projected, tile):
    group_rows, total = projected.shape
    lanes = min(128, total // 3)
    if lanes % 128 == 0:
        specs = [
            pl.BlockSpec((group_rows, lanes), functools.partial(lambda n, i, *_: (0, n), 3 * tile + n))
            for n in range(3)
        ]
        return [projected] * 3, specs
    parts = [projected[:, n * lanes : (n + 1) * lanes] for n in range(3)]
    return parts, [fixed((group_rows, lanes))] * 3


def all_operands(projected):
    width = projected.shape[1] // 3
    operands, specs = [], []
    for tile in range(width // min(128, width)):
        more, places = qkv_operands(projected, tile)
        operands += more
        specs += places
    return operands, specs


def attend_forward(projected, geometry, spots, rows):
    begin, code = geometry
    group_rows, total = projected.shape
    width = total // 3
    blocks = group_rows // rows
    images = begin.shape[0]
    operands, specs = all_operands(projected)
    out = plain_call(
        functools.partial(attend_forward_kernel, blocks),
        (shaped((rows, width), bf16),) * blocks + (shaped((images, 8, WINDOW), f32),),
        code,
        *operands,
        grid=begin.shape,
        in_specs=[fixed(code.shape)] + specs,
        out_specs=(fixed((rows, width)),) * blocks
        + (pl.BlockSpec((1, 8, WINDOW), lambda i, *_: (i, 0, 0)),),
        scratch=[pltpu.VMEM((group_rows, width), bf16), pltpu.VMEM((WINDOW, WINDOW), f32)],
        scalars=(begin, spots),
        mebibytes=20,
        name="attention_forward",
    )
    return out[:blocks], out[blocks]


def attend_backward(projected, go_blocks, spots, begin, bias, tile, into):
    group_rows, total = projected.shape
    lanes = min(128, total // 3)
    operands, specs = qkv_operands(projected, tile)
    return plain_call(
        functools.partial(attend_backward_kernel, len(go_blocks)),
        shaped((group_rows, total), bf16),
        bias,
        *operands,
        *go_blocks,
        grid=begin.shape,
        in_specs=[pl.BlockSpec((1, 8, WINDOW), lambda i, *_: (i, 0, 0))]
        + specs
        + [fixed(block.shape) for block in go_blocks],
        out_specs=pl.BlockSpec((group_rows, 3 * lanes), lambda i, *_: (0, tile)),
        scratch=[pltpu.VMEM((WINDOW, WINDOW), bf16)] * 2
        + [pltpu.VMEM((group_rows, lanes), bf16), pltpu.VMEM((WINDOW, WINDOW), f32)],
        scalars=(begin, spots),
        into=into,
        mebibytes=56 if into else 16,
        name="attention_backward",
    )


def attend_geometry(segments, live_mask):
    group_rows = segments.shape[0]
    numbers = jnp.arange(group_rows // PATCHES, dtype=jnp.int32)
    positions = jnp.arange(group_rows, dtype=jnp.int32)
    begin = jnp.min(
        jnp.where(segments[None, :] == numbers[:, None], positions[None, :], group_rows - PATCHES),
        axis=1,
    )
    code = jnp.where(live_mask == 1, segments, -1)
    return begin, jnp.broadcast_to(code[:, None], (group_rows, 128))


def plain_call(kernel, out_shape, *operands, grid=(), in_specs=None, out_specs=None, scratch=(), scalars=(), into=(), mebibytes=16, name=None):
    params = pltpu.CompilerParams(vmem_limit_bytes=mebibytes * 1024 * 1024)
    if in_specs is None:
        in_specs = [pl.BlockSpec(a.shape, functools.partial(lambda n, *_: (0,) * n, a.ndim)) for a in operands]
    in_specs = list(in_specs) + [pl.BlockSpec(memory_space=pl.ANY)] * len(into)
    if out_specs is None:
        out_specs = jax.tree.map(
            lambda s: pl.BlockSpec(s.shape, functools.partial(lambda n, *_: (0,) * n, len(s.shape))), out_shape
        )
    return pl.pallas_call(
        kernel,
        grid_spec=pltpu.PrefetchScalarGridSpec(
            num_scalar_prefetch=len(scalars),
            grid=grid,
            in_specs=in_specs,
            out_specs=out_specs,
            scratch_shapes=list(scratch),
        ),
        out_shape=out_shape,
        input_output_aliases={len(scalars) + len(operands) + n: n for n in range(len(into))},
        compiler_params=params,
        cost_estimate=SMALL,
        name=name,
    )(*scalars, *operands, *into)


def shaped(shape, dtype):
    return jax.ShapeDtypeStruct(tuple(shape), dtype)


def row_blocks(rows, *widths):
    return [pl.BlockSpec((rows, w), lambda i, *_: (i, 0)) for w in widths]


def fixed(shape):
    return pl.BlockSpec(tuple(shape), functools.partial(lambda n, *_: (0,) * n, len(shape)))


def pack_kernel(live_ref, qkv_ref, proj_ref, up_ref, down_ref, qkv_out, up_out, down_out):
    count, slab, width = qkv_ref.shape
    lanes = min(128, width)
    for n in range(count):
        for t in range(width // lanes):
            at = (count * t + n) * lanes
            qkv_out[:, at : at + lanes] = qkv_ref[n][:, t * lanes : (t + 1) * lanes].astype(bf16)
    qkv_out[:, count * width :] = proj_ref[...].T.astype(bf16)
    up_out[:slab, :] = up_ref[...].astype(bf16)
    live = jnp.sum(jnp.sum(live_ref[...].astype(f32), axis=0, keepdims=True), axis=1, keepdims=True)
    high = jnp.floor(live * (1.0 / 256.0))
    middle = jnp.floor(live * (1.0 / 16.0)) - 16.0 * high
    low = live - 256.0 * high - 16.0 * middle
    row = lax.broadcasted_iota(jnp.int32, (DIGITS, up_out.shape[1]), 0)
    digits = jnp.where(row == 0, high, jnp.where(row == 1, middle, jnp.where(row == 2, low, 0.0)))
    up_out[slab:, :] = digits.astype(bf16)
    down_out[...] = down_ref[...].T.astype(bf16)


def first_kernel(tok_ref, par_ref, low_out):
    normed, _, _ = norm_forward(tok_ref[...], par_ref[0:1, :], par_ref[1:2, :])
    low_out[...] = normed.astype(bf16)


def place_blocks(blocks, spots):
    rows, width = blocks[0].shape

    def kernel(spot_ref, *refs):
        for n, ref in enumerate(refs[:-1]):
            refs[-1][pl.ds(pl.multiple_of(spot_ref[n], rows), rows), :] = ref[...]

    return plain_call(
        kernel,
        shaped((rows * len(blocks), width), bf16),
        *blocks,
        scalars=(spots,),
        mebibytes=20,
        name="place_blocks",
    )


def block_rows(block, slab):
    return pl.ds(pl.multiple_of(block * slab, slab), slab)


def stack_z(pieces, slab, places, count=1):
    height, width = pieces[0].shape
    extra = height - slab
    shapes = (shaped((N_Z * slab // count + extra, width), bf16),) * count

    def kernel(at_ref, *refs):
        held = refs[-1]
        for k, ref in enumerate(refs[:N_Z]):
            held[block_rows(lax.rem(at_ref[0] + N_Z - k, N_Z), slab), :] = ref[:slab, :]
        for n, out in enumerate(refs[N_Z:-1]):
            rows = N_Z * slab // count
            out[:rows, :] = held[n * rows : (n + 1) * rows, :]
            if extra:
                digits = refs[0][slab:, :].astype(f32)
                for ref in refs[1:N_Z]:
                    digits = digits + ref[slab:, :].astype(f32)
                out[rows:, :] = digits.astype(bf16)

    out = plain_call(
        kernel,
        shapes,
        *pieces,
        scalars=(places,),
        scratch=[pltpu.VMEM((N_Z * slab, width), bf16)],
        mebibytes=8,
        name="stack_z",
    )
    return out if count > 1 else out[0]


def weave(columns, cuts, slab, places):
    n_x = len(columns[0])
    width = columns[0][0][0].shape[1]
    flat = [piece for column in columns for half in column for piece in half]
    edges = [0, *cuts, width]
    sizes = [stop - start for start, stop in zip(edges[:-1], edges[1:])]

    def kernel(at_ref, *refs):
        outs = refs[len(flat) :]
        used = 0
        for y, column in enumerate(columns):
            for dx, half in enumerate(column):
                x = lax.rem(at_ref[1] + dx, n_x)
                share = N_Z // len(half)
                for z in range(N_Z):
                    piece = refs[used + z // share]
                    at = block_rows(z * n_x + x, slab)
                    row = z % share * slab
                    for out, start, size in zip(outs, edges, sizes):
                        out[at, y * size : (y + 1) * size] = piece[
                            row : row + slab, start : start + size
                        ]
                used += len(half)

    out = plain_call(
        kernel,
        tuple(shaped((N_Z * n_x * slab, size * len(columns)), bf16) for size in sizes),
        *flat,
        scalars=(places,),
        mebibytes=12,
        name="weave",
    )
    return out if cuts else out[0]


def proj_kernel(count, each, *refs):
    blocks, parts = refs[:count], refs[count : count + count // each]
    tok_ref, par_ref, res_out, low_out = refs[count + count // each :]
    total = tok_ref[...]
    for n, block in enumerate(blocks):
        size = block.shape[1]
        part = parts[n // each][:, n % each * size : (n % each + 1) * size]
        total = total + dot(block[...], part, 1, 1)
    res_out[...] = total
    normed, _, _ = norm_forward(total, par_ref[2:3, :], par_ref[3:4, :])
    low_out[...] = normed.astype(bf16)


ERF_TOP = (
    -2.72614225801306e-10,
    2.77068142495902e-08,
    -2.10102402082508e-06,
    -5.69250639462346e-05,
    -7.34990630326855e-04,
    -2.95459980854025e-03,
    -1.60960333262415e-02,
)
ERF_LOW = (
    -1.45660718464996e-05,
    -2.13374055278905e-04,
    -1.68282697438203e-03,
    -7.37332916720468e-03,
    -1.42647390514189e-02,
)


def erf(value):
    value = jnp.clip(value, -4.0, 4.0)
    square = value * value
    top = jnp.full_like(square, ERF_TOP[0])
    for number in ERF_TOP[1:]:
        top = top * square + number
    low = jnp.full_like(square, ERF_LOW[0])
    for number in ERF_LOW[1:]:
        low = low * square + number
    inverse = pl.reciprocal(low, approx=True)
    inverse = inverse * (2.0 - low * inverse)
    return value * top * inverse


def up_kernel(count, low_ref, *refs):
    outs = refs[-2 * count :]
    for n, part in enumerate(refs[:count]):
        hidden = dot(low_ref[...], part[...], 1, 0)
        share = 0.5 * (1.0 + erf(hidden * 0.7071067811865476))
        outs[2 * n][...] = (hidden * share).astype(bf16)
        slope = share + hidden * jnp.exp(-0.5 * hidden * hidden) * 0.3989422804014327
        outs[2 * n + 1][...] = slope.astype(bf16)


def up_call(low, parts, rows_all, spot, into):
    rows, model = low.shape
    width = parts[0].shape[1]
    cols = pl.BlockSpec((rows, TILE), lambda i, *_: (spot, i))
    return plain_call(
        functools.partial(up_kernel, len(parts)),
        (shaped((rows_all, width), bf16),) * (2 * len(parts)),
        low,
        *parts,
        grid=(width // TILE,),
        in_specs=[fixed(low.shape)] + [pl.BlockSpec((model, TILE), lambda i, *_: (0, i))] * len(parts),
        out_specs=(cols,) * (2 * len(parts)),
        into=into,
        mebibytes=14,
        name="up",
    )


def hidden_kernel(count, low_ref, *refs):
    outs = refs[-count:]
    for n in range(count):
        slope, part = refs[n], refs[count + n]
        outs[n][...] = (dot(low_ref[...], part[...], 1, 0) * slope[...].astype(f32)).astype(bf16)


def hidden_call(low, slopes, parts, spot, into):
    rows, model = low.shape
    width = parts[0].shape[1]
    cols = pl.BlockSpec((rows, TILE), lambda i, *_: (spot, i))
    return plain_call(
        functools.partial(hidden_kernel, len(parts)),
        tuple(shaped(slope.shape, bf16) for slope in slopes),
        low,
        *slopes,
        *parts,
        grid=(width // TILE,),
        in_specs=[fixed(low.shape)]
        + [cols] * len(parts)
        + [pl.BlockSpec((model, TILE), lambda i, *_: (0, i))] * len(parts),
        out_specs=(cols,) * len(parts),
        into=into,
        mebibytes=14,
        name="hidden",
    )


def wide_kernel(count, extra, *refs):
    total = dot(refs[0][...], refs[count][...], 1, 1)
    for n in range(1, count):
        total = total + dot(refs[n][...], refs[count + n][...], 1, 1)
    if extra:
        total = total + (refs[2 * count][...] - refs[2 * count + 1][...])
    refs[-1][...] = total.astype(refs[-1].dtype)


def wide_call(values, parts, rows, spot, kind, extra=()):
    model, width = parts[0].shape
    return plain_call(
        functools.partial(wide_kernel, len(values), bool(extra)),
        shaped((rows, model), kind),
        *values,
        *parts,
        *extra,
        grid=(model // TILE,),
        in_specs=[pl.BlockSpec((rows, width), lambda i, *_: (spot, 0))] * len(values)
        + [pl.BlockSpec((TILE, width), lambda i, *_: (i, 0))] * len(parts)
        + [pl.BlockSpec((rows, TILE), lambda i, *_: (0, i))] * len(extra),
        out_specs=pl.BlockSpec((rows, TILE), lambda i, *_: (0, i)),
        mebibytes=16 if extra else 14,
        name="wide",
    )


def loss_kernel(chunks, each, *refs):
    own_ref, received = refs[0], refs[1 : 1 + chunks * each]
    live_ref, count_ref, grad_out, low_out, loss_out, far_ref = refs[1 + chunks * each :]
    add_received(received, each, far_ref)
    error = own_ref[...] + far_ref[...]
    weighted = live_ref[...] * error
    grad = 2.0 * weighted / count_ref[...]
    grad_out[...] = grad
    low_out[...] = grad.astype(bf16)
    sums = jnp.sum(weighted * error, axis=0, keepdims=True)
    sums = jnp.concatenate([sums, jnp.zeros((7, sums.shape[1]), f32)], axis=0)
    loss_out[...] = jnp.where(pl.program_id(0) == 0, sums, loss_out[...] + sums)


def add_received(received, each, far_ref):
    for n in range(len(received) // each):

        @pl.when(pl.program_id(0) == n)
        def _():
            total = received[n * each][...].astype(f32)
            for ref in received[n * each + 1 : (n + 1) * each]:
                total = total + ref[...].astype(f32)
            far_ref[...] = total


def beside_call(parts):
    rows, width = parts[0].shape

    def kernel(*refs):
        for n, ref in enumerate(refs[:-1]):
            refs[-1][:, n * width : (n + 1) * width] = ref[...]

    return plain_call(
        kernel, shaped((rows, width * len(parts)), bf16), *parts, mebibytes=8, name="beside"
    )


def spread_kernel(each, tiles, low_ref, *refs):
    count = len(refs) // (1 + each * tiles)
    outs = refs[count:]
    for n in range(count * each):
        size = refs[0].shape[1] // each
        part = refs[n // each][:, n % each * size : (n % each + 1) * size]
        piece = dot(low_ref[...], part, 1, 0).astype(bf16)
        lanes = size // tiles
        for tile in range(tiles):
            outs[tile * count * each + n][...] = piece[:, tile * lanes : (tile + 1) * lanes]


def spread_call(low, parts, each):
    width = parts[0].shape[1] // each
    lanes = min(128, width)
    count = len(parts) * each
    out = plain_call(
        functools.partial(spread_kernel, each, width // lanes),
        tuple(shaped((low.shape[0], lanes), bf16) for _ in range(count * (width // lanes))),
        low,
        *parts,
        mebibytes=12,
        name="spread",
    )
    return [out[n : n + count] for n in range(0, len(out), count)]


def unproject_kernel(half, spots, grad_ref, part_ref, far_out, near_out):
    piece = dot(grad_ref[...], part_ref[...], 1, 1)

    @pl.when(pl.program_id(0) < half)
    def _():
        far_out[...] = piece.astype(bf16)

    @pl.when(pl.program_id(0) >= half)
    def _():
        near_out[...] = piece.astype(bf16)


def unproject_call(grads, part, blocks, rows):
    half = len(blocks) // 2
    model, width = part.shape
    return plain_call(
        functools.partial(unproject_kernel, half),
        (shaped((half * rows, model), bf16),) * 2,
        grads,
        part,
        grid=(len(blocks),),
        in_specs=[
            pl.BlockSpec((rows, width), lambda i, spots: (spots[i], 0)),
            fixed(part.shape),
        ],
        out_specs=(
            pl.BlockSpec((rows, model), lambda i, spots: (jnp.minimum(i, half - 1), 0)),
            pl.BlockSpec((rows, model), lambda i, spots: (jnp.maximum(i - half, 0), 0)),
        ),
        scalars=(jnp.stack(blocks).astype(jnp.int32),),
        mebibytes=48,
        name="unproject",
    )


def outer_proj_kernel(half, low_ref, *refs):
    blocks, (far_out, *near) = refs[: 2 * half], refs[2 * half :]
    turned = low_ref[...].astype(f32).T.astype(bf16)
    width = blocks[0].shape[1]
    for n in range(half):
        far_out[:, n * width : (n + 1) * width] = dot(turned, blocks[half + n][...], 1, 0).astype(bf16)
        near[n][...] = dot(turned, blocks[n][...], 1, 0).astype(bf16)


def outer_proj_call(low, blocks):
    model = low.shape[1]
    width = blocks[0].shape[1]
    half = len(blocks) // 2
    out = plain_call(
        functools.partial(outer_proj_kernel, half),
        (shaped((model, half * width), bf16),) + (shaped((model, width), bf16),) * half,
        low,
        *blocks,
        mebibytes=14,
        name="outer_proj",
    )
    return out[0], out[1:]


def add_lanes(own, received):
    width = own[0].shape[1]

    def kernel(*refs):
        got = refs[len(own)]
        for n, ref in enumerate(refs[: len(own)]):
            other = got[:, n * width : (n + 1) * width].astype(f32)
            refs[len(own) + 1 + n][...] = (ref[...].astype(f32) + other).astype(bf16)

    return plain_call(
        kernel,
        tuple(shaped(part.shape, bf16) for part in own),
        *own,
        received,
        mebibytes=8,
        name="add_lanes",
    )


def norm_sums(grad, scaled, out_ref, first):
    sums = jnp.concatenate(
        [
            jnp.sum(grad * scaled, axis=0, keepdims=True),
            jnp.sum(grad, axis=0, keepdims=True),
            jnp.zeros((6, grad.shape[1]), f32),
        ],
        axis=0,
    )
    out_ref[...] = jnp.where(first, sums, out_ref[...] + sums)


def middle_kernel(chunks, each, *refs):
    grad_ref, received = refs[0], refs[1 : 1 + chunks * each]
    res_ref, gout_ref, par_ref, full_out, low_out, sum_out, far_ref = refs[1 + chunks * each :]
    add_received(received, each, far_ref)
    _, scaled, inverse = norm_forward(res_ref[...], par_ref[2:3, :], par_ref[3:4, :])
    grad = grad_ref[...] + far_ref[...]
    full = gout_ref[...] + norm_backward(grad, scaled, inverse, par_ref[2:3, :])
    full_out[...] = full
    low_out[...] = full.astype(bf16)
    norm_sums(grad, scaled, sum_out, pl.program_id(0) == 0)


def leave_kernel(count, *refs):
    own_ref, received = refs[0], refs[1 : 1 + count]
    tok_ref, res_ref, par_ref, two_ref, loss_ref, out_ref, sum_out, sum_ref = refs[1 + count :]
    _, scaled, inverse = norm_forward(tok_ref[...], par_ref[0:1, :], par_ref[1:2, :])
    grad = own_ref[...]
    for ref in received:
        grad = grad + ref[...].astype(f32)
    out_ref[...] = res_ref[...] + norm_backward(grad, scaled, inverse, par_ref[0:1, :])
    norm_sums(grad, scaled, sum_ref, pl.program_id(0) == 0)
    sum_out[...] = jnp.concatenate(
        [sum_ref[0:2, :], two_ref[0:2, :], loss_ref[0:1, :], jnp.zeros((3, grad.shape[1]), f32)],
        axis=0,
    )


def split_x(parts, n_x, places):
    model = parts[0][0].shape[0]
    slab = model // (N_Z * n_x)
    total = sum(part[0].shape[1] for part in parts)
    flat = [piece for part in parts for piece in part]

    def kernel(at_ref, *refs):
        outs = refs[len(flat) :]
        for dx in range(n_x):
            x = lax.rem(at_ref[1] + dx, n_x)
            for z in range(N_Z):
                at = block_rows(z * n_x + x, slab)
                lane = 0
                used = 0
                for part in parts:
                    value = refs[used][at, :]
                    size = value.shape[1]
                    if len(part) > 1:
                        value = value.astype(f32)
                        for ref in refs[used + 1 : used + len(part)]:
                            value = value + ref[at, :].astype(f32)
                        value = value.astype(bf16)
                    outs[dx][z * slab : (z + 1) * slab, lane : lane + size] = value
                    lane += size
                    used += len(part)

    return plain_call(
        kernel,
        tuple(shaped((model // n_x, total), bf16) for _ in range(n_x)),
        *flat,
        scalars=(places,),
        mebibytes=12,
        name="split_x",
    )


def split_z(parts, places):
    rows, width = parts[0].shape
    slab = rows // N_Z

    def kernel(at_ref, *refs):
        for k, out in enumerate(refs[len(parts) :]):
            at = block_rows(lax.rem(at_ref[0] + k, N_Z), slab)
            total = refs[0][at, :].astype(f32)
            for ref in refs[1 : len(parts)]:
                total = total + ref[at, :].astype(f32)
            out[...] = total.astype(out.dtype)

    shapes = (shaped((slab, width), f32),) + (shaped((slab, width), bf16),) * (N_Z - 1)
    return plain_call(kernel, shapes, *parts, scalars=(places,), mebibytes=8, name="split_z")


def adam_kernel(layout, counts, *refs):
    grads = []
    for count in counts:
        grad = refs[0][...].astype(f32)
        for ref in refs[1:count]:
            grad = grad + ref[...].astype(f32)
        grads.append(grad)
        refs = refs[count:]
    count = len(layout)
    states, outs = refs[: 3 * count], refs[3 * count :]
    for n, (source, start, size, turned) in enumerate(layout):
        weight, first, second = states[3 * n : 3 * n + 3]
        if len(weight.shape) == 3:
            matrices = weight.shape[0]
            lanes = size // matrices
            for k in range(matrices):
                own = [
                    grads[at][:, lane + k * lanes : lane + (k + 1) * lanes] for at, lane in start
                ]
                own = own[0] if len(own) == 1 else jnp.concatenate(own, axis=1)
                new = adam_step(weight[k], own, first[k], second[k], weight_decay, learn_rate)
                for out, value in zip(outs[3 * n : 3 * n + 3], new):
                    out[k] = value
        else:
            part = grads[source][:, start : start + size]
            if turned:
                part = part.T
            new = adam_step(weight[...], part, first[...], second[...], weight_decay, learn_rate)
            for out, value in zip(outs[3 * n : 3 * n + 3], new):
                out[...] = value


def adam_call(groups, layout, *states):
    shapes = tuple(shaped(s.shape, f32) for s in states)
    out = plain_call(
        functools.partial(adam_kernel, layout, [len(group) for group in groups]),
        shapes,
        *[piece for group in groups for piece in group],
        *states,
        mebibytes=16,
        name="adam",
    )
    return [out[3 * n : 3 * n + 3] for n in range(len(layout))]


def tie(*values):
    return lax.optimization_barrier(values)


def local(
    n_x,
    n_y,
    tokens,
    teacher,
    segments,
    live_mask,
    weight_qkv,
    weight_proj,
    weight_up,
    weight_down,
    norm_params,
    first_qkv,
    first_proj,
    first_up,
    first_down,
    first_norms,
    second_qkv,
    second_proj,
    second_up,
    second_down,
    second_norms,
):
    z_at, x_at = lax.axis_index("z"), lax.axis_index("x")
    y_at, core_at = lax.axis_index("y"), lax.axis_index("core")
    rows, model = tokens.shape
    group_rows = segments.shape[0]
    slab = weight_qkv.shape[1]
    width = weight_qkv.shape[2]
    unit = weight_up.shape[1]
    part_rows = min(128, rows)
    wide_rows = min(256, rows)
    depth = N_Z * slab
    sizes = {"z": N_Z, "x": n_x, "y": n_y, "core": N_CORE}
    places = jnp.stack([z_at, x_at]).astype(jnp.int32)
    offsets = [(dc, dy) for dc in range(N_CORE) for dy in range(n_y)]
    other = N_CORE - 1

    def send(value, axis, step):
        size = sizes[axis]
        return lax.ppermute(value, axis, [(i, (i + step) % size) for i in range(size)])

    def send_col(value, dy, dc):
        perm = [
            (y * N_CORE + c, (y + dy) % n_y * N_CORE + (c + dc) % N_CORE)
            for y in range(n_y)
            for c in range(N_CORE)
        ]
        return lax.ppermute(value, ("y", "core"), perm)

    def fetch(value, axis):
        return [value] + [send(value, axis, -k) for k in range(1, sizes[axis])]

    def fetch_z(value):
        return [value] + [send(value, "z", k) for k in range(1, N_Z)]

    def place(dy, dc):
        return ((y_at + dy) % n_y * N_CORE + (core_at + dc) % N_CORE) * rows

    shard_qkv, shard_up, shard_down = plain_call(
        pack_kernel,
        (
            shaped((slab, 4 * width), bf16),
            shaped((slab + DIGITS, unit), bf16),
            shaped((slab, unit), bf16),
        ),
        live_mask.reshape(-1, 128),
        weight_qkv,
        weight_proj,
        weight_up,
        weight_down,
        mebibytes=56,
        name="pack",
    )
    near_qkv = fetch_z(shard_qkv)
    block_qkv = stack_z(near_qkv, slab, places)
    geometry = attend_geometry(segments, live_mask)
    own_live = lax.dynamic_slice_in_dim(
        live_mask, (y_at * N_CORE + core_at) * rows, rows, 0
    ).astype(f32)[:, None]
    spots_here = jnp.stack([place(dy, dc) for dc, dy in offsets]).astype(jnp.int32)
    spots = jnp.stack([place(-dy, -dc) for dc, dy in offsets]).astype(jnp.int32)
    block_qkv, shard_down, shard_up, tokens, geometry, own_live, spots_here, spots = tie(
        block_qkv, shard_down, shard_up, tokens, geometry, own_live, spots_here, spots
    )

    beside_qkv = fetch(block_qkv, "x")
    near_up = fetch_z(shard_up)
    low_one = plain_call(
        first_kernel,
        shaped(tokens.shape, bf16),
        tokens,
        norm_params,
        grid=(rows // part_rows,),
        in_specs=row_blocks(part_rows, model) + [fixed(norm_params.shape)],
        out_specs=row_blocks(part_rows, model)[0],
        mebibytes=8,
        name="first",
    )
    blocks_one = fetch(low_one, "y")
    beside_qkv, near_up, blocks_one, shard_down = tie(beside_qkv, near_up, blocks_one, shard_down)

    block_up = stack_z(near_up, slab, places)
    full_qkv, part_proj = weave([[[part] for part in beside_qkv]], [3 * width], slab, places)
    block_up, part_proj, blocks_one = tie(block_up, part_proj, blocks_one)
    blocks_one = blocks_one + [send(block, "core", -1) for block in blocks_one]
    group_one = place_blocks(blocks_one, spots_here)
    beside_up = fetch(block_up, "x")
    near_down = fetch_z(shard_down)
    full_proj = fetch(part_proj, "y")
    projected = dot(group_one, full_qkv, 1, 0).astype(bf16)
    mixed, bias = attend_forward(projected, geometry, spots, rows)
    mixed, beside_up, near_down, full_proj = tie(mixed, beside_up, near_down, full_proj)

    blocks_mixed = [
        piece if key == (0, 0) else send_col(piece, -key[1], -key[0])
        for key, piece in zip(offsets, mixed)
    ]
    full_proj = [beside_call(full_proj)]
    full_proj.append(send(full_proj[0], "core", -1))
    blocks_down = stack_z(near_down, slab, places, 2)
    beside_down = [fetch(blocks_down[0], "x")]
    full_up = [weave([[[part] for part in beside_up]], [], slab, places)]
    live_count = sum(
        256.0 * part[depth, 0].astype(f32) + 16.0 * part[depth + 1, 0].astype(f32)
        + part[depth + 2, 0].astype(f32)
        for part in beside_up
    ).reshape(1, 1)
    blocks_mixed, full_proj, full_up, live_count, beside_down, blocks_down = tie(
        blocks_mixed, full_proj, full_up, live_count, beside_down, blocks_down
    )
    full_up.append(send(full_up[0], "core", -1))
    count = len(offsets)
    residual, low_two = plain_call(
        functools.partial(proj_kernel, count, n_y),
        (shaped(tokens.shape, f32), shaped(tokens.shape, bf16)),
        *blocks_mixed,
        *full_proj,
        tokens,
        norm_params,
        grid=(rows // wide_rows,),
        in_specs=row_blocks(wide_rows, *([width] * count))
        + [fixed(part.shape) for part in full_proj]
        + row_blocks(wide_rows, model)
        + [fixed(norm_params.shape)],
        out_specs=tuple(row_blocks(wide_rows, model, model)),
        mebibytes=18,
        name="proj",
    )
    low_two, full_up, blocks_down = tie(low_two, full_up, blocks_down)
    beside_down.append(fetch(blocks_down[1], "x"))

    chunk = min(256, rows)
    chunks = range(rows // chunk)
    neighbours = range(1, n_y)
    rows_all = n_y * rows

    def cross(value, n):
        piece = value[n * chunk : (n + 1) * chunk]
        return {dy: send(piece, "y", -dy) for dy in neighbours}

    def spot_of(dy, n):
        return (dy * rows) // chunk + n

    low_far = {0: cross(low_two, 0)}
    hidden = up_call(low_two, full_up, rows_all, 0, ())
    low_far[0], hidden, low_two, beside_down = tie(low_far[0], hidden, low_two, beside_down)
    if len(chunks) > 1:
        low_far[1] = cross(low_two, 1)
    full_down = [weave([list(zip(*beside_down))], [], slab, places)]
    full_down.append(send(full_down[0], "core", -1))
    far_out = {}
    for n in chunks:
        if n and n + 1 in chunks:
            low_far[n + 1] = cross(low_two, n + 1)
        for dy in neighbours:
            hidden = up_call(low_far[n][dy], full_up, rows_all, spot_of(dy, n), hidden)
        outs = {
            dy: wide_call(hidden[::2], full_down, chunk, spot_of(dy, n), bf16) for dy in neighbours
        }
        if n + 1 in chunks:
            outs, hidden, low_far[n + 1] = tie(outs, hidden, low_far[n + 1])
        else:
            outs, hidden = tie(outs, hidden)
        if n:
            far_out[n - 1] = tie(far_out[n - 1], outs)[0]
        far_out[n] = {dy: send(outs[dy], "y", dy) for dy in neighbours}
    own_out = wide_call(hidden[::2], full_down, rows, 0, f32, (residual, teacher))
    own_out, far_out = tie(own_out, far_out)
    far_out = [far_out[n][dy] for n in chunks for dy in neighbours]
    each = len(neighbours)
    grad_output, grad_branch, loss_rows = plain_call(
        functools.partial(loss_kernel, len(chunks), each),
        (shaped(tokens.shape, f32), shaped(tokens.shape, bf16), shaped((8, model), f32)),
        own_out,
        *far_out,
        own_live,
        live_count,
        grid=(len(chunks),),
        in_specs=row_blocks(chunk, model)
        + [fixed((chunk, model))] * len(far_out)
        + row_blocks(chunk, 1)
        + [fixed((1, 1))],
        out_specs=tuple(row_blocks(chunk, model, model) + [fixed((8, model))]),
        scratch=[pltpu.VMEM((chunk, model), f32)],
        mebibytes=20,
        name="loss",
    )
    active, slope = hidden[::2], hidden[1::2]

    grad_far = {0: cross(grad_branch, 0)}
    grad_hidden = hidden_call(grad_branch, slope, full_down, 0, ())
    own_two = wide_call(grad_hidden, full_up, rows, 0, f32)
    grad_far[0], grad_hidden, own_two, grad_branch = tie(
        grad_far[0], grad_hidden, own_two, grad_branch
    )
    def gather_rows(own, far):
        return jnp.concatenate([own] + [far[n][dy] for dy in neighbours for n in chunks], axis=0)

    far_two = {}
    for n in chunks:
        if n + 1 in chunks:
            grad_far[n + 1] = cross(grad_branch, n + 1)
        for dy in neighbours:
            grad_hidden = hidden_call(
                grad_far[n][dy], slope, full_down, spot_of(dy, n), grad_hidden
            )
        outs = {
            dy: wide_call(grad_hidden, full_up, chunk, spot_of(dy, n), bf16) for dy in neighbours
        }
        if n + 1 in chunks:
            outs, grad_hidden, grad_far[n + 1] = tie(outs, grad_hidden, grad_far[n + 1])
        else:
            grad_all = gather_rows(grad_branch, grad_far)
            far_down = dot(grad_all, active[other], 0, 0).astype(bf16)
            outs, grad_hidden, grad_all, far_down, far_two = tie(
                outs, grad_hidden, grad_all, far_down, far_two
            )
        far_two[n] = {dy: send(outs[dy], "y", dy) for dy in neighbours}

    low_all = gather_rows(low_two, low_far)
    far_up = dot(low_all, grad_hidden[other], 0, 0).astype(bf16)
    sent_down, sent_up = send(far_down, "core", 1), send(far_up, "core", 1)
    hold_down = (dot(grad_all, active[0], 0, 0) + sent_down.astype(f32)).astype(bf16)
    halves_down = split_x([[hold_down]], n_x, places)
    hold_up = (dot(low_all, grad_hidden[0], 0, 0) + sent_up.astype(f32)).astype(bf16)
    halves_up = split_x([[hold_up]], n_x, places)
    far_two, halves_down, halves_up = tie(far_two, halves_down, halves_up)
    far_two = [far_two[n][dy] for n in chunks for dy in neighbours]
    grad_residual, grad_low, sums_two = plain_call(
        functools.partial(middle_kernel, len(chunks), each),
        (shaped(tokens.shape, f32), shaped(tokens.shape, bf16), shaped((8, model), f32)),
        own_two,
        *far_two,
        residual,
        grad_output,
        norm_params,
        grid=(len(chunks),),
        in_specs=row_blocks(chunk, model)
        + [fixed((chunk, model))] * len(far_two)
        + row_blocks(chunk, model, model)
        + [fixed(norm_params.shape)],
        out_specs=tuple(row_blocks(chunk, model, model) + [fixed((8, model))]),
        scratch=[pltpu.VMEM((chunk, model), f32)],
        mebibytes=20,
        name="middle",
    )
    pieces_attn = spread_call(grad_low, full_proj, n_y)
    pieces_attn, halves_down, halves_up, grad_low = tie(
        pieces_attn, halves_down, halves_up, grad_low
    )

    def send_back(pieces):
        return [
            piece if key == (0, 0) else send_col(piece, key[1], key[0])
            for key, piece in zip(offsets, pieces)
        ]

    def hop_x(halves):
        return [halves[0]] + [send(halves[dx], "x", dx) for dx in range(1, n_x)]

    def spread_z(pieces):
        return [pieces[0]] + [send(pieces[k], "z", k) for k in range(1, N_Z)]

    lanes = 3 * min(128, width)
    tiles = 3 * width // lanes
    sent_attn = send_back(pieces_attn[0])
    parts_down = hop_x(halves_down)
    far_proj, grad_proj = outer_proj_call(grad_low, blocks_mixed)
    sent_attn, far_proj, grad_proj = tie(sent_attn, far_proj, grad_proj)

    sent_later = [send_back(pieces) for pieces in pieces_attn[1:]]
    sent_proj = send(far_proj, "core", 1)
    grad_projected = attend_backward(projected, sent_attn, spots, geometry[0], bias, 0, ())
    grad_projected, sent_later, sent_proj, parts_down, halves_up = tie(
        grad_projected, sent_later, sent_proj, parts_down, halves_up
    )

    hold_proj = add_lanes(grad_proj, sent_proj)
    pieces_down = split_z(parts_down, places)
    grad_projected, pieces_down, hold_proj, halves_up = tie(
        grad_projected, pieces_down, hold_proj, halves_up
    )
    parts_up = hop_x(halves_up)
    last_down = spread_z(pieces_down)
    part_proj = [hold_proj[0]] + [send(hold_proj[k], "y", k) for k in range(1, n_y)]
    for tile in range(1, tiles):
        grad_projected = attend_backward(
            projected, sent_later[tile - 1], spots, geometry[0], bias, tile, (grad_projected,)
        )
    grad_projected, parts_up, last_down, part_proj = tie(
        grad_projected, parts_up, last_down, part_proj
    )

    far_one, near_one = unproject_call(
        grad_projected,
        full_qkv,
        [place(dy, dc) // rows for dc in reversed(range(N_CORE)) for dy in range(n_y)],
        rows,
    )
    far_one, grad_projected = tie(far_one, grad_projected)
    sent_one = send(far_one, "core", 1)
    grad_qkv = dot(group_one, grad_projected, 0, 0).astype(bf16)
    halves_qkv = split_x([[grad_qkv], part_proj], n_x, places)
    halves_qkv, sent_one, near_one, parts_up = tie(halves_qkv, sent_one, near_one, parts_up)

    parts = [
        near_one[dy * rows : (dy + 1) * rows].astype(f32)
        + sent_one[dy * rows : (dy + 1) * rows].astype(f32)
        for dy in range(n_y)
    ]
    sent_parts = [parts[k].astype(bf16) for k in range(1, n_y)]
    halves_qkv, sent_parts, parts_up = tie(halves_qkv, sent_parts, parts_up)
    received = [send(part, "y", k) for k, part in enumerate(sent_parts, 1)]
    parts_qkv = hop_x(halves_qkv)
    last_up = spread_z(split_z(parts_up, places))
    (new_down,) = adam_call(
        [last_down], [(0, 0, unit, True)], weight_down, first_down, second_down
    )
    parts_qkv, received, last_up, new_down = tie(parts_qkv, received, last_up, new_down)

    pieces_qkv = split_z(parts_qkv, places)
    token_grad, sums = plain_call(
        functools.partial(leave_kernel, len(received)),
        (shaped(tokens.shape, f32), shaped((8, model), f32)),
        parts[0],
        *received,
        tokens,
        grad_residual,
        norm_params,
        sums_two,
        loss_rows,
        grid=(rows // part_rows,),
        in_specs=row_blocks(part_rows, *([model] * (3 + len(received))))
        + [fixed(norm_params.shape), fixed((8, model)), fixed((8, model))],
        out_specs=tuple(row_blocks(part_rows, model) + [fixed((8, model))]),
        scratch=[pltpu.VMEM((8, model), f32)],
        mebibytes=14,
        name="leave",
    )
    sums, token_grad, pieces_qkv = tie(sums, token_grad, pieces_qkv)
    last_qkv = spread_z(pieces_qkv)
    for axis in ("core", "y", "x", "z"):
        step = 1
        while step < sizes[axis]:
            pairs = [(i, i ^ step) for i in range(sizes[axis])]
            sums = sums + lax.ppermute(sums, axis, pairs)
            step *= 2
    (new_up,) = adam_call([last_up], [(0, 0, unit, False)], weight_up, first_up, second_up)
    sums, last_qkv, new_up = tie(sums, last_qkv, new_up)
    loss_sum = jnp.sum(sums[4])
    live_count = live_count[0, 0]

    new_qkv, new_proj = adam_call(
        [last_qkv],
        [(0, [(0, n * lanes) for n in range(tiles)], lanes, False), (0, 3 * width, width, True)],
        weight_qkv,
        first_qkv,
        second_qkv,
        weight_proj,
        first_proj,
        second_proj,
    )
    new_norms = adam_step(norm_params, sums[:4], first_norms, second_norms, 0.0, norm_rate)
    return (
        loss_sum / live_count,
        token_grad,
        new_qkv[0],
        new_proj[0],
        new_up[0],
        new_down[0],
        new_norms[0],
        new_qkv[1],
        new_proj[1],
        new_up[1],
        new_down[1],
        new_norms[1],
        new_qkv[2],
        new_proj[2],
        new_up[2],
        new_down[2],
        new_norms[2],
    )


def solution(mesh):
    n_x = mesh.shape["row"] // N_Z
    n_y = mesh.shape["col"] // N_CORE
    mesh = jax.sharding.Mesh(
        mesh.devices.reshape(N_Z, n_x, n_y, N_CORE), ("z", "x", "y", "core")
    )
    row, col = ("z", "x"), ("y", "core")
    matrices = (P(None, row, col), P(col, row), P(row, col), P(col, row), P())
    tokens = P(row + col, None)
    return jax.shard_map(
        functools.partial(local, n_x, n_y),
        mesh=mesh,
        in_specs=(tokens, tokens, P(row), P(row)) + matrices * 3,
        out_specs=(P(), tokens) + matrices * 3,
        check_vma=False,
    )
```

```python
import functools

import jax
import jax.numpy as jnp
from jax import lax
from jax.experimental import pallas as pl
from jax.experimental.pallas import tpu as pltpu
from jax.sharding import PartitionSpec as P

HEAD_DIM = 64
PATCHES = 577
STEP = 10
WINDOW = 640
QROWS = 640
TILE = 256
DIGITS = 16
SMALL = pl.CostEstimate(flops=1024, bytes_accessed=1024, transcendentals=0)
N_Z = 4
N_CORE = 2

layer_eps = 1e-06
adam_eps = 1e-08
learn_rate = 0.03
norm_rate = 0.25
moment_decay = 0.5
weight_decay = 0.05

bf16 = jnp.bfloat16
f32 = jnp.float32


def norm_forward(values, gain_row, bias_row):
    average = jnp.mean(values, axis=-1, keepdims=True)
    centred = values - average
    variance = jnp.mean(centred * centred, axis=-1, keepdims=True)
    inverse = lax.rsqrt(variance + layer_eps)
    scaled = centred * inverse
    return (scaled * gain_row + bias_row, scaled, inverse)


def norm_backward(upstream, scaled, inverse, gain_row):
    weighted = upstream * gain_row
    return inverse * (
        weighted
        - jnp.mean(weighted, axis=-1, keepdims=True)
        - scaled * jnp.mean(weighted * scaled, axis=-1, keepdims=True)
    )


def gelu_slope(hidden):
    return (
        0.5 * (1.0 + lax.erf(hidden * 0.7071067811865476))
        + hidden * jnp.exp(-0.5 * hidden * hidden) * 0.3989422804014327
    )


def adam_step(weight, gradient, momentum, variance, decay_rate, rate):
    momentum = moment_decay * momentum + (1.0 - moment_decay) * gradient
    variance = moment_decay * variance + (1.0 - moment_decay) * gradient * gradient
    correction = 1.0 - moment_decay**STEP
    direction = momentum / correction / (jnp.sqrt(variance / correction) + adam_eps)
    return (weight - rate * (direction + decay_rate * weight), momentum, variance)


def dot(left, right, left_dim, right_dim):
    return lax.dot_general(
        left, right, (((left_dim,), (right_dim,)), ((), ())), preferred_element_type=f32
    )


def head_lanes(width, head):
    lanes = lax.broadcasted_iota(jnp.int32, (1, width), 1)
    return (lanes >= head * HEAD_DIM) & (lanes < (head + 1) * HEAD_DIM)


def attend_scores(q_part, k_all, mask):
    scores = dot(q_part, k_all, 1, 1) + mask
    weights = jnp.exp(scores - jnp.max(scores, axis=-1, keepdims=True))
    return weights, jnp.sum(weights, axis=-1, keepdims=True)


def image_window(begin, group_rows):
    image = pl.program_id(0)
    start = jnp.minimum(begin[image] // 16 * 16, group_rows - WINDOW)
    first = begin[image] - start
    return image, pl.multiple_of(start, 16), first


def fill_mask(bias, mask_ref):
    for row in range(0, WINDOW, 128):
        rows = row + lax.broadcasted_iota(jnp.int32, (128, WINDOW), 0)
        cols = lax.broadcasted_iota(jnp.int32, (128, WINDOW), 1)
        mask_ref[row : row + 128, :] = jnp.where(rows == cols, 0.0, bias)


def rows_inside(rows, row_start, first):
    ids = row_start + lax.broadcasted_iota(jnp.int32, (rows, 1), 0)
    return (ids >= first) & (ids < first + PATCHES)


def attend_forward_kernel(blocks, begin, spots, code_ref, *refs):
    bias_out, out_ref, mask_ref = refs[-3:]
    image, start, first = image_window(begin, refs[0].shape[0])
    code = code_ref[pl.ds(start, WINDOW), :]
    bias = jnp.where(code == image, 0.0, -1e30).astype(f32).T
    bias_out[0] = bias[0:8, :]
    fill_mask(bias[0:1, :], mask_ref)
    lanes = refs[0].shape[1]

    for tile in range((len(refs) - 3 - blocks) // 3):
        q_ref, k_ref, v_ref = refs[3 * tile : 3 * tile + 3]
        cols = slice(tile * lanes, (tile + 1) * lanes)

        @pl.when(image == 0)
        def _():
            out_ref[:, cols] = v_ref[...]

        k_all = k_ref[pl.ds(start, WINDOW), :]
        v_all = v_ref[pl.ds(start, WINDOW), :]
        for row in range(0, WINDOW, QROWS):
            at = pl.ds(pl.multiple_of(start + row, 16), QROWS)
            q_part = q_ref[at, :] * jnp.asarray(HEAD_DIM ** (-0.5), bf16)
            inside = rows_inside(QROWS, row, first)
            mixed = None
            for head in range(lanes // HEAD_DIM):
                mine = head_lanes(lanes, head)
                q_head = jnp.where(mine, q_part, jnp.zeros_like(q_part))
                weights, totals = attend_scores(q_head, k_all, mask_ref[row : row + QROWS, :])
                part = dot(weights.astype(bf16), v_all, 1, 0) * (1.0 / totals)
                mixed = part if mixed is None else jnp.where(mine, part, mixed)
            out_ref[at, cols] = jnp.where(inside, mixed.astype(bf16), out_ref[at, cols])

    @pl.when(image == pl.num_programs(0) - 1)
    def _():
        for n, block in enumerate(refs[-3 - blocks : -3]):
            rows = block.shape[0]
            block[...] = out_ref[pl.ds(pl.multiple_of(spots[n], rows), rows), :]


def attend_backward_kernel(blocks, begin, spots, bias_ref, *refs):
    out_ref, p_ref, s_ref, go_ref, mask_ref = refs[-5:]
    go_blocks, refs = refs[3 : 3 + blocks], refs[:3]
    image, start, first = image_window(begin, refs[0].shape[0])
    fill_mask(bias_ref[0, 0:1, :], mask_ref)
    lanes = refs[0].shape[1]
    rows = go_blocks[0].shape[0]
    whole = pl.ds(start, WINDOW)
    inside_all = rows_inside(WINDOW, 0, first)

    @pl.when(image == 0)
    def _():
        for n, block_ref in enumerate(go_blocks):
            go_ref[pl.ds(pl.multiple_of(spots[n], rows), rows), :] = block_ref[...]

    for tile in range(len(refs) // 3):
        q_ref, k_ref, v_ref = refs[3 * tile : 3 * tile + 3]
        cols = slice(tile * lanes, (tile + 1) * lanes)
        base = 3 * tile * lanes
        q_cols, k_cols, v_cols = [
            slice(base + n * lanes, base + (n + 1) * lanes) for n in range(3)
        ]

        @pl.when(image == 0)
        def _():
            out_ref[:, base : base + 2 * lanes] = jnp.zeros((out_ref.shape[0], 2 * lanes), bf16)
            out_ref[:, v_cols] = go_ref[:, cols]

        k_all = k_ref[whole, :]
        v_all = v_ref[whole, :]
        q_all = q_ref[whole, :] * jnp.asarray(HEAD_DIM ** (-0.5), bf16)
        go_all = go_ref[whole, cols]
        key_grad = None
        value_grad = None
        for head in range(lanes // HEAD_DIM):
            mine = head_lanes(lanes, head)
            q_mine = jnp.where(mine, q_all, jnp.zeros_like(q_all))
            go_mine = jnp.where(mine, go_all, jnp.zeros_like(go_all))
            for row in range(0, WINDOW, QROWS):
                part = slice(row, row + QROWS)
                at = pl.ds(pl.multiple_of(start + row, 16), QROWS)
                inside = rows_inside(QROWS, row, first)
                weights, totals = attend_scores(q_mine[part], k_all, mask_ref[part, :])
                weights = weights * jnp.where(inside, 1.0 / totals, 0.0)
                weight_grad = dot(go_mine[part], v_all, 1, 1)
                product = weights * weight_grad
                score_grad = (
                    product - weights * jnp.sum(product, axis=-1, keepdims=True)
                ).astype(bf16)
                p_ref[part, :] = weights.astype(bf16)
                s_ref[part, :] = score_grad
                query_grad = (dot(score_grad, k_all, 1, 0) * HEAD_DIM ** (-0.5)).astype(bf16)
                out_ref[at, q_cols] = jnp.where(inside & mine, query_grad, out_ref[at, q_cols])
            key_part = dot(q_mine, s_ref[...], 0, 0)
            value_part = dot(go_mine, p_ref[...], 0, 0)
            key_grad = key_part if key_grad is None else key_grad + key_part
            value_grad = value_part if value_grad is None else value_grad + value_part
        key_rows = key_grad.T.astype(bf16)
        value_rows = value_grad.T.astype(bf16)
        out_ref[whole, k_cols] = jnp.where(inside_all, key_rows, out_ref[whole, k_cols])
        out_ref[whole, v_cols] = jnp.where(inside_all, value_rows, out_ref[whole, v_cols])


def qkv_operands(projected, tile):
    group_rows, total = projected.shape
    lanes = min(128, total // 3)
    if lanes % 128 == 0:
        specs = [
            pl.BlockSpec((group_rows, lanes), functools.partial(lambda n, i, *_: (0, n), 3 * tile + n))
            for n in range(3)
        ]
        return [projected] * 3, specs
    parts = [projected[:, n * lanes : (n + 1) * lanes] for n in range(3)]
    return parts, [fixed((group_rows, lanes))] * 3


def all_operands(projected):
    width = projected.shape[1] // 3
    operands, specs = [], []
    for tile in range(width // min(128, width)):
        more, places = qkv_operands(projected, tile)
        operands += more
        specs += places
    return operands, specs


def attend_forward(projected, geometry, spots, rows):
    begin, code = geometry
    group_rows, total = projected.shape
    width = total // 3
    blocks = group_rows // rows
    images = begin.shape[0]
    operands, specs = all_operands(projected)
    out = plain_call(
        functools.partial(attend_forward_kernel, blocks),
        (shaped((rows, width), bf16),) * blocks + (shaped((images, 8, WINDOW), f32),),
        code,
        *operands,
        grid=begin.shape,
        in_specs=[fixed(code.shape)] + specs,
        out_specs=(fixed((rows, width)),) * blocks
        + (pl.BlockSpec((1, 8, WINDOW), lambda i, *_: (i, 0, 0)),),
        scratch=[pltpu.VMEM((group_rows, width), bf16), pltpu.VMEM((WINDOW, WINDOW), f32)],
        scalars=(begin, spots),
        mebibytes=24,
        name="attention_forward",
    )
    return out[:blocks], out[blocks]


def attend_backward(projected, go_blocks, spots, begin, bias, tile, into):
    group_rows, total = projected.shape
    lanes = min(128, total // 3)
    operands, specs = qkv_operands(projected, tile)
    return plain_call(
        functools.partial(attend_backward_kernel, len(go_blocks)),
        shaped((group_rows, total), bf16),
        bias,
        *operands,
        *go_blocks,
        grid=begin.shape,
        in_specs=[pl.BlockSpec((1, 8, WINDOW), lambda i, *_: (i, 0, 0))]
        + specs
        + [fixed(block.shape) for block in go_blocks],
        out_specs=pl.BlockSpec((group_rows, 3 * lanes), lambda i, *_: (0, tile)),
        scratch=[pltpu.VMEM((WINDOW, WINDOW), bf16)] * 2
        + [pltpu.VMEM((group_rows, lanes), bf16), pltpu.VMEM((WINDOW, WINDOW), f32)],
        scalars=(begin, spots),
        into=into,
        mebibytes=56 if into else 24,
        name="attention_backward",
    )


def attend_geometry(segments, live_mask):
    group_rows = segments.shape[0]
    numbers = jnp.arange(group_rows // PATCHES, dtype=jnp.int32)
    positions = jnp.arange(group_rows, dtype=jnp.int32)
    begin = jnp.min(
        jnp.where(segments[None, :] == numbers[:, None], positions[None, :], group_rows - PATCHES),
        axis=1,
    )
    code = jnp.where(live_mask == 1, segments, -1)
    return begin, jnp.broadcast_to(code[:, None], (group_rows, 128))


def plain_call(kernel, out_shape, *operands, grid=(), in_specs=None, out_specs=None, scratch=(), scalars=(), into=(), mebibytes=16, name=None):
    params = pltpu.CompilerParams(vmem_limit_bytes=mebibytes * 1024 * 1024)
    if in_specs is None:
        in_specs = [pl.BlockSpec(a.shape, functools.partial(lambda n, *_: (0,) * n, a.ndim)) for a in operands]
    in_specs = list(in_specs) + [pl.BlockSpec(memory_space=pl.ANY)] * len(into)
    if out_specs is None:
        out_specs = jax.tree.map(
            lambda s: pl.BlockSpec(s.shape, functools.partial(lambda n, *_: (0,) * n, len(s.shape))), out_shape
        )
    return pl.pallas_call(
        kernel,
        grid_spec=pltpu.PrefetchScalarGridSpec(
            num_scalar_prefetch=len(scalars),
            grid=grid,
            in_specs=in_specs,
            out_specs=out_specs,
            scratch_shapes=list(scratch),
        ),
        out_shape=out_shape,
        input_output_aliases={len(scalars) + len(operands) + n: n for n in range(len(into))},
        compiler_params=params,
        cost_estimate=SMALL,
        name=name,
    )(*scalars, *operands, *into)


def shaped(shape, dtype):
    return jax.ShapeDtypeStruct(tuple(shape), dtype)


def row_blocks(rows, *widths):
    return [pl.BlockSpec((rows, w), lambda i, *_: (i, 0)) for w in widths]


def fixed(shape):
    return pl.BlockSpec(tuple(shape), functools.partial(lambda n, *_: (0,) * n, len(shape)))


def pack_kernel(live_ref, qkv_ref, proj_ref, up_ref, down_ref, qkv_out, up_out, down_out):
    count, slab, width = qkv_ref.shape
    lanes = min(128, width)
    for n in range(count):
        for t in range(width // lanes):
            at = (count * t + n) * lanes
            qkv_out[:, at : at + lanes] = qkv_ref[n][:, t * lanes : (t + 1) * lanes].astype(bf16)
    qkv_out[:, count * width :] = proj_ref[...].T.astype(bf16)
    up_out[:slab, :] = up_ref[...].astype(bf16)
    live = jnp.sum(jnp.sum(live_ref[...].astype(f32), axis=0, keepdims=True), axis=1, keepdims=True)
    high = jnp.floor(live * (1.0 / 256.0))
    middle = jnp.floor(live * (1.0 / 16.0)) - 16.0 * high
    low = live - 256.0 * high - 16.0 * middle
    row = lax.broadcasted_iota(jnp.int32, (DIGITS, up_out.shape[1]), 0)
    digits = jnp.where(row == 0, high, jnp.where(row == 1, middle, jnp.where(row == 2, low, 0.0)))
    up_out[slab:, :] = digits.astype(bf16)
    down_out[...] = down_ref[...].T.astype(bf16)


def first_kernel(tok_ref, par_ref, low_out):
    normed, _, _ = norm_forward(tok_ref[...], par_ref[0:1, :], par_ref[1:2, :])
    low_out[...] = normed.astype(bf16)


def place_blocks(blocks, spots):
    rows, width = blocks[0].shape

    def kernel(spot_ref, *refs):
        for n, ref in enumerate(refs[:-1]):
            refs[-1][pl.ds(pl.multiple_of(spot_ref[n], rows), rows), :] = ref[...]

    return plain_call(
        kernel,
        shaped((rows * len(blocks), width), bf16),
        *blocks,
        scalars=(spots,),
        mebibytes=20,
        name="place_blocks",
    )


def block_rows(block, slab):
    return pl.ds(pl.multiple_of(block * slab, slab), slab)


def stack_z(pieces, slab, places, count=1):
    height, width = pieces[0].shape
    extra = height - slab
    shapes = (shaped((N_Z * slab // count + extra, width), bf16),) * count

    def kernel(at_ref, *refs):
        held = refs[-1]
        for k, ref in enumerate(refs[:N_Z]):
            held[block_rows(lax.rem(at_ref[0] + N_Z - k, N_Z), slab), :] = ref[:slab, :]
        for n, out in enumerate(refs[N_Z:-1]):
            rows = N_Z * slab // count
            out[:rows, :] = held[n * rows : (n + 1) * rows, :]
            if extra:
                digits = refs[0][slab:, :].astype(f32)
                for ref in refs[1:N_Z]:
                    digits = digits + ref[slab:, :].astype(f32)
                out[rows:, :] = digits.astype(bf16)

    out = plain_call(
        kernel,
        shapes,
        *pieces,
        scalars=(places,),
        scratch=[pltpu.VMEM((N_Z * slab, width), bf16)],
        mebibytes=8,
        name="stack_z",
    )
    return out if count > 1 else out[0]


def weave(columns, cuts, slab, places):
    n_x = len(columns[0])
    width = columns[0][0][0].shape[1]
    flat = [piece for column in columns for half in column for piece in half]
    edges = [0, *cuts, width]
    sizes = [stop - start for start, stop in zip(edges[:-1], edges[1:])]

    def kernel(at_ref, *refs):
        outs = refs[len(flat) :]
        used = 0
        for y, column in enumerate(columns):
            for dx, half in enumerate(column):
                x = lax.rem(at_ref[1] + dx, n_x)
                share = N_Z // len(half)
                for z in range(N_Z):
                    piece = refs[used + z // share]
                    at = block_rows(z * n_x + x, slab)
                    row = z % share * slab
                    for out, start, size in zip(outs, edges, sizes):
                        out[at, y * size : (y + 1) * size] = piece[
                            row : row + slab, start : start + size
                        ]
                used += len(half)

    out = plain_call(
        kernel,
        tuple(shaped((N_Z * n_x * slab, size * len(columns)), bf16) for size in sizes),
        *flat,
        scalars=(places,),
        mebibytes=12,
        name="weave",
    )
    return out if cuts else out[0]


def proj_kernel(count, each, *refs):
    blocks, parts = refs[:count], refs[count : count + count // each]
    tok_ref, par_ref, res_out, low_out = refs[count + count // each :]
    total = tok_ref[...]
    for n, block in enumerate(blocks):
        size = block.shape[1]
        part = parts[n // each][:, n % each * size : (n % each + 1) * size]
        total = total + dot(block[...], part, 1, 1)
    res_out[...] = total
    normed, _, _ = norm_forward(total, par_ref[2:3, :], par_ref[3:4, :])
    low_out[...] = normed.astype(bf16)


ERF_TOP = (
    -2.72614225801306e-10,
    2.77068142495902e-08,
    -2.10102402082508e-06,
    -5.69250639462346e-05,
    -7.34990630326855e-04,
    -2.95459980854025e-03,
    -1.60960333262415e-02,
)
ERF_LOW = (
    -1.45660718464996e-05,
    -2.13374055278905e-04,
    -1.68282697438203e-03,
    -7.37332916720468e-03,
    -1.42647390514189e-02,
)


def erf(value):
    value = jnp.clip(value, -4.0, 4.0)
    square = value * value
    top = jnp.full_like(square, ERF_TOP[0])
    for number in ERF_TOP[1:]:
        top = top * square + number
    low = jnp.full_like(square, ERF_LOW[0])
    for number in ERF_LOW[1:]:
        low = low * square + number
    inverse = pl.reciprocal(low, approx=True)
    inverse = inverse * (2.0 - low * inverse)
    return value * top * inverse


def up_kernel(count, low_ref, *refs):
    outs = refs[-2 * count :]
    for n, part in enumerate(refs[:count]):
        hidden = dot(low_ref[...], part[...], 1, 0)
        share = 0.5 * (1.0 + erf(hidden * 0.7071067811865476))
        outs[2 * n][...] = (hidden * share).astype(bf16)
        slope = share + hidden * jnp.exp(-0.5 * hidden * hidden) * 0.3989422804014327
        outs[2 * n + 1][...] = slope.astype(bf16)


def up_call(low, parts, rows_all, spot, into):
    rows, model = low.shape
    width = parts[0].shape[1]
    cols = pl.BlockSpec((rows, TILE), lambda i, *_: (spot, i))
    return plain_call(
        functools.partial(up_kernel, len(parts)),
        (shaped((rows_all, width), bf16),) * (2 * len(parts)),
        low,
        *parts,
        grid=(width // TILE,),
        in_specs=[fixed(low.shape)] + [pl.BlockSpec((model, TILE), lambda i, *_: (0, i))] * len(parts),
        out_specs=(cols,) * (2 * len(parts)),
        into=into,
        mebibytes=14,
        name="up",
    )


def hidden_kernel(count, low_ref, *refs):
    outs = refs[-count:]
    for n in range(count):
        slope, part = refs[n], refs[count + n]
        outs[n][...] = (dot(low_ref[...], part[...], 1, 0) * slope[...].astype(f32)).astype(bf16)


def hidden_call(low, slopes, parts, spot, into):
    rows, model = low.shape
    width = parts[0].shape[1]
    cols = pl.BlockSpec((rows, TILE), lambda i, *_: (spot, i))
    return plain_call(
        functools.partial(hidden_kernel, len(parts)),
        tuple(shaped(slope.shape, bf16) for slope in slopes),
        low,
        *slopes,
        *parts,
        grid=(width // TILE,),
        in_specs=[fixed(low.shape)]
        + [cols] * len(parts)
        + [pl.BlockSpec((model, TILE), lambda i, *_: (0, i))] * len(parts),
        out_specs=(cols,) * len(parts),
        into=into,
        mebibytes=14,
        name="hidden",
    )


def wide_kernel(count, *refs):
    total = dot(refs[0][...], refs[count][...], 1, 1)
    for n in range(1, count):
        total = total + dot(refs[n][...], refs[count + n][...], 1, 1)
    refs[-1][...] = total.astype(refs[-1].dtype)


def wide_call(values, parts, rows, spot, kind):
    model, width = parts[0].shape
    return plain_call(
        functools.partial(wide_kernel, len(values)),
        shaped((rows, model), kind),
        *values,
        *parts,
        grid=(model // TILE,),
        in_specs=[pl.BlockSpec((rows, width), lambda i, *_: (spot, 0))] * len(values)
        + [pl.BlockSpec((TILE, width), lambda i, *_: (i, 0))] * len(parts),
        out_specs=pl.BlockSpec((rows, TILE), lambda i, *_: (0, i)),
        mebibytes=14,
        name="wide",
    )


def loss_kernel(chunks, each, *refs):
    res_ref, tea_ref, own_ref = refs[:3]
    received = refs[3 : 3 + chunks * each]
    live_ref, count_ref, grad_out, low_out, loss_out, far_ref = refs[3 + chunks * each :]
    add_received(received, each, far_ref)
    error = res_ref[...] - tea_ref[...] + own_ref[...] + far_ref[...]
    weighted = live_ref[...] * error
    grad = 2.0 * weighted / count_ref[...]
    grad_out[...] = grad
    low_out[...] = grad.astype(bf16)
    sums = jnp.sum(weighted * error, axis=0, keepdims=True)
    sums = jnp.concatenate([sums, jnp.zeros((7, sums.shape[1]), f32)], axis=0)
    loss_out[...] = jnp.where(pl.program_id(0) == 0, sums, loss_out[...] + sums)


def add_received(received, each, far_ref):
    for n in range(len(received) // each):

        @pl.when(pl.program_id(0) == n)
        def _():
            total = received[n * each][...].astype(f32)
            for ref in received[n * each + 1 : (n + 1) * each]:
                total = total + ref[...].astype(f32)
            far_ref[...] = total


def beside_call(parts):
    rows, width = parts[0].shape

    def kernel(*refs):
        for n, ref in enumerate(refs[:-1]):
            refs[-1][:, n * width : (n + 1) * width] = ref[...]

    return plain_call(
        kernel, shaped((rows, width * len(parts)), bf16), *parts, mebibytes=8, name="beside"
    )


def spread_kernel(each, tiles, low_ref, *refs):
    count = len(refs) // (1 + each * tiles)
    outs = refs[count:]
    for n in range(count * each):
        size = refs[0].shape[1] // each
        part = refs[n // each][:, n % each * size : (n % each + 1) * size]
        piece = dot(low_ref[...], part, 1, 0).astype(bf16)
        lanes = size // tiles
        for tile in range(tiles):
            outs[tile * count * each + n][...] = piece[:, tile * lanes : (tile + 1) * lanes]


def spread_call(low, parts, each):
    width = parts[0].shape[1] // each
    lanes = min(128, width)
    count = len(parts) * each
    out = plain_call(
        functools.partial(spread_kernel, each, width // lanes),
        tuple(shaped((low.shape[0], lanes), bf16) for _ in range(count * (width // lanes))),
        low,
        *parts,
        mebibytes=12,
        name="spread",
    )
    return [out[n : n + count] for n in range(0, len(out), count)]


def unproject_kernel(half, spots, grad_ref, part_ref, far_out, near_out):
    piece = dot(grad_ref[...], part_ref[...], 1, 1)

    @pl.when(pl.program_id(0) < half)
    def _():
        far_out[...] = piece.astype(bf16)

    @pl.when(pl.program_id(0) >= half)
    def _():
        near_out[...] = piece.astype(bf16)


def unproject_call(grads, part, blocks, rows):
    half = len(blocks) // 2
    model, width = part.shape
    return plain_call(
        functools.partial(unproject_kernel, half),
        (shaped((half * rows, model), bf16),) * 2,
        grads,
        part,
        grid=(len(blocks),),
        in_specs=[
            pl.BlockSpec((rows, width), lambda i, spots: (spots[i], 0)),
            fixed(part.shape),
        ],
        out_specs=(
            pl.BlockSpec((rows, model), lambda i, spots: (jnp.minimum(i, half - 1), 0)),
            pl.BlockSpec((rows, model), lambda i, spots: (jnp.maximum(i - half, 0), 0)),
        ),
        scalars=(jnp.stack(blocks).astype(jnp.int32),),
        mebibytes=48,
        name="unproject",
    )


def outer_proj_kernel(half, low_ref, *refs):
    blocks, (far_out, *near) = refs[: 2 * half], refs[2 * half :]
    turned = low_ref[...].astype(f32).T.astype(bf16)
    width = blocks[0].shape[1]
    for n in range(half):
        far_out[:, n * width : (n + 1) * width] = dot(turned, blocks[half + n][...], 1, 0).astype(bf16)
        near[n][...] = dot(turned, blocks[n][...], 1, 0).astype(bf16)


def outer_proj_call(low, blocks):
    model = low.shape[1]
    width = blocks[0].shape[1]
    half = len(blocks) // 2
    out = plain_call(
        functools.partial(outer_proj_kernel, half),
        (shaped((model, half * width), bf16),) + (shaped((model, width), bf16),) * half,
        low,
        *blocks,
        mebibytes=14,
        name="outer_proj",
    )
    return out[0], out[1:]


def add_lanes(own, received):
    width = own[0].shape[1]

    def kernel(*refs):
        got = refs[len(own)]
        for n, ref in enumerate(refs[: len(own)]):
            other = got[:, n * width : (n + 1) * width].astype(f32)
            refs[len(own) + 1 + n][...] = (ref[...].astype(f32) + other).astype(bf16)

    return plain_call(
        kernel,
        tuple(shaped(part.shape, bf16) for part in own),
        *own,
        received,
        mebibytes=8,
        name="add_lanes",
    )


def norm_sums(grad, scaled, out_ref, first):
    sums = jnp.concatenate(
        [
            jnp.sum(grad * scaled, axis=0, keepdims=True),
            jnp.sum(grad, axis=0, keepdims=True),
            jnp.zeros((6, grad.shape[1]), f32),
        ],
        axis=0,
    )
    out_ref[...] = jnp.where(first, sums, out_ref[...] + sums)


def middle_kernel(chunks, each, *refs):
    grad_ref, received = refs[0], refs[1 : 1 + chunks * each]
    res_ref, gout_ref, par_ref, full_out, low_out, sum_out, far_ref = refs[1 + chunks * each :]
    add_received(received, each, far_ref)
    _, scaled, inverse = norm_forward(res_ref[...], par_ref[2:3, :], par_ref[3:4, :])
    grad = grad_ref[...] + far_ref[...]
    full = gout_ref[...] + norm_backward(grad, scaled, inverse, par_ref[2:3, :])
    full_out[...] = full
    low_out[...] = full.astype(bf16)
    norm_sums(grad, scaled, sum_out, pl.program_id(0) == 0)


def leave_kernel(count, *refs):
    own_ref, received = refs[0], refs[1 : 1 + count]
    tok_ref, res_ref, par_ref, two_ref, loss_ref, out_ref, sum_out, sum_ref = refs[1 + count :]
    _, scaled, inverse = norm_forward(tok_ref[...], par_ref[0:1, :], par_ref[1:2, :])
    grad = own_ref[...]
    for ref in received:
        grad = grad + ref[...].astype(f32)
    out_ref[...] = res_ref[...] + norm_backward(grad, scaled, inverse, par_ref[0:1, :])
    norm_sums(grad, scaled, sum_ref, pl.program_id(0) == 0)
    sum_out[...] = jnp.concatenate(
        [sum_ref[0:2, :], two_ref[0:2, :], loss_ref[0:1, :], jnp.zeros((3, grad.shape[1]), f32)],
        axis=0,
    )


def split_x(parts, n_x, places):
    model = parts[0][0].shape[0]
    slab = model // (N_Z * n_x)
    total = sum(part[0].shape[1] for part in parts)
    flat = [piece for part in parts for piece in part]

    def kernel(at_ref, *refs):
        outs = refs[len(flat) :]
        for dx in range(n_x):
            x = lax.rem(at_ref[1] + dx, n_x)
            for z in range(N_Z):
                at = block_rows(z * n_x + x, slab)
                lane = 0
                used = 0
                for part in parts:
                    value = refs[used][at, :]
                    size = value.shape[1]
                    if len(part) > 1:
                        value = value.astype(f32)
                        for ref in refs[used + 1 : used + len(part)]:
                            value = value + ref[at, :].astype(f32)
                        value = value.astype(bf16)
                    outs[dx][z * slab : (z + 1) * slab, lane : lane + size] = value
                    lane += size
                    used += len(part)

    return plain_call(
        kernel,
        tuple(shaped((model // n_x, total), bf16) for _ in range(n_x)),
        *flat,
        scalars=(places,),
        mebibytes=12,
        name="split_x",
    )


def split_z(parts, places):
    rows, width = parts[0].shape
    slab = rows // N_Z

    def kernel(at_ref, *refs):
        for k, out in enumerate(refs[len(parts) :]):
            at = block_rows(lax.rem(at_ref[0] + k, N_Z), slab)
            total = refs[0][at, :].astype(f32)
            for ref in refs[1 : len(parts)]:
                total = total + ref[at, :].astype(f32)
            out[...] = total.astype(out.dtype)

    shapes = (shaped((slab, width), f32),) + (shaped((slab, width), bf16),) * (N_Z - 1)
    return plain_call(kernel, shapes, *parts, scalars=(places,), mebibytes=8, name="split_z")


def adam_kernel(layout, counts, *refs):
    grads = []
    for count in counts:
        grad = refs[0][...].astype(f32)
        for ref in refs[1:count]:
            grad = grad + ref[...].astype(f32)
        grads.append(grad)
        refs = refs[count:]
    count = len(layout)
    states, outs = refs[: 3 * count], refs[3 * count :]
    for n, (source, start, size, turned) in enumerate(layout):
        weight, first, second = states[3 * n : 3 * n + 3]
        if len(weight.shape) == 3:
            matrices = weight.shape[0]
            lanes = size // matrices
            for k in range(matrices):
                own = [
                    grads[at][:, lane + k * lanes : lane + (k + 1) * lanes] for at, lane in start
                ]
                own = own[0] if len(own) == 1 else jnp.concatenate(own, axis=1)
                new = adam_step(weight[k], own, first[k], second[k], weight_decay, learn_rate)
                for out, value in zip(outs[3 * n : 3 * n + 3], new):
                    out[k] = value
        else:
            part = grads[source][:, start : start + size]
            if turned:
                part = part.T
            new = adam_step(weight[...], part, first[...], second[...], weight_decay, learn_rate)
            for out, value in zip(outs[3 * n : 3 * n + 3], new):
                out[...] = value


def adam_call(groups, layout, *states):
    shapes = tuple(shaped(s.shape, f32) for s in states)
    out = plain_call(
        functools.partial(adam_kernel, layout, [len(group) for group in groups]),
        shapes,
        *[piece for group in groups for piece in group],
        *states,
        mebibytes=16,
        name="adam",
    )
    return [out[3 * n : 3 * n + 3] for n in range(len(layout))]


def tie(*values):
    return lax.optimization_barrier(values)


def local(
    n_x,
    n_y,
    tokens,
    teacher,
    segments,
    live_mask,
    weight_qkv,
    weight_proj,
    weight_up,
    weight_down,
    norm_params,
    first_qkv,
    first_proj,
    first_up,
    first_down,
    first_norms,
    second_qkv,
    second_proj,
    second_up,
    second_down,
    second_norms,
):
    z_at, x_at = lax.axis_index("z"), lax.axis_index("x")
    y_at, core_at = lax.axis_index("y"), lax.axis_index("core")
    rows, model = tokens.shape
    group_rows = segments.shape[0]
    slab = weight_qkv.shape[1]
    width = weight_qkv.shape[2]
    unit = weight_up.shape[1]
    part_rows = min(128, rows)
    wide_rows = min(256, rows)
    depth = N_Z * slab
    sizes = {"z": N_Z, "x": n_x, "y": n_y, "core": N_CORE}
    places = jnp.stack([z_at, x_at]).astype(jnp.int32)
    offsets = [(dc, dy) for dc in range(N_CORE) for dy in range(n_y)]
    other = N_CORE - 1

    def send(value, axis, step):
        size = sizes[axis]
        return lax.ppermute(value, axis, [(i, (i + step) % size) for i in range(size)])

    def send_col(value, dy, dc):
        perm = [
            (y * N_CORE + c, (y + dy) % n_y * N_CORE + (c + dc) % N_CORE)
            for y in range(n_y)
            for c in range(N_CORE)
        ]
        return lax.ppermute(value, ("y", "core"), perm)

    def fetch(value, axis):
        return [value] + [send(value, axis, -k) for k in range(1, sizes[axis])]

    def fetch_z(value):
        return [value] + [send(value, "z", k) for k in range(1, N_Z)]

    def place(dy, dc):
        return ((y_at + dy) % n_y * N_CORE + (core_at + dc) % N_CORE) * rows

    shard_qkv, shard_up, shard_down = plain_call(
        pack_kernel,
        (
            shaped((slab, 4 * width), bf16),
            shaped((slab + DIGITS, unit), bf16),
            shaped((slab, unit), bf16),
        ),
        live_mask.reshape(-1, 128),
        weight_qkv,
        weight_proj,
        weight_up,
        weight_down,
        mebibytes=56,
        name="pack",
    )
    near_qkv = fetch_z(shard_qkv)
    block_qkv = stack_z(near_qkv, slab, places)
    geometry = attend_geometry(segments, live_mask)
    own_live = lax.dynamic_slice_in_dim(
        live_mask, (y_at * N_CORE + core_at) * rows, rows, 0
    ).astype(f32)[:, None]
    spots_here = jnp.stack([place(dy, dc) for dc, dy in offsets]).astype(jnp.int32)
    spots = jnp.stack([place(-dy, -dc) for dc, dy in offsets]).astype(jnp.int32)
    block_qkv, shard_down, shard_up, tokens, geometry, own_live, spots_here, spots = tie(
        block_qkv, shard_down, shard_up, tokens, geometry, own_live, spots_here, spots
    )

    beside_qkv = fetch(block_qkv, "x")
    near_up = fetch_z(shard_up)
    low_one = plain_call(
        first_kernel,
        shaped(tokens.shape, bf16),
        tokens,
        norm_params,
        grid=(rows // part_rows,),
        in_specs=row_blocks(part_rows, model) + [fixed(norm_params.shape)],
        out_specs=row_blocks(part_rows, model)[0],
        mebibytes=8,
        name="first",
    )
    blocks_one = fetch(low_one, "y")
    beside_qkv, near_up, blocks_one, shard_down = tie(beside_qkv, near_up, blocks_one, shard_down)

    block_up = stack_z(near_up, slab, places)
    full_qkv, part_proj = weave([[[part] for part in beside_qkv]], [3 * width], slab, places)
    block_up, part_proj, blocks_one = tie(block_up, part_proj, blocks_one)
    blocks_one = blocks_one + [send(block, "core", -1) for block in blocks_one]
    group_one = place_blocks(blocks_one, spots_here)
    beside_up = fetch(block_up, "x")
    near_down = fetch_z(shard_down)
    full_proj = fetch(part_proj, "y")
    projected = dot(group_one, full_qkv, 1, 0).astype(bf16)
    mixed, bias = attend_forward(projected, geometry, spots, rows)
    mixed, beside_up, near_down, full_proj = tie(mixed, beside_up, near_down, full_proj)

    blocks_mixed = [
        piece if key == (0, 0) else send_col(piece, -key[1], -key[0])
        for key, piece in zip(offsets, mixed)
    ]
    full_proj = [beside_call(full_proj)]
    full_proj.append(send(full_proj[0], "core", -1))
    blocks_down = stack_z(near_down, slab, places, 2)
    beside_down = [fetch(blocks_down[0], "x")]
    full_up = [weave([[[part] for part in beside_up]], [], slab, places)]
    live_count = sum(
        256.0 * part[depth, 0].astype(f32) + 16.0 * part[depth + 1, 0].astype(f32)
        + part[depth + 2, 0].astype(f32)
        for part in beside_up
    ).reshape(1, 1)
    blocks_mixed, full_proj, full_up, live_count, beside_down, blocks_down = tie(
        blocks_mixed, full_proj, full_up, live_count, beside_down, blocks_down
    )
    beside_down.append(fetch(blocks_down[1], "x"))
    full_up.append(send(full_up[0], "core", -1))
    count = len(offsets)
    residual, low_two = plain_call(
        functools.partial(proj_kernel, count, n_y),
        (shaped(tokens.shape, f32), shaped(tokens.shape, bf16)),
        *blocks_mixed,
        *full_proj,
        tokens,
        norm_params,
        grid=(rows // wide_rows,),
        in_specs=row_blocks(wide_rows, *([width] * count))
        + [fixed(part.shape) for part in full_proj]
        + row_blocks(wide_rows, model)
        + [fixed(norm_params.shape)],
        out_specs=tuple(row_blocks(wide_rows, model, model)),
        mebibytes=18,
        name="proj",
    )
    low_two, full_up = tie(low_two, full_up)

    chunk = min(256, rows)
    chunks = range(rows // chunk)
    neighbours = range(1, n_y)
    rows_all = n_y * rows

    def cross(value, n):
        piece = value[n * chunk : (n + 1) * chunk]
        return {dy: send(piece, "y", -dy) for dy in neighbours}

    def spot_of(dy, n):
        return (dy * rows) // chunk + n

    low_far = {0: cross(low_two, 0)}
    hidden = up_call(low_two, full_up, rows_all, 0, ())
    low_far[0], hidden, low_two, beside_down = tie(low_far[0], hidden, low_two, beside_down)
    full_down = [weave([list(zip(*beside_down))], [], slab, places)]
    full_down.append(send(full_down[0], "core", -1))
    far_out = {}
    for n in chunks:
        if n + 1 in chunks:
            low_far[n + 1] = cross(low_two, n + 1)
        for dy in neighbours:
            hidden = up_call(low_far[n][dy], full_up, rows_all, spot_of(dy, n), hidden)
        outs = {
            dy: wide_call(hidden[::2], full_down, chunk, spot_of(dy, n), bf16) for dy in neighbours
        }
        if n + 1 in chunks:
            outs, hidden, low_far[n + 1] = tie(outs, hidden, low_far[n + 1])
        else:
            outs, hidden = tie(outs, hidden)
        if n:
            far_out[n - 1] = tie(far_out[n - 1], outs)[0]
        far_out[n] = {dy: send(outs[dy], "y", dy) for dy in neighbours}
    own_out = wide_call(hidden[::2], full_down, rows, 0, f32)
    own_out, far_out = tie(own_out, far_out)
    far_out = [far_out[n][dy] for n in chunks for dy in neighbours]
    each = len(neighbours)
    grad_output, grad_branch, loss_rows = plain_call(
        functools.partial(loss_kernel, len(chunks), each),
        (shaped(tokens.shape, f32), shaped(tokens.shape, bf16), shaped((8, model), f32)),
        residual,
        teacher,
        own_out,
        *far_out,
        own_live,
        live_count,
        grid=(len(chunks),),
        in_specs=row_blocks(chunk, model, model, model)
        + [fixed((chunk, model))] * len(far_out)
        + row_blocks(chunk, 1)
        + [fixed((1, 1))],
        out_specs=tuple(row_blocks(chunk, model, model) + [fixed((8, model))]),
        scratch=[pltpu.VMEM((chunk, model), f32)],
        mebibytes=20,
        name="loss",
    )
    active, slope = hidden[::2], hidden[1::2]

    grad_far = {0: cross(grad_branch, 0)}
    grad_hidden = hidden_call(grad_branch, slope, full_down, 0, ())
    own_two = wide_call(grad_hidden, full_up, rows, 0, f32)
    grad_far[0], grad_hidden, own_two, grad_branch = tie(
        grad_far[0], grad_hidden, own_two, grad_branch
    )
    def gather_rows(own, far):
        return jnp.concatenate([own] + [far[n][dy] for dy in neighbours for n in chunks], axis=0)

    far_two = {}
    for n in chunks:
        if n + 1 in chunks:
            grad_far[n + 1] = cross(grad_branch, n + 1)
        for dy in neighbours:
            grad_hidden = hidden_call(
                grad_far[n][dy], slope, full_down, spot_of(dy, n), grad_hidden
            )
        outs = {
            dy: wide_call(grad_hidden, full_up, chunk, spot_of(dy, n), bf16) for dy in neighbours
        }
        if n + 1 in chunks:
            outs, grad_hidden, grad_far[n + 1] = tie(outs, grad_hidden, grad_far[n + 1])
        else:
            grad_all = gather_rows(grad_branch, grad_far)
            far_down = dot(grad_all, active[other], 0, 0).astype(bf16)
            outs, grad_hidden, grad_all, far_down, far_two = tie(
                outs, grad_hidden, grad_all, far_down, far_two
            )
        far_two[n] = {dy: send(outs[dy], "y", dy) for dy in neighbours}

    low_all = gather_rows(low_two, low_far)
    far_up = dot(low_all, grad_hidden[other], 0, 0).astype(bf16)
    sent_down, sent_up = send(far_down, "core", 1), send(far_up, "core", 1)
    hold_down = (dot(grad_all, active[0], 0, 0) + sent_down.astype(f32)).astype(bf16)
    halves_down = split_x([[hold_down]], n_x, places)
    hold_up = (dot(low_all, grad_hidden[0], 0, 0) + sent_up.astype(f32)).astype(bf16)
    halves_up = split_x([[hold_up]], n_x, places)
    far_two, halves_down, halves_up = tie(far_two, halves_down, halves_up)
    far_two = [far_two[n][dy] for n in chunks for dy in neighbours]
    grad_residual, grad_low, sums_two = plain_call(
        functools.partial(middle_kernel, len(chunks), each),
        (shaped(tokens.shape, f32), shaped(tokens.shape, bf16), shaped((8, model), f32)),
        own_two,
        *far_two,
        residual,
        grad_output,
        norm_params,
        grid=(len(chunks),),
        in_specs=row_blocks(chunk, model)
        + [fixed((chunk, model))] * len(far_two)
        + row_blocks(chunk, model, model)
        + [fixed(norm_params.shape)],
        out_specs=tuple(row_blocks(chunk, model, model) + [fixed((8, model))]),
        scratch=[pltpu.VMEM((chunk, model), f32)],
        mebibytes=20,
        name="middle",
    )
    pieces_attn = spread_call(grad_low, full_proj, n_y)
    pieces_attn, halves_down, halves_up, grad_low = tie(
        pieces_attn, halves_down, halves_up, grad_low
    )

    def send_back(pieces):
        return [
            piece if key == (0, 0) else send_col(piece, key[1], key[0])
            for key, piece in zip(offsets, pieces)
        ]

    def hop_x(halves):
        return [halves[0]] + [send(halves[dx], "x", dx) for dx in range(1, n_x)]

    def spread_z(pieces):
        return [pieces[0]] + [send(pieces[k], "z", k) for k in range(1, N_Z)]

    lanes = 3 * min(128, width)
    tiles = 3 * width // lanes
    sent_attn = send_back(pieces_attn[0])
    parts_down = hop_x(halves_down)
    far_proj, grad_proj = outer_proj_call(grad_low, blocks_mixed)
    sent_attn, far_proj, grad_proj = tie(sent_attn, far_proj, grad_proj)

    sent_later = [send_back(pieces) for pieces in pieces_attn[1:]]
    sent_proj = send(far_proj, "core", 1)
    grad_projected = attend_backward(projected, sent_attn, spots, geometry[0], bias, 0, ())
    grad_projected, sent_later, sent_proj, parts_down, halves_up = tie(
        grad_projected, sent_later, sent_proj, parts_down, halves_up
    )

    hold_proj = add_lanes(grad_proj, sent_proj)
    pieces_down = split_z(parts_down, places)
    grad_projected, pieces_down, hold_proj, halves_up = tie(
        grad_projected, pieces_down, hold_proj, halves_up
    )
    parts_up = hop_x(halves_up)
    last_down = spread_z(pieces_down)
    part_proj = [hold_proj[0]] + [send(hold_proj[k], "y", k) for k in range(1, n_y)]
    for tile in range(1, tiles):
        grad_projected = attend_backward(
            projected, sent_later[tile - 1], spots, geometry[0], bias, tile, (grad_projected,)
        )
    grad_projected, parts_up, last_down, part_proj = tie(
        grad_projected, parts_up, last_down, part_proj
    )

    far_one, near_one = unproject_call(
        grad_projected,
        full_qkv,
        [place(dy, dc) // rows for dc in reversed(range(N_CORE)) for dy in range(n_y)],
        rows,
    )
    far_one, grad_projected = tie(far_one, grad_projected)
    sent_one = send(far_one, "core", 1)
    grad_qkv = dot(group_one, grad_projected, 0, 0).astype(bf16)
    halves_qkv = split_x([[grad_qkv], part_proj], n_x, places)
    pieces_up = split_z(parts_up, places)
    halves_qkv, sent_one, near_one, pieces_up = tie(halves_qkv, sent_one, near_one, pieces_up)

    parts = [
        near_one[dy * rows : (dy + 1) * rows].astype(f32)
        + sent_one[dy * rows : (dy + 1) * rows].astype(f32)
        for dy in range(n_y)
    ]
    sent_parts = [parts[k].astype(bf16) for k in range(1, n_y)]
    halves_qkv, sent_parts, pieces_up = tie(halves_qkv, sent_parts, pieces_up)
    received = [send(part, "y", k) for k, part in enumerate(sent_parts, 1)]
    parts_qkv = hop_x(halves_qkv)
    last_up = spread_z(pieces_up)
    (new_down,) = adam_call(
        [last_down], [(0, 0, unit, True)], weight_down, first_down, second_down
    )
    parts_qkv, received, last_up, new_down = tie(parts_qkv, received, last_up, new_down)

    pieces_qkv = split_z(parts_qkv, places)
    token_grad, sums = plain_call(
        functools.partial(leave_kernel, len(received)),
        (shaped(tokens.shape, f32), shaped((8, model), f32)),
        parts[0],
        *received,
        tokens,
        grad_residual,
        norm_params,
        sums_two,
        loss_rows,
        grid=(rows // part_rows,),
        in_specs=row_blocks(part_rows, *([model] * (3 + len(received))))
        + [fixed(norm_params.shape), fixed((8, model)), fixed((8, model))],
        out_specs=tuple(row_blocks(part_rows, model) + [fixed((8, model))]),
        scratch=[pltpu.VMEM((8, model), f32)],
        mebibytes=14,
        name="leave",
    )
    sums, token_grad, pieces_qkv = tie(sums, token_grad, pieces_qkv)
    last_qkv = spread_z(pieces_qkv)
    for axis in ("core", "y", "x", "z"):
        step = 1
        while step < sizes[axis]:
            pairs = [(i, i ^ step) for i in range(sizes[axis])]
            sums = sums + lax.ppermute(sums, axis, pairs)
            step *= 2
    (new_up,) = adam_call([last_up], [(0, 0, unit, False)], weight_up, first_up, second_up)
    sums, last_qkv, new_up = tie(sums, last_qkv, new_up)
    loss_sum = jnp.sum(sums[4])
    live_count = live_count[0, 0]

    new_qkv, new_proj = adam_call(
        [last_qkv],
        [(0, [(0, n * lanes) for n in range(tiles)], lanes, False), (0, 3 * width, width, True)],
        weight_qkv,
        first_qkv,
        second_qkv,
        weight_proj,
        first_proj,
        second_proj,
    )
    new_norms = adam_step(norm_params, sums[:4], first_norms, second_norms, 0.0, norm_rate)
    return (
        loss_sum / live_count,
        token_grad,
        new_qkv[0],
        new_proj[0],
        new_up[0],
        new_down[0],
        new_norms[0],
        new_qkv[1],
        new_proj[1],
        new_up[1],
        new_down[1],
        new_norms[1],
        new_qkv[2],
        new_proj[2],
        new_up[2],
        new_down[2],
        new_norms[2],
    )


def solution(mesh):
    n_x = mesh.shape["row"] // N_Z
    n_y = mesh.shape["col"] // N_CORE
    mesh = jax.sharding.Mesh(
        mesh.devices.reshape(N_Z, n_x, n_y, N_CORE), ("z", "x", "y", "core")
    )
    row, col = ("z", "x"), ("y", "core")
    matrices = (P(None, row, col), P(col, row), P(row, col), P(col, row), P())
    tokens = P(row + col, None)
    return jax.shard_map(
        functools.partial(local, n_x, n_y),
        mesh=mesh,
        in_specs=(tokens, tokens, P(row), P(row)) + matrices * 3,
        out_specs=(P(), tokens) + matrices * 3,
        check_vma=False,
    )
```

```python
import functools

import jax
import jax.numpy as jnp
from jax import lax
from jax.experimental import pallas as pl
from jax.experimental.pallas import tpu as pltpu
from jax.sharding import PartitionSpec as P

HEAD_DIM = 64
PATCHES = 577
STEP = 10
WINDOW = 640
QROWS = 640
TILE = 256
DIGITS = 16
SMALL = pl.CostEstimate(flops=1024, bytes_accessed=1024, transcendentals=0)
N_Z = 4
N_CORE = 2

layer_eps = 1e-06
adam_eps = 1e-08
learn_rate = 0.03
norm_rate = 0.25
moment_decay = 0.5
weight_decay = 0.05

bf16 = jnp.bfloat16
f32 = jnp.float32


def norm_forward(values, gain_row, bias_row):
    average = jnp.mean(values, axis=-1, keepdims=True)
    centred = values - average
    variance = jnp.mean(centred * centred, axis=-1, keepdims=True)
    inverse = lax.rsqrt(variance + layer_eps)
    scaled = centred * inverse
    return (scaled * gain_row + bias_row, scaled, inverse)


def norm_backward(upstream, scaled, inverse, gain_row):
    weighted = upstream * gain_row
    return inverse * (
        weighted
        - jnp.mean(weighted, axis=-1, keepdims=True)
        - scaled * jnp.mean(weighted * scaled, axis=-1, keepdims=True)
    )


def gelu_slope(hidden):
    return (
        0.5 * (1.0 + lax.erf(hidden * 0.7071067811865476))
        + hidden * jnp.exp(-0.5 * hidden * hidden) * 0.3989422804014327
    )


def adam_step(weight, gradient, momentum, variance, decay_rate, rate):
    momentum = moment_decay * momentum + (1.0 - moment_decay) * gradient
    variance = moment_decay * variance + (1.0 - moment_decay) * gradient * gradient
    correction = 1.0 - moment_decay**STEP
    direction = momentum / correction / (jnp.sqrt(variance / correction) + adam_eps)
    return (weight - rate * (direction + decay_rate * weight), momentum, variance)


def dot(left, right, left_dim, right_dim):
    return lax.dot_general(
        left, right, (((left_dim,), (right_dim,)), ((), ())), preferred_element_type=f32
    )


def head_lanes(width, head):
    lanes = lax.broadcasted_iota(jnp.int32, (1, width), 1)
    return (lanes >= head * HEAD_DIM) & (lanes < (head + 1) * HEAD_DIM)


def attend_scores(q_part, k_all, mask):
    scores = dot(q_part, k_all, 1, 1) + mask
    weights = jnp.exp(scores - jnp.max(scores, axis=-1, keepdims=True))
    return weights, jnp.sum(weights, axis=-1, keepdims=True)


def image_window(begin, group_rows):
    image = pl.program_id(0)
    start = jnp.minimum(begin[image] // 16 * 16, group_rows - WINDOW)
    first = begin[image] - start
    return image, pl.multiple_of(start, 16), first


def fill_mask(bias, mask_ref):
    for row in range(0, WINDOW, 128):
        rows = row + lax.broadcasted_iota(jnp.int32, (128, WINDOW), 0)
        cols = lax.broadcasted_iota(jnp.int32, (128, WINDOW), 1)
        mask_ref[row : row + 128, :] = jnp.where(rows == cols, 0.0, bias)


def rows_inside(rows, row_start, first):
    ids = row_start + lax.broadcasted_iota(jnp.int32, (rows, 1), 0)
    return (ids >= first) & (ids < first + PATCHES)


def attend_forward_kernel(blocks, begin, spots, code_ref, *refs):
    bias_out, out_ref, mask_ref = refs[-3:]
    image, start, first = image_window(begin, refs[0].shape[0])
    code = code_ref[pl.ds(start, WINDOW), :]
    bias = jnp.where(code == image, 0.0, -1e30).astype(f32).T
    bias_out[0] = bias[0:8, :]
    fill_mask(bias[0:1, :], mask_ref)
    lanes = refs[0].shape[1]

    for tile in range((len(refs) - 3 - blocks) // 3):
        q_ref, k_ref, v_ref = refs[3 * tile : 3 * tile + 3]
        cols = slice(tile * lanes, (tile + 1) * lanes)

        @pl.when(image == 0)
        def _():
            out_ref[:, cols] = v_ref[...]

        k_all = k_ref[pl.ds(start, WINDOW), :]
        v_all = v_ref[pl.ds(start, WINDOW), :]
        for row in range(0, WINDOW, QROWS):
            at = pl.ds(pl.multiple_of(start + row, 16), QROWS)
            q_part = q_ref[at, :] * jnp.asarray(HEAD_DIM ** (-0.5), bf16)
            inside = rows_inside(QROWS, row, first)
            mixed = None
            for head in range(lanes // HEAD_DIM):
                mine = head_lanes(lanes, head)
                q_head = jnp.where(mine, q_part, jnp.zeros_like(q_part))
                weights, totals = attend_scores(q_head, k_all, mask_ref[row : row + QROWS, :])
                part = dot(weights.astype(bf16), v_all, 1, 0) * (1.0 / totals)
                mixed = part if mixed is None else jnp.where(mine, part, mixed)
            out_ref[at, cols] = jnp.where(inside, mixed.astype(bf16), out_ref[at, cols])

    @pl.when(image == pl.num_programs(0) - 1)
    def _():
        for n, block in enumerate(refs[-3 - blocks : -3]):
            rows = block.shape[0]
            block[...] = out_ref[pl.ds(pl.multiple_of(spots[n], rows), rows), :]


def attend_backward_kernel(blocks, begin, spots, bias_ref, *refs):
    out_ref, p_ref, s_ref, go_ref, mask_ref = refs[-5:]
    go_blocks, refs = refs[3 : 3 + blocks], refs[:3]
    image, start, first = image_window(begin, refs[0].shape[0])
    fill_mask(bias_ref[0, 0:1, :], mask_ref)
    lanes = refs[0].shape[1]
    rows = go_blocks[0].shape[0]
    whole = pl.ds(start, WINDOW)
    inside_all = rows_inside(WINDOW, 0, first)

    @pl.when(image == 0)
    def _():
        for n, block_ref in enumerate(go_blocks):
            go_ref[pl.ds(pl.multiple_of(spots[n], rows), rows), :] = block_ref[...]

    for tile in range(len(refs) // 3):
        q_ref, k_ref, v_ref = refs[3 * tile : 3 * tile + 3]
        cols = slice(tile * lanes, (tile + 1) * lanes)
        base = 3 * tile * lanes
        q_cols, k_cols, v_cols = [
            slice(base + n * lanes, base + (n + 1) * lanes) for n in range(3)
        ]

        @pl.when(image == 0)
        def _():
            out_ref[:, base : base + 2 * lanes] = jnp.zeros((out_ref.shape[0], 2 * lanes), bf16)
            out_ref[:, v_cols] = go_ref[:, cols]

        k_all = k_ref[whole, :]
        v_all = v_ref[whole, :]
        q_all = q_ref[whole, :] * jnp.asarray(HEAD_DIM ** (-0.5), bf16)
        go_all = go_ref[whole, cols]
        key_grad = None
        value_grad = None
        for head in range(lanes // HEAD_DIM):
            mine = head_lanes(lanes, head)
            q_mine = jnp.where(mine, q_all, jnp.zeros_like(q_all))
            go_mine = jnp.where(mine, go_all, jnp.zeros_like(go_all))
            for row in range(0, WINDOW, QROWS):
                part = slice(row, row + QROWS)
                at = pl.ds(pl.multiple_of(start + row, 16), QROWS)
                inside = rows_inside(QROWS, row, first)
                weights, totals = attend_scores(q_mine[part], k_all, mask_ref[part, :])
                weights = weights * jnp.where(inside, 1.0 / totals, 0.0)
                weight_grad = dot(go_mine[part], v_all, 1, 1)
                product = weights * weight_grad
                score_grad = (
                    product - weights * jnp.sum(product, axis=-1, keepdims=True)
                ).astype(bf16)
                p_ref[part, :] = weights.astype(bf16)
                s_ref[part, :] = score_grad
                query_grad = (dot(score_grad, k_all, 1, 0) * HEAD_DIM ** (-0.5)).astype(bf16)
                out_ref[at, q_cols] = jnp.where(inside & mine, query_grad, out_ref[at, q_cols])
            key_part = dot(q_mine, s_ref[...], 0, 0)
            value_part = dot(go_mine, p_ref[...], 0, 0)
            key_grad = key_part if key_grad is None else key_grad + key_part
            value_grad = value_part if value_grad is None else value_grad + value_part
        key_rows = key_grad.T.astype(bf16)
        value_rows = value_grad.T.astype(bf16)
        out_ref[whole, k_cols] = jnp.where(inside_all, key_rows, out_ref[whole, k_cols])
        out_ref[whole, v_cols] = jnp.where(inside_all, value_rows, out_ref[whole, v_cols])


def qkv_operands(projected, tile):
    group_rows, total = projected.shape
    lanes = min(128, total // 3)
    if lanes % 128 == 0:
        specs = [
            pl.BlockSpec((group_rows, lanes), functools.partial(lambda n, i, *_: (0, n), 3 * tile + n))
            for n in range(3)
        ]
        return [projected] * 3, specs
    parts = [projected[:, n * lanes : (n + 1) * lanes] for n in range(3)]
    return parts, [fixed((group_rows, lanes))] * 3


def all_operands(projected):
    width = projected.shape[1] // 3
    operands, specs = [], []
    for tile in range(width // min(128, width)):
        more, places = qkv_operands(projected, tile)
        operands += more
        specs += places
    return operands, specs


def attend_forward(projected, geometry, spots, rows):
    begin, code = geometry
    group_rows, total = projected.shape
    width = total // 3
    blocks = group_rows // rows
    images = begin.shape[0]
    operands, specs = all_operands(projected)
    out = plain_call(
        functools.partial(attend_forward_kernel, blocks),
        (shaped((rows, width), bf16),) * blocks + (shaped((images, 8, WINDOW), f32),),
        code,
        *operands,
        grid=begin.shape,
        in_specs=[fixed(code.shape)] + specs,
        out_specs=(fixed((rows, width)),) * blocks
        + (pl.BlockSpec((1, 8, WINDOW), lambda i, *_: (i, 0, 0)),),
        scratch=[pltpu.VMEM((group_rows, width), bf16), pltpu.VMEM((WINDOW, WINDOW), f32)],
        scalars=(begin, spots),
        mebibytes=24,
        name="attention_forward",
    )
    return out[:blocks], out[blocks]


def attend_backward(projected, go_blocks, spots, begin, bias, tile, into):
    group_rows, total = projected.shape
    lanes = min(128, total // 3)
    operands, specs = qkv_operands(projected, tile)
    return plain_call(
        functools.partial(attend_backward_kernel, len(go_blocks)),
        shaped((group_rows, total), bf16),
        bias,
        *operands,
        *go_blocks,
        grid=begin.shape,
        in_specs=[pl.BlockSpec((1, 8, WINDOW), lambda i, *_: (i, 0, 0))]
        + specs
        + [fixed(block.shape) for block in go_blocks],
        out_specs=pl.BlockSpec((group_rows, 3 * lanes), lambda i, *_: (0, tile)),
        scratch=[pltpu.VMEM((WINDOW, WINDOW), bf16)] * 2
        + [pltpu.VMEM((group_rows, lanes), bf16), pltpu.VMEM((WINDOW, WINDOW), f32)],
        scalars=(begin, spots),
        into=into,
        mebibytes=56 if into else 24,
        name="attention_backward",
    )


def attend_geometry(segments, live_mask):
    group_rows = segments.shape[0]
    numbers = jnp.arange(group_rows // PATCHES, dtype=jnp.int32)
    positions = jnp.arange(group_rows, dtype=jnp.int32)
    begin = jnp.min(
        jnp.where(segments[None, :] == numbers[:, None], positions[None, :], group_rows - PATCHES),
        axis=1,
    )
    code = jnp.where(live_mask == 1, segments, -1)
    return begin, jnp.broadcast_to(code[:, None], (group_rows, 128))


def plain_call(kernel, out_shape, *operands, grid=(), in_specs=None, out_specs=None, scratch=(), scalars=(), into=(), mebibytes=16, name=None):
    params = pltpu.CompilerParams(vmem_limit_bytes=mebibytes * 1024 * 1024)
    if in_specs is None:
        in_specs = [pl.BlockSpec(a.shape, functools.partial(lambda n, *_: (0,) * n, a.ndim)) for a in operands]
    in_specs = list(in_specs) + [pl.BlockSpec(memory_space=pl.ANY)] * len(into)
    if out_specs is None:
        out_specs = jax.tree.map(
            lambda s: pl.BlockSpec(s.shape, functools.partial(lambda n, *_: (0,) * n, len(s.shape))), out_shape
        )
    return pl.pallas_call(
        kernel,
        grid_spec=pltpu.PrefetchScalarGridSpec(
            num_scalar_prefetch=len(scalars),
            grid=grid,
            in_specs=in_specs,
            out_specs=out_specs,
            scratch_shapes=list(scratch),
        ),
        out_shape=out_shape,
        input_output_aliases={len(scalars) + len(operands) + n: n for n in range(len(into))},
        compiler_params=params,
        cost_estimate=SMALL,
        name=name,
    )(*scalars, *operands, *into)


def shaped(shape, dtype):
    return jax.ShapeDtypeStruct(tuple(shape), dtype)


def row_blocks(rows, *widths):
    return [pl.BlockSpec((rows, w), lambda i, *_: (i, 0)) for w in widths]


def fixed(shape):
    return pl.BlockSpec(tuple(shape), functools.partial(lambda n, *_: (0,) * n, len(shape)))


def pack_kernel(live_ref, qkv_ref, proj_ref, up_ref, down_ref, qkv_out, up_out, down_out):
    count, slab, width = qkv_ref.shape
    lanes = min(128, width)
    for n in range(count):
        for t in range(width // lanes):
            at = (count * t + n) * lanes
            qkv_out[:, at : at + lanes] = qkv_ref[n][:, t * lanes : (t + 1) * lanes].astype(bf16)
    qkv_out[:, count * width :] = proj_ref[...].T.astype(bf16)
    up_out[:slab, :] = up_ref[...].astype(bf16)
    live = jnp.sum(jnp.sum(live_ref[...].astype(f32), axis=0, keepdims=True), axis=1, keepdims=True)
    high = jnp.floor(live * (1.0 / 256.0))
    middle = jnp.floor(live * (1.0 / 16.0)) - 16.0 * high
    low = live - 256.0 * high - 16.0 * middle
    row = lax.broadcasted_iota(jnp.int32, (DIGITS, up_out.shape[1]), 0)
    digits = jnp.where(row == 0, high, jnp.where(row == 1, middle, jnp.where(row == 2, low, 0.0)))
    up_out[slab:, :] = digits.astype(bf16)
    down_out[...] = down_ref[...].T.astype(bf16)


def first_kernel(tok_ref, par_ref, low_out):
    normed, _, _ = norm_forward(tok_ref[...], par_ref[0:1, :], par_ref[1:2, :])
    low_out[...] = normed.astype(bf16)


def place_blocks(blocks, spots):
    rows, width = blocks[0].shape

    def kernel(spot_ref, *refs):
        for n, ref in enumerate(refs[:-1]):
            refs[-1][pl.ds(pl.multiple_of(spot_ref[n], rows), rows), :] = ref[...]

    return plain_call(
        kernel,
        shaped((rows * len(blocks), width), bf16),
        *blocks,
        scalars=(spots,),
        mebibytes=20,
        name="place_blocks",
    )


def block_rows(block, slab):
    return pl.ds(pl.multiple_of(block * slab, slab), slab)


def stack_z(pieces, slab, places, count=1):
    height, width = pieces[0].shape
    extra = height - slab
    shapes = (shaped((N_Z * slab // count + extra, width), bf16),) * count

    def kernel(at_ref, *refs):
        held = refs[-1]
        for k, ref in enumerate(refs[:N_Z]):
            held[block_rows(lax.rem(at_ref[0] + N_Z - k, N_Z), slab), :] = ref[:slab, :]
        for n, out in enumerate(refs[N_Z:-1]):
            rows = N_Z * slab // count
            out[:rows, :] = held[n * rows : (n + 1) * rows, :]
            if extra:
                digits = refs[0][slab:, :].astype(f32)
                for ref in refs[1:N_Z]:
                    digits = digits + ref[slab:, :].astype(f32)
                out[rows:, :] = digits.astype(bf16)

    out = plain_call(
        kernel,
        shapes,
        *pieces,
        scalars=(places,),
        scratch=[pltpu.VMEM((N_Z * slab, width), bf16)],
        mebibytes=8,
        name="stack_z",
    )
    return out if count > 1 else out[0]


def weave(columns, cuts, slab, places):
    n_x = len(columns[0])
    width = columns[0][0][0].shape[1]
    flat = [piece for column in columns for half in column for piece in half]
    edges = [0, *cuts, width]
    sizes = [stop - start for start, stop in zip(edges[:-1], edges[1:])]

    def kernel(at_ref, *refs):
        outs = refs[len(flat) :]
        used = 0
        for y, column in enumerate(columns):
            for dx, half in enumerate(column):
                x = lax.rem(at_ref[1] + dx, n_x)
                share = N_Z // len(half)
                for z in range(N_Z):
                    piece = refs[used + z // share]
                    at = block_rows(z * n_x + x, slab)
                    row = z % share * slab
                    for out, start, size in zip(outs, edges, sizes):
                        out[at, y * size : (y + 1) * size] = piece[
                            row : row + slab, start : start + size
                        ]
                used += len(half)

    out = plain_call(
        kernel,
        tuple(shaped((N_Z * n_x * slab, size * len(columns)), bf16) for size in sizes),
        *flat,
        scalars=(places,),
        mebibytes=12,
        name="weave",
    )
    return out if cuts else out[0]


def proj_kernel(count, each, *refs):
    blocks, parts = refs[:count], refs[count : count + count // each]
    tok_ref, par_ref, res_out, low_out = refs[count + count // each :]
    total = tok_ref[...]
    for n, block in enumerate(blocks):
        size = block.shape[1]
        part = parts[n // each][:, n % each * size : (n % each + 1) * size]
        total = total + dot(block[...], part, 1, 1)
    res_out[...] = total
    normed, _, _ = norm_forward(total, par_ref[2:3, :], par_ref[3:4, :])
    low_out[...] = normed.astype(bf16)


ERF_TOP = (
    -2.72614225801306e-10,
    2.77068142495902e-08,
    -2.10102402082508e-06,
    -5.69250639462346e-05,
    -7.34990630326855e-04,
    -2.95459980854025e-03,
    -1.60960333262415e-02,
)
ERF_LOW = (
    -1.45660718464996e-05,
    -2.13374055278905e-04,
    -1.68282697438203e-03,
    -7.37332916720468e-03,
    -1.42647390514189e-02,
)


def erf(value):
    value = jnp.clip(value, -4.0, 4.0)
    square = value * value
    top = jnp.full_like(square, ERF_TOP[0])
    for number in ERF_TOP[1:]:
        top = top * square + number
    low = jnp.full_like(square, ERF_LOW[0])
    for number in ERF_LOW[1:]:
        low = low * square + number
    inverse = pl.reciprocal(low, approx=True)
    inverse = inverse * (2.0 - low * inverse)
    return value * top * inverse


def up_kernel(count, low_ref, *refs):
    outs = refs[-2 * count :]
    for n, part in enumerate(refs[:count]):
        hidden = dot(low_ref[...], part[...], 1, 0)
        share = 0.5 * (1.0 + erf(hidden * 0.7071067811865476))
        outs[2 * n][...] = (hidden * share).astype(bf16)
        slope = share + hidden * jnp.exp(-0.5 * hidden * hidden) * 0.3989422804014327
        outs[2 * n + 1][...] = slope.astype(bf16)


def up_call(low, parts, rows_all, spot, into):
    rows, model = low.shape
    width = parts[0].shape[1]
    cols = pl.BlockSpec((rows, TILE), lambda i, *_: (spot, i))
    return plain_call(
        functools.partial(up_kernel, len(parts)),
        (shaped((rows_all, width), bf16),) * (2 * len(parts)),
        low,
        *parts,
        grid=(width // TILE,),
        in_specs=[fixed(low.shape)] + [pl.BlockSpec((model, TILE), lambda i, *_: (0, i))] * len(parts),
        out_specs=(cols,) * (2 * len(parts)),
        into=into,
        mebibytes=14,
        name="up",
    )


def hidden_kernel(count, low_ref, *refs):
    outs = refs[-count:]
    for n in range(count):
        slope, part = refs[n], refs[count + n]
        outs[n][...] = (dot(low_ref[...], part[...], 1, 0) * slope[...].astype(f32)).astype(bf16)


def hidden_call(low, slopes, parts, spot, into):
    rows, model = low.shape
    width = parts[0].shape[1]
    cols = pl.BlockSpec((rows, TILE), lambda i, *_: (spot, i))
    return plain_call(
        functools.partial(hidden_kernel, len(parts)),
        tuple(shaped(slope.shape, bf16) for slope in slopes),
        low,
        *slopes,
        *parts,
        grid=(width // TILE,),
        in_specs=[fixed(low.shape)]
        + [cols] * len(parts)
        + [pl.BlockSpec((model, TILE), lambda i, *_: (0, i))] * len(parts),
        out_specs=(cols,) * len(parts),
        into=into,
        mebibytes=14,
        name="hidden",
    )


def wide_kernel(count, *refs):
    total = dot(refs[0][...], refs[count][...], 1, 1)
    for n in range(1, count):
        total = total + dot(refs[n][...], refs[count + n][...], 1, 1)
    refs[-1][...] = total.astype(refs[-1].dtype)


def wide_call(values, parts, rows, spot, kind):
    model, width = parts[0].shape
    return plain_call(
        functools.partial(wide_kernel, len(values)),
        shaped((rows, model), kind),
        *values,
        *parts,
        grid=(model // TILE,),
        in_specs=[pl.BlockSpec((rows, width), lambda i, *_: (spot, 0))] * len(values)
        + [pl.BlockSpec((TILE, width), lambda i, *_: (i, 0))] * len(parts),
        out_specs=pl.BlockSpec((rows, TILE), lambda i, *_: (0, i)),
        mebibytes=14,
        name="wide",
    )


def loss_kernel(chunks, each, *refs):
    res_ref, tea_ref, own_ref = refs[:3]
    received = refs[3 : 3 + chunks * each]
    live_ref, count_ref, grad_out, low_out, loss_out, far_ref = refs[3 + chunks * each :]
    add_received(received, each, far_ref)
    error = res_ref[...] - tea_ref[...] + own_ref[...] + far_ref[...]
    weighted = live_ref[...] * error
    grad = 2.0 * weighted / count_ref[...]
    grad_out[...] = grad
    low_out[...] = grad.astype(bf16)
    sums = jnp.sum(weighted * error, axis=0, keepdims=True)
    sums = jnp.concatenate([sums, jnp.zeros((7, sums.shape[1]), f32)], axis=0)
    loss_out[...] = jnp.where(pl.program_id(0) == 0, sums, loss_out[...] + sums)


def add_received(received, each, far_ref):
    for n in range(len(received) // each):

        @pl.when(pl.program_id(0) == n)
        def _():
            total = received[n * each][...].astype(f32)
            for ref in received[n * each + 1 : (n + 1) * each]:
                total = total + ref[...].astype(f32)
            far_ref[...] = total


def beside_call(parts):
    rows, width = parts[0].shape

    def kernel(*refs):
        for n, ref in enumerate(refs[:-1]):
            refs[-1][:, n * width : (n + 1) * width] = ref[...]

    return plain_call(
        kernel, shaped((rows, width * len(parts)), bf16), *parts, mebibytes=8, name="beside"
    )


def spread_kernel(each, tiles, low_ref, *refs):
    count = len(refs) // (1 + each * tiles)
    outs = refs[count:]
    for n in range(count * each):
        size = refs[0].shape[1] // each
        part = refs[n // each][:, n % each * size : (n % each + 1) * size]
        piece = dot(low_ref[...], part, 1, 0).astype(bf16)
        lanes = size // tiles
        for tile in range(tiles):
            outs[tile * count * each + n][...] = piece[:, tile * lanes : (tile + 1) * lanes]


def spread_call(low, parts, each):
    width = parts[0].shape[1] // each
    lanes = min(128, width)
    count = len(parts) * each
    out = plain_call(
        functools.partial(spread_kernel, each, width // lanes),
        tuple(shaped((low.shape[0], lanes), bf16) for _ in range(count * (width // lanes))),
        low,
        *parts,
        mebibytes=12,
        name="spread",
    )
    return [out[n : n + count] for n in range(0, len(out), count)]


def unproject_kernel(half, spots, grad_ref, part_ref, far_out, near_out):
    piece = dot(grad_ref[...], part_ref[...], 1, 1)

    @pl.when(pl.program_id(0) < half)
    def _():
        far_out[...] = piece.astype(bf16)

    @pl.when(pl.program_id(0) >= half)
    def _():
        near_out[...] = piece.astype(bf16)


def unproject_call(grads, part, blocks, rows):
    half = len(blocks) // 2
    model, width = part.shape
    return plain_call(
        functools.partial(unproject_kernel, half),
        (shaped((half * rows, model), bf16),) * 2,
        grads,
        part,
        grid=(len(blocks),),
        in_specs=[
            pl.BlockSpec((rows, width), lambda i, spots: (spots[i], 0)),
            fixed(part.shape),
        ],
        out_specs=(
            pl.BlockSpec((rows, model), lambda i, spots: (jnp.minimum(i, half - 1), 0)),
            pl.BlockSpec((rows, model), lambda i, spots: (jnp.maximum(i - half, 0), 0)),
        ),
        scalars=(jnp.stack(blocks).astype(jnp.int32),),
        mebibytes=48,
        name="unproject",
    )


def outer_proj_kernel(half, low_ref, *refs):
    blocks, (far_out, *near) = refs[: 2 * half], refs[2 * half :]
    turned = low_ref[...].astype(f32).T.astype(bf16)
    width = blocks[0].shape[1]
    for n in range(half):
        far_out[:, n * width : (n + 1) * width] = dot(turned, blocks[half + n][...], 1, 0).astype(bf16)
        near[n][...] = dot(turned, blocks[n][...], 1, 0).astype(bf16)


def outer_proj_call(low, blocks):
    model = low.shape[1]
    width = blocks[0].shape[1]
    half = len(blocks) // 2
    out = plain_call(
        functools.partial(outer_proj_kernel, half),
        (shaped((model, half * width), bf16),) + (shaped((model, width), bf16),) * half,
        low,
        *blocks,
        mebibytes=14,
        name="outer_proj",
    )
    return out[0], out[1:]


def add_lanes(own, received):
    width = own[0].shape[1]

    def kernel(*refs):
        got = refs[len(own)]
        for n, ref in enumerate(refs[: len(own)]):
            other = got[:, n * width : (n + 1) * width].astype(f32)
            refs[len(own) + 1 + n][...] = (ref[...].astype(f32) + other).astype(bf16)

    return plain_call(
        kernel,
        tuple(shaped(part.shape, bf16) for part in own),
        *own,
        received,
        mebibytes=8,
        name="add_lanes",
    )


def norm_sums(grad, scaled, out_ref, first):
    sums = jnp.concatenate(
        [
            jnp.sum(grad * scaled, axis=0, keepdims=True),
            jnp.sum(grad, axis=0, keepdims=True),
            jnp.zeros((6, grad.shape[1]), f32),
        ],
        axis=0,
    )
    out_ref[...] = jnp.where(first, sums, out_ref[...] + sums)


def middle_kernel(chunks, each, *refs):
    grad_ref, received = refs[0], refs[1 : 1 + chunks * each]
    res_ref, gout_ref, par_ref, full_out, low_out, sum_out, far_ref = refs[1 + chunks * each :]
    add_received(received, each, far_ref)
    _, scaled, inverse = norm_forward(res_ref[...], par_ref[2:3, :], par_ref[3:4, :])
    grad = grad_ref[...] + far_ref[...]
    full = gout_ref[...] + norm_backward(grad, scaled, inverse, par_ref[2:3, :])
    full_out[...] = full
    low_out[...] = full.astype(bf16)
    norm_sums(grad, scaled, sum_out, pl.program_id(0) == 0)


def leave_kernel(count, *refs):
    own_ref, received = refs[0], refs[1 : 1 + count]
    tok_ref, res_ref, par_ref, two_ref, loss_ref, out_ref, sum_out, sum_ref = refs[1 + count :]
    _, scaled, inverse = norm_forward(tok_ref[...], par_ref[0:1, :], par_ref[1:2, :])
    grad = own_ref[...]
    for ref in received:
        grad = grad + ref[...].astype(f32)
    out_ref[...] = res_ref[...] + norm_backward(grad, scaled, inverse, par_ref[0:1, :])
    norm_sums(grad, scaled, sum_ref, pl.program_id(0) == 0)
    sum_out[...] = jnp.concatenate(
        [sum_ref[0:2, :], two_ref[0:2, :], loss_ref[0:1, :], jnp.zeros((3, grad.shape[1]), f32)],
        axis=0,
    )


def split_x(parts, n_x, places):
    model = parts[0][0].shape[0]
    slab = model // (N_Z * n_x)
    total = sum(part[0].shape[1] for part in parts)
    flat = [piece for part in parts for piece in part]

    def kernel(at_ref, *refs):
        outs = refs[len(flat) :]
        for dx in range(n_x):
            x = lax.rem(at_ref[1] + dx, n_x)
            for z in range(N_Z):
                at = block_rows(z * n_x + x, slab)
                lane = 0
                used = 0
                for part in parts:
                    value = refs[used][at, :]
                    size = value.shape[1]
                    if len(part) > 1:
                        value = value.astype(f32)
                        for ref in refs[used + 1 : used + len(part)]:
                            value = value + ref[at, :].astype(f32)
                        value = value.astype(bf16)
                    outs[dx][z * slab : (z + 1) * slab, lane : lane + size] = value
                    lane += size
                    used += len(part)

    return plain_call(
        kernel,
        tuple(shaped((model // n_x, total), bf16) for _ in range(n_x)),
        *flat,
        scalars=(places,),
        mebibytes=12,
        name="split_x",
    )


def split_z(parts, places):
    rows, width = parts[0].shape
    slab = rows // N_Z

    def kernel(at_ref, *refs):
        for k, out in enumerate(refs[len(parts) :]):
            at = block_rows(lax.rem(at_ref[0] + k, N_Z), slab)
            total = refs[0][at, :].astype(f32)
            for ref in refs[1 : len(parts)]:
                total = total + ref[at, :].astype(f32)
            out[...] = total.astype(out.dtype)

    shapes = (shaped((slab, width), f32),) + (shaped((slab, width), bf16),) * (N_Z - 1)
    return plain_call(kernel, shapes, *parts, scalars=(places,), mebibytes=8, name="split_z")


def adam_kernel(layout, counts, *refs):
    grads = []
    for count in counts:
        grad = refs[0][...].astype(f32)
        for ref in refs[1:count]:
            grad = grad + ref[...].astype(f32)
        grads.append(grad)
        refs = refs[count:]
    count = len(layout)
    states, outs = refs[: 3 * count], refs[3 * count :]
    for n, (source, start, size, turned) in enumerate(layout):
        weight, first, second = states[3 * n : 3 * n + 3]
        if len(weight.shape) == 3:
            matrices = weight.shape[0]
            lanes = size // matrices
            for k in range(matrices):
                own = [
                    grads[at][:, lane + k * lanes : lane + (k + 1) * lanes] for at, lane in start
                ]
                own = own[0] if len(own) == 1 else jnp.concatenate(own, axis=1)
                new = adam_step(weight[k], own, first[k], second[k], weight_decay, learn_rate)
                for out, value in zip(outs[3 * n : 3 * n + 3], new):
                    out[k] = value
        else:
            part = grads[source][:, start : start + size]
            if turned:
                part = part.T
            new = adam_step(weight[...], part, first[...], second[...], weight_decay, learn_rate)
            for out, value in zip(outs[3 * n : 3 * n + 3], new):
                out[...] = value


def adam_call(groups, layout, *states):
    shapes = tuple(shaped(s.shape, f32) for s in states)
    out = plain_call(
        functools.partial(adam_kernel, layout, [len(group) for group in groups]),
        shapes,
        *[piece for group in groups for piece in group],
        *states,
        mebibytes=16,
        name="adam",
    )
    return [out[3 * n : 3 * n + 3] for n in range(len(layout))]


def tie(*values):
    return lax.optimization_barrier(values)


def local(
    n_x,
    n_y,
    tokens,
    teacher,
    segments,
    live_mask,
    weight_qkv,
    weight_proj,
    weight_up,
    weight_down,
    norm_params,
    first_qkv,
    first_proj,
    first_up,
    first_down,
    first_norms,
    second_qkv,
    second_proj,
    second_up,
    second_down,
    second_norms,
):
    z_at, x_at = lax.axis_index("z"), lax.axis_index("x")
    y_at, core_at = lax.axis_index("y"), lax.axis_index("core")
    rows, model = tokens.shape
    group_rows = segments.shape[0]
    slab = weight_qkv.shape[1]
    width = weight_qkv.shape[2]
    unit = weight_up.shape[1]
    part_rows = min(128, rows)
    wide_rows = min(256, rows)
    depth = N_Z * slab
    sizes = {"z": N_Z, "x": n_x, "y": n_y, "core": N_CORE}
    places = jnp.stack([z_at, x_at]).astype(jnp.int32)
    offsets = [(dc, dy) for dc in range(N_CORE) for dy in range(n_y)]
    other = N_CORE - 1

    def send(value, axis, step):
        size = sizes[axis]
        return lax.ppermute(value, axis, [(i, (i + step) % size) for i in range(size)])

    def send_col(value, dy, dc):
        perm = [
            (y * N_CORE + c, (y + dy) % n_y * N_CORE + (c + dc) % N_CORE)
            for y in range(n_y)
            for c in range(N_CORE)
        ]
        return lax.ppermute(value, ("y", "core"), perm)

    def fetch(value, axis):
        return [value] + [send(value, axis, -k) for k in range(1, sizes[axis])]

    def fetch_z(value):
        return [value] + [send(value, "z", k) for k in range(1, N_Z)]

    def place(dy, dc):
        return ((y_at + dy) % n_y * N_CORE + (core_at + dc) % N_CORE) * rows

    shard_qkv, shard_up, shard_down = plain_call(
        pack_kernel,
        (
            shaped((slab, 4 * width), bf16),
            shaped((slab + DIGITS, unit), bf16),
            shaped((slab, unit), bf16),
        ),
        live_mask.reshape(-1, 128),
        weight_qkv,
        weight_proj,
        weight_up,
        weight_down,
        mebibytes=56,
        name="pack",
    )
    near_qkv = fetch_z(shard_qkv)
    block_qkv = stack_z(near_qkv, slab, places)
    geometry = attend_geometry(segments, live_mask)
    own_live = lax.dynamic_slice_in_dim(
        live_mask, (y_at * N_CORE + core_at) * rows, rows, 0
    ).astype(f32)[:, None]
    spots_here = jnp.stack([place(dy, dc) for dc, dy in offsets]).astype(jnp.int32)
    spots = jnp.stack([place(-dy, -dc) for dc, dy in offsets]).astype(jnp.int32)
    block_qkv, shard_down, shard_up, tokens, geometry, own_live, spots_here, spots = tie(
        block_qkv, shard_down, shard_up, tokens, geometry, own_live, spots_here, spots
    )

    beside_qkv = fetch(block_qkv, "x")
    near_up = fetch_z(shard_up)
    low_one = plain_call(
        first_kernel,
        shaped(tokens.shape, bf16),
        tokens,
        norm_params,
        grid=(rows // part_rows,),
        in_specs=row_blocks(part_rows, model) + [fixed(norm_params.shape)],
        out_specs=row_blocks(part_rows, model)[0],
        mebibytes=8,
        name="first",
    )
    blocks_one = fetch(low_one, "y")
    beside_qkv, near_up, blocks_one, shard_down = tie(beside_qkv, near_up, blocks_one, shard_down)

    block_up = stack_z(near_up, slab, places)
    full_qkv, part_proj = weave([[[part] for part in beside_qkv]], [3 * width], slab, places)
    block_up, part_proj, blocks_one = tie(block_up, part_proj, blocks_one)
    blocks_one = blocks_one + [send(block, "core", -1) for block in blocks_one]
    group_one = place_blocks(blocks_one, spots_here)
    beside_up = fetch(block_up, "x")
    near_down = fetch_z(shard_down)
    full_proj = fetch(part_proj, "y")
    projected = dot(group_one, full_qkv, 1, 0).astype(bf16)
    mixed, bias = attend_forward(projected, geometry, spots, rows)
    mixed, beside_up, near_down, full_proj = tie(mixed, beside_up, near_down, full_proj)

    blocks_mixed = [
        piece if key == (0, 0) else send_col(piece, -key[1], -key[0])
        for key, piece in zip(offsets, mixed)
    ]
    full_proj = [beside_call(full_proj)]
    full_proj.append(send(full_proj[0], "core", -1))
    blocks_down = stack_z(near_down, slab, places, 2)
    beside_down = [fetch(blocks_down[0], "x")]
    full_up = [weave([[[part] for part in beside_up]], [], slab, places)]
    live_count = sum(
        256.0 * part[depth, 0].astype(f32) + 16.0 * part[depth + 1, 0].astype(f32)
        + part[depth + 2, 0].astype(f32)
        for part in beside_up
    ).reshape(1, 1)
    blocks_mixed, full_proj, full_up, live_count, beside_down, blocks_down = tie(
        blocks_mixed, full_proj, full_up, live_count, beside_down, blocks_down
    )
    beside_down.append(fetch(blocks_down[1], "x"))
    full_up.append(send(full_up[0], "core", -1))
    count = len(offsets)
    residual, low_two = plain_call(
        functools.partial(proj_kernel, count, n_y),
        (shaped(tokens.shape, f32), shaped(tokens.shape, bf16)),
        *blocks_mixed,
        *full_proj,
        tokens,
        norm_params,
        grid=(rows // wide_rows,),
        in_specs=row_blocks(wide_rows, *([width] * count))
        + [fixed(part.shape) for part in full_proj]
        + row_blocks(wide_rows, model)
        + [fixed(norm_params.shape)],
        out_specs=tuple(row_blocks(wide_rows, model, model)),
        mebibytes=18,
        name="proj",
    )
    low_two, full_up = tie(low_two, full_up)

    chunk = min(256, rows)
    chunks = range(rows // chunk)
    neighbours = range(1, n_y)
    rows_all = n_y * rows

    def cross(value, n):
        piece = value[n * chunk : (n + 1) * chunk]
        return {dy: send(piece, "y", -dy) for dy in neighbours}

    def spot_of(dy, n):
        return (dy * rows) // chunk + n

    low_far = {0: cross(low_two, 0)}
    hidden = up_call(low_two, full_up, rows_all, 0, ())
    low_far[0], hidden, low_two, beside_down = tie(low_far[0], hidden, low_two, beside_down)
    full_down = [weave([list(zip(*beside_down))], [], slab, places)]
    full_down.append(send(full_down[0], "core", -1))
    far_out = {}
    for n in chunks:
        if n + 1 in chunks:
            low_far[n + 1] = cross(low_two, n + 1)
        for dy in neighbours:
            hidden = up_call(low_far[n][dy], full_up, rows_all, spot_of(dy, n), hidden)
        outs = {
            dy: wide_call(hidden[::2], full_down, chunk, spot_of(dy, n), bf16) for dy in neighbours
        }
        if n + 1 in chunks:
            outs, hidden, low_far[n + 1] = tie(outs, hidden, low_far[n + 1])
        else:
            outs, hidden = tie(outs, hidden)
        if n:
            far_out[n - 1] = tie(far_out[n - 1], outs)[0]
        far_out[n] = {dy: send(outs[dy], "y", dy) for dy in neighbours}
    own_out = wide_call(hidden[::2], full_down, rows, 0, f32)
    own_out, far_out = tie(own_out, far_out)
    far_out = [far_out[n][dy] for n in chunks for dy in neighbours]
    each = len(neighbours)
    grad_output, grad_branch, loss_rows = plain_call(
        functools.partial(loss_kernel, len(chunks), each),
        (shaped(tokens.shape, f32), shaped(tokens.shape, bf16), shaped((8, model), f32)),
        residual,
        teacher,
        own_out,
        *far_out,
        own_live,
        live_count,
        grid=(len(chunks),),
        in_specs=row_blocks(chunk, model, model, model)
        + [fixed((chunk, model))] * len(far_out)
        + row_blocks(chunk, 1)
        + [fixed((1, 1))],
        out_specs=tuple(row_blocks(chunk, model, model) + [fixed((8, model))]),
        scratch=[pltpu.VMEM((chunk, model), f32)],
        mebibytes=20,
        name="loss",
    )
    active, slope = hidden[::2], hidden[1::2]

    grad_far = {0: cross(grad_branch, 0)}
    grad_hidden = hidden_call(grad_branch, slope, full_down, 0, ())
    own_two = wide_call(grad_hidden, full_up, rows, 0, f32)
    grad_far[0], grad_hidden, own_two, grad_branch = tie(
        grad_far[0], grad_hidden, own_two, grad_branch
    )
    def gather_rows(own, far):
        return jnp.concatenate([own] + [far[n][dy] for dy in neighbours for n in chunks], axis=0)

    far_two = {}
    for n in chunks:
        if n + 1 in chunks:
            grad_far[n + 1] = cross(grad_branch, n + 1)
        for dy in neighbours:
            grad_hidden = hidden_call(
                grad_far[n][dy], slope, full_down, spot_of(dy, n), grad_hidden
            )
        outs = {
            dy: wide_call(grad_hidden, full_up, chunk, spot_of(dy, n), bf16) for dy in neighbours
        }
        if n + 1 in chunks:
            outs, grad_hidden, grad_far[n + 1] = tie(outs, grad_hidden, grad_far[n + 1])
        else:
            grad_all = gather_rows(grad_branch, grad_far)
            far_down = dot(grad_all, active[other], 0, 0).astype(bf16)
            outs, grad_hidden, grad_all, far_down, far_two = tie(
                outs, grad_hidden, grad_all, far_down, far_two
            )
        far_two[n] = {dy: send(outs[dy], "y", dy) for dy in neighbours}

    low_all = gather_rows(low_two, low_far)
    far_up = dot(low_all, grad_hidden[other], 0, 0).astype(bf16)
    sent_down, sent_up = send(far_down, "core", 1), send(far_up, "core", 1)
    hold_down = (dot(grad_all, active[0], 0, 0) + sent_down.astype(f32)).astype(bf16)
    halves_down = split_x([[hold_down]], n_x, places)
    hold_up = (dot(low_all, grad_hidden[0], 0, 0) + sent_up.astype(f32)).astype(bf16)
    halves_up = split_x([[hold_up]], n_x, places)
    far_two, halves_down, halves_up = tie(far_two, halves_down, halves_up)
    far_two = [far_two[n][dy] for n in chunks for dy in neighbours]
    grad_residual, grad_low, sums_two = plain_call(
        functools.partial(middle_kernel, len(chunks), each),
        (shaped(tokens.shape, f32), shaped(tokens.shape, bf16), shaped((8, model), f32)),
        own_two,
        *far_two,
        residual,
        grad_output,
        norm_params,
        grid=(len(chunks),),
        in_specs=row_blocks(chunk, model)
        + [fixed((chunk, model))] * len(far_two)
        + row_blocks(chunk, model, model)
        + [fixed(norm_params.shape)],
        out_specs=tuple(row_blocks(chunk, model, model) + [fixed((8, model))]),
        scratch=[pltpu.VMEM((chunk, model), f32)],
        mebibytes=20,
        name="middle",
    )
    pieces_attn = spread_call(grad_low, full_proj, n_y)
    pieces_attn, halves_down, halves_up, grad_low = tie(
        pieces_attn, halves_down, halves_up, grad_low
    )

    def send_back(pieces):
        return [
            piece if key == (0, 0) else send_col(piece, key[1], key[0])
            for key, piece in zip(offsets, pieces)
        ]

    def hop_x(halves):
        return [halves[0]] + [send(halves[dx], "x", dx) for dx in range(1, n_x)]

    def spread_z(pieces):
        return [pieces[0]] + [send(pieces[k], "z", k) for k in range(1, N_Z)]

    lanes = 3 * min(128, width)
    tiles = 3 * width // lanes
    sent_attn = send_back(pieces_attn[0])
    parts_down = hop_x(halves_down)
    far_proj, grad_proj = outer_proj_call(grad_low, blocks_mixed)
    sent_attn, far_proj, grad_proj = tie(sent_attn, far_proj, grad_proj)

    sent_later = [send_back(pieces) for pieces in pieces_attn[1:]]
    sent_proj = send(far_proj, "core", 1)
    grad_projected = attend_backward(projected, sent_attn, spots, geometry[0], bias, 0, ())

    def grad_tile(tile):
        cols = slice(tile * lanes, (tile + 1) * lanes)
        return dot(group_one, grad_projected[:, cols], 0, 0).astype(bf16)

    tile_grads = [grad_tile(0)] if tiles > 1 else []
    grad_projected, sent_later, sent_proj, parts_down, halves_up, tile_grads = tie(
        grad_projected, sent_later, sent_proj, parts_down, halves_up, tile_grads
    )

    hold_proj = add_lanes(grad_proj, sent_proj)
    pieces_down = split_z(parts_down, places)
    grad_projected, pieces_down, hold_proj, halves_up = tie(
        grad_projected, pieces_down, hold_proj, halves_up
    )
    parts_up = hop_x(halves_up)
    last_down = spread_z(pieces_down)
    part_proj = [hold_proj[0]] + [send(hold_proj[k], "y", k) for k in range(1, n_y)]
    for tile in range(1, tiles):
        grad_projected = attend_backward(
            projected, sent_later[tile - 1], spots, geometry[0], bias, tile, (grad_projected,)
        )
    grad_projected, parts_up, last_down, part_proj = tie(
        grad_projected, parts_up, last_down, part_proj
    )

    far_one, near_one = unproject_call(
        grad_projected,
        full_qkv,
        [place(dy, dc) // rows for dc in reversed(range(N_CORE)) for dy in range(n_y)],
        rows,
    )
    far_one, grad_projected = tie(far_one, grad_projected)
    sent_one = send(far_one, "core", 1)
    tile_grads += [grad_tile(tile) for tile in range(len(tile_grads), tiles)]
    halves_qkv = split_x([[part] for part in tile_grads] + [part_proj], n_x, places)
    pieces_up = split_z(parts_up, places)
    halves_qkv, sent_one, near_one, pieces_up = tie(halves_qkv, sent_one, near_one, pieces_up)

    parts = [
        near_one[dy * rows : (dy + 1) * rows].astype(f32)
        + sent_one[dy * rows : (dy + 1) * rows].astype(f32)
        for dy in range(n_y)
    ]
    sent_parts = [parts[k].astype(bf16) for k in range(1, n_y)]
    halves_qkv, sent_parts, pieces_up = tie(halves_qkv, sent_parts, pieces_up)
    received = [send(part, "y", k) for k, part in enumerate(sent_parts, 1)]
    parts_qkv = hop_x(halves_qkv)
    last_up = spread_z(pieces_up)
    (new_down,) = adam_call(
        [last_down], [(0, 0, unit, True)], weight_down, first_down, second_down
    )
    parts_qkv, received, last_up, new_down = tie(parts_qkv, received, last_up, new_down)

    pieces_qkv = split_z(parts_qkv, places)
    token_grad, sums = plain_call(
        functools.partial(leave_kernel, len(received)),
        (shaped(tokens.shape, f32), shaped((8, model), f32)),
        parts[0],
        *received,
        tokens,
        grad_residual,
        norm_params,
        sums_two,
        loss_rows,
        grid=(rows // part_rows,),
        in_specs=row_blocks(part_rows, *([model] * (3 + len(received))))
        + [fixed(norm_params.shape), fixed((8, model)), fixed((8, model))],
        out_specs=tuple(row_blocks(part_rows, model) + [fixed((8, model))]),
        scratch=[pltpu.VMEM((8, model), f32)],
        mebibytes=14,
        name="leave",
    )
    sums, token_grad, pieces_qkv = tie(sums, token_grad, pieces_qkv)
    last_qkv = spread_z(pieces_qkv)
    for axis in ("core", "y", "x", "z"):
        step = 1
        while step < sizes[axis]:
            pairs = [(i, i ^ step) for i in range(sizes[axis])]
            sums = sums + lax.ppermute(sums, axis, pairs)
            step *= 2
    (new_up,) = adam_call([last_up], [(0, 0, unit, False)], weight_up, first_up, second_up)
    new_qkv, new_proj = adam_call(
        [last_qkv],
        [(0, [(0, n * lanes) for n in range(tiles)], lanes, False), (0, 3 * width, width, True)],
        weight_qkv,
        first_qkv,
        second_qkv,
        weight_proj,
        first_proj,
        second_proj,
    )
    sums, new_qkv, new_proj, new_up = tie(sums, new_qkv, new_proj, new_up)
    loss_sum = jnp.sum(sums[4])
    live_count = live_count[0, 0]

    new_norms = adam_step(norm_params, sums[:4], first_norms, second_norms, 0.0, norm_rate)
    return (
        loss_sum / live_count,
        token_grad,
        new_qkv[0],
        new_proj[0],
        new_up[0],
        new_down[0],
        new_norms[0],
        new_qkv[1],
        new_proj[1],
        new_up[1],
        new_down[1],
        new_norms[1],
        new_qkv[2],
        new_proj[2],
        new_up[2],
        new_down[2],
        new_norms[2],
    )


def solution(mesh):
    n_x = mesh.shape["row"] // N_Z
    n_y = mesh.shape["col"] // N_CORE
    mesh = jax.sharding.Mesh(
        mesh.devices.reshape(N_Z, n_x, n_y, N_CORE), ("z", "x", "y", "core")
    )
    row, col = ("z", "x"), ("y", "core")
    matrices = (P(None, row, col), P(col, row), P(row, col), P(col, row), P())
    tokens = P(row + col, None)
    return jax.shard_map(
        functools.partial(local, n_x, n_y),
        mesh=mesh,
        in_specs=(tokens, tokens, P(row), P(row)) + matrices * 3,
        out_specs=(P(), tokens) + matrices * 3,
        check_vma=False,
    )
```
